32 devices in a mesh: dp: 4 (over y, x), fsdp: 8 (over z, core).
Axes of the slice: x: 2, y: 2, z: 4, core: 2. Of those that a mesh axis runs over, the one named last changes fastest.
Arguments:
- x_short: bfloat16 [256, 128, 768], P(('dp', 'fsdp')), may hold values from -6 to 6
- x_long: bfloat16 [64, 512, 768], P(('dp', 'fsdp')), may hold values from -6 to 6
- cot_short: bfloat16 [256, 128, 768], P(('dp', 'fsdp')), may hold values from -6 to 6
- cot_long: bfloat16 [64, 512, 768], P(('dp', 'fsdp')), may hold values from -6 to 6
- logit_cot_short: float32 [256, 14], P(('dp', 'fsdp'))
- logit_cot_long: float32 [64, 14], P(('dp', 'fsdp'))
- len_short: int32 [256], P(('dp', 'fsdp')), may hold values from 64 to 128, as said below
- len_long: int32 [64], P(('dp', 'fsdp')), may hold values from 256 to 512, as said below
- block_slot: int32 [439], replicated, may hold values from 0 to 439, as said below
- master: float32 [440, 128, 128], P('fsdp')
- left_stat: float32 [440, 128, 128], P('fsdp'), as said below
- right_stat: float32 [440, 128, 128], P('fsdp'), as said below
- left_root: float32 [440, 128, 128], P('fsdp'), as said below
- right_root: float32 [440, 128, 128], P('fsdp'), as said below
- small_params: float32 [11406], replicated
- small_first: float32 [11406], replicated
- small_second: float32 [11406], replicated, as said below
Outputs:
- encoded_short: bfloat16 [256, 128, 768], P(('dp', 'fsdp'))
- logits_short: float32 [256, 14], P(('dp', 'fsdp'))
- encoded_long: bfloat16 [64, 512, 768], P(('dp', 'fsdp'))
- logits_long: float32 [64, 14], P(('dp', 'fsdp'))
- input_grad_short: float32 [256, 128, 768], P(('dp', 'fsdp'))
- input_grad_long: float32 [64, 512, 768], P(('dp', 'fsdp'))
- slot_grad: float32 [440, 128, 128], P('fsdp')
- new_left: float32 [440, 128, 128], P('fsdp')
- new_right: float32 [440, 128, 128], P('fsdp')
- new_master: float32 [440, 128, 128], P('fsdp')
- new_first: float32 [11406], replicated
- new_second: float32 [11406], replicated
- new_small: float32 [11406], replicated
The draws below stay inside these ranges and needn't reach their ends.
Inputs may be any that keep to these rules, and one draw needn't show every extreme that they name: `len_short`: each sequence's tokens fill its first positions; some sequence of every draw fills all 128. `len_long`: each sequence's tokens fill its first positions; some sequence of every draw fills all 512. `block_slot`: all different; slot s lies on index s // 55 of fsdp; the slots that no block names hold no block. `left_stat`: symmetric in every slot. `right_stat`: symmetric in every slot. `left_root`: symmetric in every slot. `right_root`: symmetric in every slot. `small_second`: positive.
All inputs are finite; a program needn't handle non-finite values.
Results may differ from the reference program's by a relative error of at most 0.014.
The reference program's roundings to bfloat16 on the way count: a program that leaves them out, or rounds other values in their place, can miss the bound.
Values may be sent and summed in bfloat16 or wider, within the bound.
A program may use at most 320 MiB of HBM per device.

```python
import math
import jax
import jax.numpy as jnp
from jax import lax

D = 768
HEADS = 12
FF = 3072
SD = 128
PH = 2
NCLS = 14
BLK = 128
LEN_A = 128
LEN_B = 512
STEP = 10
SEQ_A = 256
SEQ_B = 64
NBLK = 439
SLOT_ALL = 440
SMALL = 11406


def slot_table(key):
    empty_count = SLOT_ALL - NBLK
    inner = jax.random.permutation(jax.random.fold_in(key, 101), SLOT_ALL - 2) + 1
    marks = jnp.zeros((SLOT_ALL,), jnp.int32).at[inner[:empty_count]].set(1)
    used = jnp.argsort(marks, stable=True)[:NBLK]
    order = jax.random.permutation(jax.random.fold_in(key, 102), NBLK)
    return used[order].astype(jnp.int32)


def token_grad():
    return 0.5 * math.sqrt(SEQ_A * LEN_A + SEQ_B * LEN_B)


def sequence_grad():
    return 0.5 * math.sqrt(SEQ_A + SEQ_B)


def class_cotangent(key, row_count, offset_size, noise_bound):
    noise = jnp.clip(jax.random.normal(jax.random.fold_in(key, 1), (row_count, NCLS), jnp.float32), -noise_bound, noise_bound)
    offsets = jax.random.uniform(jax.random.fold_in(key, 2), (NCLS,), jnp.float32, -1.0, 1.0)
    return offset_size * offsets[None, :] + noise


def draw_logit_cot_short(key, part):
    key = jax.random.fold_in(key, 61)
    return class_cotangent(key, SEQ_A, 0.5, 5.5)


def draw_logit_cot_long(key, part):
    key = jax.random.fold_in(key, 62)
    return class_cotangent(key, SEQ_B, 0.5, 5.5)


def draw_block_slot(key, part):
    return slot_table(key)


def draw_master(key, part):
    table = slot_table(key)
    key = jax.random.fold_in(key, 3)
    block_index = jnp.arange(NBLK)
    square = (D // BLK) ** 2
    wide = D // BLK * (FF // BLK)
    student_count = D // BLK * (SD // BLK)
    scales = jnp.where(block_index < 3 * square, D ** (-0.5), jnp.where(block_index < 4 * square, (D // 16) ** (-0.5), jnp.where(block_index < 4 * square + wide, D ** (-0.5), jnp.where(block_index < 4 * square + 2 * wide, FF ** (-0.5), jnp.where(block_index < 4 * square + 2 * wide + student_count, D ** (-0.5), SD ** (-0.5))))))
    slot_scale = jnp.full((SLOT_ALL,), D ** (-0.5), jnp.float32).at[table].set(scales.astype(jnp.float32))
    return jax.random.normal(key, (SLOT_ALL, BLK, BLK), jnp.float32) * slot_scale[:, None, None]


def symmetric_draw(key, diag_power, diag_base, off_size):
    diag_key = jax.random.fold_in(key, 11)
    off_key = jax.random.fold_in(key, 12)
    spread = jnp.exp(jax.random.uniform(diag_key, (SLOT_ALL, BLK), jnp.float32, 0.0, math.log(4.0)))
    noise = jax.random.normal(off_key, (SLOT_ALL, BLK, BLK), jnp.float32)
    noise = 0.5 * (noise + jnp.swapaxes(noise, 1, 2))
    places = jnp.arange(BLK)
    identity = (places[:, None] == places[None, :]).astype(jnp.float32)
    diagonal = diag_base * spread ** diag_power
    return diagonal[:, :, None] * identity[None] + off_size * noise * (1.0 - identity[None])


def draw_left_stat(key, part):
    key = jax.random.fold_in(key, 21)
    base = BLK * token_grad() ** 2
    return symmetric_draw(key, 1.0, base, 0.3 * base / math.sqrt(BLK))


def draw_right_stat(key, part):
    key = jax.random.fold_in(key, 22)
    base = BLK * token_grad() ** 2
    return symmetric_draw(key, 1.0, base, 0.3 * base / math.sqrt(BLK))


def draw_left_root(key, part):
    key = jax.random.fold_in(key, 23)
    base = (BLK * token_grad() ** 2) ** (-0.25)
    return symmetric_draw(key, -0.5, base, 0.05 * base)


def draw_right_root(key, part):
    key = jax.random.fold_in(key, 24)
    base = (BLK * token_grad() ** 2) ** (-0.25)
    return symmetric_draw(key, -0.5, base, 0.05 * base)


def draw_small_params(key, part):
    key = jax.random.fold_in(key, 31)
    place = jnp.arange(SMALL)
    normal = jax.random.normal(key, (SMALL,), jnp.float32)
    gains = 1.0 + 0.3 * jax.random.uniform(jax.random.fold_in(key, 1), (SMALL,), jnp.float32, -1.0, 1.0)
    head_start = 8 * D + FF
    is_gain = (place >= 3 * D) & (place < 4 * D) | (place >= 6 * D + FF) & (place < 7 * D + FF)
    is_query = (place >= head_start + SD) & (place < head_start + 2 * SD)
    is_class = (place >= head_start + 3 * SD) & (place < head_start + 3 * SD + SD * NCLS)
    scale = jnp.where(is_query, 2.0, jnp.where(is_class, SD ** (-0.5), 0.1))
    return jnp.where(is_gain, gains, normal * scale)


def segment_scale():
    place = jnp.arange(SMALL)
    return jnp.where(place < 8 * D + FF, token_grad(), sequence_grad()).astype(jnp.float32)


def draw_small_first(key, part):
    key = jax.random.fold_in(key, 41)
    return jax.random.normal(key, (SMALL,), jnp.float32) * 0.11 * segment_scale()


def draw_small_second(key, part):
    key = jax.random.fold_in(key, 42)
    spread = jnp.exp(jax.random.uniform(key, (SMALL,), jnp.float32, 0.0, math.log(4.0)))
    return 0.001 * spread * segment_scale() ** 2


def draw_len_short(key, part):
    key = jax.random.fold_in(key, 51)
    base = jax.random.randint(key, (SEQ_A,), LEN_A // 2, LEN_A + 1)
    chosen = jax.random.randint(jax.random.fold_in(key, 1), (), 0, SEQ_A)
    return base.at[chosen].set(LEN_A).astype(jnp.int32)


def draw_len_long(key, part):
    key = jax.random.fold_in(key, 52)
    base = jax.random.randint(key, (SEQ_B,), LEN_B // 2, LEN_B + 1)
    chosen = jax.random.randint(jax.random.fold_in(key, 1), (), 0, SEQ_B)
    return base.at[chosen].set(LEN_B).astype(jnp.int32)


def block_scale(rng, dims, cuts, least, top_value):
    def one(position, parts):
        steps = jax.random.uniform(jax.random.fold_in(jax.random.fold_in(rng, 6), position), (parts,), jnp.float32, least / len(cuts), top_value / len(cuts))
        return jnp.repeat(jnp.exp(steps), dims[position] // parts).reshape((-1,) + (1,) * (len(dims) - position - 1))

    gain = one(*cuts[0])
    for cut in cuts[1:]:
        gain = gain * one(*cut)
    return gain


def gaussian(stream_key, shape, scale, bound, cuts=(), held_as=jnp.bfloat16):
    drawn = scale * jax.random.normal(stream_key, shape, jnp.float32)
    if cuts:
        drawn = drawn * block_scale(stream_key, shape, cuts, -0.22, 0.18)
    return jnp.clip(drawn, -bound, bound).astype(held_as)


def setup_inputs(seed: int = 0) -> dict:
    arg_keys = jax.random.split(jax.random.key(seed), 18)
    return {
        "x_short": gaussian(arg_keys[0], (SEQ_A, LEN_A, D), 1.0, 6.0, ((0, 32),)),
        "x_long": gaussian(arg_keys[1], (SEQ_B, LEN_B, D), 1.0, 6.0, ((0, 32),)),
        "cot_short": gaussian(arg_keys[2], (SEQ_A, LEN_A, D), 1.0, 6.0, ((0, 32),)),
        "cot_long": gaussian(arg_keys[3], (SEQ_B, LEN_B, D), 1.0, 6.0, ((0, 32),)),
        "logit_cot_short": draw_logit_cot_short(jax.random.fold_in(arg_keys[17], 71), 0),
        "logit_cot_long": draw_logit_cot_long(jax.random.fold_in(arg_keys[17], 71), 0),
        "len_short": draw_len_short(jax.random.fold_in(arg_keys[17], 71), 0),
        "len_long": draw_len_long(jax.random.fold_in(arg_keys[17], 71), 0),
        "block_slot": draw_block_slot(jax.random.fold_in(arg_keys[17], 71), 0),
        "master": draw_master(jax.random.fold_in(arg_keys[17], 71), 0),
        "left_stat": draw_left_stat(jax.random.fold_in(arg_keys[17], 71), 0),
        "right_stat": draw_right_stat(jax.random.fold_in(arg_keys[17], 71), 0),
        "left_root": draw_left_root(jax.random.fold_in(arg_keys[17], 71), 0),
        "right_root": draw_right_root(jax.random.fold_in(arg_keys[17], 71), 0),
        "small_params": draw_small_params(jax.random.fold_in(arg_keys[17], 71), 0),
        "small_first": draw_small_first(jax.random.fold_in(arg_keys[17], 71), 0),
        "small_second": draw_small_second(jax.random.fold_in(arg_keys[17], 71), 0),
    }


NORM_EPSILON = 1e-12
BETA_ONE = 0.9
BETA_TWO = 0.999
ADAM_EPSILON = 1e-08
ADAM_RATE = 0.1
MATRIX_RATE = 0.2
STAT_DECAY = 0.5
MASKED_SCORE = -1e+30
HIGHEST_PRECISION = lax.Precision.HIGHEST

@jax.custom_vjp
def low(v):
    return lax.optimization_barrier(v.astype(jnp.bfloat16)).astype(jnp.float32)

@jax.custom_vjp
def low_back(v):
    return v

def low_keep(v):
    return (low(v), None)

def low_pass(kept, grad):
    return (grad,)

def back_keep(v):
    return (v, None)

def back_low(kept, grad):
    return (low(grad),)
low.defvjp(low_keep, low_pass)
low_back.defvjp(back_keep, back_low)

def rounded_both(values):
    return low_back(low(values))

def matmul(former, latter):
    return jnp.dot(former, latter, precision=HIGHEST_PRECISION, preferred_element_type=jnp.float32)

def norm_rows(values, gain_vector, shift_vector):
    center = values - lax.optimization_barrier(jnp.mean(values, axis=-1, keepdims=True))
    spread = lax.optimization_barrier(jnp.mean(center * center, axis=-1, keepdims=True))
    return center * lax.rsqrt(spread + NORM_EPSILON) * gain_vector + shift_vector

def softmax_last(scores):
    highest = lax.optimization_barrier(jnp.max(scores, axis=-1, keepdims=True))
    powers = jnp.exp(scores - highest)
    return powers / lax.optimization_barrier(jnp.sum(powers, axis=-1, keepdims=True))

def split_blocks(blocks):
    shapes = ((D, D), (D, D), (D, D), (D, D), (D, FF), (FF, D), (D, SD), (SD, SD))
    matrices = []
    offset = 0
    for row_count, col_count in shapes:
        row_blocks = row_count // BLK
        col_blocks = col_count // BLK
        block_count = row_blocks * col_blocks
        block_piece = blocks[offset:offset + block_count].reshape(row_blocks, col_blocks, BLK, BLK)
        matrices.append(block_piece.transpose(0, 2, 1, 3).reshape(row_count, col_count))
        offset += block_count
    return matrices

def unpack(small_values):
    widths = (D, D, D, D, D, FF, D, D, D, SD, SD, SD, SD * NCLS, NCLS)
    pieces = []
    offset = 0
    for column_count in widths:
        pieces.append(small_values[offset:offset + column_count])
        offset += column_count
    return pieces

def head_tail(student, pool_query, w_hidden, b_hidden, w_class, b_class, visible):
    seq_count, seq_length = visible.shape
    part_width = SD // PH
    head_view = student.reshape(seq_count, seq_length, PH, part_width)
    pool_scores = jnp.einsum('slhe,he->shl', head_view, pool_query.reshape(PH, part_width), precision=HIGHEST_PRECISION) * part_width ** (-0.5)
    pool_scores = jnp.where(visible[:, None, :], pool_scores, MASKED_SCORE)
    pool_weights = softmax_last(pool_scores)
    pooled = jnp.einsum('shl,slhe->she', pool_weights, head_view, precision=HIGHEST_PRECISION)
    hidden = jnp.tanh(matmul(pooled.reshape(seq_count, SD), w_hidden) + b_hidden)
    return matmul(hidden, w_class.reshape(SD, NCLS)) + b_class

def group_layer(weights, vectors, inputs, lengths):
    w_query, w_key, w_value, w_out, w_up, w_down, w_student, w_hidden = weights
    b_query, b_value, b_out, gain_one, shift_one, b_up, b_down, gain_two, shift_two, b_student, pool_query, b_hidden, w_class, b_class = vectors
    seq_count, seq_length = (inputs.shape[0], inputs.shape[1])
    head_shape = (seq_count, seq_length, HEADS, D // HEADS)
    token_rows = inputs.reshape(seq_count * seq_length, D)
    queries = rounded_both(matmul(token_rows, w_query) + b_query).reshape(head_shape)
    key_rows = rounded_both(matmul(token_rows, w_key)).reshape(head_shape)
    value_rows = rounded_both(matmul(token_rows, w_value) + b_value).reshape(head_shape)
    scores = jnp.einsum('sqhd,skhd->shqk', queries, key_rows, precision=HIGHEST_PRECISION) * (D // HEADS) ** (-0.5)
    scores = low_back(scores)
    visible = jnp.arange(seq_length)[None, :] < lengths[:, None]
    scores = jnp.where(visible[:, None, None, :], scores, MASKED_SCORE)
    probs = low(softmax_last(scores))
    context = jnp.einsum('shqk,skhd->sqhd', probs, value_rows, precision=HIGHEST_PRECISION)
    context = rounded_both(context.reshape(seq_count * seq_length, D))
    branch = low_back(matmul(context, w_out) + b_out)
    first = low(norm_rows(token_rows + branch, gain_one, shift_one))
    upward = low_back(matmul(first, w_up) + b_up)
    active = low(jax.nn.gelu(upward, approximate=False))
    downward = low_back(matmul(active, w_down) + b_down)
    second = norm_rows(first + downward, gain_two, shift_two)
    student = low_back(matmul(low(second), w_student) + b_student)
    logits = head_tail(student, pool_query, w_hidden, b_hidden, w_class, b_class, visible)
    return (second.reshape(seq_count, seq_length, D), logits)

def run_batch(weights, vectors, inputs, lengths):
    seq_count, seq_length = (inputs.shape[0], inputs.shape[1])
    per_group = math.gcd(seq_count, max(1, 4096 // seq_length))
    grouped = inputs.reshape(seq_count // per_group, per_group, seq_length, D)
    length_groups = lengths.reshape(seq_count // per_group, per_group)

    def group_step(couple):
        return group_layer(weights, vectors, couple[0], couple[1])
    encoded, logits = lax.map(jax.checkpoint(group_step), (grouped, length_groups))
    return (encoded.reshape(seq_count, seq_length, D), logits.reshape(seq_count, NCLS))

def reference(x_short, x_long, cot_short, cot_long, logit_cot_short, logit_cot_long, len_short, len_long, block_slot, master, left_stat, right_stat, left_root, right_root, small_params, small_first, small_second):
    slot_values = low(master)

    def forward(slot_weights, small_values, inputs_short, inputs_long):
        weights = split_blocks(jnp.take(slot_weights, block_slot, axis=0))
        vectors = unpack(small_values)
        encoded_short, logits_short = run_batch(weights, vectors, inputs_short, len_short)
        encoded_long, logits_long = run_batch(weights, vectors, inputs_long, len_long)
        return (encoded_short, logits_short, encoded_long, logits_long)
    outputs, pullback = jax.vjp(forward, slot_values, small_params, x_short.astype(jnp.float32), x_long.astype(jnp.float32))
    slot_grad, small_grad, grad_short, grad_long = pullback((cot_short.astype(jnp.float32), logit_cot_short, cot_long.astype(jnp.float32), logit_cot_long))
    encoded_short, logits_short, encoded_long, logits_long = outputs
    outer_left = jnp.einsum('sij,skj->sik', slot_grad, slot_grad, precision=HIGHEST_PRECISION)
    outer_right = jnp.einsum('sji,sjk->sik', slot_grad, slot_grad, precision=HIGHEST_PRECISION)
    new_left = STAT_DECAY * left_stat + (1.0 - STAT_DECAY) * outer_left
    new_right = STAT_DECAY * right_stat + (1.0 - STAT_DECAY) * outer_right
    left_applied = jnp.einsum('sij,sjk->sik', left_root, slot_grad, precision=HIGHEST_PRECISION)
    conditioned = jnp.einsum('sij,sjk->sik', left_applied, right_root, precision=HIGHEST_PRECISION)
    new_master = master - MATRIX_RATE * conditioned
    new_first = BETA_ONE * small_first + (1.0 - BETA_ONE) * small_grad
    new_second = BETA_TWO * small_second + (1.0 - BETA_TWO) * small_grad * small_grad
    first_hat = new_first / (1.0 - BETA_ONE ** STEP)
    second_hat = new_second / (1.0 - BETA_TWO ** STEP)
    new_small = small_params - ADAM_RATE * first_hat / (jnp.sqrt(second_hat) + ADAM_EPSILON)
    return (encoded_short.astype(jnp.bfloat16), logits_short, encoded_long.astype(jnp.bfloat16), logits_long, grad_short, grad_long, slot_grad, new_left, new_right, new_master, new_first, new_second, new_small)
```

```python
from functools import partial

import jax
import jax.numpy as jnp
from jax import lax
from jax.experimental import pallas as pl
from jax.experimental.pallas import tpu as pltpu
from jax.sharding import PartitionSpec as P

D = 768
HEADS = 12
FF = 3072
SD = 128
PH = 2
NCLS = 14
BLK = 128
STEP = 10
NBLK = 439
TILE = 512
PAIRS = 3
GROUPS = 2
CHUNK = 768

NORM_EPSILON = 1e-12
BETA_ONE = 0.9
BETA_TWO = 0.999
ADAM_EPSILON = 1e-08
ADAM_RATE = 0.1
MATRIX_RATE = 0.2
STAT_DECAY = 0.5
MASKED_SCORE = -1e30
HIGHEST_PRECISION = lax.Precision.HIGHEST
MIB = 1024 * 1024
F32 = jnp.float32
BF16 = jnp.bfloat16

PLACES = (
    (0, 6, 6, 0, 0),
    (36, 6, 6, 0, 6),
    (72, 6, 6, 0, 12),
    (108, 6, 6, 1, 0),
    (144, 6, 24, 2, 0),
    (288, 24, 6, 3, 0),
    (432, 6, 1, 4, 0),
    (438, 1, 1, 5, 0),
)


def product(former, latter, precision=None):
    return jnp.dot(former, latter, preferred_element_type=F32, precision=precision)


def left_product(former, latter, precision=None):
    return lax.dot_general(
        former, latter, (((0,), (0,)), ((), ())), preferred_element_type=F32, precision=precision
    )


def right_product(former, latter, precision=None):
    return lax.dot_general(
        former, latter, (((1,), (1,)), ((), ())), preferred_element_type=F32, precision=precision
    )


def unpack(small_values):
    widths = (D, D, D, D, D, FF, D, D, D, SD, SD, SD, SD * NCLS, NCLS)
    pieces = []
    offset = 0
    for column_count in widths:
        pieces.append(small_values[offset : offset + column_count])
        offset += column_count
    return pieces


def inverse_of(values):
    guess = pl.reciprocal(values, approx=True)
    return guess * (2.0 - values * guess)


def assemble_kernel(slot_ref, blocks, *refs):
    outs, sems = refs[:-1], refs[-1]
    for first, row_count, col_count, which, col_start in PLACES:

        def move(index, carry, first=first, col_count=col_count, which=which, col_start=col_start):
            row = pl.multiple_of((index // col_count) * BLK, BLK)
            col = pl.multiple_of((index % col_count + col_start) * BLK, BLK)
            pltpu.make_async_copy(
                blocks.at[slot_ref[first + index]],
                outs[which].at[pl.ds(row, BLK), pl.ds(col, BLK)],
                sems.at[which],
            ).start()
            return carry

        lax.fori_loop(0, row_count * col_count, move, 0)
    for which, out in enumerate(outs):
        pltpu.make_async_copy(out, out, sems.at[which]).wait()


def assemble(block_slot, blocks):
    shapes = ((D, 3 * D), (D, D), (D, FF), (FF, D), (D, SD), (SD, SD))
    return pl.pallas_call(
        assemble_kernel,
        grid_spec=pltpu.PrefetchScalarGridSpec(
            num_scalar_prefetch=1,
            grid=(1,),
            in_specs=[pl.BlockSpec(memory_space=pl.ANY)],
            out_specs=[pl.BlockSpec(memory_space=pl.ANY)] * len(shapes),
            scratch_shapes=[pltpu.SemaphoreType.DMA((len(shapes),))],
        ),
        out_shape=[jax.ShapeDtypeStruct(shape, BF16) for shape in shapes],
        name="assemble",
    )(block_slot, blocks)


SOURCES = (
    (0, 6, 6),
    (36, 6, 6),
    (72, 6, 6),
    (108, 6, 6),
    (144, 6, 24),
    (288, 24, 6),
    (432, 6, 1),
    (438, 1, 1),
)


def spread_kernel(slot_ref, empty_ref, *refs):
    grads, zero, out, sem = refs[:-3], refs[-3], refs[-2], refs[-1]
    for grad, (first, row_count, col_count) in zip(grads, SOURCES):

        def move(index, carry, grad=grad, first=first, col_count=col_count):
            row = pl.multiple_of((index // col_count) * BLK, BLK)
            col = pl.multiple_of((index % col_count) * BLK, BLK)
            pltpu.make_async_copy(
                grad.at[pl.ds(row, BLK), pl.ds(col, BLK)],
                out.at[slot_ref[first + index]],
                sem,
            ).start()
            return carry

        lax.fori_loop(0, row_count * col_count, move, 0)
    for index in range(empty_ref.shape[0]):
        pltpu.make_async_copy(zero, out.at[empty_ref[index]], sem).start()
    pltpu.make_async_copy(out, out, sem).wait()


def spread(block_slot, empty, grads, slot_count):
    return pl.pallas_call(
        spread_kernel,
        grid_spec=pltpu.PrefetchScalarGridSpec(
            num_scalar_prefetch=2,
            grid=(1,),
            in_specs=[pl.BlockSpec(memory_space=pl.ANY)] * (len(grads) + 1),
            out_specs=pl.BlockSpec(memory_space=pl.ANY),
            scratch_shapes=[pltpu.SemaphoreType.DMA],
        ),
        out_shape=jax.ShapeDtypeStruct((slot_count, BLK, BLK), BF16),
        name="spread",
    )(block_slot, empty, *grads, jnp.zeros((BLK, BLK), BF16))


def half_masks():
    lane = lax.broadcasted_iota(jnp.int32, (1, BLK), 1)
    low = (lane < BLK // 2).astype(BF16)
    return low, (1.0 - low.astype(F32)).astype(BF16)


def stack_heads(values, low, high):
    return jnp.concatenate([values * low, values * high], axis=0)


def pick_heads(values):
    rows = values.shape[0] // 2
    lane = lax.broadcasted_iota(jnp.int32, (rows, BLK), 1)
    return jnp.where(lane < BLK // 2, values[:rows], values[rows:])


def attend(queries, key_rows, value_rows, length, low, high):
    scores = right_product(stack_heads(queries, low, high), key_rows)
    place = lax.broadcasted_iota(jnp.int32, scores.shape, 1)
    scores = jnp.where(place < length, scores, MASKED_SCORE)
    powers = jnp.exp(scores - jnp.max(scores, axis=-1, keepdims=True))
    total = jnp.sum(powers, axis=-1, keepdims=True)
    probs = (powers * (1.0 / total)).astype(BF16)
    return probs, pick_heads(product(probs, value_rows)).astype(BF16)


def attention_kernel(
    len_short, len_long, q_ref, k_ref, v_ref, context_ref, short_ref, long_ref, *, short_tiles
):
    tile = pl.program_id(0)
    low, high = half_masks()
    per_tile = TILE // short_ref.shape[-1]
    width = short_ref.shape[-1]

    @pl.when(tile < short_tiles)
    def _():
        for pair in range(PAIRS):
            cols = slice(pair * BLK, (pair + 1) * BLK)
            for seq in range(per_tile):
                rows = slice(seq * width, (seq + 1) * width)
                probs, context = attend(
                    q_ref[rows, cols],
                    k_ref[rows, cols],
                    v_ref[rows, cols],
                    len_short[tile * per_tile + seq],
                    low,
                    high,
                )
                short_ref[0, pair, seq] = probs
                context_ref[rows, cols] = context

    @pl.when(tile >= short_tiles)
    def _():
        length = len_long[tile - short_tiles]
        half = TILE // 2
        for pair in range(PAIRS):
            cols = slice(pair * BLK, (pair + 1) * BLK)
            for part in range(2):
                rows = slice(part * half, (part + 1) * half)
                probs, context = attend(
                    q_ref[rows, cols], k_ref[:, cols], v_ref[:, cols], length, low, high
                )
                long_ref[0, pair, part] = probs
                context_ref[rows, cols] = context


def probs_shapes(short_tiles, long_tiles, width):
    per_tile = TILE // width
    return (
        (short_tiles, 2 * PAIRS, per_tile, 2 * width, width),
        (long_tiles, 2 * PAIRS, 2, TILE, TILE),
    )


def short_index(tile, short_tiles):
    return jnp.minimum(tile, short_tiles - 1)


def long_index(tile, short_tiles):
    return jnp.maximum(tile - short_tiles, 0)


def attention(len_short, len_long, qkv, short_tiles, width):
    tiles = qkv.shape[0] // TILE
    wide = PAIRS * BLK
    short_shape, long_shape = probs_shapes(short_tiles, tiles - short_tiles, width)

    def short_map(tile, group, *_):
        return (short_index(tile, short_tiles), jnp.where(tile < short_tiles, group, GROUPS - 1), 0, 0, 0)

    def long_map(tile, group, *_):
        return (long_index(tile, short_tiles), jnp.where(tile < short_tiles, 0, group), 0, 0, 0)

    flops = 4 * D * TILE * TILE * tiles
    return pl.pallas_call(
        partial(attention_kernel, short_tiles=short_tiles),
        grid_spec=pltpu.PrefetchScalarGridSpec(
            num_scalar_prefetch=2,
            grid=(tiles, GROUPS),
            in_specs=[
                pl.BlockSpec((TILE, wide), lambda tile, group, *_: (tile, group)),
                pl.BlockSpec((TILE, wide), lambda tile, group, *_: (tile, GROUPS + group)),
                pl.BlockSpec((TILE, wide), lambda tile, group, *_: (tile, 2 * GROUPS + group)),
            ],
            out_specs=[
                pl.BlockSpec((TILE, wide), lambda tile, group, *_: (tile, group)),
                pl.BlockSpec((1, PAIRS) + short_shape[2:], short_map),
                pl.BlockSpec((1, PAIRS) + long_shape[2:], long_map),
            ],
        ),
        out_shape=[
            jax.ShapeDtypeStruct((tiles * TILE, D), BF16),
            jax.ShapeDtypeStruct(short_shape, BF16),
            jax.ShapeDtypeStruct(long_shape, BF16),
        ],
        compiler_params=pltpu.CompilerParams(vmem_limit_bytes=48 * MIB),
        cost_estimate=pl.CostEstimate(
            flops=flops, bytes_accessed=30 * MIB, transcendentals=HEADS * TILE * TILE * tiles // 2
        ),
        name="attention",
    )(len_short, len_long, qkv, qkv, qkv)


def attend_back(queries, key_rows, value_rows, d_context, probs, low, high):
    stacked = stack_heads(d_context, low, high)
    d_probs = right_product(stacked, value_rows)
    wide = probs.astype(F32)
    weighted = wide * d_probs
    d_scores = (weighted - wide * jnp.sum(weighted, axis=-1, keepdims=True)).astype(BF16)
    d_queries = pick_heads(product(d_scores, key_rows)) * 0.125
    d_keys = left_product(d_scores, stack_heads(queries, low, high))
    d_values = left_product(probs, stacked)
    return d_queries.astype(BF16), d_keys, d_values


def attention_back_kernel(
    q_ref,
    k_ref,
    v_ref,
    short_ref,
    long_ref,
    dc_ref,
    resid_ref,
    w_ref,
    dq_ref,
    dk_ref,
    dv_ref,
    in_short_ref,
    in_long_ref,
    bq_ref,
    bv_ref,
    *,
    short_tiles,
):
    tile = pl.program_id(0)
    group = pl.program_id(1)
    low, high = half_masks()
    width = short_ref.shape[-1]
    per_tile = TILE // width

    @pl.when(tile < short_tiles)
    def _():
        for pair in range(PAIRS):
            cols = slice(pair * BLK, (pair + 1) * BLK)
            for seq in range(per_tile):
                rows = slice(seq * width, (seq + 1) * width)
                d_queries, d_keys, d_values = attend_back(
                    q_ref[rows, cols],
                    k_ref[rows, cols],
                    v_ref[rows, cols],
                    dc_ref[rows, cols],
                    short_ref[0, pair, seq],
                    low,
                    high,
                )
                dq_ref[rows, cols] = d_queries
                dk_ref[rows, cols] = d_keys.astype(BF16)
                dv_ref[rows, cols] = d_values.astype(BF16)

    @pl.when(tile >= short_tiles)
    def _():
        half = TILE // 2
        for pair in range(PAIRS):
            cols = slice(pair * BLK, (pair + 1) * BLK)
            keys_sum = None
            values_sum = None
            for part in range(2):
                rows = slice(part * half, (part + 1) * half)
                d_queries, d_keys, d_values = attend_back(
                    q_ref[rows, cols],
                    k_ref[:, cols],
                    v_ref[:, cols],
                    dc_ref[rows, cols],
                    long_ref[0, pair, part],
                    low,
                    high,
                )
                dq_ref[rows, cols] = d_queries
                keys_sum = d_keys if keys_sum is None else keys_sum + d_keys
                values_sum = d_values if values_sum is None else values_sum + d_values
            dk_ref[:, cols] = keys_sum.astype(BF16)
            dv_ref[:, cols] = values_sum.astype(BF16)

    wide = PAIRS * BLK
    start = pl.multiple_of(group * wide, wide)

    @pl.when((tile == 0) & (group == 0))
    def _():
        bq_ref[...] = jnp.zeros_like(bq_ref)
        bv_ref[...] = jnp.zeros_like(bv_ref)

    bq_ref[:, pl.ds(start, wide)] += jnp.sum(dq_ref[...].astype(F32), axis=0, keepdims=True)
    bv_ref[:, pl.ds(start, wide)] += jnp.sum(dv_ref[...].astype(F32), axis=0, keepdims=True)
    total = (
        right_product(dq_ref[...], w_ref[:, pl.ds(start, wide)])
        + right_product(dk_ref[...], w_ref[:, pl.ds(D + start, wide)])
        + right_product(dv_ref[...], w_ref[:, pl.ds(2 * D + start, wide)])
    )

    @pl.when((tile < short_tiles) & (group == 0))
    def _():
        in_short_ref[...] = resid_ref[...] + total

    @pl.when((tile < short_tiles) & (group > 0))
    def _():
        in_short_ref[...] += total

    @pl.when((tile >= short_tiles) & (group == 0))
    def _():
        in_long_ref[...] = resid_ref[...] + total

    @pl.when((tile >= short_tiles) & (group > 0))
    def _():
        in_long_ref[...] += total


def attention_back(qkv, probs_short, probs_long, d_context, resid, w_qkv, short_tiles):
    tiles = qkv.shape[0] // TILE
    wide = PAIRS * BLK

    def short_map(tile, group, *_):
        return (short_index(tile, short_tiles), jnp.where(tile < short_tiles, group, GROUPS - 1), 0, 0, 0)

    def long_map(tile, group, *_):
        return (long_index(tile, short_tiles), jnp.where(tile < short_tiles, 0, group), 0, 0, 0)

    def part(offset):
        return pl.BlockSpec((TILE, wide), lambda tile, group: (tile, offset * GROUPS + group))

    row = pl.BlockSpec((1, D), lambda tile, group: (0, 0))
    flops = 10 * D * TILE * TILE * tiles + 6 * D * D * TILE * tiles
    return pl.pallas_call(
        partial(attention_back_kernel, short_tiles=short_tiles),
        grid=(tiles, GROUPS),
        in_specs=[
            part(0),
            part(1),
            part(2),
            pl.BlockSpec((1, PAIRS) + probs_short.shape[2:], short_map),
            pl.BlockSpec((1, PAIRS) + probs_long.shape[2:], long_map),
            part(0),
            pl.BlockSpec((TILE, D), lambda tile, group: (tile, 0)),
            pl.BlockSpec((D, 3 * D), lambda tile, group: (0, 0), pipeline_mode=pl.Buffered(1)),
        ],
        out_specs=[
            part(0),
            part(0),
            part(0),
            pl.BlockSpec((TILE, D), lambda tile, group: (short_index(tile, short_tiles), 0)),
            pl.BlockSpec((TILE, D), lambda tile, group: (long_index(tile, short_tiles), 0)),
            row,
            row,
        ],
        out_shape=[
            jax.ShapeDtypeStruct((tiles * TILE, D), BF16),
            jax.ShapeDtypeStruct((tiles * TILE, D), BF16),
            jax.ShapeDtypeStruct((tiles * TILE, D), BF16),
            jax.ShapeDtypeStruct((short_tiles * TILE, D), F32),
            jax.ShapeDtypeStruct(((tiles - short_tiles) * TILE, D), F32),
            jax.ShapeDtypeStruct((1, D), F32),
            jax.ShapeDtypeStruct((1, D), F32),
        ],
        compiler_params=pltpu.CompilerParams(vmem_limit_bytes=56 * MIB),
        cost_estimate=pl.CostEstimate(flops=flops, bytes_accessed=50 * MIB, transcendentals=0),
        name="attention_back",
    )(qkv, qkv, qkv, probs_short, probs_long, d_context, resid, w_qkv)


def normal_parts(values):
    size = jnp.abs(values)
    power = jnp.exp(-0.5 * values * values)
    step = inverse_of(1.0 + (0.3275911 * 0.7071067811865476) * size)
    tail = 0.5 * 1.061405429
    for coefficient in (-1.453152027, 1.421413741, -0.284496736, 0.254829592):
        tail = tail * step + 0.5 * coefficient
    tail = tail * step * power
    return jnp.where(values >= 0.0, 1.0 - tail, tail), power * 0.3989422804014327


def norm_parts(values):
    center = values - jnp.mean(values, axis=-1, keepdims=True)
    spread = jnp.mean(center * center, axis=-1, keepdims=True)
    inverse = lax.rsqrt(spread + NORM_EPSILON)
    return center * inverse, inverse


def norm_back(d_values, gain, unit, inverse):
    d_unit = d_values * gain
    return inverse * (
        d_unit
        - jnp.mean(d_unit, axis=-1, keepdims=True)
        - unit * jnp.mean(d_unit * unit, axis=-1, keepdims=True)
    )


def column_sum(values):
    return jnp.sum(values.astype(F32), axis=0, keepdims=True)


def pool_weights(student, query, length):
    scaled = student * query
    lane = lax.broadcasted_iota(jnp.int32, scaled.shape, 1)
    place = lax.broadcasted_iota(jnp.int32, (scaled.shape[0], 1), 0)
    weights = []
    for side in (lane < SD // PH, lane >= SD // PH):
        scores = jnp.sum(jnp.where(side, scaled, 0.0), axis=-1, keepdims=True)
        scores = jnp.where(place < length, scores, MASKED_SCORE)
        powers = jnp.exp(scores - jnp.max(scores, axis=0, keepdims=True))
        weights.append(powers / jnp.sum(powers, axis=0, keepdims=True))
    return jnp.where(lane < SD // PH, weights[0], weights[1]), weights


def student_back(student, query, weights, both, d_pooled):
    lane = lax.broadcasted_iota(jnp.int32, student.shape, 1)
    moved = student * d_pooled
    d_scores = []
    for side, weight in zip((lane < SD // PH, lane >= SD // PH), weights):
        d_weight = jnp.sum(jnp.where(side, moved, 0.0), axis=-1, keepdims=True)
        d_scores.append(weight * (d_weight - jnp.sum(weight * d_weight, axis=0, keepdims=True)))
    d_score = jnp.where(lane < SD // PH, d_scores[0], d_scores[1])
    d_query = jnp.sum(d_score * student, axis=0, keepdims=True) * 0.125
    return both * d_pooled + d_score * query, d_query


def feed_kernel(
    len_short,
    len_long,
    x_ref,
    context_ref,
    cot_short_ref,
    cot_long_ref,
    logit_cot_ref,
    b_out,
    gain_one,
    shift_one,
    b_up,
    b_down,
    gain_two,
    shift_two,
    b_student,
    pool_query,
    b_hidden,
    w_class,
    b_class,
    w_out,
    w_up,
    w_down,
    w_student,
    w_hidden,
    enc_short_ref,
    enc_long_ref,
    logit_ref,
    first_ref,
    active_ref,
    d_up_ref,
    d_down_ref,
    d_branch_ref,
    d_context_ref,
    d_resid_ref,
    g_student,
    g_hidden,
    g_b_out,
    g_gain_one,
    g_shift_one,
    g_b_up,
    g_b_down,
    g_gain_two,
    g_shift_two,
    g_b_student,
    g_pool_query,
    g_b_hidden,
    g_w_class,
    g_b_class,
    slope,
    pooled_ref,
    d_student_ref,
    *,
    short_tiles,
    width,
):
    tile = pl.program_id(0)
    per_tile = TILE // width

    @pl.when(tile == 0)
    def _():
        for ref in (
            g_student,
            g_hidden,
            g_b_out,
            g_gain_one,
            g_shift_one,
            g_b_up,
            g_b_down,
            g_gain_two,
            g_shift_two,
            g_b_student,
            g_pool_query,
            g_b_hidden,
            g_w_class,
            g_b_class,
        ):
            ref[...] = jnp.zeros_like(ref)

    branch = product(context_ref[...], w_out[...]) + b_out[...]
    unit_one, inverse_one = norm_parts(x_ref[...].astype(F32) + branch)
    first = (unit_one * gain_one[...] + shift_one[...]).astype(BF16)
    first_ref[...] = first
    for start in range(0, FF, CHUNK):
        cols = slice(start, start + CHUNK)
        upward = product(first, w_up[:, cols]) + b_up[:, cols]
        below, density = normal_parts(upward)
        active_ref[:, cols] = (upward * below).astype(BF16)
        slope[:, cols] = (below + upward * density).astype(BF16)
    downward = product(active_ref[...], w_down[...]) + b_down[...]
    unit_two, inverse_two = norm_parts(first.astype(F32) + downward)
    encoded = (unit_two * gain_two[...] + shift_two[...]).astype(BF16)

    @pl.when(tile < short_tiles)
    def _():
        enc_short_ref[...] = encoded

    @pl.when(tile >= short_tiles)
    def _():
        enc_long_ref[...] = encoded

    student = product(encoded, w_student[...]) + b_student[...]
    query = pool_query[...] * 0.125
    pooled_ref[...] = jnp.zeros_like(pooled_ref)

    def head():
        pooled = pooled_ref[...]
        wide_hidden = w_hidden[...].astype(F32)
        hidden = jnp.tanh(product(pooled, wide_hidden, HIGHEST_PRECISION) + b_hidden[...])
        logit_ref[0] = product(hidden, w_class[...], HIGHEST_PRECISION) + b_class[...]
        d_logits = logit_cot_ref[0]
        g_b_class[...] += column_sum(d_logits)
        g_w_class[...] += left_product(hidden, d_logits, HIGHEST_PRECISION)
        d_hidden = right_product(d_logits, w_class[...], HIGHEST_PRECISION)
        d_hidden = d_hidden * (1.0 - hidden * hidden)
        g_b_hidden[...] += column_sum(d_hidden)
        g_hidden[...] += left_product(pooled, d_hidden, HIGHEST_PRECISION)
        return right_product(d_hidden, wide_hidden, HIGHEST_PRECISION)

    def pool(starts, size, lengths):
        kept = []
        for index, (start, length) in enumerate(zip(starts, lengths)):
            rows = student[start : start + size]
            both, weights = pool_weights(rows, query, length)
            pooled_ref[index : index + 1, :] = column_sum(both * rows)
            kept.append((start, rows, both, weights))
        d_pooled = head()
        for index, (start, rows, both, weights) in enumerate(kept):
            d_rows, d_query = student_back(rows, query, weights, both, d_pooled[index : index + 1])
            d_student_ref[start : start + size, :] = d_rows.astype(BF16)
            g_pool_query[...] += d_query

    @pl.when(tile < short_tiles)
    def _():
        pool(
            [seq * width for seq in range(per_tile)],
            width,
            [len_short[tile * per_tile + seq] for seq in range(per_tile)],
        )

    @pl.when(tile >= short_tiles)
    def _():
        pool([0], TILE, [len_long[tile - short_tiles]])

    d_student = d_student_ref[...]
    g_b_student[...] += column_sum(d_student)
    g_student[...] += left_product(encoded, d_student)
    cotangent = jnp.where(tile < short_tiles, cot_short_ref[...], cot_long_ref[...])
    d_second = cotangent.astype(F32) + right_product(d_student, w_student[...])
    g_gain_two[...] += column_sum(d_second * unit_two)
    g_shift_two[...] += column_sum(d_second)
    d_resid_two = norm_back(d_second, gain_two[...], unit_two, inverse_two)
    d_down = d_resid_two.astype(BF16)
    d_down_ref[...] = d_down
    g_b_down[...] += column_sum(d_down)
    for start in range(0, FF, CHUNK):
        cols = slice(start, start + CHUNK)
        d_active = right_product(d_down, w_down[cols, :])
        d_up = (d_active * slope[:, cols].astype(F32)).astype(BF16)
        d_up_ref[:, cols] = d_up
        g_b_up[:, cols] += column_sum(d_up)
    d_first = d_resid_two + right_product(d_up_ref[...], w_up[...])
    g_gain_one[...] += column_sum(d_first * unit_one)
    g_shift_one[...] += column_sum(d_first)
    d_resid_one = norm_back(d_first, gain_one[...], unit_one, inverse_one)
    d_resid_ref[...] = d_resid_one
    d_branch = d_resid_one.astype(BF16)
    d_branch_ref[...] = d_branch
    g_b_out[...] += column_sum(d_branch)
    d_context_ref[...] = right_product(d_branch, w_out[...]).astype(BF16)


def feed(len_short, len_long, x, context, cot_short, cot_long, logit_cot, vectors, weights, short_tiles, width):
    tiles = x.shape[0] // TILE
    long_tiles = tiles - short_tiles

    def whole(shape):
        return pl.BlockSpec(shape, lambda tile, *_: (0,) * len(shape), pipeline_mode=pl.Buffered(1))

    def kept(shape):
        return pl.BlockSpec(shape, lambda tile, *_: (0,) * len(shape))

    def rows(columns):
        return pl.BlockSpec((TILE, columns), lambda tile, *_: (tile, 0))

    short_rows = pl.BlockSpec((TILE, D), lambda tile, *_: (short_index(tile, short_tiles), 0))
    long_rows = pl.BlockSpec((TILE, D), lambda tile, *_: (long_index(tile, short_tiles), 0))
    logit_rows = pl.BlockSpec((1, 8, SD), lambda tile, *_: (tile, 0, 0))
    grad_shapes = (
        (D, SD),
        (SD, SD),
        (1, D),
        (1, D),
        (1, D),
        (1, FF),
        (1, D),
        (1, D),
        (1, D),
        (1, SD),
        (1, SD),
        (1, SD),
        (SD, SD),
        (1, SD),
    )
    total = tiles * TILE
    return pl.pallas_call(
        partial(feed_kernel, short_tiles=short_tiles, width=width),
        grid_spec=pltpu.PrefetchScalarGridSpec(
            num_scalar_prefetch=2,
            grid=(tiles,),
            in_specs=[rows(D), rows(D), short_rows, long_rows, logit_rows]
            + [whole(vector.shape) for vector in vectors]
            + [whole(weight.shape) for weight in weights],
            out_specs=[
                short_rows,
                long_rows,
                logit_rows,
                rows(D),
                rows(FF),
                rows(FF),
                rows(D),
                rows(D),
                rows(D),
                rows(D),
            ]
            + [kept(shape) for shape in grad_shapes],
            scratch_shapes=[
                pltpu.VMEM((TILE, FF), BF16),
                pltpu.VMEM((8, SD), F32),
                pltpu.VMEM((TILE, SD), BF16),
            ],
        ),
        out_shape=[
            jax.ShapeDtypeStruct((short_tiles * TILE, D), BF16),
            jax.ShapeDtypeStruct((long_tiles * TILE, D), BF16),
            jax.ShapeDtypeStruct((tiles, 8, SD), F32),
            jax.ShapeDtypeStruct((total, D), BF16),
            jax.ShapeDtypeStruct((total, FF), BF16),
            jax.ShapeDtypeStruct((total, FF), BF16),
            jax.ShapeDtypeStruct((total, D), BF16),
            jax.ShapeDtypeStruct((total, D), BF16),
            jax.ShapeDtypeStruct((total, D), BF16),
            jax.ShapeDtypeStruct((total, D), F32),
        ]
        + [jax.ShapeDtypeStruct(shape, F32) for shape in grad_shapes],
        compiler_params=pltpu.CompilerParams(vmem_limit_bytes=60 * MIB),
        cost_estimate=pl.CostEstimate(
            flops=total * (8 * D * FF + 4 * D * D), bytes_accessed=70 * MIB, transcendentals=total * FF
        ),
        name="feed",
    )(len_short, len_long, x, context, cot_short, cot_long, logit_cot, *vectors, *weights)


def body(
    x_short,
    x_long,
    cot_short,
    cot_long,
    logit_cot_short,
    logit_cot_long,
    len_short,
    len_long,
    block_slot,
    master,
    left_stat,
    right_stat,
    left_root,
    right_root,
    small_params,
    small_first,
    small_second,
):
    slot_count = master.shape[0]
    all_slots = slot_count * lax.axis_size("fsdp")
    short_seqs, width = x_short.shape[:2]
    long_seqs = x_long.shape[0]
    short_tiles = short_seqs * width // TILE
    per_tile = TILE // width

    gathered = lax.all_gather(master.astype(BF16), "fsdp", axis=0, tiled=True)
    w_qkv, w_out, w_up, w_down, w_student, w_hidden = assemble(block_slot, gathered)
    (
        b_query,
        b_value,
        b_out,
        gain_one,
        shift_one,
        b_up,
        b_down,
        gain_two,
        shift_two,
        b_student,
        pool_query,
        b_hidden,
        w_class,
        b_class,
    ) = unpack(small_params)
    vectors = [
        vector.reshape(1, -1)
        for vector in (b_out, gain_one, shift_one, b_up, b_down, gain_two, shift_two, b_student, pool_query, b_hidden)
    ]
    vectors.append(jnp.pad(w_class.reshape(SD, NCLS), ((0, 0), (0, SD - NCLS))))
    vectors.append(jnp.pad(b_class.reshape(1, NCLS), ((0, 0), (0, SD - NCLS))))

    x = jnp.concatenate([x_short.reshape(-1, D), x_long.reshape(-1, D)], axis=0)
    b_qkv = jnp.concatenate([b_query, jnp.zeros((D,), F32), b_value])
    scales = jnp.concatenate([jnp.full((D,), 0.125, F32), jnp.ones((2 * D,), F32)])
    qkv = ((product(x, w_qkv) + b_qkv) * scales).astype(BF16)
    context, probs_short, probs_long = attention(len_short, len_long, qkv, short_tiles, width)

    logit_cot = jnp.concatenate(
        [
            jnp.pad(
                logit_cot_short.reshape(short_tiles, per_tile, NCLS),
                ((0, 0), (0, 8 - per_tile), (0, SD - NCLS)),
            ),
            jnp.pad(logit_cot_long.reshape(long_seqs, 1, NCLS), ((0, 0), (0, 7), (0, SD - NCLS))),
        ],
        axis=0,
    )
    (
        enc_short,
        enc_long,
        logits,
        first,
        active,
        d_up,
        d_down,
        d_branch,
        d_context,
        d_resid,
        g_student,
        g_hidden,
        g_b_out,
        g_gain_one,
        g_shift_one,
        g_b_up,
        g_b_down,
        g_gain_two,
        g_shift_two,
        g_b_student,
        g_pool_query,
        g_b_hidden,
        g_w_class,
        g_b_class,
    ) = feed(
        len_short,
        len_long,
        x,
        context,
        cot_short.reshape(-1, D),
        cot_long.reshape(-1, D),
        logit_cot,
        vectors,
        (w_out, w_up, w_down, w_student, w_hidden),
        short_tiles,
        width,
    )
    g_down = left_product(active, d_down).astype(BF16)
    g_up = left_product(first, d_up).astype(BF16)
    g_out = left_product(context, d_branch).astype(BF16)
    d_query, d_key, d_value, in_short, in_long, g_b_query, g_b_value = attention_back(
        qkv, probs_short, probs_long, d_context, d_resid, w_qkv, short_tiles
    )
    g_query = left_product(x, d_query).astype(BF16)
    g_key = left_product(x, d_key).astype(BF16)
    g_value = left_product(x, d_value).astype(BF16)

    used = jnp.ones((all_slots,), jnp.int32).at[block_slot].set(0)
    empty = jnp.nonzero(used, size=all_slots - NBLK)[0].astype(jnp.int32)
    slot_terms = spread(
        block_slot,
        empty,
        (g_query, g_key, g_value, g_out, g_up, g_down, g_student.astype(BF16), g_hidden.astype(BF16)),
        all_slots,
    )
    shard_grad = lax.psum_scatter(slot_terms, "fsdp", scatter_dimension=0, tiled=True)
    slot_grad = lax.psum(shard_grad, "dp").astype(F32)
    small_grad = lax.psum(
        jnp.concatenate(
            [
                vector.reshape(-1)
                for vector in (
                    g_b_query,
                    g_b_value,
                    g_b_out,
                    g_gain_one,
                    g_shift_one,
                    g_b_up,
                    g_b_down,
                    g_gain_two,
                    g_shift_two,
                    g_b_student,
                    g_pool_query,
                    g_b_hidden,
                    g_w_class[:, :NCLS],
                    g_b_class[:, :NCLS],
                )
            ]
        ),
        ("dp", "fsdp"),
    )
    outer_left = jnp.einsum("sij,skj->sik", slot_grad, slot_grad, precision=HIGHEST_PRECISION)
    outer_right = jnp.einsum("sji,sjk->sik", slot_grad, slot_grad, precision=HIGHEST_PRECISION)
    new_left = STAT_DECAY * left_stat + (1.0 - STAT_DECAY) * outer_left
    new_right = STAT_DECAY * right_stat + (1.0 - STAT_DECAY) * outer_right
    left_applied = jnp.einsum("sij,sjk->sik", left_root, slot_grad, precision=HIGHEST_PRECISION)
    conditioned = jnp.einsum("sij,sjk->sik", left_applied, right_root, precision=HIGHEST_PRECISION)
    new_master = master - MATRIX_RATE * conditioned
    new_first = BETA_ONE * small_first + (1.0 - BETA_ONE) * small_grad
    new_second = BETA_TWO * small_second + (1.0 - BETA_TWO) * small_grad * small_grad
    first_hat = new_first / (1.0 - BETA_ONE**STEP)
    second_hat = new_second / (1.0 - BETA_TWO**STEP)
    new_small = small_params - ADAM_RATE * first_hat / (jnp.sqrt(second_hat) + ADAM_EPSILON)
    return (
        enc_short.reshape(x_short.shape),
        logits[:short_tiles, :per_tile, :NCLS].reshape(short_seqs, NCLS),
        enc_long.reshape(x_long.shape),
        logits[short_tiles:, 0, :NCLS],
        in_short.reshape(x_short.shape),
        in_long.reshape(x_long.shape),
        slot_grad,
        new_left,
        new_right,
        new_master,
        new_first,
        new_second,
        new_small,
    )


def solution(mesh):
    both = ("dp", "fsdp")
    placed = (
        P(both, None, None),
        P(both, None, None),
        P(both, None, None),
        P(both, None, None),
        P(both, None),
        P(both, None),
        P(both),
        P(both),
        P(),
        P("fsdp", None, None),
        P("fsdp", None, None),
        P("fsdp", None, None),
        P("fsdp", None, None),
        P("fsdp", None, None),
        P(),
        P(),
        P(),
    )
    return jax.shard_map(
        body,
        mesh=mesh,
        in_specs=placed,
        out_specs=(
            P(both, None, None),
            P(both, None),
            P(both, None, None),
            P(both, None),
            P(both, None, None),
            P(both, None, None),
            P("fsdp", None, None),
            P("fsdp", None, None),
            P("fsdp", None, None),
            P("fsdp", None, None),
            P(),
            P(),
            P(),
        ),
        check_vma=False,
    )
```

```python
from functools import partial

import jax
import jax.numpy as jnp
from jax import lax
from jax.experimental import pallas as pl
from jax.experimental.pallas import tpu as pltpu
from jax.sharding import PartitionSpec as P

D = 768
HEADS = 12
FF = 3072
SD = 128
PH = 2
NCLS = 14
BLK = 128
STEP = 10
NBLK = 439
TILE = 512
PAIRS = 3
GROUPS = 2
CHUNK = 768

NORM_EPSILON = 1e-12
BETA_ONE = 0.9
BETA_TWO = 0.999
ADAM_EPSILON = 1e-08
ADAM_RATE = 0.1
MATRIX_RATE = 0.2
STAT_DECAY = 0.5
MASKED_SCORE = -1e30
HIGHEST_PRECISION = lax.Precision.HIGHEST
MIB = 1024 * 1024
F32 = jnp.float32
BF16 = jnp.bfloat16

def product(former, latter, precision=None):
    return jnp.dot(former, latter, preferred_element_type=F32, precision=precision)


def left_product(former, latter, precision=None):
    return lax.dot_general(
        former, latter, (((0,), (0,)), ((), ())), preferred_element_type=F32, precision=precision
    )


def right_product(former, latter, precision=None):
    return lax.dot_general(
        former, latter, (((1,), (1,)), ((), ())), preferred_element_type=F32, precision=precision
    )


def unpack(small_values):
    widths = (D, D, D, D, D, FF, D, D, D, SD, SD, SD, SD * NCLS, NCLS)
    pieces = []
    offset = 0
    for column_count in widths:
        pieces.append(small_values[offset : offset + column_count])
        offset += column_count
    return pieces


def load_blocks(slot_ref, blocks, target, sem, first, row_count, col_count, col_start=0):
    def move(index, carry):
        row = pl.multiple_of((index // col_count) * BLK, BLK)
        col = pl.multiple_of((index % col_count + col_start) * BLK, BLK)
        pltpu.make_async_copy(
            blocks.at[slot_ref[first + index]],
            target.at[pl.ds(row, BLK), pl.ds(col, BLK)],
            sem,
        ).start()
        return carry

    lax.fori_loop(0, row_count * col_count, move, 0)


def wait_whole(target, sem):
    pltpu.make_async_copy(target, target, sem).wait()


def load_qkv(slot_ref, blocks, target, sem):
    load_blocks(slot_ref, blocks, target, sem, 0, 6, 6, 0)
    load_blocks(slot_ref, blocks, target, sem, 36, 6, 6, 6)
    load_blocks(slot_ref, blocks, target, sem, 72, 6, 6, 12)


SOURCES = (
    (0, 6, 6),
    (36, 6, 6),
    (72, 6, 6),
    (108, 6, 6),
    (144, 6, 24),
    (288, 24, 6),
    (432, 6, 1),
    (438, 1, 1),
)


def spread_kernel(slot_ref, empty_ref, *refs):
    grads, zero, out, sem = refs[:-3], refs[-3], refs[-2], refs[-1]
    for grad, (first, row_count, col_count) in zip(grads, SOURCES):

        def move(index, carry, grad=grad, first=first, col_count=col_count):
            row = pl.multiple_of((index // col_count) * BLK, BLK)
            col = pl.multiple_of((index % col_count) * BLK, BLK)
            pltpu.make_async_copy(
                grad.at[pl.ds(row, BLK), pl.ds(col, BLK)],
                out.at[slot_ref[first + index]],
                sem,
            ).start()
            return carry

        lax.fori_loop(0, row_count * col_count, move, 0)
    for index in range(empty_ref.shape[0]):
        pltpu.make_async_copy(zero, out.at[empty_ref[index]], sem).start()
    pltpu.make_async_copy(out, out, sem).wait()


def spread(block_slot, empty, grads, slot_count):
    return pl.pallas_call(
        spread_kernel,
        grid_spec=pltpu.PrefetchScalarGridSpec(
            num_scalar_prefetch=2,
            grid=(1,),
            in_specs=[pl.BlockSpec(memory_space=pltpu.VMEM)] * (len(grads) + 1),
            out_specs=pl.BlockSpec(memory_space=pl.ANY),
            scratch_shapes=[pltpu.SemaphoreType.DMA],
        ),
        out_shape=jax.ShapeDtypeStruct((slot_count, BLK, BLK), BF16),
        compiler_params=pltpu.CompilerParams(vmem_limit_bytes=32 * MIB),
        name="spread",
    )(block_slot, empty, *grads, jnp.zeros((BLK, BLK), BF16))


def half_masks():
    lane = lax.broadcasted_iota(jnp.int32, (1, BLK), 1)
    low = (lane < BLK // 2).astype(BF16)
    return low, (1.0 - low.astype(F32)).astype(BF16)


def stack_heads(values, low, high):
    return jnp.concatenate([values * low, values * high], axis=0)


def pick_heads(values):
    rows = values.shape[0] // 2
    lane = lax.broadcasted_iota(jnp.int32, (rows, BLK), 1)
    return jnp.where(lane < BLK // 2, values[:rows], values[rows:])


def attend(queries, key_rows, value_rows, length, low, high):
    scores = right_product(stack_heads(queries, low, high), key_rows)
    place = lax.broadcasted_iota(jnp.int32, scores.shape, 1)
    scores = jnp.where(place < length, scores, MASKED_SCORE)
    powers = jnp.exp(scores - jnp.max(scores, axis=-1, keepdims=True))
    total = jnp.sum(powers, axis=-1, keepdims=True)
    probs = (powers * (1.0 / total)).astype(BF16)
    return probs, pick_heads(product(probs, value_rows)).astype(BF16)


def attention_kernel(
    len_short,
    len_long,
    slot_ref,
    x_ref,
    b_query,
    b_value,
    blocks,
    q_ref,
    k_ref,
    v_ref,
    context_ref,
    short_ref,
    long_ref,
    w_ref,
    sem,
    *,
    short_tiles,
):
    tile = pl.program_id(0)
    group = pl.program_id(1)
    low, high = half_masks()
    per_tile = TILE // short_ref.shape[-1]
    width = short_ref.shape[-1]

    @pl.when((tile == 0) & (group == 0))
    def _():
        load_qkv(slot_ref, blocks, w_ref, sem)
        wait_whole(w_ref, sem)

    wide = PAIRS * BLK
    start = pl.multiple_of(group * wide, wide)
    rows_in = x_ref[...]
    queries = product(rows_in, w_ref[:, pl.ds(start, wide)]) + b_query[:, pl.ds(start, wide)]
    q_ref[...] = (queries * 0.125).astype(BF16)
    k_ref[...] = product(rows_in, w_ref[:, pl.ds(D + start, wide)]).astype(BF16)
    values = product(rows_in, w_ref[:, pl.ds(2 * D + start, wide)]) + b_value[:, pl.ds(start, wide)]
    v_ref[...] = values.astype(BF16)

    @pl.when(tile < short_tiles)
    def _():
        for pair in range(PAIRS):
            cols = slice(pair * BLK, (pair + 1) * BLK)
            for seq in range(per_tile):
                rows = slice(seq * width, (seq + 1) * width)
                probs, context = attend(
                    q_ref[rows, cols],
                    k_ref[rows, cols],
                    v_ref[rows, cols],
                    len_short[tile * per_tile + seq],
                    low,
                    high,
                )
                short_ref[0, pair, seq] = probs
                context_ref[rows, cols] = context

    @pl.when(tile >= short_tiles)
    def _():
        length = len_long[tile - short_tiles]
        half = TILE // 2
        for pair in range(PAIRS):
            cols = slice(pair * BLK, (pair + 1) * BLK)
            for part in range(2):
                rows = slice(part * half, (part + 1) * half)
                probs, context = attend(
                    q_ref[rows, cols], k_ref[:, cols], v_ref[:, cols], length, low, high
                )
                long_ref[0, pair, part] = probs
                context_ref[rows, cols] = context


def probs_shapes(short_tiles, long_tiles, width):
    per_tile = TILE // width
    return (
        (short_tiles, 2 * PAIRS, per_tile, 2 * width, width),
        (long_tiles, 2 * PAIRS, 2, TILE, TILE),
    )


def short_index(tile, short_tiles):
    return jnp.minimum(tile, short_tiles - 1)


def long_index(tile, short_tiles):
    return jnp.maximum(tile - short_tiles, 0)


def attention(len_short, len_long, block_slot, x, b_query, b_value, blocks, short_tiles, width):
    tiles = x.shape[0] // TILE
    wide = PAIRS * BLK
    short_shape, long_shape = probs_shapes(short_tiles, tiles - short_tiles, width)

    def short_map(tile, group, *_):
        return (short_index(tile, short_tiles), jnp.where(tile < short_tiles, group, GROUPS - 1), 0, 0, 0)

    def long_map(tile, group, *_):
        return (long_index(tile, short_tiles), jnp.where(tile < short_tiles, 0, group), 0, 0, 0)

    flops = 4 * D * TILE * TILE * tiles + 6 * D * D * TILE * tiles
    rows = pl.BlockSpec((TILE, wide), lambda tile, group, *_: (tile, group))
    bias = pl.BlockSpec((1, D), lambda tile, group, *_: (0, 0))
    return pl.pallas_call(
        partial(attention_kernel, short_tiles=short_tiles),
        grid_spec=pltpu.PrefetchScalarGridSpec(
            num_scalar_prefetch=3,
            grid=(tiles, GROUPS),
            in_specs=[
                pl.BlockSpec((TILE, D), lambda tile, group, *_: (tile, 0)),
                bias,
                bias,
                pl.BlockSpec(memory_space=pl.ANY),
            ],
            out_specs=[
                rows,
                rows,
                rows,
                rows,
                pl.BlockSpec((1, PAIRS) + short_shape[2:], short_map),
                pl.BlockSpec((1, PAIRS) + long_shape[2:], long_map),
            ],
            scratch_shapes=[pltpu.VMEM((D, 3 * D), BF16), pltpu.SemaphoreType.DMA],
        ),
        out_shape=[jax.ShapeDtypeStruct((tiles * TILE, D), BF16)] * 4
        + [
            jax.ShapeDtypeStruct(short_shape, BF16),
            jax.ShapeDtypeStruct(long_shape, BF16),
        ],
        compiler_params=pltpu.CompilerParams(vmem_limit_bytes=48 * MIB),
        cost_estimate=pl.CostEstimate(
            flops=flops, bytes_accessed=35 * MIB, transcendentals=HEADS * TILE * TILE * tiles // 2
        ),
        name="attention",
    )(len_short, len_long, block_slot, x, b_query, b_value, blocks)


def attend_back(queries, key_rows, value_rows, d_context, probs, low, high):
    stacked = stack_heads(d_context, low, high)
    d_probs = right_product(stacked, value_rows)
    wide = probs.astype(F32)
    weighted = wide * d_probs
    d_scores = (weighted - wide * jnp.sum(weighted, axis=-1, keepdims=True)).astype(BF16)
    d_queries = pick_heads(product(d_scores, key_rows)) * 0.125
    d_keys = left_product(d_scores, stack_heads(queries, low, high))
    d_values = left_product(probs, stacked)
    return d_queries.astype(BF16), d_keys, d_values


def attention_back_kernel(
    slot_ref,
    q_ref,
    k_ref,
    v_ref,
    short_ref,
    long_ref,
    dc_ref,
    resid_ref,
    blocks,
    dq_ref,
    dk_ref,
    dv_ref,
    in_short_ref,
    in_long_ref,
    bq_ref,
    bv_ref,
    w_ref,
    sem,
    *,
    short_tiles,
):
    tile = pl.program_id(0)
    group = pl.program_id(1)
    low, high = half_masks()
    width = short_ref.shape[-1]
    per_tile = TILE // width
    first_step = (tile == 0) & (group == 0)

    @pl.when(first_step)
    def _():
        load_qkv(slot_ref, blocks, w_ref, sem)

    @pl.when(tile < short_tiles)
    def _():
        for pair in range(PAIRS):
            cols = slice(pair * BLK, (pair + 1) * BLK)
            for seq in range(per_tile):
                rows = slice(seq * width, (seq + 1) * width)
                d_queries, d_keys, d_values = attend_back(
                    q_ref[rows, cols],
                    k_ref[rows, cols],
                    v_ref[rows, cols],
                    dc_ref[rows, cols],
                    short_ref[0, pair, seq],
                    low,
                    high,
                )
                dq_ref[rows, cols] = d_queries
                dk_ref[rows, cols] = d_keys.astype(BF16)
                dv_ref[rows, cols] = d_values.astype(BF16)

    @pl.when(tile >= short_tiles)
    def _():
        half = TILE // 2
        for pair in range(PAIRS):
            cols = slice(pair * BLK, (pair + 1) * BLK)
            keys_sum = None
            values_sum = None
            for part in range(2):
                rows = slice(part * half, (part + 1) * half)
                d_queries, d_keys, d_values = attend_back(
                    q_ref[rows, cols],
                    k_ref[:, cols],
                    v_ref[:, cols],
                    dc_ref[rows, cols],
                    long_ref[0, pair, part],
                    low,
                    high,
                )
                dq_ref[rows, cols] = d_queries
                keys_sum = d_keys if keys_sum is None else keys_sum + d_keys
                values_sum = d_values if values_sum is None else values_sum + d_values
            dk_ref[:, cols] = keys_sum.astype(BF16)
            dv_ref[:, cols] = values_sum.astype(BF16)

    wide = PAIRS * BLK
    start = pl.multiple_of(group * wide, wide)

    @pl.when(first_step)
    def _():
        wait_whole(w_ref, sem)
        bq_ref[...] = jnp.zeros_like(bq_ref)
        bv_ref[...] = jnp.zeros_like(bv_ref)

    bq_ref[:, pl.ds(start, wide)] += jnp.sum(dq_ref[...].astype(F32), axis=0, keepdims=True)
    bv_ref[:, pl.ds(start, wide)] += jnp.sum(dv_ref[...].astype(F32), axis=0, keepdims=True)
    total = (
        right_product(dq_ref[...], w_ref[:, pl.ds(start, wide)])
        + right_product(dk_ref[...], w_ref[:, pl.ds(D + start, wide)])
        + right_product(dv_ref[...], w_ref[:, pl.ds(2 * D + start, wide)])
    )

    @pl.when((tile < short_tiles) & (group == 0))
    def _():
        in_short_ref[...] = resid_ref[...] + total

    @pl.when((tile < short_tiles) & (group > 0))
    def _():
        in_short_ref[...] += total

    @pl.when((tile >= short_tiles) & (group == 0))
    def _():
        in_long_ref[...] = resid_ref[...] + total

    @pl.when((tile >= short_tiles) & (group > 0))
    def _():
        in_long_ref[...] += total


def attention_back(block_slot, qkv, probs_short, probs_long, d_context, resid, blocks, short_tiles):
    tiles = d_context.shape[0] // TILE
    wide = PAIRS * BLK

    def short_map(tile, group, *_):
        return (short_index(tile, short_tiles), jnp.where(tile < short_tiles, group, GROUPS - 1), 0, 0, 0)

    def long_map(tile, group, *_):
        return (long_index(tile, short_tiles), jnp.where(tile < short_tiles, 0, group), 0, 0, 0)

    rows = pl.BlockSpec((TILE, wide), lambda tile, group, *_: (tile, group))
    row = pl.BlockSpec((1, D), lambda tile, group, *_: (0, 0))
    flops = 10 * D * TILE * TILE * tiles + 6 * D * D * TILE * tiles
    return pl.pallas_call(
        partial(attention_back_kernel, short_tiles=short_tiles),
        grid_spec=pltpu.PrefetchScalarGridSpec(
            num_scalar_prefetch=1,
            grid=(tiles, GROUPS),
            in_specs=[
                rows,
                rows,
                rows,
                pl.BlockSpec((1, PAIRS) + probs_short.shape[2:], short_map),
                pl.BlockSpec((1, PAIRS) + probs_long.shape[2:], long_map),
                rows,
                pl.BlockSpec((TILE, D), lambda tile, group, *_: (tile, 0)),
                pl.BlockSpec(memory_space=pl.ANY),
            ],
            out_specs=[
                rows,
                rows,
                rows,
                pl.BlockSpec((TILE, D), lambda tile, group, *_: (short_index(tile, short_tiles), 0)),
                pl.BlockSpec((TILE, D), lambda tile, group, *_: (long_index(tile, short_tiles), 0)),
                row,
                row,
            ],
            scratch_shapes=[pltpu.VMEM((D, 3 * D), BF16), pltpu.SemaphoreType.DMA],
        ),
        out_shape=[
            jax.ShapeDtypeStruct((tiles * TILE, D), BF16),
            jax.ShapeDtypeStruct((tiles * TILE, D), BF16),
            jax.ShapeDtypeStruct((tiles * TILE, D), BF16),
            jax.ShapeDtypeStruct((short_tiles * TILE, D), F32),
            jax.ShapeDtypeStruct(((tiles - short_tiles) * TILE, D), F32),
            jax.ShapeDtypeStruct((1, D), F32),
            jax.ShapeDtypeStruct((1, D), F32),
        ],
        compiler_params=pltpu.CompilerParams(
            vmem_limit_bytes=56 * MIB, fuse_transposed_lhs_in_matmul=True
        ),
        cost_estimate=pl.CostEstimate(flops=flops, bytes_accessed=50 * MIB, transcendentals=0),
        name="attention_back",
    )(block_slot, *qkv, probs_short, probs_long, d_context, resid, blocks)


def normal_parts(values):
    below = 0.5 * lax.erf(values * 0.7071067811865476) + 0.5
    return below, jnp.exp(-0.5 * values * values) * 0.3989422804014327


def norm_parts(values):
    center = values - jnp.mean(values, axis=-1, keepdims=True)
    spread = jnp.mean(center * center, axis=-1, keepdims=True)
    inverse = lax.rsqrt(spread + NORM_EPSILON)
    return center * inverse, inverse


def norm_back(d_values, gain, unit, inverse):
    d_unit = d_values * gain
    return inverse * (
        d_unit
        - jnp.mean(d_unit, axis=-1, keepdims=True)
        - unit * jnp.mean(d_unit * unit, axis=-1, keepdims=True)
    )


def column_sum(values):
    return jnp.sum(values.astype(F32), axis=0, keepdims=True)


def pool_weights(student, query, length):
    scaled = student * query
    lane = lax.broadcasted_iota(jnp.int32, scaled.shape, 1)
    place = lax.broadcasted_iota(jnp.int32, (scaled.shape[0], 1), 0)
    weights = []
    for side in (lane < SD // PH, lane >= SD // PH):
        scores = jnp.sum(jnp.where(side, scaled, 0.0), axis=-1, keepdims=True)
        scores = jnp.where(place < length, scores, MASKED_SCORE)
        powers = jnp.exp(scores - jnp.max(scores, axis=0, keepdims=True))
        weights.append(powers / jnp.sum(powers, axis=0, keepdims=True))
    return jnp.where(lane < SD // PH, weights[0], weights[1]), weights


def student_back(student, query, weights, both, d_pooled):
    lane = lax.broadcasted_iota(jnp.int32, student.shape, 1)
    moved = student * d_pooled
    d_scores = []
    for side, weight in zip((lane < SD // PH, lane >= SD // PH), weights):
        d_weight = jnp.sum(jnp.where(side, moved, 0.0), axis=-1, keepdims=True)
        d_scores.append(weight * (d_weight - jnp.sum(weight * d_weight, axis=0, keepdims=True)))
    d_score = jnp.where(lane < SD // PH, d_scores[0], d_scores[1])
    d_query = jnp.sum(d_score * student, axis=0, keepdims=True) * 0.125
    return both * d_pooled + d_score * query, d_query


def feed_kernel(
    len_short,
    len_long,
    slot_ref,
    x_ref,
    context_ref,
    cot_short_ref,
    cot_long_ref,
    logit_cot_ref,
    b_out,
    gain_one,
    shift_one,
    b_up,
    b_down,
    gain_two,
    shift_two,
    b_student,
    pool_query,
    b_hidden,
    w_class,
    b_class,
    blocks,
    enc_short_ref,
    enc_long_ref,
    logit_ref,
    first_ref,
    active_ref,
    d_up_ref,
    d_down_ref,
    d_branch_ref,
    d_context_ref,
    d_resid_ref,
    g_student,
    g_hidden,
    g_b_out,
    g_gain_one,
    g_shift_one,
    g_b_up,
    g_b_down,
    g_gain_two,
    g_shift_two,
    g_b_student,
    g_pool_query,
    g_b_hidden,
    g_w_class,
    g_b_class,
    slope,
    pooled_ref,
    d_student_ref,
    w_out,
    w_up,
    w_down,
    w_student,
    w_hidden,
    sems,
    *,
    short_tiles,
    width,
):
    tile = pl.program_id(0)
    per_tile = TILE // width

    @pl.when(tile == 0)
    def _():
        for ref in (
            g_student,
            g_hidden,
            g_b_out,
            g_gain_one,
            g_shift_one,
            g_b_up,
            g_b_down,
            g_gain_two,
            g_shift_two,
            g_b_student,
            g_pool_query,
            g_b_hidden,
            g_w_class,
            g_b_class,
        ):
            ref[...] = jnp.zeros_like(ref)

    loads = ((w_out, 108, 6, 6), (w_up, 144, 6, 24), (w_down, 288, 24, 6), (w_student, 432, 6, 1), (w_hidden, 438, 1, 1))

    @pl.when(tile == 0)
    def _():
        for index, (target, block, row_count, col_count) in enumerate(loads):
            load_blocks(slot_ref, blocks, target, sems.at[index], block, row_count, col_count)
        for index, (target, *_) in enumerate(loads):
            wait_whole(target, sems.at[index])

    branch = product(context_ref[...], w_out[...]) + b_out[...]
    unit_one, inverse_one = norm_parts(x_ref[...].astype(F32) + branch)
    first = (unit_one * gain_one[...] + shift_one[...]).astype(BF16)
    first_ref[...] = first
    for start in range(0, FF, CHUNK):
        cols = slice(start, start + CHUNK)
        upward = product(first, w_up[:, cols]) + b_up[:, cols]
        below, density = normal_parts(upward)
        active_ref[:, cols] = (upward * below).astype(BF16)
        slope[:, cols] = (below + upward * density).astype(BF16)
    downward = product(active_ref[...], w_down[...]) + b_down[...]
    unit_two, inverse_two = norm_parts(first.astype(F32) + downward)
    encoded = (unit_two * gain_two[...] + shift_two[...]).astype(BF16)

    @pl.when(tile < short_tiles)
    def _():
        enc_short_ref[...] = encoded

    @pl.when(tile >= short_tiles)
    def _():
        enc_long_ref[...] = encoded

    student = product(encoded, w_student[...]) + b_student[...]
    query = pool_query[...] * 0.125
    pooled_ref[...] = jnp.zeros_like(pooled_ref)

    def head():
        pooled = pooled_ref[...]
        wide_hidden = w_hidden[...].astype(F32)
        hidden = jnp.tanh(product(pooled, wide_hidden, HIGHEST_PRECISION) + b_hidden[...])
        logit_ref[0] = product(hidden, w_class[...], HIGHEST_PRECISION) + b_class[...]
        d_logits = logit_cot_ref[0]
        g_b_class[...] += column_sum(d_logits)
        g_w_class[...] += left_product(hidden, d_logits, HIGHEST_PRECISION)
        d_hidden = right_product(d_logits, w_class[...], HIGHEST_PRECISION)
        d_hidden = d_hidden * (1.0 - hidden * hidden)
        g_b_hidden[...] += column_sum(d_hidden)
        g_hidden[...] += left_product(pooled, d_hidden, HIGHEST_PRECISION)
        return right_product(d_hidden, wide_hidden, HIGHEST_PRECISION)

    def pool(starts, size, lengths):
        kept = []
        for index, (start, length) in enumerate(zip(starts, lengths)):
            rows = student[start : start + size]
            both, weights = pool_weights(rows, query, length)
            pooled_ref[index : index + 1, :] = column_sum(both * rows)
            kept.append((start, rows, both, weights))
        d_pooled = head()
        for index, (start, rows, both, weights) in enumerate(kept):
            d_rows, d_query = student_back(rows, query, weights, both, d_pooled[index : index + 1])
            d_student_ref[start : start + size, :] = d_rows.astype(BF16)
            g_pool_query[...] += d_query

    @pl.when(tile < short_tiles)
    def _():
        pool(
            [seq * width for seq in range(per_tile)],
            width,
            [len_short[tile * per_tile + seq] for seq in range(per_tile)],
        )

    @pl.when(tile >= short_tiles)
    def _():
        pool([0], TILE, [len_long[tile - short_tiles]])

    d_student = d_student_ref[...]
    g_b_student[...] += column_sum(d_student)
    g_student[...] += left_product(encoded, d_student)
    cotangent = jnp.where(tile < short_tiles, cot_short_ref[...], cot_long_ref[...])
    d_second = cotangent.astype(F32) + right_product(d_student, w_student[...])
    g_gain_two[...] += column_sum(d_second * unit_two)
    g_shift_two[...] += column_sum(d_second)
    d_resid_two = norm_back(d_second, gain_two[...], unit_two, inverse_two)
    d_down = d_resid_two.astype(BF16)
    d_down_ref[...] = d_down
    g_b_down[...] += column_sum(d_down)
    for start in range(0, FF, CHUNK):
        cols = slice(start, start + CHUNK)
        d_active = right_product(d_down, w_down[cols, :])
        d_up = (d_active * slope[:, cols].astype(F32)).astype(BF16)
        d_up_ref[:, cols] = d_up
        g_b_up[:, cols] += column_sum(d_up)
    d_first = d_resid_two + right_product(d_up_ref[...], w_up[...])
    g_gain_one[...] += column_sum(d_first * unit_one)
    g_shift_one[...] += column_sum(d_first)
    d_resid_one = norm_back(d_first, gain_one[...], unit_one, inverse_one)
    d_resid_ref[...] = d_resid_one
    d_branch = d_resid_one.astype(BF16)
    d_branch_ref[...] = d_branch
    g_b_out[...] += column_sum(d_branch)
    d_context_ref[...] = right_product(d_branch, w_out[...]).astype(BF16)


def feed(len_short, len_long, block_slot, x, context, cot_short, cot_long, logit_cot, vectors, blocks, short_tiles, width):
    tiles = x.shape[0] // TILE
    long_tiles = tiles - short_tiles

    def whole(shape):
        return pl.BlockSpec(shape, lambda tile, *_: (0,) * len(shape), pipeline_mode=pl.Buffered(1))

    def kept(shape):
        return pl.BlockSpec(shape, lambda tile, *_: (0,) * len(shape))

    def rows(columns):
        return pl.BlockSpec((TILE, columns), lambda tile, *_: (tile, 0))

    short_rows = pl.BlockSpec((TILE, D), lambda tile, *_: (short_index(tile, short_tiles), 0))
    long_rows = pl.BlockSpec((TILE, D), lambda tile, *_: (long_index(tile, short_tiles), 0))
    logit_rows = pl.BlockSpec((1, 8, SD), lambda tile, *_: (tile, 0, 0))
    grad_shapes = (
        (D, SD),
        (SD, SD),
        (1, D),
        (1, D),
        (1, D),
        (1, FF),
        (1, D),
        (1, D),
        (1, D),
        (1, SD),
        (1, SD),
        (1, SD),
        (SD, SD),
        (1, SD),
    )
    total = tiles * TILE
    return pl.pallas_call(
        partial(feed_kernel, short_tiles=short_tiles, width=width),
        grid_spec=pltpu.PrefetchScalarGridSpec(
            num_scalar_prefetch=3,
            grid=(tiles,),
            in_specs=[rows(D), rows(D), short_rows, long_rows, logit_rows]
            + [whole(vector.shape) for vector in vectors]
            + [pl.BlockSpec(memory_space=pl.ANY)],
            out_specs=[
                short_rows,
                long_rows,
                logit_rows,
                rows(D),
                rows(FF),
                rows(FF),
                rows(D),
                rows(D),
                rows(D),
                rows(D),
            ]
            + [kept(shape) for shape in grad_shapes],
            scratch_shapes=[
                pltpu.VMEM((TILE, FF), BF16),
                pltpu.VMEM((8, SD), F32),
                pltpu.VMEM((TILE, SD), BF16),
                pltpu.VMEM((D, D), BF16),
                pltpu.VMEM((D, FF), BF16),
                pltpu.VMEM((FF, D), BF16),
                pltpu.VMEM((D, SD), BF16),
                pltpu.VMEM((SD, SD), BF16),
                pltpu.SemaphoreType.DMA((5,)),
            ],
        ),
        out_shape=[
            jax.ShapeDtypeStruct((short_tiles * TILE, D), BF16),
            jax.ShapeDtypeStruct((long_tiles * TILE, D), BF16),
            jax.ShapeDtypeStruct((tiles, 8, SD), F32),
            jax.ShapeDtypeStruct((total, D), BF16),
            jax.ShapeDtypeStruct((total, FF), BF16),
            jax.ShapeDtypeStruct((total, FF), BF16),
            jax.ShapeDtypeStruct((total, D), BF16),
            jax.ShapeDtypeStruct((total, D), BF16),
            jax.ShapeDtypeStruct((total, D), BF16),
            jax.ShapeDtypeStruct((total, D), F32),
        ]
        + [jax.ShapeDtypeStruct(shape, F32) for shape in grad_shapes],
        compiler_params=pltpu.CompilerParams(vmem_limit_bytes=60 * MIB),
        cost_estimate=pl.CostEstimate(
            flops=total * (8 * D * FF + 4 * D * D), bytes_accessed=70 * MIB, transcendentals=total * FF
        ),
        name="feed",
    )(len_short, len_long, block_slot, x, context, cot_short, cot_long, logit_cot, *vectors, blocks)


def body(
    x_short,
    x_long,
    cot_short,
    cot_long,
    logit_cot_short,
    logit_cot_long,
    len_short,
    len_long,
    block_slot,
    master,
    left_stat,
    right_stat,
    left_root,
    right_root,
    small_params,
    small_first,
    small_second,
):
    slot_count = master.shape[0]
    all_slots = slot_count * lax.axis_size("fsdp")
    short_seqs, width = x_short.shape[:2]
    long_seqs = x_long.shape[0]
    short_tiles = short_seqs * width // TILE
    per_tile = TILE // width

    gathered = lax.all_gather(master.astype(BF16), "fsdp", axis=0, tiled=True)
    (
        b_query,
        b_value,
        b_out,
        gain_one,
        shift_one,
        b_up,
        b_down,
        gain_two,
        shift_two,
        b_student,
        pool_query,
        b_hidden,
        w_class,
        b_class,
    ) = unpack(small_params)
    vectors = [
        vector.reshape(1, -1)
        for vector in (b_out, gain_one, shift_one, b_up, b_down, gain_two, shift_two, b_student, pool_query, b_hidden)
    ]
    vectors.append(jnp.pad(w_class.reshape(SD, NCLS), ((0, 0), (0, SD - NCLS))))
    vectors.append(jnp.pad(b_class.reshape(1, NCLS), ((0, 0), (0, SD - NCLS))))

    x = jnp.concatenate([x_short.reshape(-1, D), x_long.reshape(-1, D)], axis=0)
    *qkv, context, probs_short, probs_long = attention(
        len_short,
        len_long,
        block_slot,
        x,
        b_query.reshape(1, D),
        b_value.reshape(1, D),
        gathered,
        short_tiles,
        width,
    )

    logit_cot = jnp.concatenate(
        [
            jnp.pad(
                logit_cot_short.reshape(short_tiles, per_tile, NCLS),
                ((0, 0), (0, 8 - per_tile), (0, SD - NCLS)),
            ),
            jnp.pad(logit_cot_long.reshape(long_seqs, 1, NCLS), ((0, 0), (0, 7), (0, SD - NCLS))),
        ],
        axis=0,
    )
    (
        enc_short,
        enc_long,
        logits,
        first,
        active,
        d_up,
        d_down,
        d_branch,
        d_context,
        d_resid,
        g_student,
        g_hidden,
        g_b_out,
        g_gain_one,
        g_shift_one,
        g_b_up,
        g_b_down,
        g_gain_two,
        g_shift_two,
        g_b_student,
        g_pool_query,
        g_b_hidden,
        g_w_class,
        g_b_class,
    ) = feed(
        len_short,
        len_long,
        block_slot,
        x,
        context,
        cot_short.reshape(-1, D),
        cot_long.reshape(-1, D),
        logit_cot,
        vectors,
        gathered,
        short_tiles,
        width,
    )
    g_down = left_product(active, d_down).astype(BF16)
    g_up = left_product(first, d_up).astype(BF16)
    g_out = left_product(context, d_branch).astype(BF16)
    d_query, d_key, d_value, in_short, in_long, g_b_query, g_b_value = attention_back(
        block_slot, qkv, probs_short, probs_long, d_context, d_resid, gathered, short_tiles
    )
    g_query = left_product(x, d_query).astype(BF16)
    g_key = left_product(x, d_key).astype(BF16)
    g_value = left_product(x, d_value).astype(BF16)

    used = jnp.ones((all_slots,), jnp.int32).at[block_slot].set(0)
    empty = jnp.nonzero(used, size=all_slots - NBLK)[0].astype(jnp.int32)
    slot_terms = spread(
        block_slot,
        empty,
        (g_query, g_key, g_value, g_out, g_up, g_down, g_student.astype(BF16), g_hidden.astype(BF16)),
        all_slots,
    )
    shard_grad = lax.psum_scatter(slot_terms, "fsdp", scatter_dimension=0, tiled=True)
    slot_grad = lax.psum(shard_grad, "dp").astype(F32)
    small_grad = lax.psum(
        jnp.concatenate(
            [
                vector.reshape(-1)
                for vector in (
                    g_b_query,
                    g_b_value,
                    g_b_out,
                    g_gain_one,
                    g_shift_one,
                    g_b_up,
                    g_b_down,
                    g_gain_two,
                    g_shift_two,
                    g_b_student,
                    g_pool_query,
                    g_b_hidden,
                    g_w_class[:, :NCLS],
                    g_b_class[:, :NCLS],
                )
            ]
        ),
        ("dp", "fsdp"),
    )
    outer_left = jnp.einsum("sij,skj->sik", slot_grad, slot_grad, precision=HIGHEST_PRECISION)
    outer_right = jnp.einsum("sji,sjk->sik", slot_grad, slot_grad, precision=HIGHEST_PRECISION)
    new_left = STAT_DECAY * left_stat + (1.0 - STAT_DECAY) * outer_left
    new_right = STAT_DECAY * right_stat + (1.0 - STAT_DECAY) * outer_right
    left_applied = jnp.einsum("sij,sjk->sik", left_root, slot_grad, precision=HIGHEST_PRECISION)
    conditioned = jnp.einsum("sij,sjk->sik", left_applied, right_root, precision=HIGHEST_PRECISION)
    new_master = master - MATRIX_RATE * conditioned
    new_first = BETA_ONE * small_first + (1.0 - BETA_ONE) * small_grad
    new_second = BETA_TWO * small_second + (1.0 - BETA_TWO) * small_grad * small_grad
    first_hat = new_first / (1.0 - BETA_ONE**STEP)
    second_hat = new_second / (1.0 - BETA_TWO**STEP)
    new_small = small_params - ADAM_RATE * first_hat / (jnp.sqrt(second_hat) + ADAM_EPSILON)
    return (
        enc_short.reshape(x_short.shape),
        logits[:short_tiles, :per_tile, :NCLS].reshape(short_seqs, NCLS),
        enc_long.reshape(x_long.shape),
        logits[short_tiles:, 0, :NCLS],
        in_short.reshape(x_short.shape),
        in_long.reshape(x_long.shape),
        slot_grad,
        new_left,
        new_right,
        new_master,
        new_first,
        new_second,
        new_small,
    )


def solution(mesh):
    both = ("dp", "fsdp")
    placed = (
        P(both, None, None),
        P(both, None, None),
        P(both, None, None),
        P(both, None, None),
        P(both, None),
        P(both, None),
        P(both),
        P(both),
        P(),
        P("fsdp", None, None),
        P("fsdp", None, None),
        P("fsdp", None, None),
        P("fsdp", None, None),
        P("fsdp", None, None),
        P(),
        P(),
        P(),
    )
    return jax.shard_map(
        body,
        mesh=mesh,
        in_specs=placed,
        out_specs=(
            P(both, None, None),
            P(both, None),
            P(both, None, None),
            P(both, None),
            P(both, None, None),
            P(both, None, None),
            P("fsdp", None, None),
            P("fsdp", None, None),
            P("fsdp", None, None),
            P("fsdp", None, None),
            P(),
            P(),
            P(),
        ),
        check_vma=False,
    )
```

```python
from functools import partial

import jax
import jax.numpy as jnp
from jax import lax
from jax.experimental import pallas as pl
from jax.experimental.pallas import tpu as pltpu
from jax.sharding import PartitionSpec as P

D = 768
HEADS = 12
FF = 3072
SD = 128
PH = 2
NCLS = 14
BLK = 128
STEP = 10
NBLK = 439
TILE = 512
PAIRS = 3
GROUPS = 2
CHUNK = 768

NORM_EPSILON = 1e-12
BETA_ONE = 0.9
BETA_TWO = 0.999
ADAM_EPSILON = 1e-08
ADAM_RATE = 0.1
MATRIX_RATE = 0.2
STAT_DECAY = 0.5
MASKED_SCORE = -1e30
HIGHEST_PRECISION = lax.Precision.HIGHEST
MIB = 1024 * 1024
F32 = jnp.float32
BF16 = jnp.bfloat16

def product(former, latter, precision=None):
    return jnp.dot(former, latter, preferred_element_type=F32, precision=precision)


def left_product(former, latter, precision=None):
    return lax.dot_general(
        former, latter, (((0,), (0,)), ((), ())), preferred_element_type=F32, precision=precision
    )


def right_product(former, latter, precision=None):
    return lax.dot_general(
        former, latter, (((1,), (1,)), ((), ())), preferred_element_type=F32, precision=precision
    )


def unpack(small_values):
    widths = (D, D, D, D, D, FF, D, D, D, SD, SD, SD, SD * NCLS, NCLS)
    pieces = []
    offset = 0
    for column_count in widths:
        pieces.append(small_values[offset : offset + column_count])
        offset += column_count
    return pieces


def load_blocks(slot_ref, blocks, target, sem, first, row_count, col_count, col_start=0):
    def move(index, carry):
        row = pl.multiple_of((index // col_count) * BLK, BLK)
        col = pl.multiple_of((index % col_count + col_start) * BLK, BLK)
        pltpu.make_async_copy(
            blocks.at[slot_ref[first + index]],
            target.at[pl.ds(row, BLK), pl.ds(col, BLK)],
            sem,
        ).start()
        return carry

    lax.fori_loop(0, row_count * col_count, move, 0)


def wait_whole(target, sem):
    pltpu.make_async_copy(target, target, sem).wait()


def load_qkv(slot_ref, blocks, target, sem):
    load_blocks(slot_ref, blocks, target, sem, 0, 6, 6, 0)
    load_blocks(slot_ref, blocks, target, sem, 36, 6, 6, 6)
    load_blocks(slot_ref, blocks, target, sem, 72, 6, 6, 12)


SOURCES = (
    (0, 6, 6),
    (36, 6, 6),
    (72, 6, 6),
    (108, 6, 6),
    (144, 6, 24),
    (288, 24, 6),
    (432, 6, 1),
    (438, 1, 1),
)


def spread_kernel(slot_ref, empty_ref, *refs):
    grads, zero, out, sem = refs[:-3], refs[-3], refs[-2], refs[-1]
    for grad, (first, row_count, col_count) in zip(grads, SOURCES):

        def move(index, carry, grad=grad, first=first, col_count=col_count):
            row = pl.multiple_of((index // col_count) * BLK, BLK)
            col = pl.multiple_of((index % col_count) * BLK, BLK)
            pltpu.make_async_copy(
                grad.at[pl.ds(row, BLK), pl.ds(col, BLK)],
                out.at[slot_ref[first + index]],
                sem,
            ).start()
            return carry

        lax.fori_loop(0, row_count * col_count, move, 0)
    for index in range(empty_ref.shape[0]):
        pltpu.make_async_copy(zero, out.at[empty_ref[index]], sem).start()
    pltpu.make_async_copy(out, out, sem).wait()


def spread(block_slot, empty, grads, slot_count):
    return pl.pallas_call(
        spread_kernel,
        grid_spec=pltpu.PrefetchScalarGridSpec(
            num_scalar_prefetch=2,
            grid=(1,),
            in_specs=[pl.BlockSpec(memory_space=pltpu.VMEM)] * (len(grads) + 1),
            out_specs=pl.BlockSpec(memory_space=pl.ANY),
            scratch_shapes=[pltpu.SemaphoreType.DMA],
        ),
        out_shape=jax.ShapeDtypeStruct((slot_count, BLK, BLK), BF16),
        compiler_params=pltpu.CompilerParams(vmem_limit_bytes=32 * MIB),
        name="spread",
    )(block_slot, empty, *grads, jnp.zeros((BLK, BLK), BF16))


def half_masks():
    lane = lax.broadcasted_iota(jnp.int32, (1, BLK), 1)
    low = (lane < BLK // 2).astype(BF16)
    return low, (1.0 - low.astype(F32)).astype(BF16)


def stack_heads(values, low, high):
    return jnp.concatenate([values * low, values * high], axis=0)


def pick_heads(values):
    rows = values.shape[0] // 2
    lane = lax.broadcasted_iota(jnp.int32, (rows, BLK), 1)
    return jnp.where(lane < BLK // 2, values[:rows], values[rows:])


def attend(queries, key_rows, value_rows, length, low, high):
    scores = right_product(stack_heads(queries, low, high), key_rows)
    place = lax.broadcasted_iota(jnp.int32, scores.shape, 1)
    scores = jnp.where(place < length, scores, MASKED_SCORE)
    powers = jnp.exp(scores - jnp.max(scores, axis=-1, keepdims=True))
    total = jnp.sum(powers, axis=-1, keepdims=True)
    probs = (powers * (1.0 / total)).astype(BF16)
    return probs, pick_heads(product(probs, value_rows)).astype(BF16)


def attention_kernel(
    len_short,
    len_long,
    slot_ref,
    x_ref,
    b_query,
    b_value,
    blocks,
    q_ref,
    k_ref,
    v_ref,
    context_ref,
    short_ref,
    long_ref,
    w_ref,
    sem,
    *,
    short_tiles,
):
    tile = pl.program_id(0)
    group = pl.program_id(1)
    low, high = half_masks()
    per_tile = TILE // short_ref.shape[-1]
    width = short_ref.shape[-1]

    @pl.when((tile == 0) & (group == 0))
    def _():
        load_qkv(slot_ref, blocks, w_ref, sem)
        wait_whole(w_ref, sem)

    wide = PAIRS * BLK
    start = pl.multiple_of(group * wide, wide)
    rows_in = x_ref[...]
    queries = product(rows_in, w_ref[:, pl.ds(start, wide)]) + b_query[:, pl.ds(start, wide)]
    q_ref[...] = (queries * 0.125).astype(BF16)
    k_ref[...] = product(rows_in, w_ref[:, pl.ds(D + start, wide)]).astype(BF16)
    values = product(rows_in, w_ref[:, pl.ds(2 * D + start, wide)]) + b_value[:, pl.ds(start, wide)]
    v_ref[...] = values.astype(BF16)

    @pl.when(tile < short_tiles)
    def _():
        for pair in range(PAIRS):
            cols = slice(pair * BLK, (pair + 1) * BLK)
            for seq in range(per_tile):
                rows = slice(seq * width, (seq + 1) * width)
                probs, context = attend(
                    q_ref[rows, cols],
                    k_ref[rows, cols],
                    v_ref[rows, cols],
                    len_short[tile * per_tile + seq],
                    low,
                    high,
                )
                short_ref[0, pair, seq] = probs
                context_ref[rows, cols] = context

    @pl.when(tile >= short_tiles)
    def _():
        length = len_long[tile - short_tiles]
        half = TILE // 2
        for pair in range(PAIRS):
            cols = slice(pair * BLK, (pair + 1) * BLK)
            for part in range(2):
                rows = slice(part * half, (part + 1) * half)
                probs, context = attend(
                    q_ref[rows, cols], k_ref[:, cols], v_ref[:, cols], length, low, high
                )
                long_ref[0, pair, part] = probs
                context_ref[rows, cols] = context


def probs_shapes(short_tiles, long_tiles, width):
    per_tile = TILE // width
    return (
        (short_tiles, 2 * PAIRS, per_tile, 2 * width, width),
        (long_tiles, 2 * PAIRS, 2, TILE, TILE),
    )


def short_index(tile, short_tiles):
    return jnp.minimum(tile, short_tiles - 1)


def long_index(tile, short_tiles):
    return jnp.maximum(tile - short_tiles, 0)


def attention(len_short, len_long, block_slot, x, b_query, b_value, blocks, short_tiles, width):
    tiles = x.shape[0] // TILE
    wide = PAIRS * BLK
    short_shape, long_shape = probs_shapes(short_tiles, tiles - short_tiles, width)

    def short_map(tile, group, *_):
        return (short_index(tile, short_tiles), jnp.where(tile < short_tiles, group, GROUPS - 1), 0, 0, 0)

    def long_map(tile, group, *_):
        return (long_index(tile, short_tiles), jnp.where(tile < short_tiles, 0, group), 0, 0, 0)

    flops = 4 * D * TILE * TILE * tiles + 6 * D * D * TILE * tiles
    rows = pl.BlockSpec((TILE, wide), lambda tile, group, *_: (tile, group))
    bias = pl.BlockSpec((1, D), lambda tile, group, *_: (0, 0))
    return pl.pallas_call(
        partial(attention_kernel, short_tiles=short_tiles),
        grid_spec=pltpu.PrefetchScalarGridSpec(
            num_scalar_prefetch=3,
            grid=(tiles, GROUPS),
            in_specs=[
                pl.BlockSpec((TILE, D), lambda tile, group, *_: (tile, 0)),
                bias,
                bias,
                pl.BlockSpec(memory_space=pl.ANY),
            ],
            out_specs=[
                rows,
                rows,
                rows,
                rows,
                pl.BlockSpec((1, PAIRS) + short_shape[2:], short_map),
                pl.BlockSpec((1, PAIRS) + long_shape[2:], long_map),
            ],
            scratch_shapes=[pltpu.VMEM((D, 3 * D), BF16), pltpu.SemaphoreType.DMA],
        ),
        out_shape=[jax.ShapeDtypeStruct((tiles * TILE, D), BF16)] * 4
        + [
            jax.ShapeDtypeStruct(short_shape, BF16),
            jax.ShapeDtypeStruct(long_shape, BF16),
        ],
        compiler_params=pltpu.CompilerParams(vmem_limit_bytes=48 * MIB),
        cost_estimate=pl.CostEstimate(
            flops=flops, bytes_accessed=35 * MIB, transcendentals=HEADS * TILE * TILE * tiles // 2
        ),
        name="attention",
    )(len_short, len_long, block_slot, x, b_query, b_value, blocks)


def attend_back(queries, key_rows, value_rows, d_context, probs, low, high):
    stacked = stack_heads(d_context, low, high)
    d_probs = right_product(stacked, value_rows)
    wide = probs.astype(F32)
    weighted = wide * d_probs
    d_scores = (weighted - wide * jnp.sum(weighted, axis=-1, keepdims=True)).astype(BF16)
    d_queries = pick_heads(product(d_scores, key_rows)) * 0.125
    d_keys = left_product(d_scores, stack_heads(queries, low, high))
    d_values = left_product(probs, stacked)
    return d_queries.astype(BF16), d_keys, d_values


def attention_back_kernel(
    slot_ref,
    q_ref,
    k_ref,
    v_ref,
    short_ref,
    long_ref,
    dc_ref,
    resid_ref,
    blocks,
    dq_ref,
    dk_ref,
    dv_ref,
    in_short_ref,
    in_long_ref,
    bq_ref,
    bv_ref,
    w_ref,
    sem,
    *,
    short_tiles,
):
    tile = pl.program_id(0)
    group = pl.program_id(1)
    low, high = half_masks()
    width = short_ref.shape[-1]
    per_tile = TILE // width
    first_step = (tile == 0) & (group == 0)

    @pl.when(first_step)
    def _():
        load_qkv(slot_ref, blocks, w_ref, sem)

    @pl.when(tile < short_tiles)
    def _():
        for pair in range(PAIRS):
            cols = slice(pair * BLK, (pair + 1) * BLK)
            for seq in range(per_tile):
                rows = slice(seq * width, (seq + 1) * width)
                d_queries, d_keys, d_values = attend_back(
                    q_ref[rows, cols],
                    k_ref[rows, cols],
                    v_ref[rows, cols],
                    dc_ref[rows, cols],
                    short_ref[0, pair, seq],
                    low,
                    high,
                )
                dq_ref[rows, cols] = d_queries
                dk_ref[rows, cols] = d_keys.astype(BF16)
                dv_ref[rows, cols] = d_values.astype(BF16)

    @pl.when(tile >= short_tiles)
    def _():
        half = TILE // 2
        for pair in range(PAIRS):
            cols = slice(pair * BLK, (pair + 1) * BLK)
            keys_sum = None
            values_sum = None
            for part in range(2):
                rows = slice(part * half, (part + 1) * half)
                d_queries, d_keys, d_values = attend_back(
                    q_ref[rows, cols],
                    k_ref[:, cols],
                    v_ref[:, cols],
                    dc_ref[rows, cols],
                    long_ref[0, pair, part],
                    low,
                    high,
                )
                dq_ref[rows, cols] = d_queries
                keys_sum = d_keys if keys_sum is None else keys_sum + d_keys
                values_sum = d_values if values_sum is None else values_sum + d_values
            dk_ref[:, cols] = keys_sum.astype(BF16)
            dv_ref[:, cols] = values_sum.astype(BF16)

    wide = PAIRS * BLK
    start = pl.multiple_of(group * wide, wide)

    @pl.when(first_step)
    def _():
        wait_whole(w_ref, sem)
        bq_ref[...] = jnp.zeros_like(bq_ref)
        bv_ref[...] = jnp.zeros_like(bv_ref)

    bq_ref[:, pl.ds(start, wide)] += jnp.sum(dq_ref[...].astype(F32), axis=0, keepdims=True)
    bv_ref[:, pl.ds(start, wide)] += jnp.sum(dv_ref[...].astype(F32), axis=0, keepdims=True)
    total = (
        right_product(dq_ref[...], w_ref[:, pl.ds(start, wide)])
        + right_product(dk_ref[...], w_ref[:, pl.ds(D + start, wide)])
        + right_product(dv_ref[...], w_ref[:, pl.ds(2 * D + start, wide)])
    )

    @pl.when((tile < short_tiles) & (group == 0))
    def _():
        in_short_ref[...] = resid_ref[...] + total

    @pl.when((tile < short_tiles) & (group > 0))
    def _():
        in_short_ref[...] += total

    @pl.when((tile >= short_tiles) & (group == 0))
    def _():
        in_long_ref[...] = resid_ref[...] + total

    @pl.when((tile >= short_tiles) & (group > 0))
    def _():
        in_long_ref[...] += total


def attention_back(block_slot, qkv, probs_short, probs_long, d_context, resid, blocks, short_tiles):
    tiles = d_context.shape[0] // TILE
    wide = PAIRS * BLK

    def short_map(tile, group, *_):
        return (short_index(tile, short_tiles), jnp.where(tile < short_tiles, group, GROUPS - 1), 0, 0, 0)

    def long_map(tile, group, *_):
        return (long_index(tile, short_tiles), jnp.where(tile < short_tiles, 0, group), 0, 0, 0)

    rows = pl.BlockSpec((TILE, wide), lambda tile, group, *_: (tile, group))
    row = pl.BlockSpec((1, D), lambda tile, group, *_: (0, 0))
    flops = 10 * D * TILE * TILE * tiles + 6 * D * D * TILE * tiles
    return pl.pallas_call(
        partial(attention_back_kernel, short_tiles=short_tiles),
        grid_spec=pltpu.PrefetchScalarGridSpec(
            num_scalar_prefetch=1,
            grid=(tiles, GROUPS),
            in_specs=[
                rows,
                rows,
                rows,
                pl.BlockSpec((1, PAIRS) + probs_short.shape[2:], short_map),
                pl.BlockSpec((1, PAIRS) + probs_long.shape[2:], long_map),
                rows,
                pl.BlockSpec((TILE, D), lambda tile, group, *_: (tile, 0)),
                pl.BlockSpec(memory_space=pl.ANY),
            ],
            out_specs=[
                rows,
                rows,
                rows,
                pl.BlockSpec((TILE, D), lambda tile, group, *_: (short_index(tile, short_tiles), 0)),
                pl.BlockSpec((TILE, D), lambda tile, group, *_: (long_index(tile, short_tiles), 0)),
                row,
                row,
            ],
            scratch_shapes=[pltpu.VMEM((D, 3 * D), BF16), pltpu.SemaphoreType.DMA],
        ),
        out_shape=[
            jax.ShapeDtypeStruct((tiles * TILE, D), BF16),
            jax.ShapeDtypeStruct((tiles * TILE, D), BF16),
            jax.ShapeDtypeStruct((tiles * TILE, D), BF16),
            jax.ShapeDtypeStruct((short_tiles * TILE, D), F32),
            jax.ShapeDtypeStruct(((tiles - short_tiles) * TILE, D), F32),
            jax.ShapeDtypeStruct((1, D), F32),
            jax.ShapeDtypeStruct((1, D), F32),
        ],
        compiler_params=pltpu.CompilerParams(
            vmem_limit_bytes=56 * MIB, fuse_transposed_lhs_in_matmul=True
        ),
        cost_estimate=pl.CostEstimate(flops=flops, bytes_accessed=50 * MIB, transcendentals=0),
        name="attention_back",
    )(block_slot, *qkv, probs_short, probs_long, d_context, resid, blocks)


def normal_parts(values):
    below = 0.5 * lax.erf(values * 0.7071067811865476) + 0.5
    return below, jnp.exp(-0.5 * values * values) * 0.3989422804014327


def norm_parts(values):
    center = values - jnp.mean(values, axis=-1, keepdims=True)
    spread = jnp.mean(center * center, axis=-1, keepdims=True)
    inverse = lax.rsqrt(spread + NORM_EPSILON)
    return center * inverse, inverse


def norm_back(d_values, gain, unit, inverse):
    d_unit = d_values * gain
    return inverse * (
        d_unit
        - jnp.mean(d_unit, axis=-1, keepdims=True)
        - unit * jnp.mean(d_unit * unit, axis=-1, keepdims=True)
    )


def column_sum(values):
    return jnp.sum(values.astype(F32), axis=0, keepdims=True)


def pool_weights(student, query, length):
    scaled = student * query
    lane = lax.broadcasted_iota(jnp.int32, scaled.shape, 1)
    place = lax.broadcasted_iota(jnp.int32, (scaled.shape[0], 1), 0)
    weights = []
    for side in (lane < SD // PH, lane >= SD // PH):
        scores = jnp.sum(jnp.where(side, scaled, 0.0), axis=-1, keepdims=True)
        scores = jnp.where(place < length, scores, MASKED_SCORE)
        powers = jnp.exp(scores - jnp.max(scores, axis=0, keepdims=True))
        weights.append(powers / jnp.sum(powers, axis=0, keepdims=True))
    return jnp.where(lane < SD // PH, weights[0], weights[1]), weights


def student_back(student, query, weights, both, d_pooled):
    lane = lax.broadcasted_iota(jnp.int32, student.shape, 1)
    moved = student * d_pooled
    d_scores = []
    for side, weight in zip((lane < SD // PH, lane >= SD // PH), weights):
        d_weight = jnp.sum(jnp.where(side, moved, 0.0), axis=-1, keepdims=True)
        d_scores.append(weight * (d_weight - jnp.sum(weight * d_weight, axis=0, keepdims=True)))
    d_score = jnp.where(lane < SD // PH, d_scores[0], d_scores[1])
    d_query = jnp.sum(d_score * student, axis=0, keepdims=True) * 0.125
    return both * d_pooled + d_score * query, d_query


def feed_kernel(
    len_short,
    len_long,
    slot_ref,
    x_ref,
    context_ref,
    cot_short_ref,
    cot_long_ref,
    logit_cot_ref,
    b_out,
    gain_one,
    shift_one,
    b_up,
    b_down,
    gain_two,
    shift_two,
    b_student,
    pool_query,
    b_hidden,
    w_class,
    b_class,
    blocks,
    enc_short_ref,
    enc_long_ref,
    logit_ref,
    first_ref,
    active_ref,
    d_up_ref,
    d_down_ref,
    d_branch_ref,
    d_context_ref,
    d_resid_ref,
    g_student,
    g_hidden,
    g_b_out,
    g_gain_one,
    g_shift_one,
    g_b_up,
    g_b_down,
    g_gain_two,
    g_shift_two,
    g_b_student,
    g_pool_query,
    g_b_hidden,
    g_w_class,
    g_b_class,
    slope,
    pooled_ref,
    d_student_ref,
    w_out,
    w_up,
    w_down,
    w_student,
    w_hidden,
    sems,
    *,
    short_tiles,
    width,
):
    tile = pl.program_id(0)
    per_tile = TILE // width

    @pl.when(tile == 0)
    def _():
        for ref in (
            g_student,
            g_hidden,
            g_b_out,
            g_gain_one,
            g_shift_one,
            g_b_up,
            g_b_down,
            g_gain_two,
            g_shift_two,
            g_b_student,
            g_pool_query,
            g_b_hidden,
            g_w_class,
            g_b_class,
        ):
            ref[...] = jnp.zeros_like(ref)

    loads = ((w_out, 108, 6, 6), (w_up, 144, 6, 24), (w_down, 288, 24, 6), (w_student, 432, 6, 1), (w_hidden, 438, 1, 1))

    @pl.when(tile == 0)
    def _():
        for index, (target, block, row_count, col_count) in enumerate(loads):
            load_blocks(slot_ref, blocks, target, sems.at[index], block, row_count, col_count)
        for index, (target, *_) in enumerate(loads):
            wait_whole(target, sems.at[index])

    branch = product(context_ref[...], w_out[...]) + b_out[...]
    unit_one, inverse_one = norm_parts(x_ref[...].astype(F32) + branch)
    first = (unit_one * gain_one[...] + shift_one[...]).astype(BF16)
    first_ref[...] = first
    for start in range(0, FF, CHUNK):
        cols = slice(start, start + CHUNK)
        upward = product(first, w_up[:, cols]) + b_up[:, cols]
        below, density = normal_parts(upward)
        active_ref[:, cols] = (upward * below).astype(BF16)
        slope[:, cols] = (below + upward * density).astype(BF16)
    downward = product(active_ref[...], w_down[...]) + b_down[...]
    unit_two, inverse_two = norm_parts(first.astype(F32) + downward)
    encoded = (unit_two * gain_two[...] + shift_two[...]).astype(BF16)

    @pl.when(tile < short_tiles)
    def _():
        enc_short_ref[...] = encoded

    @pl.when(tile >= short_tiles)
    def _():
        enc_long_ref[...] = encoded

    student = product(encoded, w_student[...]) + b_student[...]
    query = pool_query[...] * 0.125
    pooled_ref[...] = jnp.zeros_like(pooled_ref)

    def head():
        pooled = pooled_ref[...]
        wide_hidden = w_hidden[...].astype(F32)
        hidden = jnp.tanh(product(pooled, wide_hidden, HIGHEST_PRECISION) + b_hidden[...])
        logit_ref[0] = product(hidden, w_class[...], HIGHEST_PRECISION) + b_class[...]
        d_logits = logit_cot_ref[0]
        g_b_class[...] += column_sum(d_logits)
        g_w_class[...] += left_product(hidden, d_logits, HIGHEST_PRECISION)
        d_hidden = right_product(d_logits, w_class[...], HIGHEST_PRECISION)
        d_hidden = d_hidden * (1.0 - hidden * hidden)
        g_b_hidden[...] += column_sum(d_hidden)
        g_hidden[...] += left_product(pooled, d_hidden, HIGHEST_PRECISION)
        return right_product(d_hidden, wide_hidden, HIGHEST_PRECISION)

    def pool(starts, size, lengths):
        kept = []
        for index, (start, length) in enumerate(zip(starts, lengths)):
            rows = student[start : start + size]
            both, weights = pool_weights(rows, query, length)
            pooled_ref[index : index + 1, :] = column_sum(both * rows)
            kept.append((start, rows, both, weights))
        d_pooled = head()
        for index, (start, rows, both, weights) in enumerate(kept):
            d_rows, d_query = student_back(rows, query, weights, both, d_pooled[index : index + 1])
            d_student_ref[start : start + size, :] = d_rows.astype(BF16)
            g_pool_query[...] += d_query

    @pl.when(tile < short_tiles)
    def _():
        pool(
            [seq * width for seq in range(per_tile)],
            width,
            [len_short[tile * per_tile + seq] for seq in range(per_tile)],
        )

    @pl.when(tile >= short_tiles)
    def _():
        pool([0], TILE, [len_long[tile - short_tiles]])

    d_student = d_student_ref[...]
    g_b_student[...] += column_sum(d_student)
    g_student[...] += left_product(encoded, d_student)
    cotangent = jnp.where(tile < short_tiles, cot_short_ref[...], cot_long_ref[...])
    d_second = cotangent.astype(F32) + right_product(d_student, w_student[...])
    g_gain_two[...] += column_sum(d_second * unit_two)
    g_shift_two[...] += column_sum(d_second)
    d_resid_two = norm_back(d_second, gain_two[...], unit_two, inverse_two)
    d_down = d_resid_two.astype(BF16)
    d_down_ref[...] = d_down
    g_b_down[...] += column_sum(d_down)
    for start in range(0, FF, CHUNK):
        cols = slice(start, start + CHUNK)
        d_active = right_product(d_down, w_down[cols, :])
        d_up = (d_active * slope[:, cols].astype(F32)).astype(BF16)
        d_up_ref[:, cols] = d_up
        g_b_up[:, cols] += column_sum(d_up)
    d_first = d_resid_two + right_product(d_up_ref[...], w_up[...])
    g_gain_one[...] += column_sum(d_first * unit_one)
    g_shift_one[...] += column_sum(d_first)
    d_resid_one = norm_back(d_first, gain_one[...], unit_one, inverse_one)
    d_resid_ref[...] = d_resid_one
    d_branch = d_resid_one.astype(BF16)
    d_branch_ref[...] = d_branch
    g_b_out[...] += column_sum(d_branch)
    d_context_ref[...] = right_product(d_branch, w_out[...]).astype(BF16)


def feed(len_short, len_long, block_slot, x, context, cot_short, cot_long, logit_cot, vectors, blocks, short_tiles, width):
    tiles = x.shape[0] // TILE
    long_tiles = tiles - short_tiles

    def whole(shape):
        return pl.BlockSpec(shape, lambda tile, *_: (0,) * len(shape), pipeline_mode=pl.Buffered(1))

    def kept(shape):
        return pl.BlockSpec(shape, lambda tile, *_: (0,) * len(shape))

    def rows(columns):
        return pl.BlockSpec((TILE, columns), lambda tile, *_: (tile, 0))

    short_rows = pl.BlockSpec((TILE, D), lambda tile, *_: (short_index(tile, short_tiles), 0))
    long_rows = pl.BlockSpec((TILE, D), lambda tile, *_: (long_index(tile, short_tiles), 0))
    logit_rows = pl.BlockSpec((1, 8, SD), lambda tile, *_: (tile, 0, 0))
    grad_shapes = (
        (D, SD),
        (SD, SD),
        (1, D),
        (1, D),
        (1, D),
        (1, FF),
        (1, D),
        (1, D),
        (1, D),
        (1, SD),
        (1, SD),
        (1, SD),
        (SD, SD),
        (1, SD),
    )
    total = tiles * TILE
    return pl.pallas_call(
        partial(feed_kernel, short_tiles=short_tiles, width=width),
        grid_spec=pltpu.PrefetchScalarGridSpec(
            num_scalar_prefetch=3,
            grid=(tiles,),
            in_specs=[rows(D), rows(D), short_rows, long_rows, logit_rows]
            + [whole(vector.shape) for vector in vectors]
            + [pl.BlockSpec(memory_space=pl.ANY)],
            out_specs=[
                short_rows,
                long_rows,
                logit_rows,
                rows(D),
                rows(FF),
                rows(FF),
                rows(D),
                rows(D),
                rows(D),
                rows(D),
            ]
            + [kept(shape) for shape in grad_shapes],
            scratch_shapes=[
                pltpu.VMEM((TILE, FF), BF16),
                pltpu.VMEM((8, SD), F32),
                pltpu.VMEM((TILE, SD), BF16),
                pltpu.VMEM((D, D), BF16),
                pltpu.VMEM((D, FF), BF16),
                pltpu.VMEM((FF, D), BF16),
                pltpu.VMEM((D, SD), BF16),
                pltpu.VMEM((SD, SD), BF16),
                pltpu.SemaphoreType.DMA((5,)),
            ],
        ),
        out_shape=[
            jax.ShapeDtypeStruct((short_tiles * TILE, D), BF16),
            jax.ShapeDtypeStruct((long_tiles * TILE, D), BF16),
            jax.ShapeDtypeStruct((tiles, 8, SD), F32),
            jax.ShapeDtypeStruct((total, D), BF16),
            jax.ShapeDtypeStruct((total, FF), BF16),
            jax.ShapeDtypeStruct((total, FF), BF16),
            jax.ShapeDtypeStruct((total, D), BF16),
            jax.ShapeDtypeStruct((total, D), BF16),
            jax.ShapeDtypeStruct((total, D), BF16),
            jax.ShapeDtypeStruct((total, D), F32),
        ]
        + [jax.ShapeDtypeStruct(shape, F32) for shape in grad_shapes],
        compiler_params=pltpu.CompilerParams(vmem_limit_bytes=60 * MIB),
        cost_estimate=pl.CostEstimate(
            flops=total * (8 * D * FF + 4 * D * D), bytes_accessed=70 * MIB, transcendentals=total * FF
        ),
        name="feed",
    )(len_short, len_long, block_slot, x, context, cot_short, cot_long, logit_cot, *vectors, blocks)


class Place:
    def __init__(self):
        self.quarter = lax.axis_index("dp")
        self.shard = lax.axis_index("fsdp")
        x = self.quarter % 2
        y = self.quarter // 2
        self.core = self.shard % 2
        self.z = self.shard // 2
        self.high = self.z // 2
        self.by_x = 2 * y + 1 - x
        self.by_y = 2 * (1 - y) + x
        self.across = 2 * (1 - y) + 1 - x
        self.sibling = (self.quarter, 2 * self.z + 1 - self.core)
        self.next_x = (self.by_x, self.shard)
        self.next_y = (self.by_y, self.shard)
        self.inner = (self.z > 0) & (self.z < 3)

    def at_z(self, z):
        return (self.quarter, 2 * z + self.core)


def send(source, target, send_sem, recv_sem, device):
    copy = pltpu.make_async_remote_copy(
        src_ref=source,
        dst_ref=target,
        send_sem=send_sem,
        recv_sem=recv_sem,
        device_id=device,
        device_id_type=pl.DeviceIdType.MESH,
    )
    copy.start()
    return copy


def landing(target, send_sem, recv_sem, device):
    return pltpu.make_async_remote_copy(
        src_ref=target,
        dst_ref=target,
        send_sem=send_sem,
        recv_sem=recv_sem,
        device_id=device,
        device_id_type=pl.DeviceIdType.MESH,
    )


def greet(place, extra=()):
    barrier = pltpu.get_barrier_semaphore()

    def signal(device):
        pl.semaphore_signal(barrier, inc=1, device_id=device, device_id_type=pl.DeviceIdType.MESH)

    near = (place.sibling, place.next_x, place.next_y) + tuple(extra)
    for device in near:
        signal(device)

    @pl.when(place.z > 0)
    def _():
        signal(place.at_z(place.z - 1))

    @pl.when(place.z < 3)
    def _():
        signal(place.at_z(place.z + 1))

    pl.semaphore_wait(barrier, len(near) + 1 + (place.z + 1) // 2 % 2)


def gather_kernel(
    master_ref,
    out_ref,
    full,
    own_send,
    relay_send,
    z_recv,
    xy_send,
    xy_recv,
    core_send,
    core_recv,
    out_sems,
):
    place = Place()
    z, core, shard = place.z, place.core, place.shard
    rows = master_ref.shape[0]
    quarter = rows // 4
    half = quarter // 2

    full[shard] = master_ref[...].astype(BF16)
    greet(place)

    def region(which, start, size):
        return full.at[which, pl.ds(pl.multiple_of(start, 16), size)]

    stores = []
    sends = []

    def to_core(index, ref):
        sends.append(send(ref, ref, core_send.at[index], core_recv.at[index], place.sibling))

    def store(index, which):
        copy = pltpu.make_async_copy(full.at[which], out_ref.at[which], out_sems.at[index])
        copy.start()
        stores.append(copy)

    mine = region(shard, place.quarter * quarter, quarter)

    @pl.when(z > 0)
    def _():
        send(mine, mine, own_send.at[0], z_recv.at[z], place.at_z(z - 1))

    @pl.when(z < 3)
    def _():
        send(mine, mine, own_send.at[1], z_recv.at[z], place.at_z(z + 1))

    whole = full.at[shard]
    own_core = send(whole, whole, core_send.at[0], core_recv.at[0], place.sibling)
    store(0, shard)

    origins = (z + 1 - 2 * (z % 2), 2 - place.high, 3 * (1 - place.high))
    relays = (3 - z, 3 * (z - 1), 3 * (z - 1))
    kept = []

    def arrive_xy(step):
        pieces = kept[step]
        base = 1 + 5 * step
        landing(pieces[1], xy_send.at[4 * step], xy_recv.at[4 * step], place.next_x).wait_recv()
        first = pieces[1].at[pl.ds(0, half)]
        sends.append(send(first, first, xy_send.at[4 * step + 2], xy_recv.at[4 * step + 2], place.next_y))
        to_core(base + 1, pieces[1])
        landing(pieces[2], xy_send.at[4 * step + 1], xy_recv.at[4 * step + 1], place.next_y).wait_recv()
        last = pieces[2].at[pl.ds(half, half)]
        sends.append(send(last, last, xy_send.at[4 * step + 3], xy_recv.at[4 * step + 3], place.next_x))
        to_core(base + 2, pieces[2])

    def arrive_across(step):
        pieces = kept[step]
        base = 1 + 5 * step
        landing(pieces[3], xy_send.at[4 * step + 2], xy_recv.at[4 * step + 2], place.next_y).wait_recv()
        to_core(base + 3, pieces[3])
        landing(pieces[4], xy_send.at[4 * step + 3], xy_recv.at[4 * step + 3], place.next_x).wait_recv()
        to_core(base + 4, pieces[4])
        store(2 + 2 * step, kept[step][5])

    def arrive_core(step):
        for index, (start, size) in enumerate(
            (
                (place.quarter * quarter, quarter),
                (place.by_x * quarter, quarter),
                (place.by_y * quarter, quarter),
                (place.across * quarter, half),
                (place.across * quarter + half, half),
            )
        ):
            ref = region(kept[step][6], start, size)
            landing(
                ref, core_send.at[1 + 5 * step + index], core_recv.at[1 + 5 * step + index], place.sibling
            ).wait_recv()
        store(3 + 2 * step, kept[step][6])

    for step in range(3):
        origin = origins[step]
        which = 2 * origin + core
        piece = region(which, place.quarter * quarter, quarter)
        landing(piece, relay_send.at[step], z_recv.at[origin], place.next_x).wait_recv()

        @pl.when(place.inner)
        def _():
            send(piece, piece, relay_send.at[step], z_recv.at[origin], place.at_z(relays[step]))

        sends.append(send(piece, piece, xy_send.at[4 * step], xy_recv.at[4 * step], place.next_x))
        sends.append(send(piece, piece, xy_send.at[4 * step + 1], xy_recv.at[4 * step + 1], place.next_y))
        to_core(1 + 5 * step, piece)
        kept.append(
            (
                piece,
                region(which, place.by_x * quarter, quarter),
                region(which, place.by_y * quarter, quarter),
                region(which, place.across * quarter, half),
                region(which, place.across * quarter + half, half),
                which,
                2 * origin + 1 - core,
            )
        )
        if step >= 1:
            arrive_xy(step - 1)
        if step >= 2:
            arrive_across(step - 2)
    sibling_whole = full.at[2 * z + 1 - core]
    landing(sibling_whole, core_send.at[0], core_recv.at[0], place.sibling).wait_recv()
    store(1, 2 * z + 1 - core)
    arrive_xy(2)
    arrive_across(1)
    arrive_core(0)
    arrive_across(2)
    arrive_core(1)
    arrive_core(2)

    @pl.when(z > 0)
    def _():
        landing(mine, own_send.at[0], z_recv.at[z], place.at_z(z - 1)).wait_send()

    @pl.when(z < 3)
    def _():
        landing(mine, own_send.at[1], z_recv.at[z], place.at_z(z + 1)).wait_send()

    for step in range(3):

        @pl.when(place.inner)
        def _():
            landing(
                kept[step][0], relay_send.at[step], z_recv.at[0], place.at_z(relays[step])
            ).wait_send()

    own_core.wait_send()
    for copy in sends:
        copy.wait_send()
    for copy in stores:
        copy.wait()


def gather_shards(master):
    slot_count = master.shape[0]
    rows = slot_count * BLK
    shards = lax.axis_size("fsdp")
    full = pl.pallas_call(
        gather_kernel,
        in_specs=[pl.BlockSpec(memory_space=pltpu.VMEM)],
        out_specs=pl.BlockSpec(memory_space=pl.ANY),
        out_shape=jax.ShapeDtypeStruct((shards, rows, BLK), BF16),
        scratch_shapes=[
            pltpu.VMEM((shards, rows, BLK), BF16),
            pltpu.SemaphoreType.DMA((2,)),
            pltpu.SemaphoreType.DMA((3,)),
            pltpu.SemaphoreType.DMA((4,)),
            pltpu.SemaphoreType.DMA((12,)),
            pltpu.SemaphoreType.DMA((12,)),
            pltpu.SemaphoreType.DMA((16,)),
            pltpu.SemaphoreType.DMA((16,)),
            pltpu.SemaphoreType.DMA((8,)),
        ],
        compiler_params=pltpu.CompilerParams(
            collective_id=0, has_side_effects=True, vmem_limit_bytes=32 * MIB
        ),
        cost_estimate=pl.CostEstimate(flops=0, bytes_accessed=200 * MIB, transcendentals=0),
        name="gather",
    )(master.reshape(rows, BLK))
    return full.reshape(shards * slot_count, BLK, BLK)


SMALL_ROWS = 96


def add_rows(target, former, latter, rows, step):
    @pl.loop(0, rows // step)
    def _(index):
        part = pl.ds(pl.multiple_of(index * step, 16), step)
        target[part] = (former[part].astype(F32) + latter[part].astype(F32)).astype(BF16)


def reduce_kernel(
    terms,
    small_ref,
    out_ref,
    small_out,
    mine,
    sib,
    from_x,
    from_y,
    late_y,
    late_x,
    from_z,
    small_in,
    small_sum,
    load_sems,
    core_send,
    core_recv,
    xy_send,
    xy_recv,
    z_send,
    z_recv,
    last_send,
    last_recv,
    small_send,
    small_recv,
):
    place = Place()
    z, core = place.z, place.core
    rows = terms.shape[1]
    quarter = rows // 4
    half = quarter // 2
    far = place.at_z(z + 2 - 4 * place.high)
    near = place.at_z(z + 1 - 2 * (z % 2))
    greet(place, (far,))

    low_z = 1 - place.high
    order = (
        3 * low_z,
        low_z * (2 - 2 * z) + place.high * (7 - 2 * z),
        1 + z % 2,
        z,
    )
    onward = (z + 1 - 2 * place.high, z + 1 - 2 * (z % 2), z + 1 - 2 * place.high)
    closing = (0, (z % 2) * low_z, place.high)

    sends = []
    loads = []
    small_sum[0] = small_ref[...]
    small_partners = (place.sibling, place.next_x, place.next_y, near, far)

    def small_step(level):
        if level > 0:
            landing(
                small_in.at[level - 1],
                small_send.at[level - 1],
                small_recv.at[level - 1],
                small_partners[level - 1],
            ).wait_recv()
            small_sum[level] = small_sum[level - 1] + small_in[level - 1]
        if level < 5:
            sends.append(
                send(
                    small_sum.at[level],
                    small_in.at[level],
                    small_send.at[level],
                    small_recv.at[level],
                    small_partners[level],
                )
            )

    for step in range(4):
        goal = order[step]
        load = pltpu.make_async_copy(terms.at[2 * goal + core], mine.at[step], load_sems.at[step])
        load.start()
        loads.append(load)
        sends.append(
            send(
                terms.at[2 * goal + 1 - core],
                sib.at[step],
                core_send.at[step],
                core_recv.at[step],
                place.sibling,
            )
        )
        if step == 0:
            small_step(0)

    def part(step, which, side):
        start = pl.multiple_of(which * quarter + side * half, 16)
        return mine.at[step, pl.ds(start, half)]

    def stage_core(step):
        loads[step].wait()
        landing(sib.at[step], core_send.at[step], core_recv.at[step], place.sibling).wait_recv()
        for index, which in enumerate((place.by_x, place.across, place.by_y, place.quarter)):
            start = pl.multiple_of(which * quarter, 16)
            block = pl.ds(start, quarter)
            add_rows(mine.at[step, block], mine.at[step, block], sib.at[step, block], quarter, half)
            if which is place.across:
                for slot, source in enumerate((place.by_x, place.across)):
                    sends.append(
                        send(
                            part(step, source, 0),
                            from_x.at[step, slot],
                            xy_send.at[6 * step + slot],
                            xy_recv.at[6 * step + slot],
                            place.next_x,
                        )
                    )
            if which is place.by_y:
                for slot, source in enumerate((place.by_y, place.across)):
                    sends.append(
                        send(
                            part(step, source, 1),
                            from_y.at[step, slot],
                            xy_send.at[6 * step + 2 + slot],
                            xy_recv.at[6 * step + 2 + slot],
                            place.next_y,
                        )
                    )

    def take(target, source, index, device):
        landing(source, xy_send.at[index], xy_recv.at[index], device).wait_recv()
        add_rows(target, target, source, half, half)

    def stage_first(step):
        base = 6 * step
        take(part(step, place.by_y, 0), from_x.at[step, 1], base + 1, place.next_x)
        sends.append(
            send(
                part(step, place.by_y, 0),
                late_y.at[step],
                xy_send.at[base + 4],
                xy_recv.at[base + 4],
                place.next_y,
            )
        )
        take(part(step, place.by_x, 1), from_y.at[step, 1], base + 3, place.next_y)
        sends.append(
            send(
                part(step, place.by_x, 1),
                late_x.at[step],
                xy_send.at[base + 5],
                xy_recv.at[base + 5],
                place.next_x,
            )
        )
        take(part(step, place.quarter, 0), from_x.at[step, 0], base, place.next_x)
        take(part(step, place.quarter, 1), from_y.at[step, 0], base + 2, place.next_y)

    def own_block(step):
        return mine.at[step, pl.ds(pl.multiple_of(place.quarter * quarter, 16), quarter)]

    def stage_second(step):
        base = 6 * step
        take(part(step, place.quarter, 0), late_y.at[step], base + 4, place.next_y)
        take(part(step, place.quarter, 1), late_x.at[step], base + 5, place.next_x)
        block = own_block(step)
        goal = order[step]
        if step < 3:

            @pl.when(place.inner)
            def _():
                landing(from_z.at[goal], z_send.at[step], z_recv.at[goal], near).wait_recv()
                add_rows(block, block, from_z.at[goal], quarter, half)

            slot = goal + closing[step] * (4 - goal)
            sends.append(
                send(
                    block, from_z.at[slot], z_send.at[step], z_recv.at[slot], place.at_z(onward[step])
                )
            )
        else:

            @pl.when(z > 0)
            def _():
                landing(from_z.at[z], z_send.at[0], z_recv.at[z], near).wait_recv()
                add_rows(block, block, from_z.at[z], quarter, half)

            @pl.when(z < 3)
            def _():
                landing(from_z.at[4], z_send.at[0], z_recv.at[4], near).wait_recv()
                add_rows(block, block, from_z.at[4], quarter, half)

    stage_core(0)
    small_step(1)
    stage_core(1)
    stage_first(0)
    small_step(2)
    stage_core(2)
    stage_first(1)
    stage_second(0)
    small_step(3)
    stage_core(3)
    stage_first(2)
    stage_second(1)
    small_step(4)
    stage_first(3)
    stage_second(2)
    small_step(5)
    small_out[...] = small_sum[5]
    stage_second(3)

    def final(which, side=None):
        start = pl.multiple_of(which * quarter + (0 if side is None else side * half), 16)
        return out_ref.at[pl.ds(start, quarter if side is None else half)]

    final(place.quarter)[...] = own_block(3)[...]
    own = final(place.quarter)
    sends.append(send(own, own, last_send.at[0], last_recv.at[0], place.next_x))
    sends.append(send(own, own, last_send.at[1], last_recv.at[1], place.next_y))
    landing(final(place.by_x), last_send.at[0], last_recv.at[0], place.next_x).wait_recv()
    piece = final(place.by_x, 0)
    sends.append(send(piece, piece, last_send.at[2], last_recv.at[2], place.next_y))
    landing(final(place.by_y), last_send.at[1], last_recv.at[1], place.next_y).wait_recv()
    piece = final(place.by_y, 1)
    sends.append(send(piece, piece, last_send.at[3], last_recv.at[3], place.next_x))
    landing(final(place.across, 0), last_send.at[2], last_recv.at[2], place.next_y).wait_recv()
    landing(final(place.across, 1), last_send.at[3], last_recv.at[3], place.next_x).wait_recv()
    for copy in sends:
        copy.wait_send()


def reduce_shards(terms, small):
    all_slots = terms.shape[0]
    shards = lax.axis_size("fsdp")
    rows = all_slots // shards * BLK
    quarter = rows // 4
    half = quarter // 2
    vmem = pl.BlockSpec(memory_space=pltpu.VMEM)
    padded = jnp.pad(small, (0, SMALL_ROWS * BLK - small.shape[0])).reshape(SMALL_ROWS, BLK)
    shard, total = pl.pallas_call(
        reduce_kernel,
        in_specs=[pl.BlockSpec(memory_space=pl.ANY), vmem],
        out_specs=[vmem, vmem],
        out_shape=[
            jax.ShapeDtypeStruct((rows, BLK), BF16),
            jax.ShapeDtypeStruct((SMALL_ROWS, BLK), F32),
        ],
        scratch_shapes=[
            pltpu.VMEM((4, rows, BLK), BF16),
            pltpu.VMEM((4, rows, BLK), BF16),
            pltpu.VMEM((4, 2, half, BLK), BF16),
            pltpu.VMEM((4, 2, half, BLK), BF16),
            pltpu.VMEM((4, half, BLK), BF16),
            pltpu.VMEM((4, half, BLK), BF16),
            pltpu.VMEM((5, quarter, BLK), BF16),
            pltpu.VMEM((5, SMALL_ROWS, BLK), F32),
            pltpu.VMEM((6, SMALL_ROWS, BLK), F32),
            pltpu.SemaphoreType.DMA((4,)),
            pltpu.SemaphoreType.DMA((4,)),
            pltpu.SemaphoreType.DMA((4,)),
            pltpu.SemaphoreType.DMA((24,)),
            pltpu.SemaphoreType.DMA((24,)),
            pltpu.SemaphoreType.DMA((3,)),
            pltpu.SemaphoreType.DMA((5,)),
            pltpu.SemaphoreType.DMA((4,)),
            pltpu.SemaphoreType.DMA((4,)),
            pltpu.SemaphoreType.DMA((5,)),
            pltpu.SemaphoreType.DMA((5,)),
        ],
        compiler_params=pltpu.CompilerParams(
            collective_id=1, has_side_effects=True, vmem_limit_bytes=48 * MIB
        ),
        cost_estimate=pl.CostEstimate(flops=0, bytes_accessed=400 * MIB, transcendentals=0),
        name="reduce",
    )(terms.reshape(shards, rows, BLK), padded)
    return shard.reshape(all_slots // shards, BLK, BLK), total.reshape(-1)[: small.shape[0]]


def body(
    x_short,
    x_long,
    cot_short,
    cot_long,
    logit_cot_short,
    logit_cot_long,
    len_short,
    len_long,
    block_slot,
    master,
    left_stat,
    right_stat,
    left_root,
    right_root,
    small_params,
    small_first,
    small_second,
    own_transfers,
):
    slot_count = master.shape[0]
    all_slots = slot_count * lax.axis_size("fsdp")
    short_seqs, width = x_short.shape[:2]
    long_seqs = x_long.shape[0]
    short_tiles = short_seqs * width // TILE
    per_tile = TILE // width

    if own_transfers:
        gathered = gather_shards(master)
    else:
        gathered = lax.all_gather(master.astype(BF16), "fsdp", axis=0, tiled=True)
    (
        b_query,
        b_value,
        b_out,
        gain_one,
        shift_one,
        b_up,
        b_down,
        gain_two,
        shift_two,
        b_student,
        pool_query,
        b_hidden,
        w_class,
        b_class,
    ) = unpack(small_params)
    vectors = [
        vector.reshape(1, -1)
        for vector in (b_out, gain_one, shift_one, b_up, b_down, gain_two, shift_two, b_student, pool_query, b_hidden)
    ]
    vectors.append(jnp.pad(w_class.reshape(SD, NCLS), ((0, 0), (0, SD - NCLS))))
    vectors.append(jnp.pad(b_class.reshape(1, NCLS), ((0, 0), (0, SD - NCLS))))

    x = jnp.concatenate([x_short.reshape(-1, D), x_long.reshape(-1, D)], axis=0)
    *qkv, context, probs_short, probs_long = attention(
        len_short,
        len_long,
        block_slot,
        x,
        b_query.reshape(1, D),
        b_value.reshape(1, D),
        gathered,
        short_tiles,
        width,
    )

    logit_cot = jnp.concatenate(
        [
            jnp.pad(
                logit_cot_short.reshape(short_tiles, per_tile, NCLS),
                ((0, 0), (0, 8 - per_tile), (0, SD - NCLS)),
            ),
            jnp.pad(logit_cot_long.reshape(long_seqs, 1, NCLS), ((0, 0), (0, 7), (0, SD - NCLS))),
        ],
        axis=0,
    )
    (
        enc_short,
        enc_long,
        logits,
        first,
        active,
        d_up,
        d_down,
        d_branch,
        d_context,
        d_resid,
        g_student,
        g_hidden,
        g_b_out,
        g_gain_one,
        g_shift_one,
        g_b_up,
        g_b_down,
        g_gain_two,
        g_shift_two,
        g_b_student,
        g_pool_query,
        g_b_hidden,
        g_w_class,
        g_b_class,
    ) = feed(
        len_short,
        len_long,
        block_slot,
        x,
        context,
        cot_short.reshape(-1, D),
        cot_long.reshape(-1, D),
        logit_cot,
        vectors,
        gathered,
        short_tiles,
        width,
    )
    g_down = left_product(active, d_down).astype(BF16)
    g_up = left_product(first, d_up).astype(BF16)
    g_out = left_product(context, d_branch).astype(BF16)
    d_query, d_key, d_value, in_short, in_long, g_b_query, g_b_value = attention_back(
        block_slot, qkv, probs_short, probs_long, d_context, d_resid, gathered, short_tiles
    )
    g_query = left_product(x, d_query).astype(BF16)
    g_key = left_product(x, d_key).astype(BF16)
    g_value = left_product(x, d_value).astype(BF16)

    used = jnp.ones((all_slots,), jnp.int32).at[block_slot].set(0)
    empty = jnp.nonzero(used, size=all_slots - NBLK)[0].astype(jnp.int32)
    slot_terms = spread(
        block_slot,
        empty,
        (g_query, g_key, g_value, g_out, g_up, g_down, g_student.astype(BF16), g_hidden.astype(BF16)),
        all_slots,
    )
    small_terms = jnp.concatenate(
        [
            vector.reshape(-1)
            for vector in (
                g_b_query,
                g_b_value,
                g_b_out,
                g_gain_one,
                g_shift_one,
                g_b_up,
                g_b_down,
                g_gain_two,
                g_shift_two,
                g_b_student,
                g_pool_query,
                g_b_hidden,
                g_w_class[:, :NCLS],
                g_b_class[:, :NCLS],
            )
        ]
    )
    if own_transfers:
        slot_grad, small_grad = reduce_shards(slot_terms, small_terms)
    else:
        shard_grad = lax.psum_scatter(slot_terms, "fsdp", scatter_dimension=0, tiled=True)
        slot_grad = lax.psum(shard_grad, "dp")
        small_grad = lax.psum(small_terms, ("dp", "fsdp"))
    slot_grad = slot_grad.astype(F32)
    outer_left = jnp.einsum("sij,skj->sik", slot_grad, slot_grad, precision=HIGHEST_PRECISION)
    outer_right = jnp.einsum("sji,sjk->sik", slot_grad, slot_grad, precision=HIGHEST_PRECISION)
    new_left = STAT_DECAY * left_stat + (1.0 - STAT_DECAY) * outer_left
    new_right = STAT_DECAY * right_stat + (1.0 - STAT_DECAY) * outer_right
    left_applied = jnp.einsum("sij,sjk->sik", left_root, slot_grad, precision=HIGHEST_PRECISION)
    conditioned = jnp.einsum("sij,sjk->sik", left_applied, right_root, precision=HIGHEST_PRECISION)
    new_master = master - MATRIX_RATE * conditioned
    new_first = BETA_ONE * small_first + (1.0 - BETA_ONE) * small_grad
    new_second = BETA_TWO * small_second + (1.0 - BETA_TWO) * small_grad * small_grad
    first_hat = new_first / (1.0 - BETA_ONE**STEP)
    second_hat = new_second / (1.0 - BETA_TWO**STEP)
    new_small = small_params - ADAM_RATE * first_hat / (jnp.sqrt(second_hat) + ADAM_EPSILON)
    return (
        enc_short.reshape(x_short.shape),
        logits[:short_tiles, :per_tile, :NCLS].reshape(short_seqs, NCLS),
        enc_long.reshape(x_long.shape),
        logits[short_tiles:, 0, :NCLS],
        in_short.reshape(x_short.shape),
        in_long.reshape(x_long.shape),
        slot_grad,
        new_left,
        new_right,
        new_master,
        new_first,
        new_second,
        new_small,
    )


def solution(mesh):
    both = ("dp", "fsdp")
    placed = (
        P(both, None, None),
        P(both, None, None),
        P(both, None, None),
        P(both, None, None),
        P(both, None),
        P(both, None),
        P(both),
        P(both),
        P(),
        P("fsdp", None, None),
        P("fsdp", None, None),
        P("fsdp", None, None),
        P("fsdp", None, None),
        P("fsdp", None, None),
        P(),
        P(),
        P(),
    )
    return jax.shard_map(
        partial(body, own_transfers=(mesh.shape["dp"], mesh.shape["fsdp"]) == (4, 8)),
        mesh=mesh,
        in_specs=placed,
        out_specs=(
            P(both, None, None),
            P(both, None),
            P(both, None, None),
            P(both, None),
            P(both, None, None),
            P(both, None, None),
            P("fsdp", None, None),
            P("fsdp", None, None),
            P("fsdp", None, None),
            P("fsdp", None, None),
            P(),
            P(),
            P(),
        ),
        check_vma=False,
    )
```

```python
from functools import partial

import jax
import jax.numpy as jnp
from jax import lax
from jax.experimental import pallas as pl
from jax.experimental.pallas import tpu as pltpu
from jax.sharding import PartitionSpec as P

D = 768
HEADS = 12
FF = 3072
SD = 128
PH = 2
NCLS = 14
BLK = 128
STEP = 10
NBLK = 439
TILE = 512
PAIRS = 3
GROUPS = 2
CHUNK = 256

NORM_EPSILON = 1e-12
BETA_ONE = 0.9
BETA_TWO = 0.999
ADAM_EPSILON = 1e-08
ADAM_RATE = 0.1
MATRIX_RATE = 0.2
STAT_DECAY = 0.5
MASKED_SCORE = -1e30
HIGHEST_PRECISION = lax.Precision.HIGHEST
MIB = 1024 * 1024
F32 = jnp.float32
BF16 = jnp.bfloat16

def product(former, latter, precision=None):
    return jnp.dot(former, latter, preferred_element_type=F32, precision=precision)


def left_product(former, latter, precision=None):
    return lax.dot_general(
        former, latter, (((0,), (0,)), ((), ())), preferred_element_type=F32, precision=precision
    )


def right_product(former, latter, precision=None):
    return lax.dot_general(
        former, latter, (((1,), (1,)), ((), ())), preferred_element_type=F32, precision=precision
    )


def unpack(small_values):
    widths = (D, D, D, D, D, FF, D, D, D, SD, SD, SD, SD * NCLS, NCLS)
    pieces = []
    offset = 0
    for column_count in widths:
        pieces.append(small_values[offset : offset + column_count])
        offset += column_count
    return pieces


def load_blocks(slot_ref, blocks, target, sem, first, row_count, col_count, col_start=0):
    def move(index, carry):
        row = pl.multiple_of((index // col_count) * BLK, BLK)
        col = pl.multiple_of((index % col_count + col_start) * BLK, BLK)
        pltpu.make_async_copy(
            blocks.at[slot_ref[first + index]],
            target.at[pl.ds(row, BLK), pl.ds(col, BLK)],
            sem,
        ).start()
        return carry

    lax.fori_loop(0, row_count * col_count, move, 0)


def wait_whole(target, sem):
    pltpu.make_async_copy(target, target, sem).wait()


def load_qkv(slot_ref, blocks, target, sem):
    load_blocks(slot_ref, blocks, target, sem, 0, 6, 6, 0)
    load_blocks(slot_ref, blocks, target, sem, 36, 6, 6, 6)
    load_blocks(slot_ref, blocks, target, sem, 72, 6, 6, 12)


SOURCES = (
    (0, 6, 6),
    (36, 6, 6),
    (72, 6, 6),
    (108, 6, 6),
    (144, 6, 24),
    (288, 24, 6),
    (432, 6, 1),
    (438, 1, 1),
)


def spread_kernel(slot_ref, empty_ref, *refs):
    grads = refs[: len(SOURCES)]
    zero, small_ref, query_ref, value_ref, out, small_out, sem = refs[len(SOURCES) :]
    for grad, (first, row_count, col_count) in zip(grads, SOURCES):

        def move(index, carry, grad=grad, first=first, col_count=col_count):
            row = pl.multiple_of((index // col_count) * BLK, BLK)
            col = pl.multiple_of((index % col_count) * BLK, BLK)
            pltpu.make_async_copy(
                grad.at[pl.ds(row, BLK), pl.ds(col, BLK)],
                out.at[slot_ref[first + index]],
                sem,
            ).start()
            return carry

        lax.fori_loop(0, row_count * col_count, move, 0)
    for index in range(empty_ref.shape[0]):
        pltpu.make_async_copy(zero, out.at[empty_ref[index]], sem).start()
    small_out[...] = small_ref[...]
    for start, ref in ((0, query_ref), (D // BLK, value_ref)):
        for index in range(D // BLK):
            small_out[start + index : start + index + 1, :] = ref[:, index * BLK : (index + 1) * BLK]
    pltpu.make_async_copy(out, out, sem).wait()


def spread(block_slot, empty, grads, small, g_query, g_value, slot_count):
    vmem = pl.BlockSpec(memory_space=pltpu.VMEM)
    return pl.pallas_call(
        spread_kernel,
        grid_spec=pltpu.PrefetchScalarGridSpec(
            num_scalar_prefetch=2,
            grid=(1,),
            in_specs=[vmem] * (len(grads) + 4),
            out_specs=[pl.BlockSpec(memory_space=pl.ANY), vmem],
            scratch_shapes=[pltpu.SemaphoreType.DMA],
        ),
        out_shape=[
            jax.ShapeDtypeStruct((slot_count, BLK, BLK), BF16),
            jax.ShapeDtypeStruct(small.shape, F32),
        ],
        compiler_params=pltpu.CompilerParams(vmem_limit_bytes=60 * MIB),
        name="spread",
    )(block_slot, empty, *grads, jnp.zeros((BLK, BLK), BF16), small, g_query, g_value)


def half_masks():
    lane = lax.broadcasted_iota(jnp.int32, (1, BLK), 1)
    low = (lane < BLK // 2).astype(BF16)
    return low, (1.0 - low.astype(F32)).astype(BF16)


def stack_heads(values, low, high):
    return jnp.concatenate([values * low, values * high], axis=0)


def pick_heads(values):
    rows = values.shape[0] // 2
    lane = lax.broadcasted_iota(jnp.int32, (rows, BLK), 1)
    return jnp.where(lane < BLK // 2, values[:rows], values[rows:])


def attend(queries, key_rows, value_rows, length, low, high, probs_ref):
    scores = right_product(stack_heads(queries, low, high), key_rows)
    visible = lax.broadcasted_iota(jnp.int32, (1, scores.shape[1]), 1) < length
    step = 16 * BLK * 8 // scores.shape[1]
    for start in range(0, scores.shape[0], step):
        rows = slice(start, start + step)
        part = jnp.where(visible, scores[rows], MASKED_SCORE)
        powers = jnp.exp(part - jnp.max(part, axis=-1, keepdims=True))
        total = jnp.sum(powers, axis=-1, keepdims=True)
        probs_ref[rows] = (powers * (1.0 / total)).astype(BF16)
    return pick_heads(product(probs_ref[...], value_rows)).astype(BF16)


def attention_kernel(
    len_short,
    len_long,
    slot_ref,
    x_ref,
    b_query,
    b_value,
    blocks,
    q_ref,
    k_ref,
    v_ref,
    context_ref,
    short_ref,
    long_ref,
    w_ref,
    sem,
    *,
    short_tiles,
):
    tile = pl.program_id(0)
    group = pl.program_id(1)
    low, high = half_masks()
    per_tile = TILE // short_ref.shape[-1]
    width = short_ref.shape[-1]

    @pl.when((tile == 0) & (group == 0))
    def _():
        load_qkv(slot_ref, blocks, w_ref, sem)
        wait_whole(w_ref, sem)

    wide = PAIRS * BLK
    start = pl.multiple_of(group * wide, wide)
    rows_in = x_ref[...]
    queries = product(rows_in, w_ref[:, pl.ds(start, wide)]) + b_query[:, pl.ds(start, wide)]
    q_ref[...] = (queries * 0.125).astype(BF16)
    k_ref[...] = product(rows_in, w_ref[:, pl.ds(D + start, wide)]).astype(BF16)
    values = product(rows_in, w_ref[:, pl.ds(2 * D + start, wide)]) + b_value[:, pl.ds(start, wide)]
    v_ref[...] = values.astype(BF16)

    @pl.when(tile < short_tiles)
    def _():
        for pair in range(PAIRS):
            cols = slice(pair * BLK, (pair + 1) * BLK)
            for seq in range(per_tile):
                rows = slice(seq * width, (seq + 1) * width)
                context_ref[rows, cols] = attend(
                    q_ref[rows, cols],
                    k_ref[rows, cols],
                    v_ref[rows, cols],
                    len_short[tile * per_tile + seq],
                    low,
                    high,
                    short_ref.at[0, pair, seq],
                )

    @pl.when(tile >= short_tiles)
    def _():
        length = len_long[tile - short_tiles]
        half = TILE // 2
        for pair in range(PAIRS):
            cols = slice(pair * BLK, (pair + 1) * BLK)
            for part in range(2):
                rows = slice(part * half, (part + 1) * half)
                context_ref[rows, cols] = attend(
                    q_ref[rows, cols],
                    k_ref[:, cols],
                    v_ref[:, cols],
                    length,
                    low,
                    high,
                    long_ref.at[0, pair, part],
                )


def probs_shapes(short_tiles, long_tiles, width):
    per_tile = TILE // width
    return (
        (short_tiles, 2 * PAIRS, per_tile, 2 * width, width),
        (long_tiles, 2 * PAIRS, 2, TILE, TILE),
    )


def short_index(tile, short_tiles):
    return jnp.minimum(tile, short_tiles - 1)


def long_index(tile, short_tiles):
    return jnp.maximum(tile - short_tiles, 0)


def attention(len_short, len_long, block_slot, x, b_query, b_value, blocks, short_tiles, width):
    tiles = x.shape[0] // TILE
    wide = PAIRS * BLK
    short_shape, long_shape = probs_shapes(short_tiles, tiles - short_tiles, width)

    def short_map(tile, group, *_):
        return (short_index(tile, short_tiles), jnp.where(tile < short_tiles, group, GROUPS - 1), 0, 0, 0)

    def long_map(tile, group, *_):
        return (long_index(tile, short_tiles), jnp.where(tile < short_tiles, 0, group), 0, 0, 0)

    flops = 4 * D * TILE * TILE * tiles + 6 * D * D * TILE * tiles
    rows = pl.BlockSpec((TILE, wide), lambda tile, group, *_: (tile, group))
    bias = pl.BlockSpec((1, D), lambda tile, group, *_: (0, 0))
    return pl.pallas_call(
        partial(attention_kernel, short_tiles=short_tiles),
        grid_spec=pltpu.PrefetchScalarGridSpec(
            num_scalar_prefetch=3,
            grid=(tiles, GROUPS),
            in_specs=[
                pl.BlockSpec((TILE, D), lambda tile, group, *_: (tile, 0)),
                bias,
                bias,
                pl.BlockSpec(memory_space=pl.ANY),
            ],
            out_specs=[
                rows,
                rows,
                rows,
                rows,
                pl.BlockSpec((1, PAIRS) + short_shape[2:], short_map),
                pl.BlockSpec((1, PAIRS) + long_shape[2:], long_map),
            ],
            scratch_shapes=[pltpu.VMEM((D, 3 * D), BF16), pltpu.SemaphoreType.DMA],
        ),
        out_shape=[jax.ShapeDtypeStruct((tiles * TILE, D), BF16)] * 4
        + [
            jax.ShapeDtypeStruct(short_shape, BF16),
            jax.ShapeDtypeStruct(long_shape, BF16),
        ],
        compiler_params=pltpu.CompilerParams(vmem_limit_bytes=60 * MIB),
        cost_estimate=pl.CostEstimate(
            flops=flops, bytes_accessed=35 * MIB, transcendentals=HEADS * TILE * TILE * tiles // 2
        ),
        name="attention",
    )(len_short, len_long, block_slot, x, b_query, b_value, blocks)


def attend_back(queries, key_rows, value_rows, d_context, probs_ref, low, high, scores_ref):
    stacked = stack_heads(d_context, low, high)
    d_probs = right_product(stacked, value_rows)
    step = 16 * BLK * 8 // d_probs.shape[1]
    for start in range(0, d_probs.shape[0], step):
        rows = slice(start, start + step)
        wide = probs_ref[rows].astype(F32)
        weighted = wide * d_probs[rows]
        scores_ref[rows] = (weighted - wide * jnp.sum(weighted, axis=-1, keepdims=True)).astype(BF16)
    d_scores = scores_ref[...]
    d_queries = pick_heads(product(d_scores, key_rows)) * 0.125
    d_keys = left_product(d_scores, stack_heads(queries, low, high))
    d_values = left_product(probs_ref[...], stacked)
    return d_queries.astype(BF16), d_keys, d_values


def attention_back_kernel(
    slot_ref,
    q_ref,
    k_ref,
    v_ref,
    short_ref,
    long_ref,
    dc_ref,
    resid_ref,
    blocks,
    dq_ref,
    dk_ref,
    dv_ref,
    in_short_ref,
    in_long_ref,
    bq_ref,
    bv_ref,
    w_ref,
    sem,
    narrow_ref,
    wide_ref,
    *,
    short_tiles,
):
    tile = pl.program_id(0)
    group = pl.program_id(1)
    low, high = half_masks()
    width = short_ref.shape[-1]
    per_tile = TILE // width
    first_step = (tile == 0) & (group == 0)

    @pl.when(first_step)
    def _():
        load_qkv(slot_ref, blocks, w_ref, sem)

    @pl.when(tile < short_tiles)
    def _():
        for pair in range(PAIRS):
            cols = slice(pair * BLK, (pair + 1) * BLK)
            for seq in range(per_tile):
                rows = slice(seq * width, (seq + 1) * width)
                d_queries, d_keys, d_values = attend_back(
                    q_ref[rows, cols],
                    k_ref[rows, cols],
                    v_ref[rows, cols],
                    dc_ref[rows, cols],
                    short_ref.at[0, pair, seq],
                    low,
                    high,
                    narrow_ref.at[(pair * per_tile + seq) % 2],
                )
                dq_ref[rows, cols] = d_queries
                dk_ref[rows, cols] = d_keys.astype(BF16)
                dv_ref[rows, cols] = d_values.astype(BF16)

    @pl.when(tile >= short_tiles)
    def _():
        half = TILE // 2
        for pair in range(PAIRS):
            cols = slice(pair * BLK, (pair + 1) * BLK)
            keys_sum = None
            values_sum = None
            for part in range(2):
                rows = slice(part * half, (part + 1) * half)
                d_queries, d_keys, d_values = attend_back(
                    q_ref[rows, cols],
                    k_ref[:, cols],
                    v_ref[:, cols],
                    dc_ref[rows, cols],
                    long_ref.at[0, pair, part],
                    low,
                    high,
                    wide_ref.at[part],
                )
                dq_ref[rows, cols] = d_queries
                keys_sum = d_keys if keys_sum is None else keys_sum + d_keys
                values_sum = d_values if values_sum is None else values_sum + d_values
            dk_ref[:, cols] = keys_sum.astype(BF16)
            dv_ref[:, cols] = values_sum.astype(BF16)

    wide = PAIRS * BLK
    start = pl.multiple_of(group * wide, wide)

    @pl.when(first_step)
    def _():
        wait_whole(w_ref, sem)
        bq_ref[...] = jnp.zeros_like(bq_ref)
        bv_ref[...] = jnp.zeros_like(bv_ref)

    bq_ref[:, pl.ds(start, wide)] += jnp.sum(dq_ref[...].astype(F32), axis=0, keepdims=True)
    bv_ref[:, pl.ds(start, wide)] += jnp.sum(dv_ref[...].astype(F32), axis=0, keepdims=True)
    total = (
        right_product(dq_ref[...], w_ref[:, pl.ds(start, wide)])
        + right_product(dk_ref[...], w_ref[:, pl.ds(D + start, wide)])
        + right_product(dv_ref[...], w_ref[:, pl.ds(2 * D + start, wide)])
    )

    @pl.when((tile < short_tiles) & (group == 0))
    def _():
        in_short_ref[...] = resid_ref[...] + total

    @pl.when((tile < short_tiles) & (group > 0))
    def _():
        in_short_ref[...] += total

    @pl.when((tile >= short_tiles) & (group == 0))
    def _():
        in_long_ref[...] = resid_ref[...] + total

    @pl.when((tile >= short_tiles) & (group > 0))
    def _():
        in_long_ref[...] += total


def attention_back(block_slot, qkv, probs_short, probs_long, d_context, resid, blocks, short_tiles):
    tiles = d_context.shape[0] // TILE
    wide = PAIRS * BLK

    def short_map(tile, group, *_):
        return (short_index(tile, short_tiles), jnp.where(tile < short_tiles, group, GROUPS - 1), 0, 0, 0)

    def long_map(tile, group, *_):
        return (long_index(tile, short_tiles), jnp.where(tile < short_tiles, 0, group), 0, 0, 0)

    rows = pl.BlockSpec((TILE, wide), lambda tile, group, *_: (tile, group))
    row = pl.BlockSpec((1, D), lambda tile, group, *_: (0, 0))
    flops = 10 * D * TILE * TILE * tiles + 6 * D * D * TILE * tiles
    return pl.pallas_call(
        partial(attention_back_kernel, short_tiles=short_tiles),
        grid_spec=pltpu.PrefetchScalarGridSpec(
            num_scalar_prefetch=1,
            grid=(tiles, GROUPS),
            in_specs=[
                rows,
                rows,
                rows,
                pl.BlockSpec((1, PAIRS) + probs_short.shape[2:], short_map),
                pl.BlockSpec((1, PAIRS) + probs_long.shape[2:], long_map),
                rows,
                pl.BlockSpec((TILE, D), lambda tile, group, *_: (tile, 0)),
                pl.BlockSpec(memory_space=pl.ANY),
            ],
            out_specs=[
                rows,
                rows,
                rows,
                pl.BlockSpec((TILE, D), lambda tile, group, *_: (short_index(tile, short_tiles), 0)),
                pl.BlockSpec((TILE, D), lambda tile, group, *_: (long_index(tile, short_tiles), 0)),
                row,
                row,
            ],
            scratch_shapes=[
                pltpu.VMEM((D, 3 * D), BF16),
                pltpu.SemaphoreType.DMA,
                pltpu.VMEM((2,) + probs_short.shape[-2:], BF16),
                pltpu.VMEM((2,) + probs_long.shape[-2:], BF16),
            ],
        ),
        out_shape=[
            jax.ShapeDtypeStruct((tiles * TILE, D), BF16),
            jax.ShapeDtypeStruct((tiles * TILE, D), BF16),
            jax.ShapeDtypeStruct((tiles * TILE, D), BF16),
            jax.ShapeDtypeStruct((short_tiles * TILE, D), F32),
            jax.ShapeDtypeStruct(((tiles - short_tiles) * TILE, D), F32),
            jax.ShapeDtypeStruct((1, D), F32),
            jax.ShapeDtypeStruct((1, D), F32),
        ],
        compiler_params=pltpu.CompilerParams(
            vmem_limit_bytes=60 * MIB, fuse_transposed_lhs_in_matmul=True
        ),
        cost_estimate=pl.CostEstimate(flops=flops, bytes_accessed=50 * MIB, transcendentals=0),
        name="attention_back",
    )(block_slot, *qkv, probs_short, probs_long, d_context, resid, blocks)


def normal_parts(values):
    below = 0.5 * lax.erf(values * 0.7071067811865476) + 0.5
    return below, jnp.exp(-0.5 * values * values) * 0.3989422804014327


ROWS = 32
PARTS = tuple(slice(start, start + ROWS) for start in range(0, TILE, ROWS))
B_OUT, GAIN_ONE, SHIFT_ONE, B_UP, B_DOWN, GAIN_TWO, SHIFT_TWO, B_STUDENT, POOL_QUERY, B_HIDDEN = range(10)
VECTORS = (
    (12, 6),
    (18, 6),
    (24, 6),
    (30, 24),
    (54, 6),
    (60, 6),
    (66, 6),
    (72, 1),
    (73, 1),
    (74, 1),
)
CLASS_ROW = 75
LAST_ROW = 91
SMALL_ROWS = 96


def norm_parts(values):
    center = values - jnp.mean(values, axis=-1, keepdims=True)
    spread = jnp.mean(center * center, axis=-1, keepdims=True)
    inverse = lax.rsqrt(spread + NORM_EPSILON)
    return center * inverse, inverse


def norm_back(d_values, gain, unit, inverse):
    d_unit = d_values * gain
    return inverse * (
        d_unit
        - jnp.mean(d_unit, axis=-1, keepdims=True)
        - unit * jnp.mean(d_unit * unit, axis=-1, keepdims=True)
    )


def column_sum(values):
    return jnp.sum(values.astype(F32), axis=0, keepdims=True)


def fold_rows(values):
    return jnp.sum(values.reshape(values.shape[0] // 8, 8, values.shape[1]), axis=0)


def add_up(total, values):
    folded = fold_rows(values)
    return folded if total is None else total + folded


def pool_weights(student, query, length):
    scaled = student * query
    lane = lax.broadcasted_iota(jnp.int32, scaled.shape, 1)
    place = lax.broadcasted_iota(jnp.int32, (scaled.shape[0], 1), 0)
    weights = []
    for side in (lane < SD // PH, lane >= SD // PH):
        scores = jnp.sum(jnp.where(side, scaled, 0.0), axis=-1, keepdims=True)
        scores = jnp.where(place < length, scores, MASKED_SCORE)
        powers = jnp.exp(scores - jnp.max(scores, axis=0, keepdims=True))
        weights.append(powers / jnp.sum(powers, axis=0, keepdims=True))
    return jnp.where(lane < SD // PH, weights[0], weights[1]), weights


def student_back(student, query, weights, both, d_pooled):
    lane = lax.broadcasted_iota(jnp.int32, student.shape, 1)
    moved = student * d_pooled
    d_scores = []
    for side, weight in zip((lane < SD // PH, lane >= SD // PH), weights):
        d_weight = jnp.sum(jnp.where(side, moved, 0.0), axis=-1, keepdims=True)
        d_scores.append(weight * (d_weight - jnp.sum(weight * d_weight, axis=0, keepdims=True)))
    d_score = jnp.where(lane < SD // PH, d_scores[0], d_scores[1])
    d_query = jnp.sum(d_score * student, axis=0, keepdims=True) * 0.125
    return both * d_pooled + d_score * query, d_query


def feed_kernel(
    len_short,
    len_long,
    slot_ref,
    x_ref,
    context_ref,
    cot_short_ref,
    cot_long_ref,
    logit_cot_ref,
    params,
    w_class,
    b_class,
    blocks,
    enc_short_ref,
    enc_long_ref,
    logit_ref,
    first_ref,
    active_ref,
    d_up_ref,
    d_down_ref,
    d_branch_ref,
    d_context_ref,
    d_resid_ref,
    g_student,
    g_hidden,
    g_small,
    slope,
    pooled_ref,
    d_student_ref,
    w_out,
    w_up,
    w_down,
    w_student,
    w_hidden,
    vectors,
    totals,
    g_class,
    g_last,
    unit_one,
    unit_two,
    encoded_ref,
    resid_ref,
    sems,
    *,
    short_tiles,
    width,
):
    tile = pl.program_id(0)
    per_tile = TILE // width
    loads = ((w_out, 108, 6, 6), (w_up, 144, 6, 24), (w_down, 288, 24, 6), (w_student, 432, 6, 1), (w_hidden, 438, 1, 1))

    def arrive(*indices):
        @pl.when(tile == 0)
        def _():
            for index in indices:
                wait_whole(loads[index][0], sems.at[index])

    @pl.when(tile == 0)
    def _():
        for index, (target, block, row_count, col_count) in enumerate(loads):
            load_blocks(slot_ref, blocks, target, sems.at[index], block, row_count, col_count)
        for index, (start, count) in enumerate(VECTORS):
            for place in range(count):
                vectors[index : index + 1, place * BLK : (place + 1) * BLK] = params[
                    start + place : start + place + 1, :
                ]
        for ref in (totals, g_class, g_last, g_student, g_hidden):
            ref[...] = jnp.zeros_like(ref)

    def vector(index):
        return vectors[index : index + 1, : VECTORS[index][1] * BLK]

    def add_total(index, folded):
        totals[index : index + 1, : VECTORS[index][1] * BLK] += jnp.sum(folded, axis=0, keepdims=True)

    arrive(0)
    branch = product(context_ref[...], w_out[...])
    inverse_one = []
    for rows in PARTS:
        unit, inverse = norm_parts(x_ref[rows].astype(F32) + (branch[rows] + vector(B_OUT)))
        inverse_one.append(inverse)
        unit_one[rows] = unit
        first_ref[rows] = (unit * vector(GAIN_ONE) + vector(SHIFT_ONE)).astype(BF16)
    arrive(1)
    for start in range(0, FF, CHUNK):
        cols = slice(start, start + CHUNK)
        upward = product(first_ref[...], w_up[:, cols])
        for top in range(0, TILE, 64):
            rows = slice(top, top + 64)
            part = upward[rows] + vectors[B_UP : B_UP + 1, cols]
            below, density = normal_parts(part)
            active_ref[rows, cols] = (part * below).astype(BF16)
            slope[rows, cols] = (below + part * density).astype(BF16)
    arrive(2, 3, 4)
    downward = product(active_ref[...], w_down[...])
    inverse_two = []
    for rows in PARTS:
        unit, inverse = norm_parts(first_ref[rows].astype(F32) + (downward[rows] + vector(B_DOWN)))
        inverse_two.append(inverse)
        unit_two[rows] = unit
        encoded_ref[rows] = (unit * vector(GAIN_TWO) + vector(SHIFT_TWO)).astype(BF16)

    @pl.when(tile < short_tiles)
    def _():
        enc_short_ref[...] = encoded_ref[...]

    @pl.when(tile >= short_tiles)
    def _():
        enc_long_ref[...] = encoded_ref[...]

    student = product(encoded_ref[...], w_student[...]) + vector(B_STUDENT)
    query = vector(POOL_QUERY) * 0.125
    pooled_ref[...] = jnp.zeros_like(pooled_ref)

    def head():
        pooled = pooled_ref[...]
        wide_hidden = w_hidden[...].astype(F32)
        hidden = jnp.tanh(product(pooled, wide_hidden, HIGHEST_PRECISION) + vector(B_HIDDEN))
        logit_ref[0] = product(hidden, w_class[...], HIGHEST_PRECISION) + b_class[...]
        d_logits = logit_cot_ref[0]
        g_last[...] += column_sum(d_logits)
        g_class[...] += left_product(d_logits, hidden, HIGHEST_PRECISION)
        d_hidden = right_product(d_logits, w_class[...], HIGHEST_PRECISION)
        d_hidden = d_hidden * (1.0 - hidden * hidden)
        add_total(B_HIDDEN, d_hidden)
        g_hidden[...] += left_product(pooled, d_hidden, HIGHEST_PRECISION)
        return right_product(d_hidden, wide_hidden, HIGHEST_PRECISION)

    def pool(starts, size, lengths):
        kept = []
        for index, (start, length) in enumerate(zip(starts, lengths)):
            rows = student[start : start + size]
            both, weights = pool_weights(rows, query, length)
            pooled_ref[index : index + 1, :] = column_sum(both * rows)
            kept.append((start, rows, both, weights))
        d_pooled = head()
        for index, (start, rows, both, weights) in enumerate(kept):
            d_rows, d_query = student_back(rows, query, weights, both, d_pooled[index : index + 1])
            d_student_ref[start : start + size, :] = d_rows.astype(BF16)
            add_total(POOL_QUERY, d_query)

    @pl.when(tile < short_tiles)
    def _():
        pool(
            [seq * width for seq in range(per_tile)],
            width,
            [len_short[tile * per_tile + seq] for seq in range(per_tile)],
        )

    @pl.when(tile >= short_tiles)
    def _():
        pool([0], TILE, [len_long[tile - short_tiles]])

    d_student = d_student_ref[...]
    add_total(B_STUDENT, fold_rows(d_student.astype(F32)))
    g_student[...] += left_product(encoded_ref[...], d_student)
    through = right_product(d_student, w_student[...])
    gain_total = shift_total = bias_total = None
    for rows, inverse in zip(PARTS, inverse_two):
        cotangent = jnp.where(tile < short_tiles, cot_short_ref[rows], cot_long_ref[rows])
        d_second = cotangent.astype(F32) + through[rows]
        unit = unit_two[rows]
        gain_total = add_up(gain_total, d_second * unit)
        shift_total = add_up(shift_total, d_second)
        d_resid = norm_back(d_second, vector(GAIN_TWO), unit, inverse)
        resid_ref[rows] = d_resid
        d_down = d_resid.astype(BF16)
        d_down_ref[rows] = d_down
        bias_total = add_up(bias_total, d_down.astype(F32))
    add_total(GAIN_TWO, gain_total)
    add_total(SHIFT_TWO, shift_total)
    add_total(B_DOWN, bias_total)
    for start in range(0, FF, CHUNK):
        cols = slice(start, start + CHUNK)
        d_active = right_product(d_down_ref[...], w_down[cols, :])
        bias_total = None
        for top in range(0, TILE, 64):
            rows = slice(top, top + 64)
            d_up = (d_active[rows] * slope[rows, cols].astype(F32)).astype(BF16)
            d_up_ref[rows, cols] = d_up
            bias_total = add_up(bias_total, d_up.astype(F32))
        totals[B_UP : B_UP + 1, cols] += jnp.sum(bias_total, axis=0, keepdims=True)
    through = right_product(d_up_ref[...], w_up[...])
    gain_total = shift_total = bias_total = None
    for rows, inverse in zip(PARTS, inverse_one):
        d_first = resid_ref[rows] + through[rows]
        unit = unit_one[rows]
        gain_total = add_up(gain_total, d_first * unit)
        shift_total = add_up(shift_total, d_first)
        d_resid = norm_back(d_first, vector(GAIN_ONE), unit, inverse)
        d_resid_ref[rows] = d_resid
        d_branch = d_resid.astype(BF16)
        d_branch_ref[rows] = d_branch
        bias_total = add_up(bias_total, d_branch.astype(F32))
    add_total(GAIN_ONE, gain_total)
    add_total(SHIFT_ONE, shift_total)
    add_total(B_OUT, bias_total)
    d_context_ref[...] = right_product(d_branch_ref[...], w_out[...]).astype(BF16)

    @pl.when(tile == pl.num_programs(0) - 1)
    def _():
        g_small[...] = jnp.zeros_like(g_small)
        for index, (start, count) in enumerate(VECTORS):
            for place in range(count):
                g_small[start + place : start + place + 1, :] = totals[
                    index : index + 1, place * BLK : (place + 1) * BLK
                ]
        g_small[CLASS_ROW : CLASS_ROW + NCLS, :] = g_class[:NCLS, :]
        g_small[LAST_ROW : LAST_ROW + 1, :] = g_last[...]


def feed(
    len_short, len_long, block_slot, x, context, cot_short, cot_long, logit_cot, small, blocks, short_tiles, width
):
    tiles = x.shape[0] // TILE
    long_tiles = tiles - short_tiles

    def whole(shape):
        return pl.BlockSpec(shape, lambda tile, *_: (0,) * len(shape), pipeline_mode=pl.Buffered(1))

    def kept(shape):
        return pl.BlockSpec(shape, lambda tile, *_: (0,) * len(shape))

    def rows(columns):
        return pl.BlockSpec((TILE, columns), lambda tile, *_: (tile, 0))

    short_rows = pl.BlockSpec((TILE, D), lambda tile, *_: (short_index(tile, short_tiles), 0))
    long_rows = pl.BlockSpec((TILE, D), lambda tile, *_: (long_index(tile, short_tiles), 0))
    logit_rows = pl.BlockSpec((1, 8, SD), lambda tile, *_: (tile, 0, 0))
    grad_shapes = ((D, SD), (SD, SD), (SMALL_ROWS, BLK))
    total = tiles * TILE
    return pl.pallas_call(
        partial(feed_kernel, short_tiles=short_tiles, width=width),
        grid_spec=pltpu.PrefetchScalarGridSpec(
            num_scalar_prefetch=3,
            grid=(tiles,),
            in_specs=[rows(D), rows(D), short_rows, long_rows, logit_rows]
            + [whole(array.shape) for array in small]
            + [pl.BlockSpec(memory_space=pl.ANY)],
            out_specs=[
                short_rows,
                long_rows,
                logit_rows,
                rows(D),
                rows(FF),
                rows(FF),
                rows(D),
                rows(D),
                rows(D),
                rows(D),
            ]
            + [kept(shape) for shape in grad_shapes],
            scratch_shapes=[
                pltpu.VMEM((TILE, FF), BF16),
                pltpu.VMEM((8, SD), F32),
                pltpu.VMEM((TILE, SD), BF16),
                pltpu.VMEM((D, D), BF16),
                pltpu.VMEM((D, FF), BF16),
                pltpu.VMEM((FF, D), BF16),
                pltpu.VMEM((D, SD), BF16),
                pltpu.VMEM((SD, SD), BF16),
                pltpu.VMEM((16, FF), F32),
                pltpu.VMEM((16, FF), F32),
                pltpu.VMEM((SD, SD), F32),
                pltpu.VMEM((1, SD), F32),
                pltpu.VMEM((TILE, D), F32),
                pltpu.VMEM((TILE, D), F32),
                pltpu.VMEM((TILE, D), BF16),
                pltpu.VMEM((TILE, D), F32),
                pltpu.SemaphoreType.DMA((5,)),
            ],
        ),
        out_shape=[
            jax.ShapeDtypeStruct((short_tiles * TILE, D), BF16),
            jax.ShapeDtypeStruct((long_tiles * TILE, D), BF16),
            jax.ShapeDtypeStruct((tiles, 8, SD), F32),
            jax.ShapeDtypeStruct((total, D), BF16),
            jax.ShapeDtypeStruct((total, FF), BF16),
            jax.ShapeDtypeStruct((total, FF), BF16),
            jax.ShapeDtypeStruct((total, D), BF16),
            jax.ShapeDtypeStruct((total, D), BF16),
            jax.ShapeDtypeStruct((total, D), BF16),
            jax.ShapeDtypeStruct((total, D), F32),
        ]
        + [jax.ShapeDtypeStruct(shape, F32) for shape in grad_shapes],
        compiler_params=pltpu.CompilerParams(vmem_limit_bytes=62 * MIB),
        cost_estimate=pl.CostEstimate(
            flops=total * (8 * D * FF + 4 * D * D), bytes_accessed=70 * MIB, transcendentals=total * FF
        ),
        name="feed",
    )(len_short, len_long, block_slot, x, context, cot_short, cot_long, logit_cot, *small, blocks)


class Place:
    def __init__(self):
        self.quarter = lax.axis_index("dp")
        self.shard = lax.axis_index("fsdp")
        x = self.quarter % 2
        y = self.quarter // 2
        self.core = self.shard % 2
        self.z = self.shard // 2
        self.high = self.z // 2
        self.by_x = 2 * y + 1 - x
        self.by_y = 2 * (1 - y) + x
        self.across = 2 * (1 - y) + 1 - x
        self.sibling = (self.quarter, 2 * self.z + 1 - self.core)
        self.next_x = (self.by_x, self.shard)
        self.next_y = (self.by_y, self.shard)
        self.inner = (self.z > 0) & (self.z < 3)

    def at_z(self, z):
        return (self.quarter, 2 * z + self.core)


def send(source, target, send_sem, recv_sem, device):
    copy = pltpu.make_async_remote_copy(
        src_ref=source,
        dst_ref=target,
        send_sem=send_sem,
        recv_sem=recv_sem,
        device_id=device,
        device_id_type=pl.DeviceIdType.MESH,
    )
    copy.start()
    return copy


def landing(target, send_sem, recv_sem, device):
    return pltpu.make_async_remote_copy(
        src_ref=target,
        dst_ref=target,
        send_sem=send_sem,
        recv_sem=recv_sem,
        device_id=device,
        device_id_type=pl.DeviceIdType.MESH,
    )


def greet(place, extra=()):
    barrier = pltpu.get_barrier_semaphore()

    def signal(device):
        pl.semaphore_signal(barrier, inc=1, device_id=device, device_id_type=pl.DeviceIdType.MESH)

    near = (place.sibling, place.next_x, place.next_y) + tuple(extra)
    for device in near:
        signal(device)

    @pl.when(place.z > 0)
    def _():
        signal(place.at_z(place.z - 1))

    @pl.when(place.z < 3)
    def _():
        signal(place.at_z(place.z + 1))

    pl.semaphore_wait(barrier, len(near) + 1 + (place.z + 1) // 2 % 2)


def gather_kernel(
    master_ref,
    out_ref,
    full,
    own_send,
    relay_send,
    z_recv,
    xy_send,
    xy_recv,
    core_send,
    core_recv,
    out_sems,
):
    place = Place()
    z, core, shard = place.z, place.core, place.shard
    rows = master_ref.shape[0]
    quarter = rows // 4
    half = quarter // 2

    full[shard] = master_ref[...].astype(BF16)
    greet(place)

    def region(which, start, size):
        return full.at[which, pl.ds(pl.multiple_of(start, 16), size)]

    stores = []
    sends = []

    def to_core(index, ref):
        sends.append(send(ref, ref, core_send.at[index], core_recv.at[index], place.sibling))

    def store(index, which):
        copy = pltpu.make_async_copy(full.at[which], out_ref.at[which], out_sems.at[index])
        copy.start()
        stores.append(copy)

    mine = region(shard, place.quarter * quarter, quarter)

    @pl.when(z > 0)
    def _():
        send(mine, mine, own_send.at[0], z_recv.at[z], place.at_z(z - 1))

    @pl.when(z < 3)
    def _():
        send(mine, mine, own_send.at[1], z_recv.at[z], place.at_z(z + 1))

    whole = full.at[shard]
    own_core = send(whole, whole, core_send.at[0], core_recv.at[0], place.sibling)
    store(0, shard)

    origins = (z + 1 - 2 * (z % 2), 2 - place.high, 3 * (1 - place.high))
    relays = (3 - z, 3 * (z - 1), 3 * (z - 1))
    kept = []

    def arrive_xy(step):
        pieces = kept[step]
        base = 1 + 5 * step
        landing(pieces[1], xy_send.at[4 * step], xy_recv.at[4 * step], place.next_x).wait_recv()
        first = pieces[1].at[pl.ds(0, half)]
        sends.append(send(first, first, xy_send.at[4 * step + 2], xy_recv.at[4 * step + 2], place.next_y))
        to_core(base + 1, pieces[1])
        landing(pieces[2], xy_send.at[4 * step + 1], xy_recv.at[4 * step + 1], place.next_y).wait_recv()
        last = pieces[2].at[pl.ds(half, half)]
        sends.append(send(last, last, xy_send.at[4 * step + 3], xy_recv.at[4 * step + 3], place.next_x))
        to_core(base + 2, pieces[2])

    def arrive_across(step):
        pieces = kept[step]
        base = 1 + 5 * step
        landing(pieces[3], xy_send.at[4 * step + 2], xy_recv.at[4 * step + 2], place.next_y).wait_recv()
        to_core(base + 3, pieces[3])
        landing(pieces[4], xy_send.at[4 * step + 3], xy_recv.at[4 * step + 3], place.next_x).wait_recv()
        to_core(base + 4, pieces[4])
        store(2 + 2 * step, kept[step][5])

    def arrive_core(step):
        for index, (start, size) in enumerate(
            (
                (place.quarter * quarter, quarter),
                (place.by_x * quarter, quarter),
                (place.by_y * quarter, quarter),
                (place.across * quarter, half),
                (place.across * quarter + half, half),
            )
        ):
            ref = region(kept[step][6], start, size)
            landing(
                ref, core_send.at[1 + 5 * step + index], core_recv.at[1 + 5 * step + index], place.sibling
            ).wait_recv()
        store(3 + 2 * step, kept[step][6])

    for step in range(3):
        origin = origins[step]
        which = 2 * origin + core
        piece = region(which, place.quarter * quarter, quarter)
        landing(piece, relay_send.at[step], z_recv.at[origin], place.next_x).wait_recv()

        @pl.when(place.inner)
        def _():
            send(piece, piece, relay_send.at[step], z_recv.at[origin], place.at_z(relays[step]))

        sends.append(send(piece, piece, xy_send.at[4 * step], xy_recv.at[4 * step], place.next_x))
        sends.append(send(piece, piece, xy_send.at[4 * step + 1], xy_recv.at[4 * step + 1], place.next_y))
        to_core(1 + 5 * step, piece)
        kept.append(
            (
                piece,
                region(which, place.by_x * quarter, quarter),
                region(which, place.by_y * quarter, quarter),
                region(which, place.across * quarter, half),
                region(which, place.across * quarter + half, half),
                which,
                2 * origin + 1 - core,
            )
        )
        if step >= 1:
            arrive_xy(step - 1)
        if step >= 2:
            arrive_across(step - 2)
    sibling_whole = full.at[2 * z + 1 - core]
    landing(sibling_whole, core_send.at[0], core_recv.at[0], place.sibling).wait_recv()
    store(1, 2 * z + 1 - core)
    arrive_xy(2)
    arrive_across(1)
    arrive_core(0)
    arrive_across(2)
    arrive_core(1)
    arrive_core(2)

    @pl.when(z > 0)
    def _():
        landing(mine, own_send.at[0], z_recv.at[z], place.at_z(z - 1)).wait_send()

    @pl.when(z < 3)
    def _():
        landing(mine, own_send.at[1], z_recv.at[z], place.at_z(z + 1)).wait_send()

    for step in range(3):

        @pl.when(place.inner)
        def _():
            landing(
                kept[step][0], relay_send.at[step], z_recv.at[0], place.at_z(relays[step])
            ).wait_send()

    own_core.wait_send()
    for copy in sends:
        copy.wait_send()
    for copy in stores:
        copy.wait()


def gather_shards(master):
    slot_count = master.shape[0]
    rows = slot_count * BLK
    shards = lax.axis_size("fsdp")
    full = pl.pallas_call(
        gather_kernel,
        in_specs=[pl.BlockSpec(memory_space=pltpu.VMEM)],
        out_specs=pl.BlockSpec(memory_space=pl.ANY),
        out_shape=jax.ShapeDtypeStruct((shards, rows, BLK), BF16),
        scratch_shapes=[
            pltpu.VMEM((shards, rows, BLK), BF16),
            pltpu.SemaphoreType.DMA((2,)),
            pltpu.SemaphoreType.DMA((3,)),
            pltpu.SemaphoreType.DMA((4,)),
            pltpu.SemaphoreType.DMA((12,)),
            pltpu.SemaphoreType.DMA((12,)),
            pltpu.SemaphoreType.DMA((16,)),
            pltpu.SemaphoreType.DMA((16,)),
            pltpu.SemaphoreType.DMA((8,)),
        ],
        compiler_params=pltpu.CompilerParams(
            collective_id=0, has_side_effects=True, vmem_limit_bytes=60 * MIB
        ),
        cost_estimate=pl.CostEstimate(flops=0, bytes_accessed=200 * MIB, transcendentals=0),
        name="gather",
    )(master.reshape(rows, BLK))
    return full.reshape(shards * slot_count, BLK, BLK)


def add_rows(target, former, latter, rows, step):
    @pl.loop(0, rows // step)
    def _(index):
        part = pl.ds(pl.multiple_of(index * step, 16), step)
        target[part] = (former[part].astype(F32) + latter[part].astype(F32)).astype(BF16)


def reduce_kernel(
    terms,
    small_ref,
    out_ref,
    small_out,
    mine,
    sib,
    from_x,
    from_y,
    late_y,
    late_x,
    from_z,
    small_in,
    small_sum,
    load_sems,
    core_send,
    core_recv,
    xy_send,
    xy_recv,
    z_send,
    z_recv,
    last_send,
    last_recv,
    small_send,
    small_recv,
):
    place = Place()
    z, core = place.z, place.core
    rows = terms.shape[1]
    quarter = rows // 4
    half = quarter // 2
    far = place.at_z(z + 2 - 4 * place.high)
    near = place.at_z(z + 1 - 2 * (z % 2))
    greet(place, (far,))

    low_z = 1 - place.high
    order = (
        3 * low_z,
        low_z * (2 - 2 * z) + place.high * (7 - 2 * z),
        1 + z % 2,
        z,
    )
    onward = (z + 1 - 2 * place.high, z + 1 - 2 * (z % 2), z + 1 - 2 * place.high)
    closing = (0, (z % 2) * low_z, place.high)

    sends = []
    loads = []
    small_sum[0] = small_ref[...]
    small_partners = (place.sibling, place.next_x, place.next_y, near, far)

    def small_step(level):
        if level > 0:
            landing(
                small_in.at[level - 1],
                small_send.at[level - 1],
                small_recv.at[level - 1],
                small_partners[level - 1],
            ).wait_recv()
            small_sum[level] = small_sum[level - 1] + small_in[level - 1]
        if level < 5:
            sends.append(
                send(
                    small_sum.at[level],
                    small_in.at[level],
                    small_send.at[level],
                    small_recv.at[level],
                    small_partners[level],
                )
            )

    for step in range(4):
        goal = order[step]
        load = pltpu.make_async_copy(terms.at[2 * goal + core], mine.at[step], load_sems.at[step])
        load.start()
        loads.append(load)
        sends.append(
            send(
                terms.at[2 * goal + 1 - core],
                sib.at[step],
                core_send.at[step],
                core_recv.at[step],
                place.sibling,
            )
        )
        if step == 0:
            small_step(0)

    def part(step, which, side):
        start = pl.multiple_of(which * quarter + side * half, 16)
        return mine.at[step, pl.ds(start, half)]

    def stage_core(step):
        loads[step].wait()
        landing(sib.at[step], core_send.at[step], core_recv.at[step], place.sibling).wait_recv()
        for index, which in enumerate((place.by_x, place.across, place.by_y, place.quarter)):
            start = pl.multiple_of(which * quarter, 16)
            block = pl.ds(start, quarter)
            add_rows(mine.at[step, block], mine.at[step, block], sib.at[step, block], quarter, half)
            if which is place.across:
                for slot, source in enumerate((place.by_x, place.across)):
                    sends.append(
                        send(
                            part(step, source, 0),
                            from_x.at[step, slot],
                            xy_send.at[6 * step + slot],
                            xy_recv.at[6 * step + slot],
                            place.next_x,
                        )
                    )
            if which is place.by_y:
                for slot, source in enumerate((place.by_y, place.across)):
                    sends.append(
                        send(
                            part(step, source, 1),
                            from_y.at[step, slot],
                            xy_send.at[6 * step + 2 + slot],
                            xy_recv.at[6 * step + 2 + slot],
                            place.next_y,
                        )
                    )

    def take(target, source, index, device):
        landing(source, xy_send.at[index], xy_recv.at[index], device).wait_recv()
        add_rows(target, target, source, half, half)

    def stage_first(step):
        base = 6 * step
        take(part(step, place.by_y, 0), from_x.at[step, 1], base + 1, place.next_x)
        sends.append(
            send(
                part(step, place.by_y, 0),
                late_y.at[step],
                xy_send.at[base + 4],
                xy_recv.at[base + 4],
                place.next_y,
            )
        )
        take(part(step, place.by_x, 1), from_y.at[step, 1], base + 3, place.next_y)
        sends.append(
            send(
                part(step, place.by_x, 1),
                late_x.at[step],
                xy_send.at[base + 5],
                xy_recv.at[base + 5],
                place.next_x,
            )
        )
        take(part(step, place.quarter, 0), from_x.at[step, 0], base, place.next_x)
        take(part(step, place.quarter, 1), from_y.at[step, 0], base + 2, place.next_y)

    def own_block(step):
        return mine.at[step, pl.ds(pl.multiple_of(place.quarter * quarter, 16), quarter)]

    def stage_second(step):
        base = 6 * step
        take(part(step, place.quarter, 0), late_y.at[step], base + 4, place.next_y)
        take(part(step, place.quarter, 1), late_x.at[step], base + 5, place.next_x)
        block = own_block(step)
        goal = order[step]
        if step < 3:

            @pl.when(place.inner)
            def _():
                landing(from_z.at[goal], z_send.at[step], z_recv.at[goal], near).wait_recv()
                add_rows(block, block, from_z.at[goal], quarter, half)

            slot = goal + closing[step] * (4 - goal)
            sends.append(
                send(
                    block, from_z.at[slot], z_send.at[step], z_recv.at[slot], place.at_z(onward[step])
                )
            )
        else:

            @pl.when(z > 0)
            def _():
                landing(from_z.at[z], z_send.at[0], z_recv.at[z], near).wait_recv()
                add_rows(block, block, from_z.at[z], quarter, half)

            @pl.when(z < 3)
            def _():
                landing(from_z.at[4], z_send.at[0], z_recv.at[4], near).wait_recv()
                add_rows(block, block, from_z.at[4], quarter, half)

    stage_core(0)
    small_step(1)
    stage_core(1)
    stage_first(0)
    small_step(2)
    stage_core(2)
    stage_first(1)
    stage_second(0)
    small_step(3)
    stage_core(3)
    stage_first(2)
    stage_second(1)
    small_step(4)
    stage_first(3)
    stage_second(2)
    small_step(5)
    small_out[...] = small_sum[5]
    stage_second(3)

    def final(which, side=None):
        start = pl.multiple_of(which * quarter + (0 if side is None else side * half), 16)
        return out_ref.at[pl.ds(start, quarter if side is None else half)]

    final(place.quarter)[...] = own_block(3)[...]
    own = final(place.quarter)
    sends.append(send(own, own, last_send.at[0], last_recv.at[0], place.next_x))
    sends.append(send(own, own, last_send.at[1], last_recv.at[1], place.next_y))
    landing(final(place.by_x), last_send.at[0], last_recv.at[0], place.next_x).wait_recv()
    piece = final(place.by_x, 0)
    sends.append(send(piece, piece, last_send.at[2], last_recv.at[2], place.next_y))
    landing(final(place.by_y), last_send.at[1], last_recv.at[1], place.next_y).wait_recv()
    piece = final(place.by_y, 1)
    sends.append(send(piece, piece, last_send.at[3], last_recv.at[3], place.next_x))
    landing(final(place.across, 0), last_send.at[2], last_recv.at[2], place.next_y).wait_recv()
    landing(final(place.across, 1), last_send.at[3], last_recv.at[3], place.next_x).wait_recv()
    for copy in sends:
        copy.wait_send()


def reduce_shards(terms, small):
    all_slots = terms.shape[0]
    shards = lax.axis_size("fsdp")
    rows = all_slots // shards * BLK
    quarter = rows // 4
    half = quarter // 2
    vmem = pl.BlockSpec(memory_space=pltpu.VMEM)
    shard, total = pl.pallas_call(
        reduce_kernel,
        in_specs=[pl.BlockSpec(memory_space=pl.ANY), vmem],
        out_specs=[vmem, vmem],
        out_shape=[
            jax.ShapeDtypeStruct((rows, BLK), BF16),
            jax.ShapeDtypeStruct((SMALL_ROWS, BLK), F32),
        ],
        scratch_shapes=[
            pltpu.VMEM((4, rows, BLK), BF16),
            pltpu.VMEM((4, rows, BLK), BF16),
            pltpu.VMEM((4, 2, half, BLK), BF16),
            pltpu.VMEM((4, 2, half, BLK), BF16),
            pltpu.VMEM((4, half, BLK), BF16),
            pltpu.VMEM((4, half, BLK), BF16),
            pltpu.VMEM((5, quarter, BLK), BF16),
            pltpu.VMEM((5, SMALL_ROWS, BLK), F32),
            pltpu.VMEM((6, SMALL_ROWS, BLK), F32),
            pltpu.SemaphoreType.DMA((4,)),
            pltpu.SemaphoreType.DMA((4,)),
            pltpu.SemaphoreType.DMA((4,)),
            pltpu.SemaphoreType.DMA((24,)),
            pltpu.SemaphoreType.DMA((24,)),
            pltpu.SemaphoreType.DMA((3,)),
            pltpu.SemaphoreType.DMA((5,)),
            pltpu.SemaphoreType.DMA((4,)),
            pltpu.SemaphoreType.DMA((4,)),
            pltpu.SemaphoreType.DMA((5,)),
            pltpu.SemaphoreType.DMA((5,)),
        ],
        compiler_params=pltpu.CompilerParams(
            collective_id=1, has_side_effects=True, vmem_limit_bytes=60 * MIB
        ),
        cost_estimate=pl.CostEstimate(flops=0, bytes_accessed=400 * MIB, transcendentals=0),
        name="reduce",
    )(terms.reshape(shards, rows, BLK), small)
    return shard.reshape(all_slots // shards, BLK, BLK), total


def body(
    x_short,
    x_long,
    cot_short,
    cot_long,
    logit_cot_short,
    logit_cot_long,
    len_short,
    len_long,
    block_slot,
    master,
    left_stat,
    right_stat,
    left_root,
    right_root,
    small_params,
    small_first,
    small_second,
    own_transfers,
):
    slot_count = master.shape[0]
    all_slots = slot_count * lax.axis_size("fsdp")
    short_seqs, width = x_short.shape[:2]
    long_seqs = x_long.shape[0]
    short_tiles = short_seqs * width // TILE
    per_tile = TILE // width

    if own_transfers:
        gathered = gather_shards(master)
    else:
        gathered = lax.all_gather(master.astype(BF16), "fsdp", axis=0, tiled=True)
    pieces = unpack(small_params)
    params = jnp.pad(small_params, (0, SMALL_ROWS * BLK - small_params.shape[0])).reshape(SMALL_ROWS, BLK)
    w_class = jnp.pad(pieces[-2].reshape(SD, NCLS), ((0, 0), (0, SD - NCLS)))
    b_class = jnp.pad(pieces[-1].reshape(1, NCLS), ((0, 0), (0, SD - NCLS)))

    x = jnp.concatenate([x_short.reshape(-1, D), x_long.reshape(-1, D)], axis=0)
    *qkv, context, probs_short, probs_long = attention(
        len_short,
        len_long,
        block_slot,
        x,
        pieces[0].reshape(1, D),
        pieces[1].reshape(1, D),
        gathered,
        short_tiles,
        width,
    )

    logit_cot = jnp.concatenate(
        [
            jnp.pad(
                logit_cot_short.reshape(short_tiles, per_tile, NCLS),
                ((0, 0), (0, 8 - per_tile), (0, SD - NCLS)),
            ),
            jnp.pad(logit_cot_long.reshape(long_seqs, 1, NCLS), ((0, 0), (0, 7), (0, SD - NCLS))),
        ],
        axis=0,
    )
    (
        enc_short,
        enc_long,
        logits,
        first,
        active,
        d_up,
        d_down,
        d_branch,
        d_context,
        d_resid,
        g_student,
        g_hidden,
        g_small,
    ) = feed(
        len_short,
        len_long,
        block_slot,
        x,
        context,
        cot_short.reshape(-1, D),
        cot_long.reshape(-1, D),
        logit_cot,
        (params, w_class, b_class),
        gathered,
        short_tiles,
        width,
    )
    g_down = left_product(active, d_down).astype(BF16)
    g_up = left_product(first, d_up).astype(BF16)
    g_out = left_product(context, d_branch).astype(BF16)
    d_query, d_key, d_value, in_short, in_long, g_b_query, g_b_value = attention_back(
        block_slot, qkv, probs_short, probs_long, d_context, d_resid, gathered, short_tiles
    )
    g_query = left_product(x, d_query).astype(BF16)
    g_key = left_product(x, d_key).astype(BF16)
    g_value = left_product(x, d_value).astype(BF16)

    places = jnp.arange(all_slots, dtype=jnp.int32)
    empty_before = places + 1 - jnp.sum((block_slot[None, :] <= places[:, None]).astype(jnp.int32), axis=1)
    empty_index = jnp.arange(all_slots - NBLK, dtype=jnp.int32)
    empty = jnp.sum((empty_before[None, :] <= empty_index[:, None]).astype(jnp.int32), axis=1)
    slot_terms, small_terms = spread(
        block_slot,
        empty,
        (g_query, g_key, g_value, g_out, g_up, g_down, g_student.astype(BF16), g_hidden.astype(BF16)),
        g_small,
        g_b_query,
        g_b_value,
        all_slots,
    )
    if own_transfers:
        slot_grad, small_total = reduce_shards(slot_terms, small_terms)
    else:
        shard_grad = lax.psum_scatter(slot_terms, "fsdp", scatter_dimension=0, tiled=True)
        slot_grad = lax.psum(shard_grad, "dp")
        small_total = lax.psum(small_terms, ("dp", "fsdp"))
    slot_grad = slot_grad.astype(F32)
    small_grad = jnp.concatenate(
        [
            small_total[:CLASS_ROW].reshape(-1),
            small_total[CLASS_ROW : CLASS_ROW + NCLS].T.reshape(-1),
            small_total[LAST_ROW, :NCLS],
        ]
    )
    outer_left = jnp.einsum("sij,skj->sik", slot_grad, slot_grad, precision=HIGHEST_PRECISION)
    outer_right = jnp.einsum("sji,sjk->sik", slot_grad, slot_grad, precision=HIGHEST_PRECISION)
    new_left = STAT_DECAY * left_stat + (1.0 - STAT_DECAY) * outer_left
    new_right = STAT_DECAY * right_stat + (1.0 - STAT_DECAY) * outer_right
    left_applied = jnp.einsum("sij,sjk->sik", left_root, slot_grad, precision=HIGHEST_PRECISION)
    conditioned = jnp.einsum("sij,sjk->sik", left_applied, right_root, precision=HIGHEST_PRECISION)
    new_master = master - MATRIX_RATE * conditioned
    new_first = BETA_ONE * small_first + (1.0 - BETA_ONE) * small_grad
    new_second = BETA_TWO * small_second + (1.0 - BETA_TWO) * small_grad * small_grad
    first_hat = new_first / (1.0 - BETA_ONE**STEP)
    second_hat = new_second / (1.0 - BETA_TWO**STEP)
    new_small = small_params - ADAM_RATE * first_hat / (jnp.sqrt(second_hat) + ADAM_EPSILON)
    return (
        enc_short.reshape(x_short.shape),
        logits[:short_tiles, :per_tile, :NCLS].reshape(short_seqs, NCLS),
        enc_long.reshape(x_long.shape),
        logits[short_tiles:, 0, :NCLS],
        in_short.reshape(x_short.shape),
        in_long.reshape(x_long.shape),
        slot_grad,
        new_left,
        new_right,
        new_master,
        new_first,
        new_second,
        new_small,
    )


def solution(mesh):
    both = ("dp", "fsdp")
    placed = (
        P(both, None, None),
        P(both, None, None),
        P(both, None, None),
        P(both, None, None),
        P(both, None),
        P(both, None),
        P(both),
        P(both),
        P(),
        P("fsdp", None, None),
        P("fsdp", None, None),
        P("fsdp", None, None),
        P("fsdp", None, None),
        P("fsdp", None, None),
        P(),
        P(),
        P(),
    )
    return jax.shard_map(
        partial(body, own_transfers=(mesh.shape["dp"], mesh.shape["fsdp"]) == (4, 8)),
        mesh=mesh,
        in_specs=placed,
        out_specs=(
            P(both, None, None),
            P(both, None),
            P(both, None, None),
            P(both, None),
            P(both, None, None),
            P(both, None, None),
            P("fsdp", None, None),
            P("fsdp", None, None),
            P("fsdp", None, None),
            P("fsdp", None, None),
            P(),
            P(),
            P(),
        ),
        check_vma=False,
    )
```

```python
from functools import partial

import jax
import jax.numpy as jnp
from jax import lax
from jax.experimental import pallas as pl
from jax.experimental.pallas import tpu as pltpu
from jax.sharding import PartitionSpec as P

D = 768
HEADS = 12
FF = 3072
SD = 128
PH = 2
NCLS = 14
BLK = 128
STEP = 10
NBLK = 439
TILE = 512
PAIRS = 3
GROUPS = 2
CHUNK = 768
LATE = 24

NORM_EPSILON = 1e-12
BETA_ONE = 0.9
BETA_TWO = 0.999
ADAM_EPSILON = 1e-08
ADAM_RATE = 0.1
MATRIX_RATE = 0.2
STAT_DECAY = 0.5
MASKED_SCORE = -1e30
HIGHEST_PRECISION = lax.Precision.HIGHEST
MIB = 1024 * 1024
F32 = jnp.float32
BF16 = jnp.bfloat16

def product(former, latter, precision=None):
    return jnp.dot(former, latter, preferred_element_type=F32, precision=precision)


def left_product(former, latter, precision=None):
    return lax.dot_general(
        former, latter, (((0,), (0,)), ((), ())), preferred_element_type=F32, precision=precision
    )


def right_product(former, latter, precision=None):
    return lax.dot_general(
        former, latter, (((1,), (1,)), ((), ())), preferred_element_type=F32, precision=precision
    )


def unpack(small_values):
    widths = (D, D, D, D, D, FF, D, D, D, SD, SD, SD, SD * NCLS, NCLS)
    pieces = []
    offset = 0
    for column_count in widths:
        pieces.append(small_values[offset : offset + column_count])
        offset += column_count
    return pieces


def load_blocks(code_ref, early, late, target, sem, first, row_count, col_count):
    split = early.shape[0]

    def move(index, carry):
        row = pl.multiple_of((index // col_count) * BLK, BLK)
        col = pl.multiple_of((index % col_count) * BLK, BLK)
        place = target.at[pl.ds(row, BLK), pl.ds(col, BLK)]
        code = code_ref[first + index]

        @pl.when(code < split)
        def _():
            pltpu.make_async_copy(early.at[code], place, sem).start()

        @pl.when(code >= split)
        def _():
            pltpu.make_async_copy(late.at[code - split], place, sem).start()

        return carry

    lax.fori_loop(0, row_count * col_count, move, 0)


def wait_whole(target, sem):
    pltpu.make_async_copy(target, target, sem).wait()


def assemble_kernel(index_ref, blocks, out, sem):
    for which in range(3):

        def move(index, carry, which=which):
            row = pl.multiple_of((index // 6) * BLK, BLK)
            col = pl.multiple_of((index % 6 + 6 * which) * BLK, BLK)
            pltpu.make_async_copy(
                blocks.at[index_ref[36 * which + index]],
                out.at[pl.ds(row, BLK), pl.ds(col, BLK)],
                sem,
            ).start()
            return carry

        lax.fori_loop(0, 36, move, 0)
    wait_whole(out, sem)


def assemble(index, blocks):
    return pl.pallas_call(
        assemble_kernel,
        grid_spec=pltpu.PrefetchScalarGridSpec(
            num_scalar_prefetch=1,
            grid=(1,),
            in_specs=[pl.BlockSpec(memory_space=pl.ANY)],
            out_specs=pl.BlockSpec(memory_space=pltpu.VMEM),
            scratch_shapes=[pltpu.SemaphoreType.DMA],
        ),
        out_shape=jax.ShapeDtypeStruct((D, 3 * D), BF16),
        compiler_params=pltpu.CompilerParams(vmem_limit_bytes=60 * MIB),
        name="assemble",
    )(index, blocks)


QKV_PLACES = ((0, 6, 6), (36, 6, 6), (72, 6, 6))
OTHER_PLACES = ((108, 6, 6), (144, 6, 24), (288, 24, 6), (432, 6, 1), (438, 1, 1))


def spread_kernel(code_ref, empty_ref, *refs, places):
    grads = refs[: len(places)]
    zero, early, late, sems = refs[len(places) :]
    split = early.shape[0]

    def put(source, code, sem):
        @pl.when(code < split)
        def _():
            pltpu.make_async_copy(source, early.at[code], sem).start()

        @pl.when(code >= split)
        def _():
            pltpu.make_async_copy(source, late.at[code - split], sem).start()

    for which, (grad, (first, row_count, col_count)) in enumerate(zip(grads, places)):

        def move(index, carry, which=which, grad=grad, first=first, col_count=col_count):
            row = pl.multiple_of((index // col_count) * BLK, BLK)
            col = pl.multiple_of((index % col_count) * BLK, BLK)
            put(grad.at[pl.ds(row, BLK), pl.ds(col, BLK)], code_ref[first + index], sems.at[which])
            return carry

        lax.fori_loop(0, row_count * col_count, move, 0)
    for index in range(empty_ref.shape[0]):
        put(zero, empty_ref[index], sems.at[len(places) + index])
    for which, grad in enumerate(grads):
        wait_whole(grad, sems.at[which])
    for index in range(empty_ref.shape[0]):
        wait_whole(zero, sems.at[len(places) + index])


def spread(code, empty, grads, places, early_count, late_count):
    vmem = pl.BlockSpec(memory_space=pltpu.VMEM)
    anywhere = pl.BlockSpec(memory_space=pl.ANY)
    return pl.pallas_call(
        partial(spread_kernel, places=places),
        grid_spec=pltpu.PrefetchScalarGridSpec(
            num_scalar_prefetch=2,
            grid=(1,),
            in_specs=[vmem] * (len(grads) + 1),
            out_specs=[anywhere, anywhere],
            scratch_shapes=[pltpu.SemaphoreType.DMA((len(grads) + empty.shape[0],))],
        ),
        out_shape=[
            jax.ShapeDtypeStruct((early_count, BLK, BLK), BF16),
            jax.ShapeDtypeStruct((late_count, BLK, BLK), BF16),
        ],
        compiler_params=pltpu.CompilerParams(vmem_limit_bytes=32 * MIB),
        name="spread",
    )(code, empty, *grads, jnp.zeros((BLK, BLK), BF16))


def spread_late_kernel(index_ref, *refs):
    grads = refs[:3]
    small_ref, query_ref, value_ref, _, late, small_out, sems = refs[3:]
    for which, (grad, (first, row_count, col_count)) in enumerate(zip(grads, QKV_PLACES)):

        def move(index, carry, which=which, grad=grad, first=first, col_count=col_count):
            row = pl.multiple_of((index // col_count) * BLK, BLK)
            col = pl.multiple_of((index % col_count) * BLK, BLK)
            pltpu.make_async_copy(
                grad.at[pl.ds(row, BLK), pl.ds(col, BLK)],
                late.at[index_ref[first + index]],
                sems.at[which],
            ).start()
            return carry

        lax.fori_loop(0, row_count * col_count, move, 0)
    join_small(small_ref, query_ref, value_ref, small_out)
    for which, grad in enumerate(grads):
        wait_whole(grad, sems.at[which])


def join_small(small_ref, query_ref, value_ref, small_out):
    small_out[...] = small_ref[...]
    for start, ref in ((0, query_ref), (D // BLK, value_ref)):
        for index in range(D // BLK):
            small_out[start + index : start + index + 1, :] = ref[:, index * BLK : (index + 1) * BLK]


def spread_late(index, grads, small, g_query, g_value, late):
    vmem = pl.BlockSpec(memory_space=pltpu.VMEM)
    anywhere = pl.BlockSpec(memory_space=pl.ANY)
    return pl.pallas_call(
        spread_late_kernel,
        grid_spec=pltpu.PrefetchScalarGridSpec(
            num_scalar_prefetch=1,
            grid=(1,),
            in_specs=[vmem] * 6 + [anywhere],
            out_specs=[anywhere, vmem],
            scratch_shapes=[pltpu.SemaphoreType.DMA((3,))],
        ),
        out_shape=[
            jax.ShapeDtypeStruct(late.shape, BF16),
            jax.ShapeDtypeStruct(small.shape, F32),
        ],
        input_output_aliases={7: 0},
        compiler_params=pltpu.CompilerParams(vmem_limit_bytes=32 * MIB),
        name="spread_late",
    )(index, *grads, small, g_query, g_value, late)


def half_masks():
    lane = lax.broadcasted_iota(jnp.int32, (1, BLK), 1)
    low = (lane < BLK // 2).astype(BF16)
    return low, (1.0 - low.astype(F32)).astype(BF16)


def stack_heads(values, low, high):
    return jnp.concatenate([values * low, values * high], axis=0)


def pick_heads(values):
    rows = values.shape[0] // 2
    lane = lax.broadcasted_iota(jnp.int32, (rows, BLK), 1)
    return jnp.where(lane < BLK // 2, values[:rows], values[rows:])


def attend(queries, key_rows, value_rows, length, low, high):
    scores = right_product(stack_heads(queries, low, high), key_rows)
    visible = lax.broadcasted_iota(jnp.int32, scores.shape, 1) < length
    scores = jnp.where(visible, scores, MASKED_SCORE)
    powers = jnp.exp(scores - jnp.max(scores, axis=-1, keepdims=True))
    total = jnp.sum(powers, axis=-1, keepdims=True)
    probs = (powers * (1.0 / total)).astype(BF16)
    return probs, pick_heads(product(probs, value_rows)).astype(BF16)


def attention_kernel(*refs, short_tiles, transfers):
    len_short, len_long, x_ref, b_query, b_value, w_ref = refs[:6]
    refs = refs[6:]
    if transfers:
        early_ref, refs = refs[0], refs[1:]
    q_ref, k_ref, v_ref, context_ref, short_ref, long_ref = refs[:6]
    tile = pl.program_id(0)
    group = pl.program_id(1)
    low, high = half_masks()
    width = short_ref.shape[-1]
    per_tile = TILE // width
    if transfers:
        gather = Gather(refs[7], refs[6], refs[8:])

        def begin():
            refs[7][gather.place.shard] = early_ref[...]
            gather.start()

        run_events(
            tile * GROUPS + group,
            (
                (begin,),
                (partial(gather.along_z, 0),),
                (partial(gather.along_z, 1), partial(gather.along_xy, 0)),
                (partial(gather.along_z, 2), partial(gather.along_xy, 1), partial(gather.across, 0)),
                (gather.core_own, partial(gather.along_xy, 2), partial(gather.across, 1)),
                (partial(gather.across, 2), partial(gather.core, 0)),
                (partial(gather.core, 1),),
                (partial(gather.core, 2),),
            ),
        )

    wide = PAIRS * BLK
    start = pl.multiple_of(group * wide, wide)
    rows_in = x_ref[...]
    queries = product(rows_in, w_ref[:, pl.ds(start, wide)]) + b_query[:, pl.ds(start, wide)]
    q_ref[...] = (queries * 0.125).astype(BF16)
    k_ref[...] = product(rows_in, w_ref[:, pl.ds(D + start, wide)]).astype(BF16)
    values = product(rows_in, w_ref[:, pl.ds(2 * D + start, wide)]) + b_value[:, pl.ds(start, wide)]
    v_ref[...] = values.astype(BF16)

    @pl.when(tile < short_tiles)
    def _():
        for pair in range(PAIRS):
            cols = slice(pair * BLK, (pair + 1) * BLK)
            for seq in range(per_tile):
                rows = slice(seq * width, (seq + 1) * width)
                probs, context = attend(
                    q_ref[rows, cols],
                    k_ref[rows, cols],
                    v_ref[rows, cols],
                    len_short[tile * per_tile + seq],
                    low,
                    high,
                )
                short_ref[0, pair, seq] = probs
                context_ref[rows, cols] = context

    @pl.when(tile >= short_tiles)
    def _():
        length = len_long[tile - short_tiles]
        half = TILE // 2
        for pair in range(PAIRS):
            cols = slice(pair * BLK, (pair + 1) * BLK)
            for part in range(2):
                rows = slice(part * half, (part + 1) * half)
                probs, context = attend(
                    q_ref[rows, cols], k_ref[:, cols], v_ref[:, cols], length, low, high
                )
                long_ref[0, pair, part] = probs
                context_ref[rows, cols] = context

    if transfers:

        @pl.when((tile == pl.num_programs(0) - 1) & (group == GROUPS - 1))
        def _():
            gather.finish()


def run_events(step, events):
    for index, actions in enumerate(events):

        @pl.when(step == index)
        def _(actions=actions):
            for action in actions:
                action()


def probs_shapes(short_tiles, long_tiles, width):
    per_tile = TILE // width
    return (
        (short_tiles, 2 * PAIRS, per_tile, 2 * width, width),
        (long_tiles, 2 * PAIRS, 2, TILE, TILE),
    )


def short_index(tile, short_tiles):
    return jnp.minimum(tile, short_tiles - 1)


def long_index(tile, short_tiles):
    return jnp.maximum(tile - short_tiles, 0)


def probs_maps(short_tiles):
    def short_map(tile, group):
        last = jnp.minimum(tile // short_tiles, 1)
        return (short_index(tile, short_tiles), group + last * (GROUPS - 1 - group), 0, 0, 0)

    def long_map(tile, group):
        begun = jnp.minimum(tile // short_tiles, 1)
        return (long_index(tile, short_tiles), begun * group, 0, 0, 0)

    return short_map, long_map


def attention(len_short, len_long, x, b_query, b_value, w_qkv, short_tiles, width, early=None):
    tiles = x.shape[0] // TILE
    wide = PAIRS * BLK
    short_shape, long_shape = probs_shapes(short_tiles, tiles - short_tiles, width)
    short_map, long_map = probs_maps(short_tiles)
    flops = 4 * D * TILE * TILE * tiles + 6 * D * D * TILE * tiles
    rows = pl.BlockSpec((TILE, wide), lambda tile, group: (tile, group))
    scalars = pl.BlockSpec(memory_space=pltpu.SMEM)

    def whole(shape):
        return pl.BlockSpec(shape, lambda tile, group: (0,) * len(shape), pipeline_mode=pl.Buffered(1))

    in_specs = [
        scalars,
        scalars,
        pl.BlockSpec((TILE, D), lambda tile, group: (tile, 0)),
        whole((1, D)),
        whole((1, D)),
        whole((D, 3 * D)),
    ]
    out_specs = [
        rows,
        rows,
        rows,
        rows,
        pl.BlockSpec((1, PAIRS) + short_shape[2:], short_map),
        pl.BlockSpec((1, PAIRS) + long_shape[2:], long_map),
    ]
    out_shape = [jax.ShapeDtypeStruct((tiles * TILE, D), BF16)] * 4 + [
        jax.ShapeDtypeStruct(short_shape, BF16),
        jax.ShapeDtypeStruct(long_shape, BF16),
    ]
    arguments = [len_short, len_long, x, b_query, b_value, w_qkv]
    scratch = []
    params = dict(vmem_limit_bytes=60 * MIB)
    if early is not None:
        gathered = (lax.axis_size("fsdp"),) + early.shape
        arguments.append(early)
        in_specs.append(whole(early.shape))
        out_specs.append(pl.BlockSpec(memory_space=pl.ANY))
        out_shape.append(jax.ShapeDtypeStruct(gathered, BF16))
        scratch = [pltpu.VMEM(gathered, BF16)] + GATHER_SEMAPHORES
        params.update(collective_id=1, has_side_effects=True)
    return pl.pallas_call(
        partial(attention_kernel, short_tiles=short_tiles, transfers=early is not None),
        grid=(tiles, GROUPS),
        in_specs=in_specs,
        out_specs=out_specs,
        out_shape=out_shape,
        scratch_shapes=scratch,
        compiler_params=pltpu.CompilerParams(**params),
        cost_estimate=pl.CostEstimate(
            flops=flops, bytes_accessed=35 * MIB, transcendentals=HEADS * TILE * TILE * tiles // 2
        ),
        name="attention",
    )(*arguments)


def attend_back(queries, key_rows, value_rows, d_context, probs, low, high):
    stacked = stack_heads(d_context, low, high)
    d_probs = right_product(stacked, value_rows)
    wide = probs.astype(F32)
    weighted = wide * d_probs
    d_scores = (weighted - wide * jnp.sum(weighted, axis=-1, keepdims=True)).astype(BF16)
    d_queries = pick_heads(product(d_scores, key_rows)) * 0.125
    d_keys = left_product(d_scores, stack_heads(queries, low, high))
    d_values = left_product(probs, stacked)
    return d_queries.astype(BF16), d_keys, d_values


def attention_back_kernel(*refs, short_tiles, transfers):
    q_ref, k_ref, v_ref, short_ref, long_ref, dc_ref, resid_ref, w_ref = refs[:8]
    refs = refs[8:]
    if transfers:
        terms_ref, refs = refs[0], refs[1:]
    dq_ref, dk_ref, dv_ref, in_short_ref, in_long_ref, bq_ref, bv_ref = refs[:7]
    tile = pl.program_id(0)
    group = pl.program_id(1)
    low, high = half_masks()
    width = short_ref.shape[-1]
    per_tile = TILE // width
    if transfers:
        reduce = Reduce(terms_ref, refs[7], refs[8:])
        run_events(
            tile * GROUPS + group,
            (
                (reduce.start,),
                (partial(reduce.core, 0),),
                (partial(reduce.core, 1), partial(reduce.first, 0)),
                (partial(reduce.core, 2), partial(reduce.first, 1), partial(reduce.second, 0)),
                (partial(reduce.core, 3), partial(reduce.first, 2), partial(reduce.second, 1)),
                (partial(reduce.first, 3), partial(reduce.second, 2)),
                (partial(reduce.second, 3), reduce.share),
                (reduce.share_on,),
            ),
        )

    @pl.when(tile < short_tiles)
    def _():
        for pair in range(PAIRS):
            cols = slice(pair * BLK, (pair + 1) * BLK)
            for seq in range(per_tile):
                rows = slice(seq * width, (seq + 1) * width)
                d_queries, d_keys, d_values = attend_back(
                    q_ref[rows, cols],
                    k_ref[rows, cols],
                    v_ref[rows, cols],
                    dc_ref[rows, cols],
                    short_ref[0, pair, seq],
                    low,
                    high,
                )
                dq_ref[rows, cols] = d_queries
                dk_ref[rows, cols] = d_keys.astype(BF16)
                dv_ref[rows, cols] = d_values.astype(BF16)

    @pl.when(tile >= short_tiles)
    def _():
        half = TILE // 2
        for pair in range(PAIRS):
            cols = slice(pair * BLK, (pair + 1) * BLK)
            keys_sum = None
            values_sum = None
            for part in range(2):
                rows = slice(part * half, (part + 1) * half)
                d_queries, d_keys, d_values = attend_back(
                    q_ref[rows, cols],
                    k_ref[:, cols],
                    v_ref[:, cols],
                    dc_ref[rows, cols],
                    long_ref[0, pair, part],
                    low,
                    high,
                )
                dq_ref[rows, cols] = d_queries
                keys_sum = d_keys if keys_sum is None else keys_sum + d_keys
                values_sum = d_values if values_sum is None else values_sum + d_values
            dk_ref[:, cols] = keys_sum.astype(BF16)
            dv_ref[:, cols] = values_sum.astype(BF16)

    wide = PAIRS * BLK
    start = pl.multiple_of(group * wide, wide)

    @pl.when((tile == 0) & (group == 0))
    def _():
        bq_ref[...] = jnp.zeros_like(bq_ref)
        bv_ref[...] = jnp.zeros_like(bv_ref)

    bq_ref[:, pl.ds(start, wide)] += jnp.sum(dq_ref[...].astype(F32), axis=0, keepdims=True)
    bv_ref[:, pl.ds(start, wide)] += jnp.sum(dv_ref[...].astype(F32), axis=0, keepdims=True)
    total = (
        right_product(dq_ref[...], w_ref[:, pl.ds(start, wide)])
        + right_product(dk_ref[...], w_ref[:, pl.ds(D + start, wide)])
        + right_product(dv_ref[...], w_ref[:, pl.ds(2 * D + start, wide)])
    )

    @pl.when((tile < short_tiles) & (group == 0))
    def _():
        in_short_ref[...] = resid_ref[...] + total

    @pl.when((tile < short_tiles) & (group > 0))
    def _():
        in_short_ref[...] += total

    @pl.when((tile >= short_tiles) & (group == 0))
    def _():
        in_long_ref[...] = resid_ref[...] + total

    @pl.when((tile >= short_tiles) & (group > 0))
    def _():
        in_long_ref[...] += total

    if transfers:

        @pl.when((tile == pl.num_programs(0) - 1) & (group == GROUPS - 1))
        def _():
            reduce.finish()


def attention_back(qkv, probs_short, probs_long, d_context, resid, w_qkv, short_tiles, terms=None):
    tiles = d_context.shape[0] // TILE
    wide = PAIRS * BLK
    short_map, long_map = probs_maps(short_tiles)
    rows = pl.BlockSpec((TILE, wide), lambda tile, group: (tile, group))
    row = pl.BlockSpec((1, D), lambda tile, group: (0, 0))
    flops = 10 * D * TILE * TILE * tiles + 6 * D * D * TILE * tiles
    in_specs = [
        rows,
        rows,
        rows,
        pl.BlockSpec((1, PAIRS) + probs_short.shape[2:], short_map),
        pl.BlockSpec((1, PAIRS) + probs_long.shape[2:], long_map),
        rows,
        pl.BlockSpec((TILE, D), lambda tile, group: (tile, 0)),
        pl.BlockSpec((D, 3 * D), lambda tile, group: (0, 0), pipeline_mode=pl.Buffered(1)),
    ]
    out_specs = [
        rows,
        rows,
        rows,
        pl.BlockSpec((TILE, D), lambda tile, group: (short_index(tile, short_tiles), 0)),
        pl.BlockSpec((TILE, D), lambda tile, group: (long_index(tile, short_tiles), 0)),
        row,
        row,
    ]
    out_shape = [
        jax.ShapeDtypeStruct((tiles * TILE, D), BF16),
        jax.ShapeDtypeStruct((tiles * TILE, D), BF16),
        jax.ShapeDtypeStruct((tiles * TILE, D), BF16),
        jax.ShapeDtypeStruct((short_tiles * TILE, D), F32),
        jax.ShapeDtypeStruct(((tiles - short_tiles) * TILE, D), F32),
        jax.ShapeDtypeStruct((1, D), F32),
        jax.ShapeDtypeStruct((1, D), F32),
    ]
    arguments = [*qkv, probs_short, probs_long, d_context, resid, w_qkv]
    scratch = []
    params = dict(vmem_limit_bytes=60 * MIB)
    if terms is not None:
        count = terms.shape[1]
        arguments.append(terms)
        in_specs.append(pl.BlockSpec(memory_space=pl.ANY))
        out_specs.append(pl.BlockSpec((count, BLK), lambda tile, group: (0, 0)))
        out_shape.append(jax.ShapeDtypeStruct((count, BLK), BF16))
        scratch = reduce_scratch(count)
        params.update(collective_id=2, has_side_effects=True)
    return pl.pallas_call(
        partial(attention_back_kernel, short_tiles=short_tiles, transfers=terms is not None),
        grid=(tiles, GROUPS),
        in_specs=in_specs,
        out_specs=out_specs,
        out_shape=out_shape,
        scratch_shapes=scratch,
        compiler_params=pltpu.CompilerParams(**params),
        cost_estimate=pl.CostEstimate(flops=flops, bytes_accessed=50 * MIB, transcendentals=0),
        name="attention_back",
    )(*arguments)


def normal_parts(values):
    below = 0.5 * lax.erf(values * 0.7071067811865476) + 0.5
    return below, jnp.exp(-0.5 * values * values) * 0.3989422804014327


B_OUT, GAIN_ONE, SHIFT_ONE, B_UP, B_DOWN, GAIN_TWO, SHIFT_TWO, B_STUDENT, POOL_QUERY, B_HIDDEN = range(10)
VECTORS = (
    (12, 6),
    (18, 6),
    (24, 6),
    (30, 24),
    (54, 6),
    (60, 6),
    (66, 6),
    (72, 1),
    (73, 1),
    (74, 1),
)
CLASS_ROW = 75
LAST_ROW = 91
SMALL_ROWS = 96


def norm_parts(values):
    center = values - jnp.mean(values, axis=-1, keepdims=True)
    spread = jnp.mean(center * center, axis=-1, keepdims=True)
    inverse = lax.rsqrt(spread + NORM_EPSILON)
    return center * inverse, inverse


def norm_back(d_values, gain, unit, inverse):
    d_unit = d_values * gain
    return inverse * (
        d_unit
        - jnp.mean(d_unit, axis=-1, keepdims=True)
        - unit * jnp.mean(d_unit * unit, axis=-1, keepdims=True)
    )


def column_sum(values):
    return jnp.sum(values.astype(F32), axis=0, keepdims=True)


def pool_weights(student, query, length):
    scaled = student * query
    lane = lax.broadcasted_iota(jnp.int32, scaled.shape, 1)
    place = lax.broadcasted_iota(jnp.int32, (scaled.shape[0], 1), 0)
    weights = []
    for side in (lane < SD // PH, lane >= SD // PH):
        scores = jnp.sum(jnp.where(side, scaled, 0.0), axis=-1, keepdims=True)
        scores = jnp.where(place < length, scores, MASKED_SCORE)
        powers = jnp.exp(scores - jnp.max(scores, axis=0, keepdims=True))
        weights.append(powers / jnp.sum(powers, axis=0, keepdims=True))
    return jnp.where(lane < SD // PH, weights[0], weights[1]), weights


def student_back(student, query, weights, both, d_pooled):
    lane = lax.broadcasted_iota(jnp.int32, student.shape, 1)
    moved = student * d_pooled
    d_scores = []
    for side, weight in zip((lane < SD // PH, lane >= SD // PH), weights):
        d_weight = jnp.sum(jnp.where(side, moved, 0.0), axis=-1, keepdims=True)
        d_scores.append(weight * (d_weight - jnp.sum(weight * d_weight, axis=0, keepdims=True)))
    d_score = jnp.where(lane < SD // PH, d_scores[0], d_scores[1])
    d_query = jnp.sum(d_score * student, axis=0, keepdims=True) * 0.125
    return both * d_pooled + d_score * query, d_query


def feed_kernel(
    len_short,
    len_long,
    code_ref,
    x_ref,
    context_ref,
    cot_short_ref,
    cot_long_ref,
    logit_cot_ref,
    params,
    w_class,
    b_class,
    early,
    late,
    enc_short_ref,
    enc_long_ref,
    logit_ref,
    first_ref,
    active_ref,
    d_up_ref,
    d_down_ref,
    d_branch_ref,
    d_context_ref,
    d_resid_ref,
    g_student,
    g_hidden,
    g_small,
    slope,
    pooled_ref,
    d_student_ref,
    w_out,
    w_up,
    w_down,
    w_student,
    w_hidden,
    vectors,
    totals,
    g_class,
    g_last,
    sems,
    *,
    short_tiles,
    width,
):
    tile = pl.program_id(0)
    per_tile = TILE // width
    loads = ((w_out, 108, 6, 6), (w_up, 144, 6, 24), (w_down, 288, 24, 6), (w_student, 432, 6, 1), (w_hidden, 438, 1, 1))

    def arrive(*indices):
        @pl.when(tile == 0)
        def _():
            for index in indices:
                wait_whole(loads[index][0], sems.at[index])

    @pl.when(tile == 0)
    def _():
        for index, (target, block, row_count, col_count) in enumerate(loads):
            load_blocks(code_ref, early, late, target, sems.at[index], block, row_count, col_count)
        for index, (start, count) in enumerate(VECTORS):
            for place in range(count):
                vectors[index : index + 1, place * BLK : (place + 1) * BLK] = params[
                    start + place : start + place + 1, :
                ]
        for ref in (totals, g_class, g_last, g_student, g_hidden):
            ref[...] = jnp.zeros_like(ref)

    def vector(index):
        return vectors[index : index + 1, : VECTORS[index][1] * BLK]

    def add_total(index, values):
        totals[index : index + 1, : VECTORS[index][1] * BLK] += column_sum(values)

    arrive(0)
    branch = product(context_ref[...], w_out[...]) + vector(B_OUT)
    unit_one, inverse_one = norm_parts(x_ref[...].astype(F32) + branch)
    first = (unit_one * vector(GAIN_ONE) + vector(SHIFT_ONE)).astype(BF16)
    first_ref[...] = first
    arrive(1)
    for start in range(0, FF, CHUNK):
        cols = slice(start, start + CHUNK)
        upward = product(first, w_up[:, cols]) + vectors[B_UP : B_UP + 1, cols]
        below, density = normal_parts(upward)
        active_ref[:, cols] = (upward * below).astype(BF16)
        slope[:, cols] = (below + upward * density).astype(BF16)
    arrive(2, 3, 4)
    downward = product(active_ref[...], w_down[...]) + vector(B_DOWN)
    unit_two, inverse_two = norm_parts(first.astype(F32) + downward)
    encoded = (unit_two * vector(GAIN_TWO) + vector(SHIFT_TWO)).astype(BF16)

    @pl.when(tile < short_tiles)
    def _():
        enc_short_ref[...] = encoded

    @pl.when(tile >= short_tiles)
    def _():
        enc_long_ref[...] = encoded

    student = product(encoded, w_student[...]) + vector(B_STUDENT)
    query = vector(POOL_QUERY) * 0.125
    pooled_ref[...] = jnp.zeros_like(pooled_ref)

    def head():
        pooled = pooled_ref[...]
        wide_hidden = w_hidden[...].astype(F32)
        hidden = jnp.tanh(product(pooled, wide_hidden, HIGHEST_PRECISION) + vector(B_HIDDEN))
        logit_ref[0] = product(hidden, w_class[...], HIGHEST_PRECISION) + b_class[...]
        d_logits = logit_cot_ref[0]
        g_last[...] += column_sum(d_logits)
        g_class[...] += left_product(d_logits, hidden, HIGHEST_PRECISION)
        d_hidden = right_product(d_logits, w_class[...], HIGHEST_PRECISION)
        d_hidden = d_hidden * (1.0 - hidden * hidden)
        add_total(B_HIDDEN, d_hidden)
        g_hidden[...] += left_product(pooled, d_hidden, HIGHEST_PRECISION)
        return right_product(d_hidden, wide_hidden, HIGHEST_PRECISION)

    def pool(starts, size, lengths):
        kept = []
        for index, (start, length) in enumerate(zip(starts, lengths)):
            rows = student[start : start + size]
            both, weights = pool_weights(rows, query, length)
            pooled_ref[index : index + 1, :] = column_sum(both * rows)
            kept.append((start, rows, both, weights))
        d_pooled = head()
        for index, (start, rows, both, weights) in enumerate(kept):
            d_rows, d_query = student_back(rows, query, weights, both, d_pooled[index : index + 1])
            d_student_ref[start : start + size, :] = d_rows.astype(BF16)
            add_total(POOL_QUERY, d_query)

    @pl.when(tile < short_tiles)
    def _():
        pool(
            [seq * width for seq in range(per_tile)],
            width,
            [len_short[tile * per_tile + seq] for seq in range(per_tile)],
        )

    @pl.when(tile >= short_tiles)
    def _():
        pool([0], TILE, [len_long[tile - short_tiles]])

    d_student = d_student_ref[...]
    add_total(B_STUDENT, d_student)
    g_student[...] += left_product(encoded, d_student)
    cotangent = jnp.where(tile < short_tiles, cot_short_ref[...], cot_long_ref[...])
    d_second = cotangent.astype(F32) + right_product(d_student, w_student[...])
    add_total(GAIN_TWO, d_second * unit_two)
    add_total(SHIFT_TWO, d_second)
    d_resid_two = norm_back(d_second, vector(GAIN_TWO), unit_two, inverse_two)
    d_down = d_resid_two.astype(BF16)
    d_down_ref[...] = d_down
    add_total(B_DOWN, d_down)
    for start in range(0, FF, CHUNK):
        cols = slice(start, start + CHUNK)
        d_active = right_product(d_down, w_down[cols, :])
        d_up = (d_active * slope[:, cols].astype(F32)).astype(BF16)
        d_up_ref[:, cols] = d_up
        totals[B_UP : B_UP + 1, cols] += column_sum(d_up)
    d_first = d_resid_two + right_product(d_up_ref[...], w_up[...])
    add_total(GAIN_ONE, d_first * unit_one)
    add_total(SHIFT_ONE, d_first)
    d_resid_one = norm_back(d_first, vector(GAIN_ONE), unit_one, inverse_one)
    d_resid_ref[...] = d_resid_one
    d_branch = d_resid_one.astype(BF16)
    d_branch_ref[...] = d_branch
    add_total(B_OUT, d_branch)
    d_context_ref[...] = right_product(d_branch, w_out[...]).astype(BF16)

    @pl.when(tile == pl.num_programs(0) - 1)
    def _():
        g_small[...] = jnp.zeros_like(g_small)
        for index, (start, count) in enumerate(VECTORS):
            for place in range(count):
                g_small[start + place : start + place + 1, :] = totals[
                    index : index + 1, place * BLK : (place + 1) * BLK
                ]
        g_small[CLASS_ROW : CLASS_ROW + NCLS, :] = g_class[:NCLS, :]
        g_small[LAST_ROW : LAST_ROW + 1, :] = g_last[...]


def feed(
    len_short, len_long, code, x, context, cot_short, cot_long, logit_cot, small, early, late, short_tiles, width
):
    tiles = x.shape[0] // TILE
    long_tiles = tiles - short_tiles

    def whole(shape):
        return pl.BlockSpec(shape, lambda tile, *_: (0,) * len(shape), pipeline_mode=pl.Buffered(1))

    def kept(shape):
        return pl.BlockSpec(shape, lambda tile, *_: (0,) * len(shape))

    def rows(columns):
        return pl.BlockSpec((TILE, columns), lambda tile, *_: (tile, 0))

    short_rows = pl.BlockSpec((TILE, D), lambda tile, *_: (short_index(tile, short_tiles), 0))
    long_rows = pl.BlockSpec((TILE, D), lambda tile, *_: (long_index(tile, short_tiles), 0))
    logit_rows = pl.BlockSpec((1, 8, SD), lambda tile, *_: (tile, 0, 0))
    grad_shapes = ((D, SD), (SD, SD), (SMALL_ROWS, BLK))
    total = tiles * TILE
    return pl.pallas_call(
        partial(feed_kernel, short_tiles=short_tiles, width=width),
        grid_spec=pltpu.PrefetchScalarGridSpec(
            num_scalar_prefetch=3,
            grid=(tiles,),
            in_specs=[rows(D), rows(D), short_rows, long_rows, logit_rows]
            + [whole(array.shape) for array in small]
            + [pl.BlockSpec(memory_space=pl.ANY)] * 2,
            out_specs=[
                short_rows,
                long_rows,
                logit_rows,
                rows(D),
                rows(FF),
                rows(FF),
                rows(D),
                rows(D),
                rows(D),
                rows(D),
            ]
            + [kept(shape) for shape in grad_shapes],
            scratch_shapes=[
                pltpu.VMEM((TILE, FF), BF16),
                pltpu.VMEM((8, SD), F32),
                pltpu.VMEM((TILE, SD), BF16),
                pltpu.VMEM((D, D), BF16),
                pltpu.VMEM((D, FF), BF16),
                pltpu.VMEM((FF, D), BF16),
                pltpu.VMEM((D, SD), BF16),
                pltpu.VMEM((SD, SD), BF16),
                pltpu.VMEM((16, FF), F32),
                pltpu.VMEM((16, FF), F32),
                pltpu.VMEM((SD, SD), F32),
                pltpu.VMEM((1, SD), F32),
                pltpu.SemaphoreType.DMA((5,)),
            ],
        ),
        out_shape=[
            jax.ShapeDtypeStruct((short_tiles * TILE, D), BF16),
            jax.ShapeDtypeStruct((long_tiles * TILE, D), BF16),
            jax.ShapeDtypeStruct((tiles, 8, SD), F32),
            jax.ShapeDtypeStruct((total, D), BF16),
            jax.ShapeDtypeStruct((total, FF), BF16),
            jax.ShapeDtypeStruct((total, FF), BF16),
            jax.ShapeDtypeStruct((total, D), BF16),
            jax.ShapeDtypeStruct((total, D), BF16),
            jax.ShapeDtypeStruct((total, D), BF16),
            jax.ShapeDtypeStruct((total, D), F32),
        ]
        + [jax.ShapeDtypeStruct(shape, F32) for shape in grad_shapes],
        compiler_params=pltpu.CompilerParams(vmem_limit_bytes=62 * MIB),
        cost_estimate=pl.CostEstimate(
            flops=total * (8 * D * FF + 4 * D * D), bytes_accessed=70 * MIB, transcendentals=total * FF
        ),
        name="feed",
    )(len_short, len_long, code, x, context, cot_short, cot_long, logit_cot, *small, early, late)


class Place:
    def __init__(self):
        self.quarter = lax.axis_index("dp")
        self.shard = lax.axis_index("fsdp")
        x = self.quarter % 2
        y = self.quarter // 2
        self.core = self.shard % 2
        self.z = self.shard // 2
        self.high = self.z // 2
        self.by_x = 2 * y + 1 - x
        self.by_y = 2 * (1 - y) + x
        self.across = 2 * (1 - y) + 1 - x
        self.sibling = (self.quarter, 2 * self.z + 1 - self.core)
        self.next_x = (self.by_x, self.shard)
        self.next_y = (self.by_y, self.shard)
        self.inner = (self.z > 0) & (self.z < 3)

    def at_z(self, z):
        return (self.quarter, 2 * z + self.core)


def transfer(source, target, send_sem, recv_sem, device):
    return pltpu.make_async_remote_copy(
        src_ref=source,
        dst_ref=target,
        send_sem=send_sem,
        recv_sem=recv_sem,
        device_id=device,
        device_id_type=pl.DeviceIdType.MESH,
    )


def greet(place, extra=()):
    barrier = pltpu.get_barrier_semaphore()

    def signal(device):
        pl.semaphore_signal(barrier, inc=1, device_id=device, device_id_type=pl.DeviceIdType.MESH)

    near = (place.sibling, place.next_x, place.next_y) + tuple(extra)
    for device in near:
        signal(device)

    @pl.when(place.z > 0)
    def _():
        signal(place.at_z(place.z - 1))

    @pl.when(place.z < 3)
    def _():
        signal(place.at_z(place.z + 1))

    pl.semaphore_wait(barrier, len(near) + 1 + (place.z + 1) // 2 % 2)


GATHER_SEMAPHORES = [
    pltpu.SemaphoreType.DMA((2,)),
    pltpu.SemaphoreType.DMA((3,)),
    pltpu.SemaphoreType.DMA((4,)),
    pltpu.SemaphoreType.DMA((12,)),
    pltpu.SemaphoreType.DMA((12,)),
    pltpu.SemaphoreType.DMA((16,)),
    pltpu.SemaphoreType.DMA((16,)),
    pltpu.SemaphoreType.DMA((8,)),
]


class Gather:
    def __init__(self, full, out, sems):
        self.place = place = Place()
        self.full, self.out = full, out
        (
            self.own_send,
            self.relay_send,
            self.z_recv,
            self.xy_send,
            self.xy_recv,
            self.core_send,
            self.core_recv,
            self.out_sems,
        ) = sems
        self.quarter = full.shape[1] // 4
        self.half = self.quarter // 2
        z = place.z
        self.origins = (z + 1 - 2 * (z % 2), 2 - place.high, 3 * (1 - place.high))
        self.relays = (3 - z, 3 * (z - 1), 3 * (z - 1))

    def region(self, which, start, size):
        return self.full.at[which, pl.ds(pl.multiple_of(start, 16), size)]

    def pieces(self, which):
        place, quarter, half = self.place, self.quarter, self.half
        return (
            self.region(which, place.quarter * quarter, quarter),
            self.region(which, place.by_x * quarter, quarter),
            self.region(which, place.by_y * quarter, quarter),
            self.region(which, place.across * quarter, half),
            self.region(which, place.across * quarter + half, half),
        )

    def mine(self):
        return self.region(self.place.shard, self.place.quarter * self.quarter, self.quarter)

    def own_copy(self, side):
        place = self.place
        mine = self.mine()
        device = place.at_z(place.z - 1 + 2 * side)
        return transfer(mine, mine, self.own_send.at[side], self.z_recv.at[place.z], device)

    def core_copy(self, index, ref):
        return transfer(ref, ref, self.core_send.at[index], self.core_recv.at[index], self.place.sibling)

    def xy_copy(self, index, ref, device):
        return transfer(ref, ref, self.xy_send.at[index], self.xy_recv.at[index], device)

    def store(self, index, which):
        return pltpu.make_async_copy(self.full.at[which], self.out.at[which], self.out_sems.at[index])

    def mirrored(self, step):
        return 2 * self.origins[step] + 1 - self.place.core

    def held(self, step):
        return 2 * self.origins[step] + self.place.core

    def start(self):
        place = self.place
        greet(place)

        @pl.when(place.z > 0)
        def _():
            self.own_copy(0).start()

        @pl.when(place.z < 3)
        def _():
            self.own_copy(1).start()

        self.core_copy(0, self.full.at[place.shard]).start()
        self.store(0, place.shard).start()

    def relay(self, step):
        piece = self.pieces(self.held(step))[0]
        device = self.place.at_z(self.relays[step])
        return transfer(
            piece, piece, self.relay_send.at[step], self.z_recv.at[self.origins[step]], device
        )

    def along_z(self, step):
        place = self.place
        self.relay(step).wait_recv()

        @pl.when(place.inner)
        def _():
            self.relay(step).start()

        piece = self.pieces(self.held(step))[0]
        self.xy_copy(4 * step, piece, place.next_x).start()
        self.xy_copy(4 * step + 1, piece, place.next_y).start()
        self.core_copy(1 + 5 * step, piece).start()

    def along_xy(self, step):
        place, half = self.place, self.half
        _, by_x, by_y, _, _ = self.pieces(self.held(step))
        self.xy_copy(4 * step, by_x, place.next_x).wait_recv()
        self.xy_copy(4 * step + 2, by_x.at[pl.ds(0, half)], place.next_y).start()
        self.core_copy(2 + 5 * step, by_x).start()
        self.xy_copy(4 * step + 1, by_y, place.next_y).wait_recv()
        self.xy_copy(4 * step + 3, by_y.at[pl.ds(half, half)], place.next_x).start()
        self.core_copy(3 + 5 * step, by_y).start()

    def across(self, step):
        place = self.place
        _, _, _, first, last = self.pieces(self.held(step))
        self.xy_copy(4 * step + 2, first, place.next_y).wait_recv()
        self.core_copy(4 + 5 * step, first).start()
        self.xy_copy(4 * step + 3, last, place.next_x).wait_recv()
        self.core_copy(5 + 5 * step, last).start()
        self.store(2 + 2 * step, self.held(step)).start()

    def core_own(self):
        which = 2 * self.place.z + 1 - self.place.core
        self.core_copy(0, self.full.at[which]).wait_recv()
        self.store(1, which).start()

    def core(self, step):
        which = self.mirrored(step)
        for index, ref in enumerate(self.pieces(which)):
            self.core_copy(1 + 5 * step + index, ref).wait_recv()
        self.store(3 + 2 * step, which).start()

    def finish(self):
        place = self.place

        @pl.when(place.z > 0)
        def _():
            self.own_copy(0).wait_send()

        @pl.when(place.z < 3)
        def _():
            self.own_copy(1).wait_send()

        self.core_copy(0, self.full.at[place.shard]).wait_send()
        self.store(0, place.shard).wait()
        self.store(1, 2 * place.z + 1 - place.core).wait()
        for step in range(3):

            @pl.when(place.inner)
            def _():
                self.relay(step).wait_send()

            pieces = self.pieces(self.held(step))
            self.xy_copy(4 * step, pieces[0], place.next_x).wait_send()
            self.xy_copy(4 * step + 1, pieces[0], place.next_y).wait_send()
            self.xy_copy(4 * step + 2, pieces[3], place.next_y).wait_send()
            self.xy_copy(4 * step + 3, pieces[4], place.next_x).wait_send()
            for index, ref in enumerate(pieces):
                self.core_copy(1 + 5 * step + index, ref).wait_send()
            self.store(2 + 2 * step, self.held(step)).wait()
            self.store(3 + 2 * step, self.mirrored(step)).wait()


def gather_kernel(order_ref, master_ref, early_ref, out_ref, full, *sems):
    gather = Gather(full, out_ref, sems)
    late = full.shape[1] // BLK
    early = master_ref.shape[0] - late

    @pl.loop(0, late)
    def _(index):
        rows = pl.ds(pl.multiple_of(index * BLK, BLK), BLK)
        full[gather.place.shard, rows] = master_ref[order_ref[early + index]].astype(BF16)

    gather.start()

    @pl.loop(0, early)
    def _(index):
        rows = pl.ds(pl.multiple_of(index * BLK, BLK), BLK)
        early_ref[rows] = master_ref[order_ref[index]].astype(BF16)

    gather.along_z(0)
    gather.along_z(1)
    gather.along_xy(0)
    gather.along_z(2)
    gather.along_xy(1)
    gather.across(0)
    gather.core_own()
    gather.along_xy(2)
    gather.across(1)
    gather.core(0)
    gather.across(2)
    gather.core(1)
    gather.core(2)
    gather.finish()


def gather_late(order, master):
    rows = LATE * BLK
    shards = lax.axis_size("fsdp")
    vmem = pl.BlockSpec(memory_space=pltpu.VMEM)
    return pl.pallas_call(
        gather_kernel,
        in_specs=[pl.BlockSpec(memory_space=pltpu.SMEM), vmem],
        out_specs=[vmem, pl.BlockSpec(memory_space=pl.ANY)],
        out_shape=[
            jax.ShapeDtypeStruct((master.shape[0] * BLK - rows, BLK), BF16),
            jax.ShapeDtypeStruct((shards, rows, BLK), BF16),
        ],
        scratch_shapes=[pltpu.VMEM((shards, rows, BLK), BF16)] + GATHER_SEMAPHORES,
        compiler_params=pltpu.CompilerParams(
            collective_id=0, has_side_effects=True, vmem_limit_bytes=60 * MIB
        ),
        cost_estimate=pl.CostEstimate(flops=0, bytes_accessed=100 * MIB, transcendentals=0),
        name="gather",
    )(order, master)


def add_rows(target, former, latter, rows, step):
    @pl.loop(0, rows // step)
    def _(index):
        part = pl.ds(pl.multiple_of(index * step, 16), step)
        target[part] = (former[part].astype(F32) + latter[part].astype(F32)).astype(BF16)


def reduce_scratch(rows):
    quarter = rows // 4
    half = quarter // 2
    return [
        pltpu.VMEM((4, rows, BLK), BF16),
        pltpu.VMEM((4, rows, BLK), BF16),
        pltpu.VMEM((4, 2, half, BLK), BF16),
        pltpu.VMEM((4, 2, half, BLK), BF16),
        pltpu.VMEM((4, half, BLK), BF16),
        pltpu.VMEM((4, half, BLK), BF16),
        pltpu.VMEM((5, quarter, BLK), BF16),
        pltpu.VMEM((rows, BLK), BF16),
        pltpu.SemaphoreType.DMA((4,)),
        pltpu.SemaphoreType.DMA((4,)),
        pltpu.SemaphoreType.DMA((4,)),
        pltpu.SemaphoreType.DMA((24,)),
        pltpu.SemaphoreType.DMA((24,)),
        pltpu.SemaphoreType.DMA((3,)),
        pltpu.SemaphoreType.DMA((5,)),
        pltpu.SemaphoreType.DMA((4,)),
        pltpu.SemaphoreType.DMA((4,)),
    ]


class Reduce:
    def __init__(self, terms, out, scratch):
        self.place = place = Place()
        self.terms, self.out = terms, out
        (
            self.mine,
            self.sib,
            self.from_x,
            self.from_y,
            self.late_y,
            self.late_x,
            self.from_z,
            self.result,
            self.load_sems,
            self.core_send,
            self.core_recv,
            self.xy_send,
            self.xy_recv,
            self.z_send,
            self.z_recv,
            self.last_send,
            self.last_recv,
        ) = scratch
        self.quarter = out.shape[0] // 4
        self.half = self.quarter // 2
        z, high = place.z, place.high
        low = 1 - high
        self.order = (3 * low, low * (2 - 2 * z) + high * (7 - 2 * z), 1 + z % 2, z)
        self.onward = (z + 1 - 2 * high, z + 1 - 2 * (z % 2), z + 1 - 2 * high)
        self.closing = (0, (z % 2) * low, high)
        self.far = place.at_z(z + 2 - 4 * high)
        self.near = place.at_z(z + 1 - 2 * (z % 2))

    def load(self, step):
        source = self.terms.at[2 * self.order[step] + self.place.core]
        return pltpu.make_async_copy(source, self.mine.at[step], self.load_sems.at[step])

    def core_copy(self, step):
        return transfer(
            self.terms.at[2 * self.order[step] + 1 - self.place.core],
            self.sib.at[step],
            self.core_send.at[step],
            self.core_recv.at[step],
            self.place.sibling,
        )

    def part(self, step, which, side):
        start = pl.multiple_of(which * self.quarter + side * self.half, 16)
        return self.mine.at[step, pl.ds(start, self.half)]

    def xy_copy(self, step, index):
        place = self.place
        source, target, device = (
            (self.part(step, place.by_x, 0), self.from_x.at[step, 0], place.next_x),
            (self.part(step, place.across, 0), self.from_x.at[step, 1], place.next_x),
            (self.part(step, place.by_y, 1), self.from_y.at[step, 0], place.next_y),
            (self.part(step, place.across, 1), self.from_y.at[step, 1], place.next_y),
            (self.part(step, place.by_y, 0), self.late_y.at[step], place.next_y),
            (self.part(step, place.by_x, 1), self.late_x.at[step], place.next_x),
        )[index]
        place = 6 * step + index
        return transfer(source, target, self.xy_send.at[place], self.xy_recv.at[place], device)

    def start(self):
        greet(self.place, (self.far,))
        for step in range(4):
            self.load(step).start()
            self.core_copy(step).start()

    def core(self, step):
        place, quarter = self.place, self.quarter
        self.load(step).wait()
        self.core_copy(step).wait_recv()

        def add(which):
            block = pl.ds(pl.multiple_of(which * quarter, 16), quarter)
            mine = self.mine.at[step, block]
            add_rows(mine, mine, self.sib.at[step, block], quarter, self.half)

        add(place.by_x)
        add(place.across)
        self.xy_copy(step, 0).start()
        self.xy_copy(step, 1).start()
        add(place.by_y)
        self.xy_copy(step, 2).start()
        self.xy_copy(step, 3).start()
        add(place.quarter)

    def take(self, step, which, side, index, source):
        self.xy_copy(step, index).wait_recv()
        target = self.part(step, which, side)
        add_rows(target, target, source, self.half, self.half)

    def first(self, step):
        place = self.place
        self.take(step, place.by_y, 0, 1, self.from_x.at[step, 1])
        self.xy_copy(step, 4).start()
        self.take(step, place.by_x, 1, 3, self.from_y.at[step, 1])
        self.xy_copy(step, 5).start()
        self.take(step, place.quarter, 0, 0, self.from_x.at[step, 0])
        self.take(step, place.quarter, 1, 2, self.from_y.at[step, 0])

    def own_block(self, step):
        return self.mine.at[step, pl.ds(pl.multiple_of(self.place.quarter * self.quarter, 16), self.quarter)]

    def z_copy(self, step):
        goal = self.order[step]
        slot = goal + self.closing[step] * (4 - goal)
        return transfer(
            self.own_block(step),
            self.from_z.at[slot],
            self.z_send.at[step],
            self.z_recv.at[slot],
            self.place.at_z(self.onward[step]),
        )

    def take_z(self, step, slot):
        source = self.from_z.at[slot]
        transfer(source, source, self.z_send.at[0], self.z_recv.at[slot], self.near).wait_recv()
        block = self.own_block(step)
        add_rows(block, block, source, self.quarter, self.half)

    def second(self, step):
        place = self.place
        self.take(step, place.quarter, 0, 4, self.late_y.at[step])
        self.take(step, place.quarter, 1, 5, self.late_x.at[step])
        if step < 3:

            @pl.when(place.inner)
            def _():
                self.take_z(step, self.order[step])

            self.z_copy(step).start()
        else:

            @pl.when(place.z > 0)
            def _():
                self.take_z(step, place.z)

            @pl.when(place.z < 3)
            def _():
                self.take_z(step, 4)

    def final(self, which, side=None):
        start = pl.multiple_of(which * self.quarter + (0 if side is None else side * self.half), 16)
        return self.result.at[pl.ds(start, self.quarter if side is None else self.half)]

    def last_copy(self, index, ref):
        device = (self.place.next_x, self.place.next_y, self.place.next_y, self.place.next_x)[index]
        return transfer(ref, ref, self.last_send.at[index], self.last_recv.at[index], device)

    def share(self):
        own = self.final(self.place.quarter)
        own[...] = self.own_block(3)[...]
        self.last_copy(0, own).start()
        self.last_copy(1, own).start()

    def share_on(self):
        place = self.place
        self.last_copy(0, self.final(place.by_x)).wait_recv()
        self.last_copy(2, self.final(place.by_x, 0)).start()
        self.last_copy(1, self.final(place.by_y)).wait_recv()
        self.last_copy(3, self.final(place.by_y, 1)).start()

    def finish(self):
        place = self.place
        self.last_copy(2, self.final(place.across, 0)).wait_recv()
        self.last_copy(3, self.final(place.across, 1)).wait_recv()
        self.out[...] = self.result[...]
        for step in range(4):
            self.core_copy(step).wait_send()
            for index in range(6):
                self.xy_copy(step, index).wait_send()
            if step < 3:
                self.z_copy(step).wait_send()
        own = self.final(place.quarter)
        self.last_copy(0, own).wait_send()
        self.last_copy(1, own).wait_send()
        self.last_copy(2, self.final(place.by_x, 0)).wait_send()
        self.last_copy(3, self.final(place.by_y, 1)).wait_send()


def reduce_kernel(terms, small_ref, out_ref, small_out, small_in, small_sum, small_send, small_recv, *scratch):
    reduce = Reduce(terms, out_ref, scratch)
    place = reduce.place
    partners = (place.sibling, place.next_x, place.next_y, reduce.near, reduce.far)

    def small_copy(level):
        return transfer(
            small_sum.at[level],
            small_in.at[level],
            small_send.at[level],
            small_recv.at[level],
            partners[level],
        )

    def small_step(level):
        small_copy(level - 1).wait_recv()
        small_sum[level] = small_sum[level - 1] + small_in[level - 1]
        if level < 5:
            small_copy(level).start()

    small_sum[0] = small_ref[...]
    reduce.start()
    small_copy(0).start()
    reduce.core(0)
    small_step(1)
    reduce.core(1)
    reduce.first(0)
    small_step(2)
    reduce.core(2)
    reduce.first(1)
    reduce.second(0)
    small_step(3)
    reduce.core(3)
    reduce.first(2)
    reduce.second(1)
    small_step(4)
    reduce.first(3)
    reduce.second(2)
    small_step(5)
    small_out[...] = small_sum[5]
    reduce.second(3)
    reduce.share()
    reduce.share_on()
    reduce.finish()
    for level in range(5):
        small_copy(level).wait_send()


def reduce_late(terms, small):
    rows = terms.shape[1]
    vmem = pl.BlockSpec(memory_space=pltpu.VMEM)
    return pl.pallas_call(
        reduce_kernel,
        in_specs=[pl.BlockSpec(memory_space=pl.ANY), vmem],
        out_specs=[vmem, vmem],
        out_shape=[
            jax.ShapeDtypeStruct((rows, BLK), BF16),
            jax.ShapeDtypeStruct((SMALL_ROWS, BLK), F32),
        ],
        scratch_shapes=[
            pltpu.VMEM((5, SMALL_ROWS, BLK), F32),
            pltpu.VMEM((6, SMALL_ROWS, BLK), F32),
            pltpu.SemaphoreType.DMA((5,)),
            pltpu.SemaphoreType.DMA((5,)),
        ]
        + reduce_scratch(rows),
        compiler_params=pltpu.CompilerParams(
            collective_id=3, has_side_effects=True, vmem_limit_bytes=48 * MIB
        ),
        cost_estimate=pl.CostEstimate(flops=0, bytes_accessed=200 * MIB, transcendentals=0),
        name="reduce",
    )(terms, small)


def count_where(condition, axis):
    return jnp.sum(condition.astype(jnp.int32), axis=axis)


def slot_codes(slots, qkv_slots, slot_count, shards):
    early = slot_count - LATE
    shard = slots // slot_count
    begin = shard * slot_count
    inside = (qkv_slots[None, :] >= begin[:, None]) & (qkv_slots[None, :] < (begin + slot_count)[:, None])
    own = count_where(qkv_slots[None, :] == slots[:, None], 1)
    before = count_where(inside & (qkv_slots[None, :] < slots[:, None]), 1)
    number = count_where(inside, 1)
    position = jnp.where(own > 0, slot_count - number + before, slots - begin - before)
    return jnp.where(
        position < early,
        shard * early + position,
        shards * early + shard * LATE + position - early,
    ), position


def empty_slots(block_slot, all_slots):
    places = jnp.arange(all_slots, dtype=jnp.int32)
    empty_before = places + 1 - count_where(block_slot[None, :] <= places[:, None], 1)
    empty_index = jnp.arange(all_slots - NBLK, dtype=jnp.int32)
    return count_where(empty_before[None, :] <= empty_index[:, None], 1)


def body(
    x_short,
    x_long,
    cot_short,
    cot_long,
    logit_cot_short,
    logit_cot_long,
    len_short,
    len_long,
    block_slot,
    master,
    left_stat,
    right_stat,
    left_root,
    right_root,
    small_params,
    small_first,
    small_second,
    own_transfers,
):
    slot_count = master.shape[0]
    shards = lax.axis_size("fsdp")
    all_slots = slot_count * shards
    short_seqs, width = x_short.shape[:2]
    long_seqs = x_long.shape[0]
    short_tiles = short_seqs * width // TILE
    per_tile = TILE // width
    empty = empty_slots(block_slot, all_slots)

    def gather_all():
        return lax.all_gather(master.astype(BF16), "fsdp", axis=0, tiled=True)

    if own_transfers:
        early_count = slot_count - LATE
        qkv_slots = block_slot[: 3 * 36]
        code, _ = slot_codes(block_slot, qkv_slots, slot_count, shards)
        empty_code, _ = slot_codes(empty, qkv_slots, slot_count, shards)
        own = jnp.arange(slot_count, dtype=jnp.int32)
        _, position = slot_codes(
            own + slot_count * lax.axis_index("fsdp"), qkv_slots, slot_count, shards
        )
        order = jnp.sum(jnp.where(position[None, :] == own[:, None], own[None, :], 0), axis=1)
        qkv_index = jnp.maximum(code[: 3 * 36] - shards * early_count, 0)
        shard_index = jnp.arange(shards, dtype=jnp.int32)
        most = jnp.max(count_where(qkv_slots[None, :] // slot_count == shard_index[:, None], 1))
        fits = most <= LATE
        early, late = gather_late(order, master)
        late = late.reshape(-1, BLK, BLK)
        w_qkv = lax.cond(
            fits,
            lambda: assemble(qkv_index, late),
            lambda: assemble(block_slot, gather_all()),
        )
    else:
        code, early = block_slot, None
        gathered = late = gather_all()
        w_qkv = assemble(block_slot, gathered)
    pieces = unpack(small_params)
    params = jnp.pad(small_params, (0, SMALL_ROWS * BLK - small_params.shape[0])).reshape(SMALL_ROWS, BLK)
    w_class = jnp.pad(pieces[-2].reshape(SD, NCLS), ((0, 0), (0, SD - NCLS)))
    b_class = jnp.pad(pieces[-1].reshape(1, NCLS), ((0, 0), (0, SD - NCLS)))

    x = jnp.concatenate([x_short.reshape(-1, D), x_long.reshape(-1, D)], axis=0)
    *qkv, context, probs_short, probs_long = attention(
        len_short,
        len_long,
        x,
        pieces[0].reshape(1, D),
        pieces[1].reshape(1, D),
        w_qkv,
        short_tiles,
        width,
        early,
    )
    if own_transfers:
        qkv, context, probs_short, probs_long, gathered = qkv[:3], qkv[3], context, probs_short, probs_long
        gathered = gathered.reshape(-1, BLK, BLK)

    logit_cot = jnp.concatenate(
        [
            jnp.pad(
                logit_cot_short.reshape(short_tiles, per_tile, NCLS),
                ((0, 0), (0, 8 - per_tile), (0, SD - NCLS)),
            ),
            jnp.pad(logit_cot_long.reshape(long_seqs, 1, NCLS), ((0, 0), (0, 7), (0, SD - NCLS))),
        ],
        axis=0,
    )
    (
        enc_short,
        enc_long,
        logits,
        first,
        active,
        d_up,
        d_down,
        d_branch,
        d_context,
        d_resid,
        g_student,
        g_hidden,
        g_small,
    ) = feed(
        len_short,
        len_long,
        code,
        x,
        context,
        cot_short.reshape(-1, D),
        cot_long.reshape(-1, D),
        logit_cot,
        (params, w_class, b_class),
        gathered,
        late,
        short_tiles,
        width,
    )
    g_down = left_product(active, d_down).astype(BF16)
    g_up = left_product(first, d_up).astype(BF16)
    g_out = left_product(context, d_branch).astype(BF16)
    others = (g_out, g_up, g_down, g_student.astype(BF16), g_hidden.astype(BF16))
    terms = None
    if own_transfers:
        early_terms, late_terms = spread(
            code, empty_code, others, OTHER_PLACES, shards * early_count, shards * LATE
        )
        terms = early_terms.reshape(shards, early_count * BLK, BLK)
    d_query, d_key, d_value, in_short, in_long, g_b_query, g_b_value, *reduced = attention_back(
        qkv, probs_short, probs_long, d_context, d_resid, w_qkv, short_tiles, terms
    )
    qkv_grads = tuple(left_product(x, d_rows).astype(BF16) for d_rows in (d_query, d_key, d_value))

    def reduce_all():
        slot_terms, _ = spread(
            block_slot, empty, qkv_grads + others, QKV_PLACES + OTHER_PLACES, all_slots, 1
        )
        return lax.psum(lax.psum_scatter(slot_terms, "fsdp", scatter_dimension=0, tiled=True), "dp")

    if own_transfers:
        late_terms, small_terms = spread_late(
            qkv_index, qkv_grads, g_small, g_b_query, g_b_value, late_terms
        )
        late_reduced, small_total = reduce_late(late_terms.reshape(shards, LATE * BLK, BLK), small_terms)

        def join():
            blocks = jnp.concatenate([reduced[0], late_reduced], axis=0).reshape(slot_count, BLK, BLK)
            return jnp.take(blocks, position, axis=0)

        slot_grad = lax.cond(fits, join, reduce_all)
    else:
        slot_grad = reduce_all()
        small_terms = jnp.concatenate(
            [g_b_query.reshape(-1, BLK), g_b_value.reshape(-1, BLK), g_small[2 * D // BLK :]], axis=0
        )
        small_total = lax.psum(small_terms, ("dp", "fsdp"))
    slot_grad = slot_grad.astype(F32)
    small_grad = jnp.concatenate(
        [
            small_total[:CLASS_ROW].reshape(-1),
            small_total[CLASS_ROW : CLASS_ROW + NCLS].T.reshape(-1),
            small_total[LAST_ROW, :NCLS],
        ]
    )
    outer_left = jnp.einsum("sij,skj->sik", slot_grad, slot_grad, precision=HIGHEST_PRECISION)
    outer_right = jnp.einsum("sji,sjk->sik", slot_grad, slot_grad, precision=HIGHEST_PRECISION)
    new_left = STAT_DECAY * left_stat + (1.0 - STAT_DECAY) * outer_left
    new_right = STAT_DECAY * right_stat + (1.0 - STAT_DECAY) * outer_right
    left_applied = jnp.einsum("sij,sjk->sik", left_root, slot_grad, precision=HIGHEST_PRECISION)
    conditioned = jnp.einsum("sij,sjk->sik", left_applied, right_root, precision=HIGHEST_PRECISION)
    new_master = master - MATRIX_RATE * conditioned
    new_first = BETA_ONE * small_first + (1.0 - BETA_ONE) * small_grad
    new_second = BETA_TWO * small_second + (1.0 - BETA_TWO) * small_grad * small_grad
    first_hat = new_first / (1.0 - BETA_ONE**STEP)
    second_hat = new_second / (1.0 - BETA_TWO**STEP)
    new_small = small_params - ADAM_RATE * first_hat / (jnp.sqrt(second_hat) + ADAM_EPSILON)
    return (
        enc_short.reshape(x_short.shape),
        logits[:short_tiles, :per_tile, :NCLS].reshape(short_seqs, NCLS),
        enc_long.reshape(x_long.shape),
        logits[short_tiles:, 0, :NCLS],
        in_short.reshape(x_short.shape),
        in_long.reshape(x_long.shape),
        slot_grad,
        new_left,
        new_right,
        new_master,
        new_first,
        new_second,
        new_small,
    )


def solution(mesh):
    both = ("dp", "fsdp")
    placed = (
        P(both, None, None),
        P(both, None, None),
        P(both, None, None),
        P(both, None, None),
        P(both, None),
        P(both, None),
        P(both),
        P(both),
        P(),
        P("fsdp", None, None),
        P("fsdp", None, None),
        P("fsdp", None, None),
        P("fsdp", None, None),
        P("fsdp", None, None),
        P(),
        P(),
        P(),
    )
    return jax.shard_map(
        partial(body, own_transfers=(mesh.shape["dp"], mesh.shape["fsdp"]) == (4, 8)),
        mesh=mesh,
        in_specs=placed,
        out_specs=(
            P(both, None, None),
            P(both, None),
            P(both, None, None),
            P(both, None),
            P(both, None, None),
            P(both, None, None),
            P("fsdp", None, None),
            P("fsdp", None, None),
            P("fsdp", None, None),
            P("fsdp", None, None),
            P(),
            P(),
            P(),
        ),
        check_vma=False,
    )
```

```python
from functools import partial

import jax
import jax.numpy as jnp
from jax import lax
from jax.experimental import pallas as pl
from jax.experimental.pallas import tpu as pltpu
from jax.sharding import PartitionSpec as P

D = 768
HEADS = 12
FF = 3072
SD = 128
PH = 2
NCLS = 14
BLK = 128
STEP = 10
NBLK = 439
TILE = 512
PAIRS = 3
GROUPS = 2
CHUNK = 768
LATE = 24

NORM_EPSILON = 1e-12
BETA_ONE = 0.9
BETA_TWO = 0.999
ADAM_EPSILON = 1e-08
ADAM_RATE = 0.1
MATRIX_RATE = 0.2
STAT_DECAY = 0.5
MASKED_SCORE = -1e30
HIGHEST_PRECISION = lax.Precision.HIGHEST
MIB = 1024 * 1024
F32 = jnp.float32
BF16 = jnp.bfloat16

def product(former, latter, precision=None):
    return jnp.dot(former, latter, preferred_element_type=F32, precision=precision)


def left_product(former, latter, precision=None):
    return lax.dot_general(
        former, latter, (((0,), (0,)), ((), ())), preferred_element_type=F32, precision=precision
    )


def right_product(former, latter, precision=None):
    return lax.dot_general(
        former, latter, (((1,), (1,)), ((), ())), preferred_element_type=F32, precision=precision
    )


def unpack(small_values):
    widths = (D, D, D, D, D, FF, D, D, D, SD, SD, SD, SD * NCLS, NCLS)
    pieces = []
    offset = 0
    for column_count in widths:
        pieces.append(small_values[offset : offset + column_count])
        offset += column_count
    return pieces


def load_blocks(slot_ref, blocks, target, sem, first, row_count, col_count, col_start=0):
    def move(index, carry):
        row = pl.multiple_of((index // col_count) * BLK, BLK)
        col = pl.multiple_of((index % col_count + col_start) * BLK, BLK)
        pltpu.make_async_copy(
            blocks.at[slot_ref[first + index]],
            target.at[pl.ds(row, BLK), pl.ds(col, BLK)],
            sem,
        ).start()
        return carry

    lax.fori_loop(0, row_count * col_count, move, 0)


def wait_whole(target, sem):
    pltpu.make_async_copy(target, target, sem).wait()


def assemble_kernel(slot_ref, blocks, out, sem):
    for which in range(3):
        load_blocks(slot_ref, blocks, out, sem, 36 * which, 6, 6, 6 * which)
    wait_whole(out, sem)


def assemble(block_slot, blocks):
    return pl.pallas_call(
        assemble_kernel,
        grid_spec=pltpu.PrefetchScalarGridSpec(
            num_scalar_prefetch=1,
            grid=(1,),
            in_specs=[pl.BlockSpec(memory_space=pl.ANY)],
            out_specs=pl.BlockSpec(memory_space=pltpu.VMEM),
            scratch_shapes=[pltpu.SemaphoreType.DMA],
        ),
        out_shape=jax.ShapeDtypeStruct((D, 3 * D), BF16),
        compiler_params=pltpu.CompilerParams(vmem_limit_bytes=16 * MIB),
        name="assemble",
    )(block_slot, blocks)


QKV_PLACES = ((0, 6, 6), (36, 6, 6), (72, 6, 6))
OTHER_PLACES = ((108, 6, 6), (144, 6, 24), (288, 24, 6), (432, 6, 1), (438, 1, 1))


def spread_kernel(code_ref, empty_ref, *refs, places):
    grads = refs[: len(places)]
    zero, out, sems = refs[len(places) :]
    for which, (grad, (first, row_count, col_count)) in enumerate(zip(grads, places)):

        def move(index, carry, which=which, grad=grad, first=first, col_count=col_count):
            row = pl.multiple_of((index // col_count) * BLK, BLK)
            col = pl.multiple_of((index % col_count) * BLK, BLK)
            pltpu.make_async_copy(
                grad.at[pl.ds(row, BLK), pl.ds(col, BLK)],
                out.at[code_ref[first + index]],
                sems.at[which],
            ).start()
            return carry

        lax.fori_loop(0, row_count * col_count, move, 0)
    for index in range(empty_ref.shape[0]):
        pltpu.make_async_copy(zero, out.at[empty_ref[index]], sems.at[len(places) + index]).start()
    for which, grad in enumerate(grads):
        wait_whole(grad, sems.at[which])
    for index in range(empty_ref.shape[0]):
        wait_whole(zero, sems.at[len(places) + index])


def spread(code, empty, grads, places, slot_count):
    vmem = pl.BlockSpec(memory_space=pltpu.VMEM)
    return pl.pallas_call(
        partial(spread_kernel, places=places),
        grid_spec=pltpu.PrefetchScalarGridSpec(
            num_scalar_prefetch=2,
            grid=(1,),
            in_specs=[vmem] * (len(grads) + 1),
            out_specs=pl.BlockSpec(memory_space=pl.ANY),
            scratch_shapes=[pltpu.SemaphoreType.DMA((len(grads) + empty.shape[0],))],
        ),
        out_shape=jax.ShapeDtypeStruct((slot_count, BLK, BLK), BF16),
        compiler_params=pltpu.CompilerParams(vmem_limit_bytes=24 * MIB),
        name="spread",
    )(code, empty, *grads, jnp.zeros((BLK, BLK), BF16))


def spread_late_kernel(code_ref, *refs):
    grads = refs[:3]
    small_ref, query_ref, value_ref, _, out, small_out, sems = refs[3:]
    for which, (grad, (first, row_count, col_count)) in enumerate(zip(grads, QKV_PLACES)):

        def move(index, carry, which=which, grad=grad, first=first, col_count=col_count):
            row = pl.multiple_of((index // col_count) * BLK, BLK)
            col = pl.multiple_of((index % col_count) * BLK, BLK)
            pltpu.make_async_copy(
                grad.at[pl.ds(row, BLK), pl.ds(col, BLK)],
                out.at[code_ref[first + index]],
                sems.at[which],
            ).start()
            return carry

        lax.fori_loop(0, row_count * col_count, move, 0)
    join_small(small_ref, query_ref, value_ref, small_out)
    for which, grad in enumerate(grads):
        wait_whole(grad, sems.at[which])


def join_small(small_ref, query_ref, value_ref, small_out):
    small_out[...] = small_ref[...]
    for start, ref in ((0, query_ref), (D // BLK, value_ref)):
        for index in range(D // BLK):
            small_out[start + index : start + index + 1, :] = ref[:, index * BLK : (index + 1) * BLK]


def spread_late(code, grads, small, g_query, g_value, terms):
    vmem = pl.BlockSpec(memory_space=pltpu.VMEM)
    anywhere = pl.BlockSpec(memory_space=pl.ANY)
    return pl.pallas_call(
        spread_late_kernel,
        grid_spec=pltpu.PrefetchScalarGridSpec(
            num_scalar_prefetch=1,
            grid=(1,),
            in_specs=[vmem] * 6 + [anywhere],
            out_specs=[anywhere, vmem],
            scratch_shapes=[pltpu.SemaphoreType.DMA((3,))],
        ),
        out_shape=[
            jax.ShapeDtypeStruct(terms.shape, BF16),
            jax.ShapeDtypeStruct(small.shape, F32),
        ],
        input_output_aliases={7: 0},
        compiler_params=pltpu.CompilerParams(vmem_limit_bytes=24 * MIB),
        name="spread_late",
    )(code, *grads, small, g_query, g_value, terms)


def half_masks():
    lane = lax.broadcasted_iota(jnp.int32, (1, BLK), 1)
    low = (lane < BLK // 2).astype(BF16)
    return low, (1.0 - low.astype(F32)).astype(BF16)


def stack_heads(values, low, high):
    return jnp.concatenate([values * low, values * high], axis=0)


def pick_heads(values):
    rows = values.shape[0] // 2
    lane = lax.broadcasted_iota(jnp.int32, (rows, BLK), 1)
    return jnp.where(lane < BLK // 2, values[:rows], values[rows:])


def attend(queries, key_rows, value_rows, length, low, high):
    scores = right_product(stack_heads(queries, low, high), key_rows)
    visible = lax.broadcasted_iota(jnp.int32, scores.shape, 1) < length
    scores = jnp.where(visible, scores, MASKED_SCORE)
    powers = jnp.exp(scores - jnp.max(scores, axis=-1, keepdims=True))
    total = jnp.sum(powers, axis=-1, keepdims=True)
    probs = (powers * (1.0 / total)).astype(BF16)
    return probs, pick_heads(product(probs, value_rows)).astype(BF16)


def attention_kernel(
    len_short,
    len_long,
    x_ref,
    b_query,
    b_value,
    w_ref,
    q_ref,
    k_ref,
    v_ref,
    context_ref,
    short_ref,
    long_ref,
    *,
    short_tiles,
):
    tile = pl.program_id(0)
    group = pl.program_id(1)
    low, high = half_masks()
    width = short_ref.shape[-1]
    per_tile = TILE // width

    wide = PAIRS * BLK
    start = pl.multiple_of(group * wide, wide)
    rows_in = x_ref[...]
    queries = product(rows_in, w_ref[:, pl.ds(start, wide)]) + b_query[:, pl.ds(start, wide)]
    q_ref[...] = (queries * 0.125).astype(BF16)
    k_ref[...] = product(rows_in, w_ref[:, pl.ds(D + start, wide)]).astype(BF16)
    values = product(rows_in, w_ref[:, pl.ds(2 * D + start, wide)]) + b_value[:, pl.ds(start, wide)]
    v_ref[...] = values.astype(BF16)

    @pl.when(tile < short_tiles)
    def _():
        for pair in range(PAIRS):
            cols = slice(pair * BLK, (pair + 1) * BLK)
            for seq in range(per_tile):
                rows = slice(seq * width, (seq + 1) * width)
                probs, context = attend(
                    q_ref[rows, cols],
                    k_ref[rows, cols],
                    v_ref[rows, cols],
                    len_short[tile * per_tile + seq],
                    low,
                    high,
                )
                short_ref[0, pair, seq] = probs
                context_ref[rows, cols] = context

    @pl.when(tile >= short_tiles)
    def _():
        length = len_long[tile - short_tiles]
        half = TILE // 2
        for pair in range(PAIRS):
            cols = slice(pair * BLK, (pair + 1) * BLK)
            for part in range(2):
                rows = slice(part * half, (part + 1) * half)
                probs, context = attend(
                    q_ref[rows, cols], k_ref[:, cols], v_ref[:, cols], length, low, high
                )
                long_ref[0, pair, part] = probs
                context_ref[rows, cols] = context


def run_events(step, events):
    for index, actions in enumerate(events):

        @pl.when(step == index)
        def _(actions=actions):
            for action in actions:
                action()


def probs_shapes(short_tiles, long_tiles, width):
    per_tile = TILE // width
    return (
        (short_tiles, 2 * PAIRS, per_tile, 2 * width, width),
        (long_tiles, 2 * PAIRS, 2, TILE, TILE),
    )


def short_index(tile, short_tiles):
    return jnp.minimum(tile, short_tiles - 1)


def long_index(tile, short_tiles):
    return jnp.maximum(tile - short_tiles, 0)


def probs_maps(short_tiles):
    def short_map(tile, group):
        last = jnp.minimum(tile // short_tiles, 1)
        return (short_index(tile, short_tiles), group + last * (GROUPS - 1 - group), 0, 0, 0)

    def long_map(tile, group):
        begun = jnp.minimum(tile // short_tiles, 1)
        return (long_index(tile, short_tiles), begun * group, 0, 0, 0)

    return short_map, long_map


def attention(len_short, len_long, x, b_query, b_value, w_qkv, short_tiles, width):
    tiles = x.shape[0] // TILE
    wide = PAIRS * BLK
    short_shape, long_shape = probs_shapes(short_tiles, tiles - short_tiles, width)
    short_map, long_map = probs_maps(short_tiles)
    flops = 4 * D * TILE * TILE * tiles + 6 * D * D * TILE * tiles
    rows = pl.BlockSpec((TILE, wide), lambda tile, group: (tile, group))
    scalars = pl.BlockSpec(memory_space=pltpu.SMEM)

    def whole(shape):
        return pl.BlockSpec(shape, lambda tile, group: (0,) * len(shape), pipeline_mode=pl.Buffered(1))

    in_specs = [
        scalars,
        scalars,
        pl.BlockSpec((TILE, D), lambda tile, group: (tile, 0)),
        whole((1, D)),
        whole((1, D)),
        whole((D, 3 * D)),
    ]
    out_specs = [
        rows,
        rows,
        rows,
        rows,
        pl.BlockSpec((1, PAIRS) + short_shape[2:], short_map),
        pl.BlockSpec((1, PAIRS) + long_shape[2:], long_map),
    ]
    out_shape = [jax.ShapeDtypeStruct((tiles * TILE, D), BF16)] * 4 + [
        jax.ShapeDtypeStruct(short_shape, BF16),
        jax.ShapeDtypeStruct(long_shape, BF16),
    ]
    arguments = [len_short, len_long, x, b_query, b_value, w_qkv]
    return pl.pallas_call(
        partial(attention_kernel, short_tiles=short_tiles),
        grid=(tiles, GROUPS),
        in_specs=in_specs,
        out_specs=out_specs,
        out_shape=out_shape,
        compiler_params=pltpu.CompilerParams(vmem_limit_bytes=40 * MIB),
        cost_estimate=pl.CostEstimate(
            flops=flops, bytes_accessed=35 * MIB, transcendentals=HEADS * TILE * TILE * tiles // 2
        ),
        name="attention",
    )(*arguments)


def attend_back(queries, key_rows, value_rows, d_context, probs, low, high):
    stacked = stack_heads(d_context, low, high)
    d_probs = right_product(stacked, value_rows)
    wide = probs.astype(F32)
    weighted = wide * d_probs
    d_scores = (weighted - wide * jnp.sum(weighted, axis=-1, keepdims=True)).astype(BF16)
    d_queries = pick_heads(product(d_scores, key_rows)) * 0.125
    d_keys = left_product(d_scores, stack_heads(queries, low, high))
    d_values = left_product(probs, stacked)
    return d_queries.astype(BF16), d_keys, d_values


def attention_back_kernel(*refs, short_tiles, transfers):
    q_ref, k_ref, v_ref, short_ref, long_ref, dc_ref, resid_ref, w_ref = refs[:8]
    refs = refs[8:]
    if transfers:
        terms_ref, refs = refs[0], refs[1:]
    dq_ref, dk_ref, dv_ref, in_short_ref, in_long_ref, bq_ref, bv_ref = refs[:7]
    tile = pl.program_id(0)
    group = pl.program_id(1)
    low, high = half_masks()
    width = short_ref.shape[-1]
    per_tile = TILE // width
    if transfers:
        reduce = Reduce(terms_ref, 0, refs[7], refs[8:])
        run_events(
            tile * GROUPS + group,
            (
                (reduce.start,),
                (partial(reduce.core, 0),),
                (partial(reduce.core, 1), partial(reduce.first, 0)),
                (partial(reduce.core, 2), partial(reduce.first, 1), partial(reduce.second, 0)),
                (partial(reduce.core, 3), partial(reduce.first, 2), partial(reduce.second, 1)),
                (partial(reduce.first, 3), partial(reduce.second, 2)),
                (partial(reduce.second, 3), reduce.share),
                (reduce.share_on,),
            ),
        )

    @pl.when(tile < short_tiles)
    def _():
        for pair in range(PAIRS):
            cols = slice(pair * BLK, (pair + 1) * BLK)
            for seq in range(per_tile):
                rows = slice(seq * width, (seq + 1) * width)
                d_queries, d_keys, d_values = attend_back(
                    q_ref[rows, cols],
                    k_ref[rows, cols],
                    v_ref[rows, cols],
                    dc_ref[rows, cols],
                    short_ref[0, pair, seq],
                    low,
                    high,
                )
                dq_ref[rows, cols] = d_queries
                dk_ref[rows, cols] = d_keys.astype(BF16)
                dv_ref[rows, cols] = d_values.astype(BF16)

    @pl.when(tile >= short_tiles)
    def _():
        half = TILE // 2
        for pair in range(PAIRS):
            cols = slice(pair * BLK, (pair + 1) * BLK)
            keys_sum = None
            values_sum = None
            for part in range(2):
                rows = slice(part * half, (part + 1) * half)
                d_queries, d_keys, d_values = attend_back(
                    q_ref[rows, cols],
                    k_ref[:, cols],
                    v_ref[:, cols],
                    dc_ref[rows, cols],
                    long_ref[0, pair, part],
                    low,
                    high,
                )
                dq_ref[rows, cols] = d_queries
                keys_sum = d_keys if keys_sum is None else keys_sum + d_keys
                values_sum = d_values if values_sum is None else values_sum + d_values
            dk_ref[:, cols] = keys_sum.astype(BF16)
            dv_ref[:, cols] = values_sum.astype(BF16)

    wide = PAIRS * BLK
    start = pl.multiple_of(group * wide, wide)

    @pl.when((tile == 0) & (group == 0))
    def _():
        bq_ref[...] = jnp.zeros_like(bq_ref)
        bv_ref[...] = jnp.zeros_like(bv_ref)

    bq_ref[:, pl.ds(start, wide)] += jnp.sum(dq_ref[...].astype(F32), axis=0, keepdims=True)
    bv_ref[:, pl.ds(start, wide)] += jnp.sum(dv_ref[...].astype(F32), axis=0, keepdims=True)
    total = (
        right_product(dq_ref[...], w_ref[:, pl.ds(start, wide)])
        + right_product(dk_ref[...], w_ref[:, pl.ds(D + start, wide)])
        + right_product(dv_ref[...], w_ref[:, pl.ds(2 * D + start, wide)])
    )

    @pl.when((tile < short_tiles) & (group == 0))
    def _():
        in_short_ref[...] = resid_ref[...] + total

    @pl.when((tile < short_tiles) & (group > 0))
    def _():
        in_short_ref[...] += total

    @pl.when((tile >= short_tiles) & (group == 0))
    def _():
        in_long_ref[...] = resid_ref[...] + total

    @pl.when((tile >= short_tiles) & (group > 0))
    def _():
        in_long_ref[...] += total

    if transfers:

        @pl.when((tile == pl.num_programs(0) - 1) & (group == GROUPS - 1))
        def _():
            reduce.finish()


def attention_back(qkv, probs_short, probs_long, d_context, resid, w_qkv, short_tiles, terms=None, count=0):
    tiles = d_context.shape[0] // TILE
    wide = PAIRS * BLK
    short_map, long_map = probs_maps(short_tiles)
    rows = pl.BlockSpec((TILE, wide), lambda tile, group: (tile, group))
    row = pl.BlockSpec((1, D), lambda tile, group: (0, 0))
    flops = 10 * D * TILE * TILE * tiles + 6 * D * D * TILE * tiles
    in_specs = [
        rows,
        rows,
        rows,
        pl.BlockSpec((1, PAIRS) + probs_short.shape[2:], short_map),
        pl.BlockSpec((1, PAIRS) + probs_long.shape[2:], long_map),
        rows,
        pl.BlockSpec((TILE, D), lambda tile, group: (tile, 0)),
        pl.BlockSpec((D, 3 * D), lambda tile, group: (0, 0), pipeline_mode=pl.Buffered(1)),
    ]
    out_specs = [
        rows,
        rows,
        rows,
        pl.BlockSpec((TILE, D), lambda tile, group: (short_index(tile, short_tiles), 0)),
        pl.BlockSpec((TILE, D), lambda tile, group: (long_index(tile, short_tiles), 0)),
        row,
        row,
    ]
    out_shape = [
        jax.ShapeDtypeStruct((tiles * TILE, D), BF16),
        jax.ShapeDtypeStruct((tiles * TILE, D), BF16),
        jax.ShapeDtypeStruct((tiles * TILE, D), BF16),
        jax.ShapeDtypeStruct((short_tiles * TILE, D), F32),
        jax.ShapeDtypeStruct(((tiles - short_tiles) * TILE, D), F32),
        jax.ShapeDtypeStruct((1, D), F32),
        jax.ShapeDtypeStruct((1, D), F32),
    ]
    arguments = [*qkv, probs_short, probs_long, d_context, resid, w_qkv]
    scratch = []
    params = dict(vmem_limit_bytes=52 * MIB)
    if terms is not None:
        arguments.append(terms)
        in_specs.append(pl.BlockSpec(memory_space=pl.ANY))
        out_specs.append(pl.BlockSpec((count, BLK), lambda tile, group: (0, 0)))
        out_shape.append(jax.ShapeDtypeStruct((count, BLK), BF16))
        scratch = reduce_scratch(count)
        params.update(collective_id=2, has_side_effects=True)
    return pl.pallas_call(
        partial(attention_back_kernel, short_tiles=short_tiles, transfers=terms is not None),
        grid=(tiles, GROUPS),
        in_specs=in_specs,
        out_specs=out_specs,
        out_shape=out_shape,
        scratch_shapes=scratch,
        compiler_params=pltpu.CompilerParams(**params),
        cost_estimate=pl.CostEstimate(flops=flops, bytes_accessed=50 * MIB, transcendentals=0),
        name="attention_back",
    )(*arguments)


def normal_parts(values):
    below = 0.5 * lax.erf(values * 0.7071067811865476) + 0.5
    return below, jnp.exp(-0.5 * values * values) * 0.3989422804014327


B_OUT, GAIN_ONE, SHIFT_ONE, B_UP, B_DOWN, GAIN_TWO, SHIFT_TWO, B_STUDENT, POOL_QUERY, B_HIDDEN = range(10)
VECTORS = (
    (12, 6),
    (18, 6),
    (24, 6),
    (30, 24),
    (54, 6),
    (60, 6),
    (66, 6),
    (72, 1),
    (73, 1),
    (74, 1),
)
CLASS_ROW = 75
LAST_ROW = 91
SMALL_ROWS = 96


def norm_parts(values):
    center = values - jnp.mean(values, axis=-1, keepdims=True)
    spread = jnp.mean(center * center, axis=-1, keepdims=True)
    inverse = lax.rsqrt(spread + NORM_EPSILON)
    return center * inverse, inverse


def norm_back(d_values, gain, unit, inverse):
    d_unit = d_values * gain
    return inverse * (
        d_unit
        - jnp.mean(d_unit, axis=-1, keepdims=True)
        - unit * jnp.mean(d_unit * unit, axis=-1, keepdims=True)
    )


def column_sum(values):
    return jnp.sum(values.astype(F32), axis=0, keepdims=True)


def pool_weights(student, query, length):
    scaled = student * query
    lane = lax.broadcasted_iota(jnp.int32, scaled.shape, 1)
    place = lax.broadcasted_iota(jnp.int32, (scaled.shape[0], 1), 0)
    weights = []
    for side in (lane < SD // PH, lane >= SD // PH):
        scores = jnp.sum(jnp.where(side, scaled, 0.0), axis=-1, keepdims=True)
        scores = jnp.where(place < length, scores, MASKED_SCORE)
        powers = jnp.exp(scores - jnp.max(scores, axis=0, keepdims=True))
        weights.append(powers / jnp.sum(powers, axis=0, keepdims=True))
    return jnp.where(lane < SD // PH, weights[0], weights[1]), weights


def student_back(student, query, weights, both, d_pooled):
    lane = lax.broadcasted_iota(jnp.int32, student.shape, 1)
    moved = student * d_pooled
    d_scores = []
    for side, weight in zip((lane < SD // PH, lane >= SD // PH), weights):
        d_weight = jnp.sum(jnp.where(side, moved, 0.0), axis=-1, keepdims=True)
        d_scores.append(weight * (d_weight - jnp.sum(weight * d_weight, axis=0, keepdims=True)))
    d_score = jnp.where(lane < SD // PH, d_scores[0], d_scores[1])
    d_query = jnp.sum(d_score * student, axis=0, keepdims=True) * 0.125
    return both * d_pooled + d_score * query, d_query


def feed_kernel(
    len_short,
    len_long,
    slot_ref,
    x_ref,
    context_ref,
    cot_short_ref,
    cot_long_ref,
    logit_cot_ref,
    params,
    w_class,
    b_class,
    blocks,
    enc_short_ref,
    enc_long_ref,
    logit_ref,
    first_ref,
    active_ref,
    d_up_ref,
    d_down_ref,
    d_branch_ref,
    d_context_ref,
    d_resid_ref,
    g_student,
    g_hidden,
    g_small,
    slope,
    pooled_ref,
    d_student_ref,
    w_out,
    w_up,
    w_down,
    w_student,
    w_hidden,
    vectors,
    totals,
    g_class,
    g_last,
    sems,
    *,
    short_tiles,
    width,
):
    tile = pl.program_id(0)
    per_tile = TILE // width
    loads = ((w_out, 108, 6, 6), (w_up, 144, 6, 24), (w_down, 288, 24, 6), (w_student, 432, 6, 1), (w_hidden, 438, 1, 1))

    def arrive(*indices):
        @pl.when(tile == 0)
        def _():
            for index in indices:
                wait_whole(loads[index][0], sems.at[index])

    @pl.when(tile == 0)
    def _():
        for index, (target, block, row_count, col_count) in enumerate(loads):
            load_blocks(slot_ref, blocks, target, sems.at[index], block, row_count, col_count)
        for index, (start, count) in enumerate(VECTORS):
            for place in range(count):
                vectors[index : index + 1, place * BLK : (place + 1) * BLK] = params[
                    start + place : start + place + 1, :
                ]
        for ref in (totals, g_class, g_last, g_student, g_hidden):
            ref[...] = jnp.zeros_like(ref)

    def vector(index):
        return vectors[index : index + 1, : VECTORS[index][1] * BLK]

    def add_total(index, values):
        totals[index : index + 1, : VECTORS[index][1] * BLK] += column_sum(values)

    arrive(0)
    branch = product(context_ref[...], w_out[...]) + vector(B_OUT)
    unit_one, inverse_one = norm_parts(x_ref[...].astype(F32) + branch)
    first = (unit_one * vector(GAIN_ONE) + vector(SHIFT_ONE)).astype(BF16)
    first_ref[...] = first
    arrive(1)
    for start in range(0, FF, CHUNK):
        cols = slice(start, start + CHUNK)
        upward = product(first, w_up[:, cols]) + vectors[B_UP : B_UP + 1, cols]
        below, density = normal_parts(upward)
        active_ref[:, cols] = (upward * below).astype(BF16)
        slope[:, cols] = (below + upward * density).astype(BF16)
    arrive(2, 3, 4)
    downward = product(active_ref[...], w_down[...]) + vector(B_DOWN)
    unit_two, inverse_two = norm_parts(first.astype(F32) + downward)
    encoded = (unit_two * vector(GAIN_TWO) + vector(SHIFT_TWO)).astype(BF16)

    @pl.when(tile < short_tiles)
    def _():
        enc_short_ref[...] = encoded

    @pl.when(tile >= short_tiles)
    def _():
        enc_long_ref[...] = encoded

    student = product(encoded, w_student[...]) + vector(B_STUDENT)
    query = vector(POOL_QUERY) * 0.125
    pooled_ref[...] = jnp.zeros_like(pooled_ref)

    def head():
        pooled = pooled_ref[...]
        wide_hidden = w_hidden[...].astype(F32)
        hidden = jnp.tanh(product(pooled, wide_hidden, HIGHEST_PRECISION) + vector(B_HIDDEN))
        logit_ref[0] = product(hidden, w_class[...], HIGHEST_PRECISION) + b_class[...]
        d_logits = logit_cot_ref[0]
        g_last[...] += column_sum(d_logits)
        g_class[...] += left_product(d_logits, hidden, HIGHEST_PRECISION)
        d_hidden = right_product(d_logits, w_class[...], HIGHEST_PRECISION)
        d_hidden = d_hidden * (1.0 - hidden * hidden)
        add_total(B_HIDDEN, d_hidden)
        g_hidden[...] += left_product(pooled, d_hidden, HIGHEST_PRECISION)
        return right_product(d_hidden, wide_hidden, HIGHEST_PRECISION)

    def pool(starts, size, lengths):
        kept = []
        for index, (start, length) in enumerate(zip(starts, lengths)):
            rows = student[start : start + size]
            both, weights = pool_weights(rows, query, length)
            pooled_ref[index : index + 1, :] = column_sum(both * rows)
            kept.append((start, rows, both, weights))
        d_pooled = head()
        for index, (start, rows, both, weights) in enumerate(kept):
            d_rows, d_query = student_back(rows, query, weights, both, d_pooled[index : index + 1])
            d_student_ref[start : start + size, :] = d_rows.astype(BF16)
            add_total(POOL_QUERY, d_query)

    @pl.when(tile < short_tiles)
    def _():
        pool(
            [seq * width for seq in range(per_tile)],
            width,
            [len_short[tile * per_tile + seq] for seq in range(per_tile)],
        )

    @pl.when(tile >= short_tiles)
    def _():
        pool([0], TILE, [len_long[tile - short_tiles]])

    d_student = d_student_ref[...]
    add_total(B_STUDENT, d_student)
    g_student[...] += left_product(encoded, d_student)
    cotangent = jnp.where(tile < short_tiles, cot_short_ref[...], cot_long_ref[...])
    d_second = cotangent.astype(F32) + right_product(d_student, w_student[...])
    add_total(GAIN_TWO, d_second * unit_two)
    add_total(SHIFT_TWO, d_second)
    d_resid_two = norm_back(d_second, vector(GAIN_TWO), unit_two, inverse_two)
    d_down = d_resid_two.astype(BF16)
    d_down_ref[...] = d_down
    add_total(B_DOWN, d_down)
    for start in range(0, FF, CHUNK):
        cols = slice(start, start + CHUNK)
        d_active = right_product(d_down, w_down[cols, :])
        d_up = (d_active * slope[:, cols].astype(F32)).astype(BF16)
        d_up_ref[:, cols] = d_up
        totals[B_UP : B_UP + 1, cols] += column_sum(d_up)
    d_first = d_resid_two + right_product(d_up_ref[...], w_up[...])
    add_total(GAIN_ONE, d_first * unit_one)
    add_total(SHIFT_ONE, d_first)
    d_resid_one = norm_back(d_first, vector(GAIN_ONE), unit_one, inverse_one)
    d_resid_ref[...] = d_resid_one
    d_branch = d_resid_one.astype(BF16)
    d_branch_ref[...] = d_branch
    add_total(B_OUT, d_branch)
    d_context_ref[...] = right_product(d_branch, w_out[...]).astype(BF16)

    @pl.when(tile == pl.num_programs(0) - 1)
    def _():
        g_small[...] = jnp.zeros_like(g_small)
        for index, (start, count) in enumerate(VECTORS):
            for place in range(count):
                g_small[start + place : start + place + 1, :] = totals[
                    index : index + 1, place * BLK : (place + 1) * BLK
                ]
        g_small[CLASS_ROW : CLASS_ROW + NCLS, :] = g_class[:NCLS, :]
        g_small[LAST_ROW : LAST_ROW + 1, :] = g_last[...]


def feed(
    len_short, len_long, block_slot, x, context, cot_short, cot_long, logit_cot, small, blocks, short_tiles, width
):
    tiles = x.shape[0] // TILE
    long_tiles = tiles - short_tiles

    def whole(shape):
        return pl.BlockSpec(shape, lambda tile, *_: (0,) * len(shape), pipeline_mode=pl.Buffered(1))

    def kept(shape):
        return pl.BlockSpec(shape, lambda tile, *_: (0,) * len(shape))

    def rows(columns):
        return pl.BlockSpec((TILE, columns), lambda tile, *_: (tile, 0))

    short_rows = pl.BlockSpec((TILE, D), lambda tile, *_: (short_index(tile, short_tiles), 0))
    long_rows = pl.BlockSpec((TILE, D), lambda tile, *_: (long_index(tile, short_tiles), 0))
    logit_rows = pl.BlockSpec((1, 8, SD), lambda tile, *_: (tile, 0, 0))
    grad_shapes = ((D, SD), (SD, SD), (SMALL_ROWS, BLK))
    total = tiles * TILE
    return pl.pallas_call(
        partial(feed_kernel, short_tiles=short_tiles, width=width),
        grid_spec=pltpu.PrefetchScalarGridSpec(
            num_scalar_prefetch=3,
            grid=(tiles,),
            in_specs=[rows(D), rows(D), short_rows, long_rows, logit_rows]
            + [whole(array.shape) for array in small]
            + [pl.BlockSpec(memory_space=pl.ANY)],
            out_specs=[
                short_rows,
                long_rows,
                logit_rows,
                rows(D),
                rows(FF),
                rows(FF),
                rows(D),
                rows(D),
                rows(D),
                rows(D),
            ]
            + [kept(shape) for shape in grad_shapes],
            scratch_shapes=[
                pltpu.VMEM((TILE, FF), BF16),
                pltpu.VMEM((8, SD), F32),
                pltpu.VMEM((TILE, SD), BF16),
                pltpu.VMEM((D, D), BF16),
                pltpu.VMEM((D, FF), BF16),
                pltpu.VMEM((FF, D), BF16),
                pltpu.VMEM((D, SD), BF16),
                pltpu.VMEM((SD, SD), BF16),
                pltpu.VMEM((16, FF), F32),
                pltpu.VMEM((16, FF), F32),
                pltpu.VMEM((SD, SD), F32),
                pltpu.VMEM((1, SD), F32),
                pltpu.SemaphoreType.DMA((5,)),
            ],
        ),
        out_shape=[
            jax.ShapeDtypeStruct((short_tiles * TILE, D), BF16),
            jax.ShapeDtypeStruct((long_tiles * TILE, D), BF16),
            jax.ShapeDtypeStruct((tiles, 8, SD), F32),
            jax.ShapeDtypeStruct((total, D), BF16),
            jax.ShapeDtypeStruct((total, FF), BF16),
            jax.ShapeDtypeStruct((total, FF), BF16),
            jax.ShapeDtypeStruct((total, D), BF16),
            jax.ShapeDtypeStruct((total, D), BF16),
            jax.ShapeDtypeStruct((total, D), BF16),
            jax.ShapeDtypeStruct((total, D), F32),
        ]
        + [jax.ShapeDtypeStruct(shape, F32) for shape in grad_shapes],
        compiler_params=pltpu.CompilerParams(vmem_limit_bytes=62 * MIB),
        cost_estimate=pl.CostEstimate(
            flops=total * (8 * D * FF + 4 * D * D), bytes_accessed=70 * MIB, transcendentals=total * FF
        ),
        name="feed",
    )(len_short, len_long, block_slot, x, context, cot_short, cot_long, logit_cot, *small, blocks)


class Place:
    def __init__(self):
        self.quarter = lax.axis_index("dp")
        self.shard = lax.axis_index("fsdp")
        x = self.quarter % 2
        y = self.quarter // 2
        self.core = self.shard % 2
        self.z = self.shard // 2
        self.high = self.z // 2
        self.by_x = 2 * y + 1 - x
        self.by_y = 2 * (1 - y) + x
        self.across = 2 * (1 - y) + 1 - x
        self.sibling = (self.quarter, 2 * self.z + 1 - self.core)
        self.next_x = (self.by_x, self.shard)
        self.next_y = (self.by_y, self.shard)
        self.inner = (self.z > 0) & (self.z < 3)

    def at_z(self, z):
        return (self.quarter, 2 * z + self.core)


def transfer(source, target, send_sem, recv_sem, device):
    return pltpu.make_async_remote_copy(
        src_ref=source,
        dst_ref=target,
        send_sem=send_sem,
        recv_sem=recv_sem,
        device_id=device,
        device_id_type=pl.DeviceIdType.MESH,
    )


def greet(place, extra=()):
    barrier = pltpu.get_barrier_semaphore()

    def signal(device):
        pl.semaphore_signal(barrier, inc=1, device_id=device, device_id_type=pl.DeviceIdType.MESH)

    near = (place.sibling, place.next_x, place.next_y) + tuple(extra)
    for device in near:
        signal(device)

    @pl.when(place.z > 0)
    def _():
        signal(place.at_z(place.z - 1))

    @pl.when(place.z < 3)
    def _():
        signal(place.at_z(place.z + 1))

    pl.semaphore_wait(barrier, len(near) + 1 + (place.z + 1) // 2 % 2)


GATHER_SEMAPHORES = [
    pltpu.SemaphoreType.DMA((2,)),
    pltpu.SemaphoreType.DMA((3,)),
    pltpu.SemaphoreType.DMA((4,)),
    pltpu.SemaphoreType.DMA((12,)),
    pltpu.SemaphoreType.DMA((12,)),
    pltpu.SemaphoreType.DMA((16,)),
    pltpu.SemaphoreType.DMA((16,)),
    pltpu.SemaphoreType.DMA((8,)),
]


class Gather:
    def __init__(self, full, out, sems):
        self.place = place = Place()
        self.full, self.out = full, out
        (
            self.own_send,
            self.relay_send,
            self.z_recv,
            self.xy_send,
            self.xy_recv,
            self.core_send,
            self.core_recv,
            self.out_sems,
        ) = sems
        self.quarter = full.shape[1] // 4
        self.half = self.quarter // 2
        z = place.z
        self.origins = (z + 1 - 2 * (z % 2), 2 - place.high, 3 * (1 - place.high))
        self.relays = (3 - z, 3 * (z - 1), 3 * (z - 1))

    def region(self, which, start, size):
        return self.full.at[which, pl.ds(pl.multiple_of(start, 16), size)]

    def pieces(self, which):
        place, quarter, half = self.place, self.quarter, self.half
        return (
            self.region(which, place.quarter * quarter, quarter),
            self.region(which, place.by_x * quarter, quarter),
            self.region(which, place.by_y * quarter, quarter),
            self.region(which, place.across * quarter, half),
            self.region(which, place.across * quarter + half, half),
        )

    def mine(self):
        return self.region(self.place.shard, self.place.quarter * self.quarter, self.quarter)

    def own_copy(self, side):
        place = self.place
        mine = self.mine()
        device = place.at_z(place.z - 1 + 2 * side)
        return transfer(mine, mine, self.own_send.at[side], self.z_recv.at[place.z], device)

    def core_copy(self, index, ref):
        return transfer(ref, ref, self.core_send.at[index], self.core_recv.at[index], self.place.sibling)

    def xy_copy(self, index, ref, device):
        return transfer(ref, ref, self.xy_send.at[index], self.xy_recv.at[index], device)

    def store(self, index, which):
        return pltpu.make_async_copy(self.full.at[which], self.out.at[which], self.out_sems.at[index])

    def mirrored(self, step):
        return 2 * self.origins[step] + 1 - self.place.core

    def held(self, step):
        return 2 * self.origins[step] + self.place.core

    def start(self):
        place = self.place
        greet(place)

        @pl.when(place.z > 0)
        def _():
            self.own_copy(0).start()

        @pl.when(place.z < 3)
        def _():
            self.own_copy(1).start()

        self.core_copy(0, self.full.at[place.shard]).start()
        self.store(0, place.shard).start()

    def relay(self, step):
        piece = self.pieces(self.held(step))[0]
        device = self.place.at_z(self.relays[step])
        return transfer(
            piece, piece, self.relay_send.at[step], self.z_recv.at[self.origins[step]], device
        )

    def along_z(self, step):
        place = self.place
        self.relay(step).wait_recv()

        @pl.when(place.inner)
        def _():
            self.relay(step).start()

        piece = self.pieces(self.held(step))[0]
        self.xy_copy(4 * step, piece, place.next_x).start()
        self.xy_copy(4 * step + 1, piece, place.next_y).start()
        self.core_copy(1 + 5 * step, piece).start()

    def along_xy(self, step):
        place, half = self.place, self.half
        _, by_x, by_y, _, _ = self.pieces(self.held(step))
        self.xy_copy(4 * step, by_x, place.next_x).wait_recv()
        self.xy_copy(4 * step + 2, by_x.at[pl.ds(0, half)], place.next_y).start()
        self.core_copy(2 + 5 * step, by_x).start()
        self.xy_copy(4 * step + 1, by_y, place.next_y).wait_recv()
        self.xy_copy(4 * step + 3, by_y.at[pl.ds(half, half)], place.next_x).start()
        self.core_copy(3 + 5 * step, by_y).start()

    def across(self, step):
        place = self.place
        _, _, _, first, last = self.pieces(self.held(step))
        self.xy_copy(4 * step + 2, first, place.next_y).wait_recv()
        self.core_copy(4 + 5 * step, first).start()
        self.xy_copy(4 * step + 3, last, place.next_x).wait_recv()
        self.core_copy(5 + 5 * step, last).start()
        self.store(2 + 2 * step, self.held(step)).start()

    def core_own(self):
        which = 2 * self.place.z + 1 - self.place.core
        self.core_copy(0, self.full.at[which]).wait_recv()
        self.store(1, which).start()

    def core(self, step):
        which = self.mirrored(step)
        for index, ref in enumerate(self.pieces(which)):
            self.core_copy(1 + 5 * step + index, ref).wait_recv()
        self.store(3 + 2 * step, which).start()

    def finish(self):
        place = self.place

        @pl.when(place.z > 0)
        def _():
            self.own_copy(0).wait_send()

        @pl.when(place.z < 3)
        def _():
            self.own_copy(1).wait_send()

        self.core_copy(0, self.full.at[place.shard]).wait_send()
        self.store(0, place.shard).wait()
        self.store(1, 2 * place.z + 1 - place.core).wait()
        for step in range(3):

            @pl.when(place.inner)
            def _():
                self.relay(step).wait_send()

            pieces = self.pieces(self.held(step))
            self.xy_copy(4 * step, pieces[0], place.next_x).wait_send()
            self.xy_copy(4 * step + 1, pieces[0], place.next_y).wait_send()
            self.xy_copy(4 * step + 2, pieces[3], place.next_y).wait_send()
            self.xy_copy(4 * step + 3, pieces[4], place.next_x).wait_send()
            for index, ref in enumerate(pieces):
                self.core_copy(1 + 5 * step + index, ref).wait_send()
            self.store(2 + 2 * step, self.held(step)).wait()
            self.store(3 + 2 * step, self.mirrored(step)).wait()


def gather_kernel(master_ref, out_ref, full, *sems):
    gather = Gather(full, out_ref, sems)
    full[gather.place.shard] = master_ref[...].astype(BF16)
    gather.start()
    gather.along_z(0)
    gather.along_z(1)
    gather.along_xy(0)
    gather.along_z(2)
    gather.along_xy(1)
    gather.across(0)
    gather.core_own()
    gather.along_xy(2)
    gather.across(1)
    gather.core(0)
    gather.across(2)
    gather.core(1)
    gather.core(2)
    gather.finish()


def gather_shards(master):
    rows = master.shape[0] * BLK
    shards = lax.axis_size("fsdp")
    return pl.pallas_call(
        gather_kernel,
        in_specs=[pl.BlockSpec(memory_space=pltpu.VMEM)],
        out_specs=pl.BlockSpec(memory_space=pl.ANY),
        out_shape=jax.ShapeDtypeStruct((shards, rows, BLK), BF16),
        scratch_shapes=[pltpu.VMEM((shards, rows, BLK), BF16)] + GATHER_SEMAPHORES,
        compiler_params=pltpu.CompilerParams(
            collective_id=0, has_side_effects=True, vmem_limit_bytes=56 * MIB
        ),
        cost_estimate=pl.CostEstimate(flops=0, bytes_accessed=200 * MIB, transcendentals=0),
        name="gather",
    )(master.reshape(rows, BLK)).reshape(-1, BLK, BLK)


def add_rows(target, former, latter, rows, step):
    @pl.loop(0, rows // step)
    def _(index):
        part = pl.ds(pl.multiple_of(index * step, 16), step)
        target[part] = (former[part].astype(F32) + latter[part].astype(F32)).astype(BF16)


def reduce_scratch(rows):
    quarter = rows // 4
    half = quarter // 2
    return [
        pltpu.VMEM((4, rows, BLK), BF16),
        pltpu.VMEM((4, rows, BLK), BF16),
        pltpu.VMEM((4, 2, half, BLK), BF16),
        pltpu.VMEM((4, 2, half, BLK), BF16),
        pltpu.VMEM((4, half, BLK), BF16),
        pltpu.VMEM((4, half, BLK), BF16),
        pltpu.VMEM((5, quarter, BLK), BF16),
        pltpu.VMEM((rows, BLK), BF16),
        pltpu.SemaphoreType.DMA((4,)),
        pltpu.SemaphoreType.DMA((4,)),
        pltpu.SemaphoreType.DMA((4,)),
        pltpu.SemaphoreType.DMA((24,)),
        pltpu.SemaphoreType.DMA((24,)),
        pltpu.SemaphoreType.DMA((3,)),
        pltpu.SemaphoreType.DMA((5,)),
        pltpu.SemaphoreType.DMA((4,)),
        pltpu.SemaphoreType.DMA((4,)),
    ]


class Reduce:
    def __init__(self, terms, base, out, scratch):
        self.place = place = Place()
        self.terms, self.base, self.out = terms, base, out
        (
            self.mine,
            self.sib,
            self.from_x,
            self.from_y,
            self.late_y,
            self.late_x,
            self.from_z,
            self.result,
            self.load_sems,
            self.core_send,
            self.core_recv,
            self.xy_send,
            self.xy_recv,
            self.z_send,
            self.z_recv,
            self.last_send,
            self.last_recv,
        ) = scratch
        self.quarter = out.shape[0] // 4
        self.half = self.quarter // 2
        z, high = place.z, place.high
        low = 1 - high
        self.order = (3 * low, low * (2 - 2 * z) + high * (7 - 2 * z), 1 + z % 2, z)
        self.onward = (z + 1 - 2 * high, z + 1 - 2 * (z % 2), z + 1 - 2 * high)
        self.closing = (0, (z % 2) * low, high)
        self.far = place.at_z(z + 2 - 4 * high)
        self.near = place.at_z(z + 1 - 2 * (z % 2))

    def shard_terms(self, shard):
        rows = self.out.shape[0]
        return self.terms.at[pl.ds(pl.multiple_of(self.base + shard * rows, 16), rows)]

    def load(self, step):
        source = self.shard_terms(2 * self.order[step] + self.place.core)
        return pltpu.make_async_copy(source, self.mine.at[step], self.load_sems.at[step])

    def core_copy(self, step):
        return transfer(
            self.shard_terms(2 * self.order[step] + 1 - self.place.core),
            self.sib.at[step],
            self.core_send.at[step],
            self.core_recv.at[step],
            self.place.sibling,
        )

    def part(self, step, which, side):
        start = pl.multiple_of(which * self.quarter + side * self.half, 16)
        return self.mine.at[step, pl.ds(start, self.half)]

    def xy_copy(self, step, index):
        place = self.place
        source, target, device = (
            (self.part(step, place.by_x, 0), self.from_x.at[step, 0], place.next_x),
            (self.part(step, place.across, 0), self.from_x.at[step, 1], place.next_x),
            (self.part(step, place.by_y, 1), self.from_y.at[step, 0], place.next_y),
            (self.part(step, place.across, 1), self.from_y.at[step, 1], place.next_y),
            (self.part(step, place.by_y, 0), self.late_y.at[step], place.next_y),
            (self.part(step, place.by_x, 1), self.late_x.at[step], place.next_x),
        )[index]
        place = 6 * step + index
        return transfer(source, target, self.xy_send.at[place], self.xy_recv.at[place], device)

    def start(self):
        greet(self.place, (self.far,))
        for step in range(2):
            self.core_copy(step).start()
        for step in range(4):
            self.load(step).start()

    def core(self, step):
        place, quarter = self.place, self.quarter
        self.load(step).wait()
        self.core_copy(step).wait_recv()
        if step < 2:
            self.core_copy(step + 2).start()

        def add(which):
            block = pl.ds(pl.multiple_of(which * quarter, 16), quarter)
            mine = self.mine.at[step, block]
            add_rows(mine, mine, self.sib.at[step, block], quarter, self.half)

        add(place.by_x)
        add(place.across)
        self.xy_copy(step, 0).start()
        self.xy_copy(step, 1).start()
        add(place.by_y)
        self.xy_copy(step, 2).start()
        self.xy_copy(step, 3).start()
        add(place.quarter)

    def take(self, step, which, side, index, source):
        self.xy_copy(step, index).wait_recv()
        target = self.part(step, which, side)
        add_rows(target, target, source, self.half, self.half)

    def first(self, step):
        place = self.place
        self.take(step, place.by_y, 0, 1, self.from_x.at[step, 1])
        self.xy_copy(step, 4).start()
        self.take(step, place.by_x, 1, 3, self.from_y.at[step, 1])
        self.xy_copy(step, 5).start()
        self.take(step, place.quarter, 0, 0, self.from_x.at[step, 0])
        self.take(step, place.quarter, 1, 2, self.from_y.at[step, 0])

    def own_block(self, step):
        return self.mine.at[step, pl.ds(pl.multiple_of(self.place.quarter * self.quarter, 16), self.quarter)]

    def z_copy(self, step):
        goal = self.order[step]
        slot = goal + self.closing[step] * (4 - goal)
        return transfer(
            self.own_block(step),
            self.from_z.at[slot],
            self.z_send.at[step],
            self.z_recv.at[slot],
            self.place.at_z(self.onward[step]),
        )

    def take_z(self, step, slot):
        source = self.from_z.at[slot]
        transfer(source, source, self.z_send.at[0], self.z_recv.at[slot], self.near).wait_recv()
        block = self.own_block(step)
        add_rows(block, block, source, self.quarter, self.half)

    def second(self, step):
        place = self.place
        self.take(step, place.quarter, 0, 4, self.late_y.at[step])
        self.take(step, place.quarter, 1, 5, self.late_x.at[step])
        if step < 3:

            @pl.when(place.inner)
            def _():
                self.take_z(step, self.order[step])

            self.z_copy(step).start()
        else:

            @pl.when(place.z > 0)
            def _():
                self.take_z(step, place.z)

            @pl.when(place.z < 3)
            def _():
                self.take_z(step, 4)

    def final(self, which, side=None):
        start = pl.multiple_of(which * self.quarter + (0 if side is None else side * self.half), 16)
        return self.result.at[pl.ds(start, self.quarter if side is None else self.half)]

    def last_copy(self, index, ref):
        device = (self.place.next_x, self.place.next_y, self.place.next_y, self.place.next_x)[index]
        return transfer(ref, ref, self.last_send.at[index], self.last_recv.at[index], device)

    def share(self):
        own = self.final(self.place.quarter)
        own[...] = self.own_block(3)[...]
        self.last_copy(0, own).start()
        self.last_copy(1, own).start()

    def share_on(self):
        place = self.place
        self.last_copy(0, self.final(place.by_x)).wait_recv()
        self.last_copy(2, self.final(place.by_x, 0)).start()
        self.last_copy(1, self.final(place.by_y)).wait_recv()
        self.last_copy(3, self.final(place.by_y, 1)).start()

    def finish(self):
        place = self.place
        self.last_copy(2, self.final(place.across, 0)).wait_recv()
        self.last_copy(3, self.final(place.across, 1)).wait_recv()
        self.out[...] = self.result[...]
        for step in range(4):
            self.core_copy(step).wait_send()
            for index in range(6):
                self.xy_copy(step, index).wait_send()
            if step < 3:
                self.z_copy(step).wait_send()
        own = self.final(place.quarter)
        self.last_copy(0, own).wait_send()
        self.last_copy(1, own).wait_send()
        self.last_copy(2, self.final(place.by_x, 0)).wait_send()
        self.last_copy(3, self.final(place.by_y, 1)).wait_send()


def reduce_kernel(
    terms, small_ref, out_ref, small_out, small_in, small_sum, small_send, small_recv, *scratch, base
):
    reduce = Reduce(terms, base, out_ref, scratch)
    place = reduce.place
    partners = (place.sibling, place.next_x, place.next_y, reduce.near, reduce.far)

    def small_copy(level):
        return transfer(
            small_sum.at[level],
            small_in.at[level],
            small_send.at[level],
            small_recv.at[level],
            partners[level],
        )

    def small_step(level):
        small_copy(level - 1).wait_recv()
        small_sum[level] = small_sum[level - 1] + small_in[level - 1]
        if level < 5:
            small_copy(level).start()

    small_sum[0] = small_ref[...]
    reduce.start()
    small_copy(0).start()
    reduce.core(0)
    small_step(1)
    reduce.core(1)
    reduce.first(0)
    small_step(2)
    reduce.core(2)
    reduce.first(1)
    reduce.second(0)
    small_step(3)
    reduce.core(3)
    reduce.first(2)
    reduce.second(1)
    small_step(4)
    reduce.first(3)
    reduce.second(2)
    small_step(5)
    small_out[...] = small_sum[5]
    reduce.second(3)
    reduce.share()
    reduce.share_on()
    reduce.finish()
    for level in range(5):
        small_copy(level).wait_send()


def reduce_late(terms, base, rows, small):
    vmem = pl.BlockSpec(memory_space=pltpu.VMEM)
    return pl.pallas_call(
        partial(reduce_kernel, base=base),
        in_specs=[pl.BlockSpec(memory_space=pl.ANY), vmem],
        out_specs=[vmem, vmem],
        out_shape=[
            jax.ShapeDtypeStruct((rows, BLK), BF16),
            jax.ShapeDtypeStruct((SMALL_ROWS, BLK), F32),
        ],
        scratch_shapes=[
            pltpu.VMEM((5, SMALL_ROWS, BLK), F32),
            pltpu.VMEM((6, SMALL_ROWS, BLK), F32),
            pltpu.SemaphoreType.DMA((5,)),
            pltpu.SemaphoreType.DMA((5,)),
        ]
        + reduce_scratch(rows),
        compiler_params=pltpu.CompilerParams(
            collective_id=3, has_side_effects=True, vmem_limit_bytes=48 * MIB
        ),
        cost_estimate=pl.CostEstimate(flops=0, bytes_accessed=200 * MIB, transcendentals=0),
        name="reduce",
    )(terms, small)


def count_where(condition, axis):
    return jnp.sum(condition.astype(jnp.int32), axis=axis)


def slot_codes(slots, qkv_slots, slot_count, shards):
    early = slot_count - LATE
    shard = slots // slot_count
    begin = shard * slot_count
    inside = (qkv_slots[None, :] >= begin[:, None]) & (qkv_slots[None, :] < (begin + slot_count)[:, None])
    own = count_where(qkv_slots[None, :] == slots[:, None], 1)
    before = count_where(inside & (qkv_slots[None, :] < slots[:, None]), 1)
    number = count_where(inside, 1)
    position = jnp.where(own > 0, slot_count - number + before, slots - begin - before)
    return jnp.where(
        position < early,
        shard * early + position,
        shards * early + shard * LATE + position - early,
    ), position


def empty_slots(block_slot, all_slots):
    places = jnp.arange(all_slots, dtype=jnp.int32)
    empty_before = places + 1 - count_where(block_slot[None, :] <= places[:, None], 1)
    empty_index = jnp.arange(all_slots - NBLK, dtype=jnp.int32)
    return count_where(empty_before[None, :] <= empty_index[:, None], 1)


def body(
    x_short,
    x_long,
    cot_short,
    cot_long,
    logit_cot_short,
    logit_cot_long,
    len_short,
    len_long,
    block_slot,
    master,
    left_stat,
    right_stat,
    left_root,
    right_root,
    small_params,
    small_first,
    small_second,
    own_transfers,
):
    slot_count = master.shape[0]
    shards = lax.axis_size("fsdp")
    all_slots = slot_count * shards
    short_seqs, width = x_short.shape[:2]
    long_seqs = x_long.shape[0]
    short_tiles = short_seqs * width // TILE
    per_tile = TILE // width
    empty = empty_slots(block_slot, all_slots)

    if own_transfers:
        early_count = slot_count - LATE
        qkv_slots = block_slot[: 3 * 36]
        code, _ = slot_codes(block_slot, qkv_slots, slot_count, shards)
        empty_code, _ = slot_codes(empty, qkv_slots, slot_count, shards)
        own = jnp.arange(slot_count, dtype=jnp.int32) + slot_count * lax.axis_index("fsdp")
        _, position = slot_codes(own, qkv_slots, slot_count, shards)
        shard_index = jnp.arange(shards, dtype=jnp.int32)
        most = jnp.max(count_where(qkv_slots[None, :] // slot_count == shard_index[:, None], 1))
        fits = most <= LATE
        gathered = gather_shards(master)
    else:
        gathered = lax.all_gather(master.astype(BF16), "fsdp", axis=0, tiled=True)
    w_qkv = assemble(block_slot, gathered)
    pieces = unpack(small_params)
    params = jnp.pad(small_params, (0, SMALL_ROWS * BLK - small_params.shape[0])).reshape(SMALL_ROWS, BLK)
    w_class = jnp.pad(pieces[-2].reshape(SD, NCLS), ((0, 0), (0, SD - NCLS)))
    b_class = jnp.pad(pieces[-1].reshape(1, NCLS), ((0, 0), (0, SD - NCLS)))

    x = jnp.concatenate([x_short.reshape(-1, D), x_long.reshape(-1, D)], axis=0)
    *qkv, context, probs_short, probs_long = attention(
        len_short,
        len_long,
        x,
        pieces[0].reshape(1, D),
        pieces[1].reshape(1, D),
        w_qkv,
        short_tiles,
        width,
    )

    logit_cot = jnp.concatenate(
        [
            jnp.pad(
                logit_cot_short.reshape(short_tiles, per_tile, NCLS),
                ((0, 0), (0, 8 - per_tile), (0, SD - NCLS)),
            ),
            jnp.pad(logit_cot_long.reshape(long_seqs, 1, NCLS), ((0, 0), (0, 7), (0, SD - NCLS))),
        ],
        axis=0,
    )
    (
        enc_short,
        enc_long,
        logits,
        first,
        active,
        d_up,
        d_down,
        d_branch,
        d_context,
        d_resid,
        g_student,
        g_hidden,
        g_small,
    ) = feed(
        len_short,
        len_long,
        block_slot,
        x,
        context,
        cot_short.reshape(-1, D),
        cot_long.reshape(-1, D),
        logit_cot,
        (params, w_class, b_class),
        gathered,
        short_tiles,
        width,
    )
    g_down = left_product(active, d_down).astype(BF16)
    g_up = left_product(first, d_up).astype(BF16)
    g_out = left_product(context, d_branch).astype(BF16)
    others = (g_out, g_up, g_down, g_student.astype(BF16), g_hidden.astype(BF16))
    if own_transfers:
        terms = spread(code, empty_code, others, OTHER_PLACES, all_slots)
        *back, early_reduced = attention_back(
            qkv,
            probs_short,
            probs_long,
            d_context,
            d_resid,
            w_qkv,
            short_tiles,
            terms.reshape(-1, BLK),
            early_count * BLK,
        )
    else:
        back = attention_back(qkv, probs_short, probs_long, d_context, d_resid, w_qkv, short_tiles)
    d_query, d_key, d_value, in_short, in_long, g_b_query, g_b_value = back
    qkv_grads = tuple(left_product(x, d_rows).astype(BF16) for d_rows in (d_query, d_key, d_value))

    def reduce_all():
        slot_terms = spread(block_slot, empty, qkv_grads + others, QKV_PLACES + OTHER_PLACES, all_slots)
        return lax.psum(lax.psum_scatter(slot_terms, "fsdp", scatter_dimension=0, tiled=True), "dp")

    if own_transfers:
        terms, small_terms = spread_late(code, qkv_grads, g_small, g_b_query, g_b_value, terms)
        late_reduced, small_total = reduce_late(
            terms.reshape(-1, BLK), shards * early_count * BLK, LATE * BLK, small_terms
        )

        def join():
            blocks = jnp.concatenate([early_reduced, late_reduced], axis=0).reshape(slot_count, BLK, BLK)
            return blocks.at[position].get(mode="promise_in_bounds")

        slot_grad = lax.cond(fits, join, reduce_all)
    else:
        slot_grad = reduce_all()
        small_terms = jnp.concatenate(
            [g_b_query.reshape(-1, BLK), g_b_value.reshape(-1, BLK), g_small[2 * D // BLK :]], axis=0
        )
        small_total = lax.psum(small_terms, ("dp", "fsdp"))
    slot_grad = slot_grad.astype(F32)
    small_grad = jnp.concatenate(
        [
            small_total[:CLASS_ROW].reshape(-1),
            small_total[CLASS_ROW : CLASS_ROW + NCLS].T.reshape(-1),
            small_total[LAST_ROW, :NCLS],
        ]
    )
    outer_left = jnp.einsum("sij,skj->sik", slot_grad, slot_grad, precision=HIGHEST_PRECISION)
    outer_right = jnp.einsum("sji,sjk->sik", slot_grad, slot_grad, precision=HIGHEST_PRECISION)
    new_left = STAT_DECAY * left_stat + (1.0 - STAT_DECAY) * outer_left
    new_right = STAT_DECAY * right_stat + (1.0 - STAT_DECAY) * outer_right
    left_applied = jnp.einsum("sij,sjk->sik", left_root, slot_grad, precision=HIGHEST_PRECISION)
    conditioned = jnp.einsum("sij,sjk->sik", left_applied, right_root, precision=HIGHEST_PRECISION)
    new_master = master - MATRIX_RATE * conditioned
    new_first = BETA_ONE * small_first + (1.0 - BETA_ONE) * small_grad
    new_second = BETA_TWO * small_second + (1.0 - BETA_TWO) * small_grad * small_grad
    first_hat = new_first / (1.0 - BETA_ONE**STEP)
    second_hat = new_second / (1.0 - BETA_TWO**STEP)
    new_small = small_params - ADAM_RATE * first_hat / (jnp.sqrt(second_hat) + ADAM_EPSILON)
    return (
        enc_short.reshape(x_short.shape),
        logits[:short_tiles, :per_tile, :NCLS].reshape(short_seqs, NCLS),
        enc_long.reshape(x_long.shape),
        logits[short_tiles:, 0, :NCLS],
        in_short.reshape(x_short.shape),
        in_long.reshape(x_long.shape),
        slot_grad,
        new_left,
        new_right,
        new_master,
        new_first,
        new_second,
        new_small,
    )


def solution(mesh):
    both = ("dp", "fsdp")
    placed = (
        P(both, None, None),
        P(both, None, None),
        P(both, None, None),
        P(both, None, None),
        P(both, None),
        P(both, None),
        P(both),
        P(both),
        P(),
        P("fsdp", None, None),
        P("fsdp", None, None),
        P("fsdp", None, None),
        P("fsdp", None, None),
        P("fsdp", None, None),
        P(),
        P(),
        P(),
    )
    return jax.shard_map(
        partial(body, own_transfers=(mesh.shape["dp"], mesh.shape["fsdp"]) == (4, 8)),
        mesh=mesh,
        in_specs=placed,
        out_specs=(
            P(both, None, None),
            P(both, None),
            P(both, None, None),
            P(both, None),
            P(both, None, None),
            P(both, None, None),
            P("fsdp", None, None),
            P("fsdp", None, None),
            P("fsdp", None, None),
            P("fsdp", None, None),
            P(),
            P(),
            P(),
        ),
        check_vma=False,
    )
```

```python
from functools import partial

import jax
import jax.numpy as jnp
from jax import lax
from jax.experimental import pallas as pl
from jax.experimental.pallas import tpu as pltpu
from jax.sharding import PartitionSpec as P

D = 768
HEADS = 12
FF = 3072
SD = 128
PH = 2
NCLS = 14
BLK = 128
STEP = 10
NBLK = 439
TILE = 512
PAIRS = 3
GROUPS = 2
CHUNK = 768
LATE = 24

NORM_EPSILON = 1e-12
BETA_ONE = 0.9
BETA_TWO = 0.999
ADAM_EPSILON = 1e-08
ADAM_RATE = 0.1
MATRIX_RATE = 0.2
STAT_DECAY = 0.5
MASKED_SCORE = -1e30
HIGHEST_PRECISION = lax.Precision.HIGHEST
MIB = 1024 * 1024
F32 = jnp.float32
BF16 = jnp.bfloat16

def product(former, latter, precision=None):
    return jnp.dot(former, latter, preferred_element_type=F32, precision=precision)


def left_product(former, latter, precision=None):
    return lax.dot_general(
        former, latter, (((0,), (0,)), ((), ())), preferred_element_type=F32, precision=precision
    )


def right_product(former, latter, precision=None):
    return lax.dot_general(
        former, latter, (((1,), (1,)), ((), ())), preferred_element_type=F32, precision=precision
    )


def unpack(small_values):
    widths = (D, D, D, D, D, FF, D, D, D, SD, SD, SD, SD * NCLS, NCLS)
    pieces = []
    offset = 0
    for column_count in widths:
        pieces.append(small_values[offset : offset + column_count])
        offset += column_count
    return pieces


def each_block(first, row_count, col_count, action):
    def one_row(index, carry):
        row = pl.multiple_of(index * BLK, BLK)
        for col in range(col_count):
            action(first + index * col_count + col, row, col * BLK)
        return carry

    lax.fori_loop(0, row_count, one_row, 0)


def load_blocks(slot_ref, blocks, target, sem, first, row_count, col_count, col_start=0):
    def move(block, row, col):
        pltpu.make_async_copy(
            blocks.at[slot_ref[block]],
            target.at[pl.ds(row, BLK), pl.ds(col + col_start * BLK, BLK)],
            sem,
        ).start()

    each_block(first, row_count, col_count, move)


def wait_whole(target, sem):
    pltpu.make_async_copy(target, target, sem).wait()


def assemble_kernel(slot_ref, blocks, out, sem):
    for which in range(3):
        load_blocks(slot_ref, blocks, out, sem, 36 * which, 6, 6, 6 * which)
    wait_whole(out, sem)


def assemble(block_slot, blocks):
    return pl.pallas_call(
        assemble_kernel,
        grid_spec=pltpu.PrefetchScalarGridSpec(
            num_scalar_prefetch=1,
            grid=(1,),
            in_specs=[pl.BlockSpec(memory_space=pltpu.HBM)],
            out_specs=pl.BlockSpec(memory_space=pltpu.VMEM),
            scratch_shapes=[pltpu.SemaphoreType.DMA],
        ),
        out_shape=jax.ShapeDtypeStruct((D, 3 * D), BF16),
        compiler_params=pltpu.CompilerParams(vmem_limit_bytes=60 * MIB),
        name="assemble",
    )(block_slot, blocks)


QKV_PLACES = ((0, 6, 6), (36, 6, 6), (72, 6, 6))
OTHER_PLACES = ((108, 6, 6), (144, 6, 24), (288, 24, 6), (432, 6, 1), (438, 1, 1))


def spread_kernel(code_ref, empty_ref, *refs, places):
    grads = refs[: len(places)]
    zero, out, sems = refs[len(places) :]
    for which, (grad, place) in enumerate(zip(grads, places)):

        def move(block, row, col, which=which, grad=grad):
            pltpu.make_async_copy(
                grad.at[pl.ds(row, BLK), pl.ds(col, BLK)], out.at[code_ref[block]], sems.at[which]
            ).start()

        each_block(*place, move)
    for index in range(empty_ref.shape[0]):
        pltpu.make_async_copy(zero, out.at[empty_ref[index]], sems.at[len(places) + index]).start()
    for which, grad in enumerate(grads):
        wait_whole(grad, sems.at[which])
    for index in range(empty_ref.shape[0]):
        wait_whole(zero, sems.at[len(places) + index])


def spread(code, empty, grads, places, slot_count):
    vmem = pl.BlockSpec(memory_space=pltpu.VMEM)
    return pl.pallas_call(
        partial(spread_kernel, places=places),
        grid_spec=pltpu.PrefetchScalarGridSpec(
            num_scalar_prefetch=2,
            grid=(1,),
            in_specs=[vmem] * (len(grads) + 1),
            out_specs=pl.BlockSpec(memory_space=pltpu.HBM),
            scratch_shapes=[pltpu.SemaphoreType.DMA((len(grads) + empty.shape[0],))],
        ),
        out_shape=jax.ShapeDtypeStruct((slot_count, BLK, BLK), BF16),
        compiler_params=pltpu.CompilerParams(vmem_limit_bytes=24 * MIB),
        name="spread",
    )(code, empty, *grads, jnp.zeros((BLK, BLK), BF16))


def spread_late_kernel(code_ref, *refs):
    grads = refs[:3]
    small_ref, query_ref, value_ref, _, out, small_out, sems = refs[3:]
    for which, (grad, place) in enumerate(zip(grads, QKV_PLACES)):

        def move(block, row, col, which=which, grad=grad):
            pltpu.make_async_copy(
                grad.at[pl.ds(row, BLK), pl.ds(col, BLK)], out.at[code_ref[block]], sems.at[which]
            ).start()

        each_block(*place, move)
    join_small(small_ref, query_ref, value_ref, small_out)
    for which, grad in enumerate(grads):
        wait_whole(grad, sems.at[which])


def join_small(small_ref, query_ref, value_ref, small_out):
    small_out[...] = small_ref[...]
    for start, ref in ((0, query_ref), (D // BLK, value_ref)):
        for index in range(D // BLK):
            small_out[start + index : start + index + 1, :] = ref[:, index * BLK : (index + 1) * BLK]


def spread_late(code, grads, small, g_query, g_value, terms):
    vmem = pl.BlockSpec(memory_space=pltpu.VMEM)
    anywhere = pl.BlockSpec(memory_space=pltpu.HBM)
    return pl.pallas_call(
        spread_late_kernel,
        grid_spec=pltpu.PrefetchScalarGridSpec(
            num_scalar_prefetch=1,
            grid=(1,),
            in_specs=[vmem] * 6 + [anywhere],
            out_specs=[anywhere, vmem],
            scratch_shapes=[pltpu.SemaphoreType.DMA((3,))],
        ),
        out_shape=[
            jax.ShapeDtypeStruct(terms.shape, BF16),
            jax.ShapeDtypeStruct(small.shape, F32),
        ],
        input_output_aliases={7: 0},
        compiler_params=pltpu.CompilerParams(vmem_limit_bytes=24 * MIB),
        name="spread_late",
    )(code, *grads, small, g_query, g_value, terms)


def half_masks():
    lane = lax.broadcasted_iota(jnp.int32, (1, BLK), 1)
    low = (lane < BLK // 2).astype(BF16)
    return low, (1.0 - low.astype(F32)).astype(BF16)


def stack_heads(values, low, high):
    return jnp.concatenate([values * low, values * high], axis=0)


def pick_heads(values):
    rows = values.shape[0] // 2
    lane = lax.broadcasted_iota(jnp.int32, (rows, BLK), 1)
    return jnp.where(lane < BLK // 2, values[:rows], values[rows:])


def pipelined(count, before, middle, after):
    started = before(0)
    done = None
    for index in range(count):
        current = started
        if index + 1 < count:
            started = before(index + 1)
        if done is not None:
            after(index - 1, done)
        done = middle(index, current)
    after(count - 1, done)


def softmax(scores, length):
    visible = lax.broadcasted_iota(jnp.int32, scores.shape, 1) < length
    scores = jnp.where(visible, scores, MASKED_SCORE)
    powers = jnp.exp(scores - jnp.max(scores, axis=-1, keepdims=True))
    total = jnp.sum(powers, axis=-1, keepdims=True)
    return (powers * (1.0 / total)).astype(BF16)


def attention_kernel(
    len_short,
    len_long,
    x_ref,
    b_query,
    b_value,
    w_ref,
    q_ref,
    k_ref,
    v_ref,
    context_ref,
    short_ref,
    long_ref,
    *,
    short_tiles,
):
    tile = pl.program_id(0)
    group = pl.program_id(1)
    low, high = half_masks()
    width = short_ref.shape[-1]
    per_tile = TILE // width

    wide = PAIRS * BLK
    start = pl.multiple_of(group * wide, wide)
    rows_in = x_ref[...]
    queries = product(rows_in, w_ref[:, pl.ds(start, wide)]) + b_query[:, pl.ds(start, wide)]
    q_ref[...] = (queries * 0.125).astype(BF16)
    k_ref[...] = product(rows_in, w_ref[:, pl.ds(D + start, wide)]).astype(BF16)
    values = product(rows_in, w_ref[:, pl.ds(2 * D + start, wide)]) + b_value[:, pl.ds(start, wide)]
    v_ref[...] = values.astype(BF16)

    def attend(units, kept_ref):
        def scores(index):
            rows, keys, cols, _, _ = units[index]
            return right_product(stack_heads(q_ref[rows, cols], low, high), k_ref[keys, cols])

        def weigh(index, values):
            _, _, _, length, place = units[index]
            probs = softmax(values, length)
            kept_ref[place] = probs
            return probs

        def mix(index, probs):
            rows, keys, cols, _, _ = units[index]
            context_ref[rows, cols] = pick_heads(product(probs, v_ref[keys, cols])).astype(BF16)

        pipelined(len(units), scores, weigh, mix)

    @pl.when(tile < short_tiles)
    def _():
        units = []
        for seq in range(per_tile):
            rows = slice(seq * width, (seq + 1) * width)
            length = len_short[tile * per_tile + seq]
            for pair in range(PAIRS):
                cols = slice(pair * BLK, (pair + 1) * BLK)
                units.append((rows, rows, cols, length, (0, pair, seq)))
        attend(units, short_ref)

    @pl.when(tile >= short_tiles)
    def _():
        length = len_long[tile - short_tiles]
        half = TILE // 2
        units = []
        for pair in range(PAIRS):
            cols = slice(pair * BLK, (pair + 1) * BLK)
            for part in range(2):
                rows = slice(part * half, (part + 1) * half)
                units.append((rows, slice(0, TILE), cols, length, (0, pair, part)))
        attend(units, long_ref)


def run_events(step, events):
    for index, actions in enumerate(events):

        @pl.when(step == index)
        def _(actions=actions):
            for action in actions:
                action()


def probs_shapes(short_tiles, long_tiles, width):
    per_tile = TILE // width
    return (
        (short_tiles, 2 * PAIRS, per_tile, 2 * width, width),
        (long_tiles, 2 * PAIRS, 2, TILE, TILE),
    )


def short_index(tile, short_tiles):
    return jnp.minimum(tile, short_tiles - 1)


def long_index(tile, short_tiles):
    return jnp.maximum(tile - short_tiles, 0)


def probs_maps(short_tiles):
    def short_map(tile, group):
        last = jnp.minimum(tile // short_tiles, 1)
        return (short_index(tile, short_tiles), group + last * (GROUPS - 1 - group), 0, 0, 0)

    def long_map(tile, group):
        begun = jnp.minimum(tile // short_tiles, 1)
        return (long_index(tile, short_tiles), begun * group, 0, 0, 0)

    return short_map, long_map


def attention(len_short, len_long, x, b_query, b_value, w_qkv, short_tiles, width):
    tiles = x.shape[0] // TILE
    wide = PAIRS * BLK
    short_shape, long_shape = probs_shapes(short_tiles, tiles - short_tiles, width)
    short_map, long_map = probs_maps(short_tiles)
    flops = 4 * D * TILE * TILE * tiles + 6 * D * D * TILE * tiles
    rows = pl.BlockSpec((TILE, wide), lambda tile, group: (tile, group))
    scalars = pl.BlockSpec(memory_space=pltpu.SMEM)

    def whole(shape):
        return pl.BlockSpec(shape, lambda tile, group: (0,) * len(shape), pipeline_mode=pl.Buffered(1))

    in_specs = [
        scalars,
        scalars,
        pl.BlockSpec((TILE, D), lambda tile, group: (tile, 0)),
        whole((1, D)),
        whole((1, D)),
        whole((D, 3 * D)),
    ]
    out_specs = [
        rows,
        rows,
        rows,
        rows,
        pl.BlockSpec((1, PAIRS) + short_shape[2:], short_map),
        pl.BlockSpec((1, PAIRS) + long_shape[2:], long_map),
    ]
    out_shape = [jax.ShapeDtypeStruct((tiles * TILE, D), BF16)] * 4 + [
        jax.ShapeDtypeStruct(short_shape, BF16),
        jax.ShapeDtypeStruct(long_shape, BF16),
    ]
    arguments = [len_short, len_long, x, b_query, b_value, w_qkv]
    return pl.pallas_call(
        partial(attention_kernel, short_tiles=short_tiles),
        grid=(tiles, GROUPS),
        in_specs=in_specs,
        out_specs=out_specs,
        out_shape=out_shape,
        compiler_params=pltpu.CompilerParams(vmem_limit_bytes=60 * MIB),
        cost_estimate=pl.CostEstimate(
            flops=flops, bytes_accessed=35 * MIB, transcendentals=HEADS * TILE * TILE * tiles // 2
        ),
        name="attention",
    )(*arguments)


def attention_back_kernel(*refs, short_tiles, transfers):
    q_ref, k_ref, v_ref, short_ref, long_ref, dc_ref = refs[:6]
    refs = refs[6:]
    if transfers:
        terms_ref, refs = refs[0], refs[1:]
    dq_ref, dk_ref, dv_ref, bq_ref, bv_ref = refs[:5]
    tile = pl.program_id(0)
    group = pl.program_id(1)
    low, high = half_masks()
    width = short_ref.shape[-1]
    per_tile = TILE // width
    if transfers:
        reduce = Reduce(terms_ref, 0, refs[5], refs[6:])
        run_events(
            tile * GROUPS + group,
            (
                (reduce.start,),
                (partial(reduce.core, 0),),
                (partial(reduce.core, 1), partial(reduce.first, 0)),
                (partial(reduce.core, 2), partial(reduce.first, 1), partial(reduce.second, 0)),
                (partial(reduce.core, 3), partial(reduce.first, 2), partial(reduce.second, 1)),
                (partial(reduce.first, 3), partial(reduce.second, 2)),
                (partial(reduce.second, 3), reduce.share),
                (reduce.share_on,),
            ),
        )

    def go_back(units, kept_ref, parts):
        sums = {}

        def spread_in(index):
            rows, keys, cols, _ = units[index]
            return right_product(stack_heads(dc_ref[rows, cols], low, high), v_ref[keys, cols])

        def differ(index, d_probs):
            wide = kept_ref[units[index][3]].astype(F32)
            weighted = wide * d_probs
            return (weighted - wide * jnp.sum(weighted, axis=-1, keepdims=True)).astype(BF16)

        def gather_up(index, d_scores):
            rows, keys, cols, place = units[index]
            d_queries = pick_heads(product(d_scores, k_ref[keys, cols])) * 0.125
            dq_ref[rows, cols] = d_queries.astype(BF16)
            d_keys = left_product(d_scores, stack_heads(q_ref[rows, cols], low, high))
            d_values = left_product(kept_ref[place], stack_heads(dc_ref[rows, cols], low, high))
            if index % parts:
                d_keys += sums["keys"]
                d_values += sums["values"]
            if index % parts == parts - 1:
                dk_ref[keys, cols] = d_keys.astype(BF16)
                dv_ref[keys, cols] = d_values.astype(BF16)
            else:
                sums.update(keys=d_keys, values=d_values)

        pipelined(len(units), spread_in, differ, gather_up)

    @pl.when(tile < short_tiles)
    def _():
        units = []
        for seq in range(per_tile):
            rows = slice(seq * width, (seq + 1) * width)
            for pair in range(PAIRS):
                cols = slice(pair * BLK, (pair + 1) * BLK)
                units.append((rows, rows, cols, (0, pair, seq)))
        go_back(units, short_ref, 1)

    @pl.when(tile >= short_tiles)
    def _():
        half = TILE // 2
        units = []
        for pair in range(PAIRS):
            cols = slice(pair * BLK, (pair + 1) * BLK)
            for part in range(2):
                rows = slice(part * half, (part + 1) * half)
                units.append((rows, slice(0, TILE), cols, (0, pair, part)))
        go_back(units, long_ref, 2)

    wide = PAIRS * BLK
    start = pl.multiple_of(group * wide, wide)

    @pl.when((tile == 0) & (group == 0))
    def _():
        bq_ref[...] = jnp.zeros_like(bq_ref)
        bv_ref[...] = jnp.zeros_like(bv_ref)

    bq_ref[:, pl.ds(start, wide)] += jnp.sum(dq_ref[...].astype(F32), axis=0, keepdims=True)
    bv_ref[:, pl.ds(start, wide)] += jnp.sum(dv_ref[...].astype(F32), axis=0, keepdims=True)

    if transfers:

        @pl.when((tile == pl.num_programs(0) - 1) & (group == GROUPS - 1))
        def _():
            reduce.finish()


def attention_back(qkv, probs_short, probs_long, d_context, short_tiles, terms=None, count=0):
    tiles = d_context.shape[0] // TILE
    wide = PAIRS * BLK
    short_map, long_map = probs_maps(short_tiles)
    rows = pl.BlockSpec((TILE, wide), lambda tile, group: (tile, group))
    row = pl.BlockSpec((1, D), lambda tile, group: (0, 0))
    flops = 10 * D * TILE * TILE * tiles
    in_specs = [
        rows,
        rows,
        rows,
        pl.BlockSpec((1, PAIRS) + probs_short.shape[2:], short_map),
        pl.BlockSpec((1, PAIRS) + probs_long.shape[2:], long_map),
        rows,
    ]
    out_specs = [rows, rows, rows, row, row]
    out_shape = [
        jax.ShapeDtypeStruct((tiles * TILE, D), BF16),
        jax.ShapeDtypeStruct((tiles * TILE, D), BF16),
        jax.ShapeDtypeStruct((tiles * TILE, D), BF16),
        jax.ShapeDtypeStruct((1, D), F32),
        jax.ShapeDtypeStruct((1, D), F32),
    ]
    arguments = [*qkv, probs_short, probs_long, d_context]
    scratch = []
    params = dict(vmem_limit_bytes=60 * MIB)
    if terms is not None:
        arguments.append(terms)
        in_specs.append(pl.BlockSpec(memory_space=pltpu.HBM))
        out_specs.append(pl.BlockSpec((count, BLK), lambda tile, group: (0, 0)))
        out_shape.append(jax.ShapeDtypeStruct((count, BLK), BF16))
        scratch = reduce_scratch(count)
        params.update(collective_id=2, has_side_effects=True)
    return pl.pallas_call(
        partial(attention_back_kernel, short_tiles=short_tiles, transfers=terms is not None),
        grid=(tiles, GROUPS),
        in_specs=in_specs,
        out_specs=out_specs,
        out_shape=out_shape,
        scratch_shapes=scratch,
        compiler_params=pltpu.CompilerParams(**params),
        cost_estimate=pl.CostEstimate(flops=flops, bytes_accessed=50 * MIB, transcendentals=0),
        name="attention_back",
    )(*arguments)


def input_kernel(dq_ref, dk_ref, dv_ref, resid_ref, w_ref, short_ref, long_ref, *, short_tiles):
    tile = pl.program_id(0)
    total = resid_ref[...]
    for index, ref in enumerate((dq_ref, dk_ref, dv_ref)):
        total += right_product(ref[...], w_ref[:, index * D : (index + 1) * D])

    @pl.when(tile < short_tiles)
    def _():
        short_ref[...] = total

    @pl.when(tile >= short_tiles)
    def _():
        long_ref[...] = total


def input_grads(d_qkv, resid, w_qkv, short_tiles):
    tiles = resid.shape[0] // TILE
    rows = pl.BlockSpec((TILE, D), lambda tile: (tile, 0))
    return pl.pallas_call(
        partial(input_kernel, short_tiles=short_tiles),
        grid=(tiles,),
        in_specs=[
            rows,
            rows,
            rows,
            rows,
            pl.BlockSpec((D, 3 * D), lambda tile: (0, 0), pipeline_mode=pl.Buffered(1)),
        ],
        out_specs=[
            pl.BlockSpec((TILE, D), lambda tile: (short_index(tile, short_tiles), 0)),
            pl.BlockSpec((TILE, D), lambda tile: (long_index(tile, short_tiles), 0)),
        ],
        out_shape=[
            jax.ShapeDtypeStruct((short_tiles * TILE, D), F32),
            jax.ShapeDtypeStruct(((tiles - short_tiles) * TILE, D), F32),
        ],
        compiler_params=pltpu.CompilerParams(vmem_limit_bytes=40 * MIB),
        cost_estimate=pl.CostEstimate(
            flops=6 * D * D * TILE * tiles, bytes_accessed=25 * MIB, transcendentals=0
        ),
        name="input_grads",
    )(*d_qkv, resid, w_qkv)


def normal_parts(values):
    below = 0.5 * lax.erf(values * 0.7071067811865476) + 0.5
    return below, jnp.exp(-0.5 * values * values) * 0.3989422804014327


B_OUT, GAIN_ONE, SHIFT_ONE, B_UP, B_DOWN, GAIN_TWO, SHIFT_TWO, B_STUDENT, POOL_QUERY, B_HIDDEN = range(10)
VECTORS = (
    (12, 6),
    (18, 6),
    (24, 6),
    (30, 24),
    (54, 6),
    (60, 6),
    (66, 6),
    (72, 1),
    (73, 1),
    (74, 1),
)
CLASS_ROW = 75
LAST_ROW = 91
SMALL_ROWS = 96


def norm_parts(values):
    center = values - jnp.mean(values, axis=-1, keepdims=True)
    spread = jnp.mean(center * center, axis=-1, keepdims=True)
    inverse = lax.rsqrt(spread + NORM_EPSILON)
    return center * inverse, inverse


def norm_back(d_values, gain, unit, inverse):
    d_unit = d_values * gain
    return inverse * (
        d_unit
        - jnp.mean(d_unit, axis=-1, keepdims=True)
        - unit * jnp.mean(d_unit * unit, axis=-1, keepdims=True)
    )


def column_sum(values):
    return jnp.sum(values.astype(F32), axis=0, keepdims=True)


def pool_weights(student, query, length):
    scaled = student * query
    lane = lax.broadcasted_iota(jnp.int32, scaled.shape, 1)
    place = lax.broadcasted_iota(jnp.int32, (scaled.shape[0], 1), 0)
    weights = []
    for side in (lane < SD // PH, lane >= SD // PH):
        scores = jnp.sum(jnp.where(side, scaled, 0.0), axis=-1, keepdims=True)
        scores = jnp.where(place < length, scores, MASKED_SCORE)
        powers = jnp.exp(scores - jnp.max(scores, axis=0, keepdims=True))
        weights.append(powers / jnp.sum(powers, axis=0, keepdims=True))
    return jnp.where(lane < SD // PH, weights[0], weights[1]), weights


def student_back(student, query, weights, both, d_pooled):
    lane = lax.broadcasted_iota(jnp.int32, student.shape, 1)
    moved = student * d_pooled
    d_scores = []
    for side, weight in zip((lane < SD // PH, lane >= SD // PH), weights):
        d_weight = jnp.sum(jnp.where(side, moved, 0.0), axis=-1, keepdims=True)
        d_scores.append(weight * (d_weight - jnp.sum(weight * d_weight, axis=0, keepdims=True)))
    d_score = jnp.where(lane < SD // PH, d_scores[0], d_scores[1])
    d_query = jnp.sum(d_score * student, axis=0, keepdims=True) * 0.125
    return both * d_pooled + d_score * query, d_query


def feed_kernel(
    len_short,
    len_long,
    slot_ref,
    x_ref,
    context_ref,
    cot_short_ref,
    cot_long_ref,
    logit_cot_ref,
    params,
    w_class,
    b_class,
    blocks,
    enc_short_ref,
    enc_long_ref,
    logit_ref,
    first_ref,
    active_ref,
    d_up_ref,
    d_down_ref,
    d_branch_ref,
    d_context_ref,
    d_resid_ref,
    g_student,
    g_hidden,
    g_small,
    slope,
    pooled_ref,
    d_student_ref,
    w_out,
    w_up,
    w_down,
    w_student,
    w_hidden,
    vectors,
    totals,
    g_class,
    g_last,
    sems,
    *,
    short_tiles,
    width,
):
    tile = pl.program_id(0)
    per_tile = TILE // width
    loads = ((w_out, 108, 6, 6), (w_up, 144, 6, 24), (w_down, 288, 24, 6), (w_student, 432, 6, 1), (w_hidden, 438, 1, 1))

    def arrive(*indices):
        @pl.when(tile == 0)
        def _():
            for index in indices:
                wait_whole(loads[index][0], sems.at[index])

    @pl.when(tile == 0)
    def _():
        for index, (target, block, row_count, col_count) in enumerate(loads):
            load_blocks(slot_ref, blocks, target, sems.at[index], block, row_count, col_count)
        for index, (start, count) in enumerate(VECTORS):
            for place in range(count):
                vectors[index : index + 1, place * BLK : (place + 1) * BLK] = params[
                    start + place : start + place + 1, :
                ]
        for ref in (totals, g_class, g_last, g_student, g_hidden):
            ref[...] = jnp.zeros_like(ref)

    def vector(index):
        return vectors[index : index + 1, : VECTORS[index][1] * BLK]

    def add_total(index, values):
        totals[index : index + 1, : VECTORS[index][1] * BLK] += column_sum(values)

    arrive(0)
    branch = product(context_ref[...], w_out[...]) + vector(B_OUT)
    unit_one, inverse_one = norm_parts(x_ref[...].astype(F32) + branch)
    first = (unit_one * vector(GAIN_ONE) + vector(SHIFT_ONE)).astype(BF16)
    first_ref[...] = first
    arrive(1)
    chunks = [slice(start, start + CHUNK) for start in range(0, FF, CHUNK)]

    def rise(index):
        return product(first, w_up[:, chunks[index]])

    def bend(index, upward):
        upward = upward + vectors[B_UP : B_UP + 1, chunks[index]]
        below, density = normal_parts(upward)
        active_ref[:, chunks[index]] = (upward * below).astype(BF16)
        slope[:, chunks[index]] = (below + upward * density).astype(BF16)

    pipelined(len(chunks), rise, bend, lambda *_: None)
    arrive(2, 3, 4)
    downward = product(active_ref[...], w_down[...]) + vector(B_DOWN)
    unit_two, inverse_two = norm_parts(first.astype(F32) + downward)
    encoded = (unit_two * vector(GAIN_TWO) + vector(SHIFT_TWO)).astype(BF16)

    @pl.when(tile < short_tiles)
    def _():
        enc_short_ref[...] = encoded

    @pl.when(tile >= short_tiles)
    def _():
        enc_long_ref[...] = encoded

    student = product(encoded, w_student[...]) + vector(B_STUDENT)
    query = vector(POOL_QUERY) * 0.125
    pooled_ref[...] = jnp.zeros_like(pooled_ref)

    def head():
        pooled = pooled_ref[...]
        wide_hidden = w_hidden[...].astype(F32)
        hidden = jnp.tanh(product(pooled, wide_hidden, HIGHEST_PRECISION) + vector(B_HIDDEN))
        logit_ref[0] = product(hidden, w_class[...], HIGHEST_PRECISION) + b_class[...]
        d_logits = logit_cot_ref[0]
        g_last[...] += column_sum(d_logits)
        g_class[...] += left_product(d_logits, hidden, HIGHEST_PRECISION)
        d_hidden = right_product(d_logits, w_class[...], HIGHEST_PRECISION)
        d_hidden = d_hidden * (1.0 - hidden * hidden)
        add_total(B_HIDDEN, d_hidden)
        g_hidden[...] += left_product(pooled, d_hidden, HIGHEST_PRECISION)
        return right_product(d_hidden, wide_hidden, HIGHEST_PRECISION)

    def pool(starts, size, lengths):
        kept = []
        for index, (start, length) in enumerate(zip(starts, lengths)):
            rows = student[start : start + size]
            both, weights = pool_weights(rows, query, length)
            pooled_ref[index : index + 1, :] = column_sum(both * rows)
            kept.append((start, rows, both, weights))
        d_pooled = head()
        for index, (start, rows, both, weights) in enumerate(kept):
            d_rows, d_query = student_back(rows, query, weights, both, d_pooled[index : index + 1])
            d_student_ref[start : start + size, :] = d_rows.astype(BF16)
            add_total(POOL_QUERY, d_query)

    @pl.when(tile < short_tiles)
    def _():
        pool(
            [seq * width for seq in range(per_tile)],
            width,
            [len_short[tile * per_tile + seq] for seq in range(per_tile)],
        )

    @pl.when(tile >= short_tiles)
    def _():
        pool([0], TILE, [len_long[tile - short_tiles]])

    d_student = d_student_ref[...]
    add_total(B_STUDENT, d_student)
    g_student[...] += left_product(encoded, d_student)
    cotangent = jnp.where(tile < short_tiles, cot_short_ref[...], cot_long_ref[...])
    d_second = cotangent.astype(F32) + right_product(d_student, w_student[...])
    add_total(GAIN_TWO, d_second * unit_two)
    add_total(SHIFT_TWO, d_second)
    d_resid_two = norm_back(d_second, vector(GAIN_TWO), unit_two, inverse_two)
    d_down = d_resid_two.astype(BF16)
    d_down_ref[...] = d_down
    add_total(B_DOWN, d_down)

    def fall(index):
        return right_product(d_down, w_down[chunks[index], :])

    def bend_back(index, d_active):
        d_up = (d_active * slope[:, chunks[index]].astype(F32)).astype(BF16)
        d_up_ref[:, chunks[index]] = d_up
        totals[B_UP : B_UP + 1, chunks[index]] += column_sum(d_up)

    pipelined(len(chunks), fall, bend_back, lambda *_: None)
    d_first = d_resid_two + right_product(d_up_ref[...], w_up[...])
    add_total(GAIN_ONE, d_first * unit_one)
    add_total(SHIFT_ONE, d_first)
    d_resid_one = norm_back(d_first, vector(GAIN_ONE), unit_one, inverse_one)
    d_resid_ref[...] = d_resid_one
    d_branch = d_resid_one.astype(BF16)
    d_branch_ref[...] = d_branch
    add_total(B_OUT, d_branch)
    d_context_ref[...] = right_product(d_branch, w_out[...]).astype(BF16)

    @pl.when(tile == pl.num_programs(0) - 1)
    def _():
        g_small[...] = jnp.zeros_like(g_small)
        for index, (start, count) in enumerate(VECTORS):
            for place in range(count):
                g_small[start + place : start + place + 1, :] = totals[
                    index : index + 1, place * BLK : (place + 1) * BLK
                ]
        g_small[CLASS_ROW : CLASS_ROW + NCLS, :] = g_class[:NCLS, :]
        g_small[LAST_ROW : LAST_ROW + 1, :] = g_last[...]


def feed(
    len_short, len_long, block_slot, x, context, cot_short, cot_long, logit_cot, small, blocks, short_tiles, width
):
    tiles = x.shape[0] // TILE
    long_tiles = tiles - short_tiles

    def whole(shape):
        return pl.BlockSpec(shape, lambda tile, *_: (0,) * len(shape), pipeline_mode=pl.Buffered(1))

    def kept(shape):
        return pl.BlockSpec(shape, lambda tile, *_: (0,) * len(shape))

    def rows(columns):
        return pl.BlockSpec((TILE, columns), lambda tile, *_: (tile, 0))

    short_rows = pl.BlockSpec((TILE, D), lambda tile, *_: (short_index(tile, short_tiles), 0))
    long_rows = pl.BlockSpec((TILE, D), lambda tile, *_: (long_index(tile, short_tiles), 0))
    logit_rows = pl.BlockSpec((1, 8, SD), lambda tile, *_: (tile, 0, 0))
    grad_shapes = ((D, SD), (SD, SD), (SMALL_ROWS, BLK))
    total = tiles * TILE
    return pl.pallas_call(
        partial(feed_kernel, short_tiles=short_tiles, width=width),
        grid_spec=pltpu.PrefetchScalarGridSpec(
            num_scalar_prefetch=3,
            grid=(tiles,),
            in_specs=[rows(D), rows(D), short_rows, long_rows, logit_rows]
            + [whole(array.shape) for array in small]
            + [pl.BlockSpec(memory_space=pltpu.HBM)],
            out_specs=[
                short_rows,
                long_rows,
                logit_rows,
                rows(D),
                rows(FF),
                rows(FF),
                rows(D),
                rows(D),
                rows(D),
                rows(D),
            ]
            + [kept(shape) for shape in grad_shapes],
            scratch_shapes=[
                pltpu.VMEM((TILE, FF), BF16),
                pltpu.VMEM((8, SD), F32),
                pltpu.VMEM((TILE, SD), BF16),
                pltpu.VMEM((D, D), BF16),
                pltpu.VMEM((D, FF), BF16),
                pltpu.VMEM((FF, D), BF16),
                pltpu.VMEM((D, SD), BF16),
                pltpu.VMEM((SD, SD), BF16),
                pltpu.VMEM((16, FF), F32),
                pltpu.VMEM((16, FF), F32),
                pltpu.VMEM((SD, SD), F32),
                pltpu.VMEM((1, SD), F32),
                pltpu.SemaphoreType.DMA((5,)),
            ],
        ),
        out_shape=[
            jax.ShapeDtypeStruct((short_tiles * TILE, D), BF16),
            jax.ShapeDtypeStruct((long_tiles * TILE, D), BF16),
            jax.ShapeDtypeStruct((tiles, 8, SD), F32),
            jax.ShapeDtypeStruct((total, D), BF16),
            jax.ShapeDtypeStruct((total, FF), BF16),
            jax.ShapeDtypeStruct((total, FF), BF16),
            jax.ShapeDtypeStruct((total, D), BF16),
            jax.ShapeDtypeStruct((total, D), BF16),
            jax.ShapeDtypeStruct((total, D), BF16),
            jax.ShapeDtypeStruct((total, D), F32),
        ]
        + [jax.ShapeDtypeStruct(shape, F32) for shape in grad_shapes],
        compiler_params=pltpu.CompilerParams(vmem_limit_bytes=62 * MIB),
        cost_estimate=pl.CostEstimate(
            flops=total * (8 * D * FF + 4 * D * D), bytes_accessed=70 * MIB, transcendentals=total * FF
        ),
        name="feed",
    )(len_short, len_long, block_slot, x, context, cot_short, cot_long, logit_cot, *small, blocks)


class Place:
    def __init__(self):
        self.quarter = lax.axis_index("dp")
        self.shard = lax.axis_index("fsdp")
        x = self.quarter % 2
        y = self.quarter // 2
        self.core = self.shard % 2
        self.z = self.shard // 2
        self.high = self.z // 2
        self.by_x = 2 * y + 1 - x
        self.by_y = 2 * (1 - y) + x
        self.across = 2 * (1 - y) + 1 - x
        self.sibling = (self.quarter, 2 * self.z + 1 - self.core)
        self.next_x = (self.by_x, self.shard)
        self.next_y = (self.by_y, self.shard)
        self.inner = (self.z > 0) & (self.z < 3)

    def at_z(self, z):
        return (self.quarter, 2 * z + self.core)


def transfer(source, target, send_sem, recv_sem, device):
    return pltpu.make_async_remote_copy(
        src_ref=source,
        dst_ref=target,
        send_sem=send_sem,
        recv_sem=recv_sem,
        device_id=device,
        device_id_type=pl.DeviceIdType.MESH,
    )


def greet(place, extra=()):
    barrier = pltpu.get_barrier_semaphore()

    def signal(device):
        pl.semaphore_signal(barrier, inc=1, device_id=device, device_id_type=pl.DeviceIdType.MESH)

    near = (place.sibling, place.next_x, place.next_y) + tuple(extra)
    for device in near:
        signal(device)

    @pl.when(place.z > 0)
    def _():
        signal(place.at_z(place.z - 1))

    @pl.when(place.z < 3)
    def _():
        signal(place.at_z(place.z + 1))

    pl.semaphore_wait(barrier, len(near) + 1 + (place.z + 1) // 2 % 2)


GATHER_SEMAPHORES = [
    pltpu.SemaphoreType.DMA((2,)),
    pltpu.SemaphoreType.DMA((3,)),
    pltpu.SemaphoreType.DMA((4,)),
    pltpu.SemaphoreType.DMA((12,)),
    pltpu.SemaphoreType.DMA((12,)),
    pltpu.SemaphoreType.DMA((16,)),
    pltpu.SemaphoreType.DMA((16,)),
    pltpu.SemaphoreType.DMA((8,)),
]


class Gather:
    def __init__(self, full, out, sems):
        self.place = place = Place()
        self.full, self.out = full, out
        (
            self.own_send,
            self.relay_send,
            self.z_recv,
            self.xy_send,
            self.xy_recv,
            self.core_send,
            self.core_recv,
            self.out_sems,
        ) = sems
        self.quarter = full.shape[1] // 4
        self.half = self.quarter // 2
        z = place.z
        self.origins = (z + 1 - 2 * (z % 2), 2 - place.high, 3 * (1 - place.high))
        self.relays = (3 - z, 3 * (z - 1), 3 * (z - 1))

    def region(self, which, start, size):
        return self.full.at[which, pl.ds(pl.multiple_of(start, 16), size)]

    def pieces(self, which):
        place, quarter, half = self.place, self.quarter, self.half
        return (
            self.region(which, place.quarter * quarter, quarter),
            self.region(which, place.by_x * quarter, quarter),
            self.region(which, place.by_y * quarter, quarter),
            self.region(which, place.across * quarter, half),
            self.region(which, place.across * quarter + half, half),
        )

    def mine(self):
        return self.region(self.place.shard, self.place.quarter * self.quarter, self.quarter)

    def own_copy(self, side):
        place = self.place
        mine = self.mine()
        device = place.at_z(place.z - 1 + 2 * side)
        return transfer(mine, mine, self.own_send.at[side], self.z_recv.at[place.z], device)

    def core_copy(self, index, ref):
        return transfer(ref, ref, self.core_send.at[index], self.core_recv.at[index], self.place.sibling)

    def xy_copy(self, index, ref, device):
        return transfer(ref, ref, self.xy_send.at[index], self.xy_recv.at[index], device)

    def store(self, index, which):
        return pltpu.make_async_copy(self.full.at[which], self.out.at[which], self.out_sems.at[index])

    def mirrored(self, step):
        return 2 * self.origins[step] + 1 - self.place.core

    def held(self, step):
        return 2 * self.origins[step] + self.place.core

    def start(self):
        place = self.place
        greet(place)

        @pl.when(place.z > 0)
        def _():
            self.own_copy(0).start()

        @pl.when(place.z < 3)
        def _():
            self.own_copy(1).start()

        self.core_copy(0, self.full.at[place.shard]).start()
        self.store(0, place.shard).start()

    def relay(self, step):
        piece = self.pieces(self.held(step))[0]
        device = self.place.at_z(self.relays[step])
        return transfer(
            piece, piece, self.relay_send.at[step], self.z_recv.at[self.origins[step]], device
        )

    def along_z(self, step):
        place = self.place
        self.relay(step).wait_recv()

        @pl.when(place.inner)
        def _():
            self.relay(step).start()

        piece = self.pieces(self.held(step))[0]
        self.xy_copy(4 * step, piece, place.next_x).start()
        self.xy_copy(4 * step + 1, piece, place.next_y).start()
        self.core_copy(1 + 5 * step, piece).start()

    def along_xy(self, step):
        place, half = self.place, self.half
        _, by_x, by_y, _, _ = self.pieces(self.held(step))
        self.xy_copy(4 * step, by_x, place.next_x).wait_recv()
        self.xy_copy(4 * step + 2, by_x.at[pl.ds(0, half)], place.next_y).start()
        self.core_copy(2 + 5 * step, by_x).start()
        self.xy_copy(4 * step + 1, by_y, place.next_y).wait_recv()
        self.xy_copy(4 * step + 3, by_y.at[pl.ds(half, half)], place.next_x).start()
        self.core_copy(3 + 5 * step, by_y).start()

    def across(self, step):
        place = self.place
        _, _, _, first, last = self.pieces(self.held(step))
        self.xy_copy(4 * step + 2, first, place.next_y).wait_recv()
        self.core_copy(4 + 5 * step, first).start()
        self.xy_copy(4 * step + 3, last, place.next_x).wait_recv()
        self.core_copy(5 + 5 * step, last).start()
        self.store(2 + 2 * step, self.held(step)).start()

    def core_own(self):
        which = 2 * self.place.z + 1 - self.place.core
        self.core_copy(0, self.full.at[which]).wait_recv()
        self.store(1, which).start()

    def core(self, step):
        which = self.mirrored(step)
        for index, ref in enumerate(self.pieces(which)):
            self.core_copy(1 + 5 * step + index, ref).wait_recv()
        self.store(3 + 2 * step, which).start()

    def finish(self):
        place = self.place

        @pl.when(place.z > 0)
        def _():
            self.own_copy(0).wait_send()

        @pl.when(place.z < 3)
        def _():
            self.own_copy(1).wait_send()

        self.core_copy(0, self.full.at[place.shard]).wait_send()
        self.store(0, place.shard).wait()
        self.store(1, 2 * place.z + 1 - place.core).wait()
        for step in range(3):

            @pl.when(place.inner)
            def _():
                self.relay(step).wait_send()

            pieces = self.pieces(self.held(step))
            self.xy_copy(4 * step, pieces[0], place.next_x).wait_send()
            self.xy_copy(4 * step + 1, pieces[0], place.next_y).wait_send()
            self.xy_copy(4 * step + 2, pieces[3], place.next_y).wait_send()
            self.xy_copy(4 * step + 3, pieces[4], place.next_x).wait_send()
            for index, ref in enumerate(pieces):
                self.core_copy(1 + 5 * step + index, ref).wait_send()
            self.store(2 + 2 * step, self.held(step)).wait()
            self.store(3 + 2 * step, self.mirrored(step)).wait()


def gather_kernel(master_ref, out_ref, full, *sems):
    gather = Gather(full, out_ref, sems)
    full[gather.place.shard] = master_ref[...].astype(BF16)
    gather.start()
    gather.along_z(0)
    gather.along_z(1)
    gather.along_xy(0)
    gather.along_z(2)
    gather.along_xy(1)
    gather.across(0)
    gather.core_own()
    gather.along_xy(2)
    gather.across(1)
    gather.core(0)
    gather.across(2)
    gather.core(1)
    gather.core(2)
    gather.finish()


def gather_shards(master):
    rows = master.shape[0] * BLK
    shards = lax.axis_size("fsdp")
    return pl.pallas_call(
        gather_kernel,
        in_specs=[pl.BlockSpec(memory_space=pltpu.VMEM)],
        out_specs=pl.BlockSpec(memory_space=pltpu.HBM),
        out_shape=jax.ShapeDtypeStruct((shards, rows, BLK), BF16),
        scratch_shapes=[pltpu.VMEM((shards, rows, BLK), BF16)] + GATHER_SEMAPHORES,
        compiler_params=pltpu.CompilerParams(
            collective_id=0, has_side_effects=True, vmem_limit_bytes=60 * MIB
        ),
        cost_estimate=pl.CostEstimate(flops=0, bytes_accessed=200 * MIB, transcendentals=0),
        name="gather",
    )(master.reshape(rows, BLK)).reshape(-1, BLK, BLK)


def add_rows(target, former, latter, rows, step):
    @pl.loop(0, rows // step)
    def _(index):
        part = pl.ds(pl.multiple_of(index * step, 16), step)
        target[part] = (former[part].astype(F32) + latter[part].astype(F32)).astype(BF16)


def reduce_scratch(rows):
    quarter = rows // 4
    half = quarter // 2
    return [
        pltpu.VMEM((4, rows, BLK), BF16),
        pltpu.VMEM((4, rows, BLK), BF16),
        pltpu.VMEM((4, 2, half, BLK), BF16),
        pltpu.VMEM((4, 2, half, BLK), BF16),
        pltpu.VMEM((4, half, BLK), BF16),
        pltpu.VMEM((4, half, BLK), BF16),
        pltpu.VMEM((5, quarter, BLK), BF16),
        pltpu.VMEM((rows, BLK), BF16),
        pltpu.SemaphoreType.DMA((4,)),
        pltpu.SemaphoreType.DMA((4,)),
        pltpu.SemaphoreType.DMA((4,)),
        pltpu.SemaphoreType.DMA((24,)),
        pltpu.SemaphoreType.DMA((24,)),
        pltpu.SemaphoreType.DMA((3,)),
        pltpu.SemaphoreType.DMA((5,)),
        pltpu.SemaphoreType.DMA((4,)),
        pltpu.SemaphoreType.DMA((4,)),
    ]


class Reduce:
    def __init__(self, terms, base, out, scratch):
        self.place = place = Place()
        self.terms, self.base, self.out = terms, base, out
        (
            self.mine,
            self.sib,
            self.from_x,
            self.from_y,
            self.late_y,
            self.late_x,
            self.from_z,
            self.result,
            self.load_sems,
            self.core_send,
            self.core_recv,
            self.xy_send,
            self.xy_recv,
            self.z_send,
            self.z_recv,
            self.last_send,
            self.last_recv,
        ) = scratch
        self.quarter = out.shape[0] // 4
        self.half = self.quarter // 2
        z, high = place.z, place.high
        low = 1 - high
        self.order = (3 * low, low * (2 - 2 * z) + high * (7 - 2 * z), 1 + z % 2, z)
        self.onward = (z + 1 - 2 * high, z + 1 - 2 * (z % 2), z + 1 - 2 * high)
        self.closing = (0, (z % 2) * low, high)
        self.far = place.at_z(z + 2 - 4 * high)
        self.near = place.at_z(z + 1 - 2 * (z % 2))

    def shard_terms(self, shard):
        rows = self.out.shape[0]
        return self.terms.at[pl.ds(pl.multiple_of(self.base + shard * rows, 16), rows)]

    def load(self, step):
        source = self.shard_terms(2 * self.order[step] + self.place.core)
        return pltpu.make_async_copy(source, self.mine.at[step], self.load_sems.at[step])

    def core_copy(self, step):
        return transfer(
            self.shard_terms(2 * self.order[step] + 1 - self.place.core),
            self.sib.at[step],
            self.core_send.at[step],
            self.core_recv.at[step],
            self.place.sibling,
        )

    def part(self, step, which, side):
        start = pl.multiple_of(which * self.quarter + side * self.half, 16)
        return self.mine.at[step, pl.ds(start, self.half)]

    def xy_copy(self, step, index):
        place = self.place
        source, target, device = (
            (self.part(step, place.by_x, 0), self.from_x.at[step, 0], place.next_x),
            (self.part(step, place.across, 0), self.from_x.at[step, 1], place.next_x),
            (self.part(step, place.by_y, 1), self.from_y.at[step, 0], place.next_y),
            (self.part(step, place.across, 1), self.from_y.at[step, 1], place.next_y),
            (self.part(step, place.by_y, 0), self.late_y.at[step], place.next_y),
            (self.part(step, place.by_x, 1), self.late_x.at[step], place.next_x),
        )[index]
        place = 6 * step + index
        return transfer(source, target, self.xy_send.at[place], self.xy_recv.at[place], device)

    def start(self):
        greet(self.place, (self.far,))
        for step in range(2):
            self.core_copy(step).start()
        for step in range(4):
            self.load(step).start()

    def core(self, step):
        place, quarter = self.place, self.quarter
        self.load(step).wait()
        self.core_copy(step).wait_recv()
        if step < 2:
            self.core_copy(step + 2).start()

        def add(which):
            block = pl.ds(pl.multiple_of(which * quarter, 16), quarter)
            mine = self.mine.at[step, block]
            add_rows(mine, mine, self.sib.at[step, block], quarter, self.half)

        add(place.by_x)
        add(place.across)
        self.xy_copy(step, 0).start()
        self.xy_copy(step, 1).start()
        add(place.by_y)
        self.xy_copy(step, 2).start()
        self.xy_copy(step, 3).start()
        add(place.quarter)

    def take(self, step, which, side, index, source):
        self.xy_copy(step, index).wait_recv()
        target = self.part(step, which, side)
        add_rows(target, target, source, self.half, self.half)

    def first(self, step):
        place = self.place
        self.take(step, place.by_y, 0, 1, self.from_x.at[step, 1])
        self.xy_copy(step, 4).start()
        self.take(step, place.by_x, 1, 3, self.from_y.at[step, 1])
        self.xy_copy(step, 5).start()
        self.take(step, place.quarter, 0, 0, self.from_x.at[step, 0])
        self.take(step, place.quarter, 1, 2, self.from_y.at[step, 0])

    def own_block(self, step):
        return self.mine.at[step, pl.ds(pl.multiple_of(self.place.quarter * self.quarter, 16), self.quarter)]

    def z_copy(self, step):
        goal = self.order[step]
        slot = goal + self.closing[step] * (4 - goal)
        return transfer(
            self.own_block(step),
            self.from_z.at[slot],
            self.z_send.at[step],
            self.z_recv.at[slot],
            self.place.at_z(self.onward[step]),
        )

    def take_z(self, step, slot):
        source = self.from_z.at[slot]
        transfer(source, source, self.z_send.at[0], self.z_recv.at[slot], self.near).wait_recv()
        block = self.own_block(step)
        add_rows(block, block, source, self.quarter, self.half)

    def second(self, step):
        place = self.place
        self.take(step, place.quarter, 0, 4, self.late_y.at[step])
        self.take(step, place.quarter, 1, 5, self.late_x.at[step])
        if step < 3:

            @pl.when(place.inner)
            def _():
                self.take_z(step, self.order[step])

            self.z_copy(step).start()
        else:

            @pl.when(place.z > 0)
            def _():
                self.take_z(step, place.z)

            @pl.when(place.z < 3)
            def _():
                self.take_z(step, 4)

    def final(self, which, side=None):
        start = pl.multiple_of(which * self.quarter + (0 if side is None else side * self.half), 16)
        return self.result.at[pl.ds(start, self.quarter if side is None else self.half)]

    def last_copy(self, index, ref):
        device = (self.place.next_x, self.place.next_y, self.place.next_y, self.place.next_x)[index]
        return transfer(ref, ref, self.last_send.at[index], self.last_recv.at[index], device)

    def share(self):
        own = self.final(self.place.quarter)
        own[...] = self.own_block(3)[...]
        self.last_copy(0, own).start()
        self.last_copy(1, own).start()

    def share_on(self):
        place = self.place
        self.last_copy(0, self.final(place.by_x)).wait_recv()
        self.last_copy(2, self.final(place.by_x, 0)).start()
        self.last_copy(1, self.final(place.by_y)).wait_recv()
        self.last_copy(3, self.final(place.by_y, 1)).start()

    def finish(self):
        place = self.place
        self.last_copy(2, self.final(place.across, 0)).wait_recv()
        self.last_copy(3, self.final(place.across, 1)).wait_recv()
        self.out[...] = self.result[...]
        for step in range(4):
            self.core_copy(step).wait_send()
            for index in range(6):
                self.xy_copy(step, index).wait_send()
            if step < 3:
                self.z_copy(step).wait_send()
        own = self.final(place.quarter)
        self.last_copy(0, own).wait_send()
        self.last_copy(1, own).wait_send()
        self.last_copy(2, self.final(place.by_x, 0)).wait_send()
        self.last_copy(3, self.final(place.by_y, 1)).wait_send()


def reduce_kernel(
    terms, small_ref, out_ref, small_out, small_in, small_sum, small_send, small_recv, *scratch, base
):
    reduce = Reduce(terms, base, out_ref, scratch)
    place = reduce.place
    partners = (place.sibling, place.next_x, place.next_y, reduce.near, reduce.far)

    def small_copy(level):
        return transfer(
            small_sum.at[level],
            small_in.at[level],
            small_send.at[level],
            small_recv.at[level],
            partners[level],
        )

    def small_step(level):
        small_copy(level - 1).wait_recv()
        small_sum[level] = small_sum[level - 1] + small_in[level - 1]
        if level < 5:
            small_copy(level).start()

    small_sum[0] = small_ref[...]
    reduce.start()
    small_copy(0).start()
    reduce.core(0)
    small_step(1)
    reduce.core(1)
    reduce.first(0)
    small_step(2)
    reduce.core(2)
    reduce.first(1)
    reduce.second(0)
    small_step(3)
    reduce.core(3)
    reduce.first(2)
    reduce.second(1)
    small_step(4)
    reduce.first(3)
    reduce.second(2)
    small_step(5)
    small_out[...] = small_sum[5]
    reduce.second(3)
    reduce.share()
    reduce.share_on()
    reduce.finish()
    for level in range(5):
        small_copy(level).wait_send()


def reduce_late(terms, base, rows, small):
    vmem = pl.BlockSpec(memory_space=pltpu.VMEM)
    return pl.pallas_call(
        partial(reduce_kernel, base=base),
        in_specs=[pl.BlockSpec(memory_space=pltpu.HBM), vmem],
        out_specs=[vmem, vmem],
        out_shape=[
            jax.ShapeDtypeStruct((rows, BLK), BF16),
            jax.ShapeDtypeStruct((SMALL_ROWS, BLK), F32),
        ],
        scratch_shapes=[
            pltpu.VMEM((5, SMALL_ROWS, BLK), F32),
            pltpu.VMEM((6, SMALL_ROWS, BLK), F32),
            pltpu.SemaphoreType.DMA((5,)),
            pltpu.SemaphoreType.DMA((5,)),
        ]
        + reduce_scratch(rows),
        compiler_params=pltpu.CompilerParams(
            collective_id=3, has_side_effects=True, vmem_limit_bytes=48 * MIB
        ),
        cost_estimate=pl.CostEstimate(flops=0, bytes_accessed=200 * MIB, transcendentals=0),
        name="reduce",
    )(terms, small)


def count_where(condition, axis):
    return jnp.sum(condition.astype(jnp.int32), axis=axis)


def slot_codes(slots, qkv_slots, slot_count, shards):
    early = slot_count - LATE
    shard = slots // slot_count
    begin = shard * slot_count
    inside = (qkv_slots[None, :] >= begin[:, None]) & (qkv_slots[None, :] < (begin + slot_count)[:, None])
    own = count_where(qkv_slots[None, :] == slots[:, None], 1)
    before = count_where(inside & (qkv_slots[None, :] < slots[:, None]), 1)
    number = count_where(inside, 1)
    position = jnp.where(own > 0, slot_count - number + before, slots - begin - before)
    return jnp.where(
        position < early,
        shard * early + position,
        shards * early + shard * LATE + position - early,
    ), position


def empty_slots(block_slot, all_slots):
    places = jnp.arange(all_slots, dtype=jnp.int32)
    empty_before = places + 1 - count_where(block_slot[None, :] <= places[:, None], 1)
    empty_index = jnp.arange(all_slots - NBLK, dtype=jnp.int32)
    return count_where(empty_before[None, :] <= empty_index[:, None], 1)


def body(
    x_short,
    x_long,
    cot_short,
    cot_long,
    logit_cot_short,
    logit_cot_long,
    len_short,
    len_long,
    block_slot,
    master,
    left_stat,
    right_stat,
    left_root,
    right_root,
    small_params,
    small_first,
    small_second,
    own_transfers,
):
    slot_count = master.shape[0]
    shards = lax.axis_size("fsdp")
    all_slots = slot_count * shards
    short_seqs, width = x_short.shape[:2]
    long_seqs = x_long.shape[0]
    short_tiles = short_seqs * width // TILE
    per_tile = TILE // width
    empty = empty_slots(block_slot, all_slots)

    if own_transfers:
        early_count = slot_count - LATE
        qkv_slots = block_slot[: 3 * 36]
        code, _ = slot_codes(block_slot, qkv_slots, slot_count, shards)
        empty_code, _ = slot_codes(empty, qkv_slots, slot_count, shards)
        own = jnp.arange(slot_count, dtype=jnp.int32) + slot_count * lax.axis_index("fsdp")
        _, position = slot_codes(own, qkv_slots, slot_count, shards)
        shard_index = jnp.arange(shards, dtype=jnp.int32)
        most = jnp.max(count_where(qkv_slots[None, :] // slot_count == shard_index[:, None], 1))
        fits = most <= LATE
        gathered = gather_shards(master)
    else:
        gathered = lax.all_gather(master.astype(BF16), "fsdp", axis=0, tiled=True)
    w_qkv = assemble(block_slot, gathered)
    pieces = unpack(small_params)
    params = jnp.pad(small_params, (0, SMALL_ROWS * BLK - small_params.shape[0])).reshape(SMALL_ROWS, BLK)
    w_class = jnp.pad(pieces[-2].reshape(SD, NCLS), ((0, 0), (0, SD - NCLS)))
    b_class = jnp.pad(pieces[-1].reshape(1, NCLS), ((0, 0), (0, SD - NCLS)))

    x = jnp.concatenate([x_short.reshape(-1, D), x_long.reshape(-1, D)], axis=0)
    *qkv, context, probs_short, probs_long = attention(
        len_short,
        len_long,
        x,
        pieces[0].reshape(1, D),
        pieces[1].reshape(1, D),
        w_qkv,
        short_tiles,
        width,
    )

    logit_cot = jnp.concatenate(
        [
            jnp.pad(
                logit_cot_short.reshape(short_tiles, per_tile, NCLS),
                ((0, 0), (0, 8 - per_tile), (0, SD - NCLS)),
            ),
            jnp.pad(logit_cot_long.reshape(long_seqs, 1, NCLS), ((0, 0), (0, 7), (0, SD - NCLS))),
        ],
        axis=0,
    )
    (
        enc_short,
        enc_long,
        logits,
        first,
        active,
        d_up,
        d_down,
        d_branch,
        d_context,
        d_resid,
        g_student,
        g_hidden,
        g_small,
    ) = feed(
        len_short,
        len_long,
        block_slot,
        x,
        context,
        cot_short.reshape(-1, D),
        cot_long.reshape(-1, D),
        logit_cot,
        (params, w_class, b_class),
        gathered,
        short_tiles,
        width,
    )
    g_down = left_product(active, d_down).astype(BF16)
    g_up = left_product(first, d_up).astype(BF16)
    g_out = left_product(context, d_branch).astype(BF16)
    others = (g_out, g_up, g_down, g_student.astype(BF16), g_hidden.astype(BF16))
    if own_transfers:
        terms = spread(code, empty_code, others, OTHER_PLACES, all_slots)
        *back, early_reduced = attention_back(
            qkv,
            probs_short,
            probs_long,
            d_context,
            short_tiles,
            terms.reshape(-1, BLK),
            early_count * BLK,
        )
    else:
        back = attention_back(qkv, probs_short, probs_long, d_context, short_tiles)
    *d_qkv, g_b_query, g_b_value = back
    in_short, in_long = input_grads(d_qkv, d_resid, w_qkv, short_tiles)
    qkv_grads = tuple(left_product(x, d_rows).astype(BF16) for d_rows in d_qkv)

    def reduce_all():
        slot_terms = spread(block_slot, empty, qkv_grads + others, QKV_PLACES + OTHER_PLACES, all_slots)
        return lax.psum(lax.psum_scatter(slot_terms, "fsdp", scatter_dimension=0, tiled=True), "dp")

    if own_transfers:
        terms, small_terms = spread_late(code, qkv_grads, g_small, g_b_query, g_b_value, terms)
        late_reduced, small_total = reduce_late(
            terms.reshape(-1, BLK), shards * early_count * BLK, LATE * BLK, small_terms
        )

        def join():
            blocks = jnp.concatenate([early_reduced, late_reduced], axis=0).reshape(slot_count, BLK, BLK)
            return blocks.at[position].get(mode="promise_in_bounds")

        slot_grad = lax.cond(fits, join, reduce_all)
    else:
        slot_grad = reduce_all()
        small_terms = jnp.concatenate(
            [g_b_query.reshape(-1, BLK), g_b_value.reshape(-1, BLK), g_small[2 * D // BLK :]], axis=0
        )
        small_total = lax.psum(small_terms, ("dp", "fsdp"))
    slot_grad = slot_grad.astype(F32)
    small_grad = jnp.concatenate(
        [
            small_total[:CLASS_ROW].reshape(-1),
            small_total[CLASS_ROW : CLASS_ROW + NCLS].T.reshape(-1),
            small_total[LAST_ROW, :NCLS],
        ]
    )
    outer_left = jnp.einsum("sij,skj->sik", slot_grad, slot_grad, precision=HIGHEST_PRECISION)
    outer_right = jnp.einsum("sji,sjk->sik", slot_grad, slot_grad, precision=HIGHEST_PRECISION)
    new_left = STAT_DECAY * left_stat + (1.0 - STAT_DECAY) * outer_left
    new_right = STAT_DECAY * right_stat + (1.0 - STAT_DECAY) * outer_right
    left_applied = jnp.einsum("sij,sjk->sik", left_root, slot_grad, precision=HIGHEST_PRECISION)
    conditioned = jnp.einsum("sij,sjk->sik", left_applied, right_root, precision=HIGHEST_PRECISION)
    new_master = master - MATRIX_RATE * conditioned
    new_first = BETA_ONE * small_first + (1.0 - BETA_ONE) * small_grad
    new_second = BETA_TWO * small_second + (1.0 - BETA_TWO) * small_grad * small_grad
    first_hat = new_first / (1.0 - BETA_ONE**STEP)
    second_hat = new_second / (1.0 - BETA_TWO**STEP)
    new_small = small_params - ADAM_RATE * first_hat / (jnp.sqrt(second_hat) + ADAM_EPSILON)
    return (
        enc_short.reshape(x_short.shape),
        logits[:short_tiles, :per_tile, :NCLS].reshape(short_seqs, NCLS),
        enc_long.reshape(x_long.shape),
        logits[short_tiles:, 0, :NCLS],
        in_short.reshape(x_short.shape),
        in_long.reshape(x_long.shape),
        slot_grad,
        new_left,
        new_right,
        new_master,
        new_first,
        new_second,
        new_small,
    )


def solution(mesh):
    both = ("dp", "fsdp")
    placed = (
        P(both, None, None),
        P(both, None, None),
        P(both, None, None),
        P(both, None, None),
        P(both, None),
        P(both, None),
        P(both),
        P(both),
        P(),
        P("fsdp", None, None),
        P("fsdp", None, None),
        P("fsdp", None, None),
        P("fsdp", None, None),
        P("fsdp", None, None),
        P(),
        P(),
        P(),
    )
    return jax.shard_map(
        partial(body, own_transfers=(mesh.shape["dp"], mesh.shape["fsdp"]) == (4, 8)),
        mesh=mesh,
        in_specs=placed,
        out_specs=(
            P(both, None, None),
            P(both, None),
            P(both, None, None),
            P(both, None),
            P(both, None, None),
            P(both, None, None),
            P("fsdp", None, None),
            P("fsdp", None, None),
            P("fsdp", None, None),
            P("fsdp", None, None),
            P(),
            P(),
            P(),
        ),
        check_vma=False,
    )
```

```python
from functools import partial

import jax
import jax.numpy as jnp
from jax import lax
from jax.experimental import pallas as pl
from jax.experimental.pallas import tpu as pltpu
from jax.sharding import PartitionSpec as P

D = 768
HEADS = 12
FF = 3072
SD = 128
PH = 2
NCLS = 14
BLK = 128
STEP = 10
NBLK = 439
TILE = 512
PAIRS = 3
GROUPS = 2
CHUNK = 768
LATE = 24

NORM_EPSILON = 1e-12
BETA_ONE = 0.9
BETA_TWO = 0.999
ADAM_EPSILON = 1e-08
ADAM_RATE = 0.1
MATRIX_RATE = 0.2
STAT_DECAY = 0.5
MASKED_SCORE = -1e30
HIGHEST_PRECISION = lax.Precision.HIGHEST
MIB = 1024 * 1024
F32 = jnp.float32
BF16 = jnp.bfloat16

def product(former, latter, precision=None):
    return jnp.dot(former, latter, preferred_element_type=F32, precision=precision)


def left_product(former, latter, precision=None):
    return lax.dot_general(
        former, latter, (((0,), (0,)), ((), ())), preferred_element_type=F32, precision=precision
    )


def right_product(former, latter, precision=None):
    return lax.dot_general(
        former, latter, (((1,), (1,)), ((), ())), preferred_element_type=F32, precision=precision
    )


def unpack(small_values):
    widths = (D, D, D, D, D, FF, D, D, D, SD, SD, SD, SD * NCLS, NCLS)
    pieces = []
    offset = 0
    for column_count in widths:
        pieces.append(small_values[offset : offset + column_count])
        offset += column_count
    return pieces


def each_block(first, row_count, col_count, action):
    def one_row(index, carry):
        row = pl.multiple_of(index * BLK, BLK)
        for col in range(col_count):
            action(first + index * col_count + col, row, col * BLK)
        return carry

    lax.fori_loop(0, row_count, one_row, 0)


def load_blocks(slot_ref, blocks, target, sem, first, row_count, col_count, col_start=0):
    def move(block, row, col):
        pltpu.make_async_copy(
            blocks.at[slot_ref[block]],
            target.at[pl.ds(row, BLK), pl.ds(col + col_start * BLK, BLK)],
            sem,
        ).start()

    each_block(first, row_count, col_count, move)


def wait_whole(target, sem):
    pltpu.make_async_copy(target, target, sem).wait()


def assemble_kernel(slot_ref, blocks, out, sem):
    for which in range(3):
        load_blocks(slot_ref, blocks, out, sem, 36 * which, 6, 6, 6 * which)
    wait_whole(out, sem)


def assemble(block_slot, blocks):
    return pl.pallas_call(
        assemble_kernel,
        grid_spec=pltpu.PrefetchScalarGridSpec(
            num_scalar_prefetch=1,
            grid=(1,),
            in_specs=[pl.BlockSpec(memory_space=pltpu.HBM)],
            out_specs=pl.BlockSpec(memory_space=pltpu.VMEM),
            scratch_shapes=[pltpu.SemaphoreType.DMA],
        ),
        out_shape=jax.ShapeDtypeStruct((D, 3 * D), BF16),
        compiler_params=pltpu.CompilerParams(vmem_limit_bytes=60 * MIB),
        name="assemble",
    )(block_slot, blocks)


QKV_PLACES = ((0, 6, 6), (36, 6, 6), (72, 6, 6))
OTHER_PLACES = ((108, 6, 6), (144, 6, 24), (288, 24, 6), (432, 6, 1), (438, 1, 1))


def spread_kernel(code_ref, empty_ref, *refs, places):
    grads = refs[: len(places)]
    zero, out, sems = refs[len(places) :]
    for which, (grad, place) in enumerate(zip(grads, places)):

        def move(block, row, col, which=which, grad=grad):
            pltpu.make_async_copy(
                grad.at[pl.ds(row, BLK), pl.ds(col, BLK)], out.at[code_ref[block]], sems.at[which]
            ).start()

        each_block(*place, move)
    for index in range(empty_ref.shape[0]):
        pltpu.make_async_copy(zero, out.at[empty_ref[index]], sems.at[len(places) + index]).start()
    for which, grad in enumerate(grads):
        wait_whole(grad, sems.at[which])
    for index in range(empty_ref.shape[0]):
        wait_whole(zero, sems.at[len(places) + index])


def spread(code, empty, grads, places, slot_count):
    vmem = pl.BlockSpec(memory_space=pltpu.VMEM)
    return pl.pallas_call(
        partial(spread_kernel, places=places),
        grid_spec=pltpu.PrefetchScalarGridSpec(
            num_scalar_prefetch=2,
            grid=(1,),
            in_specs=[vmem] * (len(grads) + 1),
            out_specs=pl.BlockSpec(memory_space=pltpu.HBM),
            scratch_shapes=[pltpu.SemaphoreType.DMA((len(grads) + empty.shape[0],))],
        ),
        out_shape=jax.ShapeDtypeStruct((slot_count, BLK, BLK), BF16),
        compiler_params=pltpu.CompilerParams(vmem_limit_bytes=44 * MIB),
        name="spread",
    )(code, empty, *grads, jnp.zeros((BLK, BLK), BF16))


def spread_late_kernel(code_ref, *refs):
    grads = refs[:3]
    small_ref, query_ref, value_ref, _, out, small_out, sems = refs[3:]
    for which, (grad, place) in enumerate(zip(grads, QKV_PLACES)):

        def move(block, row, col, which=which, grad=grad):
            pltpu.make_async_copy(
                grad.at[pl.ds(row, BLK), pl.ds(col, BLK)], out.at[code_ref[block]], sems.at[which]
            ).start()

        each_block(*place, move)
    join_small(small_ref, query_ref, value_ref, small_out)
    for which, grad in enumerate(grads):
        wait_whole(grad, sems.at[which])


def join_small(small_ref, query_ref, value_ref, small_out):
    small_out[...] = small_ref[...]
    for start, ref in ((0, query_ref), (D // BLK, value_ref)):
        for index in range(D // BLK):
            small_out[start + index : start + index + 1, :] = ref[:, index * BLK : (index + 1) * BLK]


def spread_late(code, grads, small, g_query, g_value, terms):
    vmem = pl.BlockSpec(memory_space=pltpu.VMEM)
    anywhere = pl.BlockSpec(memory_space=pltpu.HBM)
    return pl.pallas_call(
        spread_late_kernel,
        grid_spec=pltpu.PrefetchScalarGridSpec(
            num_scalar_prefetch=1,
            grid=(1,),
            in_specs=[vmem] * 6 + [anywhere],
            out_specs=[anywhere, vmem],
            scratch_shapes=[pltpu.SemaphoreType.DMA((3,))],
        ),
        out_shape=[
            jax.ShapeDtypeStruct(terms.shape, BF16),
            jax.ShapeDtypeStruct(small.shape, F32),
        ],
        input_output_aliases={7: 0},
        compiler_params=pltpu.CompilerParams(vmem_limit_bytes=44 * MIB),
        name="spread_late",
    )(code, *grads, small, g_query, g_value, terms)


def half_masks():
    lane = lax.broadcasted_iota(jnp.int32, (1, BLK), 1)
    low = (lane < BLK // 2).astype(BF16)
    return low, (1.0 - low.astype(F32)).astype(BF16)


def stack_heads(values, low, high):
    return jnp.concatenate([values * low, values * high], axis=0)


def pick_heads(values):
    rows = values.shape[0] // 2
    lane = lax.broadcasted_iota(jnp.int32, (rows, BLK), 1)
    return jnp.where(lane < BLK // 2, values[:rows], values[rows:])


def pipelined(count, before, middle, after):
    started = before(0)
    done = None
    for index in range(count):
        current = started
        if index + 1 < count:
            started = before(index + 1)
        if done is not None:
            after(index - 1, done)
        done = middle(index, current)
    after(count - 1, done)


def softmax(scores, length):
    visible = lax.broadcasted_iota(jnp.int32, scores.shape, 1) < length
    scores = jnp.where(visible, scores, MASKED_SCORE)
    powers = jnp.exp(scores - jnp.max(scores, axis=-1, keepdims=True))
    total = jnp.sum(powers, axis=-1, keepdims=True)
    return (powers * (1.0 / total)).astype(BF16)


def attention_kernel(
    len_short,
    len_long,
    x_short_ref,
    x_long_ref,
    params,
    w_ref,
    x_ref,
    q_ref,
    k_ref,
    v_ref,
    context_ref,
    short_ref,
    long_ref,
    bias,
    *,
    short_tiles,
):
    tile = pl.program_id(0)
    group = pl.program_id(1)
    low, high = half_masks()
    width = short_ref.shape[-1]
    per_tile = TILE // width

    wide = PAIRS * BLK
    start = pl.multiple_of(group * wide, wide)

    @pl.when((tile == 0) & (group == 0))
    def _():
        for which in range(2):
            for place in range(D // BLK):
                row = which * (D // BLK) + place
                bias[which : which + 1, place * BLK : (place + 1) * BLK] = params[row : row + 1, :]

    @pl.when((tile < short_tiles) & (group == 0))
    def _():
        x_ref[...] = x_short_ref[...]

    @pl.when((tile >= short_tiles) & (group == 0))
    def _():
        x_ref[...] = x_long_ref[...]

    rows_in = x_ref[...]
    queries = product(rows_in, w_ref[:, pl.ds(start, wide)]) + bias[0:1, pl.ds(start, wide)]
    q_ref[...] = (queries * 0.125).astype(BF16)
    k_ref[...] = product(rows_in, w_ref[:, pl.ds(D + start, wide)]).astype(BF16)
    values = product(rows_in, w_ref[:, pl.ds(2 * D + start, wide)]) + bias[1:2, pl.ds(start, wide)]
    v_ref[...] = values.astype(BF16)

    def attend(units, kept_ref):
        def scores(index):
            rows, keys, cols, _, _ = units[index]
            return right_product(stack_heads(q_ref[rows, cols], low, high), k_ref[keys, cols])

        def weigh(index, values):
            _, _, _, length, place = units[index]
            probs = softmax(values, length)
            kept_ref[place] = probs
            return probs

        def mix(index, probs):
            rows, keys, cols, _, _ = units[index]
            context_ref[rows, cols] = pick_heads(product(probs, v_ref[keys, cols])).astype(BF16)

        pipelined(len(units), scores, weigh, mix)

    @pl.when(tile < short_tiles)
    def _():
        units = []
        for seq in range(per_tile):
            rows = slice(seq * width, (seq + 1) * width)
            length = len_short[tile * per_tile + seq]
            for pair in range(PAIRS):
                cols = slice(pair * BLK, (pair + 1) * BLK)
                units.append((rows, rows, cols, length, (0, pair, seq)))
        attend(units, short_ref)

    @pl.when(tile >= short_tiles)
    def _():
        length = len_long[tile - short_tiles]
        half = TILE // 2
        units = []
        for pair in range(PAIRS):
            cols = slice(pair * BLK, (pair + 1) * BLK)
            for part in range(2):
                rows = slice(part * half, (part + 1) * half)
                units.append((rows, slice(0, TILE), cols, length, (0, pair, part)))
        attend(units, long_ref)


def run_events(step, events):
    for index, actions in enumerate(events):

        @pl.when(step == index)
        def _(actions=actions):
            for action in actions:
                action()


def probs_shapes(short_tiles, long_tiles, width):
    per_tile = TILE // width
    return (
        (short_tiles, 2 * PAIRS, per_tile, 2 * width, width),
        (long_tiles, 2 * PAIRS, 2, TILE, TILE),
    )


def short_index(tile, short_tiles):
    return jnp.minimum(tile, short_tiles - 1)


def long_index(tile, short_tiles):
    return jnp.maximum(tile - short_tiles, 0)


def probs_maps(short_tiles):
    def short_map(tile, group):
        last = jnp.minimum(tile // short_tiles, 1)
        return (short_index(tile, short_tiles), group + last * (GROUPS - 1 - group), 0, 0, 0)

    def long_map(tile, group):
        begun = jnp.minimum(tile // short_tiles, 1)
        return (long_index(tile, short_tiles), begun * group, 0, 0, 0)

    return short_map, long_map


def attention(len_short, len_long, x_short, x_long, params, w_qkv, short_tiles, width):
    tiles = (x_short.shape[0] + x_long.shape[0]) // TILE
    wide = PAIRS * BLK
    short_shape, long_shape = probs_shapes(short_tiles, tiles - short_tiles, width)
    short_map, long_map = probs_maps(short_tiles)
    flops = 4 * D * TILE * TILE * tiles + 6 * D * D * TILE * tiles
    rows = pl.BlockSpec((TILE, wide), lambda tile, group: (tile, group))
    scalars = pl.BlockSpec(memory_space=pltpu.SMEM)

    def whole(shape):
        return pl.BlockSpec(shape, lambda tile, group: (0,) * len(shape), pipeline_mode=pl.Buffered(1))

    in_specs = [
        scalars,
        scalars,
        pl.BlockSpec((TILE, D), lambda tile, group: (short_index(tile, short_tiles), 0)),
        pl.BlockSpec((TILE, D), lambda tile, group: (long_index(tile, short_tiles), 0)),
        whole(params.shape),
        whole((D, 3 * D)),
    ]
    out_specs = [
        pl.BlockSpec((TILE, D), lambda tile, group: (tile, 0)),
        rows,
        rows,
        rows,
        rows,
        pl.BlockSpec((1, PAIRS) + short_shape[2:], short_map),
        pl.BlockSpec((1, PAIRS) + long_shape[2:], long_map),
    ]
    out_shape = [jax.ShapeDtypeStruct((tiles * TILE, D), BF16)] * 5 + [
        jax.ShapeDtypeStruct(short_shape, BF16),
        jax.ShapeDtypeStruct(long_shape, BF16),
    ]
    arguments = [len_short, len_long, x_short, x_long, params, w_qkv]
    return pl.pallas_call(
        partial(attention_kernel, short_tiles=short_tiles),
        grid=(tiles, GROUPS),
        in_specs=in_specs,
        out_specs=out_specs,
        out_shape=out_shape,
        scratch_shapes=[pltpu.VMEM((8, D), F32)],
        compiler_params=pltpu.CompilerParams(vmem_limit_bytes=60 * MIB),
        cost_estimate=pl.CostEstimate(
            flops=flops, bytes_accessed=35 * MIB, transcendentals=HEADS * TILE * TILE * tiles // 2
        ),
        name="attention",
    )(*arguments)


def attention_back_kernel(*refs, short_tiles, transfers):
    q_ref, k_ref, v_ref, short_ref, long_ref, dc_ref = refs[:6]
    refs = refs[6:]
    if transfers:
        terms_ref, refs = refs[0], refs[1:]
    dq_ref, dk_ref, dv_ref, bq_ref, bv_ref = refs[:5]
    tile = pl.program_id(0)
    group = pl.program_id(1)
    low, high = half_masks()
    width = short_ref.shape[-1]
    per_tile = TILE // width
    if transfers:
        reduce = Reduce(terms_ref, 0, refs[5], refs[6:])
        run_events(
            tile * GROUPS + group,
            (
                (reduce.start,),
                (partial(reduce.core, 0),),
                (partial(reduce.core, 1), partial(reduce.first, 0)),
                (partial(reduce.core, 2), partial(reduce.first, 1), partial(reduce.second, 0)),
                (partial(reduce.core, 3), partial(reduce.first, 2), partial(reduce.second, 1)),
                (partial(reduce.first, 3), partial(reduce.second, 2)),
                (partial(reduce.second, 3), reduce.share),
                (reduce.share_on,),
            ),
        )

    def go_back(units, kept_ref, parts):
        sums = {}

        def spread_in(index):
            rows, keys, cols, _ = units[index]
            return right_product(stack_heads(dc_ref[rows, cols], low, high), v_ref[keys, cols])

        def differ(index, d_probs):
            wide = kept_ref[units[index][3]].astype(F32)
            weighted = wide * d_probs
            return (weighted - wide * jnp.sum(weighted, axis=-1, keepdims=True)).astype(BF16)

        def gather_up(index, d_scores):
            rows, keys, cols, place = units[index]
            d_queries = pick_heads(product(d_scores, k_ref[keys, cols])) * 0.125
            dq_ref[rows, cols] = d_queries.astype(BF16)
            d_keys = left_product(d_scores, stack_heads(q_ref[rows, cols], low, high))
            d_values = left_product(kept_ref[place], stack_heads(dc_ref[rows, cols], low, high))
            if index % parts:
                d_keys += sums["keys"]
                d_values += sums["values"]
            if index % parts == parts - 1:
                dk_ref[keys, cols] = d_keys.astype(BF16)
                dv_ref[keys, cols] = d_values.astype(BF16)
            else:
                sums.update(keys=d_keys, values=d_values)

        pipelined(len(units), spread_in, differ, gather_up)

    @pl.when(tile < short_tiles)
    def _():
        units = []
        for seq in range(per_tile):
            rows = slice(seq * width, (seq + 1) * width)
            for pair in range(PAIRS):
                cols = slice(pair * BLK, (pair + 1) * BLK)
                units.append((rows, rows, cols, (0, pair, seq)))
        go_back(units, short_ref, 1)

    @pl.when(tile >= short_tiles)
    def _():
        half = TILE // 2
        units = []
        for pair in range(PAIRS):
            cols = slice(pair * BLK, (pair + 1) * BLK)
            for part in range(2):
                rows = slice(part * half, (part + 1) * half)
                units.append((rows, slice(0, TILE), cols, (0, pair, part)))
        go_back(units, long_ref, 2)

    wide = PAIRS * BLK
    start = pl.multiple_of(group * wide, wide)

    @pl.when((tile == 0) & (group == 0))
    def _():
        bq_ref[...] = jnp.zeros_like(bq_ref)
        bv_ref[...] = jnp.zeros_like(bv_ref)

    bq_ref[:, pl.ds(start, wide)] += jnp.sum(dq_ref[...].astype(F32), axis=0, keepdims=True)
    bv_ref[:, pl.ds(start, wide)] += jnp.sum(dv_ref[...].astype(F32), axis=0, keepdims=True)

    if transfers:

        @pl.when((tile == pl.num_programs(0) - 1) & (group == GROUPS - 1))
        def _():
            reduce.finish()


def attention_back(qkv, probs_short, probs_long, d_context, short_tiles, terms=None, count=0):
    tiles = d_context.shape[0] // TILE
    wide = PAIRS * BLK
    short_map, long_map = probs_maps(short_tiles)
    rows = pl.BlockSpec((TILE, wide), lambda tile, group: (tile, group))
    row = pl.BlockSpec((1, D), lambda tile, group: (0, 0))
    flops = 10 * D * TILE * TILE * tiles
    in_specs = [
        rows,
        rows,
        rows,
        pl.BlockSpec((1, PAIRS) + probs_short.shape[2:], short_map),
        pl.BlockSpec((1, PAIRS) + probs_long.shape[2:], long_map),
        rows,
    ]
    out_specs = [rows, rows, rows, row, row]
    out_shape = [
        jax.ShapeDtypeStruct((tiles * TILE, D), BF16),
        jax.ShapeDtypeStruct((tiles * TILE, D), BF16),
        jax.ShapeDtypeStruct((tiles * TILE, D), BF16),
        jax.ShapeDtypeStruct((1, D), F32),
        jax.ShapeDtypeStruct((1, D), F32),
    ]
    arguments = [*qkv, probs_short, probs_long, d_context]
    scratch = []
    params = dict(vmem_limit_bytes=60 * MIB)
    if terms is not None:
        arguments.append(terms)
        in_specs.append(pl.BlockSpec(memory_space=pltpu.HBM))
        out_specs.append(pl.BlockSpec((count, BLK), lambda tile, group: (0, 0)))
        out_shape.append(jax.ShapeDtypeStruct((count, BLK), BF16))
        scratch = reduce_scratch(count)
        params.update(collective_id=2, has_side_effects=True)
    return pl.pallas_call(
        partial(attention_back_kernel, short_tiles=short_tiles, transfers=terms is not None),
        grid=(tiles, GROUPS),
        in_specs=in_specs,
        out_specs=out_specs,
        out_shape=out_shape,
        scratch_shapes=scratch,
        compiler_params=pltpu.CompilerParams(**params),
        cost_estimate=pl.CostEstimate(flops=flops, bytes_accessed=50 * MIB, transcendentals=0),
        name="attention_back",
    )(*arguments)


def input_kernel(dq_ref, dk_ref, dv_ref, resid_ref, w_ref, short_ref, long_ref, *, short_tiles):
    tile = pl.program_id(0)
    total = resid_ref[...]
    for index, ref in enumerate((dq_ref, dk_ref, dv_ref)):
        total += right_product(ref[...], w_ref[:, index * D : (index + 1) * D])

    @pl.when(tile < short_tiles)
    def _():
        short_ref[...] = total

    @pl.when(tile >= short_tiles)
    def _():
        long_ref[...] = total


def input_grads(d_qkv, resid, w_qkv, short_tiles):
    tiles = resid.shape[0] // TILE
    rows = pl.BlockSpec((TILE, D), lambda tile: (tile, 0))
    return pl.pallas_call(
        partial(input_kernel, short_tiles=short_tiles),
        grid=(tiles,),
        in_specs=[
            rows,
            rows,
            rows,
            rows,
            pl.BlockSpec((D, 3 * D), lambda tile: (0, 0), pipeline_mode=pl.Buffered(1)),
        ],
        out_specs=[
            pl.BlockSpec((TILE, D), lambda tile: (short_index(tile, short_tiles), 0)),
            pl.BlockSpec((TILE, D), lambda tile: (long_index(tile, short_tiles), 0)),
        ],
        out_shape=[
            jax.ShapeDtypeStruct((short_tiles * TILE, D), F32),
            jax.ShapeDtypeStruct(((tiles - short_tiles) * TILE, D), F32),
        ],
        compiler_params=pltpu.CompilerParams(vmem_limit_bytes=60 * MIB),
        cost_estimate=pl.CostEstimate(
            flops=6 * D * D * TILE * tiles, bytes_accessed=25 * MIB, transcendentals=0
        ),
        name="input_grads",
    )(*d_qkv, resid, w_qkv)


def normal_parts(values):
    below = 0.5 * lax.erf(values * 0.7071067811865476) + 0.5
    return below, jnp.exp(-0.5 * values * values) * 0.3989422804014327


B_OUT, GAIN_ONE, SHIFT_ONE, B_UP, B_DOWN, GAIN_TWO, SHIFT_TWO, B_STUDENT, POOL_QUERY, B_HIDDEN = range(10)
VECTORS = (
    (12, 6),
    (18, 6),
    (24, 6),
    (30, 24),
    (54, 6),
    (60, 6),
    (66, 6),
    (72, 1),
    (73, 1),
    (74, 1),
)
CLASS_ROW = 75
LAST_ROW = 91
SMALL_ROWS = 96


def norm_parts(values):
    center = values - jnp.mean(values, axis=-1, keepdims=True)
    spread = jnp.mean(center * center, axis=-1, keepdims=True)
    inverse = lax.rsqrt(spread + NORM_EPSILON)
    return center * inverse, inverse


def norm_back(d_values, gain, unit, inverse):
    d_unit = d_values * gain
    return inverse * (
        d_unit
        - jnp.mean(d_unit, axis=-1, keepdims=True)
        - unit * jnp.mean(d_unit * unit, axis=-1, keepdims=True)
    )


def column_sum(values):
    return jnp.sum(values.astype(F32), axis=0, keepdims=True)


def pool_weights(student, query, length):
    scaled = student * query
    lane = lax.broadcasted_iota(jnp.int32, scaled.shape, 1)
    place = lax.broadcasted_iota(jnp.int32, (scaled.shape[0], 1), 0)
    weights = []
    for side in (lane < SD // PH, lane >= SD // PH):
        scores = jnp.sum(jnp.where(side, scaled, 0.0), axis=-1, keepdims=True)
        scores = jnp.where(place < length, scores, MASKED_SCORE)
        powers = jnp.exp(scores - jnp.max(scores, axis=0, keepdims=True))
        weights.append(powers / jnp.sum(powers, axis=0, keepdims=True))
    return jnp.where(lane < SD // PH, weights[0], weights[1]), weights


def student_back(student, query, weights, both, d_pooled):
    lane = lax.broadcasted_iota(jnp.int32, student.shape, 1)
    moved = student * d_pooled
    d_scores = []
    for side, weight in zip((lane < SD // PH, lane >= SD // PH), weights):
        d_weight = jnp.sum(jnp.where(side, moved, 0.0), axis=-1, keepdims=True)
        d_scores.append(weight * (d_weight - jnp.sum(weight * d_weight, axis=0, keepdims=True)))
    d_score = jnp.where(lane < SD // PH, d_scores[0], d_scores[1])
    d_query = jnp.sum(d_score * student, axis=0, keepdims=True) * 0.125
    return both * d_pooled + d_score * query, d_query


def feed_kernel(
    len_short,
    len_long,
    slot_ref,
    x_ref,
    context_ref,
    cot_short_ref,
    cot_long_ref,
    logit_cot_ref,
    params,
    w_class,
    b_class,
    blocks,
    enc_short_ref,
    enc_long_ref,
    logit_ref,
    first_ref,
    active_ref,
    d_up_ref,
    d_down_ref,
    d_branch_ref,
    d_context_ref,
    d_resid_ref,
    g_student,
    g_hidden,
    g_small,
    slope,
    pooled_ref,
    d_student_ref,
    w_out,
    w_up,
    w_down,
    w_student,
    w_hidden,
    vectors,
    totals,
    g_class,
    g_last,
    sems,
    *,
    short_tiles,
    width,
):
    tile = pl.program_id(0)
    per_tile = TILE // width
    loads = ((w_out, 108, 6, 6), (w_up, 144, 6, 24), (w_down, 288, 24, 6), (w_student, 432, 6, 1), (w_hidden, 438, 1, 1))

    def arrive(*indices):
        @pl.when(tile == 0)
        def _():
            for index in indices:
                wait_whole(loads[index][0], sems.at[index])

    @pl.when(tile == 0)
    def _():
        for index, (target, block, row_count, col_count) in enumerate(loads):
            load_blocks(slot_ref, blocks, target, sems.at[index], block, row_count, col_count)
        for index, (start, count) in enumerate(VECTORS):
            for place in range(count):
                vectors[index : index + 1, place * BLK : (place + 1) * BLK] = params[
                    start + place : start + place + 1, :
                ]
        for ref in (totals, g_class, g_last, g_student, g_hidden):
            ref[...] = jnp.zeros_like(ref)

    def vector(index):
        return vectors[index : index + 1, : VECTORS[index][1] * BLK]

    def add_total(index, values):
        totals[index : index + 1, : VECTORS[index][1] * BLK] += column_sum(values)

    arrive(0)
    branch = product(context_ref[...], w_out[...]) + vector(B_OUT)
    unit_one, inverse_one = norm_parts(x_ref[...].astype(F32) + branch)
    first = (unit_one * vector(GAIN_ONE) + vector(SHIFT_ONE)).astype(BF16)
    first_ref[...] = first
    arrive(1)
    chunks = [slice(start, start + CHUNK) for start in range(0, FF, CHUNK)]

    def rise(index):
        return product(first, w_up[:, chunks[index]])

    def bend(index, upward):
        upward = upward + vectors[B_UP : B_UP + 1, chunks[index]]
        below, density = normal_parts(upward)
        active_ref[:, chunks[index]] = (upward * below).astype(BF16)
        slope[:, chunks[index]] = (below + upward * density).astype(BF16)

    pipelined(len(chunks), rise, bend, lambda *_: None)
    arrive(2, 3, 4)
    downward = product(active_ref[...], w_down[...]) + vector(B_DOWN)
    unit_two, inverse_two = norm_parts(first.astype(F32) + downward)
    encoded = (unit_two * vector(GAIN_TWO) + vector(SHIFT_TWO)).astype(BF16)

    @pl.when(tile < short_tiles)
    def _():
        enc_short_ref[...] = encoded

    @pl.when(tile >= short_tiles)
    def _():
        enc_long_ref[...] = encoded

    student = product(encoded, w_student[...]) + vector(B_STUDENT)
    query = vector(POOL_QUERY) * 0.125
    pooled_ref[...] = jnp.zeros_like(pooled_ref)

    def head():
        pooled = pooled_ref[...]
        wide_hidden = w_hidden[...].astype(F32)
        hidden = jnp.tanh(product(pooled, wide_hidden, HIGHEST_PRECISION) + vector(B_HIDDEN))
        logit_ref[0] = product(hidden, w_class[...], HIGHEST_PRECISION) + b_class[...]
        d_logits = logit_cot_ref[0]
        g_last[...] += column_sum(d_logits)
        g_class[...] += left_product(d_logits, hidden, HIGHEST_PRECISION)
        d_hidden = right_product(d_logits, w_class[...], HIGHEST_PRECISION)
        d_hidden = d_hidden * (1.0 - hidden * hidden)
        add_total(B_HIDDEN, d_hidden)
        g_hidden[...] += left_product(pooled, d_hidden, HIGHEST_PRECISION)
        return right_product(d_hidden, wide_hidden, HIGHEST_PRECISION)

    def pool(starts, size, lengths):
        kept = []
        for index, (start, length) in enumerate(zip(starts, lengths)):
            rows = student[start : start + size]
            both, weights = pool_weights(rows, query, length)
            pooled_ref[index : index + 1, :] = column_sum(both * rows)
            kept.append((start, rows, both, weights))
        d_pooled = head()
        for index, (start, rows, both, weights) in enumerate(kept):
            d_rows, d_query = student_back(rows, query, weights, both, d_pooled[index : index + 1])
            d_student_ref[start : start + size, :] = d_rows.astype(BF16)
            add_total(POOL_QUERY, d_query)

    @pl.when(tile < short_tiles)
    def _():
        pool(
            [seq * width for seq in range(per_tile)],
            width,
            [len_short[tile * per_tile + seq] for seq in range(per_tile)],
        )

    @pl.when(tile >= short_tiles)
    def _():
        pool([0], TILE, [len_long[tile - short_tiles]])

    d_student = d_student_ref[...]
    add_total(B_STUDENT, d_student)
    g_student[...] += left_product(encoded, d_student)
    cotangent = jnp.where(tile < short_tiles, cot_short_ref[...], cot_long_ref[...])
    d_second = cotangent.astype(F32) + right_product(d_student, w_student[...])
    add_total(GAIN_TWO, d_second * unit_two)
    add_total(SHIFT_TWO, d_second)
    d_resid_two = norm_back(d_second, vector(GAIN_TWO), unit_two, inverse_two)
    d_down = d_resid_two.astype(BF16)
    d_down_ref[...] = d_down
    add_total(B_DOWN, d_down)

    def fall(index):
        return right_product(d_down, w_down[chunks[index], :])

    def bend_back(index, d_active):
        d_up = (d_active * slope[:, chunks[index]].astype(F32)).astype(BF16)
        d_up_ref[:, chunks[index]] = d_up
        totals[B_UP : B_UP + 1, chunks[index]] += column_sum(d_up)

    pipelined(len(chunks), fall, bend_back, lambda *_: None)
    d_first = d_resid_two + right_product(d_up_ref[...], w_up[...])
    add_total(GAIN_ONE, d_first * unit_one)
    add_total(SHIFT_ONE, d_first)
    d_resid_one = norm_back(d_first, vector(GAIN_ONE), unit_one, inverse_one)
    d_resid_ref[...] = d_resid_one
    d_branch = d_resid_one.astype(BF16)
    d_branch_ref[...] = d_branch
    add_total(B_OUT, d_branch)
    d_context_ref[...] = right_product(d_branch, w_out[...]).astype(BF16)

    @pl.when(tile == pl.num_programs(0) - 1)
    def _():
        g_small[...] = jnp.zeros_like(g_small)
        for index, (start, count) in enumerate(VECTORS):
            for place in range(count):
                g_small[start + place : start + place + 1, :] = totals[
                    index : index + 1, place * BLK : (place + 1) * BLK
                ]
        g_small[CLASS_ROW : CLASS_ROW + NCLS, :] = g_class[:NCLS, :]
        g_small[LAST_ROW : LAST_ROW + 1, :] = g_last[...]


def feed(
    len_short, len_long, block_slot, x, context, cot_short, cot_long, logit_cot, small, blocks, short_tiles, width
):
    tiles = x.shape[0] // TILE
    long_tiles = tiles - short_tiles

    def whole(shape):
        return pl.BlockSpec(shape, lambda tile, *_: (0,) * len(shape), pipeline_mode=pl.Buffered(1))

    def kept(shape):
        return pl.BlockSpec(shape, lambda tile, *_: (0,) * len(shape))

    def rows(columns):
        return pl.BlockSpec((TILE, columns), lambda tile, *_: (tile, 0))

    short_rows = pl.BlockSpec((TILE, D), lambda tile, *_: (short_index(tile, short_tiles), 0))
    long_rows = pl.BlockSpec((TILE, D), lambda tile, *_: (long_index(tile, short_tiles), 0))
    logit_rows = pl.BlockSpec((1, 8, SD), lambda tile, *_: (tile, 0, 0))
    grad_shapes = ((D, SD), (SD, SD), (SMALL_ROWS, BLK))
    total = tiles * TILE
    return pl.pallas_call(
        partial(feed_kernel, short_tiles=short_tiles, width=width),
        grid_spec=pltpu.PrefetchScalarGridSpec(
            num_scalar_prefetch=3,
            grid=(tiles,),
            in_specs=[rows(D), rows(D), short_rows, long_rows, logit_rows]
            + [whole(array.shape) for array in small]
            + [pl.BlockSpec(memory_space=pltpu.HBM)],
            out_specs=[
                short_rows,
                long_rows,
                logit_rows,
                rows(D),
                rows(FF),
                rows(FF),
                rows(D),
                rows(D),
                rows(D),
                rows(D),
            ]
            + [kept(shape) for shape in grad_shapes],
            scratch_shapes=[
                pltpu.VMEM((TILE, FF), BF16),
                pltpu.VMEM((8, SD), F32),
                pltpu.VMEM((TILE, SD), BF16),
                pltpu.VMEM((D, D), BF16),
                pltpu.VMEM((D, FF), BF16),
                pltpu.VMEM((FF, D), BF16),
                pltpu.VMEM((D, SD), BF16),
                pltpu.VMEM((SD, SD), BF16),
                pltpu.VMEM((16, FF), F32),
                pltpu.VMEM((16, FF), F32),
                pltpu.VMEM((SD, SD), F32),
                pltpu.VMEM((1, SD), F32),
                pltpu.SemaphoreType.DMA((5,)),
            ],
        ),
        out_shape=[
            jax.ShapeDtypeStruct((short_tiles * TILE, D), BF16),
            jax.ShapeDtypeStruct((long_tiles * TILE, D), BF16),
            jax.ShapeDtypeStruct((tiles, 8, SD), F32),
            jax.ShapeDtypeStruct((total, D), BF16),
            jax.ShapeDtypeStruct((total, FF), BF16),
            jax.ShapeDtypeStruct((total, FF), BF16),
            jax.ShapeDtypeStruct((total, D), BF16),
            jax.ShapeDtypeStruct((total, D), BF16),
            jax.ShapeDtypeStruct((total, D), BF16),
            jax.ShapeDtypeStruct((total, D), F32),
        ]
        + [jax.ShapeDtypeStruct(shape, F32) for shape in grad_shapes],
        compiler_params=pltpu.CompilerParams(vmem_limit_bytes=62 * MIB),
        cost_estimate=pl.CostEstimate(
            flops=total * (8 * D * FF + 4 * D * D), bytes_accessed=70 * MIB, transcendentals=total * FF
        ),
        name="feed",
    )(len_short, len_long, block_slot, x, context, cot_short, cot_long, logit_cot, *small, blocks)


class Place:
    def __init__(self):
        self.quarter = lax.axis_index("dp")
        self.shard = lax.axis_index("fsdp")
        x = self.quarter % 2
        y = self.quarter // 2
        self.core = self.shard % 2
        self.z = self.shard // 2
        self.high = self.z // 2
        self.by_x = 2 * y + 1 - x
        self.by_y = 2 * (1 - y) + x
        self.across = 2 * (1 - y) + 1 - x
        self.sibling = (self.quarter, 2 * self.z + 1 - self.core)
        self.next_x = (self.by_x, self.shard)
        self.next_y = (self.by_y, self.shard)
        self.inner = (self.z > 0) & (self.z < 3)

    def at_z(self, z):
        return (self.quarter, 2 * z + self.core)


def transfer(source, target, send_sem, recv_sem, device):
    return pltpu.make_async_remote_copy(
        src_ref=source,
        dst_ref=target,
        send_sem=send_sem,
        recv_sem=recv_sem,
        device_id=device,
        device_id_type=pl.DeviceIdType.MESH,
    )


def greet(place, extra=()):
    barrier = pltpu.get_barrier_semaphore()

    def signal(device):
        pl.semaphore_signal(barrier, inc=1, device_id=device, device_id_type=pl.DeviceIdType.MESH)

    near = (place.sibling, place.next_x, place.next_y) + tuple(extra)
    for device in near:
        signal(device)

    @pl.when(place.z > 0)
    def _():
        signal(place.at_z(place.z - 1))

    @pl.when(place.z < 3)
    def _():
        signal(place.at_z(place.z + 1))

    pl.semaphore_wait(barrier, len(near) + 1 + (place.z + 1) // 2 % 2)


GATHER_SEMAPHORES = [
    pltpu.SemaphoreType.DMA((2,)),
    pltpu.SemaphoreType.DMA((3,)),
    pltpu.SemaphoreType.DMA((4,)),
    pltpu.SemaphoreType.DMA((12,)),
    pltpu.SemaphoreType.DMA((12,)),
    pltpu.SemaphoreType.DMA((16,)),
    pltpu.SemaphoreType.DMA((16,)),
    pltpu.SemaphoreType.DMA((8,)),
]


class Gather:
    def __init__(self, full, out, sems):
        self.place = place = Place()
        self.full, self.out = full, out
        (
            self.own_send,
            self.relay_send,
            self.z_recv,
            self.xy_send,
            self.xy_recv,
            self.core_send,
            self.core_recv,
            self.out_sems,
        ) = sems
        self.quarter = full.shape[1] // 4
        self.half = self.quarter // 2
        z = place.z
        self.origins = (z + 1 - 2 * (z % 2), 2 - place.high, 3 * (1 - place.high))
        self.relays = (3 - z, 3 * (z - 1), 3 * (z - 1))

    def region(self, which, start, size):
        return self.full.at[which, pl.ds(pl.multiple_of(start, 16), size)]

    def pieces(self, which):
        place, quarter, half = self.place, self.quarter, self.half
        return (
            self.region(which, place.quarter * quarter, quarter),
            self.region(which, place.by_x * quarter, quarter),
            self.region(which, place.by_y * quarter, quarter),
            self.region(which, place.across * quarter, half),
            self.region(which, place.across * quarter + half, half),
        )

    def mine(self):
        return self.region(self.place.shard, self.place.quarter * self.quarter, self.quarter)

    def own_copy(self, side):
        place = self.place
        mine = self.mine()
        device = place.at_z(place.z - 1 + 2 * side)
        return transfer(mine, mine, self.own_send.at[side], self.z_recv.at[place.z], device)

    def core_copy(self, index, ref):
        return transfer(ref, ref, self.core_send.at[index], self.core_recv.at[index], self.place.sibling)

    def xy_copy(self, index, ref, device):
        return transfer(ref, ref, self.xy_send.at[index], self.xy_recv.at[index], device)

    def store(self, index, which):
        return pltpu.make_async_copy(self.full.at[which], self.out.at[which], self.out_sems.at[index])

    def mirrored(self, step):
        return 2 * self.origins[step] + 1 - self.place.core

    def held(self, step):
        return 2 * self.origins[step] + self.place.core

    def start(self):
        place = self.place
        greet(place)

        @pl.when(place.z > 0)
        def _():
            self.own_copy(0).start()

        @pl.when(place.z < 3)
        def _():
            self.own_copy(1).start()

        self.core_copy(0, self.full.at[place.shard]).start()
        self.store(0, place.shard).start()

    def relay(self, step):
        piece = self.pieces(self.held(step))[0]
        device = self.place.at_z(self.relays[step])
        return transfer(
            piece, piece, self.relay_send.at[step], self.z_recv.at[self.origins[step]], device
        )

    def along_z(self, step):
        place = self.place
        self.relay(step).wait_recv()

        @pl.when(place.inner)
        def _():
            self.relay(step).start()

        piece = self.pieces(self.held(step))[0]
        self.xy_copy(4 * step, piece, place.next_x).start()
        self.xy_copy(4 * step + 1, piece, place.next_y).start()
        self.core_copy(1 + 5 * step, piece).start()

    def along_xy(self, step):
        place, half = self.place, self.half
        _, by_x, by_y, _, _ = self.pieces(self.held(step))
        self.xy_copy(4 * step, by_x, place.next_x).wait_recv()
        self.xy_copy(4 * step + 2, by_x.at[pl.ds(0, half)], place.next_y).start()
        self.core_copy(2 + 5 * step, by_x).start()
        self.xy_copy(4 * step + 1, by_y, place.next_y).wait_recv()
        self.xy_copy(4 * step + 3, by_y.at[pl.ds(half, half)], place.next_x).start()
        self.core_copy(3 + 5 * step, by_y).start()

    def across(self, step):
        place = self.place
        _, _, _, first, last = self.pieces(self.held(step))
        self.xy_copy(4 * step + 2, first, place.next_y).wait_recv()
        self.core_copy(4 + 5 * step, first).start()
        self.xy_copy(4 * step + 3, last, place.next_x).wait_recv()
        self.core_copy(5 + 5 * step, last).start()
        self.store(2 + 2 * step, self.held(step)).start()

    def core_own(self):
        which = 2 * self.place.z + 1 - self.place.core
        self.core_copy(0, self.full.at[which]).wait_recv()
        self.store(1, which).start()

    def core(self, step):
        which = self.mirrored(step)
        for index, ref in enumerate(self.pieces(which)):
            self.core_copy(1 + 5 * step + index, ref).wait_recv()
        self.store(3 + 2 * step, which).start()

    def finish(self):
        place = self.place

        @pl.when(place.z > 0)
        def _():
            self.own_copy(0).wait_send()

        @pl.when(place.z < 3)
        def _():
            self.own_copy(1).wait_send()

        self.core_copy(0, self.full.at[place.shard]).wait_send()
        self.store(0, place.shard).wait()
        self.store(1, 2 * place.z + 1 - place.core).wait()
        for step in range(3):

            @pl.when(place.inner)
            def _():
                self.relay(step).wait_send()

            pieces = self.pieces(self.held(step))
            self.xy_copy(4 * step, pieces[0], place.next_x).wait_send()
            self.xy_copy(4 * step + 1, pieces[0], place.next_y).wait_send()
            self.xy_copy(4 * step + 2, pieces[3], place.next_y).wait_send()
            self.xy_copy(4 * step + 3, pieces[4], place.next_x).wait_send()
            for index, ref in enumerate(pieces):
                self.core_copy(1 + 5 * step + index, ref).wait_send()
            self.store(2 + 2 * step, self.held(step)).wait()
            self.store(3 + 2 * step, self.mirrored(step)).wait()


def gather_kernel(master_ref, out_ref, full, *sems):
    gather = Gather(full, out_ref, sems)
    full[gather.place.shard] = master_ref[...].astype(BF16)
    gather.start()
    gather.along_z(0)
    gather.along_z(1)
    gather.along_xy(0)
    gather.along_z(2)
    gather.along_xy(1)
    gather.across(0)
    gather.core_own()
    gather.along_xy(2)
    gather.across(1)
    gather.core(0)
    gather.across(2)
    gather.core(1)
    gather.core(2)
    gather.finish()


def gather_shards(master):
    rows = master.shape[0] * BLK
    shards = lax.axis_size("fsdp")
    return pl.pallas_call(
        gather_kernel,
        in_specs=[pl.BlockSpec(memory_space=pltpu.VMEM)],
        out_specs=pl.BlockSpec(memory_space=pltpu.HBM),
        out_shape=jax.ShapeDtypeStruct((shards, rows, BLK), BF16),
        scratch_shapes=[pltpu.VMEM((shards, rows, BLK), BF16)] + GATHER_SEMAPHORES,
        compiler_params=pltpu.CompilerParams(
            collective_id=0, has_side_effects=True, vmem_limit_bytes=60 * MIB
        ),
        cost_estimate=pl.CostEstimate(flops=0, bytes_accessed=200 * MIB, transcendentals=0),
        name="gather",
    )(master.reshape(rows, BLK)).reshape(-1, BLK, BLK)


def add_rows(target, former, latter, rows, step):
    @pl.loop(0, rows // step)
    def _(index):
        part = pl.ds(pl.multiple_of(index * step, 16), step)
        target[part] = (former[part].astype(F32) + latter[part].astype(F32)).astype(BF16)


def reduce_scratch(rows):
    quarter = rows // 4
    half = quarter // 2
    return [
        pltpu.VMEM((4, rows, BLK), BF16),
        pltpu.VMEM((4, rows, BLK), BF16),
        pltpu.VMEM((4, 2, half, BLK), BF16),
        pltpu.VMEM((4, 2, half, BLK), BF16),
        pltpu.VMEM((4, half, BLK), BF16),
        pltpu.VMEM((4, half, BLK), BF16),
        pltpu.VMEM((5, quarter, BLK), BF16),
        pltpu.VMEM((rows, BLK), BF16),
        pltpu.SemaphoreType.DMA((4,)),
        pltpu.SemaphoreType.DMA((4,)),
        pltpu.SemaphoreType.DMA((4,)),
        pltpu.SemaphoreType.DMA((24,)),
        pltpu.SemaphoreType.DMA((24,)),
        pltpu.SemaphoreType.DMA((3,)),
        pltpu.SemaphoreType.DMA((5,)),
        pltpu.SemaphoreType.DMA((4,)),
        pltpu.SemaphoreType.DMA((4,)),
    ]


class Reduce:
    def __init__(self, terms, base, out, scratch):
        self.place = place = Place()
        self.terms, self.base, self.out = terms, base, out
        (
            self.mine,
            self.sib,
            self.from_x,
            self.from_y,
            self.late_y,
            self.late_x,
            self.from_z,
            self.result,
            self.load_sems,
            self.core_send,
            self.core_recv,
            self.xy_send,
            self.xy_recv,
            self.z_send,
            self.z_recv,
            self.last_send,
            self.last_recv,
        ) = scratch
        self.quarter = out.shape[0] // 4
        self.half = self.quarter // 2
        z, high = place.z, place.high
        low = 1 - high
        self.order = (3 * low, low * (2 - 2 * z) + high * (7 - 2 * z), 1 + z % 2, z)
        self.onward = (z + 1 - 2 * high, z + 1 - 2 * (z % 2), z + 1 - 2 * high)
        self.closing = (0, (z % 2) * low, high)
        self.far = place.at_z(z + 2 - 4 * high)
        self.near = place.at_z(z + 1 - 2 * (z % 2))

    def shard_terms(self, shard):
        rows = self.out.shape[0]
        return self.terms.at[pl.ds(pl.multiple_of(self.base + shard * rows, 16), rows)]

    def load(self, step):
        source = self.shard_terms(2 * self.order[step] + self.place.core)
        return pltpu.make_async_copy(source, self.mine.at[step], self.load_sems.at[step])

    def core_copy(self, step):
        return transfer(
            self.shard_terms(2 * self.order[step] + 1 - self.place.core),
            self.sib.at[step],
            self.core_send.at[step],
            self.core_recv.at[step],
            self.place.sibling,
        )

    def part(self, step, which, side):
        start = pl.multiple_of(which * self.quarter + side * self.half, 16)
        return self.mine.at[step, pl.ds(start, self.half)]

    def xy_copy(self, step, index):
        place = self.place
        source, target, device = (
            (self.part(step, place.by_x, 0), self.from_x.at[step, 0], place.next_x),
            (self.part(step, place.across, 0), self.from_x.at[step, 1], place.next_x),
            (self.part(step, place.by_y, 1), self.from_y.at[step, 0], place.next_y),
            (self.part(step, place.across, 1), self.from_y.at[step, 1], place.next_y),
            (self.part(step, place.by_y, 0), self.late_y.at[step], place.next_y),
            (self.part(step, place.by_x, 1), self.late_x.at[step], place.next_x),
        )[index]
        place = 6 * step + index
        return transfer(source, target, self.xy_send.at[place], self.xy_recv.at[place], device)

    def start(self):
        greet(self.place, (self.far,))
        for step in range(2):
            self.core_copy(step).start()
        for step in range(4):
            self.load(step).start()

    def core(self, step):
        place, quarter = self.place, self.quarter
        self.load(step).wait()
        self.core_copy(step).wait_recv()
        if step < 2:
            self.core_copy(step + 2).start()

        def add(which):
            block = pl.ds(pl.multiple_of(which * quarter, 16), quarter)
            mine = self.mine.at[step, block]
            add_rows(mine, mine, self.sib.at[step, block], quarter, self.half)

        add(place.by_x)
        add(place.across)
        self.xy_copy(step, 0).start()
        self.xy_copy(step, 1).start()
        add(place.by_y)
        self.xy_copy(step, 2).start()
        self.xy_copy(step, 3).start()
        add(place.quarter)

    def take(self, step, which, side, index, source):
        self.xy_copy(step, index).wait_recv()
        target = self.part(step, which, side)
        add_rows(target, target, source, self.half, self.half)

    def first(self, step):
        place = self.place
        self.take(step, place.by_y, 0, 1, self.from_x.at[step, 1])
        self.xy_copy(step, 4).start()
        self.take(step, place.by_x, 1, 3, self.from_y.at[step, 1])
        self.xy_copy(step, 5).start()
        self.take(step, place.quarter, 0, 0, self.from_x.at[step, 0])
        self.take(step, place.quarter, 1, 2, self.from_y.at[step, 0])

    def own_block(self, step):
        return self.mine.at[step, pl.ds(pl.multiple_of(self.place.quarter * self.quarter, 16), self.quarter)]

    def z_copy(self, step):
        goal = self.order[step]
        slot = goal + self.closing[step] * (4 - goal)
        return transfer(
            self.own_block(step),
            self.from_z.at[slot],
            self.z_send.at[step],
            self.z_recv.at[slot],
            self.place.at_z(self.onward[step]),
        )

    def take_z(self, step, slot):
        source = self.from_z.at[slot]
        transfer(source, source, self.z_send.at[0], self.z_recv.at[slot], self.near).wait_recv()
        block = self.own_block(step)
        add_rows(block, block, source, self.quarter, self.half)

    def second(self, step):
        place = self.place
        self.take(step, place.quarter, 0, 4, self.late_y.at[step])
        self.take(step, place.quarter, 1, 5, self.late_x.at[step])
        if step < 3:

            @pl.when(place.inner)
            def _():
                self.take_z(step, self.order[step])

            self.z_copy(step).start()
        else:

            @pl.when(place.z > 0)
            def _():
                self.take_z(step, place.z)

            @pl.when(place.z < 3)
            def _():
                self.take_z(step, 4)

    def final(self, which, side=None):
        start = pl.multiple_of(which * self.quarter + (0 if side is None else side * self.half), 16)
        return self.result.at[pl.ds(start, self.quarter if side is None else self.half)]

    def last_copy(self, index, ref):
        device = (self.place.next_x, self.place.next_y, self.place.next_y, self.place.next_x)[index]
        return transfer(ref, ref, self.last_send.at[index], self.last_recv.at[index], device)

    def share(self):
        own = self.final(self.place.quarter)
        own[...] = self.own_block(3)[...]
        self.last_copy(0, own).start()
        self.last_copy(1, own).start()

    def share_on(self):
        place = self.place
        self.last_copy(0, self.final(place.by_x)).wait_recv()
        self.last_copy(2, self.final(place.by_x, 0)).start()
        self.last_copy(1, self.final(place.by_y)).wait_recv()
        self.last_copy(3, self.final(place.by_y, 1)).start()

    def finish(self):
        place = self.place
        self.last_copy(2, self.final(place.across, 0)).wait_recv()
        self.last_copy(3, self.final(place.across, 1)).wait_recv()
        self.out[...] = self.result[...]
        for step in range(4):
            self.core_copy(step).wait_send()
            for index in range(6):
                self.xy_copy(step, index).wait_send()
            if step < 3:
                self.z_copy(step).wait_send()
        own = self.final(place.quarter)
        self.last_copy(0, own).wait_send()
        self.last_copy(1, own).wait_send()
        self.last_copy(2, self.final(place.by_x, 0)).wait_send()
        self.last_copy(3, self.final(place.by_y, 1)).wait_send()


def reduce_kernel(
    terms, small_ref, out_ref, small_out, small_in, small_sum, small_send, small_recv, *scratch, base
):
    reduce = Reduce(terms, base, out_ref, scratch)
    place = reduce.place
    partners = (place.sibling, place.next_x, place.next_y, reduce.near, reduce.far)

    def small_copy(level):
        return transfer(
            small_sum.at[level],
            small_in.at[level],
            small_send.at[level],
            small_recv.at[level],
            partners[level],
        )

    def small_step(level):
        small_copy(level - 1).wait_recv()
        small_sum[level] = small_sum[level - 1] + small_in[level - 1]
        if level < 5:
            small_copy(level).start()

    small_sum[0] = small_ref[...]
    reduce.start()
    small_copy(0).start()
    reduce.core(0)
    small_step(1)
    reduce.core(1)
    reduce.first(0)
    small_step(2)
    reduce.core(2)
    reduce.first(1)
    reduce.second(0)
    small_step(3)
    reduce.core(3)
    reduce.first(2)
    reduce.second(1)
    small_step(4)
    reduce.first(3)
    reduce.second(2)
    small_step(5)
    small_out[...] = small_sum[5]
    reduce.second(3)
    reduce.share()
    reduce.share_on()
    reduce.finish()
    for level in range(5):
        small_copy(level).wait_send()


def reduce_late(terms, base, rows, small):
    vmem = pl.BlockSpec(memory_space=pltpu.VMEM)
    return pl.pallas_call(
        partial(reduce_kernel, base=base),
        in_specs=[pl.BlockSpec(memory_space=pltpu.HBM), vmem],
        out_specs=[vmem, vmem],
        out_shape=[
            jax.ShapeDtypeStruct((rows, BLK), BF16),
            jax.ShapeDtypeStruct((SMALL_ROWS, BLK), F32),
        ],
        scratch_shapes=[
            pltpu.VMEM((5, SMALL_ROWS, BLK), F32),
            pltpu.VMEM((6, SMALL_ROWS, BLK), F32),
            pltpu.SemaphoreType.DMA((5,)),
            pltpu.SemaphoreType.DMA((5,)),
        ]
        + reduce_scratch(rows),
        compiler_params=pltpu.CompilerParams(
            collective_id=3, has_side_effects=True, vmem_limit_bytes=48 * MIB
        ),
        cost_estimate=pl.CostEstimate(flops=0, bytes_accessed=200 * MIB, transcendentals=0),
        name="reduce",
    )(terms, small)


def count_where(condition, axis):
    return jnp.sum(condition.astype(jnp.int32), axis=axis)


def slot_codes(slots, qkv_slots, slot_count, shards):
    early = slot_count - LATE
    shard = slots // slot_count
    begin = shard * slot_count
    inside = (qkv_slots[None, :] >= begin[:, None]) & (qkv_slots[None, :] < (begin + slot_count)[:, None])
    own = count_where(qkv_slots[None, :] == slots[:, None], 1)
    before = count_where(inside & (qkv_slots[None, :] < slots[:, None]), 1)
    number = count_where(inside, 1)
    position = jnp.where(own > 0, slot_count - number + before, slots - begin - before)
    code = jnp.where(
        position < early,
        shard * early + position,
        shards * early + shard * LATE + position - early,
    )
    return code, position, jnp.max(number)


def empty_slots(block_slot, all_slots):
    places = jnp.arange(all_slots, dtype=jnp.int32)
    empty_before = places + 1 - count_where(block_slot[None, :] <= places[:, None], 1)
    empty_index = jnp.arange(all_slots - NBLK, dtype=jnp.int32)
    return count_where(empty_before[None, :] <= empty_index[:, None], 1)


def halves(values):
    high = values.astype(BF16)
    return high, (values - high.astype(F32)).astype(BF16)


def update_kernel(
    position_ref,
    blocks,
    master,
    left_stat,
    right_stat,
    left_root,
    right_root,
    slot_grad,
    new_left,
    new_right,
    new_master,
):
    count = master.shape[0]
    first = pl.program_id(0) * count
    for index in range(count):
        start = pl.multiple_of(position_ref[first + index] * BLK, BLK)
        grad = blocks[pl.ds(start, BLK)]
        slot_grad[index] = grad.astype(F32)
        new_left[index] = STAT_DECAY * left_stat[index] + (1.0 - STAT_DECAY) * right_product(grad, grad)
        new_right[index] = STAT_DECAY * right_stat[index] + (1.0 - STAT_DECAY) * left_product(grad, grad)
        applied = product(jnp.concatenate(halves(left_root[index]), axis=0), grad)
        applied = jnp.concatenate(halves(applied[:BLK] + applied[BLK:]), axis=0)
        root_high, root_low = halves(right_root[index])
        wide = product(applied, root_high)
        total = wide[:BLK] + wide[BLK:] + product(applied[:BLK], root_low)
        new_master[index] = master[index] - MATRIX_RATE * total


def update(position, blocks, master, left_stat, right_stat, left_root, right_root):
    slot_count = master.shape[0]
    group = max(size for size in range(1, 12) if slot_count % size == 0)
    some = pl.BlockSpec((group, BLK, BLK), lambda step, *_: (step, 0, 0))
    return pl.pallas_call(
        update_kernel,
        grid_spec=pltpu.PrefetchScalarGridSpec(
            num_scalar_prefetch=1,
            grid=(slot_count // group,),
            in_specs=[
                pl.BlockSpec(blocks.shape, lambda step, *_: (0, 0), pipeline_mode=pl.Buffered(1))
            ]
            + [some] * 5,
            out_specs=[some] * 4,
        ),
        out_shape=[jax.ShapeDtypeStruct(master.shape, F32)] * 4,
        compiler_params=pltpu.CompilerParams(vmem_limit_bytes=40 * MIB),
        cost_estimate=pl.CostEstimate(
            flops=14 * slot_count * BLK**3, bytes_accessed=36 * slot_count * BLK**2, transcendentals=0
        ),
        name="update",
    )(position, blocks, master, left_stat, right_stat, left_root, right_root)


def body(
    x_short,
    x_long,
    cot_short,
    cot_long,
    logit_cot_short,
    logit_cot_long,
    len_short,
    len_long,
    block_slot,
    master,
    left_stat,
    right_stat,
    left_root,
    right_root,
    small_params,
    small_first,
    small_second,
    own_transfers,
):
    slot_count = master.shape[0]
    shards = lax.axis_size("fsdp")
    all_slots = slot_count * shards
    short_seqs, width = x_short.shape[:2]
    long_seqs = x_long.shape[0]
    short_tiles = short_seqs * width // TILE
    per_tile = TILE // width
    empty = empty_slots(block_slot, all_slots)

    if own_transfers:
        early_count = slot_count - LATE
        own = jnp.arange(slot_count, dtype=jnp.int32) + slot_count * lax.axis_index("fsdp")
        code, position, most = slot_codes(
            jnp.concatenate([block_slot, empty, own]), block_slot[: 3 * 36], slot_count, shards
        )
        position = position[all_slots:]
        empty_code = code[NBLK:all_slots]
        code = code[:NBLK]
        fits = most <= LATE
        gathered = gather_shards(master)
    else:
        gathered = lax.all_gather(master.astype(BF16), "fsdp", axis=0, tiled=True)
    w_qkv = assemble(block_slot, gathered)
    pieces = unpack(small_params)
    params = jnp.pad(small_params, (0, SMALL_ROWS * BLK - small_params.shape[0])).reshape(SMALL_ROWS, BLK)
    w_class = jnp.pad(pieces[-2].reshape(SD, NCLS), ((0, 0), (0, SD - NCLS)))
    b_class = jnp.pad(pieces[-1].reshape(1, NCLS), ((0, 0), (0, SD - NCLS)))

    x, *qkv, context, probs_short, probs_long = attention(
        len_short,
        len_long,
        x_short.reshape(-1, D),
        x_long.reshape(-1, D),
        params,
        w_qkv,
        short_tiles,
        width,
    )

    logit_cot = jnp.concatenate(
        [
            jnp.pad(
                logit_cot_short.reshape(short_tiles, per_tile, NCLS),
                ((0, 0), (0, 8 - per_tile), (0, SD - NCLS)),
            ),
            jnp.pad(logit_cot_long.reshape(long_seqs, 1, NCLS), ((0, 0), (0, 7), (0, SD - NCLS))),
        ],
        axis=0,
    )
    (
        enc_short,
        enc_long,
        logits,
        first,
        active,
        d_up,
        d_down,
        d_branch,
        d_context,
        d_resid,
        g_student,
        g_hidden,
        g_small,
    ) = feed(
        len_short,
        len_long,
        block_slot,
        x,
        context,
        cot_short.reshape(-1, D),
        cot_long.reshape(-1, D),
        logit_cot,
        (params, w_class, b_class),
        gathered,
        short_tiles,
        width,
    )
    g_down = left_product(active, d_down).astype(BF16)
    g_up = left_product(first, d_up).astype(BF16)
    g_out = left_product(context, d_branch).astype(BF16)
    others = (g_out, g_up, g_down, g_student.astype(BF16), g_hidden.astype(BF16))
    if own_transfers:
        terms = spread(code, empty_code, others, OTHER_PLACES, all_slots)
        *back, early_reduced = attention_back(
            qkv,
            probs_short,
            probs_long,
            d_context,
            short_tiles,
            terms.reshape(-1, BLK),
            early_count * BLK,
        )
    else:
        back = attention_back(qkv, probs_short, probs_long, d_context, short_tiles)
    *d_qkv, g_b_query, g_b_value = back
    in_short, in_long = input_grads(d_qkv, d_resid, w_qkv, short_tiles)
    qkv_grads = tuple(left_product(x, d_rows).astype(BF16) for d_rows in d_qkv)

    def reduce_all():
        slot_terms = spread(block_slot, empty, qkv_grads + others, QKV_PLACES + OTHER_PLACES, all_slots)
        return lax.psum(lax.psum_scatter(slot_terms, "fsdp", scatter_dimension=0, tiled=True), "dp")

    if own_transfers:
        terms, small_terms = spread_late(code, qkv_grads, g_small, g_b_query, g_b_value, terms)
        late_reduced, small_total = reduce_late(
            terms.reshape(-1, BLK), shards * early_count * BLK, LATE * BLK, small_terms
        )

        blocks = lax.cond(
            fits,
            lambda: jnp.concatenate([early_reduced, late_reduced], axis=0),
            lambda: reduce_all().reshape(-1, BLK),
        )
        position = jnp.where(fits, position, jnp.arange(slot_count, dtype=jnp.int32))
    else:
        blocks = reduce_all().reshape(-1, BLK)
        position = jnp.arange(slot_count, dtype=jnp.int32)
        small_terms = jnp.concatenate(
            [g_b_query.reshape(-1, BLK), g_b_value.reshape(-1, BLK), g_small[2 * D // BLK :]], axis=0
        )
        small_total = lax.psum(small_terms, ("dp", "fsdp"))
    slot_grad, new_left, new_right, new_master = update(
        position, blocks, master, left_stat, right_stat, left_root, right_root
    )
    small_grad = jnp.concatenate(
        [
            small_total[:CLASS_ROW].reshape(-1),
            small_total[CLASS_ROW : CLASS_ROW + NCLS].T.reshape(-1),
            small_total[LAST_ROW, :NCLS],
        ]
    )
    new_first = BETA_ONE * small_first + (1.0 - BETA_ONE) * small_grad
    new_second = BETA_TWO * small_second + (1.0 - BETA_TWO) * small_grad * small_grad
    first_hat = new_first / (1.0 - BETA_ONE**STEP)
    second_hat = new_second / (1.0 - BETA_TWO**STEP)
    new_small = small_params - ADAM_RATE * first_hat / (jnp.sqrt(second_hat) + ADAM_EPSILON)
    return (
        enc_short.reshape(x_short.shape),
        logits[:short_tiles, :per_tile, :NCLS].reshape(short_seqs, NCLS),
        enc_long.reshape(x_long.shape),
        logits[short_tiles:, 0, :NCLS],
        in_short.reshape(x_short.shape),
        in_long.reshape(x_long.shape),
        slot_grad,
        new_left,
        new_right,
        new_master,
        new_first,
        new_second,
        new_small,
    )


def solution(mesh):
    both = ("dp", "fsdp")
    placed = (
        P(both, None, None),
        P(both, None, None),
        P(both, None, None),
        P(both, None, None),
        P(both, None),
        P(both, None),
        P(both),
        P(both),
        P(),
        P("fsdp", None, None),
        P("fsdp", None, None),
        P("fsdp", None, None),
        P("fsdp", None, None),
        P("fsdp", None, None),
        P(),
        P(),
        P(),
    )
    return jax.shard_map(
        partial(body, own_transfers=(mesh.shape["dp"], mesh.shape["fsdp"]) == (4, 8)),
        mesh=mesh,
        in_specs=placed,
        out_specs=(
            P(both, None, None),
            P(both, None),
            P(both, None, None),
            P(both, None),
            P(both, None, None),
            P(both, None, None),
            P("fsdp", None, None),
            P("fsdp", None, None),
            P("fsdp", None, None),
            P("fsdp", None, None),
            P(),
            P(),
            P(),
        ),
        check_vma=False,
    )
```

```python
from functools import partial

import jax
import jax.numpy as jnp
from jax import lax
from jax.experimental import pallas as pl
from jax.experimental.pallas import tpu as pltpu
from jax.sharding import PartitionSpec as P

D = 768
HEADS = 12
FF = 3072
SD = 128
PH = 2
NCLS = 14
BLK = 128
STEP = 10
NBLK = 439
TILE = 512
PAIRS = 3
GROUPS = 2
CHUNK = 768
LATE = 24

NORM_EPSILON = 1e-12
BETA_ONE = 0.9
BETA_TWO = 0.999
ADAM_EPSILON = 1e-08
ADAM_RATE = 0.1
MATRIX_RATE = 0.2
STAT_DECAY = 0.5
MASKED_SCORE = -1e30
HIGHEST_PRECISION = lax.Precision.HIGHEST
MIB = 1024 * 1024
F32 = jnp.float32
BF16 = jnp.bfloat16

def product(former, latter, precision=None):
    return jnp.dot(former, latter, preferred_element_type=F32, precision=precision)


def left_product(former, latter, precision=None):
    return lax.dot_general(
        former, latter, (((0,), (0,)), ((), ())), preferred_element_type=F32, precision=precision
    )


def right_product(former, latter, precision=None):
    return lax.dot_general(
        former, latter, (((1,), (1,)), ((), ())), preferred_element_type=F32, precision=precision
    )


def unpack(small_values):
    widths = (D, D, D, D, D, FF, D, D, D, SD, SD, SD, SD * NCLS, NCLS)
    pieces = []
    offset = 0
    for column_count in widths:
        pieces.append(small_values[offset : offset + column_count])
        offset += column_count
    return pieces


def each_block(first, row_count, col_count, action):
    def one_row(index, carry):
        row = pl.multiple_of(index * BLK, BLK)
        for col in range(col_count):
            action(first + index * col_count + col, row, col * BLK)
        return carry

    lax.fori_loop(0, row_count, one_row, 0)


def load_blocks(slot_ref, blocks, target, sem, first, row_count, col_count, col_start=0):
    def move(block, row, col):
        pltpu.make_async_copy(
            blocks.at[slot_ref[block]],
            target.at[pl.ds(row, BLK), pl.ds(col + col_start * BLK, BLK)],
            sem,
        ).start()

    each_block(first, row_count, col_count, move)


def wait_whole(target, sem):
    pltpu.make_async_copy(target, target, sem).wait()


def assemble_kernel(slot_ref, blocks, out, sem):
    for which in range(3):
        load_blocks(slot_ref, blocks, out, sem, 36 * which, 6, 6, 6 * which)
    wait_whole(out, sem)


def assemble(block_slot, blocks):
    return pl.pallas_call(
        assemble_kernel,
        grid_spec=pltpu.PrefetchScalarGridSpec(
            num_scalar_prefetch=1,
            grid=(1,),
            in_specs=[pl.BlockSpec(memory_space=pltpu.HBM)],
            out_specs=pl.BlockSpec(memory_space=pltpu.VMEM),
            scratch_shapes=[pltpu.SemaphoreType.DMA],
        ),
        out_shape=jax.ShapeDtypeStruct((D, 3 * D), BF16),
        compiler_params=pltpu.CompilerParams(vmem_limit_bytes=60 * MIB),
        name="assemble",
    )(block_slot, blocks)


QKV_PLACES = ((0, 6, 6), (36, 6, 6), (72, 6, 6))
OTHER_PLACES = ((108, 6, 6), (144, 6, 24), (288, 24, 6), (432, 6, 1), (438, 1, 1))


def spread_kernel(code_ref, empty_ref, *refs, places):
    grads = refs[: len(places)]
    zero, out, sems = refs[len(places) :]
    for which, (grad, place) in enumerate(zip(grads, places)):

        def move(block, row, col, which=which, grad=grad):
            pltpu.make_async_copy(
                grad.at[pl.ds(row, BLK), pl.ds(col, BLK)], out.at[code_ref[block]], sems.at[which]
            ).start()

        each_block(*place, move)
    for index in range(empty_ref.shape[0]):
        pltpu.make_async_copy(zero, out.at[empty_ref[index]], sems.at[len(places) + index]).start()
    for which, grad in enumerate(grads):
        wait_whole(grad, sems.at[which])
    for index in range(empty_ref.shape[0]):
        wait_whole(zero, sems.at[len(places) + index])


def spread(code, empty, grads, places, slot_count):
    vmem = pl.BlockSpec(memory_space=pltpu.VMEM)
    return pl.pallas_call(
        partial(spread_kernel, places=places),
        grid_spec=pltpu.PrefetchScalarGridSpec(
            num_scalar_prefetch=2,
            grid=(1,),
            in_specs=[vmem] * (len(grads) + 1),
            out_specs=pl.BlockSpec(memory_space=pltpu.HBM),
            scratch_shapes=[pltpu.SemaphoreType.DMA((len(grads) + empty.shape[0],))],
        ),
        out_shape=jax.ShapeDtypeStruct((slot_count, BLK, BLK), BF16),
        compiler_params=pltpu.CompilerParams(vmem_limit_bytes=44 * MIB),
        name="spread",
    )(code, empty, *grads, jnp.zeros((BLK, BLK), BF16))


def spread_late_kernel(code_ref, grad, small_ref, query_ref, value_ref, _, out, small_out, sem):
    for which, place in enumerate(QKV_PLACES):

        def move(block, row, col, which=which):
            pltpu.make_async_copy(
                grad.at[pl.ds(row, BLK), pl.ds(which * D + col, BLK)], out.at[code_ref[block]], sem
            ).start()

        each_block(*place, move)
    join_small(small_ref, query_ref, value_ref, small_out)
    wait_whole(grad, sem)


def join_small(small_ref, query_ref, value_ref, small_out):
    small_out[...] = small_ref[...]
    for start, ref in ((0, query_ref), (D // BLK, value_ref)):
        for index in range(D // BLK):
            small_out[start + index : start + index + 1, :] = ref[:, index * BLK : (index + 1) * BLK]


def spread_late(code, grad, small, g_query, g_value, terms):
    vmem = pl.BlockSpec(memory_space=pltpu.VMEM)
    anywhere = pl.BlockSpec(memory_space=pltpu.HBM)
    return pl.pallas_call(
        spread_late_kernel,
        grid_spec=pltpu.PrefetchScalarGridSpec(
            num_scalar_prefetch=1,
            grid=(1,),
            in_specs=[vmem] * 4 + [anywhere],
            out_specs=[anywhere, vmem],
            scratch_shapes=[pltpu.SemaphoreType.DMA],
        ),
        out_shape=[
            jax.ShapeDtypeStruct(terms.shape, BF16),
            jax.ShapeDtypeStruct(small.shape, F32),
        ],
        input_output_aliases={5: 0},
        compiler_params=pltpu.CompilerParams(vmem_limit_bytes=44 * MIB),
        name="spread_late",
    )(code, grad, small, g_query, g_value, terms)


def half_masks():
    lane = lax.broadcasted_iota(jnp.int32, (1, BLK), 1)
    low = (lane < BLK // 2).astype(BF16)
    return low, (1.0 - low.astype(F32)).astype(BF16)


def stack_heads(values, low, high):
    return jnp.concatenate([values * low, values * high], axis=0)


def pick_heads(values):
    rows = values.shape[0] // 2
    lane = lax.broadcasted_iota(jnp.int32, (rows, BLK), 1)
    return jnp.where(lane < BLK // 2, values[:rows], values[rows:])


def pipelined(count, before, middle, after):
    started = before(0)
    done = None
    for index in range(count):
        current = started
        if index + 1 < count:
            started = before(index + 1)
        if done is not None:
            after(index - 1, done)
        done = middle(index, current)
    after(count - 1, done)


def softmax(scores, length):
    visible = lax.broadcasted_iota(jnp.int32, scores.shape, 1) < length
    scores = jnp.where(visible, scores, MASKED_SCORE)
    powers = jnp.exp(scores - jnp.max(scores, axis=-1, keepdims=True))
    total = jnp.sum(powers, axis=-1, keepdims=True)
    return (powers * (1.0 / total)).astype(BF16)


def attention_kernel(
    len_short,
    len_long,
    x_short_ref,
    x_long_ref,
    params,
    w_ref,
    x_ref,
    q_ref,
    k_ref,
    v_ref,
    context_ref,
    short_ref,
    long_ref,
    bias,
    *,
    short_tiles,
):
    tile = pl.program_id(0)
    group = pl.program_id(1)
    low, high = half_masks()
    width = short_ref.shape[-1]
    per_tile = TILE // width

    wide = PAIRS * BLK
    start = pl.multiple_of(group * wide, wide)

    @pl.when((tile == 0) & (group == 0))
    def _():
        for which in range(2):
            for place in range(D // BLK):
                row = which * (D // BLK) + place
                bias[which : which + 1, place * BLK : (place + 1) * BLK] = params[row : row + 1, :]

    @pl.when((tile < short_tiles) & (group == 0))
    def _():
        x_ref[...] = x_short_ref[...]

    @pl.when((tile >= short_tiles) & (group == 0))
    def _():
        x_ref[...] = x_long_ref[...]

    rows_in = x_ref[...]
    queries = product(rows_in, w_ref[:, pl.ds(start, wide)]) + bias[0:1, pl.ds(start, wide)]
    q_ref[...] = (queries * 0.125).astype(BF16)
    k_ref[...] = product(rows_in, w_ref[:, pl.ds(D + start, wide)]).astype(BF16)
    values = product(rows_in, w_ref[:, pl.ds(2 * D + start, wide)]) + bias[1:2, pl.ds(start, wide)]
    v_ref[...] = values.astype(BF16)

    def attend(units, kept_ref):
        def scores(index):
            rows, keys, cols, _, _ = units[index]
            return right_product(stack_heads(q_ref[rows, cols], low, high), k_ref[keys, cols])

        def weigh(index, values):
            _, _, _, length, place = units[index]
            probs = softmax(values, length)
            kept_ref[place] = probs
            return probs

        def mix(index, probs):
            rows, keys, cols, _, _ = units[index]
            context_ref[rows, cols] = pick_heads(product(probs, v_ref[keys, cols])).astype(BF16)

        pipelined(len(units), scores, weigh, mix)

    @pl.when(tile < short_tiles)
    def _():
        units = []
        for seq in range(per_tile):
            rows = slice(seq * width, (seq + 1) * width)
            length = len_short[tile * per_tile + seq]
            for pair in range(PAIRS):
                cols = slice(pair * BLK, (pair + 1) * BLK)
                units.append((rows, rows, cols, length, (0, pair, seq)))
        attend(units, short_ref)

    @pl.when(tile >= short_tiles)
    def _():
        length = len_long[tile - short_tiles]
        half = TILE // 2
        units = []
        for pair in range(PAIRS):
            cols = slice(pair * BLK, (pair + 1) * BLK)
            for part in range(2):
                rows = slice(part * half, (part + 1) * half)
                units.append((rows, slice(0, TILE), cols, length, (0, pair, part)))
        attend(units, long_ref)


def run_events(step, events):
    for index, actions in enumerate(events):

        @pl.when(step == index)
        def _(actions=actions):
            for action in actions:
                action()


def probs_shapes(short_tiles, long_tiles, width):
    per_tile = TILE // width
    return (
        (short_tiles, 2 * PAIRS, per_tile, 2 * width, width),
        (long_tiles, 2 * PAIRS, 2, TILE, TILE),
    )


def short_index(tile, short_tiles):
    return jnp.minimum(tile, short_tiles - 1)


def long_index(tile, short_tiles):
    return jnp.maximum(tile - short_tiles, 0)


def probs_maps(short_tiles):
    def short_map(tile, group):
        last = jnp.minimum(tile // short_tiles, 1)
        return (short_index(tile, short_tiles), group + last * (GROUPS - 1 - group), 0, 0, 0)

    def long_map(tile, group):
        begun = jnp.minimum(tile // short_tiles, 1)
        return (long_index(tile, short_tiles), begun * group, 0, 0, 0)

    return short_map, long_map


def attention(len_short, len_long, x_short, x_long, params, w_qkv, short_tiles, width):
    tiles = (x_short.shape[0] + x_long.shape[0]) // TILE
    wide = PAIRS * BLK
    short_shape, long_shape = probs_shapes(short_tiles, tiles - short_tiles, width)
    short_map, long_map = probs_maps(short_tiles)
    flops = 4 * D * TILE * TILE * tiles + 6 * D * D * TILE * tiles
    rows = pl.BlockSpec((TILE, wide), lambda tile, group: (tile, group))
    scalars = pl.BlockSpec(memory_space=pltpu.SMEM)

    def whole(shape):
        return pl.BlockSpec(shape, lambda tile, group: (0,) * len(shape), pipeline_mode=pl.Buffered(1))

    in_specs = [
        scalars,
        scalars,
        pl.BlockSpec((TILE, D), lambda tile, group: (short_index(tile, short_tiles), 0)),
        pl.BlockSpec((TILE, D), lambda tile, group: (long_index(tile, short_tiles), 0)),
        whole(params.shape),
        whole((D, 3 * D)),
    ]
    out_specs = [
        pl.BlockSpec((TILE, D), lambda tile, group: (tile, 0)),
        rows,
        rows,
        rows,
        rows,
        pl.BlockSpec((1, PAIRS) + short_shape[2:], short_map),
        pl.BlockSpec((1, PAIRS) + long_shape[2:], long_map),
    ]
    out_shape = [jax.ShapeDtypeStruct((tiles * TILE, D), BF16)] * 5 + [
        jax.ShapeDtypeStruct(short_shape, BF16),
        jax.ShapeDtypeStruct(long_shape, BF16),
    ]
    arguments = [len_short, len_long, x_short, x_long, params, w_qkv]
    return pl.pallas_call(
        partial(attention_kernel, short_tiles=short_tiles),
        grid=(tiles, GROUPS),
        in_specs=in_specs,
        out_specs=out_specs,
        out_shape=out_shape,
        scratch_shapes=[pltpu.VMEM((8, D), F32)],
        compiler_params=pltpu.CompilerParams(vmem_limit_bytes=60 * MIB),
        cost_estimate=pl.CostEstimate(
            flops=flops, bytes_accessed=35 * MIB, transcendentals=HEADS * TILE * TILE * tiles // 2
        ),
        name="attention",
    )(*arguments)


def attention_back_kernel(*refs, short_tiles, transfers):
    q_ref, k_ref, v_ref, short_ref, long_ref, dc_ref = refs[:6]
    refs = refs[6:]
    if transfers:
        terms_ref, refs = refs[0], refs[1:]
    out_ref, bq_ref, bv_ref = refs[:3]
    tile = pl.program_id(0)
    group = pl.program_id(1)
    low, high = half_masks()
    width = short_ref.shape[-1]
    per_tile = TILE // width
    if transfers:
        reduce = Reduce(terms_ref, 0, refs[3], refs[4:])
        run_events(
            tile * GROUPS + group,
            (
                (reduce.start,),
                (partial(reduce.core, 0),),
                (partial(reduce.core, 1), partial(reduce.first, 0)),
                (partial(reduce.core, 2), partial(reduce.first, 1), partial(reduce.second, 0)),
                (partial(reduce.core, 3), partial(reduce.first, 2), partial(reduce.second, 1)),
                (partial(reduce.first, 3), partial(reduce.second, 2)),
                (partial(reduce.second, 3), reduce.share),
                (reduce.share_on,),
            ),
        )

    wide = PAIRS * BLK
    start = pl.multiple_of(group * wide, wide)

    def columns(which, cols):
        return pl.ds(pl.multiple_of(which * D + start + cols.start, BLK), BLK)

    def go_back(units, kept_ref, parts):
        sums = {}

        def spread_in(index):
            rows, keys, cols, _ = units[index]
            return right_product(stack_heads(dc_ref[rows, cols], low, high), v_ref[keys, cols])

        def differ(index, d_probs):
            wide = kept_ref[units[index][3]].astype(F32)
            weighted = wide * d_probs
            return (weighted - wide * jnp.sum(weighted, axis=-1, keepdims=True)).astype(BF16)

        def gather_up(index, d_scores):
            rows, keys, cols, place = units[index]
            d_queries = pick_heads(product(d_scores, k_ref[keys, cols])) * 0.125
            out_ref[rows, columns(0, cols)] = d_queries.astype(BF16)
            d_keys = left_product(d_scores, stack_heads(q_ref[rows, cols], low, high))
            d_values = left_product(kept_ref[place], stack_heads(dc_ref[rows, cols], low, high))
            if index % parts:
                d_keys += sums["keys"]
                d_values += sums["values"]
            if index % parts == parts - 1:
                out_ref[keys, columns(1, cols)] = d_keys.astype(BF16)
                out_ref[keys, columns(2, cols)] = d_values.astype(BF16)
            else:
                sums.update(keys=d_keys, values=d_values)

        pipelined(len(units), spread_in, differ, gather_up)

    @pl.when(tile < short_tiles)
    def _():
        units = []
        for seq in range(per_tile):
            rows = slice(seq * width, (seq + 1) * width)
            for pair in range(PAIRS):
                cols = slice(pair * BLK, (pair + 1) * BLK)
                units.append((rows, rows, cols, (0, pair, seq)))
        go_back(units, short_ref, 1)

    @pl.when(tile >= short_tiles)
    def _():
        half = TILE // 2
        units = []
        for pair in range(PAIRS):
            cols = slice(pair * BLK, (pair + 1) * BLK)
            for part in range(2):
                rows = slice(part * half, (part + 1) * half)
                units.append((rows, slice(0, TILE), cols, (0, pair, part)))
        go_back(units, long_ref, 2)

    @pl.when((tile == 0) & (group == 0))
    def _():
        bq_ref[...] = jnp.zeros_like(bq_ref)
        bv_ref[...] = jnp.zeros_like(bv_ref)

    bq_ref[:, pl.ds(start, wide)] += column_sum(out_ref[:, pl.ds(start, wide)])
    bv_ref[:, pl.ds(start, wide)] += column_sum(out_ref[:, pl.ds(2 * D + start, wide)])

    if transfers:

        @pl.when((tile == pl.num_programs(0) - 1) & (group == GROUPS - 1))
        def _():
            reduce.finish()


def attention_back(qkv, probs_short, probs_long, d_context, short_tiles, terms=None, count=0):
    tiles = d_context.shape[0] // TILE
    wide = PAIRS * BLK
    short_map, long_map = probs_maps(short_tiles)
    rows = pl.BlockSpec((TILE, wide), lambda tile, group: (tile, group))
    row = pl.BlockSpec((1, D), lambda tile, group: (0, 0))
    flops = 10 * D * TILE * TILE * tiles
    in_specs = [
        rows,
        rows,
        rows,
        pl.BlockSpec((1, PAIRS) + probs_short.shape[2:], short_map),
        pl.BlockSpec((1, PAIRS) + probs_long.shape[2:], long_map),
        rows,
    ]
    out_specs = [pl.BlockSpec((TILE, 3 * D), lambda tile, group: (tile, 0)), row, row]
    out_shape = [
        jax.ShapeDtypeStruct((tiles * TILE, 3 * D), BF16),
        jax.ShapeDtypeStruct((1, D), F32),
        jax.ShapeDtypeStruct((1, D), F32),
    ]
    arguments = [*qkv, probs_short, probs_long, d_context]
    scratch = []
    params = dict(vmem_limit_bytes=60 * MIB)
    if terms is not None:
        arguments.append(terms)
        in_specs.append(pl.BlockSpec(memory_space=pltpu.HBM))
        out_specs.append(pl.BlockSpec((count, BLK), lambda tile, group: (0, 0)))
        out_shape.append(jax.ShapeDtypeStruct((count, BLK), BF16))
        scratch = reduce_scratch(count)
        params.update(collective_id=2, has_side_effects=True)
    return pl.pallas_call(
        partial(attention_back_kernel, short_tiles=short_tiles, transfers=terms is not None),
        grid=(tiles, GROUPS),
        in_specs=in_specs,
        out_specs=out_specs,
        out_shape=out_shape,
        scratch_shapes=scratch,
        compiler_params=pltpu.CompilerParams(**params),
        cost_estimate=pl.CostEstimate(flops=flops, bytes_accessed=50 * MIB, transcendentals=0),
        name="attention_back",
    )(*arguments)


INPUT_ROWS = 256


def input_product(d_ref, resid_ref, w_ref, short_ref, long_ref, short_steps):
    step = pl.program_id(0)
    total = resid_ref[...] + right_product(d_ref[...], w_ref[...])

    @pl.when(step < short_steps)
    def _():
        short_ref[...] = total

    @pl.when(step >= short_steps)
    def _():
        long_ref[...] = total


def input_specs(short_steps):
    rows = [pl.BlockSpec((INPUT_ROWS, width), lambda step: (step, 0)) for width in (3 * D, D)]
    whole = pl.BlockSpec((D, 3 * D), lambda step: (0, 0), pipeline_mode=pl.Buffered(1))
    outs = [
        pl.BlockSpec((INPUT_ROWS, D), lambda step: (short_index(step, short_steps), 0)),
        pl.BlockSpec((INPUT_ROWS, D), lambda step: (long_index(step, short_steps), 0)),
    ]
    return rows + [whole], outs


def input_grads(d_qkv, resid, w_qkv, short_tiles):
    steps = resid.shape[0] // INPUT_ROWS
    short_steps = short_tiles * TILE // INPUT_ROWS
    in_specs, out_specs = input_specs(short_steps)
    return pl.pallas_call(
        partial(input_product, short_steps=short_steps),
        grid=(steps,),
        in_specs=in_specs,
        out_specs=out_specs,
        out_shape=[
            jax.ShapeDtypeStruct((short_steps * INPUT_ROWS, D), F32),
            jax.ShapeDtypeStruct(((steps - short_steps) * INPUT_ROWS, D), F32),
        ],
        compiler_params=pltpu.CompilerParams(vmem_limit_bytes=60 * MIB),
        name="input_grads",
    )(d_qkv, resid, w_qkv)


def normal_parts(values):
    below = 0.5 * lax.erf(values * 0.7071067811865476) + 0.5
    return below, jnp.exp(-0.5 * values * values) * 0.3989422804014327


B_OUT, GAIN_ONE, SHIFT_ONE, B_UP, B_DOWN, GAIN_TWO, SHIFT_TWO, B_STUDENT, POOL_QUERY, B_HIDDEN = range(10)
VECTORS = (
    (12, 6),
    (18, 6),
    (24, 6),
    (30, 24),
    (54, 6),
    (60, 6),
    (66, 6),
    (72, 1),
    (73, 1),
    (74, 1),
)
CLASS_ROW = 75
LAST_ROW = 91
SMALL_ROWS = 96


def norm_parts(values):
    center = values - jnp.mean(values, axis=-1, keepdims=True)
    spread = jnp.mean(center * center, axis=-1, keepdims=True)
    inverse = lax.rsqrt(spread + NORM_EPSILON)
    return center * inverse, inverse


def norm_back(d_values, gain, unit, inverse):
    d_unit = d_values * gain
    return inverse * (
        d_unit
        - jnp.mean(d_unit, axis=-1, keepdims=True)
        - unit * jnp.mean(d_unit * unit, axis=-1, keepdims=True)
    )


def column_sum(values):
    return jnp.sum(values.astype(F32), axis=0, keepdims=True)


def pool_weights(student, query, length):
    scaled = student * query
    lane = lax.broadcasted_iota(jnp.int32, scaled.shape, 1)
    place = lax.broadcasted_iota(jnp.int32, (scaled.shape[0], 1), 0)
    weights = []
    for side in (lane < SD // PH, lane >= SD // PH):
        scores = jnp.sum(jnp.where(side, scaled, 0.0), axis=-1, keepdims=True)
        scores = jnp.where(place < length, scores, MASKED_SCORE)
        powers = jnp.exp(scores - jnp.max(scores, axis=0, keepdims=True))
        weights.append(powers / jnp.sum(powers, axis=0, keepdims=True))
    return jnp.where(lane < SD // PH, weights[0], weights[1]), weights


def student_back(student, query, weights, both, d_pooled):
    lane = lax.broadcasted_iota(jnp.int32, student.shape, 1)
    moved = student * d_pooled
    d_scores = []
    for side, weight in zip((lane < SD // PH, lane >= SD // PH), weights):
        d_weight = jnp.sum(jnp.where(side, moved, 0.0), axis=-1, keepdims=True)
        d_scores.append(weight * (d_weight - jnp.sum(weight * d_weight, axis=0, keepdims=True)))
    d_score = jnp.where(lane < SD // PH, d_scores[0], d_scores[1])
    d_query = jnp.sum(d_score * student, axis=0, keepdims=True) * 0.125
    return both * d_pooled + d_score * query, d_query


def feed_kernel(
    len_short,
    len_long,
    slot_ref,
    x_ref,
    context_ref,
    cot_short_ref,
    cot_long_ref,
    logit_cot_ref,
    params,
    w_class,
    b_class,
    blocks,
    enc_short_ref,
    enc_long_ref,
    logit_ref,
    first_ref,
    active_ref,
    d_up_ref,
    d_down_ref,
    d_branch_ref,
    d_context_ref,
    d_resid_ref,
    g_student,
    g_hidden,
    g_small,
    slope,
    pooled_ref,
    d_student_ref,
    w_out,
    w_up,
    w_down,
    w_student,
    w_hidden,
    vectors,
    totals,
    g_class,
    g_last,
    sems,
    *,
    short_tiles,
    width,
):
    tile = pl.program_id(0)
    per_tile = TILE // width
    loads = ((w_out, 108, 6, 6), (w_up, 144, 6, 24), (w_down, 288, 24, 6), (w_student, 432, 6, 1), (w_hidden, 438, 1, 1))

    def arrive(*indices):
        @pl.when(tile == 0)
        def _():
            for index in indices:
                wait_whole(loads[index][0], sems.at[index])

    @pl.when(tile == 0)
    def _():
        for index, (target, block, row_count, col_count) in enumerate(loads):
            load_blocks(slot_ref, blocks, target, sems.at[index], block, row_count, col_count)
        for index, (start, count) in enumerate(VECTORS):
            for place in range(count):
                vectors[index : index + 1, place * BLK : (place + 1) * BLK] = params[
                    start + place : start + place + 1, :
                ]
        for ref in (totals, g_class, g_last, g_student, g_hidden):
            ref[...] = jnp.zeros_like(ref)

    def vector(index):
        return vectors[index : index + 1, : VECTORS[index][1] * BLK]

    def add_total(index, values):
        totals[index : index + 1, : VECTORS[index][1] * BLK] += column_sum(values)

    arrive(0)
    branch = product(context_ref[...], w_out[...]) + vector(B_OUT)
    unit_one, inverse_one = norm_parts(x_ref[...].astype(F32) + branch)
    first = (unit_one * vector(GAIN_ONE) + vector(SHIFT_ONE)).astype(BF16)
    first_ref[...] = first
    arrive(1)
    chunks = [slice(start, start + CHUNK) for start in range(0, FF, CHUNK)]

    def rise(index):
        return product(first, w_up[:, chunks[index]])

    def bend(index, upward):
        upward = upward + vectors[B_UP : B_UP + 1, chunks[index]]
        below, density = normal_parts(upward)
        active_ref[:, chunks[index]] = (upward * below).astype(BF16)
        slope[:, chunks[index]] = (below + upward * density).astype(BF16)

    pipelined(len(chunks), rise, bend, lambda *_: None)
    arrive(2, 3, 4)
    downward = product(active_ref[...], w_down[...]) + vector(B_DOWN)
    unit_two, inverse_two = norm_parts(first.astype(F32) + downward)
    encoded = (unit_two * vector(GAIN_TWO) + vector(SHIFT_TWO)).astype(BF16)

    @pl.when(tile < short_tiles)
    def _():
        enc_short_ref[...] = encoded

    @pl.when(tile >= short_tiles)
    def _():
        enc_long_ref[...] = encoded

    student = product(encoded, w_student[...]) + vector(B_STUDENT)
    query = vector(POOL_QUERY) * 0.125
    pooled_ref[...] = jnp.zeros_like(pooled_ref)

    def head():
        pooled = pooled_ref[...]
        wide_hidden = w_hidden[...].astype(F32)
        hidden = jnp.tanh(product(pooled, wide_hidden, HIGHEST_PRECISION) + vector(B_HIDDEN))
        logit_ref[0] = product(hidden, w_class[...], HIGHEST_PRECISION) + b_class[...]
        d_logits = logit_cot_ref[0]
        g_last[...] += column_sum(d_logits)
        g_class[...] += left_product(d_logits, hidden, HIGHEST_PRECISION)
        d_hidden = right_product(d_logits, w_class[...], HIGHEST_PRECISION)
        d_hidden = d_hidden * (1.0 - hidden * hidden)
        add_total(B_HIDDEN, d_hidden)
        g_hidden[...] += left_product(pooled, d_hidden, HIGHEST_PRECISION)
        return right_product(d_hidden, wide_hidden, HIGHEST_PRECISION)

    def pool(starts, size, lengths):
        kept = []
        for index, (start, length) in enumerate(zip(starts, lengths)):
            rows = student[start : start + size]
            both, weights = pool_weights(rows, query, length)
            pooled_ref[index : index + 1, :] = column_sum(both * rows)
            kept.append((start, rows, both, weights))
        d_pooled = head()
        for index, (start, rows, both, weights) in enumerate(kept):
            d_rows, d_query = student_back(rows, query, weights, both, d_pooled[index : index + 1])
            d_student_ref[start : start + size, :] = d_rows.astype(BF16)
            add_total(POOL_QUERY, d_query)

    @pl.when(tile < short_tiles)
    def _():
        pool(
            [seq * width for seq in range(per_tile)],
            width,
            [len_short[tile * per_tile + seq] for seq in range(per_tile)],
        )

    @pl.when(tile >= short_tiles)
    def _():
        pool([0], TILE, [len_long[tile - short_tiles]])

    d_student = d_student_ref[...]
    add_total(B_STUDENT, d_student)
    g_student[...] += left_product(encoded, d_student)
    cotangent = jnp.where(tile < short_tiles, cot_short_ref[...], cot_long_ref[...])
    d_second = cotangent.astype(F32) + right_product(d_student, w_student[...])
    add_total(GAIN_TWO, d_second * unit_two)
    add_total(SHIFT_TWO, d_second)
    d_resid_two = norm_back(d_second, vector(GAIN_TWO), unit_two, inverse_two)
    d_down = d_resid_two.astype(BF16)
    d_down_ref[...] = d_down
    add_total(B_DOWN, d_down)

    def fall(index):
        return right_product(d_down, w_down[chunks[index], :])

    def bend_back(index, d_active):
        d_up = (d_active * slope[:, chunks[index]].astype(F32)).astype(BF16)
        d_up_ref[:, chunks[index]] = d_up
        totals[B_UP : B_UP + 1, chunks[index]] += column_sum(d_up)

    pipelined(len(chunks), fall, bend_back, lambda *_: None)
    d_first = d_resid_two + right_product(d_up_ref[...], w_up[...])
    add_total(GAIN_ONE, d_first * unit_one)
    add_total(SHIFT_ONE, d_first)
    d_resid_one = norm_back(d_first, vector(GAIN_ONE), unit_one, inverse_one)
    d_resid_ref[...] = d_resid_one
    d_branch = d_resid_one.astype(BF16)
    d_branch_ref[...] = d_branch
    add_total(B_OUT, d_branch)
    d_context_ref[...] = right_product(d_branch, w_out[...]).astype(BF16)

    @pl.when(tile == pl.num_programs(0) - 1)
    def _():
        g_small[...] = jnp.zeros_like(g_small)
        for index, (start, count) in enumerate(VECTORS):
            for place in range(count):
                g_small[start + place : start + place + 1, :] = totals[
                    index : index + 1, place * BLK : (place + 1) * BLK
                ]
        g_small[CLASS_ROW : CLASS_ROW + NCLS, :] = g_class[:NCLS, :]
        g_small[LAST_ROW : LAST_ROW + 1, :] = g_last[...]


def feed(
    len_short, len_long, block_slot, x, context, cot_short, cot_long, logit_cot, small, blocks, short_tiles, width
):
    tiles = x.shape[0] // TILE
    long_tiles = tiles - short_tiles

    def whole(shape):
        return pl.BlockSpec(shape, lambda tile, *_: (0,) * len(shape), pipeline_mode=pl.Buffered(1))

    def kept(shape):
        return pl.BlockSpec(shape, lambda tile, *_: (0,) * len(shape))

    def rows(columns):
        return pl.BlockSpec((TILE, columns), lambda tile, *_: (tile, 0))

    short_rows = pl.BlockSpec((TILE, D), lambda tile, *_: (short_index(tile, short_tiles), 0))
    long_rows = pl.BlockSpec((TILE, D), lambda tile, *_: (long_index(tile, short_tiles), 0))
    logit_rows = pl.BlockSpec((1, 8, SD), lambda tile, *_: (tile, 0, 0))
    grad_shapes = ((D, SD), (SD, SD), (SMALL_ROWS, BLK))
    total = tiles * TILE
    return pl.pallas_call(
        partial(feed_kernel, short_tiles=short_tiles, width=width),
        grid_spec=pltpu.PrefetchScalarGridSpec(
            num_scalar_prefetch=3,
            grid=(tiles,),
            in_specs=[rows(D), rows(D), short_rows, long_rows, logit_rows]
            + [whole(array.shape) for array in small]
            + [pl.BlockSpec(memory_space=pltpu.HBM)],
            out_specs=[
                short_rows,
                long_rows,
                logit_rows,
                rows(D),
                rows(FF),
                rows(FF),
                rows(D),
                rows(D),
                rows(D),
                rows(D),
            ]
            + [kept(shape) for shape in grad_shapes],
            scratch_shapes=[
                pltpu.VMEM((TILE, FF), BF16),
                pltpu.VMEM((8, SD), F32),
                pltpu.VMEM((TILE, SD), BF16),
                pltpu.VMEM((D, D), BF16),
                pltpu.VMEM((D, FF), BF16),
                pltpu.VMEM((FF, D), BF16),
                pltpu.VMEM((D, SD), BF16),
                pltpu.VMEM((SD, SD), BF16),
                pltpu.VMEM((16, FF), F32),
                pltpu.VMEM((16, FF), F32),
                pltpu.VMEM((SD, SD), F32),
                pltpu.VMEM((1, SD), F32),
                pltpu.SemaphoreType.DMA((5,)),
            ],
        ),
        out_shape=[
            jax.ShapeDtypeStruct((short_tiles * TILE, D), BF16),
            jax.ShapeDtypeStruct((long_tiles * TILE, D), BF16),
            jax.ShapeDtypeStruct((tiles, 8, SD), F32),
            jax.ShapeDtypeStruct((total, D), BF16),
            jax.ShapeDtypeStruct((total, FF), BF16),
            jax.ShapeDtypeStruct((total, FF), BF16),
            jax.ShapeDtypeStruct((total, D), BF16),
            jax.ShapeDtypeStruct((total, D), BF16),
            jax.ShapeDtypeStruct((total, D), BF16),
            jax.ShapeDtypeStruct((total, D), F32),
        ]
        + [jax.ShapeDtypeStruct(shape, F32) for shape in grad_shapes],
        compiler_params=pltpu.CompilerParams(vmem_limit_bytes=62 * MIB),
        cost_estimate=pl.CostEstimate(
            flops=total * (8 * D * FF + 4 * D * D), bytes_accessed=70 * MIB, transcendentals=total * FF
        ),
        name="feed",
    )(len_short, len_long, block_slot, x, context, cot_short, cot_long, logit_cot, *small, blocks)


class Place:
    def __init__(self):
        self.quarter = lax.axis_index("dp")
        self.shard = lax.axis_index("fsdp")
        x = self.quarter % 2
        y = self.quarter // 2
        self.core = self.shard % 2
        self.z = self.shard // 2
        self.high = self.z // 2
        self.by_x = 2 * y + 1 - x
        self.by_y = 2 * (1 - y) + x
        self.across = 2 * (1 - y) + 1 - x
        self.sibling = (self.quarter, 2 * self.z + 1 - self.core)
        self.next_x = (self.by_x, self.shard)
        self.next_y = (self.by_y, self.shard)
        self.inner = (self.z > 0) & (self.z < 3)

    def at_z(self, z):
        return (self.quarter, 2 * z + self.core)


def transfer(source, target, send_sem, recv_sem, device):
    return pltpu.make_async_remote_copy(
        src_ref=source,
        dst_ref=target,
        send_sem=send_sem,
        recv_sem=recv_sem,
        device_id=device,
        device_id_type=pl.DeviceIdType.MESH,
    )


def greet(place, extra=()):
    barrier = pltpu.get_barrier_semaphore()

    def signal(device):
        pl.semaphore_signal(barrier, inc=1, device_id=device, device_id_type=pl.DeviceIdType.MESH)

    near = (place.sibling, place.next_x, place.next_y) + tuple(extra)
    for device in near:
        signal(device)

    @pl.when(place.z > 0)
    def _():
        signal(place.at_z(place.z - 1))

    @pl.when(place.z < 3)
    def _():
        signal(place.at_z(place.z + 1))

    pl.semaphore_wait(barrier, len(near) + 1 + (place.z + 1) // 2 % 2)


CUTS = 2
GATHER_SEMAPHORES = [
    pltpu.SemaphoreType.DMA((2 * CUTS,)),
    pltpu.SemaphoreType.DMA((3 * CUTS,)),
    pltpu.SemaphoreType.DMA((4 * CUTS,)),
    pltpu.SemaphoreType.DMA((12 * CUTS,)),
    pltpu.SemaphoreType.DMA((12 * CUTS,)),
    pltpu.SemaphoreType.DMA((1 + 15 * CUTS,)),
    pltpu.SemaphoreType.DMA((1 + 15 * CUTS,)),
    pltpu.SemaphoreType.DMA((8,)),
]


class Gather:
    def __init__(self, full, out, sems):
        self.place = place = Place()
        self.full, self.out = full, out
        (
            self.own_send,
            self.relay_send,
            self.z_recv,
            self.xy_send,
            self.xy_recv,
            self.core_send,
            self.core_recv,
            self.out_sems,
        ) = sems
        self.quarter = full.shape[1] // 4
        self.cut = self.quarter // CUTS
        self.first_part = (self.cut // 16 + 1) // 2 * 16
        z = place.z
        self.origins = (z + 1 - 2 * (z % 2), 2 - place.high, 3 * (1 - place.high))
        self.relays = (3 - z, 3 * (z - 1), 3 * (z - 1))

    def region(self, which, start, size):
        return self.full.at[which, pl.ds(pl.multiple_of(start, 16), size)]

    def pieces(self, which, turn):
        place, quarter, cut, part = self.place, self.quarter, self.cut, self.first_part
        skip = turn % CUTS * cut
        return (
            self.region(which, place.quarter * quarter + skip, cut),
            self.region(which, place.by_x * quarter + skip, cut),
            self.region(which, place.by_y * quarter + skip, cut),
            self.region(which, place.across * quarter + skip, part),
            self.region(which, place.across * quarter + skip + part, cut - part),
        )

    def own_copy(self, side, cut):
        place = self.place
        mine = self.pieces(place.shard, cut)[0]
        device = place.at_z(place.z - 1 + 2 * side)
        return transfer(
            mine,
            mine,
            self.own_send.at[side * CUTS + cut],
            self.z_recv.at[place.z * CUTS + cut],
            device,
        )

    def core_copy(self, index, ref):
        return transfer(ref, ref, self.core_send.at[index], self.core_recv.at[index], self.place.sibling)

    def xy_copy(self, index, ref, device):
        return transfer(ref, ref, self.xy_send.at[index], self.xy_recv.at[index], device)

    def store(self, index, which):
        return pltpu.make_async_copy(self.full.at[which], self.out.at[which], self.out_sems.at[index])

    def mirrored(self, step):
        return 2 * self.origins[step] + 1 - self.place.core

    def held(self, step):
        return 2 * self.origins[step] + self.place.core

    def start(self):
        place = self.place
        greet(place)
        for cut in range(CUTS):

            @pl.when(place.z > 0)
            def _():
                self.own_copy(0, cut).start()

            @pl.when(place.z < 3)
            def _():
                self.own_copy(1, cut).start()

        self.core_copy(0, self.full.at[place.shard]).start()
        self.store(0, place.shard).start()

    def relay(self, turn):
        step = turn // CUTS
        piece = self.pieces(self.held(step), turn)[0]
        device = self.place.at_z(self.relays[step])
        sem = self.z_recv.at[self.origins[step] * CUTS + turn % CUTS]
        return transfer(piece, piece, self.relay_send.at[turn], sem, device)

    def along_z(self, turn):
        place = self.place
        self.relay(turn).wait_recv()

        @pl.when(place.inner)
        def _():
            self.relay(turn).start()

        piece = self.pieces(self.held(turn // CUTS), turn)[0]
        self.xy_copy(4 * turn, piece, place.next_x).start()
        self.xy_copy(4 * turn + 1, piece, place.next_y).start()
        self.core_copy(1 + 5 * turn, piece).start()

    def along_xy(self, turn):
        place, part = self.place, self.first_part
        _, by_x, by_y, _, _ = self.pieces(self.held(turn // CUTS), turn)
        self.xy_copy(4 * turn, by_x, place.next_x).wait_recv()
        self.xy_copy(4 * turn + 2, by_x.at[pl.ds(0, part)], place.next_y).start()
        self.core_copy(2 + 5 * turn, by_x).start()
        self.xy_copy(4 * turn + 1, by_y, place.next_y).wait_recv()
        self.xy_copy(4 * turn + 3, by_y.at[pl.ds(part, self.cut - part)], place.next_x).start()
        self.core_copy(3 + 5 * turn, by_y).start()

    def across(self, turn):
        place = self.place
        step = turn // CUTS
        _, _, _, first, last = self.pieces(self.held(step), turn)
        self.xy_copy(4 * turn + 2, first, place.next_y).wait_recv()
        self.core_copy(4 + 5 * turn, first).start()
        self.xy_copy(4 * turn + 3, last, place.next_x).wait_recv()
        self.core_copy(5 + 5 * turn, last).start()
        if turn % CUTS == CUTS - 1:
            self.store(2 + 2 * step, self.held(step)).start()

    def core_own(self):
        which = 2 * self.place.z + 1 - self.place.core
        self.core_copy(0, self.full.at[which]).wait_recv()
        self.store(1, which).start()

    def core(self, step):
        which = self.mirrored(step)
        for turn in range(step * CUTS, (step + 1) * CUTS):
            for index, ref in enumerate(self.pieces(which, turn)):
                self.core_copy(1 + 5 * turn + index, ref).wait_recv()
        self.store(3 + 2 * step, which).start()

    def finish(self):
        place = self.place
        for cut in range(CUTS):

            @pl.when(place.z > 0)
            def _():
                self.own_copy(0, cut).wait_send()

            @pl.when(place.z < 3)
            def _():
                self.own_copy(1, cut).wait_send()

        self.core_copy(0, self.full.at[place.shard]).wait_send()
        self.store(0, place.shard).wait()
        self.store(1, 2 * place.z + 1 - place.core).wait()
        for turn in range(3 * CUTS):

            @pl.when(place.inner)
            def _():
                self.relay(turn).wait_send()

            pieces = self.pieces(self.held(turn // CUTS), turn)
            self.xy_copy(4 * turn, pieces[0], place.next_x).wait_send()
            self.xy_copy(4 * turn + 1, pieces[0], place.next_y).wait_send()
            self.xy_copy(4 * turn + 2, pieces[3], place.next_y).wait_send()
            self.xy_copy(4 * turn + 3, pieces[4], place.next_x).wait_send()
            for index, ref in enumerate(pieces):
                self.core_copy(1 + 5 * turn + index, ref).wait_send()
        for step in range(3):
            self.store(2 + 2 * step, self.held(step)).wait()
            self.store(3 + 2 * step, self.mirrored(step)).wait()


def gather_kernel(master_ref, out_ref, full, *sems):
    gather = Gather(full, out_ref, sems)
    full[gather.place.shard] = master_ref[...].astype(BF16)
    gather.start()
    turns = 3 * CUTS
    for turn in range(turns + 2):
        if turn < turns:
            gather.along_z(turn)
        if 1 <= turn <= turns:
            gather.along_xy(turn - 1)
        if turn >= 2:
            gather.across(turn - 2)
        if turn == 2:
            gather.core_own()
        if turn >= 4 and turn % CUTS == 0:
            gather.core(turn // CUTS - 2)
    gather.core(2)
    gather.finish()


def gather_shards(master):
    rows = master.shape[0] * BLK
    shards = lax.axis_size("fsdp")
    return pl.pallas_call(
        gather_kernel,
        in_specs=[pl.BlockSpec(memory_space=pltpu.VMEM)],
        out_specs=pl.BlockSpec(memory_space=pltpu.HBM),
        out_shape=jax.ShapeDtypeStruct((shards, rows, BLK), BF16),
        scratch_shapes=[pltpu.VMEM((shards, rows, BLK), BF16)] + GATHER_SEMAPHORES,
        compiler_params=pltpu.CompilerParams(
            collective_id=0, has_side_effects=True, vmem_limit_bytes=60 * MIB
        ),
        cost_estimate=pl.CostEstimate(flops=0, bytes_accessed=200 * MIB, transcendentals=0),
        name="gather",
    )(master.reshape(rows, BLK)).reshape(-1, BLK, BLK)


def add_rows(target, former, latter, rows, step):
    @pl.loop(0, rows // step)
    def _(index):
        part = pl.ds(pl.multiple_of(index * step, 16), step)
        target[part] = (former[part].astype(F32) + latter[part].astype(F32)).astype(BF16)


def reduce_scratch(rows):
    quarter = rows // 4
    half = quarter // 2
    return [
        pltpu.VMEM((4, rows, BLK), BF16),
        pltpu.VMEM((4, rows, BLK), BF16),
        pltpu.VMEM((4, 2, half, BLK), BF16),
        pltpu.VMEM((4, 2, half, BLK), BF16),
        pltpu.VMEM((4, half, BLK), BF16),
        pltpu.VMEM((4, half, BLK), BF16),
        pltpu.VMEM((5, quarter, BLK), BF16),
        pltpu.VMEM((rows, BLK), BF16),
        pltpu.SemaphoreType.DMA((4,)),
        pltpu.SemaphoreType.DMA((4,)),
        pltpu.SemaphoreType.DMA((4,)),
        pltpu.SemaphoreType.DMA((24,)),
        pltpu.SemaphoreType.DMA((24,)),
        pltpu.SemaphoreType.DMA((3,)),
        pltpu.SemaphoreType.DMA((5,)),
        pltpu.SemaphoreType.DMA((4,)),
        pltpu.SemaphoreType.DMA((4,)),
    ]


class Reduce:
    def __init__(self, terms, base, out, scratch):
        self.place = place = Place()
        self.terms, self.base, self.out = terms, base, out
        (
            self.mine,
            self.sib,
            self.from_x,
            self.from_y,
            self.late_y,
            self.late_x,
            self.from_z,
            self.result,
            self.load_sems,
            self.core_send,
            self.core_recv,
            self.xy_send,
            self.xy_recv,
            self.z_send,
            self.z_recv,
            self.last_send,
            self.last_recv,
        ) = scratch
        self.quarter = out.shape[0] // 4
        self.half = self.quarter // 2
        z, high = place.z, place.high
        low = 1 - high
        self.order = (3 * low, low * (2 - 2 * z) + high * (7 - 2 * z), 1 + z % 2, z)
        self.onward = (z + 1 - 2 * high, z + 1 - 2 * (z % 2), z + 1 - 2 * high)
        self.closing = (0, (z % 2) * low, high)
        self.far = place.at_z(z + 2 - 4 * high)
        self.near = place.at_z(z + 1 - 2 * (z % 2))

    def shard_terms(self, shard):
        rows = self.out.shape[0]
        return self.terms.at[pl.ds(pl.multiple_of(self.base + shard * rows, 16), rows)]

    def load(self, step):
        source = self.shard_terms(2 * self.order[step] + self.place.core)
        return pltpu.make_async_copy(source, self.mine.at[step], self.load_sems.at[step])

    def core_copy(self, step):
        return transfer(
            self.shard_terms(2 * self.order[step] + 1 - self.place.core),
            self.sib.at[step],
            self.core_send.at[step],
            self.core_recv.at[step],
            self.place.sibling,
        )

    def part(self, step, which, side):
        start = pl.multiple_of(which * self.quarter + side * self.half, 16)
        return self.mine.at[step, pl.ds(start, self.half)]

    def xy_copy(self, step, index):
        place = self.place
        source, target, device = (
            (self.part(step, place.by_x, 0), self.from_x.at[step, 0], place.next_x),
            (self.part(step, place.across, 0), self.from_x.at[step, 1], place.next_x),
            (self.part(step, place.by_y, 1), self.from_y.at[step, 0], place.next_y),
            (self.part(step, place.across, 1), self.from_y.at[step, 1], place.next_y),
            (self.part(step, place.by_y, 0), self.late_y.at[step], place.next_y),
            (self.part(step, place.by_x, 1), self.late_x.at[step], place.next_x),
        )[index]
        place = 6 * step + index
        return transfer(source, target, self.xy_send.at[place], self.xy_recv.at[place], device)

    def start(self):
        greet(self.place, (self.far,))
        for step in range(2):
            self.core_copy(step).start()
        for step in range(4):
            self.load(step).start()

    def core(self, step):
        place, quarter = self.place, self.quarter
        self.load(step).wait()
        self.core_copy(step).wait_recv()
        if step < 2:
            self.core_copy(step + 2).start()

        def add(which):
            block = pl.ds(pl.multiple_of(which * quarter, 16), quarter)
            mine = self.mine.at[step, block]
            add_rows(mine, mine, self.sib.at[step, block], quarter, self.half)

        add(place.by_x)
        add(place.across)
        self.xy_copy(step, 0).start()
        self.xy_copy(step, 1).start()
        add(place.by_y)
        self.xy_copy(step, 2).start()
        self.xy_copy(step, 3).start()
        add(place.quarter)

    def take(self, step, which, side, index, source):
        self.xy_copy(step, index).wait_recv()
        target = self.part(step, which, side)
        add_rows(target, target, source, self.half, self.half)

    def first(self, step):
        place = self.place
        self.take(step, place.by_y, 0, 1, self.from_x.at[step, 1])
        self.xy_copy(step, 4).start()
        self.take(step, place.by_x, 1, 3, self.from_y.at[step, 1])
        self.xy_copy(step, 5).start()
        self.take(step, place.quarter, 0, 0, self.from_x.at[step, 0])
        self.take(step, place.quarter, 1, 2, self.from_y.at[step, 0])

    def own_block(self, step):
        return self.mine.at[step, pl.ds(pl.multiple_of(self.place.quarter * self.quarter, 16), self.quarter)]

    def z_copy(self, step):
        goal = self.order[step]
        slot = goal + self.closing[step] * (4 - goal)
        return transfer(
            self.own_block(step),
            self.from_z.at[slot],
            self.z_send.at[step],
            self.z_recv.at[slot],
            self.place.at_z(self.onward[step]),
        )

    def take_z(self, step, slot):
        source = self.from_z.at[slot]
        transfer(source, source, self.z_send.at[0], self.z_recv.at[slot], self.near).wait_recv()
        block = self.own_block(step)
        add_rows(block, block, source, self.quarter, self.half)

    def second(self, step):
        place = self.place
        self.take(step, place.quarter, 0, 4, self.late_y.at[step])
        self.take(step, place.quarter, 1, 5, self.late_x.at[step])
        if step < 3:

            @pl.when(place.inner)
            def _():
                self.take_z(step, self.order[step])

            self.z_copy(step).start()
        else:

            @pl.when(place.z > 0)
            def _():
                self.take_z(step, place.z)

            @pl.when(place.z < 3)
            def _():
                self.take_z(step, 4)

    def final(self, which, side=None):
        start = pl.multiple_of(which * self.quarter + (0 if side is None else side * self.half), 16)
        return self.result.at[pl.ds(start, self.quarter if side is None else self.half)]

    def last_copy(self, index, ref):
        device = (self.place.next_x, self.place.next_y, self.place.next_y, self.place.next_x)[index]
        return transfer(ref, ref, self.last_send.at[index], self.last_recv.at[index], device)

    def share(self):
        own = self.final(self.place.quarter)
        own[...] = self.own_block(3)[...]
        self.last_copy(0, own).start()
        self.last_copy(1, own).start()

    def share_on(self):
        place = self.place
        self.last_copy(0, self.final(place.by_x)).wait_recv()
        self.last_copy(2, self.final(place.by_x, 0)).start()
        self.last_copy(1, self.final(place.by_y)).wait_recv()
        self.last_copy(3, self.final(place.by_y, 1)).start()

    def finish(self):
        place = self.place
        self.last_copy(2, self.final(place.across, 0)).wait_recv()
        self.last_copy(3, self.final(place.across, 1)).wait_recv()
        self.out[...] = self.result[...]
        for step in range(4):
            self.core_copy(step).wait_send()
            for index in range(6):
                self.xy_copy(step, index).wait_send()
            if step < 3:
                self.z_copy(step).wait_send()
        own = self.final(place.quarter)
        self.last_copy(0, own).wait_send()
        self.last_copy(1, own).wait_send()
        self.last_copy(2, self.final(place.by_x, 0)).wait_send()
        self.last_copy(3, self.final(place.by_y, 1)).wait_send()


def reduce_kernel(*refs, base, short_steps):
    terms, small_ref, d_ref, resid_ref, w_ref, out_ref, small_out, short_ref, long_ref = refs[:9]
    small_in, small_sum, small_send, small_recv = refs[9:13]
    reduce = Reduce(terms, base, out_ref, refs[13:])
    place = reduce.place
    partners = (place.sibling, place.next_x, place.next_y, reduce.near, reduce.far)

    def small_copy(level):
        return transfer(
            small_sum.at[level],
            small_in.at[level],
            small_send.at[level],
            small_recv.at[level],
            partners[level],
        )

    def small_start():
        small_sum[0] = small_ref[...]
        small_copy(0).start()

    def small_step(level):
        small_copy(level - 1).wait_recv()
        small_sum[level] = small_sum[level - 1] + small_in[level - 1]
        if level < 5:
            small_copy(level).start()
        else:
            small_out[...] = small_sum[5]

    run_events(
        pl.program_id(0),
        (
            (reduce.start, small_start),
            (partial(reduce.core, 0), partial(small_step, 1)),
            (partial(reduce.core, 1), partial(reduce.first, 0), partial(small_step, 2)),
            (
                partial(reduce.core, 2),
                partial(reduce.first, 1),
                partial(reduce.second, 0),
                partial(small_step, 3),
            ),
            (
                partial(reduce.core, 3),
                partial(reduce.first, 2),
                partial(reduce.second, 1),
                partial(small_step, 4),
            ),
            (partial(reduce.first, 3), partial(reduce.second, 2), partial(small_step, 5)),
            (partial(reduce.second, 3), reduce.share),
            (reduce.share_on,),
        ),
    )
    input_product(d_ref, resid_ref, w_ref, short_ref, long_ref, short_steps)

    @pl.when(pl.program_id(0) == pl.num_programs(0) - 1)
    def _():
        reduce.finish()
        for level in range(5):
            small_copy(level).wait_send()


def reduce_late(terms, base, rows, small, d_qkv, resid, w_qkv, short_tiles):
    steps = resid.shape[0] // INPUT_ROWS
    short_steps = short_tiles * TILE // INPUT_ROWS
    in_specs, out_specs = input_specs(short_steps)

    def whole(shape):
        return pl.BlockSpec(shape, lambda step: (0, 0), pipeline_mode=pl.Buffered(1))

    return pl.pallas_call(
        partial(reduce_kernel, base=base, short_steps=short_steps),
        grid=(steps,),
        in_specs=[pl.BlockSpec(memory_space=pltpu.HBM), whole(small.shape)] + in_specs,
        out_specs=[
            pl.BlockSpec((rows, BLK), lambda step: (0, 0)),
            pl.BlockSpec(small.shape, lambda step: (0, 0)),
        ]
        + out_specs,
        out_shape=[
            jax.ShapeDtypeStruct((rows, BLK), BF16),
            jax.ShapeDtypeStruct((SMALL_ROWS, BLK), F32),
            jax.ShapeDtypeStruct((short_steps * INPUT_ROWS, D), F32),
            jax.ShapeDtypeStruct(((steps - short_steps) * INPUT_ROWS, D), F32),
        ],
        scratch_shapes=[
            pltpu.VMEM((5, SMALL_ROWS, BLK), F32),
            pltpu.VMEM((6, SMALL_ROWS, BLK), F32),
            pltpu.SemaphoreType.DMA((5,)),
            pltpu.SemaphoreType.DMA((5,)),
        ]
        + reduce_scratch(rows),
        compiler_params=pltpu.CompilerParams(
            collective_id=3, has_side_effects=True, vmem_limit_bytes=60 * MIB
        ),
        cost_estimate=pl.CostEstimate(flops=0, bytes_accessed=200 * MIB, transcendentals=0),
        name="reduce",
    )(terms, small, d_qkv, resid, w_qkv)


def count_where(condition, axis):
    return jnp.sum(condition.astype(jnp.int32), axis=axis)


def slot_codes(slots, qkv_slots, slot_count, shards):
    early = slot_count - LATE
    shard = slots // slot_count
    begin = shard * slot_count
    inside = (qkv_slots[None, :] >= begin[:, None]) & (qkv_slots[None, :] < (begin + slot_count)[:, None])
    own = count_where(qkv_slots[None, :] == slots[:, None], 1)
    before = count_where(inside & (qkv_slots[None, :] < slots[:, None]), 1)
    number = count_where(inside, 1)
    position = jnp.where(own > 0, slot_count - number + before, slots - begin - before)
    code = jnp.where(
        position < early,
        shard * early + position,
        shards * early + shard * LATE + position - early,
    )
    return code, position, jnp.max(number)


def empty_slots(block_slot, all_slots):
    places = jnp.arange(all_slots, dtype=jnp.int32)
    empty_before = places + 1 - count_where(block_slot[None, :] <= places[:, None], 1)
    empty_index = jnp.arange(all_slots - NBLK, dtype=jnp.int32)
    return count_where(empty_before[None, :] <= empty_index[:, None], 1)


def halves(values):
    high = values.astype(BF16)
    return high, (values - high.astype(F32)).astype(BF16)


def update_kernel(
    position_ref,
    blocks,
    master,
    left_stat,
    right_stat,
    left_root,
    right_root,
    slot_grad,
    new_left,
    new_right,
    new_master,
):
    count = master.shape[0]
    first = pl.program_id(0) * count
    for index in range(count):
        start = pl.multiple_of(position_ref[first + index] * BLK, BLK)
        grad = blocks[pl.ds(start, BLK)]
        slot_grad[index] = grad.astype(F32)
        new_left[index] = STAT_DECAY * left_stat[index] + (1.0 - STAT_DECAY) * right_product(grad, grad)
        new_right[index] = STAT_DECAY * right_stat[index] + (1.0 - STAT_DECAY) * left_product(grad, grad)
        applied = product(jnp.concatenate(halves(left_root[index]), axis=0), grad)
        applied = jnp.concatenate(halves(applied[:BLK] + applied[BLK:]), axis=0)
        root_high, root_low = halves(right_root[index])
        wide = product(applied, root_high)
        total = wide[:BLK] + wide[BLK:] + product(applied[:BLK], root_low)
        new_master[index] = master[index] - MATRIX_RATE * total


def update(position, blocks, master, left_stat, right_stat, left_root, right_root):
    slot_count = master.shape[0]
    group = max(size for size in range(1, 12) if slot_count % size == 0)
    some = pl.BlockSpec((group, BLK, BLK), lambda step, *_: (step, 0, 0))
    return pl.pallas_call(
        update_kernel,
        grid_spec=pltpu.PrefetchScalarGridSpec(
            num_scalar_prefetch=1,
            grid=(slot_count // group,),
            in_specs=[
                pl.BlockSpec(blocks.shape, lambda step, *_: (0, 0), pipeline_mode=pl.Buffered(1))
            ]
            + [some] * 5,
            out_specs=[some] * 4,
        ),
        out_shape=[jax.ShapeDtypeStruct(master.shape, F32)] * 4,
        compiler_params=pltpu.CompilerParams(vmem_limit_bytes=60 * MIB),
        cost_estimate=pl.CostEstimate(
            flops=14 * slot_count * BLK**3, bytes_accessed=36 * slot_count * BLK**2, transcendentals=0
        ),
        name="update",
    )(position, blocks, master, left_stat, right_stat, left_root, right_root)


def body(
    x_short,
    x_long,
    cot_short,
    cot_long,
    logit_cot_short,
    logit_cot_long,
    len_short,
    len_long,
    block_slot,
    master,
    left_stat,
    right_stat,
    left_root,
    right_root,
    small_params,
    small_first,
    small_second,
    own_transfers,
):
    slot_count = master.shape[0]
    shards = lax.axis_size("fsdp")
    all_slots = slot_count * shards
    short_seqs, width = x_short.shape[:2]
    long_seqs = x_long.shape[0]
    short_tiles = short_seqs * width // TILE
    per_tile = TILE // width
    empty = empty_slots(block_slot, all_slots)

    if own_transfers:
        early_count = slot_count - LATE
        own = jnp.arange(slot_count, dtype=jnp.int32) + slot_count * lax.axis_index("fsdp")
        code, position, most = slot_codes(
            jnp.concatenate([block_slot, empty, own]), block_slot[: 3 * 36], slot_count, shards
        )
        position = position[all_slots:]
        empty_code = code[NBLK:all_slots]
        code = code[:NBLK]
        fits = most <= LATE
        gathered = gather_shards(master)
    else:
        gathered = lax.all_gather(master.astype(BF16), "fsdp", axis=0, tiled=True)
    w_qkv = assemble(block_slot, gathered)
    pieces = unpack(small_params)
    params = jnp.pad(small_params, (0, SMALL_ROWS * BLK - small_params.shape[0])).reshape(SMALL_ROWS, BLK)
    w_class = jnp.pad(pieces[-2].reshape(SD, NCLS), ((0, 0), (0, SD - NCLS)))
    b_class = jnp.pad(pieces[-1].reshape(1, NCLS), ((0, 0), (0, SD - NCLS)))

    x, *qkv, context, probs_short, probs_long = attention(
        len_short,
        len_long,
        x_short.reshape(-1, D),
        x_long.reshape(-1, D),
        params,
        w_qkv,
        short_tiles,
        width,
    )

    logit_cot = jnp.concatenate(
        [
            jnp.pad(
                logit_cot_short.reshape(short_tiles, per_tile, NCLS),
                ((0, 0), (0, 8 - per_tile), (0, SD - NCLS)),
            ),
            jnp.pad(logit_cot_long.reshape(long_seqs, 1, NCLS), ((0, 0), (0, 7), (0, SD - NCLS))),
        ],
        axis=0,
    )
    (
        enc_short,
        enc_long,
        logits,
        first,
        active,
        d_up,
        d_down,
        d_branch,
        d_context,
        d_resid,
        g_student,
        g_hidden,
        g_small,
    ) = feed(
        len_short,
        len_long,
        block_slot,
        x,
        context,
        cot_short.reshape(-1, D),
        cot_long.reshape(-1, D),
        logit_cot,
        (params, w_class, b_class),
        gathered,
        short_tiles,
        width,
    )
    g_down = left_product(active, d_down).astype(BF16)
    g_up = left_product(first, d_up).astype(BF16)
    g_out = left_product(context, d_branch).astype(BF16)
    others = (g_out, g_up, g_down, g_student.astype(BF16), g_hidden.astype(BF16))
    if own_transfers:
        terms = spread(code, empty_code, others, OTHER_PLACES, all_slots)
        *back, early_reduced = attention_back(
            qkv,
            probs_short,
            probs_long,
            d_context,
            short_tiles,
            terms.reshape(-1, BLK),
            early_count * BLK,
        )
    else:
        back = attention_back(qkv, probs_short, probs_long, d_context, short_tiles)
    d_qkv, g_b_query, g_b_value = back
    g_qkv = left_product(x, d_qkv).astype(BF16)

    def reduce_all():
        qkv_grads = tuple(g_qkv[:, which * D : (which + 1) * D] for which in range(3))
        slot_terms = spread(block_slot, empty, qkv_grads + others, QKV_PLACES + OTHER_PLACES, all_slots)
        return lax.psum(lax.psum_scatter(slot_terms, "fsdp", scatter_dimension=0, tiled=True), "dp")

    if own_transfers:
        terms, small_terms = spread_late(code, g_qkv, g_small, g_b_query, g_b_value, terms)
        late_reduced, small_total, in_short, in_long = reduce_late(
            terms.reshape(-1, BLK),
            shards * early_count * BLK,
            LATE * BLK,
            small_terms,
            d_qkv,
            d_resid,
            w_qkv,
            short_tiles,
        )

        blocks = lax.cond(
            fits,
            lambda: jnp.concatenate([early_reduced, late_reduced], axis=0),
            lambda: reduce_all().reshape(-1, BLK),
        )
        position = jnp.where(fits, position, jnp.arange(slot_count, dtype=jnp.int32))
    else:
        in_short, in_long = input_grads(d_qkv, d_resid, w_qkv, short_tiles)
        blocks = reduce_all().reshape(-1, BLK)
        position = jnp.arange(slot_count, dtype=jnp.int32)
        small_terms = jnp.concatenate(
            [g_b_query.reshape(-1, BLK), g_b_value.reshape(-1, BLK), g_small[2 * D // BLK :]], axis=0
        )
        small_total = lax.psum(small_terms, ("dp", "fsdp"))
    slot_grad, new_left, new_right, new_master = update(
        position, blocks, master, left_stat, right_stat, left_root, right_root
    )
    small_grad = jnp.concatenate(
        [
            small_total[:CLASS_ROW].reshape(-1),
            small_total[CLASS_ROW : CLASS_ROW + NCLS].T.reshape(-1),
            small_total[LAST_ROW, :NCLS],
        ]
    )
    new_first = BETA_ONE * small_first + (1.0 - BETA_ONE) * small_grad
    new_second = BETA_TWO * small_second + (1.0 - BETA_TWO) * small_grad * small_grad
    first_hat = new_first / (1.0 - BETA_ONE**STEP)
    second_hat = new_second / (1.0 - BETA_TWO**STEP)
    new_small = small_params - ADAM_RATE * first_hat / (jnp.sqrt(second_hat) + ADAM_EPSILON)
    return (
        enc_short.reshape(x_short.shape),
        logits[:short_tiles, :per_tile, :NCLS].reshape(short_seqs, NCLS),
        enc_long.reshape(x_long.shape),
        logits[short_tiles:, 0, :NCLS],
        in_short.reshape(x_short.shape),
        in_long.reshape(x_long.shape),
        slot_grad,
        new_left,
        new_right,
        new_master,
        new_first,
        new_second,
        new_small,
    )


def solution(mesh):
    both = ("dp", "fsdp")
    placed = (
        P(both, None, None),
        P(both, None, None),
        P(both, None, None),
        P(both, None, None),
        P(both, None),
        P(both, None),
        P(both),
        P(both),
        P(),
        P("fsdp", None, None),
        P("fsdp", None, None),
        P("fsdp", None, None),
        P("fsdp", None, None),
        P("fsdp", None, None),
        P(),
        P(),
        P(),
    )
    return jax.shard_map(
        partial(body, own_transfers=(mesh.shape["dp"], mesh.shape["fsdp"]) == (4, 8)),
        mesh=mesh,
        in_specs=placed,
        out_specs=(
            P(both, None, None),
            P(both, None),
            P(both, None, None),
            P(both, None),
            P(both, None, None),
            P(both, None, None),
            P("fsdp", None, None),
            P("fsdp", None, None),
            P("fsdp", None, None),
            P("fsdp", None, None),
            P(),
            P(),
            P(),
        ),
        check_vma=False,
    )
```

```python
from functools import partial

import jax
import jax.numpy as jnp
from jax import lax
from jax.experimental import pallas as pl
from jax.experimental.pallas import tpu as pltpu
from jax.sharding import PartitionSpec as P

D = 768
HEADS = 12
FF = 3072
SD = 128
PH = 2
NCLS = 14
BLK = 128
STEP = 10
NBLK = 439
TILE = 512
PAIRS = 3
GROUPS = 2
CHUNK = 512
WIDE = 256
ROWS = 64
LATE = 24

NORM_EPSILON = 1e-12
BETA_ONE = 0.9
BETA_TWO = 0.999
ADAM_EPSILON = 1e-08
ADAM_RATE = 0.1
MATRIX_RATE = 0.2
STAT_DECAY = 0.5
MASKED_SCORE = -1e30
HIGHEST_PRECISION = lax.Precision.HIGHEST
MIB = 1024 * 1024
F32 = jnp.float32
BF16 = jnp.bfloat16

def product(former, latter, precision=None):
    return jnp.dot(former, latter, preferred_element_type=F32, precision=precision)


def left_product(former, latter, precision=None):
    return lax.dot_general(
        former, latter, (((0,), (0,)), ((), ())), preferred_element_type=F32, precision=precision
    )


def right_product(former, latter, precision=None):
    return lax.dot_general(
        former, latter, (((1,), (1,)), ((), ())), preferred_element_type=F32, precision=precision
    )


def unpack(small_values):
    widths = (D, D, D, D, D, FF, D, D, D, SD, SD, SD, SD * NCLS, NCLS)
    pieces = []
    offset = 0
    for column_count in widths:
        pieces.append(small_values[offset : offset + column_count])
        offset += column_count
    return pieces


def each_block(first, row_count, col_count, action):
    def one_row(index, carry):
        row = pl.multiple_of(index * BLK, BLK)
        for col in range(col_count):
            action(first + index * col_count + col, row, col * BLK)
        return carry

    lax.fori_loop(0, row_count, one_row, 0)


def load_blocks(slot_ref, blocks, target, sem, first, row_count, col_count, col_start=0):
    def move(block, row, col):
        pltpu.make_async_copy(
            blocks.at[slot_ref[block]],
            target.at[pl.ds(row, BLK), pl.ds(col + col_start * BLK, BLK)],
            sem,
        ).start()

    each_block(first, row_count, col_count, move)


def wait_whole(target, sem):
    pltpu.make_async_copy(target, target, sem).wait()


def assemble_kernel(slot_ref, blocks, out, sem):
    for which in range(3):
        load_blocks(slot_ref, blocks, out, sem, 36 * which, 6, 6, 6 * which)
    wait_whole(out, sem)


def assemble(block_slot, blocks):
    return pl.pallas_call(
        assemble_kernel,
        grid_spec=pltpu.PrefetchScalarGridSpec(
            num_scalar_prefetch=1,
            grid=(1,),
            in_specs=[pl.BlockSpec(memory_space=pltpu.HBM)],
            out_specs=pl.BlockSpec(memory_space=pltpu.VMEM),
            scratch_shapes=[pltpu.SemaphoreType.DMA],
        ),
        out_shape=jax.ShapeDtypeStruct((D, 3 * D), BF16),
        compiler_params=pltpu.CompilerParams(vmem_limit_bytes=60 * MIB),
        name="assemble",
    )(block_slot, blocks)


QKV_PLACES = ((0, 6, 6), (36, 6, 6), (72, 6, 6))
OTHER_PLACES = ((108, 6, 6), (144, 6, 24), (288, 24, 6), (432, 6, 1), (438, 1, 1))


def spread_kernel(code_ref, empty_ref, *refs, places):
    grads = refs[: len(places)]
    zero, out, sems = refs[len(places) :]
    for which, (grad, place) in enumerate(zip(grads, places)):

        def move(block, row, col, which=which, grad=grad):
            pltpu.make_async_copy(
                grad.at[pl.ds(row, BLK), pl.ds(col, BLK)], out.at[code_ref[block]], sems.at[which]
            ).start()

        each_block(*place, move)
    for index in range(empty_ref.shape[0]):
        pltpu.make_async_copy(zero, out.at[empty_ref[index]], sems.at[len(places) + index]).start()
    for which, grad in enumerate(grads):
        wait_whole(grad, sems.at[which])
    for index in range(empty_ref.shape[0]):
        wait_whole(zero, sems.at[len(places) + index])


def spread(code, empty, grads, places, slot_count):
    vmem = pl.BlockSpec(memory_space=pltpu.VMEM)
    return pl.pallas_call(
        partial(spread_kernel, places=places),
        grid_spec=pltpu.PrefetchScalarGridSpec(
            num_scalar_prefetch=2,
            grid=(1,),
            in_specs=[vmem] * (len(grads) + 1),
            out_specs=pl.BlockSpec(memory_space=pltpu.HBM),
            scratch_shapes=[pltpu.SemaphoreType.DMA((len(grads) + empty.shape[0],))],
        ),
        out_shape=jax.ShapeDtypeStruct((slot_count, BLK, BLK), BF16),
        compiler_params=pltpu.CompilerParams(vmem_limit_bytes=44 * MIB),
        name="spread",
    )(code, empty, *grads, jnp.zeros((BLK, BLK), BF16))


def spread_late_kernel(code_ref, grad, small_ref, query_ref, value_ref, _, out, small_out, sem):
    for which, place in enumerate(QKV_PLACES):

        def move(block, row, col, which=which):
            pltpu.make_async_copy(
                grad.at[pl.ds(row, BLK), pl.ds(which * D + col, BLK)], out.at[code_ref[block]], sem
            ).start()

        each_block(*place, move)
    join_small(small_ref, query_ref, value_ref, small_out)
    wait_whole(grad, sem)


def join_small(small_ref, query_ref, value_ref, small_out):
    small_out[...] = small_ref[...]
    for start, ref in ((0, query_ref), (D // BLK, value_ref)):
        for index in range(D // BLK):
            small_out[start + index : start + index + 1, :] = ref[:, index * BLK : (index + 1) * BLK]


def spread_late(code, grad, small, g_query, g_value, terms):
    vmem = pl.BlockSpec(memory_space=pltpu.VMEM)
    anywhere = pl.BlockSpec(memory_space=pltpu.HBM)
    return pl.pallas_call(
        spread_late_kernel,
        grid_spec=pltpu.PrefetchScalarGridSpec(
            num_scalar_prefetch=1,
            grid=(1,),
            in_specs=[vmem] * 4 + [anywhere],
            out_specs=[anywhere, vmem],
            scratch_shapes=[pltpu.SemaphoreType.DMA],
        ),
        out_shape=[
            jax.ShapeDtypeStruct(terms.shape, BF16),
            jax.ShapeDtypeStruct(small.shape, F32),
        ],
        input_output_aliases={5: 0},
        compiler_params=pltpu.CompilerParams(vmem_limit_bytes=44 * MIB),
        name="spread_late",
    )(code, grad, small, g_query, g_value, terms)


def half_masks():
    lane = lax.broadcasted_iota(jnp.int32, (1, BLK), 1)
    low = (lane < BLK // 2).astype(BF16)
    return low, (1.0 - low.astype(F32)).astype(BF16)


def stack_heads(values, low, high):
    return jnp.concatenate([values * low, values * high], axis=0)


def pick_heads(values):
    rows = values.shape[0] // 2
    lane = lax.broadcasted_iota(jnp.int32, (rows, BLK), 1)
    return jnp.where(lane < BLK // 2, values[:rows], values[rows:])


def pipelined(count, before, middle, after):
    started = before(0)
    done = None
    for index in range(count):
        current = started
        if index + 1 < count:
            started = before(index + 1)
        if done is not None:
            after(index - 1, done)
        done = middle(index, current)
    after(count - 1, done)


def softmax(scores, length):
    visible = lax.broadcasted_iota(jnp.int32, scores.shape, 1) < length
    scores = jnp.where(visible, scores, MASKED_SCORE)
    powers = jnp.exp(scores - jnp.max(scores, axis=-1, keepdims=True))
    total = jnp.sum(powers, axis=-1, keepdims=True)
    return (powers * (1.0 / total)).astype(BF16)


def attention_kernel(
    len_short,
    len_long,
    x_short_ref,
    x_long_ref,
    params,
    w_ref,
    x_ref,
    q_ref,
    k_ref,
    v_ref,
    context_ref,
    short_ref,
    long_ref,
    bias,
    *,
    short_tiles,
):
    tile = pl.program_id(0)
    group = pl.program_id(1)
    low, high = half_masks()
    width = short_ref.shape[-1]
    per_tile = TILE // width

    wide = PAIRS * BLK
    start = pl.multiple_of(group * wide, wide)

    @pl.when((tile == 0) & (group == 0))
    def _():
        for which in range(2):
            for place in range(D // BLK):
                row = which * (D // BLK) + place
                bias[which : which + 1, place * BLK : (place + 1) * BLK] = params[row : row + 1, :]

    @pl.when((tile < short_tiles) & (group == 0))
    def _():
        x_ref[...] = x_short_ref[...]

    @pl.when((tile >= short_tiles) & (group == 0))
    def _():
        x_ref[...] = x_long_ref[...]

    rows_in = x_ref[...]
    queries = product(rows_in, w_ref[:, pl.ds(start, wide)]) + bias[0:1, pl.ds(start, wide)]
    q_ref[...] = (queries * 0.125).astype(BF16)
    k_ref[...] = product(rows_in, w_ref[:, pl.ds(D + start, wide)]).astype(BF16)
    values = product(rows_in, w_ref[:, pl.ds(2 * D + start, wide)]) + bias[1:2, pl.ds(start, wide)]
    v_ref[...] = values.astype(BF16)

    def attend(units, kept_ref):
        def scores(index):
            rows, keys, cols, _, _ = units[index]
            return right_product(stack_heads(q_ref[rows, cols], low, high), k_ref[keys, cols])

        def weigh(index, values):
            _, _, _, length, place = units[index]
            probs = softmax(values, length)
            kept_ref[place] = probs
            return probs

        def mix(index, probs):
            rows, keys, cols, _, _ = units[index]
            context_ref[rows, cols] = pick_heads(product(probs, v_ref[keys, cols])).astype(BF16)

        pipelined(len(units), scores, weigh, mix)

    @pl.when(tile < short_tiles)
    def _():
        def one(seq, carry):
            rows = pl.ds(pl.multiple_of(seq * width, width), width)
            length = len_short[tile * per_tile + seq]
            attend(
                [
                    (rows, rows, slice(pair * BLK, (pair + 1) * BLK), length, (0, pair, seq))
                    for pair in range(PAIRS)
                ],
                short_ref,
            )
            return carry

        lax.fori_loop(0, per_tile, one, 0)

    @pl.when(tile >= short_tiles)
    def _():
        length = len_long[tile - short_tiles]
        half = TILE // 2

        def one(pair, carry):
            cols = pl.ds(pl.multiple_of(pair * BLK, BLK), BLK)
            attend(
                [
                    (slice(part * half, (part + 1) * half), slice(0, TILE), cols, length, (0, pair, part))
                    for part in range(2)
                ],
                long_ref,
            )
            return carry

        lax.fori_loop(0, PAIRS, one, 0)


def run_events(step, events):
    for index, actions in enumerate(events):

        @pl.when(step == index)
        def _(actions=actions):
            for action in actions:
                action()


def probs_shapes(short_tiles, long_tiles, width):
    per_tile = TILE // width
    return (
        (short_tiles, 2 * PAIRS, per_tile, 2 * width, width),
        (long_tiles, 2 * PAIRS, 2, TILE, TILE),
    )


def short_index(tile, short_tiles):
    return jnp.minimum(tile, short_tiles - 1)


def long_index(tile, short_tiles):
    return jnp.maximum(tile - short_tiles, 0)


def probs_maps(short_tiles):
    def short_map(tile, group):
        last = jnp.minimum(tile // short_tiles, 1)
        return (short_index(tile, short_tiles), group + last * (GROUPS - 1 - group), 0, 0, 0)

    def long_map(tile, group):
        begun = jnp.minimum(tile // short_tiles, 1)
        return (long_index(tile, short_tiles), begun * group, 0, 0, 0)

    return short_map, long_map


def attention(len_short, len_long, x_short, x_long, params, w_qkv, short_tiles, width):
    tiles = (x_short.shape[0] + x_long.shape[0]) // TILE
    wide = PAIRS * BLK
    short_shape, long_shape = probs_shapes(short_tiles, tiles - short_tiles, width)
    short_map, long_map = probs_maps(short_tiles)
    flops = 4 * D * TILE * TILE * tiles + 6 * D * D * TILE * tiles
    rows = pl.BlockSpec((TILE, wide), lambda tile, group: (tile, group))
    scalars = pl.BlockSpec(memory_space=pltpu.SMEM)

    def whole(shape):
        return pl.BlockSpec(shape, lambda tile, group: (0,) * len(shape), pipeline_mode=pl.Buffered(1))

    in_specs = [
        scalars,
        scalars,
        pl.BlockSpec((TILE, D), lambda tile, group: (short_index(tile, short_tiles), 0)),
        pl.BlockSpec((TILE, D), lambda tile, group: (long_index(tile, short_tiles), 0)),
        whole(params.shape),
        whole((D, 3 * D)),
    ]
    out_specs = [
        pl.BlockSpec((TILE, D), lambda tile, group: (tile, 0)),
        rows,
        rows,
        rows,
        rows,
        pl.BlockSpec((1, PAIRS) + short_shape[2:], short_map),
        pl.BlockSpec((1, PAIRS) + long_shape[2:], long_map),
    ]
    out_shape = [jax.ShapeDtypeStruct((tiles * TILE, D), BF16)] * 5 + [
        jax.ShapeDtypeStruct(short_shape, BF16),
        jax.ShapeDtypeStruct(long_shape, BF16),
    ]
    arguments = [len_short, len_long, x_short, x_long, params, w_qkv]
    return pl.pallas_call(
        partial(attention_kernel, short_tiles=short_tiles),
        grid=(tiles, GROUPS),
        in_specs=in_specs,
        out_specs=out_specs,
        out_shape=out_shape,
        scratch_shapes=[pltpu.VMEM((8, D), F32)],
        compiler_params=pltpu.CompilerParams(vmem_limit_bytes=60 * MIB),
        cost_estimate=pl.CostEstimate(
            flops=flops, bytes_accessed=35 * MIB, transcendentals=HEADS * TILE * TILE * tiles // 2
        ),
        name="attention",
    )(*arguments)


def attention_back_kernel(*refs, short_tiles, transfers):
    q_ref, k_ref, v_ref, short_ref, long_ref, dc_ref = refs[:6]
    refs = refs[6:]
    if transfers:
        terms_ref, refs = refs[0], refs[1:]
    out_ref, bq_ref, bv_ref = refs[:3]
    tile = pl.program_id(0)
    group = pl.program_id(1)
    low, high = half_masks()
    width = short_ref.shape[-1]
    per_tile = TILE // width
    if transfers:
        reduce = Reduce(terms_ref, 0, refs[3], refs[4:])
        run_events(
            tile * GROUPS + group,
            (
                (reduce.start,),
                (partial(reduce.core, 0),),
                (partial(reduce.core, 1), partial(reduce.first, 0)),
                (partial(reduce.core, 2), partial(reduce.first, 1), partial(reduce.second, 0)),
                (partial(reduce.core, 3), partial(reduce.first, 2), partial(reduce.second, 1)),
                (partial(reduce.first, 3), partial(reduce.second, 2)),
                (partial(reduce.second, 3), reduce.share),
                (reduce.share_on,),
            ),
        )

    wide = PAIRS * BLK
    start = pl.multiple_of(group * wide, wide)

    def columns(which, pair):
        return pl.ds(pl.multiple_of(which * D + start + pair * BLK, BLK), BLK)

    def pair_columns(pair):
        return pl.ds(pl.multiple_of(pair * BLK, BLK), BLK)

    def go_back(units, kept_ref, parts):
        sums = {}

        def spread_in(index):
            rows, keys, pair, _ = units[index]
            cols = pair_columns(pair)
            return right_product(stack_heads(dc_ref[rows, cols], low, high), v_ref[keys, cols])

        def differ(index, d_probs):
            wide = kept_ref[units[index][3]].astype(F32)
            weighted = wide * d_probs
            return (weighted - wide * jnp.sum(weighted, axis=-1, keepdims=True)).astype(BF16)

        def gather_up(index, d_scores):
            rows, keys, pair, place = units[index]
            cols = pair_columns(pair)
            d_queries = pick_heads(product(d_scores, k_ref[keys, cols])) * 0.125
            out_ref[rows, columns(0, pair)] = d_queries.astype(BF16)
            d_keys = left_product(d_scores, stack_heads(q_ref[rows, cols], low, high))
            d_values = left_product(kept_ref[place], stack_heads(dc_ref[rows, cols], low, high))
            if index % parts:
                d_keys += sums["keys"]
                d_values += sums["values"]
            if index % parts == parts - 1:
                out_ref[keys, columns(1, pair)] = d_keys.astype(BF16)
                out_ref[keys, columns(2, pair)] = d_values.astype(BF16)
            else:
                sums.update(keys=d_keys, values=d_values)

        pipelined(len(units), spread_in, differ, gather_up)

    @pl.when(tile < short_tiles)
    def _():
        def one(seq, carry):
            rows = pl.ds(pl.multiple_of(seq * width, width), width)
            go_back([(rows, rows, pair, (0, pair, seq)) for pair in range(PAIRS)], short_ref, 1)
            return carry

        lax.fori_loop(0, per_tile, one, 0)

    @pl.when(tile >= short_tiles)
    def _():
        half = TILE // 2

        def one(pair, carry):
            go_back(
                [
                    (slice(part * half, (part + 1) * half), slice(0, TILE), pair, (0, pair, part))
                    for part in range(2)
                ],
                long_ref,
                2,
            )
            return carry

        lax.fori_loop(0, PAIRS, one, 0)

    @pl.when((tile == 0) & (group == 0))
    def _():
        bq_ref[...] = jnp.zeros_like(bq_ref)
        bv_ref[...] = jnp.zeros_like(bv_ref)

    bq_ref[:, pl.ds(start, wide)] += column_sum(out_ref[:, pl.ds(start, wide)])
    bv_ref[:, pl.ds(start, wide)] += column_sum(out_ref[:, pl.ds(2 * D + start, wide)])

    if transfers:

        @pl.when((tile == pl.num_programs(0) - 1) & (group == GROUPS - 1))
        def _():
            reduce.finish()


def attention_back(qkv, probs_short, probs_long, d_context, short_tiles, terms=None, count=0):
    tiles = d_context.shape[0] // TILE
    wide = PAIRS * BLK
    short_map, long_map = probs_maps(short_tiles)
    rows = pl.BlockSpec((TILE, wide), lambda tile, group: (tile, group))
    row = pl.BlockSpec((1, D), lambda tile, group: (0, 0))
    flops = 10 * D * TILE * TILE * tiles
    in_specs = [
        rows,
        rows,
        rows,
        pl.BlockSpec((1, PAIRS) + probs_short.shape[2:], short_map),
        pl.BlockSpec((1, PAIRS) + probs_long.shape[2:], long_map),
        rows,
    ]
    out_specs = [pl.BlockSpec((TILE, 3 * D), lambda tile, group: (tile, 0)), row, row]
    out_shape = [
        jax.ShapeDtypeStruct((tiles * TILE, 3 * D), BF16),
        jax.ShapeDtypeStruct((1, D), F32),
        jax.ShapeDtypeStruct((1, D), F32),
    ]
    arguments = [*qkv, probs_short, probs_long, d_context]
    scratch = []
    params = dict(vmem_limit_bytes=60 * MIB)
    if terms is not None:
        arguments.append(terms)
        in_specs.append(pl.BlockSpec(memory_space=pltpu.HBM))
        out_specs.append(pl.BlockSpec((count, BLK), lambda tile, group: (0, 0)))
        out_shape.append(jax.ShapeDtypeStruct((count, BLK), BF16))
        scratch = reduce_scratch(count)
        params.update(collective_id=2, has_side_effects=True)
    return pl.pallas_call(
        partial(attention_back_kernel, short_tiles=short_tiles, transfers=terms is not None),
        grid=(tiles, GROUPS),
        in_specs=in_specs,
        out_specs=out_specs,
        out_shape=out_shape,
        scratch_shapes=scratch,
        compiler_params=pltpu.CompilerParams(**params),
        cost_estimate=pl.CostEstimate(flops=flops, bytes_accessed=50 * MIB, transcendentals=0),
        name="attention_back",
    )(*arguments)


INPUT_ROWS = 256


def input_product(d_ref, resid_ref, w_ref, short_ref, long_ref, short_steps):
    step = pl.program_id(0)
    total = resid_ref[...] + right_product(d_ref[...], w_ref[...])

    @pl.when(step < short_steps)
    def _():
        short_ref[...] = total

    @pl.when(step >= short_steps)
    def _():
        long_ref[...] = total


def input_specs(short_steps):
    rows = [pl.BlockSpec((INPUT_ROWS, width), lambda step: (step, 0)) for width in (3 * D, D)]
    whole = pl.BlockSpec((D, 3 * D), lambda step: (0, 0), pipeline_mode=pl.Buffered(1))
    outs = [
        pl.BlockSpec((INPUT_ROWS, D), lambda step: (short_index(step, short_steps), 0)),
        pl.BlockSpec((INPUT_ROWS, D), lambda step: (long_index(step, short_steps), 0)),
    ]
    return rows + [whole], outs


def input_grads(d_qkv, resid, w_qkv, short_tiles):
    steps = resid.shape[0] // INPUT_ROWS
    short_steps = short_tiles * TILE // INPUT_ROWS
    in_specs, out_specs = input_specs(short_steps)
    return pl.pallas_call(
        partial(input_product, short_steps=short_steps),
        grid=(steps,),
        in_specs=in_specs,
        out_specs=out_specs,
        out_shape=[
            jax.ShapeDtypeStruct((short_steps * INPUT_ROWS, D), F32),
            jax.ShapeDtypeStruct(((steps - short_steps) * INPUT_ROWS, D), F32),
        ],
        compiler_params=pltpu.CompilerParams(vmem_limit_bytes=60 * MIB),
        name="input_grads",
    )(d_qkv, resid, w_qkv)


def normal_parts(values):
    below = 0.5 * lax.erf(values * 0.7071067811865476) + 0.5
    return below, jnp.exp(-0.5 * values * values) * 0.3989422804014327


B_OUT, GAIN_ONE, SHIFT_ONE, B_UP, B_DOWN, GAIN_TWO, SHIFT_TWO, B_STUDENT, POOL_QUERY, B_HIDDEN = range(10)
VECTORS = (
    (12, 6),
    (18, 6),
    (24, 6),
    (30, 24),
    (54, 6),
    (60, 6),
    (66, 6),
    (72, 1),
    (73, 1),
    (74, 1),
)
CLASS_ROW = 75
LAST_ROW = 91
SMALL_ROWS = 96


def norm_parts(values):
    center = values - jnp.mean(values, axis=-1, keepdims=True)
    spread = jnp.mean(center * center, axis=-1, keepdims=True)
    inverse = lax.rsqrt(spread + NORM_EPSILON)
    return center * inverse, inverse


def norm_back(d_values, gain, unit, inverse):
    d_unit = d_values * gain
    return inverse * (
        d_unit
        - jnp.mean(d_unit, axis=-1, keepdims=True)
        - unit * jnp.mean(d_unit * unit, axis=-1, keepdims=True)
    )


def column_sum(values):
    return jnp.sum(values.astype(F32), axis=0, keepdims=True)


def pool_weights(student, query, length):
    scaled = student * query
    lane = lax.broadcasted_iota(jnp.int32, scaled.shape, 1)
    place = lax.broadcasted_iota(jnp.int32, (scaled.shape[0], 1), 0)
    weights = []
    for side in (lane < SD // PH, lane >= SD // PH):
        scores = jnp.sum(jnp.where(side, scaled, 0.0), axis=-1, keepdims=True)
        scores = jnp.where(place < length, scores, MASKED_SCORE)
        powers = jnp.exp(scores - jnp.max(scores, axis=0, keepdims=True))
        weights.append(powers / jnp.sum(powers, axis=0, keepdims=True))
    return jnp.where(lane < SD // PH, weights[0], weights[1]), weights


def student_back(student, query, weights, both, d_pooled):
    lane = lax.broadcasted_iota(jnp.int32, student.shape, 1)
    moved = student * d_pooled
    d_scores = []
    for side, weight in zip((lane < SD // PH, lane >= SD // PH), weights):
        d_weight = jnp.sum(jnp.where(side, moved, 0.0), axis=-1, keepdims=True)
        d_scores.append(weight * (d_weight - jnp.sum(weight * d_weight, axis=0, keepdims=True)))
    d_score = jnp.where(lane < SD // PH, d_scores[0], d_scores[1])
    d_query = jnp.sum(d_score * student, axis=0, keepdims=True) * 0.125
    return both * d_pooled + d_score * query, d_query


def feed_kernel(
    len_short,
    len_long,
    slot_ref,
    x_ref,
    context_ref,
    cot_short_ref,
    cot_long_ref,
    logit_cot_ref,
    params,
    w_class,
    b_class,
    blocks,
    enc_short_ref,
    enc_long_ref,
    logit_ref,
    first_ref,
    active_ref,
    d_up_ref,
    d_down_ref,
    d_branch_ref,
    d_context_ref,
    d_resid_ref,
    g_student,
    g_hidden,
    g_small,
    slope,
    pooled_ref,
    d_student_ref,
    w_out,
    w_up,
    w_down,
    w_student,
    w_hidden,
    vectors,
    totals,
    g_class,
    g_last,
    work,
    unit_one,
    unit_two,
    inverse_one,
    inverse_two,
    encoded_ref,
    sems,
    *,
    short_tiles,
    width,
):
    tile = pl.program_id(0)
    per_tile = TILE // width
    loads = ((w_out, 108, 6, 6), (w_up, 144, 6, 24), (w_down, 288, 24, 6), (w_student, 432, 6, 1), (w_hidden, 438, 1, 1))

    def arrive(*indices):
        @pl.when(tile == 0)
        def _():
            for index in indices:
                wait_whole(loads[index][0], sems.at[index])

    @pl.when(tile == 0)
    def _():
        for index, (target, block, row_count, col_count) in enumerate(loads):
            load_blocks(slot_ref, blocks, target, sems.at[index], block, row_count, col_count)
        for index, (start, count) in enumerate(VECTORS):
            for place in range(count):
                vectors[index : index + 1, place * BLK : (place + 1) * BLK] = params[
                    start + place : start + place + 1, :
                ]
        for ref in (totals, g_class, g_last, g_student, g_hidden):
            ref[...] = jnp.zeros_like(ref)

    def vector(index):
        return vectors[index : index + 1, : VECTORS[index][1] * BLK]

    def add_total(index, values):
        totals[index : index + 1, : VECTORS[index][1] * BLK] += column_sum(values)

    def by_rows(action):
        def one(index, carry):
            action(pl.ds(pl.multiple_of(index * ROWS, ROWS), ROWS))
            return carry

        lax.fori_loop(0, TILE // ROWS, one, 0)

    def by_columns(count, size, action):
        def one(index, carry):
            action(pl.ds(pl.multiple_of(index * size, size), size))
            return carry

        lax.fori_loop(0, count // size, one, 0)

    arrive(0)

    def branch(cols):
        work[:, cols] = product(context_ref[...], w_out[:, cols])

    by_columns(D, WIDE, branch)

    def norm_first(rows):
        unit, inverse = norm_parts(x_ref[rows].astype(F32) + (work[rows] + vector(B_OUT)))
        inverse_one[rows] = inverse
        unit_one[rows] = unit
        first_ref[rows] = (unit * vector(GAIN_ONE) + vector(SHIFT_ONE)).astype(BF16)

    by_rows(norm_first)
    arrive(1)

    def rise(cols):
        upward = product(first_ref[...], w_up[:, cols]) + vectors[B_UP : B_UP + 1, cols]
        below, density = normal_parts(upward)
        active_ref[:, cols] = (upward * below).astype(BF16)
        slope[:, cols] = (below + upward * density).astype(BF16)

    by_columns(FF, CHUNK, rise)
    arrive(2, 3, 4)

    def sink(cols):
        work[:, cols] = product(active_ref[...], w_down[:, cols])

    by_columns(D, WIDE, sink)

    def norm_second(rows):
        unit, inverse = norm_parts(first_ref[rows].astype(F32) + (work[rows] + vector(B_DOWN)))
        inverse_two[rows] = inverse
        unit_two[rows] = unit
        encoded_ref[rows] = (unit * vector(GAIN_TWO) + vector(SHIFT_TWO)).astype(BF16)

    by_rows(norm_second)
    encoded = encoded_ref[...]

    @pl.when(tile < short_tiles)
    def _():
        enc_short_ref[...] = encoded

    @pl.when(tile >= short_tiles)
    def _():
        enc_long_ref[...] = encoded

    student = product(encoded, w_student[...]) + vector(B_STUDENT)
    query = vector(POOL_QUERY) * 0.125
    pooled_ref[...] = jnp.zeros_like(pooled_ref)

    def head():
        pooled = pooled_ref[...]
        wide_hidden = w_hidden[...].astype(F32)
        hidden = jnp.tanh(product(pooled, wide_hidden, HIGHEST_PRECISION) + vector(B_HIDDEN))
        logit_ref[0] = product(hidden, w_class[...], HIGHEST_PRECISION) + b_class[...]
        d_logits = logit_cot_ref[0]
        g_last[...] += column_sum(d_logits)
        g_class[...] += left_product(d_logits, hidden, HIGHEST_PRECISION)
        d_hidden = right_product(d_logits, w_class[...], HIGHEST_PRECISION)
        d_hidden = d_hidden * (1.0 - hidden * hidden)
        add_total(B_HIDDEN, d_hidden)
        g_hidden[...] += left_product(pooled, d_hidden, HIGHEST_PRECISION)
        return right_product(d_hidden, wide_hidden, HIGHEST_PRECISION)

    def pool(starts, size, lengths):
        kept = []
        for index, (start, length) in enumerate(zip(starts, lengths)):
            rows = student[start : start + size]
            both, weights = pool_weights(rows, query, length)
            pooled_ref[index : index + 1, :] = column_sum(both * rows)
            kept.append((start, rows, both, weights))
        d_pooled = head()
        for index, (start, rows, both, weights) in enumerate(kept):
            d_rows, d_query = student_back(rows, query, weights, both, d_pooled[index : index + 1])
            d_student_ref[start : start + size, :] = d_rows.astype(BF16)
            add_total(POOL_QUERY, d_query)

    @pl.when(tile < short_tiles)
    def _():
        pool(
            [seq * width for seq in range(per_tile)],
            width,
            [len_short[tile * per_tile + seq] for seq in range(per_tile)],
        )

    @pl.when(tile >= short_tiles)
    def _():
        pool([0], TILE, [len_long[tile - short_tiles]])

    d_student = d_student_ref[...]
    add_total(B_STUDENT, d_student)
    g_student[...] += left_product(encoded, d_student)
    work[...] = right_product(d_student, w_student[...])

    def norm_second_back(rows):
        cotangent = jnp.where(tile < short_tiles, cot_short_ref[rows], cot_long_ref[rows])
        d_second = cotangent.astype(F32) + work[rows]
        unit = unit_two[rows]
        add_total(GAIN_TWO, d_second * unit)
        add_total(SHIFT_TWO, d_second)
        d_resid = norm_back(d_second, vector(GAIN_TWO), unit, inverse_two[rows])
        unit_two[rows] = d_resid
        d_down = d_resid.astype(BF16)
        d_down_ref[rows] = d_down
        add_total(B_DOWN, d_down)

    by_rows(norm_second_back)

    def fall(cols):
        d_active = right_product(d_down_ref[...], w_down[cols, :])
        d_up = (d_active * slope[:, cols].astype(F32)).astype(BF16)
        d_up_ref[:, cols] = d_up
        totals[B_UP : B_UP + 1, cols] += column_sum(d_up)

    by_columns(FF, CHUNK, fall)

    def rise_back(cols):
        work[:, cols] = right_product(d_up_ref[...], w_up[cols, :])

    by_columns(D, WIDE, rise_back)

    def norm_first_back(rows):
        d_first = unit_two[rows] + work[rows]
        unit = unit_one[rows]
        add_total(GAIN_ONE, d_first * unit)
        add_total(SHIFT_ONE, d_first)
        d_resid = norm_back(d_first, vector(GAIN_ONE), unit, inverse_one[rows])
        d_resid_ref[rows] = d_resid
        d_branch = d_resid.astype(BF16)
        d_branch_ref[rows] = d_branch
        add_total(B_OUT, d_branch)

    by_rows(norm_first_back)

    def branch_back(cols):
        d_context_ref[:, cols] = right_product(d_branch_ref[...], w_out[cols, :]).astype(BF16)

    by_columns(D, WIDE, branch_back)

    @pl.when(tile == pl.num_programs(0) - 1)
    def _():
        g_small[...] = jnp.zeros_like(g_small)
        for index, (start, count) in enumerate(VECTORS):
            for place in range(count):
                g_small[start + place : start + place + 1, :] = totals[
                    index : index + 1, place * BLK : (place + 1) * BLK
                ]
        g_small[CLASS_ROW : CLASS_ROW + NCLS, :] = g_class[:NCLS, :]
        g_small[LAST_ROW : LAST_ROW + 1, :] = g_last[...]


def feed(
    len_short, len_long, block_slot, x, context, cot_short, cot_long, logit_cot, small, blocks, short_tiles, width
):
    tiles = x.shape[0] // TILE
    long_tiles = tiles - short_tiles

    def whole(shape):
        return pl.BlockSpec(shape, lambda tile, *_: (0,) * len(shape), pipeline_mode=pl.Buffered(1))

    def kept(shape):
        return pl.BlockSpec(shape, lambda tile, *_: (0,) * len(shape))

    def rows(columns):
        return pl.BlockSpec((TILE, columns), lambda tile, *_: (tile, 0))

    short_rows = pl.BlockSpec((TILE, D), lambda tile, *_: (short_index(tile, short_tiles), 0))
    long_rows = pl.BlockSpec((TILE, D), lambda tile, *_: (long_index(tile, short_tiles), 0))
    logit_rows = pl.BlockSpec((1, 8, SD), lambda tile, *_: (tile, 0, 0))
    grad_shapes = ((D, SD), (SD, SD), (SMALL_ROWS, BLK))
    total = tiles * TILE
    return pl.pallas_call(
        partial(feed_kernel, short_tiles=short_tiles, width=width),
        grid_spec=pltpu.PrefetchScalarGridSpec(
            num_scalar_prefetch=3,
            grid=(tiles,),
            in_specs=[rows(D), rows(D), short_rows, long_rows, logit_rows]
            + [whole(array.shape) for array in small]
            + [pl.BlockSpec(memory_space=pltpu.HBM)],
            out_specs=[
                short_rows,
                long_rows,
                logit_rows,
                rows(D),
                rows(FF),
                rows(FF),
                rows(D),
                rows(D),
                rows(D),
                rows(D),
            ]
            + [kept(shape) for shape in grad_shapes],
            scratch_shapes=[
                pltpu.VMEM((TILE, FF), BF16),
                pltpu.VMEM((8, SD), F32),
                pltpu.VMEM((TILE, SD), BF16),
                pltpu.VMEM((D, D), BF16),
                pltpu.VMEM((D, FF), BF16),
                pltpu.VMEM((FF, D), BF16),
                pltpu.VMEM((D, SD), BF16),
                pltpu.VMEM((SD, SD), BF16),
                pltpu.VMEM((16, FF), F32),
                pltpu.VMEM((16, FF), F32),
                pltpu.VMEM((SD, SD), F32),
                pltpu.VMEM((1, SD), F32),
                pltpu.VMEM((TILE, D), F32),
                pltpu.VMEM((TILE, D), F32),
                pltpu.VMEM((TILE, D), F32),
                pltpu.VMEM((TILE, 1), F32),
                pltpu.VMEM((TILE, 1), F32),
                pltpu.VMEM((TILE, D), BF16),
                pltpu.SemaphoreType.DMA((5,)),
            ],
        ),
        out_shape=[
            jax.ShapeDtypeStruct((short_tiles * TILE, D), BF16),
            jax.ShapeDtypeStruct((long_tiles * TILE, D), BF16),
            jax.ShapeDtypeStruct((tiles, 8, SD), F32),
            jax.ShapeDtypeStruct((total, D), BF16),
            jax.ShapeDtypeStruct((total, FF), BF16),
            jax.ShapeDtypeStruct((total, FF), BF16),
            jax.ShapeDtypeStruct((total, D), BF16),
            jax.ShapeDtypeStruct((total, D), BF16),
            jax.ShapeDtypeStruct((total, D), BF16),
            jax.ShapeDtypeStruct((total, D), F32),
        ]
        + [jax.ShapeDtypeStruct(shape, F32) for shape in grad_shapes],
        compiler_params=pltpu.CompilerParams(vmem_limit_bytes=62 * MIB),
        cost_estimate=pl.CostEstimate(
            flops=total * (8 * D * FF + 4 * D * D), bytes_accessed=70 * MIB, transcendentals=total * FF
        ),
        name="feed",
    )(len_short, len_long, block_slot, x, context, cot_short, cot_long, logit_cot, *small, blocks)


class Place:
    def __init__(self):
        self.quarter = lax.axis_index("dp")
        self.shard = lax.axis_index("fsdp")
        x = self.quarter % 2
        y = self.quarter // 2
        self.core = self.shard % 2
        self.z = self.shard // 2
        self.high = self.z // 2
        self.by_x = 2 * y + 1 - x
        self.by_y = 2 * (1 - y) + x
        self.across = 2 * (1 - y) + 1 - x
        self.sibling = (self.quarter, 2 * self.z + 1 - self.core)
        self.next_x = (self.by_x, self.shard)
        self.next_y = (self.by_y, self.shard)
        self.inner = (self.z > 0) & (self.z < 3)

    def at_z(self, z):
        return (self.quarter, 2 * z + self.core)


def transfer(source, target, send_sem, recv_sem, device):
    return pltpu.make_async_remote_copy(
        src_ref=source,
        dst_ref=target,
        send_sem=send_sem,
        recv_sem=recv_sem,
        device_id=device,
        device_id_type=pl.DeviceIdType.MESH,
    )


def greet(place, extra=()):
    barrier = pltpu.get_barrier_semaphore()

    def signal(device):
        pl.semaphore_signal(barrier, inc=1, device_id=device, device_id_type=pl.DeviceIdType.MESH)

    near = (place.sibling, place.next_x, place.next_y) + tuple(extra)
    for device in near:
        signal(device)

    @pl.when(place.z > 0)
    def _():
        signal(place.at_z(place.z - 1))

    @pl.when(place.z < 3)
    def _():
        signal(place.at_z(place.z + 1))

    pl.semaphore_wait(barrier, len(near) + 1 + (place.z + 1) // 2 % 2)


CUTS = 2
GATHER_SEMAPHORES = [
    pltpu.SemaphoreType.DMA((2 * CUTS,)),
    pltpu.SemaphoreType.DMA((3 * CUTS,)),
    pltpu.SemaphoreType.DMA((4 * CUTS,)),
    pltpu.SemaphoreType.DMA((12 * CUTS,)),
    pltpu.SemaphoreType.DMA((12 * CUTS,)),
    pltpu.SemaphoreType.DMA((1 + 15 * CUTS,)),
    pltpu.SemaphoreType.DMA((1 + 15 * CUTS,)),
    pltpu.SemaphoreType.DMA((8,)),
]


class Gather:
    def __init__(self, full, out, sems):
        self.place = place = Place()
        self.full, self.out = full, out
        (
            self.own_send,
            self.relay_send,
            self.z_recv,
            self.xy_send,
            self.xy_recv,
            self.core_send,
            self.core_recv,
            self.out_sems,
        ) = sems
        self.quarter = full.shape[1] // 4
        self.cut = self.quarter // CUTS
        self.first_part = (self.cut // 16 + 1) // 2 * 16
        z = place.z
        self.origins = (z + 1 - 2 * (z % 2), 2 - place.high, 3 * (1 - place.high))
        self.relays = (3 - z, 3 * (z - 1), 3 * (z - 1))

    def region(self, which, start, size):
        return self.full.at[which, pl.ds(pl.multiple_of(start, 16), size)]

    def pieces(self, which, turn):
        place, quarter, cut, part = self.place, self.quarter, self.cut, self.first_part
        skip = turn % CUTS * cut
        return (
            self.region(which, place.quarter * quarter + skip, cut),
            self.region(which, place.by_x * quarter + skip, cut),
            self.region(which, place.by_y * quarter + skip, cut),
            self.region(which, place.across * quarter + skip, part),
            self.region(which, place.across * quarter + skip + part, cut - part),
        )

    def own_copy(self, side, cut):
        place = self.place
        mine = self.pieces(place.shard, cut)[0]
        device = place.at_z(place.z - 1 + 2 * side)
        return transfer(
            mine,
            mine,
            self.own_send.at[side * CUTS + cut],
            self.z_recv.at[place.z * CUTS + cut],
            device,
        )

    def core_copy(self, index, ref):
        return transfer(ref, ref, self.core_send.at[index], self.core_recv.at[index], self.place.sibling)

    def xy_copy(self, index, ref, device):
        return transfer(ref, ref, self.xy_send.at[index], self.xy_recv.at[index], device)

    def store(self, index, which):
        return pltpu.make_async_copy(self.full.at[which], self.out.at[which], self.out_sems.at[index])

    def mirrored(self, step):
        return 2 * self.origins[step] + 1 - self.place.core

    def held(self, step):
        return 2 * self.origins[step] + self.place.core

    def start(self):
        place = self.place
        greet(place)
        for cut in range(CUTS):

            @pl.when(place.z > 0)
            def _():
                self.own_copy(0, cut).start()

            @pl.when(place.z < 3)
            def _():
                self.own_copy(1, cut).start()

        self.core_copy(0, self.full.at[place.shard]).start()
        self.store(0, place.shard).start()

    def relay(self, turn):
        step = turn // CUTS
        piece = self.pieces(self.held(step), turn)[0]
        device = self.place.at_z(self.relays[step])
        sem = self.z_recv.at[self.origins[step] * CUTS + turn % CUTS]
        return transfer(piece, piece, self.relay_send.at[turn], sem, device)

    def along_z(self, turn):
        place = self.place
        self.relay(turn).wait_recv()

        @pl.when(place.inner)
        def _():
            self.relay(turn).start()

        piece = self.pieces(self.held(turn // CUTS), turn)[0]
        self.xy_copy(4 * turn, piece, place.next_x).start()
        self.xy_copy(4 * turn + 1, piece, place.next_y).start()
        self.core_copy(1 + 5 * turn, piece).start()

    def along_xy(self, turn):
        place, part = self.place, self.first_part
        _, by_x, by_y, _, _ = self.pieces(self.held(turn // CUTS), turn)
        self.xy_copy(4 * turn, by_x, place.next_x).wait_recv()
        self.xy_copy(4 * turn + 2, by_x.at[pl.ds(0, part)], place.next_y).start()
        self.core_copy(2 + 5 * turn, by_x).start()
        self.xy_copy(4 * turn + 1, by_y, place.next_y).wait_recv()
        self.xy_copy(4 * turn + 3, by_y.at[pl.ds(part, self.cut - part)], place.next_x).start()
        self.core_copy(3 + 5 * turn, by_y).start()

    def across(self, turn):
        place = self.place
        step = turn // CUTS
        _, _, _, first, last = self.pieces(self.held(step), turn)
        self.xy_copy(4 * turn + 2, first, place.next_y).wait_recv()
        self.core_copy(4 + 5 * turn, first).start()
        self.xy_copy(4 * turn + 3, last, place.next_x).wait_recv()
        self.core_copy(5 + 5 * turn, last).start()
        if turn % CUTS == CUTS - 1:
            self.store(2 + 2 * step, self.held(step)).start()

    def core_own(self):
        which = 2 * self.place.z + 1 - self.place.core
        self.core_copy(0, self.full.at[which]).wait_recv()
        self.store(1, which).start()

    def core(self, step):
        which = self.mirrored(step)
        for turn in range(step * CUTS, (step + 1) * CUTS):
            for index, ref in enumerate(self.pieces(which, turn)):
                self.core_copy(1 + 5 * turn + index, ref).wait_recv()
        self.store(3 + 2 * step, which).start()

    def finish(self):
        place = self.place
        for cut in range(CUTS):

            @pl.when(place.z > 0)
            def _():
                self.own_copy(0, cut).wait_send()

            @pl.when(place.z < 3)
            def _():
                self.own_copy(1, cut).wait_send()

        self.core_copy(0, self.full.at[place.shard]).wait_send()
        self.store(0, place.shard).wait()
        self.store(1, 2 * place.z + 1 - place.core).wait()
        for turn in range(3 * CUTS):

            @pl.when(place.inner)
            def _():
                self.relay(turn).wait_send()

            pieces = self.pieces(self.held(turn // CUTS), turn)
            self.xy_copy(4 * turn, pieces[0], place.next_x).wait_send()
            self.xy_copy(4 * turn + 1, pieces[0], place.next_y).wait_send()
            self.xy_copy(4 * turn + 2, pieces[3], place.next_y).wait_send()
            self.xy_copy(4 * turn + 3, pieces[4], place.next_x).wait_send()
            for index, ref in enumerate(pieces):
                self.core_copy(1 + 5 * turn + index, ref).wait_send()
        for step in range(3):
            self.store(2 + 2 * step, self.held(step)).wait()
            self.store(3 + 2 * step, self.mirrored(step)).wait()


def gather_kernel(master_ref, out_ref, full, *sems):
    gather = Gather(full, out_ref, sems)
    full[gather.place.shard] = master_ref[...].astype(BF16)
    gather.start()
    turns = 3 * CUTS
    for turn in range(turns + 2):
        if turn < turns:
            gather.along_z(turn)
        if 1 <= turn <= turns:
            gather.along_xy(turn - 1)
        if turn >= 2:
            gather.across(turn - 2)
        if turn == 2:
            gather.core_own()
        if turn >= 4 and turn % CUTS == 0:
            gather.core(turn // CUTS - 2)
    gather.core(2)
    gather.finish()


def gather_shards(master):
    rows = master.shape[0] * BLK
    shards = lax.axis_size("fsdp")
    return pl.pallas_call(
        gather_kernel,
        in_specs=[pl.BlockSpec(memory_space=pltpu.VMEM)],
        out_specs=pl.BlockSpec(memory_space=pltpu.HBM),
        out_shape=jax.ShapeDtypeStruct((shards, rows, BLK), BF16),
        scratch_shapes=[pltpu.VMEM((shards, rows, BLK), BF16)] + GATHER_SEMAPHORES,
        compiler_params=pltpu.CompilerParams(
            collective_id=0, has_side_effects=True, vmem_limit_bytes=60 * MIB
        ),
        cost_estimate=pl.CostEstimate(flops=0, bytes_accessed=200 * MIB, transcendentals=0),
        name="gather",
    )(master.reshape(rows, BLK)).reshape(-1, BLK, BLK)


def add_rows(target, former, latter, rows, step):
    @pl.loop(0, rows // step)
    def _(index):
        part = pl.ds(pl.multiple_of(index * step, 16), step)
        target[part] = (former[part].astype(F32) + latter[part].astype(F32)).astype(BF16)


def reduce_scratch(rows):
    quarter = rows // 4
    half = quarter // 2
    return [
        pltpu.VMEM((4, rows, BLK), BF16),
        pltpu.VMEM((4, rows, BLK), BF16),
        pltpu.VMEM((4, 2, half, BLK), BF16),
        pltpu.VMEM((4, 2, half, BLK), BF16),
        pltpu.VMEM((4, half, BLK), BF16),
        pltpu.VMEM((4, half, BLK), BF16),
        pltpu.VMEM((5, quarter, BLK), BF16),
        pltpu.VMEM((rows, BLK), BF16),
        pltpu.SemaphoreType.DMA((4,)),
        pltpu.SemaphoreType.DMA((4,)),
        pltpu.SemaphoreType.DMA((4,)),
        pltpu.SemaphoreType.DMA((24,)),
        pltpu.SemaphoreType.DMA((24,)),
        pltpu.SemaphoreType.DMA((3,)),
        pltpu.SemaphoreType.DMA((5,)),
        pltpu.SemaphoreType.DMA((4,)),
        pltpu.SemaphoreType.DMA((4,)),
    ]


class Reduce:
    def __init__(self, terms, base, out, scratch):
        self.place = place = Place()
        self.terms, self.base, self.out = terms, base, out
        (
            self.mine,
            self.sib,
            self.from_x,
            self.from_y,
            self.late_y,
            self.late_x,
            self.from_z,
            self.result,
            self.load_sems,
            self.core_send,
            self.core_recv,
            self.xy_send,
            self.xy_recv,
            self.z_send,
            self.z_recv,
            self.last_send,
            self.last_recv,
        ) = scratch
        self.quarter = out.shape[0] // 4
        self.half = self.quarter // 2
        z, high = place.z, place.high
        low = 1 - high
        self.order = (3 * low, low * (2 - 2 * z) + high * (7 - 2 * z), 1 + z % 2, z)
        self.onward = (z + 1 - 2 * high, z + 1 - 2 * (z % 2), z + 1 - 2 * high)
        self.closing = (0, (z % 2) * low, high)
        self.far = place.at_z(z + 2 - 4 * high)
        self.near = place.at_z(z + 1 - 2 * (z % 2))

    def shard_terms(self, shard):
        rows = self.out.shape[0]
        return self.terms.at[pl.ds(pl.multiple_of(self.base + shard * rows, 16), rows)]

    def load(self, step):
        source = self.shard_terms(2 * self.order[step] + self.place.core)
        return pltpu.make_async_copy(source, self.mine.at[step], self.load_sems.at[step])

    def core_copy(self, step):
        return transfer(
            self.shard_terms(2 * self.order[step] + 1 - self.place.core),
            self.sib.at[step],
            self.core_send.at[step],
            self.core_recv.at[step],
            self.place.sibling,
        )

    def part(self, step, which, side):
        start = pl.multiple_of(which * self.quarter + side * self.half, 16)
        return self.mine.at[step, pl.ds(start, self.half)]

    def xy_copy(self, step, index):
        place = self.place
        source, target, device = (
            (self.part(step, place.by_x, 0), self.from_x.at[step, 0], place.next_x),
            (self.part(step, place.across, 0), self.from_x.at[step, 1], place.next_x),
            (self.part(step, place.by_y, 1), self.from_y.at[step, 0], place.next_y),
            (self.part(step, place.across, 1), self.from_y.at[step, 1], place.next_y),
            (self.part(step, place.by_y, 0), self.late_y.at[step], place.next_y),
            (self.part(step, place.by_x, 1), self.late_x.at[step], place.next_x),
        )[index]
        place = 6 * step + index
        return transfer(source, target, self.xy_send.at[place], self.xy_recv.at[place], device)

    def start(self):
        greet(self.place, (self.far,))
        for step in range(2):
            self.core_copy(step).start()
        for step in range(4):
            self.load(step).start()

    def core(self, step):
        place, quarter = self.place, self.quarter
        self.load(step).wait()
        self.core_copy(step).wait_recv()
        if step < 2:
            self.core_copy(step + 2).start()

        def add(which):
            block = pl.ds(pl.multiple_of(which * quarter, 16), quarter)
            mine = self.mine.at[step, block]
            add_rows(mine, mine, self.sib.at[step, block], quarter, self.half)

        add(place.by_x)
        add(place.across)
        self.xy_copy(step, 0).start()
        self.xy_copy(step, 1).start()
        add(place.by_y)
        self.xy_copy(step, 2).start()
        self.xy_copy(step, 3).start()
        add(place.quarter)

    def take(self, step, which, side, index, source):
        self.xy_copy(step, index).wait_recv()
        target = self.part(step, which, side)
        add_rows(target, target, source, self.half, self.half)

    def first(self, step):
        place = self.place
        self.take(step, place.by_y, 0, 1, self.from_x.at[step, 1])
        self.xy_copy(step, 4).start()
        self.take(step, place.by_x, 1, 3, self.from_y.at[step, 1])
        self.xy_copy(step, 5).start()
        self.take(step, place.quarter, 0, 0, self.from_x.at[step, 0])
        self.take(step, place.quarter, 1, 2, self.from_y.at[step, 0])

    def own_block(self, step):
        return self.mine.at[step, pl.ds(pl.multiple_of(self.place.quarter * self.quarter, 16), self.quarter)]

    def z_copy(self, step):
        goal = self.order[step]
        slot = goal + self.closing[step] * (4 - goal)
        return transfer(
            self.own_block(step),
            self.from_z.at[slot],
            self.z_send.at[step],
            self.z_recv.at[slot],
            self.place.at_z(self.onward[step]),
        )

    def take_z(self, step, slot):
        source = self.from_z.at[slot]
        transfer(source, source, self.z_send.at[0], self.z_recv.at[slot], self.near).wait_recv()
        block = self.own_block(step)
        add_rows(block, block, source, self.quarter, self.half)

    def second(self, step):
        place = self.place
        self.take(step, place.quarter, 0, 4, self.late_y.at[step])
        self.take(step, place.quarter, 1, 5, self.late_x.at[step])
        if step < 3:

            @pl.when(place.inner)
            def _():
                self.take_z(step, self.order[step])

            self.z_copy(step).start()
        else:

            @pl.when(place.z > 0)
            def _():
                self.take_z(step, place.z)

            @pl.when(place.z < 3)
            def _():
                self.take_z(step, 4)

    def final(self, which, side=None):
        start = pl.multiple_of(which * self.quarter + (0 if side is None else side * self.half), 16)
        return self.result.at[pl.ds(start, self.quarter if side is None else self.half)]

    def last_copy(self, index, ref):
        device = (self.place.next_x, self.place.next_y, self.place.next_y, self.place.next_x)[index]
        return transfer(ref, ref, self.last_send.at[index], self.last_recv.at[index], device)

    def share(self):
        own = self.final(self.place.quarter)
        own[...] = self.own_block(3)[...]
        self.last_copy(0, own).start()
        self.last_copy(1, own).start()

    def share_on(self):
        place = self.place
        self.last_copy(0, self.final(place.by_x)).wait_recv()
        self.last_copy(2, self.final(place.by_x, 0)).start()
        self.last_copy(1, self.final(place.by_y)).wait_recv()
        self.last_copy(3, self.final(place.by_y, 1)).start()

    def finish(self):
        place = self.place
        self.last_copy(2, self.final(place.across, 0)).wait_recv()
        self.last_copy(3, self.final(place.across, 1)).wait_recv()
        self.out[...] = self.result[...]
        for step in range(4):
            self.core_copy(step).wait_send()
            for index in range(6):
                self.xy_copy(step, index).wait_send()
            if step < 3:
                self.z_copy(step).wait_send()
        own = self.final(place.quarter)
        self.last_copy(0, own).wait_send()
        self.last_copy(1, own).wait_send()
        self.last_copy(2, self.final(place.by_x, 0)).wait_send()
        self.last_copy(3, self.final(place.by_y, 1)).wait_send()


def reduce_kernel(*refs, base, short_steps):
    terms, small_ref, d_ref, resid_ref, w_ref, out_ref, small_out, short_ref, long_ref = refs[:9]
    small_in, small_sum, small_send, small_recv = refs[9:13]
    reduce = Reduce(terms, base, out_ref, refs[13:])
    place = reduce.place
    partners = (place.sibling, place.next_x, place.next_y, reduce.near, reduce.far)

    def small_copy(level):
        return transfer(
            small_sum.at[level],
            small_in.at[level],
            small_send.at[level],
            small_recv.at[level],
            partners[level],
        )

    def small_start():
        small_sum[0] = small_ref[...]
        small_copy(0).start()

    def small_step(level):
        small_copy(level - 1).wait_recv()
        small_sum[level] = small_sum[level - 1] + small_in[level - 1]
        if level < 5:
            small_copy(level).start()
        else:
            small_out[...] = small_sum[5]

    run_events(
        pl.program_id(0),
        (
            (reduce.start, small_start),
            (partial(reduce.core, 0), partial(small_step, 1)),
            (partial(reduce.core, 1), partial(reduce.first, 0), partial(small_step, 2)),
            (
                partial(reduce.core, 2),
                partial(reduce.first, 1),
                partial(reduce.second, 0),
                partial(small_step, 3),
            ),
            (
                partial(reduce.core, 3),
                partial(reduce.first, 2),
                partial(reduce.second, 1),
                partial(small_step, 4),
            ),
            (partial(reduce.first, 3), partial(reduce.second, 2), partial(small_step, 5)),
            (partial(reduce.second, 3), reduce.share),
            (reduce.share_on,),
        ),
    )
    input_product(d_ref, resid_ref, w_ref, short_ref, long_ref, short_steps)

    @pl.when(pl.program_id(0) == pl.num_programs(0) - 1)
    def _():
        reduce.finish()
        for level in range(5):
            small_copy(level).wait_send()


def reduce_late(terms, base, rows, small, d_qkv, resid, w_qkv, short_tiles):
    steps = resid.shape[0] // INPUT_ROWS
    short_steps = short_tiles * TILE // INPUT_ROWS
    in_specs, out_specs = input_specs(short_steps)

    def whole(shape):
        return pl.BlockSpec(shape, lambda step: (0, 0), pipeline_mode=pl.Buffered(1))

    return pl.pallas_call(
        partial(reduce_kernel, base=base, short_steps=short_steps),
        grid=(steps,),
        in_specs=[pl.BlockSpec(memory_space=pltpu.HBM), whole(small.shape)] + in_specs,
        out_specs=[
            pl.BlockSpec((rows, BLK), lambda step: (0, 0)),
            pl.BlockSpec(small.shape, lambda step: (0, 0)),
        ]
        + out_specs,
        out_shape=[
            jax.ShapeDtypeStruct((rows, BLK), BF16),
            jax.ShapeDtypeStruct((SMALL_ROWS, BLK), F32),
            jax.ShapeDtypeStruct((short_steps * INPUT_ROWS, D), F32),
            jax.ShapeDtypeStruct(((steps - short_steps) * INPUT_ROWS, D), F32),
        ],
        scratch_shapes=[
            pltpu.VMEM((5, SMALL_ROWS, BLK), F32),
            pltpu.VMEM((6, SMALL_ROWS, BLK), F32),
            pltpu.SemaphoreType.DMA((5,)),
            pltpu.SemaphoreType.DMA((5,)),
        ]
        + reduce_scratch(rows),
        compiler_params=pltpu.CompilerParams(
            collective_id=3, has_side_effects=True, vmem_limit_bytes=60 * MIB
        ),
        cost_estimate=pl.CostEstimate(flops=0, bytes_accessed=200 * MIB, transcendentals=0),
        name="reduce",
    )(terms, small, d_qkv, resid, w_qkv)


def count_where(condition, axis):
    return jnp.sum(condition.astype(jnp.int32), axis=axis)


def slot_codes(slots, qkv_slots, slot_count, shards):
    early = slot_count - LATE
    shard = slots // slot_count
    begin = shard * slot_count
    inside = (qkv_slots[None, :] >= begin[:, None]) & (qkv_slots[None, :] < (begin + slot_count)[:, None])
    own = count_where(qkv_slots[None, :] == slots[:, None], 1)
    before = count_where(inside & (qkv_slots[None, :] < slots[:, None]), 1)
    number = count_where(inside, 1)
    position = jnp.where(own > 0, slot_count - number + before, slots - begin - before)
    code = jnp.where(
        position < early,
        shard * early + position,
        shards * early + shard * LATE + position - early,
    )
    return code, position, jnp.max(number)


def empty_slots(block_slot, all_slots):
    places = jnp.arange(all_slots, dtype=jnp.int32)
    empty_before = places + 1 - count_where(block_slot[None, :] <= places[:, None], 1)
    empty_index = jnp.arange(all_slots - NBLK, dtype=jnp.int32)
    return count_where(empty_before[None, :] <= empty_index[:, None], 1)


def halves(values):
    high = values.astype(BF16)
    return high, (values - high.astype(F32)).astype(BF16)


def update_kernel(
    position_ref,
    blocks,
    master,
    left_stat,
    right_stat,
    left_root,
    right_root,
    slot_grad,
    new_left,
    new_right,
    new_master,
):
    count = master.shape[0]
    first = pl.program_id(0) * count
    for index in range(count):
        start = pl.multiple_of(position_ref[first + index] * BLK, BLK)
        grad = blocks[pl.ds(start, BLK)]
        slot_grad[index] = grad.astype(F32)
        new_left[index] = STAT_DECAY * left_stat[index] + (1.0 - STAT_DECAY) * right_product(grad, grad)
        new_right[index] = STAT_DECAY * right_stat[index] + (1.0 - STAT_DECAY) * left_product(grad, grad)
        applied = product(jnp.concatenate(halves(left_root[index]), axis=0), grad)
        applied = jnp.concatenate(halves(applied[:BLK] + applied[BLK:]), axis=0)
        root_high, root_low = halves(right_root[index])
        wide = product(applied, root_high)
        total = wide[:BLK] + wide[BLK:] + product(applied[:BLK], root_low)
        new_master[index] = master[index] - MATRIX_RATE * total


def update(position, blocks, master, left_stat, right_stat, left_root, right_root):
    slot_count = master.shape[0]
    group = max(size for size in range(1, 12) if slot_count % size == 0)
    some = pl.BlockSpec((group, BLK, BLK), lambda step, *_: (step, 0, 0))
    return pl.pallas_call(
        update_kernel,
        grid_spec=pltpu.PrefetchScalarGridSpec(
            num_scalar_prefetch=1,
            grid=(slot_count // group,),
            in_specs=[
                pl.BlockSpec(blocks.shape, lambda step, *_: (0, 0), pipeline_mode=pl.Buffered(1))
            ]
            + [some] * 5,
            out_specs=[some] * 4,
        ),
        out_shape=[jax.ShapeDtypeStruct(master.shape, F32)] * 4,
        compiler_params=pltpu.CompilerParams(vmem_limit_bytes=60 * MIB),
        cost_estimate=pl.CostEstimate(
            flops=14 * slot_count * BLK**3, bytes_accessed=36 * slot_count * BLK**2, transcendentals=0
        ),
        name="update",
    )(position, blocks, master, left_stat, right_stat, left_root, right_root)


def body(
    x_short,
    x_long,
    cot_short,
    cot_long,
    logit_cot_short,
    logit_cot_long,
    len_short,
    len_long,
    block_slot,
    master,
    left_stat,
    right_stat,
    left_root,
    right_root,
    small_params,
    small_first,
    small_second,
    own_transfers,
):
    slot_count = master.shape[0]
    shards = lax.axis_size("fsdp")
    all_slots = slot_count * shards
    short_seqs, width = x_short.shape[:2]
    long_seqs = x_long.shape[0]
    short_tiles = short_seqs * width // TILE
    per_tile = TILE // width
    empty = empty_slots(block_slot, all_slots)

    if own_transfers:
        early_count = slot_count - LATE
        own = jnp.arange(slot_count, dtype=jnp.int32) + slot_count * lax.axis_index("fsdp")
        code, position, most = slot_codes(
            jnp.concatenate([block_slot, empty, own]), block_slot[: 3 * 36], slot_count, shards
        )
        position = position[all_slots:]
        empty_code = code[NBLK:all_slots]
        code = code[:NBLK]
        fits = most <= LATE
        gathered = gather_shards(master)
    else:
        gathered = lax.all_gather(master.astype(BF16), "fsdp", axis=0, tiled=True)
    w_qkv = assemble(block_slot, gathered)
    pieces = unpack(small_params)
    params = jnp.pad(small_params, (0, SMALL_ROWS * BLK - small_params.shape[0])).reshape(SMALL_ROWS, BLK)
    w_class = jnp.pad(pieces[-2].reshape(SD, NCLS), ((0, 0), (0, SD - NCLS)))
    b_class = jnp.pad(pieces[-1].reshape(1, NCLS), ((0, 0), (0, SD - NCLS)))

    x, *qkv, context, probs_short, probs_long = attention(
        len_short,
        len_long,
        x_short.reshape(-1, D),
        x_long.reshape(-1, D),
        params,
        w_qkv,
        short_tiles,
        width,
    )

    logit_cot = jnp.concatenate(
        [
            jnp.pad(
                logit_cot_short.reshape(short_tiles, per_tile, NCLS),
                ((0, 0), (0, 8 - per_tile), (0, SD - NCLS)),
            ),
            jnp.pad(logit_cot_long.reshape(long_seqs, 1, NCLS), ((0, 0), (0, 7), (0, SD - NCLS))),
        ],
        axis=0,
    )
    (
        enc_short,
        enc_long,
        logits,
        first,
        active,
        d_up,
        d_down,
        d_branch,
        d_context,
        d_resid,
        g_student,
        g_hidden,
        g_small,
    ) = feed(
        len_short,
        len_long,
        block_slot,
        x,
        context,
        cot_short.reshape(-1, D),
        cot_long.reshape(-1, D),
        logit_cot,
        (params, w_class, b_class),
        gathered,
        short_tiles,
        width,
    )
    g_down = left_product(active, d_down).astype(BF16)
    g_up = left_product(first, d_up).astype(BF16)
    g_out = left_product(context, d_branch).astype(BF16)
    others = (g_out, g_up, g_down, g_student.astype(BF16), g_hidden.astype(BF16))
    if own_transfers:
        terms = spread(code, empty_code, others, OTHER_PLACES, all_slots)
        *back, early_reduced = attention_back(
            qkv,
            probs_short,
            probs_long,
            d_context,
            short_tiles,
            terms.reshape(-1, BLK),
            early_count * BLK,
        )
    else:
        back = attention_back(qkv, probs_short, probs_long, d_context, short_tiles)
    d_qkv, g_b_query, g_b_value = back
    g_qkv = left_product(x, d_qkv).astype(BF16)

    def reduce_all():
        qkv_grads = tuple(g_qkv[:, which * D : (which + 1) * D] for which in range(3))
        slot_terms = spread(block_slot, empty, qkv_grads + others, QKV_PLACES + OTHER_PLACES, all_slots)
        return lax.psum(lax.psum_scatter(slot_terms, "fsdp", scatter_dimension=0, tiled=True), "dp")

    if own_transfers:
        terms, small_terms = spread_late(code, g_qkv, g_small, g_b_query, g_b_value, terms)
        late_reduced, small_total, in_short, in_long = reduce_late(
            terms.reshape(-1, BLK),
            shards * early_count * BLK,
            LATE * BLK,
            small_terms,
            d_qkv,
            d_resid,
            w_qkv,
            short_tiles,
        )

        blocks = lax.cond(
            fits,
            lambda: jnp.concatenate([early_reduced, late_reduced], axis=0),
            lambda: reduce_all().reshape(-1, BLK),
        )
        position = jnp.where(fits, position, jnp.arange(slot_count, dtype=jnp.int32))
    else:
        in_short, in_long = input_grads(d_qkv, d_resid, w_qkv, short_tiles)
        blocks = reduce_all().reshape(-1, BLK)
        position = jnp.arange(slot_count, dtype=jnp.int32)
        small_terms = jnp.concatenate(
            [g_b_query.reshape(-1, BLK), g_b_value.reshape(-1, BLK), g_small[2 * D // BLK :]], axis=0
        )
        small_total = lax.psum(small_terms, ("dp", "fsdp"))
    slot_grad, new_left, new_right, new_master = update(
        position, blocks, master, left_stat, right_stat, left_root, right_root
    )
    small_grad = jnp.concatenate(
        [
            small_total[:CLASS_ROW].reshape(-1),
            small_total[CLASS_ROW : CLASS_ROW + NCLS].T.reshape(-1),
            small_total[LAST_ROW, :NCLS],
        ]
    )
    new_first = BETA_ONE * small_first + (1.0 - BETA_ONE) * small_grad
    new_second = BETA_TWO * small_second + (1.0 - BETA_TWO) * small_grad * small_grad
    first_hat = new_first / (1.0 - BETA_ONE**STEP)
    second_hat = new_second / (1.0 - BETA_TWO**STEP)
    new_small = small_params - ADAM_RATE * first_hat / (jnp.sqrt(second_hat) + ADAM_EPSILON)
    return (
        enc_short.reshape(x_short.shape),
        logits[:short_tiles, :per_tile, :NCLS].reshape(short_seqs, NCLS),
        enc_long.reshape(x_long.shape),
        logits[short_tiles:, 0, :NCLS],
        in_short.reshape(x_short.shape),
        in_long.reshape(x_long.shape),
        slot_grad,
        new_left,
        new_right,
        new_master,
        new_first,
        new_second,
        new_small,
    )


def solution(mesh):
    both = ("dp", "fsdp")
    placed = (
        P(both, None, None),
        P(both, None, None),
        P(both, None, None),
        P(both, None, None),
        P(both, None),
        P(both, None),
        P(both),
        P(both),
        P(),
        P("fsdp", None, None),
        P("fsdp", None, None),
        P("fsdp", None, None),
        P("fsdp", None, None),
        P("fsdp", None, None),
        P(),
        P(),
        P(),
    )
    return jax.shard_map(
        partial(body, own_transfers=(mesh.shape["dp"], mesh.shape["fsdp"]) == (4, 8)),
        mesh=mesh,
        in_specs=placed,
        out_specs=(
            P(both, None, None),
            P(both, None),
            P(both, None, None),
            P(both, None),
            P(both, None, None),
            P(both, None, None),
            P("fsdp", None, None),
            P("fsdp", None, None),
            P("fsdp", None, None),
            P("fsdp", None, None),
            P(),
            P(),
            P(),
        ),
        check_vma=False,
    )
```

```python
from functools import partial

import jax
import jax.numpy as jnp
from jax import lax
from jax.experimental import pallas as pl
from jax.experimental.pallas import tpu as pltpu
from jax.sharding import PartitionSpec as P

D = 768
HEADS = 12
FF = 3072
SD = 128
PH = 2
NCLS = 14
BLK = 128
STEP = 10
NBLK = 439
TILE = 512
PAIRS = 3
GROUPS = 2
CHUNK = 768
LATE = 24

NORM_EPSILON = 1e-12
BETA_ONE = 0.9
BETA_TWO = 0.999
ADAM_EPSILON = 1e-08
ADAM_RATE = 0.1
MATRIX_RATE = 0.2
STAT_DECAY = 0.5
MASKED_SCORE = -1e30
HIGHEST_PRECISION = lax.Precision.HIGHEST
MIB = 1024 * 1024
F32 = jnp.float32
BF16 = jnp.bfloat16

def product(former, latter, precision=None):
    return jnp.dot(former, latter, preferred_element_type=F32, precision=precision)


def left_product(former, latter, precision=None):
    return lax.dot_general(
        former, latter, (((0,), (0,)), ((), ())), preferred_element_type=F32, precision=precision
    )


def right_product(former, latter, precision=None):
    return lax.dot_general(
        former, latter, (((1,), (1,)), ((), ())), preferred_element_type=F32, precision=precision
    )


def unpack(small_values):
    widths = (D, D, D, D, D, FF, D, D, D, SD, SD, SD, SD * NCLS, NCLS)
    pieces = []
    offset = 0
    for column_count in widths:
        pieces.append(small_values[offset : offset + column_count])
        offset += column_count
    return pieces


def each_block(first, row_count, col_count, action):
    def one_row(index, carry):
        row = pl.multiple_of(index * BLK, BLK)
        for col in range(col_count):
            action(first + index * col_count + col, row, col * BLK)
        return carry

    lax.fori_loop(0, row_count, one_row, 0)


def load_blocks(slot_ref, blocks, target, sem, first, row_count, col_count, col_start=0):
    def move(block, row, col):
        pltpu.make_async_copy(
            blocks.at[slot_ref[block]],
            target.at[pl.ds(row, BLK), pl.ds(col + col_start * BLK, BLK)],
            sem,
        ).start()

    each_block(first, row_count, col_count, move)


def wait_whole(target, sem):
    pltpu.make_async_copy(target, target, sem).wait()


def assemble_kernel(slot_ref, blocks, out, sem):
    for which in range(3):
        load_blocks(slot_ref, blocks, out, sem, 36 * which, 6, 6, 6 * which)
    wait_whole(out, sem)


def assemble(block_slot, blocks):
    return pl.pallas_call(
        assemble_kernel,
        grid_spec=pltpu.PrefetchScalarGridSpec(
            num_scalar_prefetch=1,
            grid=(1,),
            in_specs=[pl.BlockSpec(memory_space=pltpu.HBM)],
            out_specs=pl.BlockSpec(memory_space=pltpu.VMEM),
            scratch_shapes=[pltpu.SemaphoreType.DMA],
        ),
        out_shape=jax.ShapeDtypeStruct((D, 3 * D), BF16),
        compiler_params=pltpu.CompilerParams(vmem_limit_bytes=60 * MIB),
        name="assemble",
    )(block_slot, blocks)


def join_small(small_ref, query_ref, value_ref, small_out):
    small_out[...] = small_ref[...]
    for start, ref in ((0, query_ref), (D // BLK, value_ref)):
        for index in range(D // BLK):
            small_out[start + index : start + index + 1, :] = ref[:, index * BLK : (index + 1) * BLK]


PART = 256
ACROSS = PART // BLK


def feed_grads_kernel(
    code_ref,
    empty_ref,
    first_ref,
    d_down_ref,
    active_ref,
    d_up_ref,
    g_out,
    g_student,
    g_hidden,
    zero,
    terms,
    first_turned,
    down_turned,
    up_stage,
    down_stage,
    up_sems,
    down_sems,
    other_sems,
):
    step = pl.program_id(0)
    last = pl.num_programs(0) - 1
    slot = step % 2
    others = ((g_out, 108, 6, 6), (g_student, 432, 6, 1), (g_hidden, 438, 1, 1))
    empty_count = empty_ref.shape[0]

    @pl.when(step == 0)
    def _():
        for which, (grad, first, row_count, col_count) in enumerate(others):

            def move(block, row, col, which=which, grad=grad):
                pltpu.make_async_copy(
                    grad.at[pl.ds(row, BLK), pl.ds(col, BLK)], terms.at[code_ref[block]], other_sems.at[which]
                ).start()

            each_block(first, row_count, col_count, move)
        for index in range(empty_count):
            pltpu.make_async_copy(
                zero, terms.at[empty_ref[index]], other_sems.at[len(others) + index]
            ).start()
        first_turned[...] = first_ref[...].T
        down_turned[...] = d_down_ref[...].T

    @pl.when(step >= 2)
    def _():
        wait_whole(up_stage.at[slot], up_sems.at[slot])
        wait_whole(down_stage.at[slot], down_sems.at[slot])

    up_stage[slot] = product(first_turned[...], d_up_ref[...]).astype(BF16)
    down_stage[slot] = product(down_turned[...], active_ref[...]).T.astype(BF16)
    for row in range(D // BLK):
        for col in range(ACROSS):
            pltpu.make_async_copy(
                up_stage.at[slot, pl.ds(row * BLK, BLK), pl.ds(col * BLK, BLK)],
                terms.at[code_ref[144 + row * (FF // BLK) + step * ACROSS + col]],
                up_sems.at[slot],
            ).start()
            pltpu.make_async_copy(
                down_stage.at[slot, pl.ds(col * BLK, BLK), pl.ds(row * BLK, BLK)],
                terms.at[code_ref[288 + (step * ACROSS + col) * (D // BLK) + row]],
                down_sems.at[slot],
            ).start()

    @pl.when(step == last)
    def _():
        for place in range(2):
            wait_whole(up_stage.at[place], up_sems.at[place])
            wait_whole(down_stage.at[place], down_sems.at[place])
        for which, (grad, *_) in enumerate(others):
            wait_whole(grad, other_sems.at[which])
        for index in range(empty_count):
            wait_whole(zero, other_sems.at[len(others) + index])


def feed_grads(code, empty, first, d_down, active, d_up, others, slot_count):
    tokens = first.shape[0]

    def whole(shape):
        return pl.BlockSpec(shape, lambda step, *_: (0, 0), pipeline_mode=pl.Buffered(1))

    part = pl.BlockSpec((tokens, PART), lambda step, *_: (0, step))
    return pl.pallas_call(
        feed_grads_kernel,
        grid_spec=pltpu.PrefetchScalarGridSpec(
            num_scalar_prefetch=2,
            grid=(FF // PART,),
            in_specs=[whole(first.shape), whole(d_down.shape), part, part]
            + [whole(other.shape) for other in others]
            + [whole((BLK, BLK))],
            out_specs=pl.BlockSpec(memory_space=pltpu.HBM),
            scratch_shapes=[
                pltpu.VMEM((D, tokens), BF16),
                pltpu.VMEM((D, tokens), BF16),
                pltpu.VMEM((2, D, PART), BF16),
                pltpu.VMEM((2, PART, D), BF16),
                pltpu.SemaphoreType.DMA((2,)),
                pltpu.SemaphoreType.DMA((2,)),
                pltpu.SemaphoreType.DMA((3 + empty.shape[0],)),
            ],
        ),
        out_shape=jax.ShapeDtypeStruct((slot_count, BLK, BLK), BF16),
        compiler_params=pltpu.CompilerParams(vmem_limit_bytes=60 * MIB),
        cost_estimate=pl.CostEstimate(
            flops=4 * tokens * D * FF, bytes_accessed=50 * MIB, transcendentals=0
        ),
        name="feed_grads",
    )(code, empty, first, d_down, active, d_up, *others, jnp.zeros((BLK, BLK), BF16))


def input_weights_kernel(
    code_ref, x_ref, d_ref, small_ref, query_ref, value_ref, _, terms, small_out, turned, stage, sems
):
    step = pl.program_id(0)
    slot = step % 2

    @pl.when(step == 0)
    def _():
        join_small(small_ref, query_ref, value_ref, small_out)
        turned[...] = x_ref[...].T

    @pl.when(step >= 2)
    def _():
        wait_whole(stage.at[slot], sems.at[slot])

    stage[slot] = product(turned[...], d_ref[...]).astype(BF16)
    steps = D // PART
    first = (step // steps) * 36 + step % steps * ACROSS
    for row in range(D // BLK):
        for col in range(ACROSS):
            pltpu.make_async_copy(
                stage.at[slot, pl.ds(row * BLK, BLK), pl.ds(col * BLK, BLK)],
                terms.at[code_ref[first + row * (D // BLK) + col]],
                sems.at[slot],
            ).start()

    @pl.when(step == pl.num_programs(0) - 1)
    def _():
        for place in range(2):
            wait_whole(stage.at[place], sems.at[place])


def input_weights(code, x, d_qkv, small, g_query, g_value, terms):
    tokens = x.shape[0]

    def whole(shape):
        return pl.BlockSpec(shape, lambda step, *_: (0, 0), pipeline_mode=pl.Buffered(1))

    hbm = pl.BlockSpec(memory_space=pltpu.HBM)
    return pl.pallas_call(
        input_weights_kernel,
        grid_spec=pltpu.PrefetchScalarGridSpec(
            num_scalar_prefetch=1,
            grid=(3 * D // PART,),
            in_specs=[
                whole(x.shape),
                pl.BlockSpec((tokens, PART), lambda step, *_: (0, step)),
                whole(small.shape),
                whole(g_query.shape),
                whole(g_value.shape),
                hbm,
            ],
            out_specs=[hbm, pl.BlockSpec(small.shape, lambda step, *_: (0, 0))],
            scratch_shapes=[
                pltpu.VMEM((D, tokens), BF16),
                pltpu.VMEM((2, D, PART), BF16),
                pltpu.SemaphoreType.DMA((2,)),
            ],
        ),
        out_shape=[
            jax.ShapeDtypeStruct(terms.shape, BF16),
            jax.ShapeDtypeStruct(small.shape, F32),
        ],
        input_output_aliases={6: 0},
        compiler_params=pltpu.CompilerParams(vmem_limit_bytes=60 * MIB),
        cost_estimate=pl.CostEstimate(
            flops=6 * tokens * D * D, bytes_accessed=16 * MIB, transcendentals=0
        ),
        name="input_weights",
    )(code, x, d_qkv, small, g_query, g_value, terms)


def half_masks():
    lane = lax.broadcasted_iota(jnp.int32, (1, BLK), 1)
    low = (lane < BLK // 2).astype(BF16)
    return low, (1.0 - low.astype(F32)).astype(BF16)


def stack_heads(values, low, high):
    return jnp.concatenate([values * low, values * high], axis=0)


def pick_heads(values):
    rows = values.shape[0] // 2
    lane = lax.broadcasted_iota(jnp.int32, (rows, BLK), 1)
    return jnp.where(lane < BLK // 2, values[:rows], values[rows:])


def pipelined(count, before, middle, after):
    started = before(0)
    done = None
    for index in range(count):
        current = started
        if index + 1 < count:
            started = before(index + 1)
        if done is not None:
            after(index - 1, done)
        done = middle(index, current)
    after(count - 1, done)


def softmax(scores, length):
    visible = lax.broadcasted_iota(jnp.int32, scores.shape, 1) < length
    scores = jnp.where(visible, scores, MASKED_SCORE)
    powers = jnp.exp(scores - jnp.max(scores, axis=-1, keepdims=True))
    total = jnp.sum(powers, axis=-1, keepdims=True)
    return (powers * (1.0 / total)).astype(BF16)


def attention_kernel(
    len_short,
    len_long,
    x_short_ref,
    x_long_ref,
    params,
    w_ref,
    x_ref,
    q_ref,
    k_ref,
    v_ref,
    context_ref,
    short_ref,
    long_ref,
    bias,
    *,
    short_tiles,
):
    tile = pl.program_id(0)
    group = pl.program_id(1)
    low, high = half_masks()
    width = short_ref.shape[-1]
    per_tile = TILE // width

    wide = PAIRS * BLK
    start = pl.multiple_of(group * wide, wide)

    @pl.when((tile == 0) & (group == 0))
    def _():
        for which in range(2):
            for place in range(D // BLK):
                row = which * (D // BLK) + place
                bias[which : which + 1, place * BLK : (place + 1) * BLK] = params[row : row + 1, :]

    @pl.when((tile < short_tiles) & (group == 0))
    def _():
        x_ref[...] = x_short_ref[...]

    @pl.when((tile >= short_tiles) & (group == 0))
    def _():
        x_ref[...] = x_long_ref[...]

    rows_in = x_ref[...]
    queries = product(rows_in, w_ref[:, pl.ds(start, wide)]) + bias[0:1, pl.ds(start, wide)]
    q_ref[...] = (queries * 0.125).astype(BF16)
    k_ref[...] = product(rows_in, w_ref[:, pl.ds(D + start, wide)]).astype(BF16)
    values = product(rows_in, w_ref[:, pl.ds(2 * D + start, wide)]) + bias[1:2, pl.ds(start, wide)]
    v_ref[...] = values.astype(BF16)

    def attend(units, kept_ref):
        def scores(index):
            rows, keys, cols, _, _ = units[index]
            return right_product(stack_heads(q_ref[rows, cols], low, high), k_ref[keys, cols])

        def weigh(index, values):
            _, _, _, length, place = units[index]
            probs = softmax(values, length)
            kept_ref[place] = probs
            return probs

        def mix(index, probs):
            rows, keys, cols, _, _ = units[index]
            context_ref[rows, cols] = pick_heads(product(probs, v_ref[keys, cols])).astype(BF16)

        pipelined(len(units), scores, weigh, mix)

    @pl.when(tile < short_tiles)
    def _():
        units = []
        for seq in range(per_tile):
            rows = slice(seq * width, (seq + 1) * width)
            length = len_short[tile * per_tile + seq]
            for pair in range(PAIRS):
                cols = slice(pair * BLK, (pair + 1) * BLK)
                units.append((rows, rows, cols, length, (0, pair, seq)))
        attend(units, short_ref)

    @pl.when(tile >= short_tiles)
    def _():
        length = len_long[tile - short_tiles]
        half = TILE // 2
        units = []
        for pair in range(PAIRS):
            cols = slice(pair * BLK, (pair + 1) * BLK)
            for part in range(2):
                rows = slice(part * half, (part + 1) * half)
                units.append((rows, slice(0, TILE), cols, length, (0, pair, part)))
        attend(units, long_ref)


def run_events(step, events):
    for index, actions in enumerate(events):

        @pl.when(step == index)
        def _(actions=actions):
            for action in actions:
                action()


def probs_shapes(short_tiles, long_tiles, width):
    per_tile = TILE // width
    return (
        (short_tiles, 2 * PAIRS, per_tile, 2 * width, width),
        (long_tiles, 2 * PAIRS, 2, TILE, TILE),
    )


def short_index(tile, short_tiles):
    return jnp.minimum(tile, short_tiles - 1)


def long_index(tile, short_tiles):
    return jnp.maximum(tile - short_tiles, 0)


def probs_maps(short_tiles):
    def short_map(tile, group):
        last = jnp.minimum(tile // short_tiles, 1)
        return (short_index(tile, short_tiles), group + last * (GROUPS - 1 - group), 0, 0, 0)

    def long_map(tile, group):
        begun = jnp.minimum(tile // short_tiles, 1)
        return (long_index(tile, short_tiles), begun * group, 0, 0, 0)

    return short_map, long_map


def attention(len_short, len_long, x_short, x_long, params, w_qkv, short_tiles, width):
    tiles = (x_short.shape[0] + x_long.shape[0]) // TILE
    wide = PAIRS * BLK
    short_shape, long_shape = probs_shapes(short_tiles, tiles - short_tiles, width)
    short_map, long_map = probs_maps(short_tiles)
    flops = 4 * D * TILE * TILE * tiles + 6 * D * D * TILE * tiles
    rows = pl.BlockSpec((TILE, wide), lambda tile, group: (tile, group))
    scalars = pl.BlockSpec(memory_space=pltpu.SMEM)

    def whole(shape):
        return pl.BlockSpec(shape, lambda tile, group: (0,) * len(shape), pipeline_mode=pl.Buffered(1))

    in_specs = [
        scalars,
        scalars,
        pl.BlockSpec((TILE, D), lambda tile, group: (short_index(tile, short_tiles), 0)),
        pl.BlockSpec((TILE, D), lambda tile, group: (long_index(tile, short_tiles), 0)),
        whole(params.shape),
        whole((D, 3 * D)),
    ]
    out_specs = [
        pl.BlockSpec((TILE, D), lambda tile, group: (tile, 0)),
        rows,
        rows,
        rows,
        rows,
        pl.BlockSpec((1, PAIRS) + short_shape[2:], short_map),
        pl.BlockSpec((1, PAIRS) + long_shape[2:], long_map),
    ]
    out_shape = [jax.ShapeDtypeStruct((tiles * TILE, D), BF16)] * 5 + [
        jax.ShapeDtypeStruct(short_shape, BF16),
        jax.ShapeDtypeStruct(long_shape, BF16),
    ]
    arguments = [len_short, len_long, x_short, x_long, params, w_qkv]
    return pl.pallas_call(
        partial(attention_kernel, short_tiles=short_tiles),
        grid=(tiles, GROUPS),
        in_specs=in_specs,
        out_specs=out_specs,
        out_shape=out_shape,
        scratch_shapes=[pltpu.VMEM((8, D), F32)],
        compiler_params=pltpu.CompilerParams(vmem_limit_bytes=60 * MIB),
        cost_estimate=pl.CostEstimate(
            flops=flops, bytes_accessed=35 * MIB, transcendentals=HEADS * TILE * TILE * tiles // 2
        ),
        name="attention",
    )(*arguments)


def attention_back_kernel(*refs, short_tiles, transfers):
    q_ref, k_ref, v_ref, short_ref, long_ref, dc_ref = refs[:6]
    refs = refs[6:]
    if transfers:
        terms_ref, refs = refs[0], refs[1:]
    out_ref, bq_ref, bv_ref = refs[:3]
    tile = pl.program_id(0)
    group = pl.program_id(1)
    low, high = half_masks()
    width = short_ref.shape[-1]
    per_tile = TILE // width
    if transfers:
        reduce = Reduce(terms_ref, 0, refs[3], refs[4:])
        run_events(
            tile * GROUPS + group,
            (
                (reduce.start,),
                (partial(reduce.core, 0),),
                (partial(reduce.core, 1), partial(reduce.first, 0)),
                (partial(reduce.core, 2), partial(reduce.first, 1), partial(reduce.second, 0)),
                (partial(reduce.core, 3), partial(reduce.first, 2), partial(reduce.second, 1)),
                (partial(reduce.first, 3), partial(reduce.second, 2)),
                (partial(reduce.second, 3), reduce.share),
                (reduce.share_on,),
            ),
        )

    wide = PAIRS * BLK
    start = pl.multiple_of(group * wide, wide)

    def columns(which, cols):
        return pl.ds(pl.multiple_of(which * D + start + cols.start, BLK), BLK)

    def go_back(units, kept_ref, parts):
        sums = {}

        def spread_in(index):
            rows, keys, cols, _ = units[index]
            return right_product(stack_heads(dc_ref[rows, cols], low, high), v_ref[keys, cols])

        def differ(index, d_probs):
            wide = kept_ref[units[index][3]].astype(F32)
            weighted = wide * d_probs
            return (weighted - wide * jnp.sum(weighted, axis=-1, keepdims=True)).astype(BF16)

        def gather_up(index, d_scores):
            rows, keys, cols, place = units[index]
            d_queries = pick_heads(product(d_scores, k_ref[keys, cols])) * 0.125
            out_ref[rows, columns(0, cols)] = d_queries.astype(BF16)
            d_keys = left_product(d_scores, stack_heads(q_ref[rows, cols], low, high))
            d_values = left_product(kept_ref[place], stack_heads(dc_ref[rows, cols], low, high))
            if index % parts:
                d_keys += sums["keys"]
                d_values += sums["values"]
            if index % parts == parts - 1:
                out_ref[keys, columns(1, cols)] = d_keys.astype(BF16)
                out_ref[keys, columns(2, cols)] = d_values.astype(BF16)
            else:
                sums.update(keys=d_keys, values=d_values)

        pipelined(len(units), spread_in, differ, gather_up)

    @pl.when(tile < short_tiles)
    def _():
        units = []
        for seq in range(per_tile):
            rows = slice(seq * width, (seq + 1) * width)
            for pair in range(PAIRS):
                cols = slice(pair * BLK, (pair + 1) * BLK)
                units.append((rows, rows, cols, (0, pair, seq)))
        go_back(units, short_ref, 1)

    @pl.when(tile >= short_tiles)
    def _():
        half = TILE // 2
        units = []
        for pair in range(PAIRS):
            cols = slice(pair * BLK, (pair + 1) * BLK)
            for part in range(2):
                rows = slice(part * half, (part + 1) * half)
                units.append((rows, slice(0, TILE), cols, (0, pair, part)))
        go_back(units, long_ref, 2)

    @pl.when((tile == 0) & (group == 0))
    def _():
        bq_ref[...] = jnp.zeros_like(bq_ref)
        bv_ref[...] = jnp.zeros_like(bv_ref)

    bq_ref[:, pl.ds(start, wide)] += column_sum(out_ref[:, pl.ds(start, wide)])
    bv_ref[:, pl.ds(start, wide)] += column_sum(out_ref[:, pl.ds(2 * D + start, wide)])

    if transfers:

        @pl.when((tile == pl.num_programs(0) - 1) & (group == GROUPS - 1))
        def _():
            reduce.finish()


def attention_back(qkv, probs_short, probs_long, d_context, short_tiles, terms=None, count=0):
    tiles = d_context.shape[0] // TILE
    wide = PAIRS * BLK
    short_map, long_map = probs_maps(short_tiles)
    rows = pl.BlockSpec((TILE, wide), lambda tile, group: (tile, group))
    row = pl.BlockSpec((1, D), lambda tile, group: (0, 0))
    flops = 10 * D * TILE * TILE * tiles
    in_specs = [
        rows,
        rows,
        rows,
        pl.BlockSpec((1, PAIRS) + probs_short.shape[2:], short_map),
        pl.BlockSpec((1, PAIRS) + probs_long.shape[2:], long_map),
        rows,
    ]
    out_specs = [pl.BlockSpec((TILE, 3 * D), lambda tile, group: (tile, 0)), row, row]
    out_shape = [
        jax.ShapeDtypeStruct((tiles * TILE, 3 * D), BF16),
        jax.ShapeDtypeStruct((1, D), F32),
        jax.ShapeDtypeStruct((1, D), F32),
    ]
    arguments = [*qkv, probs_short, probs_long, d_context]
    scratch = []
    params = dict(vmem_limit_bytes=60 * MIB)
    if terms is not None:
        arguments.append(terms)
        in_specs.append(pl.BlockSpec(memory_space=pltpu.HBM))
        out_specs.append(pl.BlockSpec((count, BLK), lambda tile, group: (0, 0)))
        out_shape.append(jax.ShapeDtypeStruct((count, BLK), BF16))
        scratch = reduce_scratch(count)
        params.update(collective_id=2, has_side_effects=True)
    return pl.pallas_call(
        partial(attention_back_kernel, short_tiles=short_tiles, transfers=terms is not None),
        grid=(tiles, GROUPS),
        in_specs=in_specs,
        out_specs=out_specs,
        out_shape=out_shape,
        scratch_shapes=scratch,
        compiler_params=pltpu.CompilerParams(**params),
        cost_estimate=pl.CostEstimate(flops=flops, bytes_accessed=50 * MIB, transcendentals=0),
        name="attention_back",
    )(*arguments)


INPUT_ROWS = 256


def input_product(d_ref, resid_ref, w_ref, short_ref, long_ref, short_steps):
    step = pl.program_id(0)
    total = resid_ref[...] + right_product(d_ref[...], w_ref[...])

    @pl.when(step < short_steps)
    def _():
        short_ref[...] = total

    @pl.when(step >= short_steps)
    def _():
        long_ref[...] = total


def input_specs(short_steps):
    rows = [pl.BlockSpec((INPUT_ROWS, width), lambda step: (step, 0)) for width in (3 * D, D)]
    whole = pl.BlockSpec((D, 3 * D), lambda step: (0, 0), pipeline_mode=pl.Buffered(1))
    outs = [
        pl.BlockSpec((INPUT_ROWS, D), lambda step: (short_index(step, short_steps), 0)),
        pl.BlockSpec((INPUT_ROWS, D), lambda step: (long_index(step, short_steps), 0)),
    ]
    return rows + [whole], outs


def input_grads(d_qkv, resid, w_qkv, short_tiles):
    steps = resid.shape[0] // INPUT_ROWS
    short_steps = short_tiles * TILE // INPUT_ROWS
    in_specs, out_specs = input_specs(short_steps)
    return pl.pallas_call(
        partial(input_product, short_steps=short_steps),
        grid=(steps,),
        in_specs=in_specs,
        out_specs=out_specs,
        out_shape=[
            jax.ShapeDtypeStruct((short_steps * INPUT_ROWS, D), F32),
            jax.ShapeDtypeStruct(((steps - short_steps) * INPUT_ROWS, D), F32),
        ],
        compiler_params=pltpu.CompilerParams(vmem_limit_bytes=60 * MIB),
        name="input_grads",
    )(d_qkv, resid, w_qkv)


def normal_parts(values):
    below = 0.5 * lax.erf(values * 0.7071067811865476) + 0.5
    return below, jnp.exp(-0.5 * values * values) * 0.3989422804014327


B_OUT, GAIN_ONE, SHIFT_ONE, B_UP, B_DOWN, GAIN_TWO, SHIFT_TWO, B_STUDENT, POOL_QUERY, B_HIDDEN = range(10)
VECTORS = (
    (12, 6),
    (18, 6),
    (24, 6),
    (30, 24),
    (54, 6),
    (60, 6),
    (66, 6),
    (72, 1),
    (73, 1),
    (74, 1),
)
CLASS_ROW = 75
LAST_ROW = 91
SMALL_ROWS = 96


def norm_parts(values):
    center = values - jnp.mean(values, axis=-1, keepdims=True)
    spread = jnp.mean(center * center, axis=-1, keepdims=True)
    inverse = lax.rsqrt(spread + NORM_EPSILON)
    return center * inverse, inverse


def norm_back(d_values, gain, unit, inverse):
    d_unit = d_values * gain
    return inverse * (
        d_unit
        - jnp.mean(d_unit, axis=-1, keepdims=True)
        - unit * jnp.mean(d_unit * unit, axis=-1, keepdims=True)
    )


def column_sum(values):
    return jnp.sum(values.astype(F32), axis=0, keepdims=True)


def pool_weights(student, query, length):
    scaled = student * query
    lane = lax.broadcasted_iota(jnp.int32, scaled.shape, 1)
    place = lax.broadcasted_iota(jnp.int32, (scaled.shape[0], 1), 0)
    weights = []
    for side in (lane < SD // PH, lane >= SD // PH):
        scores = jnp.sum(jnp.where(side, scaled, 0.0), axis=-1, keepdims=True)
        scores = jnp.where(place < length, scores, MASKED_SCORE)
        powers = jnp.exp(scores - jnp.max(scores, axis=0, keepdims=True))
        weights.append(powers / jnp.sum(powers, axis=0, keepdims=True))
    return jnp.where(lane < SD // PH, weights[0], weights[1]), weights


def student_back(student, query, weights, both, d_pooled):
    lane = lax.broadcasted_iota(jnp.int32, student.shape, 1)
    moved = student * d_pooled
    d_scores = []
    for side, weight in zip((lane < SD // PH, lane >= SD // PH), weights):
        d_weight = jnp.sum(jnp.where(side, moved, 0.0), axis=-1, keepdims=True)
        d_scores.append(weight * (d_weight - jnp.sum(weight * d_weight, axis=0, keepdims=True)))
    d_score = jnp.where(lane < SD // PH, d_scores[0], d_scores[1])
    d_query = jnp.sum(d_score * student, axis=0, keepdims=True) * 0.125
    return both * d_pooled + d_score * query, d_query


def feed_kernel(
    len_short,
    len_long,
    slot_ref,
    x_ref,
    context_ref,
    cot_short_ref,
    cot_long_ref,
    logit_cot_ref,
    params,
    w_class,
    b_class,
    blocks,
    enc_short_ref,
    enc_long_ref,
    logit_ref,
    first_ref,
    active_ref,
    d_up_ref,
    d_down_ref,
    d_branch_ref,
    d_context_ref,
    d_resid_ref,
    g_student,
    g_hidden,
    g_small,
    slope,
    pooled_ref,
    d_student_ref,
    w_out,
    w_up,
    w_down,
    w_student,
    w_hidden,
    vectors,
    totals,
    g_class,
    g_last,
    sems,
    *,
    short_tiles,
    width,
):
    tile = pl.program_id(0)
    per_tile = TILE // width
    loads = ((w_out, 108, 6, 6), (w_up, 144, 6, 24), (w_down, 288, 24, 6), (w_student, 432, 6, 1), (w_hidden, 438, 1, 1))

    def arrive(*indices):
        @pl.when(tile == 0)
        def _():
            for index in indices:
                wait_whole(loads[index][0], sems.at[index])

    @pl.when(tile == 0)
    def _():
        for index, (target, block, row_count, col_count) in enumerate(loads):
            load_blocks(slot_ref, blocks, target, sems.at[index], block, row_count, col_count)
        for index, (start, count) in enumerate(VECTORS):
            for place in range(count):
                vectors[index : index + 1, place * BLK : (place + 1) * BLK] = params[
                    start + place : start + place + 1, :
                ]
        for ref in (totals, g_class, g_last, g_student, g_hidden):
            ref[...] = jnp.zeros_like(ref)

    def vector(index):
        return vectors[index : index + 1, : VECTORS[index][1] * BLK]

    def add_total(index, values):
        totals[index : index + 1, : VECTORS[index][1] * BLK] += column_sum(values)

    arrive(0)
    branch = product(context_ref[...], w_out[...]) + vector(B_OUT)
    unit_one, inverse_one = norm_parts(x_ref[...].astype(F32) + branch)
    first = (unit_one * vector(GAIN_ONE) + vector(SHIFT_ONE)).astype(BF16)
    first_ref[...] = first
    arrive(1)
    chunks = [slice(start, start + CHUNK) for start in range(0, FF, CHUNK)]

    def rise(index):
        return product(first, w_up[:, chunks[index]])

    def bend(index, upward):
        upward = upward + vectors[B_UP : B_UP + 1, chunks[index]]
        below, density = normal_parts(upward)
        active_ref[:, chunks[index]] = (upward * below).astype(BF16)
        slope[:, chunks[index]] = (below + upward * density).astype(BF16)

    pipelined(len(chunks), rise, bend, lambda *_: None)
    arrive(2, 3, 4)
    downward = product(active_ref[...], w_down[...]) + vector(B_DOWN)
    unit_two, inverse_two = norm_parts(first.astype(F32) + downward)
    encoded = (unit_two * vector(GAIN_TWO) + vector(SHIFT_TWO)).astype(BF16)

    @pl.when(tile < short_tiles)
    def _():
        enc_short_ref[...] = encoded

    @pl.when(tile >= short_tiles)
    def _():
        enc_long_ref[...] = encoded

    student = product(encoded, w_student[...]) + vector(B_STUDENT)
    query = vector(POOL_QUERY) * 0.125
    pooled_ref[...] = jnp.zeros_like(pooled_ref)

    def head():
        pooled = pooled_ref[...]
        wide_hidden = w_hidden[...].astype(F32)
        hidden = jnp.tanh(product(pooled, wide_hidden, HIGHEST_PRECISION) + vector(B_HIDDEN))
        logit_ref[0] = product(hidden, w_class[...], HIGHEST_PRECISION) + b_class[...]
        d_logits = logit_cot_ref[0]
        g_last[...] += column_sum(d_logits)
        g_class[...] += left_product(d_logits, hidden, HIGHEST_PRECISION)
        d_hidden = right_product(d_logits, w_class[...], HIGHEST_PRECISION)
        d_hidden = d_hidden * (1.0 - hidden * hidden)
        add_total(B_HIDDEN, d_hidden)
        g_hidden[...] += left_product(pooled, d_hidden, HIGHEST_PRECISION)
        return right_product(d_hidden, wide_hidden, HIGHEST_PRECISION)

    def pool(starts, size, lengths):
        kept = []
        for index, (start, length) in enumerate(zip(starts, lengths)):
            rows = student[start : start + size]
            both, weights = pool_weights(rows, query, length)
            pooled_ref[index : index + 1, :] = column_sum(both * rows)
            kept.append((start, rows, both, weights))
        d_pooled = head()
        for index, (start, rows, both, weights) in enumerate(kept):
            d_rows, d_query = student_back(rows, query, weights, both, d_pooled[index : index + 1])
            d_student_ref[start : start + size, :] = d_rows.astype(BF16)
            add_total(POOL_QUERY, d_query)

    @pl.when(tile < short_tiles)
    def _():
        pool(
            [seq * width for seq in range(per_tile)],
            width,
            [len_short[tile * per_tile + seq] for seq in range(per_tile)],
        )

    @pl.when(tile >= short_tiles)
    def _():
        pool([0], TILE, [len_long[tile - short_tiles]])

    d_student = d_student_ref[...]
    add_total(B_STUDENT, d_student)
    g_student[...] += left_product(encoded, d_student)
    cotangent = jnp.where(tile < short_tiles, cot_short_ref[...], cot_long_ref[...])
    d_second = cotangent.astype(F32) + right_product(d_student, w_student[...])
    add_total(GAIN_TWO, d_second * unit_two)
    add_total(SHIFT_TWO, d_second)
    d_resid_two = norm_back(d_second, vector(GAIN_TWO), unit_two, inverse_two)
    d_down = d_resid_two.astype(BF16)
    d_down_ref[...] = d_down
    add_total(B_DOWN, d_down)

    def fall(index):
        return right_product(d_down, w_down[chunks[index], :])

    def bend_back(index, d_active):
        d_up = (d_active * slope[:, chunks[index]].astype(F32)).astype(BF16)
        d_up_ref[:, chunks[index]] = d_up
        totals[B_UP : B_UP + 1, chunks[index]] += column_sum(d_up)

    pipelined(len(chunks), fall, bend_back, lambda *_: None)
    d_first = d_resid_two + right_product(d_up_ref[...], w_up[...])
    add_total(GAIN_ONE, d_first * unit_one)
    add_total(SHIFT_ONE, d_first)
    d_resid_one = norm_back(d_first, vector(GAIN_ONE), unit_one, inverse_one)
    d_resid_ref[...] = d_resid_one
    d_branch = d_resid_one.astype(BF16)
    d_branch_ref[...] = d_branch
    add_total(B_OUT, d_branch)
    d_context_ref[...] = right_product(d_branch, w_out[...]).astype(BF16)

    @pl.when(tile == pl.num_programs(0) - 1)
    def _():
        g_small[...] = jnp.zeros_like(g_small)
        for index, (start, count) in enumerate(VECTORS):
            for place in range(count):
                g_small[start + place : start + place + 1, :] = totals[
                    index : index + 1, place * BLK : (place + 1) * BLK
                ]
        g_small[CLASS_ROW : CLASS_ROW + NCLS, :] = g_class[:NCLS, :]
        g_small[LAST_ROW : LAST_ROW + 1, :] = g_last[...]


def feed(
    len_short, len_long, block_slot, x, context, cot_short, cot_long, logit_cot, small, blocks, short_tiles, width
):
    tiles = x.shape[0] // TILE
    long_tiles = tiles - short_tiles

    def whole(shape):
        return pl.BlockSpec(shape, lambda tile, *_: (0,) * len(shape), pipeline_mode=pl.Buffered(1))

    def kept(shape):
        return pl.BlockSpec(shape, lambda tile, *_: (0,) * len(shape))

    def rows(columns):
        return pl.BlockSpec((TILE, columns), lambda tile, *_: (tile, 0))

    short_rows = pl.BlockSpec((TILE, D), lambda tile, *_: (short_index(tile, short_tiles), 0))
    long_rows = pl.BlockSpec((TILE, D), lambda tile, *_: (long_index(tile, short_tiles), 0))
    logit_rows = pl.BlockSpec((1, 8, SD), lambda tile, *_: (tile, 0, 0))
    grad_shapes = ((D, SD), (SD, SD), (SMALL_ROWS, BLK))
    total = tiles * TILE
    return pl.pallas_call(
        partial(feed_kernel, short_tiles=short_tiles, width=width),
        grid_spec=pltpu.PrefetchScalarGridSpec(
            num_scalar_prefetch=3,
            grid=(tiles,),
            in_specs=[rows(D), rows(D), short_rows, long_rows, logit_rows]
            + [whole(array.shape) for array in small]
            + [pl.BlockSpec(memory_space=pltpu.HBM)],
            out_specs=[
                short_rows,
                long_rows,
                logit_rows,
                rows(D),
                rows(FF),
                rows(FF),
                rows(D),
                rows(D),
                rows(D),
                rows(D),
            ]
            + [kept(shape) for shape in grad_shapes],
            scratch_shapes=[
                pltpu.VMEM((TILE, FF), BF16),
                pltpu.VMEM((8, SD), F32),
                pltpu.VMEM((TILE, SD), BF16),
                pltpu.VMEM((D, D), BF16),
                pltpu.VMEM((D, FF), BF16),
                pltpu.VMEM((FF, D), BF16),
                pltpu.VMEM((D, SD), BF16),
                pltpu.VMEM((SD, SD), BF16),
                pltpu.VMEM((16, FF), F32),
                pltpu.VMEM((16, FF), F32),
                pltpu.VMEM((SD, SD), F32),
                pltpu.VMEM((1, SD), F32),
                pltpu.SemaphoreType.DMA((5,)),
            ],
        ),
        out_shape=[
            jax.ShapeDtypeStruct((short_tiles * TILE, D), BF16),
            jax.ShapeDtypeStruct((long_tiles * TILE, D), BF16),
            jax.ShapeDtypeStruct((tiles, 8, SD), F32),
            jax.ShapeDtypeStruct((total, D), BF16),
            jax.ShapeDtypeStruct((total, FF), BF16),
            jax.ShapeDtypeStruct((total, FF), BF16),
            jax.ShapeDtypeStruct((total, D), BF16),
            jax.ShapeDtypeStruct((total, D), BF16),
            jax.ShapeDtypeStruct((total, D), BF16),
            jax.ShapeDtypeStruct((total, D), F32),
        ]
        + [jax.ShapeDtypeStruct(shape, F32) for shape in grad_shapes],
        compiler_params=pltpu.CompilerParams(vmem_limit_bytes=62 * MIB),
        cost_estimate=pl.CostEstimate(
            flops=total * (8 * D * FF + 4 * D * D), bytes_accessed=70 * MIB, transcendentals=total * FF
        ),
        name="feed",
    )(len_short, len_long, block_slot, x, context, cot_short, cot_long, logit_cot, *small, blocks)


class Place:
    def __init__(self):
        self.quarter = lax.axis_index("dp")
        self.shard = lax.axis_index("fsdp")
        x = self.quarter % 2
        y = self.quarter // 2
        self.core = self.shard % 2
        self.z = self.shard // 2
        self.high = self.z // 2
        self.by_x = 2 * y + 1 - x
        self.by_y = 2 * (1 - y) + x
        self.across = 2 * (1 - y) + 1 - x
        self.sibling = (self.quarter, 2 * self.z + 1 - self.core)
        self.next_x = (self.by_x, self.shard)
        self.next_y = (self.by_y, self.shard)
        self.inner = (self.z > 0) & (self.z < 3)

    def at_z(self, z):
        return (self.quarter, 2 * z + self.core)


def transfer(source, target, send_sem, recv_sem, device):
    return pltpu.make_async_remote_copy(
        src_ref=source,
        dst_ref=target,
        send_sem=send_sem,
        recv_sem=recv_sem,
        device_id=device,
        device_id_type=pl.DeviceIdType.MESH,
    )


def greet(place, extra=()):
    barrier = pltpu.get_barrier_semaphore()

    def signal(device):
        pl.semaphore_signal(barrier, inc=1, device_id=device, device_id_type=pl.DeviceIdType.MESH)

    near = (place.sibling, place.next_x, place.next_y) + tuple(extra)
    for device in near:
        signal(device)

    @pl.when(place.z > 0)
    def _():
        signal(place.at_z(place.z - 1))

    @pl.when(place.z < 3)
    def _():
        signal(place.at_z(place.z + 1))

    pl.semaphore_wait(barrier, len(near) + 1 + (place.z + 1) // 2 % 2)


CUTS = 2
GATHER_SEMAPHORES = [
    pltpu.SemaphoreType.DMA((2 * CUTS,)),
    pltpu.SemaphoreType.DMA((3 * CUTS,)),
    pltpu.SemaphoreType.DMA((4 * CUTS,)),
    pltpu.SemaphoreType.DMA((12 * CUTS,)),
    pltpu.SemaphoreType.DMA((12 * CUTS,)),
    pltpu.SemaphoreType.DMA((1 + 15 * CUTS,)),
    pltpu.SemaphoreType.DMA((1 + 15 * CUTS,)),
    pltpu.SemaphoreType.DMA((8,)),
]


class Gather:
    def __init__(self, full, out, sems):
        self.place = place = Place()
        self.full, self.out = full, out
        (
            self.own_send,
            self.relay_send,
            self.z_recv,
            self.xy_send,
            self.xy_recv,
            self.core_send,
            self.core_recv,
            self.out_sems,
        ) = sems
        self.quarter = full.shape[1] // 4
        self.cut = self.quarter // CUTS
        self.first_part = (self.cut // 16 + 1) // 2 * 16
        z = place.z
        self.origins = (z + 1 - 2 * (z % 2), 2 - place.high, 3 * (1 - place.high))
        self.relays = (3 - z, 3 * (z - 1), 3 * (z - 1))

    def region(self, which, start, size):
        return self.full.at[which, pl.ds(pl.multiple_of(start, 16), size)]

    def pieces(self, which, turn):
        place, quarter, cut, part = self.place, self.quarter, self.cut, self.first_part
        skip = turn % CUTS * cut
        return (
            self.region(which, place.quarter * quarter + skip, cut),
            self.region(which, place.by_x * quarter + skip, cut),
            self.region(which, place.by_y * quarter + skip, cut),
            self.region(which, place.across * quarter + skip, part),
            self.region(which, place.across * quarter + skip + part, cut - part),
        )

    def own_copy(self, side, cut):
        place = self.place
        mine = self.pieces(place.shard, cut)[0]
        device = place.at_z(place.z - 1 + 2 * side)
        return transfer(
            mine,
            mine,
            self.own_send.at[side * CUTS + cut],
            self.z_recv.at[place.z * CUTS + cut],
            device,
        )

    def core_copy(self, index, ref):
        return transfer(ref, ref, self.core_send.at[index], self.core_recv.at[index], self.place.sibling)

    def xy_copy(self, index, ref, device):
        return transfer(ref, ref, self.xy_send.at[index], self.xy_recv.at[index], device)

    def store(self, index, which):
        return pltpu.make_async_copy(self.full.at[which], self.out.at[which], self.out_sems.at[index])

    def mirrored(self, step):
        return 2 * self.origins[step] + 1 - self.place.core

    def held(self, step):
        return 2 * self.origins[step] + self.place.core

    def start(self):
        place = self.place
        greet(place)
        for cut in range(CUTS):

            @pl.when(place.z > 0)
            def _():
                self.own_copy(0, cut).start()

            @pl.when(place.z < 3)
            def _():
                self.own_copy(1, cut).start()

        self.core_copy(0, self.full.at[place.shard]).start()
        self.store(0, place.shard).start()

    def relay(self, turn):
        step = turn // CUTS
        piece = self.pieces(self.held(step), turn)[0]
        device = self.place.at_z(self.relays[step])
        sem = self.z_recv.at[self.origins[step] * CUTS + turn % CUTS]
        return transfer(piece, piece, self.relay_send.at[turn], sem, device)

    def along_z(self, turn):
        place = self.place
        self.relay(turn).wait_recv()

        @pl.when(place.inner)
        def _():
            self.relay(turn).start()

        piece = self.pieces(self.held(turn // CUTS), turn)[0]
        self.xy_copy(4 * turn, piece, place.next_x).start()
        self.xy_copy(4 * turn + 1, piece, place.next_y).start()
        self.core_copy(1 + 5 * turn, piece).start()

    def along_xy(self, turn):
        place, part = self.place, self.first_part
        _, by_x, by_y, _, _ = self.pieces(self.held(turn // CUTS), turn)
        self.xy_copy(4 * turn, by_x, place.next_x).wait_recv()
        self.xy_copy(4 * turn + 2, by_x.at[pl.ds(0, part)], place.next_y).start()
        self.core_copy(2 + 5 * turn, by_x).start()
        self.xy_copy(4 * turn + 1, by_y, place.next_y).wait_recv()
        self.xy_copy(4 * turn + 3, by_y.at[pl.ds(part, self.cut - part)], place.next_x).start()
        self.core_copy(3 + 5 * turn, by_y).start()

    def across(self, turn):
        place = self.place
        step = turn // CUTS
        _, _, _, first, last = self.pieces(self.held(step), turn)
        self.xy_copy(4 * turn + 2, first, place.next_y).wait_recv()
        self.core_copy(4 + 5 * turn, first).start()
        self.xy_copy(4 * turn + 3, last, place.next_x).wait_recv()
        self.core_copy(5 + 5 * turn, last).start()
        if turn % CUTS == CUTS - 1:
            self.store(2 + 2 * step, self.held(step)).start()

    def core_own(self):
        which = 2 * self.place.z + 1 - self.place.core
        self.core_copy(0, self.full.at[which]).wait_recv()
        self.store(1, which).start()

    def core(self, step):
        which = self.mirrored(step)
        for turn in range(step * CUTS, (step + 1) * CUTS):
            for index, ref in enumerate(self.pieces(which, turn)):
                self.core_copy(1 + 5 * turn + index, ref).wait_recv()
        self.store(3 + 2 * step, which).start()

    def finish(self):
        place = self.place
        for cut in range(CUTS):

            @pl.when(place.z > 0)
            def _():
                self.own_copy(0, cut).wait_send()

            @pl.when(place.z < 3)
            def _():
                self.own_copy(1, cut).wait_send()

        self.core_copy(0, self.full.at[place.shard]).wait_send()
        self.store(0, place.shard).wait()
        self.store(1, 2 * place.z + 1 - place.core).wait()
        for turn in range(3 * CUTS):

            @pl.when(place.inner)
            def _():
                self.relay(turn).wait_send()

            pieces = self.pieces(self.held(turn // CUTS), turn)
            self.xy_copy(4 * turn, pieces[0], place.next_x).wait_send()
            self.xy_copy(4 * turn + 1, pieces[0], place.next_y).wait_send()
            self.xy_copy(4 * turn + 2, pieces[3], place.next_y).wait_send()
            self.xy_copy(4 * turn + 3, pieces[4], place.next_x).wait_send()
            for index, ref in enumerate(pieces):
                self.core_copy(1 + 5 * turn + index, ref).wait_send()
        for step in range(3):
            self.store(2 + 2 * step, self.held(step)).wait()
            self.store(3 + 2 * step, self.mirrored(step)).wait()


def gather_kernel(master_ref, out_ref, full, *sems):
    gather = Gather(full, out_ref, sems)
    full[gather.place.shard] = master_ref[...].astype(BF16)
    gather.start()
    turns = 3 * CUTS
    for turn in range(turns + 2):
        if turn < turns:
            gather.along_z(turn)
        if 1 <= turn <= turns:
            gather.along_xy(turn - 1)
        if turn >= 2:
            gather.across(turn - 2)
        if turn == 2:
            gather.core_own()
        if turn >= 4 and turn % CUTS == 0:
            gather.core(turn // CUTS - 2)
    gather.core(2)
    gather.finish()


def gather_shards(master):
    rows = master.shape[0] * BLK
    shards = lax.axis_size("fsdp")
    return pl.pallas_call(
        gather_kernel,
        in_specs=[pl.BlockSpec(memory_space=pltpu.VMEM)],
        out_specs=pl.BlockSpec(memory_space=pltpu.HBM),
        out_shape=jax.ShapeDtypeStruct((shards, rows, BLK), BF16),
        scratch_shapes=[pltpu.VMEM((shards, rows, BLK), BF16)] + GATHER_SEMAPHORES,
        compiler_params=pltpu.CompilerParams(
            collective_id=0, has_side_effects=True, vmem_limit_bytes=60 * MIB
        ),
        cost_estimate=pl.CostEstimate(flops=0, bytes_accessed=200 * MIB, transcendentals=0),
        name="gather",
    )(master.reshape(rows, BLK)).reshape(-1, BLK, BLK)


def add_rows(target, former, latter, rows, step):
    @pl.loop(0, rows // step)
    def _(index):
        part = pl.ds(pl.multiple_of(index * step, 16), step)
        target[part] = (former[part].astype(F32) + latter[part].astype(F32)).astype(BF16)


def reduce_scratch(rows):
    quarter = rows // 4
    half = quarter // 2
    return [
        pltpu.VMEM((4, rows, BLK), BF16),
        pltpu.VMEM((4, rows, BLK), BF16),
        pltpu.VMEM((4, 2, half, BLK), BF16),
        pltpu.VMEM((4, 2, half, BLK), BF16),
        pltpu.VMEM((4, half, BLK), BF16),
        pltpu.VMEM((4, half, BLK), BF16),
        pltpu.VMEM((5, quarter, BLK), BF16),
        pltpu.VMEM((rows, BLK), BF16),
        pltpu.SemaphoreType.DMA((4,)),
        pltpu.SemaphoreType.DMA((4,)),
        pltpu.SemaphoreType.DMA((4,)),
        pltpu.SemaphoreType.DMA((24,)),
        pltpu.SemaphoreType.DMA((24,)),
        pltpu.SemaphoreType.DMA((3,)),
        pltpu.SemaphoreType.DMA((5,)),
        pltpu.SemaphoreType.DMA((4,)),
        pltpu.SemaphoreType.DMA((4,)),
    ]


class Reduce:
    def __init__(self, terms, base, out, scratch):
        self.place = place = Place()
        self.terms, self.base, self.out = terms, base, out
        (
            self.mine,
            self.sib,
            self.from_x,
            self.from_y,
            self.late_y,
            self.late_x,
            self.from_z,
            self.result,
            self.load_sems,
            self.core_send,
            self.core_recv,
            self.xy_send,
            self.xy_recv,
            self.z_send,
            self.z_recv,
            self.last_send,
            self.last_recv,
        ) = scratch
        self.quarter = out.shape[0] // 4
        self.half = self.quarter // 2
        z, high = place.z, place.high
        low = 1 - high
        self.order = (3 * low, low * (2 - 2 * z) + high * (7 - 2 * z), 1 + z % 2, z)
        self.onward = (z + 1 - 2 * high, z + 1 - 2 * (z % 2), z + 1 - 2 * high)
        self.closing = (0, (z % 2) * low, high)
        self.far = place.at_z(z + 2 - 4 * high)
        self.near = place.at_z(z + 1 - 2 * (z % 2))

    def shard_terms(self, shard):
        rows = self.out.shape[0]
        return self.terms.at[pl.ds(pl.multiple_of(self.base + shard * rows, 16), rows)]

    def load(self, step):
        source = self.shard_terms(2 * self.order[step] + self.place.core)
        return pltpu.make_async_copy(source, self.mine.at[step], self.load_sems.at[step])

    def core_copy(self, step):
        return transfer(
            self.shard_terms(2 * self.order[step] + 1 - self.place.core),
            self.sib.at[step],
            self.core_send.at[step],
            self.core_recv.at[step],
            self.place.sibling,
        )

    def part(self, step, which, side):
        start = pl.multiple_of(which * self.quarter + side * self.half, 16)
        return self.mine.at[step, pl.ds(start, self.half)]

    def xy_copy(self, step, index):
        place = self.place
        source, target, device = (
            (self.part(step, place.by_x, 0), self.from_x.at[step, 0], place.next_x),
            (self.part(step, place.across, 0), self.from_x.at[step, 1], place.next_x),
            (self.part(step, place.by_y, 1), self.from_y.at[step, 0], place.next_y),
            (self.part(step, place.across, 1), self.from_y.at[step, 1], place.next_y),
            (self.part(step, place.by_y, 0), self.late_y.at[step], place.next_y),
            (self.part(step, place.by_x, 1), self.late_x.at[step], place.next_x),
        )[index]
        place = 6 * step + index
        return transfer(source, target, self.xy_send.at[place], self.xy_recv.at[place], device)

    def start(self):
        greet(self.place, (self.far,))
        for step in range(2):
            self.core_copy(step).start()
        for step in range(4):
            self.load(step).start()

    def core(self, step):
        place, quarter = self.place, self.quarter
        self.load(step).wait()
        self.core_copy(step).wait_recv()
        if step < 2:
            self.core_copy(step + 2).start()

        def add(which):
            block = pl.ds(pl.multiple_of(which * quarter, 16), quarter)
            mine = self.mine.at[step, block]
            add_rows(mine, mine, self.sib.at[step, block], quarter, self.half)

        add(place.by_x)
        add(place.across)
        self.xy_copy(step, 0).start()
        self.xy_copy(step, 1).start()
        add(place.by_y)
        self.xy_copy(step, 2).start()
        self.xy_copy(step, 3).start()
        add(place.quarter)

    def take(self, step, which, side, index, source):
        self.xy_copy(step, index).wait_recv()
        target = self.part(step, which, side)
        add_rows(target, target, source, self.half, self.half)

    def first(self, step):
        place = self.place
        self.take(step, place.by_y, 0, 1, self.from_x.at[step, 1])
        self.xy_copy(step, 4).start()
        self.take(step, place.by_x, 1, 3, self.from_y.at[step, 1])
        self.xy_copy(step, 5).start()
        self.take(step, place.quarter, 0, 0, self.from_x.at[step, 0])
        self.take(step, place.quarter, 1, 2, self.from_y.at[step, 0])

    def own_block(self, step):
        return self.mine.at[step, pl.ds(pl.multiple_of(self.place.quarter * self.quarter, 16), self.quarter)]

    def z_copy(self, step):
        goal = self.order[step]
        slot = goal + self.closing[step] * (4 - goal)
        return transfer(
            self.own_block(step),
            self.from_z.at[slot],
            self.z_send.at[step],
            self.z_recv.at[slot],
            self.place.at_z(self.onward[step]),
        )

    def take_z(self, step, slot):
        source = self.from_z.at[slot]
        transfer(source, source, self.z_send.at[0], self.z_recv.at[slot], self.near).wait_recv()
        block = self.own_block(step)
        add_rows(block, block, source, self.quarter, self.half)

    def second(self, step):
        place = self.place
        self.take(step, place.quarter, 0, 4, self.late_y.at[step])
        self.take(step, place.quarter, 1, 5, self.late_x.at[step])
        if step < 3:

            @pl.when(place.inner)
            def _():
                self.take_z(step, self.order[step])

            self.z_copy(step).start()
        else:

            @pl.when(place.z > 0)
            def _():
                self.take_z(step, place.z)

            @pl.when(place.z < 3)
            def _():
                self.take_z(step, 4)

    def final(self, which, side=None):
        start = pl.multiple_of(which * self.quarter + (0 if side is None else side * self.half), 16)
        return self.result.at[pl.ds(start, self.quarter if side is None else self.half)]

    def last_copy(self, index, ref):
        device = (self.place.next_x, self.place.next_y, self.place.next_y, self.place.next_x)[index]
        return transfer(ref, ref, self.last_send.at[index], self.last_recv.at[index], device)

    def share(self):
        own = self.final(self.place.quarter)
        own[...] = self.own_block(3)[...]
        self.last_copy(0, own).start()
        self.last_copy(1, own).start()

    def share_on(self):
        place = self.place
        self.last_copy(0, self.final(place.by_x)).wait_recv()
        self.last_copy(2, self.final(place.by_x, 0)).start()
        self.last_copy(1, self.final(place.by_y)).wait_recv()
        self.last_copy(3, self.final(place.by_y, 1)).start()

    def finish(self):
        place = self.place
        self.last_copy(2, self.final(place.across, 0)).wait_recv()
        self.last_copy(3, self.final(place.across, 1)).wait_recv()
        self.out[...] = self.result[...]
        for step in range(4):
            self.core_copy(step).wait_send()
            for index in range(6):
                self.xy_copy(step, index).wait_send()
            if step < 3:
                self.z_copy(step).wait_send()
        own = self.final(place.quarter)
        self.last_copy(0, own).wait_send()
        self.last_copy(1, own).wait_send()
        self.last_copy(2, self.final(place.by_x, 0)).wait_send()
        self.last_copy(3, self.final(place.by_y, 1)).wait_send()


def reduce_kernel(*refs, base, short_steps):
    terms, small_ref, d_ref, resid_ref, w_ref, out_ref, small_out, short_ref, long_ref = refs[:9]
    small_in, small_sum, small_send, small_recv = refs[9:13]
    reduce = Reduce(terms, base, out_ref, refs[13:])
    place = reduce.place
    partners = (place.sibling, place.next_x, place.next_y, reduce.near, reduce.far)

    def small_copy(level):
        return transfer(
            small_sum.at[level],
            small_in.at[level],
            small_send.at[level],
            small_recv.at[level],
            partners[level],
        )

    def small_start():
        small_sum[0] = small_ref[...]
        small_copy(0).start()

    def small_step(level):
        small_copy(level - 1).wait_recv()
        small_sum[level] = small_sum[level - 1] + small_in[level - 1]
        if level < 5:
            small_copy(level).start()
        else:
            small_out[...] = small_sum[5]

    run_events(
        pl.program_id(0),
        (
            (reduce.start, small_start),
            (partial(reduce.core, 0), partial(small_step, 1)),
            (partial(reduce.core, 1), partial(reduce.first, 0), partial(small_step, 2)),
            (
                partial(reduce.core, 2),
                partial(reduce.first, 1),
                partial(reduce.second, 0),
                partial(small_step, 3),
            ),
            (
                partial(reduce.core, 3),
                partial(reduce.first, 2),
                partial(reduce.second, 1),
                partial(small_step, 4),
            ),
            (partial(reduce.first, 3), partial(reduce.second, 2), partial(small_step, 5)),
            (partial(reduce.second, 3), reduce.share),
            (reduce.share_on,),
        ),
    )
    input_product(d_ref, resid_ref, w_ref, short_ref, long_ref, short_steps)

    @pl.when(pl.program_id(0) == pl.num_programs(0) - 1)
    def _():
        reduce.finish()
        for level in range(5):
            small_copy(level).wait_send()


def reduce_late(terms, base, rows, small, d_qkv, resid, w_qkv, short_tiles):
    steps = resid.shape[0] // INPUT_ROWS
    short_steps = short_tiles * TILE // INPUT_ROWS
    in_specs, out_specs = input_specs(short_steps)

    def whole(shape):
        return pl.BlockSpec(shape, lambda step: (0, 0), pipeline_mode=pl.Buffered(1))

    return pl.pallas_call(
        partial(reduce_kernel, base=base, short_steps=short_steps),
        grid=(steps,),
        in_specs=[pl.BlockSpec(memory_space=pltpu.HBM), whole(small.shape)] + in_specs,
        out_specs=[
            pl.BlockSpec((rows, BLK), lambda step: (0, 0)),
            pl.BlockSpec(small.shape, lambda step: (0, 0)),
        ]
        + out_specs,
        out_shape=[
            jax.ShapeDtypeStruct((rows, BLK), BF16),
            jax.ShapeDtypeStruct((SMALL_ROWS, BLK), F32),
            jax.ShapeDtypeStruct((short_steps * INPUT_ROWS, D), F32),
            jax.ShapeDtypeStruct(((steps - short_steps) * INPUT_ROWS, D), F32),
        ],
        scratch_shapes=[
            pltpu.VMEM((5, SMALL_ROWS, BLK), F32),
            pltpu.VMEM((6, SMALL_ROWS, BLK), F32),
            pltpu.SemaphoreType.DMA((5,)),
            pltpu.SemaphoreType.DMA((5,)),
        ]
        + reduce_scratch(rows),
        compiler_params=pltpu.CompilerParams(
            collective_id=3, has_side_effects=True, vmem_limit_bytes=60 * MIB
        ),
        cost_estimate=pl.CostEstimate(flops=0, bytes_accessed=200 * MIB, transcendentals=0),
        name="reduce",
    )(terms, small, d_qkv, resid, w_qkv)


def count_where(condition, axis):
    return jnp.sum(condition.astype(jnp.int32), axis=axis)


def slot_codes(slots, qkv_slots, slot_count, shards):
    early = slot_count - LATE
    shard = slots // slot_count
    begin = shard * slot_count
    inside = (qkv_slots[None, :] >= begin[:, None]) & (qkv_slots[None, :] < (begin + slot_count)[:, None])
    own = count_where(qkv_slots[None, :] == slots[:, None], 1)
    before = count_where(inside & (qkv_slots[None, :] < slots[:, None]), 1)
    number = count_where(inside, 1)
    position = jnp.where(own > 0, slot_count - number + before, slots - begin - before)
    code = jnp.where(
        position < early,
        shard * early + position,
        shards * early + shard * LATE + position - early,
    )
    return code, position, jnp.max(number)


def empty_slots(block_slot, all_slots):
    places = jnp.arange(all_slots, dtype=jnp.int32)
    empty_before = places + 1 - count_where(block_slot[None, :] <= places[:, None], 1)
    empty_index = jnp.arange(all_slots - NBLK, dtype=jnp.int32)
    return count_where(empty_before[None, :] <= empty_index[:, None], 1)


def update_kernel(
    position_ref,
    blocks,
    master,
    left_stat,
    right_stat,
    left_root,
    right_root,
    slot_grad,
    new_left,
    new_right,
    new_master,
):
    count = master.shape[0]
    first = pl.program_id(0) * count
    for index in range(count):
        start = pl.multiple_of(position_ref[first + index] * BLK, BLK)
        grad = blocks[pl.ds(start, BLK)]
        slot_grad[index] = grad.astype(F32)
        new_left[index] = STAT_DECAY * left_stat[index] + (1.0 - STAT_DECAY) * right_product(grad, grad)
        new_right[index] = STAT_DECAY * right_stat[index] + (1.0 - STAT_DECAY) * left_product(grad, grad)
        applied = product(left_root[index].astype(BF16), grad).astype(BF16)
        total = product(applied, right_root[index].astype(BF16))
        new_master[index] = master[index] - MATRIX_RATE * total


def update(position, blocks, master, left_stat, right_stat, left_root, right_root):
    slot_count = master.shape[0]
    group = max(size for size in range(1, 12) if slot_count % size == 0)
    some = pl.BlockSpec((group, BLK, BLK), lambda step, *_: (step, 0, 0))
    return pl.pallas_call(
        update_kernel,
        grid_spec=pltpu.PrefetchScalarGridSpec(
            num_scalar_prefetch=1,
            grid=(slot_count // group,),
            in_specs=[
                pl.BlockSpec(blocks.shape, lambda step, *_: (0, 0), pipeline_mode=pl.Buffered(1))
            ]
            + [some] * 5,
            out_specs=[some] * 4,
        ),
        out_shape=[jax.ShapeDtypeStruct(master.shape, F32)] * 4,
        compiler_params=pltpu.CompilerParams(vmem_limit_bytes=60 * MIB),
        cost_estimate=pl.CostEstimate(
            flops=14 * slot_count * BLK**3, bytes_accessed=36 * slot_count * BLK**2, transcendentals=0
        ),
        name="update",
    )(position, blocks, master, left_stat, right_stat, left_root, right_root)


def body(
    x_short,
    x_long,
    cot_short,
    cot_long,
    logit_cot_short,
    logit_cot_long,
    len_short,
    len_long,
    block_slot,
    master,
    left_stat,
    right_stat,
    left_root,
    right_root,
    small_params,
    small_first,
    small_second,
    own_transfers,
):
    slot_count = master.shape[0]
    shards = lax.axis_size("fsdp")
    all_slots = slot_count * shards
    short_seqs, width = x_short.shape[:2]
    long_seqs = x_long.shape[0]
    short_tiles = short_seqs * width // TILE
    per_tile = TILE // width
    empty = empty_slots(block_slot, all_slots)

    if own_transfers:
        early_count = slot_count - LATE
        own = jnp.arange(slot_count, dtype=jnp.int32) + slot_count * lax.axis_index("fsdp")
        code, position, most = slot_codes(
            jnp.concatenate([block_slot, empty, own]), block_slot[: 3 * 36], slot_count, shards
        )
        position = position[all_slots:]
        empty_code = code[NBLK:all_slots]
        code = code[:NBLK]
        fits = most <= LATE
        gathered = gather_shards(master)
    else:
        gathered = lax.all_gather(master.astype(BF16), "fsdp", axis=0, tiled=True)
    w_qkv = assemble(block_slot, gathered)
    pieces = unpack(small_params)
    params = jnp.pad(small_params, (0, SMALL_ROWS * BLK - small_params.shape[0])).reshape(SMALL_ROWS, BLK)
    w_class = jnp.pad(pieces[-2].reshape(SD, NCLS), ((0, 0), (0, SD - NCLS)))
    b_class = jnp.pad(pieces[-1].reshape(1, NCLS), ((0, 0), (0, SD - NCLS)))

    x, *qkv, context, probs_short, probs_long = attention(
        len_short,
        len_long,
        x_short.reshape(-1, D),
        x_long.reshape(-1, D),
        params,
        w_qkv,
        short_tiles,
        width,
    )

    logit_cot = jnp.concatenate(
        [
            jnp.pad(
                logit_cot_short.reshape(short_tiles, per_tile, NCLS),
                ((0, 0), (0, 8 - per_tile), (0, SD - NCLS)),
            ),
            jnp.pad(logit_cot_long.reshape(long_seqs, 1, NCLS), ((0, 0), (0, 7), (0, SD - NCLS))),
        ],
        axis=0,
    )
    (
        enc_short,
        enc_long,
        logits,
        first,
        active,
        d_up,
        d_down,
        d_branch,
        d_context,
        d_resid,
        g_student,
        g_hidden,
        g_small,
    ) = feed(
        len_short,
        len_long,
        block_slot,
        x,
        context,
        cot_short.reshape(-1, D),
        cot_long.reshape(-1, D),
        logit_cot,
        (params, w_class, b_class),
        gathered,
        short_tiles,
        width,
    )
    g_out = left_product(context, d_branch).astype(BF16)
    others = (g_out, g_student.astype(BF16), g_hidden.astype(BF16))
    if own_transfers:
        terms = feed_grads(code, empty_code, first, d_down, active, d_up, others, all_slots)
        *back, early_reduced = attention_back(
            qkv,
            probs_short,
            probs_long,
            d_context,
            short_tiles,
            terms.reshape(-1, BLK),
            early_count * BLK,
        )
    else:
        back = attention_back(qkv, probs_short, probs_long, d_context, short_tiles)
    d_qkv, g_b_query, g_b_value = back

    def reduce_all():
        slot_terms = feed_grads(block_slot, empty, first, d_down, active, d_up, others, all_slots)
        slot_terms, small_terms = input_weights(
            block_slot, x, d_qkv, g_small, g_b_query, g_b_value, slot_terms
        )
        reduced = lax.psum_scatter(slot_terms, "fsdp", scatter_dimension=0, tiled=True)
        return lax.psum(reduced, "dp").reshape(-1, BLK), small_terms

    if own_transfers:
        terms, small_terms = input_weights(code, x, d_qkv, g_small, g_b_query, g_b_value, terms)
        late_reduced, small_total, in_short, in_long = reduce_late(
            terms.reshape(-1, BLK),
            shards * early_count * BLK,
            LATE * BLK,
            small_terms,
            d_qkv,
            d_resid,
            w_qkv,
            short_tiles,
        )

        blocks = lax.cond(
            fits,
            lambda: jnp.concatenate([early_reduced, late_reduced], axis=0),
            lambda: reduce_all()[0],
        )
        position = jnp.where(fits, position, jnp.arange(slot_count, dtype=jnp.int32))
    else:
        in_short, in_long = input_grads(d_qkv, d_resid, w_qkv, short_tiles)
        blocks, small_terms = reduce_all()
        position = jnp.arange(slot_count, dtype=jnp.int32)
        small_total = lax.psum(small_terms, ("dp", "fsdp"))
    slot_grad, new_left, new_right, new_master = update(
        position, blocks, master, left_stat, right_stat, left_root, right_root
    )
    small_grad = jnp.concatenate(
        [
            small_total[:CLASS_ROW].reshape(-1),
            small_total[CLASS_ROW : CLASS_ROW + NCLS].T.reshape(-1),
            small_total[LAST_ROW, :NCLS],
        ]
    )
    new_first = BETA_ONE * small_first + (1.0 - BETA_ONE) * small_grad
    new_second = BETA_TWO * small_second + (1.0 - BETA_TWO) * small_grad * small_grad
    first_hat = new_first / (1.0 - BETA_ONE**STEP)
    second_hat = new_second / (1.0 - BETA_TWO**STEP)
    new_small = small_params - ADAM_RATE * first_hat / (jnp.sqrt(second_hat) + ADAM_EPSILON)
    return (
        enc_short.reshape(x_short.shape),
        logits[:short_tiles, :per_tile, :NCLS].reshape(short_seqs, NCLS),
        enc_long.reshape(x_long.shape),
        logits[short_tiles:, 0, :NCLS],
        in_short.reshape(x_short.shape),
        in_long.reshape(x_long.shape),
        slot_grad,
        new_left,
        new_right,
        new_master,
        new_first,
        new_second,
        new_small,
    )


def solution(mesh):
    both = ("dp", "fsdp")
    placed = (
        P(both, None, None),
        P(both, None, None),
        P(both, None, None),
        P(both, None, None),
        P(both, None),
        P(both, None),
        P(both),
        P(both),
        P(),
        P("fsdp", None, None),
        P("fsdp", None, None),
        P("fsdp", None, None),
        P("fsdp", None, None),
        P("fsdp", None, None),
        P(),
        P(),
        P(),
    )
    return jax.shard_map(
        partial(body, own_transfers=(mesh.shape["dp"], mesh.shape["fsdp"]) == (4, 8)),
        mesh=mesh,
        in_specs=placed,
        out_specs=(
            P(both, None, None),
            P(both, None),
            P(both, None, None),
            P(both, None),
            P(both, None, None),
            P(both, None, None),
            P("fsdp", None, None),
            P("fsdp", None, None),
            P("fsdp", None, None),
            P("fsdp", None, None),
            P(),
            P(),
            P(),
        ),
        check_vma=False,
    )
```

```python
from functools import partial

import jax
import jax.numpy as jnp
from jax import lax
from jax.experimental import pallas as pl
from jax.experimental.pallas import tpu as pltpu
from jax.sharding import PartitionSpec as P

D = 768
HEADS = 12
FF = 3072
SD = 128
PH = 2
NCLS = 14
BLK = 128
STEP = 10
NBLK = 439
TILE = 512
PAIRS = 3
GROUPS = 2
CHUNK = 768
LATE = 24

NORM_EPSILON = 1e-12
BETA_ONE = 0.9
BETA_TWO = 0.999
ADAM_EPSILON = 1e-08
ADAM_RATE = 0.1
MATRIX_RATE = 0.2
STAT_DECAY = 0.5
MASKED_SCORE = -1e30
HIGHEST_PRECISION = lax.Precision.HIGHEST
MIB = 1024 * 1024
F32 = jnp.float32
BF16 = jnp.bfloat16

def product(former, latter, precision=None):
    return jnp.dot(former, latter, preferred_element_type=F32, precision=precision)


def left_product(former, latter, precision=None):
    return lax.dot_general(
        former, latter, (((0,), (0,)), ((), ())), preferred_element_type=F32, precision=precision
    )


def right_product(former, latter, precision=None):
    return lax.dot_general(
        former, latter, (((1,), (1,)), ((), ())), preferred_element_type=F32, precision=precision
    )


def unpack(small_values):
    widths = (D, D, D, D, D, FF, D, D, D, SD, SD, SD, SD * NCLS, NCLS)
    pieces = []
    offset = 0
    for column_count in widths:
        pieces.append(small_values[offset : offset + column_count])
        offset += column_count
    return pieces


def each_block(first, row_count, col_count, action):
    def one_row(index, carry):
        row = pl.multiple_of(index * BLK, BLK)
        for col in range(col_count):
            action(first + index * col_count + col, row, col * BLK)
        return carry

    lax.fori_loop(0, row_count, one_row, 0)


def load_blocks(slot_ref, blocks, target, sem, first, row_count, col_count, col_start=0):
    def move(block, row, col):
        pltpu.make_async_copy(
            blocks.at[slot_ref[block]],
            target.at[pl.ds(row, BLK), pl.ds(col + col_start * BLK, BLK)],
            sem,
        ).start()

    each_block(first, row_count, col_count, move)


def wait_whole(target, sem):
    pltpu.make_async_copy(target, target, sem).wait()


def assemble_kernel(slot_ref, blocks, out, sem):
    for which in range(3):
        load_blocks(slot_ref, blocks, out, sem, 36 * which, 6, 6, 6 * which)
    wait_whole(out, sem)


def assemble(block_slot, blocks):
    return pl.pallas_call(
        assemble_kernel,
        grid_spec=pltpu.PrefetchScalarGridSpec(
            num_scalar_prefetch=1,
            grid=(1,),
            in_specs=[pl.BlockSpec(memory_space=pltpu.HBM)],
            out_specs=pl.BlockSpec(memory_space=pltpu.VMEM),
            scratch_shapes=[pltpu.SemaphoreType.DMA],
        ),
        out_shape=jax.ShapeDtypeStruct((D, 3 * D), BF16),
        compiler_params=pltpu.CompilerParams(vmem_limit_bytes=60 * MIB),
        name="assemble",
    )(block_slot, blocks)


def join_small(small_ref, query_ref, value_ref, small_out):
    small_out[...] = small_ref[...]
    for start, ref in ((0, query_ref), (D // BLK, value_ref)):
        for index in range(D // BLK):
            small_out[start + index : start + index + 1, :] = ref[:, index * BLK : (index + 1) * BLK]


PART = 256
ACROSS = PART // BLK


def feed_grads_kernel(
    code_ref,
    first_ref,
    d_down_ref,
    active_ref,
    d_up_ref,
    g_out,
    g_student,
    g_hidden,
    terms,
    first_turned,
    down_turned,
    up_stage,
    down_stage,
    up_sems,
    down_sems,
    other_sems,
):
    step = pl.program_id(0)
    last = pl.num_programs(0) - 1
    slot = step % 2
    others = ((g_out, 108, 6, 6), (g_student, 432, 6, 1), (g_hidden, 438, 1, 1))

    @pl.when(step == 0)
    def _():
        for which, (grad, first, row_count, col_count) in enumerate(others):

            def move(block, row, col, which=which, grad=grad):
                pltpu.make_async_copy(
                    grad.at[pl.ds(row, BLK), pl.ds(col, BLK)], terms.at[code_ref[block]], other_sems.at[which]
                ).start()

            each_block(first, row_count, col_count, move)
        first_turned[...] = first_ref[...].T
        down_turned[...] = d_down_ref[...].T

    @pl.when(step >= 2)
    def _():
        wait_whole(up_stage.at[slot], up_sems.at[slot])
        wait_whole(down_stage.at[slot], down_sems.at[slot])

    up_stage[slot] = product(first_turned[...], d_up_ref[...]).astype(BF16)
    down_stage[slot] = product(down_turned[...], active_ref[...]).T.astype(BF16)
    for row in range(D // BLK):
        for col in range(ACROSS):
            pltpu.make_async_copy(
                up_stage.at[slot, pl.ds(row * BLK, BLK), pl.ds(col * BLK, BLK)],
                terms.at[code_ref[144 + row * (FF // BLK) + step * ACROSS + col]],
                up_sems.at[slot],
            ).start()
            pltpu.make_async_copy(
                down_stage.at[slot, pl.ds(col * BLK, BLK), pl.ds(row * BLK, BLK)],
                terms.at[code_ref[288 + (step * ACROSS + col) * (D // BLK) + row]],
                down_sems.at[slot],
            ).start()

    @pl.when(step == last)
    def _():
        for place in range(2):
            wait_whole(up_stage.at[place], up_sems.at[place])
            wait_whole(down_stage.at[place], down_sems.at[place])
        for which, (grad, *_) in enumerate(others):
            wait_whole(grad, other_sems.at[which])


def feed_grads(code, first, d_down, active, d_up, others, slot_count):
    tokens = first.shape[0]

    def whole(shape):
        return pl.BlockSpec(shape, lambda step, *_: (0, 0), pipeline_mode=pl.Buffered(1))

    part = pl.BlockSpec((tokens, PART), lambda step, *_: (0, step))
    return pl.pallas_call(
        feed_grads_kernel,
        grid_spec=pltpu.PrefetchScalarGridSpec(
            num_scalar_prefetch=1,
            grid=(FF // PART,),
            in_specs=[whole(first.shape), whole(d_down.shape), part, part]
            + [whole(other.shape) for other in others],
            out_specs=pl.BlockSpec(memory_space=pltpu.HBM),
            scratch_shapes=[
                pltpu.VMEM((D, tokens), BF16),
                pltpu.VMEM((D, tokens), BF16),
                pltpu.VMEM((2, D, PART), BF16),
                pltpu.VMEM((2, PART, D), BF16),
                pltpu.SemaphoreType.DMA((2,)),
                pltpu.SemaphoreType.DMA((2,)),
                pltpu.SemaphoreType.DMA((3,)),
            ],
        ),
        out_shape=jax.ShapeDtypeStruct((slot_count, BLK, BLK), BF16),
        compiler_params=pltpu.CompilerParams(vmem_limit_bytes=60 * MIB),
        cost_estimate=pl.CostEstimate(
            flops=4 * tokens * D * FF, bytes_accessed=50 * MIB, transcendentals=0
        ),
        name="feed_grads",
    )(code, first, d_down, active, d_up, *others)


def input_weights_kernel(
    code_ref, x_ref, d_ref, small_ref, query_ref, value_ref, _, terms, small_out, turned, stage, sems
):
    step = pl.program_id(0)
    slot = step % 2

    @pl.when(step == 0)
    def _():
        join_small(small_ref, query_ref, value_ref, small_out)
        turned[...] = x_ref[...].T

    @pl.when(step >= 2)
    def _():
        wait_whole(stage.at[slot], sems.at[slot])

    stage[slot] = product(turned[...], d_ref[...]).astype(BF16)
    steps = D // PART
    first = (step // steps) * 36 + step % steps * ACROSS
    for row in range(D // BLK):
        for col in range(ACROSS):
            pltpu.make_async_copy(
                stage.at[slot, pl.ds(row * BLK, BLK), pl.ds(col * BLK, BLK)],
                terms.at[code_ref[first + row * (D // BLK) + col]],
                sems.at[slot],
            ).start()

    @pl.when(step == pl.num_programs(0) - 1)
    def _():
        for place in range(2):
            wait_whole(stage.at[place], sems.at[place])


def input_weights(code, x, d_qkv, small, g_query, g_value, terms):
    tokens = x.shape[0]

    def whole(shape):
        return pl.BlockSpec(shape, lambda step, *_: (0, 0), pipeline_mode=pl.Buffered(1))

    hbm = pl.BlockSpec(memory_space=pltpu.HBM)
    return pl.pallas_call(
        input_weights_kernel,
        grid_spec=pltpu.PrefetchScalarGridSpec(
            num_scalar_prefetch=1,
            grid=(3 * D // PART,),
            in_specs=[
                whole(x.shape),
                pl.BlockSpec((tokens, PART), lambda step, *_: (0, step)),
                whole(small.shape),
                whole(g_query.shape),
                whole(g_value.shape),
                hbm,
            ],
            out_specs=[hbm, pl.BlockSpec(small.shape, lambda step, *_: (0, 0))],
            scratch_shapes=[
                pltpu.VMEM((D, tokens), BF16),
                pltpu.VMEM((2, D, PART), BF16),
                pltpu.SemaphoreType.DMA((2,)),
            ],
        ),
        out_shape=[
            jax.ShapeDtypeStruct(terms.shape, BF16),
            jax.ShapeDtypeStruct(small.shape, F32),
        ],
        input_output_aliases={6: 0},
        compiler_params=pltpu.CompilerParams(vmem_limit_bytes=60 * MIB),
        cost_estimate=pl.CostEstimate(
            flops=6 * tokens * D * D, bytes_accessed=16 * MIB, transcendentals=0
        ),
        name="input_weights",
    )(code, x, d_qkv, small, g_query, g_value, terms)


def half_masks():
    lane = lax.broadcasted_iota(jnp.int32, (1, BLK), 1)
    low = (lane < BLK // 2).astype(BF16)
    return low, (1.0 - low.astype(F32)).astype(BF16)


def stack_heads(values, low, high):
    return jnp.concatenate([values * low, values * high], axis=0)


def pick_heads(values):
    rows = values.shape[0] // 2
    lane = lax.broadcasted_iota(jnp.int32, (rows, BLK), 1)
    return jnp.where(lane < BLK // 2, values[:rows], values[rows:])


def pipelined(count, before, middle, after):
    started = before(0)
    done = None
    for index in range(count):
        current = started
        if index + 1 < count:
            started = before(index + 1)
        if done is not None:
            after(index - 1, done)
        done = middle(index, current)
    after(count - 1, done)


def softmax(scores, length):
    visible = lax.broadcasted_iota(jnp.int32, scores.shape, 1) < length
    scores = jnp.where(visible, scores, MASKED_SCORE)
    powers = jnp.exp(scores - jnp.max(scores, axis=-1, keepdims=True))
    total = jnp.sum(powers, axis=-1, keepdims=True)
    return (powers * (1.0 / total)).astype(BF16)


def attention_kernel(
    len_short,
    len_long,
    x_short_ref,
    x_long_ref,
    params,
    w_ref,
    x_ref,
    q_ref,
    k_ref,
    v_ref,
    context_ref,
    short_ref,
    long_ref,
    bias,
    *,
    short_tiles,
):
    tile = pl.program_id(0)
    group = pl.program_id(1)
    low, high = half_masks()
    width = short_ref.shape[-1]
    per_tile = TILE // width

    wide = PAIRS * BLK
    start = pl.multiple_of(group * wide, wide)

    @pl.when((tile == 0) & (group == 0))
    def _():
        for which in range(2):
            for place in range(D // BLK):
                row = which * (D // BLK) + place
                bias[which : which + 1, place * BLK : (place + 1) * BLK] = params[row : row + 1, :]

    @pl.when((tile < short_tiles) & (group == 0))
    def _():
        x_ref[...] = x_short_ref[...]

    @pl.when((tile >= short_tiles) & (group == 0))
    def _():
        x_ref[...] = x_long_ref[...]

    rows_in = x_ref[...]
    queries = product(rows_in, w_ref[:, pl.ds(start, wide)]) + bias[0:1, pl.ds(start, wide)]
    q_ref[...] = (queries * 0.125).astype(BF16)
    k_ref[...] = product(rows_in, w_ref[:, pl.ds(D + start, wide)]).astype(BF16)
    values = product(rows_in, w_ref[:, pl.ds(2 * D + start, wide)]) + bias[1:2, pl.ds(start, wide)]
    v_ref[...] = values.astype(BF16)

    def attend(units, kept_ref):
        def scores(index):
            rows, keys, cols, _, _ = units[index]
            return right_product(stack_heads(q_ref[rows, cols], low, high), k_ref[keys, cols])

        def weigh(index, values):
            _, _, _, length, place = units[index]
            probs = softmax(values, length)
            kept_ref[place] = probs
            return probs

        def mix(index, probs):
            rows, keys, cols, _, _ = units[index]
            context_ref[rows, cols] = pick_heads(product(probs, v_ref[keys, cols])).astype(BF16)

        pipelined(len(units), scores, weigh, mix)

    @pl.when(tile < short_tiles)
    def _():
        units = []
        for seq in range(per_tile):
            rows = slice(seq * width, (seq + 1) * width)
            length = len_short[tile * per_tile + seq]
            for pair in range(PAIRS):
                cols = slice(pair * BLK, (pair + 1) * BLK)
                units.append((rows, rows, cols, length, (0, pair, seq)))
        attend(units, short_ref)

    @pl.when(tile >= short_tiles)
    def _():
        length = len_long[tile - short_tiles]
        half = TILE // 2
        units = []
        for pair in range(PAIRS):
            cols = slice(pair * BLK, (pair + 1) * BLK)
            for part in range(2):
                rows = slice(part * half, (part + 1) * half)
                units.append((rows, slice(0, TILE), cols, length, (0, pair, part)))
        attend(units, long_ref)


def run_events(step, events):
    for index, actions in enumerate(events):

        @pl.when(step == index)
        def _(actions=actions):
            for action in actions:
                action()


def probs_shapes(short_tiles, long_tiles, width):
    per_tile = TILE // width
    return (
        (short_tiles, 2 * PAIRS, per_tile, 2 * width, width),
        (long_tiles, 2 * PAIRS, 2, TILE, TILE),
    )


def short_index(tile, short_tiles):
    return jnp.minimum(tile, short_tiles - 1)


def long_index(tile, short_tiles):
    return jnp.maximum(tile - short_tiles, 0)


def probs_maps(short_tiles):
    def short_map(tile, group):
        last = jnp.minimum(tile // short_tiles, 1)
        return (short_index(tile, short_tiles), group + last * (GROUPS - 1 - group), 0, 0, 0)

    def long_map(tile, group):
        begun = jnp.minimum(tile // short_tiles, 1)
        return (long_index(tile, short_tiles), begun * group, 0, 0, 0)

    return short_map, long_map


def attention(len_short, len_long, x_short, x_long, params, w_qkv, short_tiles, width):
    tiles = (x_short.shape[0] + x_long.shape[0]) // TILE
    wide = PAIRS * BLK
    short_shape, long_shape = probs_shapes(short_tiles, tiles - short_tiles, width)
    short_map, long_map = probs_maps(short_tiles)
    flops = 4 * D * TILE * TILE * tiles + 6 * D * D * TILE * tiles
    rows = pl.BlockSpec((TILE, wide), lambda tile, group: (tile, group))
    scalars = pl.BlockSpec(memory_space=pltpu.SMEM)

    def whole(shape):
        return pl.BlockSpec(shape, lambda tile, group: (0,) * len(shape), pipeline_mode=pl.Buffered(1))

    in_specs = [
        scalars,
        scalars,
        pl.BlockSpec((TILE, D), lambda tile, group: (short_index(tile, short_tiles), 0)),
        pl.BlockSpec((TILE, D), lambda tile, group: (long_index(tile, short_tiles), 0)),
        whole(params.shape),
        whole((D, 3 * D)),
    ]
    out_specs = [
        pl.BlockSpec((TILE, D), lambda tile, group: (tile, 0)),
        rows,
        rows,
        rows,
        rows,
        pl.BlockSpec((1, PAIRS) + short_shape[2:], short_map),
        pl.BlockSpec((1, PAIRS) + long_shape[2:], long_map),
    ]
    out_shape = [jax.ShapeDtypeStruct((tiles * TILE, D), BF16)] * 5 + [
        jax.ShapeDtypeStruct(short_shape, BF16),
        jax.ShapeDtypeStruct(long_shape, BF16),
    ]
    arguments = [len_short, len_long, x_short, x_long, params, w_qkv]
    return pl.pallas_call(
        partial(attention_kernel, short_tiles=short_tiles),
        grid=(tiles, GROUPS),
        in_specs=in_specs,
        out_specs=out_specs,
        out_shape=out_shape,
        scratch_shapes=[pltpu.VMEM((8, D), F32)],
        compiler_params=pltpu.CompilerParams(vmem_limit_bytes=60 * MIB),
        cost_estimate=pl.CostEstimate(
            flops=flops, bytes_accessed=35 * MIB, transcendentals=HEADS * TILE * TILE * tiles // 2
        ),
        name="attention",
    )(*arguments)


def attention_back_kernel(*refs, short_tiles, transfers):
    q_ref, k_ref, v_ref, short_ref, long_ref, dc_ref = refs[:6]
    refs = refs[6:]
    if transfers:
        terms_ref, refs = refs[0], refs[1:]
    out_ref, bq_ref, bv_ref = refs[:3]
    tile = pl.program_id(0)
    group = pl.program_id(1)
    low, high = half_masks()
    width = short_ref.shape[-1]
    per_tile = TILE // width
    if transfers:
        reduce = Reduce(terms_ref, 0, refs[3], refs[4:])
        run_events(
            tile * GROUPS + group,
            (
                (reduce.start,),
                (partial(reduce.core, 0),),
                (partial(reduce.core, 1), partial(reduce.first, 0)),
                (partial(reduce.core, 2), partial(reduce.first, 1), partial(reduce.second, 0)),
                (partial(reduce.core, 3), partial(reduce.first, 2), partial(reduce.second, 1)),
                (partial(reduce.first, 3), partial(reduce.second, 2)),
                (partial(reduce.second, 3), reduce.share),
                (reduce.share_on,),
            ),
        )

    wide = PAIRS * BLK
    start = pl.multiple_of(group * wide, wide)

    def columns(which, cols):
        return pl.ds(pl.multiple_of(which * D + start + cols.start, BLK), BLK)

    def go_back(units, kept_ref, parts):
        sums = {}

        def spread_in(index):
            rows, keys, cols, _ = units[index]
            return right_product(stack_heads(dc_ref[rows, cols], low, high), v_ref[keys, cols])

        def differ(index, d_probs):
            wide = kept_ref[units[index][3]].astype(F32)
            weighted = wide * d_probs
            return (weighted - wide * jnp.sum(weighted, axis=-1, keepdims=True)).astype(BF16)

        def gather_up(index, d_scores):
            rows, keys, cols, place = units[index]
            d_queries = pick_heads(product(d_scores, k_ref[keys, cols])) * 0.125
            out_ref[rows, columns(0, cols)] = d_queries.astype(BF16)
            d_keys = left_product(d_scores, stack_heads(q_ref[rows, cols], low, high))
            d_values = left_product(kept_ref[place], stack_heads(dc_ref[rows, cols], low, high))
            if index % parts:
                d_keys += sums["keys"]
                d_values += sums["values"]
            if index % parts == parts - 1:
                out_ref[keys, columns(1, cols)] = d_keys.astype(BF16)
                out_ref[keys, columns(2, cols)] = d_values.astype(BF16)
            else:
                sums.update(keys=d_keys, values=d_values)

        pipelined(len(units), spread_in, differ, gather_up)

    @pl.when(tile < short_tiles)
    def _():
        units = []
        for seq in range(per_tile):
            rows = slice(seq * width, (seq + 1) * width)
            for pair in range(PAIRS):
                cols = slice(pair * BLK, (pair + 1) * BLK)
                units.append((rows, rows, cols, (0, pair, seq)))
        go_back(units, short_ref, 1)

    @pl.when(tile >= short_tiles)
    def _():
        half = TILE // 2
        units = []
        for pair in range(PAIRS):
            cols = slice(pair * BLK, (pair + 1) * BLK)
            for part in range(2):
                rows = slice(part * half, (part + 1) * half)
                units.append((rows, slice(0, TILE), cols, (0, pair, part)))
        go_back(units, long_ref, 2)

    @pl.when((tile == 0) & (group == 0))
    def _():
        bq_ref[...] = jnp.zeros_like(bq_ref)
        bv_ref[...] = jnp.zeros_like(bv_ref)

    bq_ref[:, pl.ds(start, wide)] += column_sum(out_ref[:, pl.ds(start, wide)])
    bv_ref[:, pl.ds(start, wide)] += column_sum(out_ref[:, pl.ds(2 * D + start, wide)])

    if transfers:

        @pl.when((tile == pl.num_programs(0) - 1) & (group == GROUPS - 1))
        def _():
            reduce.finish()


def attention_back(qkv, probs_short, probs_long, d_context, short_tiles, terms=None, count=0):
    tiles = d_context.shape[0] // TILE
    wide = PAIRS * BLK
    short_map, long_map = probs_maps(short_tiles)
    rows = pl.BlockSpec((TILE, wide), lambda tile, group: (tile, group))
    row = pl.BlockSpec((1, D), lambda tile, group: (0, 0))
    flops = 10 * D * TILE * TILE * tiles
    in_specs = [
        rows,
        rows,
        rows,
        pl.BlockSpec((1, PAIRS) + probs_short.shape[2:], short_map),
        pl.BlockSpec((1, PAIRS) + probs_long.shape[2:], long_map),
        rows,
    ]
    out_specs = [pl.BlockSpec((TILE, 3 * D), lambda tile, group: (tile, 0)), row, row]
    out_shape = [
        jax.ShapeDtypeStruct((tiles * TILE, 3 * D), BF16),
        jax.ShapeDtypeStruct((1, D), F32),
        jax.ShapeDtypeStruct((1, D), F32),
    ]
    arguments = [*qkv, probs_short, probs_long, d_context]
    scratch = []
    params = dict(vmem_limit_bytes=60 * MIB)
    if terms is not None:
        arguments.append(terms)
        in_specs.append(pl.BlockSpec(memory_space=pltpu.HBM))
        out_specs.append(pl.BlockSpec((count, BLK), lambda tile, group: (0, 0)))
        out_shape.append(jax.ShapeDtypeStruct((count, BLK), BF16))
        scratch = reduce_scratch(count)
        params.update(collective_id=2, has_side_effects=True)
    return pl.pallas_call(
        partial(attention_back_kernel, short_tiles=short_tiles, transfers=terms is not None),
        grid=(tiles, GROUPS),
        in_specs=in_specs,
        out_specs=out_specs,
        out_shape=out_shape,
        scratch_shapes=scratch,
        compiler_params=pltpu.CompilerParams(**params),
        cost_estimate=pl.CostEstimate(flops=flops, bytes_accessed=50 * MIB, transcendentals=0),
        name="attention_back",
    )(*arguments)


INPUT_ROWS = 256


def input_product(d_ref, resid_ref, w_ref, short_ref, long_ref, short_steps):
    step = pl.program_id(0)
    total = resid_ref[...] + right_product(d_ref[...], w_ref[...])

    @pl.when(step < short_steps)
    def _():
        short_ref[...] = total

    @pl.when(step >= short_steps)
    def _():
        long_ref[...] = total


def input_specs(short_steps):
    rows = [pl.BlockSpec((INPUT_ROWS, width), lambda step: (step, 0)) for width in (3 * D, D)]
    whole = pl.BlockSpec((D, 3 * D), lambda step: (0, 0), pipeline_mode=pl.Buffered(1))
    outs = [
        pl.BlockSpec((INPUT_ROWS, D), lambda step: (short_index(step, short_steps), 0)),
        pl.BlockSpec((INPUT_ROWS, D), lambda step: (long_index(step, short_steps), 0)),
    ]
    return rows + [whole], outs


def input_grads(d_qkv, resid, w_qkv, short_tiles):
    steps = resid.shape[0] // INPUT_ROWS
    short_steps = short_tiles * TILE // INPUT_ROWS
    in_specs, out_specs = input_specs(short_steps)
    return pl.pallas_call(
        partial(input_product, short_steps=short_steps),
        grid=(steps,),
        in_specs=in_specs,
        out_specs=out_specs,
        out_shape=[
            jax.ShapeDtypeStruct((short_steps * INPUT_ROWS, D), F32),
            jax.ShapeDtypeStruct(((steps - short_steps) * INPUT_ROWS, D), F32),
        ],
        compiler_params=pltpu.CompilerParams(vmem_limit_bytes=60 * MIB),
        name="input_grads",
    )(d_qkv, resid, w_qkv)


def normal_parts(values):
    below = 0.5 * lax.erf(values * 0.7071067811865476) + 0.5
    return below, jnp.exp(-0.5 * values * values) * 0.3989422804014327


B_OUT, GAIN_ONE, SHIFT_ONE, B_UP, B_DOWN, GAIN_TWO, SHIFT_TWO, B_STUDENT, POOL_QUERY, B_HIDDEN = range(10)
VECTORS = (
    (12, 6),
    (18, 6),
    (24, 6),
    (30, 24),
    (54, 6),
    (60, 6),
    (66, 6),
    (72, 1),
    (73, 1),
    (74, 1),
)
CLASS_ROW = 75
LAST_ROW = 91
SMALL_ROWS = 96


def norm_parts(values):
    center = values - jnp.mean(values, axis=-1, keepdims=True)
    spread = jnp.mean(center * center, axis=-1, keepdims=True)
    inverse = lax.rsqrt(spread + NORM_EPSILON)
    return center * inverse, inverse


def norm_back(d_values, gain, unit, inverse):
    d_unit = d_values * gain
    return inverse * (
        d_unit
        - jnp.mean(d_unit, axis=-1, keepdims=True)
        - unit * jnp.mean(d_unit * unit, axis=-1, keepdims=True)
    )


def column_sum(values):
    return jnp.sum(values.astype(F32), axis=0, keepdims=True)


def pool_weights(student, query, length):
    scaled = student * query
    lane = lax.broadcasted_iota(jnp.int32, scaled.shape, 1)
    place = lax.broadcasted_iota(jnp.int32, (scaled.shape[0], 1), 0)
    weights = []
    for side in (lane < SD // PH, lane >= SD // PH):
        scores = jnp.sum(jnp.where(side, scaled, 0.0), axis=-1, keepdims=True)
        scores = jnp.where(place < length, scores, MASKED_SCORE)
        powers = jnp.exp(scores - jnp.max(scores, axis=0, keepdims=True))
        weights.append(powers / jnp.sum(powers, axis=0, keepdims=True))
    return jnp.where(lane < SD // PH, weights[0], weights[1]), weights


def student_back(student, query, weights, both, d_pooled):
    lane = lax.broadcasted_iota(jnp.int32, student.shape, 1)
    moved = student * d_pooled
    d_scores = []
    for side, weight in zip((lane < SD // PH, lane >= SD // PH), weights):
        d_weight = jnp.sum(jnp.where(side, moved, 0.0), axis=-1, keepdims=True)
        d_scores.append(weight * (d_weight - jnp.sum(weight * d_weight, axis=0, keepdims=True)))
    d_score = jnp.where(lane < SD // PH, d_scores[0], d_scores[1])
    d_query = jnp.sum(d_score * student, axis=0, keepdims=True) * 0.125
    return both * d_pooled + d_score * query, d_query


def feed_kernel(
    len_short,
    len_long,
    slot_ref,
    x_ref,
    context_ref,
    cot_short_ref,
    cot_long_ref,
    logit_cot_short,
    logit_cot_long,
    params,
    w_class_ref,
    b_class_ref,
    blocks,
    enc_short_ref,
    enc_long_ref,
    logits_short,
    logits_long,
    first_ref,
    active_ref,
    d_up_ref,
    d_down_ref,
    d_branch_ref,
    d_context_ref,
    d_resid_ref,
    g_student,
    g_hidden,
    g_small,
    slope,
    pooled_ref,
    d_student_ref,
    w_out,
    w_up,
    w_down,
    w_student,
    w_hidden,
    vectors,
    totals,
    g_class,
    g_last,
    w_class,
    b_class,
    logit_cot,
    sems,
    *,
    short_tiles,
    width,
):
    tile = pl.program_id(0)
    per_tile = TILE // width
    loads = ((w_out, 108, 6, 6), (w_up, 144, 6, 24), (w_down, 288, 24, 6), (w_student, 432, 6, 1), (w_hidden, 438, 1, 1))

    def arrive(*indices):
        @pl.when(tile == 0)
        def _():
            for index in indices:
                wait_whole(loads[index][0], sems.at[index])

    @pl.when(tile == 0)
    def _():
        for index, (target, block, row_count, col_count) in enumerate(loads):
            load_blocks(slot_ref, blocks, target, sems.at[index], block, row_count, col_count)
        for index, (start, count) in enumerate(VECTORS):
            for place in range(count):
                vectors[index : index + 1, place * BLK : (place + 1) * BLK] = params[
                    start + place : start + place + 1, :
                ]
        for ref in (totals, g_class, g_last, g_student, g_hidden, w_class, b_class):
            ref[...] = jnp.zeros_like(ref)
        w_class[:, :NCLS] = w_class_ref[...]
        b_class[:, :NCLS] = b_class_ref[...]

    def vector(index):
        return vectors[index : index + 1, : VECTORS[index][1] * BLK]

    def add_total(index, values):
        totals[index : index + 1, : VECTORS[index][1] * BLK] += column_sum(values)

    arrive(0)
    branch = product(context_ref[...], w_out[...]) + vector(B_OUT)
    unit_one, inverse_one = norm_parts(x_ref[...].astype(F32) + branch)
    first = (unit_one * vector(GAIN_ONE) + vector(SHIFT_ONE)).astype(BF16)
    first_ref[...] = first
    arrive(1)
    chunks = [slice(start, start + CHUNK) for start in range(0, FF, CHUNK)]

    def rise(index):
        return product(first, w_up[:, chunks[index]])

    def bend(index, upward):
        upward = upward + vectors[B_UP : B_UP + 1, chunks[index]]
        below, density = normal_parts(upward)
        active_ref[:, chunks[index]] = (upward * below).astype(BF16)
        slope[:, chunks[index]] = (below + upward * density).astype(BF16)

    pipelined(len(chunks), rise, bend, lambda *_: None)
    arrive(2, 3, 4)
    downward = product(active_ref[...], w_down[...]) + vector(B_DOWN)
    unit_two, inverse_two = norm_parts(first.astype(F32) + downward)
    encoded = (unit_two * vector(GAIN_TWO) + vector(SHIFT_TWO)).astype(BF16)

    @pl.when(tile < short_tiles)
    def _():
        enc_short_ref[...] = encoded

    @pl.when(tile >= short_tiles)
    def _():
        enc_long_ref[...] = encoded

    student = product(encoded, w_student[...]) + vector(B_STUDENT)
    query = vector(POOL_QUERY) * 0.125
    pooled_ref[...] = jnp.zeros_like(pooled_ref)

    def head():
        pooled = pooled_ref[...]
        wide_hidden = w_hidden[...].astype(F32)
        hidden = jnp.tanh(product(pooled, wide_hidden, HIGHEST_PRECISION) + vector(B_HIDDEN))
        logits = product(hidden, w_class[...], HIGHEST_PRECISION) + b_class[...]
        d_logits = logit_cot[...]
        g_last[...] += column_sum(d_logits)
        g_class[...] += left_product(d_logits, hidden, HIGHEST_PRECISION)
        d_hidden = right_product(d_logits, w_class[...], HIGHEST_PRECISION)
        d_hidden = d_hidden * (1.0 - hidden * hidden)
        add_total(B_HIDDEN, d_hidden)
        g_hidden[...] += left_product(pooled, d_hidden, HIGHEST_PRECISION)
        return logits, right_product(d_hidden, wide_hidden, HIGHEST_PRECISION)

    def pool(starts, size, lengths, cot_ref, logits_ref, first):
        count = len(starts)
        logit_cot[...] = jnp.zeros_like(logit_cot)
        for index in range(count):
            logit_cot[index : index + 1, :NCLS] = cot_ref[pl.ds(first + index, 1), :]
        kept = []
        for index, (start, length) in enumerate(zip(starts, lengths)):
            rows = student[start : start + size]
            both, weights = pool_weights(rows, query, length)
            pooled_ref[index : index + 1, :] = column_sum(both * rows)
            kept.append((start, rows, both, weights))
        logits, d_pooled = head()
        for index in range(count):
            logits_ref[pl.ds(first + index, 1), :] = logits[index : index + 1, :NCLS]
        for index, (start, rows, both, weights) in enumerate(kept):
            d_rows, d_query = student_back(rows, query, weights, both, d_pooled[index : index + 1])
            d_student_ref[start : start + size, :] = d_rows.astype(BF16)
            add_total(POOL_QUERY, d_query)

    @pl.when(tile < short_tiles)
    def _():
        pool(
            [seq * width for seq in range(per_tile)],
            width,
            [len_short[tile * per_tile + seq] for seq in range(per_tile)],
            logit_cot_short,
            logits_short,
            tile * per_tile,
        )

    @pl.when(tile >= short_tiles)
    def _():
        long = tile - short_tiles
        pool([0], TILE, [len_long[long]], logit_cot_long, logits_long, long)

    d_student = d_student_ref[...]
    add_total(B_STUDENT, d_student)
    g_student[...] += left_product(encoded, d_student)
    cotangent = jnp.where(tile < short_tiles, cot_short_ref[...], cot_long_ref[...])
    d_second = cotangent.astype(F32) + right_product(d_student, w_student[...])
    add_total(GAIN_TWO, d_second * unit_two)
    add_total(SHIFT_TWO, d_second)
    d_resid_two = norm_back(d_second, vector(GAIN_TWO), unit_two, inverse_two)
    d_down = d_resid_two.astype(BF16)
    d_down_ref[...] = d_down
    add_total(B_DOWN, d_down)

    def fall(index):
        return right_product(d_down, w_down[chunks[index], :])

    def bend_back(index, d_active):
        d_up = (d_active * slope[:, chunks[index]].astype(F32)).astype(BF16)
        d_up_ref[:, chunks[index]] = d_up
        totals[B_UP : B_UP + 1, chunks[index]] += column_sum(d_up)

    pipelined(len(chunks), fall, bend_back, lambda *_: None)
    d_first = d_resid_two + right_product(d_up_ref[...], w_up[...])
    add_total(GAIN_ONE, d_first * unit_one)
    add_total(SHIFT_ONE, d_first)
    d_resid_one = norm_back(d_first, vector(GAIN_ONE), unit_one, inverse_one)
    d_resid_ref[...] = d_resid_one
    d_branch = d_resid_one.astype(BF16)
    d_branch_ref[...] = d_branch
    add_total(B_OUT, d_branch)
    d_context_ref[...] = right_product(d_branch, w_out[...]).astype(BF16)

    @pl.when(tile == pl.num_programs(0) - 1)
    def _():
        g_small[...] = jnp.zeros_like(g_small)
        for index, (start, count) in enumerate(VECTORS):
            for place in range(count):
                g_small[start + place : start + place + 1, :] = totals[
                    index : index + 1, place * BLK : (place + 1) * BLK
                ]
        g_small[CLASS_ROW : CLASS_ROW + NCLS, :] = g_class[:NCLS, :]
        g_small[LAST_ROW : LAST_ROW + 1, :] = g_last[...]


def feed(
    len_short, len_long, block_slot, x, context, cot_short, cot_long, logit_cots, small, blocks, short_tiles, width
):
    tiles = x.shape[0] // TILE
    long_tiles = tiles - short_tiles

    def whole(shape):
        return pl.BlockSpec(shape, lambda tile, *_: (0,) * len(shape), pipeline_mode=pl.Buffered(1))

    def kept(shape):
        return pl.BlockSpec(shape, lambda tile, *_: (0,) * len(shape))

    def rows(columns):
        return pl.BlockSpec((TILE, columns), lambda tile, *_: (tile, 0))

    short_rows = pl.BlockSpec((TILE, D), lambda tile, *_: (short_index(tile, short_tiles), 0))
    long_rows = pl.BlockSpec((TILE, D), lambda tile, *_: (long_index(tile, short_tiles), 0))
    grad_shapes = ((D, SD), (SD, SD), (SMALL_ROWS, BLK))
    total = tiles * TILE
    return pl.pallas_call(
        partial(feed_kernel, short_tiles=short_tiles, width=width),
        grid_spec=pltpu.PrefetchScalarGridSpec(
            num_scalar_prefetch=3,
            grid=(tiles,),
            in_specs=[rows(D), rows(D), short_rows, long_rows]
            + [whole(array.shape) for array in (*logit_cots, *small)]
            + [pl.BlockSpec(memory_space=pltpu.HBM)],
            out_specs=[
                short_rows,
                long_rows,
                kept(logit_cots[0].shape),
                kept(logit_cots[1].shape),
                rows(D),
                rows(FF),
                rows(FF),
                rows(D),
                rows(D),
                rows(D),
                rows(D),
            ]
            + [kept(shape) for shape in grad_shapes],
            scratch_shapes=[
                pltpu.VMEM((TILE, FF), BF16),
                pltpu.VMEM((8, SD), F32),
                pltpu.VMEM((TILE, SD), BF16),
                pltpu.VMEM((D, D), BF16),
                pltpu.VMEM((D, FF), BF16),
                pltpu.VMEM((FF, D), BF16),
                pltpu.VMEM((D, SD), BF16),
                pltpu.VMEM((SD, SD), BF16),
                pltpu.VMEM((16, FF), F32),
                pltpu.VMEM((16, FF), F32),
                pltpu.VMEM((SD, SD), F32),
                pltpu.VMEM((1, SD), F32),
                pltpu.VMEM((SD, SD), F32),
                pltpu.VMEM((1, SD), F32),
                pltpu.VMEM((8, SD), F32),
                pltpu.SemaphoreType.DMA((5,)),
            ],
        ),
        out_shape=[
            jax.ShapeDtypeStruct((short_tiles * TILE, D), BF16),
            jax.ShapeDtypeStruct((long_tiles * TILE, D), BF16),
            jax.ShapeDtypeStruct(logit_cots[0].shape, F32),
            jax.ShapeDtypeStruct(logit_cots[1].shape, F32),
            jax.ShapeDtypeStruct((total, D), BF16),
            jax.ShapeDtypeStruct((total, FF), BF16),
            jax.ShapeDtypeStruct((total, FF), BF16),
            jax.ShapeDtypeStruct((total, D), BF16),
            jax.ShapeDtypeStruct((total, D), BF16),
            jax.ShapeDtypeStruct((total, D), BF16),
            jax.ShapeDtypeStruct((total, D), F32),
        ]
        + [jax.ShapeDtypeStruct(shape, F32) for shape in grad_shapes],
        compiler_params=pltpu.CompilerParams(vmem_limit_bytes=62 * MIB),
        cost_estimate=pl.CostEstimate(
            flops=total * (8 * D * FF + 4 * D * D), bytes_accessed=70 * MIB, transcendentals=total * FF
        ),
        name="feed",
    )(len_short, len_long, block_slot, x, context, cot_short, cot_long, *logit_cots, *small, blocks)


class Place:
    def __init__(self):
        self.quarter = lax.axis_index("dp")
        self.shard = lax.axis_index("fsdp")
        x = self.quarter % 2
        y = self.quarter // 2
        self.core = self.shard % 2
        self.z = self.shard // 2
        self.high = self.z // 2
        self.by_x = 2 * y + 1 - x
        self.by_y = 2 * (1 - y) + x
        self.across = 2 * (1 - y) + 1 - x
        self.sibling = (self.quarter, 2 * self.z + 1 - self.core)
        self.next_x = (self.by_x, self.shard)
        self.next_y = (self.by_y, self.shard)
        self.inner = (self.z > 0) & (self.z < 3)

    def at_z(self, z):
        return (self.quarter, 2 * z + self.core)


def transfer(source, target, send_sem, recv_sem, device):
    return pltpu.make_async_remote_copy(
        src_ref=source,
        dst_ref=target,
        send_sem=send_sem,
        recv_sem=recv_sem,
        device_id=device,
        device_id_type=pl.DeviceIdType.MESH,
    )


def greet(place, extra=()):
    barrier = pltpu.get_barrier_semaphore()

    def signal(device):
        pl.semaphore_signal(barrier, inc=1, device_id=device, device_id_type=pl.DeviceIdType.MESH)

    near = (place.sibling, place.next_x, place.next_y) + tuple(extra)
    for device in near:
        signal(device)

    @pl.when(place.z > 0)
    def _():
        signal(place.at_z(place.z - 1))

    @pl.when(place.z < 3)
    def _():
        signal(place.at_z(place.z + 1))

    pl.semaphore_wait(barrier, len(near) + 1 + (place.z + 1) // 2 % 2)


CUTS = 2
GATHER_SEMAPHORES = [
    pltpu.SemaphoreType.DMA((2 * CUTS,)),
    pltpu.SemaphoreType.DMA((3 * CUTS,)),
    pltpu.SemaphoreType.DMA((4 * CUTS,)),
    pltpu.SemaphoreType.DMA((12 * CUTS,)),
    pltpu.SemaphoreType.DMA((12 * CUTS,)),
    pltpu.SemaphoreType.DMA((1 + 15 * CUTS,)),
    pltpu.SemaphoreType.DMA((1 + 15 * CUTS,)),
    pltpu.SemaphoreType.DMA((8,)),
]


class Gather:
    def __init__(self, full, out, sems):
        self.place = place = Place()
        self.full, self.out = full, out
        (
            self.own_send,
            self.relay_send,
            self.z_recv,
            self.xy_send,
            self.xy_recv,
            self.core_send,
            self.core_recv,
            self.out_sems,
        ) = sems
        self.quarter = full.shape[1] // 4
        self.cut = self.quarter // CUTS
        self.first_part = (self.cut // 16 + 1) // 2 * 16
        z = place.z
        self.origins = (z + 1 - 2 * (z % 2), 2 - place.high, 3 * (1 - place.high))
        self.relays = (3 - z, 3 * (z - 1), 3 * (z - 1))

    def region(self, which, start, size):
        return self.full.at[which, pl.ds(pl.multiple_of(start, 16), size)]

    def pieces(self, which, turn):
        place, quarter, cut, part = self.place, self.quarter, self.cut, self.first_part
        skip = turn % CUTS * cut
        return (
            self.region(which, place.quarter * quarter + skip, cut),
            self.region(which, place.by_x * quarter + skip, cut),
            self.region(which, place.by_y * quarter + skip, cut),
            self.region(which, place.across * quarter + skip, part),
            self.region(which, place.across * quarter + skip + part, cut - part),
        )

    def own_copy(self, side, cut):
        place = self.place
        mine = self.pieces(place.shard, cut)[0]
        device = place.at_z(place.z - 1 + 2 * side)
        return transfer(
            mine,
            mine,
            self.own_send.at[side * CUTS + cut],
            self.z_recv.at[place.z * CUTS + cut],
            device,
        )

    def core_copy(self, index, ref):
        return transfer(ref, ref, self.core_send.at[index], self.core_recv.at[index], self.place.sibling)

    def xy_copy(self, index, ref, device):
        return transfer(ref, ref, self.xy_send.at[index], self.xy_recv.at[index], device)

    def store(self, index, which):
        return pltpu.make_async_copy(self.full.at[which], self.out.at[which], self.out_sems.at[index])

    def mirrored(self, step):
        return 2 * self.origins[step] + 1 - self.place.core

    def held(self, step):
        return 2 * self.origins[step] + self.place.core

    def start(self):
        place = self.place
        greet(place)
        for cut in range(CUTS):

            @pl.when(place.z > 0)
            def _():
                self.own_copy(0, cut).start()

            @pl.when(place.z < 3)
            def _():
                self.own_copy(1, cut).start()

        self.core_copy(0, self.full.at[place.shard]).start()
        self.store(0, place.shard).start()

    def relay(self, turn):
        step = turn // CUTS
        piece = self.pieces(self.held(step), turn)[0]
        device = self.place.at_z(self.relays[step])
        sem = self.z_recv.at[self.origins[step] * CUTS + turn % CUTS]
        return transfer(piece, piece, self.relay_send.at[turn], sem, device)

    def along_z(self, turn):
        place = self.place
        self.relay(turn).wait_recv()

        @pl.when(place.inner)
        def _():
            self.relay(turn).start()

        piece = self.pieces(self.held(turn // CUTS), turn)[0]
        self.xy_copy(4 * turn, piece, place.next_x).start()
        self.xy_copy(4 * turn + 1, piece, place.next_y).start()
        self.core_copy(1 + 5 * turn, piece).start()

    def along_xy(self, turn):
        place, part = self.place, self.first_part
        _, by_x, by_y, _, _ = self.pieces(self.held(turn // CUTS), turn)
        self.xy_copy(4 * turn, by_x, place.next_x).wait_recv()
        self.xy_copy(4 * turn + 2, by_x.at[pl.ds(0, part)], place.next_y).start()
        self.core_copy(2 + 5 * turn, by_x).start()
        self.xy_copy(4 * turn + 1, by_y, place.next_y).wait_recv()
        self.xy_copy(4 * turn + 3, by_y.at[pl.ds(part, self.cut - part)], place.next_x).start()
        self.core_copy(3 + 5 * turn, by_y).start()

    def across(self, turn):
        place = self.place
        step = turn // CUTS
        _, _, _, first, last = self.pieces(self.held(step), turn)
        self.xy_copy(4 * turn + 2, first, place.next_y).wait_recv()
        self.core_copy(4 + 5 * turn, first).start()
        self.xy_copy(4 * turn + 3, last, place.next_x).wait_recv()
        self.core_copy(5 + 5 * turn, last).start()
        if turn % CUTS == CUTS - 1:
            self.store(2 + 2 * step, self.held(step)).start()

    def core_own(self):
        which = 2 * self.place.z + 1 - self.place.core
        self.core_copy(0, self.full.at[which]).wait_recv()
        self.store(1, which).start()

    def core(self, step):
        which = self.mirrored(step)
        for turn in range(step * CUTS, (step + 1) * CUTS):
            for index, ref in enumerate(self.pieces(which, turn)):
                self.core_copy(1 + 5 * turn + index, ref).wait_recv()
        self.store(3 + 2 * step, which).start()

    def finish(self):
        place = self.place
        for cut in range(CUTS):

            @pl.when(place.z > 0)
            def _():
                self.own_copy(0, cut).wait_send()

            @pl.when(place.z < 3)
            def _():
                self.own_copy(1, cut).wait_send()

        self.core_copy(0, self.full.at[place.shard]).wait_send()
        self.store(0, place.shard).wait()
        self.store(1, 2 * place.z + 1 - place.core).wait()
        for turn in range(3 * CUTS):

            @pl.when(place.inner)
            def _():
                self.relay(turn).wait_send()

            pieces = self.pieces(self.held(turn // CUTS), turn)
            self.xy_copy(4 * turn, pieces[0], place.next_x).wait_send()
            self.xy_copy(4 * turn + 1, pieces[0], place.next_y).wait_send()
            self.xy_copy(4 * turn + 2, pieces[3], place.next_y).wait_send()
            self.xy_copy(4 * turn + 3, pieces[4], place.next_x).wait_send()
            for index, ref in enumerate(pieces):
                self.core_copy(1 + 5 * turn + index, ref).wait_send()
        for step in range(3):
            self.store(2 + 2 * step, self.held(step)).wait()
            self.store(3 + 2 * step, self.mirrored(step)).wait()


def gather_kernel(master_ref, out_ref, full, *sems):
    gather = Gather(full, out_ref, sems)
    full[gather.place.shard] = master_ref[...].astype(BF16)
    gather.start()
    turns = 3 * CUTS
    for turn in range(turns + 2):
        if turn < turns:
            gather.along_z(turn)
        if 1 <= turn <= turns:
            gather.along_xy(turn - 1)
        if turn >= 2:
            gather.across(turn - 2)
        if turn == 2:
            gather.core_own()
        if turn >= 4 and turn % CUTS == 0:
            gather.core(turn // CUTS - 2)
    gather.core(2)
    gather.finish()


def gather_shards(master):
    rows = master.shape[0] * BLK
    shards = lax.axis_size("fsdp")
    return pl.pallas_call(
        gather_kernel,
        in_specs=[pl.BlockSpec(memory_space=pltpu.VMEM)],
        out_specs=pl.BlockSpec(memory_space=pltpu.HBM),
        out_shape=jax.ShapeDtypeStruct((shards, rows, BLK), BF16),
        scratch_shapes=[pltpu.VMEM((shards, rows, BLK), BF16)] + GATHER_SEMAPHORES,
        compiler_params=pltpu.CompilerParams(
            collective_id=0, has_side_effects=True, vmem_limit_bytes=60 * MIB
        ),
        cost_estimate=pl.CostEstimate(flops=0, bytes_accessed=200 * MIB, transcendentals=0),
        name="gather",
    )(master.reshape(rows, BLK)).reshape(-1, BLK, BLK)


def add_rows(target, former, latter, rows, step):
    @pl.loop(0, rows // step)
    def _(index):
        part = pl.ds(pl.multiple_of(index * step, 16), step)
        target[part] = (former[part].astype(F32) + latter[part].astype(F32)).astype(BF16)


def reduce_scratch(rows):
    quarter = rows // 4
    half = quarter // 2
    return [
        pltpu.VMEM((4, rows, BLK), BF16),
        pltpu.VMEM((4, rows, BLK), BF16),
        pltpu.VMEM((4, 2, half, BLK), BF16),
        pltpu.VMEM((4, 2, half, BLK), BF16),
        pltpu.VMEM((4, half, BLK), BF16),
        pltpu.VMEM((4, half, BLK), BF16),
        pltpu.VMEM((5, quarter, BLK), BF16),
        pltpu.VMEM((rows, BLK), BF16),
        pltpu.SemaphoreType.DMA((4,)),
        pltpu.SemaphoreType.DMA((4,)),
        pltpu.SemaphoreType.DMA((4,)),
        pltpu.SemaphoreType.DMA((24,)),
        pltpu.SemaphoreType.DMA((24,)),
        pltpu.SemaphoreType.DMA((3,)),
        pltpu.SemaphoreType.DMA((5,)),
        pltpu.SemaphoreType.DMA((4,)),
        pltpu.SemaphoreType.DMA((4,)),
    ]


class Reduce:
    def __init__(self, terms, base, out, scratch):
        self.place = place = Place()
        self.terms, self.base, self.out = terms, base, out
        (
            self.mine,
            self.sib,
            self.from_x,
            self.from_y,
            self.late_y,
            self.late_x,
            self.from_z,
            self.result,
            self.load_sems,
            self.core_send,
            self.core_recv,
            self.xy_send,
            self.xy_recv,
            self.z_send,
            self.z_recv,
            self.last_send,
            self.last_recv,
        ) = scratch
        self.quarter = out.shape[0] // 4
        self.half = self.quarter // 2
        z, high = place.z, place.high
        low = 1 - high
        self.order = (3 * low, low * (2 - 2 * z) + high * (7 - 2 * z), 1 + z % 2, z)
        self.onward = (z + 1 - 2 * high, z + 1 - 2 * (z % 2), z + 1 - 2 * high)
        self.closing = (0, (z % 2) * low, high)
        self.far = place.at_z(z + 2 - 4 * high)
        self.near = place.at_z(z + 1 - 2 * (z % 2))

    def shard_terms(self, shard):
        rows = self.out.shape[0]
        return self.terms.at[pl.ds(pl.multiple_of(self.base + shard * rows, 16), rows)]

    def load(self, step):
        source = self.shard_terms(2 * self.order[step] + self.place.core)
        return pltpu.make_async_copy(source, self.mine.at[step], self.load_sems.at[step])

    def core_copy(self, step):
        return transfer(
            self.shard_terms(2 * self.order[step] + 1 - self.place.core),
            self.sib.at[step],
            self.core_send.at[step],
            self.core_recv.at[step],
            self.place.sibling,
        )

    def part(self, step, which, side):
        start = pl.multiple_of(which * self.quarter + side * self.half, 16)
        return self.mine.at[step, pl.ds(start, self.half)]

    def xy_copy(self, step, index):
        place = self.place
        source, target, device = (
            (self.part(step, place.by_x, 0), self.from_x.at[step, 0], place.next_x),
            (self.part(step, place.across, 0), self.from_x.at[step, 1], place.next_x),
            (self.part(step, place.by_y, 1), self.from_y.at[step, 0], place.next_y),
            (self.part(step, place.across, 1), self.from_y.at[step, 1], place.next_y),
            (self.part(step, place.by_y, 0), self.late_y.at[step], place.next_y),
            (self.part(step, place.by_x, 1), self.late_x.at[step], place.next_x),
        )[index]
        place = 6 * step + index
        return transfer(source, target, self.xy_send.at[place], self.xy_recv.at[place], device)

    def start(self):
        greet(self.place, (self.far,))
        for step in range(2):
            self.core_copy(step).start()
        for step in range(4):
            self.load(step).start()

    def core(self, step):
        place, quarter = self.place, self.quarter
        self.load(step).wait()
        self.core_copy(step).wait_recv()
        if step < 2:
            self.core_copy(step + 2).start()

        def add(which):
            block = pl.ds(pl.multiple_of(which * quarter, 16), quarter)
            mine = self.mine.at[step, block]
            add_rows(mine, mine, self.sib.at[step, block], quarter, self.half)

        add(place.by_x)
        add(place.across)
        self.xy_copy(step, 0).start()
        self.xy_copy(step, 1).start()
        add(place.by_y)
        self.xy_copy(step, 2).start()
        self.xy_copy(step, 3).start()
        add(place.quarter)

    def take(self, step, which, side, index, source):
        self.xy_copy(step, index).wait_recv()
        target = self.part(step, which, side)
        add_rows(target, target, source, self.half, self.half)

    def first(self, step):
        place = self.place
        self.take(step, place.by_y, 0, 1, self.from_x.at[step, 1])
        self.xy_copy(step, 4).start()
        self.take(step, place.by_x, 1, 3, self.from_y.at[step, 1])
        self.xy_copy(step, 5).start()
        self.take(step, place.quarter, 0, 0, self.from_x.at[step, 0])
        self.take(step, place.quarter, 1, 2, self.from_y.at[step, 0])

    def own_block(self, step):
        return self.mine.at[step, pl.ds(pl.multiple_of(self.place.quarter * self.quarter, 16), self.quarter)]

    def z_copy(self, step):
        goal = self.order[step]
        slot = goal + self.closing[step] * (4 - goal)
        return transfer(
            self.own_block(step),
            self.from_z.at[slot],
            self.z_send.at[step],
            self.z_recv.at[slot],
            self.place.at_z(self.onward[step]),
        )

    def take_z(self, step, slot):
        source = self.from_z.at[slot]
        transfer(source, source, self.z_send.at[0], self.z_recv.at[slot], self.near).wait_recv()
        block = self.own_block(step)
        add_rows(block, block, source, self.quarter, self.half)

    def second(self, step):
        place = self.place
        self.take(step, place.quarter, 0, 4, self.late_y.at[step])
        self.take(step, place.quarter, 1, 5, self.late_x.at[step])
        if step < 3:

            @pl.when(place.inner)
            def _():
                self.take_z(step, self.order[step])

            self.z_copy(step).start()
        else:

            @pl.when(place.z > 0)
            def _():
                self.take_z(step, place.z)

            @pl.when(place.z < 3)
            def _():
                self.take_z(step, 4)

    def final(self, which, side=None):
        start = pl.multiple_of(which * self.quarter + (0 if side is None else side * self.half), 16)
        return self.result.at[pl.ds(start, self.quarter if side is None else self.half)]

    def last_copy(self, index, ref):
        device = (self.place.next_x, self.place.next_y, self.place.next_y, self.place.next_x)[index]
        return transfer(ref, ref, self.last_send.at[index], self.last_recv.at[index], device)

    def share(self):
        own = self.final(self.place.quarter)
        own[...] = self.own_block(3)[...]
        self.last_copy(0, own).start()
        self.last_copy(1, own).start()

    def share_on(self):
        place = self.place
        self.last_copy(0, self.final(place.by_x)).wait_recv()
        self.last_copy(2, self.final(place.by_x, 0)).start()
        self.last_copy(1, self.final(place.by_y)).wait_recv()
        self.last_copy(3, self.final(place.by_y, 1)).start()

    def finish(self):
        place = self.place
        self.last_copy(2, self.final(place.across, 0)).wait_recv()
        self.last_copy(3, self.final(place.across, 1)).wait_recv()
        self.out[...] = self.result[...]
        for step in range(4):
            self.core_copy(step).wait_send()
            for index in range(6):
                self.xy_copy(step, index).wait_send()
            if step < 3:
                self.z_copy(step).wait_send()
        own = self.final(place.quarter)
        self.last_copy(0, own).wait_send()
        self.last_copy(1, own).wait_send()
        self.last_copy(2, self.final(place.by_x, 0)).wait_send()
        self.last_copy(3, self.final(place.by_y, 1)).wait_send()


def reduce_kernel(*refs, base, short_steps):
    terms, small_ref, d_ref, resid_ref, w_ref, out_ref, small_out, short_ref, long_ref = refs[:9]
    small_in, small_sum, small_send, small_recv = refs[9:13]
    reduce = Reduce(terms, base, out_ref, refs[13:])
    place = reduce.place
    partners = (place.sibling, place.next_x, place.next_y, reduce.near, reduce.far)

    def small_copy(level):
        return transfer(
            small_sum.at[level],
            small_in.at[level],
            small_send.at[level],
            small_recv.at[level],
            partners[level],
        )

    def small_start():
        small_sum[0] = small_ref[...]
        small_copy(0).start()

    def small_step(level):
        small_copy(level - 1).wait_recv()
        small_sum[level] = small_sum[level - 1] + small_in[level - 1]
        if level < 5:
            small_copy(level).start()
        else:
            small_out[...] = small_sum[5]

    run_events(
        pl.program_id(0),
        (
            (reduce.start, small_start),
            (partial(reduce.core, 0), partial(small_step, 1)),
            (partial(reduce.core, 1), partial(reduce.first, 0), partial(small_step, 2)),
            (
                partial(reduce.core, 2),
                partial(reduce.first, 1),
                partial(reduce.second, 0),
                partial(small_step, 3),
            ),
            (
                partial(reduce.core, 3),
                partial(reduce.first, 2),
                partial(reduce.second, 1),
                partial(small_step, 4),
            ),
            (partial(reduce.first, 3), partial(reduce.second, 2), partial(small_step, 5)),
            (partial(reduce.second, 3), reduce.share),
            (reduce.share_on,),
        ),
    )
    input_product(d_ref, resid_ref, w_ref, short_ref, long_ref, short_steps)

    @pl.when(pl.program_id(0) == pl.num_programs(0) - 1)
    def _():
        reduce.finish()
        for level in range(5):
            small_copy(level).wait_send()


def reduce_late(terms, base, rows, small, d_qkv, resid, w_qkv, short_tiles):
    steps = resid.shape[0] // INPUT_ROWS
    short_steps = short_tiles * TILE // INPUT_ROWS
    in_specs, out_specs = input_specs(short_steps)

    def whole(shape):
        return pl.BlockSpec(shape, lambda step: (0, 0), pipeline_mode=pl.Buffered(1))

    return pl.pallas_call(
        partial(reduce_kernel, base=base, short_steps=short_steps),
        grid=(steps,),
        in_specs=[pl.BlockSpec(memory_space=pltpu.HBM), whole(small.shape)] + in_specs,
        out_specs=[
            pl.BlockSpec((rows, BLK), lambda step: (0, 0)),
            pl.BlockSpec(small.shape, lambda step: (0, 0)),
        ]
        + out_specs,
        out_shape=[
            jax.ShapeDtypeStruct((rows, BLK), BF16),
            jax.ShapeDtypeStruct((SMALL_ROWS, BLK), F32),
            jax.ShapeDtypeStruct((short_steps * INPUT_ROWS, D), F32),
            jax.ShapeDtypeStruct(((steps - short_steps) * INPUT_ROWS, D), F32),
        ],
        scratch_shapes=[
            pltpu.VMEM((5, SMALL_ROWS, BLK), F32),
            pltpu.VMEM((6, SMALL_ROWS, BLK), F32),
            pltpu.SemaphoreType.DMA((5,)),
            pltpu.SemaphoreType.DMA((5,)),
        ]
        + reduce_scratch(rows),
        compiler_params=pltpu.CompilerParams(
            collective_id=3, has_side_effects=True, vmem_limit_bytes=60 * MIB
        ),
        cost_estimate=pl.CostEstimate(flops=0, bytes_accessed=200 * MIB, transcendentals=0),
        name="reduce",
    )(terms, small, d_qkv, resid, w_qkv)


def count_where(condition, axis):
    return jnp.sum(condition.astype(jnp.int32), axis=axis)


def slot_codes(slots, qkv_slots, slot_count, shards):
    early = slot_count - LATE
    shard = slots // slot_count
    begin = shard * slot_count
    inside = (qkv_slots[None, :] >= begin[:, None]) & (qkv_slots[None, :] < (begin + slot_count)[:, None])
    own = count_where(qkv_slots[None, :] == slots[:, None], 1)
    before = count_where(inside & (qkv_slots[None, :] < slots[:, None]), 1)
    number = count_where(inside, 1)
    position = jnp.where(own > 0, slot_count - number + before, slots - begin - before)
    code = jnp.where(
        position < early,
        shard * early + position,
        shards * early + shard * LATE + position - early,
    )
    return code, position, jnp.max(number)


def update_kernel(
    position_ref,
    held_ref,
    early,
    late,
    master,
    left_stat,
    right_stat,
    left_root,
    right_root,
    slot_grad,
    new_left,
    new_right,
    new_master,
):
    count = master.shape[0]
    first = pl.program_id(0) * count
    split = early.shape[0] // BLK

    def block(ref, place):
        return ref[pl.ds(pl.multiple_of(place * BLK, BLK), BLK)]

    def grad_of(index):
        place = position_ref[first + index]
        grad = jnp.where(
            place < split,
            block(early, jnp.minimum(place, split - 1)),
            block(late, jnp.maximum(place - split, 0)),
        )
        return jnp.where(held_ref[first + index] > 0, grad, jnp.zeros_like(grad))

    for begin in range(0, count, 4):
        some = range(begin, min(begin + 4, count))
        grads = [grad_of(index) for index in some]
        applied = [product(left_root[index].astype(BF16), grad) for index, grad in zip(some, grads)]
        outer_left = [right_product(grad, grad) for grad in grads]
        outer_right = [left_product(grad, grad) for grad in grads]
        totals = [
            product(part.astype(BF16), right_root[index].astype(BF16)) for index, part in zip(some, applied)
        ]
        for place, index in enumerate(some):
            slot_grad[index] = grads[place].astype(F32)
            new_left[index] = STAT_DECAY * left_stat[index] + (1.0 - STAT_DECAY) * outer_left[place]
            new_right[index] = STAT_DECAY * right_stat[index] + (1.0 - STAT_DECAY) * outer_right[place]
            new_master[index] = master[index] - MATRIX_RATE * totals[place]


def update(position, held, early, late, master, left_stat, right_stat, left_root, right_root):
    slot_count = master.shape[0]
    group = max(size for size in range(1, 12) if slot_count % size == 0)
    some = pl.BlockSpec((group, BLK, BLK), lambda step, *_: (step, 0, 0))

    def whole(shape):
        return pl.BlockSpec(shape, lambda step, *_: (0, 0), pipeline_mode=pl.Buffered(1))

    return pl.pallas_call(
        update_kernel,
        grid_spec=pltpu.PrefetchScalarGridSpec(
            num_scalar_prefetch=2,
            grid=(slot_count // group,),
            in_specs=[whole(early.shape), whole(late.shape)] + [some] * 5,
            out_specs=[some] * 4,
        ),
        out_shape=[jax.ShapeDtypeStruct(master.shape, F32)] * 4,
        compiler_params=pltpu.CompilerParams(vmem_limit_bytes=60 * MIB),
        cost_estimate=pl.CostEstimate(
            flops=8 * slot_count * BLK**3, bytes_accessed=36 * slot_count * BLK**2, transcendentals=0
        ),
        name="update",
    )(position, held, early, late, master, left_stat, right_stat, left_root, right_root)


def body(
    x_short,
    x_long,
    cot_short,
    cot_long,
    logit_cot_short,
    logit_cot_long,
    len_short,
    len_long,
    block_slot,
    master,
    left_stat,
    right_stat,
    left_root,
    right_root,
    small_params,
    small_first,
    small_second,
    own_transfers,
):
    slot_count = master.shape[0]
    shards = lax.axis_size("fsdp")
    all_slots = slot_count * shards
    short_seqs, width = x_short.shape[:2]
    long_seqs = x_long.shape[0]
    short_tiles = short_seqs * width // TILE
    per_tile = TILE // width

    own = jnp.arange(slot_count, dtype=jnp.int32) + slot_count * lax.axis_index("fsdp")
    held = jnp.any(block_slot[None, :] == own[:, None], axis=1).astype(jnp.int32)
    if own_transfers:
        early_count = slot_count - LATE
        code, position, most = slot_codes(
            jnp.concatenate([block_slot, own]), block_slot[: 3 * 36], slot_count, shards
        )
        position = position[NBLK:]
        code = code[:NBLK]
        fits = most <= LATE
        gathered = gather_shards(master)
    else:
        gathered = lax.all_gather(master.astype(BF16), "fsdp", axis=0, tiled=True)
    w_qkv = assemble(block_slot, gathered)
    pieces = unpack(small_params)
    params = jnp.pad(small_params, (0, SMALL_ROWS * BLK - small_params.shape[0])).reshape(SMALL_ROWS, BLK)
    w_class = pieces[-2].reshape(SD, NCLS)
    b_class = pieces[-1].reshape(1, NCLS)
    x, *qkv, context, probs_short, probs_long = attention(
        len_short,
        len_long,
        x_short.reshape(-1, D),
        x_long.reshape(-1, D),
        params,
        w_qkv,
        short_tiles,
        width,
    )

    (
        enc_short,
        enc_long,
        logits_short,
        logits_long,
        first,
        active,
        d_up,
        d_down,
        d_branch,
        d_context,
        d_resid,
        g_student,
        g_hidden,
        g_small,
    ) = feed(
        len_short,
        len_long,
        block_slot,
        x,
        context,
        cot_short.reshape(-1, D),
        cot_long.reshape(-1, D),
        (logit_cot_short, logit_cot_long),
        (params, w_class, b_class),
        gathered,
        short_tiles,
        width,
    )
    g_out = left_product(context, d_branch).astype(BF16)
    others = (g_out, g_student.astype(BF16), g_hidden.astype(BF16))
    if own_transfers:
        terms = feed_grads(code, first, d_down, active, d_up, others, all_slots)
        *back, early_reduced = attention_back(
            qkv,
            probs_short,
            probs_long,
            d_context,
            short_tiles,
            terms.reshape(-1, BLK),
            early_count * BLK,
        )
    else:
        back = attention_back(qkv, probs_short, probs_long, d_context, short_tiles)
    d_qkv, g_b_query, g_b_value = back

    def reduce_all():
        slot_terms = feed_grads(block_slot, first, d_down, active, d_up, others, all_slots)
        slot_terms, small_terms = input_weights(
            block_slot, x, d_qkv, g_small, g_b_query, g_b_value, slot_terms
        )
        reduced = lax.psum_scatter(slot_terms, "fsdp", scatter_dimension=0, tiled=True)
        return lax.psum(reduced, "dp").reshape(-1, BLK), small_terms

    def renew(places, early, late):
        return update(
            places, held, early, late, master, left_stat, right_stat, left_root, right_root
        )

    def renew_all(blocks):
        return renew(jnp.arange(slot_count, dtype=jnp.int32), blocks, blocks)

    if own_transfers:
        terms, small_terms = input_weights(code, x, d_qkv, g_small, g_b_query, g_b_value, terms)
        late_reduced, small_total, in_short, in_long = reduce_late(
            terms.reshape(-1, BLK),
            shards * early_count * BLK,
            LATE * BLK,
            small_terms,
            d_qkv,
            d_resid,
            w_qkv,
            short_tiles,
        )

        updated = lax.cond(
            fits,
            lambda: renew(position, early_reduced, late_reduced),
            lambda: renew_all(reduce_all()[0]),
        )
    else:
        in_short, in_long = input_grads(d_qkv, d_resid, w_qkv, short_tiles)
        blocks, small_terms = reduce_all()
        updated = renew_all(blocks)
        small_total = lax.psum(small_terms, ("dp", "fsdp"))
    slot_grad, new_left, new_right, new_master = updated
    small_grad = jnp.concatenate(
        [
            small_total[:CLASS_ROW].reshape(-1),
            small_total[CLASS_ROW : CLASS_ROW + NCLS].T.reshape(-1),
            small_total[LAST_ROW, :NCLS],
        ]
    )
    new_first = BETA_ONE * small_first + (1.0 - BETA_ONE) * small_grad
    new_second = BETA_TWO * small_second + (1.0 - BETA_TWO) * small_grad * small_grad
    first_hat = new_first / (1.0 - BETA_ONE**STEP)
    second_hat = new_second / (1.0 - BETA_TWO**STEP)
    new_small = small_params - ADAM_RATE * first_hat / (jnp.sqrt(second_hat) + ADAM_EPSILON)
    return (
        enc_short.reshape(x_short.shape),
        logits_short,
        enc_long.reshape(x_long.shape),
        logits_long,
        in_short.reshape(x_short.shape),
        in_long.reshape(x_long.shape),
        slot_grad,
        new_left,
        new_right,
        new_master,
        new_first,
        new_second,
        new_small,
    )


def solution(mesh):
    both = ("dp", "fsdp")
    placed = (
        P(both, None, None),
        P(both, None, None),
        P(both, None, None),
        P(both, None, None),
        P(both, None),
        P(both, None),
        P(both),
        P(both),
        P(),
        P("fsdp", None, None),
        P("fsdp", None, None),
        P("fsdp", None, None),
        P("fsdp", None, None),
        P("fsdp", None, None),
        P(),
        P(),
        P(),
    )
    return jax.shard_map(
        partial(body, own_transfers=(mesh.shape["dp"], mesh.shape["fsdp"]) == (4, 8)),
        mesh=mesh,
        in_specs=placed,
        out_specs=(
            P(both, None, None),
            P(both, None),
            P(both, None, None),
            P(both, None),
            P(both, None, None),
            P(both, None, None),
            P("fsdp", None, None),
            P("fsdp", None, None),
            P("fsdp", None, None),
            P("fsdp", None, None),
            P(),
            P(),
            P(),
        ),
        check_vma=False,
    )
```

```python
from functools import partial

import jax
import jax.numpy as jnp
from jax import lax
from jax.experimental import pallas as pl
from jax.experimental.pallas import tpu as pltpu
from jax.sharding import PartitionSpec as P

D = 768
HEADS = 12
FF = 3072
SD = 128
PH = 2
NCLS = 14
BLK = 128
STEP = 10
NBLK = 439
TILE = 512
PAIRS = 3
GROUPS = 2
CHUNK = 768
LATE = 24

NORM_EPSILON = 1e-12
BETA_ONE = 0.9
BETA_TWO = 0.999
ADAM_EPSILON = 1e-08
ADAM_RATE = 0.1
MATRIX_RATE = 0.2
STAT_DECAY = 0.5
MASKED_SCORE = -1e30
HIGHEST_PRECISION = lax.Precision.HIGHEST
MIB = 1024 * 1024
F32 = jnp.float32
BF16 = jnp.bfloat16

def product(former, latter, precision=None):
    return jnp.dot(former, latter, preferred_element_type=F32, precision=precision)


def left_product(former, latter, precision=None):
    return lax.dot_general(
        former, latter, (((0,), (0,)), ((), ())), preferred_element_type=F32, precision=precision
    )


def right_product(former, latter, precision=None):
    return lax.dot_general(
        former, latter, (((1,), (1,)), ((), ())), preferred_element_type=F32, precision=precision
    )


def unpack(small_values):
    widths = (D, D, D, D, D, FF, D, D, D, SD, SD, SD, SD * NCLS, NCLS)
    pieces = []
    offset = 0
    for column_count in widths:
        pieces.append(small_values[offset : offset + column_count])
        offset += column_count
    return pieces


def each_block(first, row_count, col_count, action):
    def one_row(index, carry):
        row = pl.multiple_of(index * BLK, BLK)
        for col in range(col_count):
            action(first + index * col_count + col, row, col * BLK)
        return carry

    lax.fori_loop(0, row_count, one_row, 0)


def load_blocks(slot_ref, blocks, target, sem, first, row_count, col_count, col_start=0):
    def move(block, row, col):
        pltpu.make_async_copy(
            blocks.at[slot_ref[block]],
            target.at[pl.ds(row, BLK), pl.ds(col + col_start * BLK, BLK)],
            sem,
        ).start()

    each_block(first, row_count, col_count, move)


def wait_whole(target, sem):
    pltpu.make_async_copy(target, target, sem).wait()


def assemble_kernel(slot_ref, blocks, out, sem):
    for which in range(3):
        load_blocks(slot_ref, blocks, out, sem, 36 * which, 6, 6, 6 * which)
    wait_whole(out, sem)


def assemble(block_slot, blocks):
    return pl.pallas_call(
        assemble_kernel,
        grid_spec=pltpu.PrefetchScalarGridSpec(
            num_scalar_prefetch=1,
            grid=(1,),
            in_specs=[pl.BlockSpec(memory_space=pltpu.HBM)],
            out_specs=pl.BlockSpec(memory_space=pltpu.VMEM),
            scratch_shapes=[pltpu.SemaphoreType.DMA],
        ),
        out_shape=jax.ShapeDtypeStruct((D, 3 * D), BF16),
        compiler_params=pltpu.CompilerParams(vmem_limit_bytes=60 * MIB),
        name="assemble",
    )(block_slot, blocks)


def join_small(small_ref, query_ref, value_ref, small_out):
    small_out[...] = small_ref[...]
    for start, ref in ((0, query_ref), (D // BLK, value_ref)):
        for index in range(D // BLK):
            small_out[start + index : start + index + 1, :] = ref[:, index * BLK : (index + 1) * BLK]


PART = 256
ACROSS = PART // BLK


def feed_grads_kernel(
    code_ref,
    first_ref,
    d_down_ref,
    active_ref,
    d_up_ref,
    g_out,
    g_student,
    g_hidden,
    terms,
    first_turned,
    down_turned,
    up_stage,
    down_stage,
    up_sems,
    down_sems,
    other_sems,
):
    step = pl.program_id(0)
    last = pl.num_programs(0) - 1
    slot = step % 2
    others = ((g_out, 108, 6, 6), (g_student, 432, 6, 1), (g_hidden, 438, 1, 1))

    @pl.when(step == 0)
    def _():
        for which, (grad, first, row_count, col_count) in enumerate(others):

            def move(block, row, col, which=which, grad=grad):
                pltpu.make_async_copy(
                    grad.at[pl.ds(row, BLK), pl.ds(col, BLK)], terms.at[code_ref[block]], other_sems.at[which]
                ).start()

            each_block(first, row_count, col_count, move)
        first_turned[...] = first_ref[...].T
        down_turned[...] = d_down_ref[...].T

    @pl.when(step >= 2)
    def _():
        wait_whole(up_stage.at[slot], up_sems.at[slot])
        wait_whole(down_stage.at[slot], down_sems.at[slot])

    up_stage[slot] = product(first_turned[...], d_up_ref[...]).astype(BF16)
    down_stage[slot] = product(down_turned[...], active_ref[...]).T.astype(BF16)
    for row in range(D // BLK):
        for col in range(ACROSS):
            pltpu.make_async_copy(
                up_stage.at[slot, pl.ds(row * BLK, BLK), pl.ds(col * BLK, BLK)],
                terms.at[code_ref[144 + row * (FF // BLK) + step * ACROSS + col]],
                up_sems.at[slot],
            ).start()
            pltpu.make_async_copy(
                down_stage.at[slot, pl.ds(col * BLK, BLK), pl.ds(row * BLK, BLK)],
                terms.at[code_ref[288 + (step * ACROSS + col) * (D // BLK) + row]],
                down_sems.at[slot],
            ).start()

    @pl.when(step == last)
    def _():
        for place in range(2):
            wait_whole(up_stage.at[place], up_sems.at[place])
            wait_whole(down_stage.at[place], down_sems.at[place])
        for which, (grad, *_) in enumerate(others):
            wait_whole(grad, other_sems.at[which])


def feed_grads(code, first, d_down, active, d_up, others, slot_count):
    tokens = first.shape[0]

    def whole(shape):
        return pl.BlockSpec(shape, lambda step, *_: (0, 0), pipeline_mode=pl.Buffered(1))

    part = pl.BlockSpec((tokens, PART), lambda step, *_: (0, step))
    return pl.pallas_call(
        feed_grads_kernel,
        grid_spec=pltpu.PrefetchScalarGridSpec(
            num_scalar_prefetch=1,
            grid=(FF // PART,),
            in_specs=[whole(first.shape), whole(d_down.shape), part, part]
            + [whole(other.shape) for other in others],
            out_specs=pl.BlockSpec(memory_space=pltpu.HBM),
            scratch_shapes=[
                pltpu.VMEM((D, tokens), BF16),
                pltpu.VMEM((D, tokens), BF16),
                pltpu.VMEM((2, D, PART), BF16),
                pltpu.VMEM((2, PART, D), BF16),
                pltpu.SemaphoreType.DMA((2,)),
                pltpu.SemaphoreType.DMA((2,)),
                pltpu.SemaphoreType.DMA((3,)),
            ],
        ),
        out_shape=jax.ShapeDtypeStruct((slot_count, BLK, BLK), BF16),
        compiler_params=pltpu.CompilerParams(vmem_limit_bytes=60 * MIB),
        cost_estimate=pl.CostEstimate(
            flops=4 * tokens * D * FF, bytes_accessed=50 * MIB, transcendentals=0
        ),
        name="feed_grads",
    )(code, first, d_down, active, d_up, *others)


def input_weights_kernel(
    code_ref, x_ref, d_ref, small_ref, query_ref, value_ref, _, terms, small_out, turned, stage, sems
):
    step = pl.program_id(0)
    slot = step % 2

    @pl.when(step == 0)
    def _():
        join_small(small_ref, query_ref, value_ref, small_out)
        turned[...] = x_ref[...].T

    @pl.when(step >= 2)
    def _():
        wait_whole(stage.at[slot], sems.at[slot])

    stage[slot] = product(turned[...], d_ref[...]).astype(BF16)
    steps = D // PART
    first = (step // steps) * 36 + step % steps * ACROSS
    for row in range(D // BLK):
        for col in range(ACROSS):
            pltpu.make_async_copy(
                stage.at[slot, pl.ds(row * BLK, BLK), pl.ds(col * BLK, BLK)],
                terms.at[code_ref[first + row * (D // BLK) + col]],
                sems.at[slot],
            ).start()

    @pl.when(step == pl.num_programs(0) - 1)
    def _():
        for place in range(2):
            wait_whole(stage.at[place], sems.at[place])


def input_weights(code, x, d_qkv, small, g_query, g_value, terms):
    tokens = x.shape[0]

    def whole(shape):
        return pl.BlockSpec(shape, lambda step, *_: (0, 0), pipeline_mode=pl.Buffered(1))

    hbm = pl.BlockSpec(memory_space=pltpu.HBM)
    return pl.pallas_call(
        input_weights_kernel,
        grid_spec=pltpu.PrefetchScalarGridSpec(
            num_scalar_prefetch=1,
            grid=(3 * D // PART,),
            in_specs=[
                whole(x.shape),
                pl.BlockSpec((tokens, PART), lambda step, *_: (0, step)),
                whole(small.shape),
                whole(g_query.shape),
                whole(g_value.shape),
                hbm,
            ],
            out_specs=[hbm, pl.BlockSpec(small.shape, lambda step, *_: (0, 0))],
            scratch_shapes=[
                pltpu.VMEM((D, tokens), BF16),
                pltpu.VMEM((2, D, PART), BF16),
                pltpu.SemaphoreType.DMA((2,)),
            ],
        ),
        out_shape=[
            jax.ShapeDtypeStruct(terms.shape, BF16),
            jax.ShapeDtypeStruct(small.shape, F32),
        ],
        input_output_aliases={6: 0},
        compiler_params=pltpu.CompilerParams(vmem_limit_bytes=60 * MIB),
        cost_estimate=pl.CostEstimate(
            flops=6 * tokens * D * D, bytes_accessed=16 * MIB, transcendentals=0
        ),
        name="input_weights",
    )(code, x, d_qkv, small, g_query, g_value, terms)


def half_masks():
    lane = lax.broadcasted_iota(jnp.int32, (1, BLK), 1)
    low = (lane < BLK // 2).astype(BF16)
    return low, (1.0 - low.astype(F32)).astype(BF16)


def stack_heads(values, low, high):
    return jnp.concatenate([values * low, values * high], axis=0)


def pick_heads(values):
    rows = values.shape[0] // 2
    lane = lax.broadcasted_iota(jnp.int32, (rows, BLK), 1)
    return jnp.where(lane < BLK // 2, values[:rows], values[rows:])


def pipelined(count, before, middle, after):
    started = before(0)
    done = None
    for index in range(count):
        current = started
        if index + 1 < count:
            started = before(index + 1)
        if done is not None:
            after(index - 1, done)
        done = middle(index, current)
    after(count - 1, done)


def softmax(scores, length):
    visible = lax.broadcasted_iota(jnp.int32, scores.shape, 1) < length
    scores = jnp.where(visible, scores, MASKED_SCORE)
    powers = jnp.exp(scores - jnp.max(scores, axis=-1, keepdims=True))
    total = jnp.sum(powers, axis=-1, keepdims=True)
    return (powers * (1.0 / total)).astype(BF16)


def attention_kernel(
    len_short,
    len_long,
    x_short_ref,
    x_long_ref,
    params,
    w_ref,
    x_ref,
    q_ref,
    k_ref,
    v_ref,
    context_ref,
    short_ref,
    long_ref,
    bias,
    *,
    short_tiles,
):
    tile = pl.program_id(0)
    group = pl.program_id(1)
    low, high = half_masks()
    width = short_ref.shape[-1]
    per_tile = TILE // width

    wide = PAIRS * BLK
    start = pl.multiple_of(group * wide, wide)

    @pl.when((tile == 0) & (group == 0))
    def _():
        for which in range(2):
            for place in range(D // BLK):
                row = which * (D // BLK) + place
                bias[which : which + 1, place * BLK : (place + 1) * BLK] = params[row : row + 1, :]

    @pl.when((tile < short_tiles) & (group == 0))
    def _():
        x_ref[...] = x_short_ref[...]

    @pl.when((tile >= short_tiles) & (group == 0))
    def _():
        x_ref[...] = x_long_ref[...]

    rows_in = x_ref[...]
    queries = product(rows_in, w_ref[:, pl.ds(start, wide)]) + bias[0:1, pl.ds(start, wide)]
    q_ref[...] = (queries * 0.125).astype(BF16)
    k_ref[...] = product(rows_in, w_ref[:, pl.ds(D + start, wide)]).astype(BF16)
    values = product(rows_in, w_ref[:, pl.ds(2 * D + start, wide)]) + bias[1:2, pl.ds(start, wide)]
    v_ref[...] = values.astype(BF16)

    def attend(units, kept_ref):
        def scores(index):
            rows, keys, cols, _, _ = units[index]
            return right_product(stack_heads(q_ref[rows, cols], low, high), k_ref[keys, cols])

        def weigh(index, values):
            _, _, _, length, place = units[index]
            probs = softmax(values, length)
            kept_ref[place] = probs
            return probs

        def mix(index, probs):
            rows, keys, cols, _, _ = units[index]
            context_ref[rows, cols] = pick_heads(product(probs, v_ref[keys, cols])).astype(BF16)

        pipelined(len(units), scores, weigh, mix)

    @pl.when(tile < short_tiles)
    def _():
        units = []
        for seq in range(per_tile):
            rows = slice(seq * width, (seq + 1) * width)
            length = len_short[tile * per_tile + seq]
            for pair in range(PAIRS):
                cols = slice(pair * BLK, (pair + 1) * BLK)
                units.append((rows, rows, cols, length, (0, pair, seq)))
        attend(units, short_ref)

    @pl.when(tile >= short_tiles)
    def _():
        length = len_long[tile - short_tiles]
        half = TILE // 2
        units = []
        for pair in range(PAIRS):
            cols = slice(pair * BLK, (pair + 1) * BLK)
            for part in range(2):
                rows = slice(part * half, (part + 1) * half)
                units.append((rows, slice(0, TILE), cols, length, (0, pair, part)))
        attend(units, long_ref)


def run_events(step, events):
    for index, actions in enumerate(events):

        @pl.when(step == index)
        def _(actions=actions):
            for action in actions:
                action()


def probs_shapes(short_tiles, long_tiles, width):
    per_tile = TILE // width
    return (
        (short_tiles, 2 * PAIRS, per_tile, 2 * width, width),
        (long_tiles, 2 * PAIRS, 2, TILE, TILE),
    )


def short_index(tile, short_tiles):
    return jnp.minimum(tile, short_tiles - 1)


def long_index(tile, short_tiles):
    return jnp.maximum(tile - short_tiles, 0)


def probs_maps(short_tiles):
    def short_map(tile, group):
        last = jnp.minimum(tile // short_tiles, 1)
        return (short_index(tile, short_tiles), group + last * (GROUPS - 1 - group), 0, 0, 0)

    def long_map(tile, group):
        begun = jnp.minimum(tile // short_tiles, 1)
        return (long_index(tile, short_tiles), begun * group, 0, 0, 0)

    return short_map, long_map


def attention(len_short, len_long, x_short, x_long, params, w_qkv, short_tiles, width):
    tiles = (x_short.shape[0] + x_long.shape[0]) // TILE
    wide = PAIRS * BLK
    short_shape, long_shape = probs_shapes(short_tiles, tiles - short_tiles, width)
    short_map, long_map = probs_maps(short_tiles)
    flops = 4 * D * TILE * TILE * tiles + 6 * D * D * TILE * tiles
    rows = pl.BlockSpec((TILE, wide), lambda tile, group: (tile, group))
    scalars = pl.BlockSpec(memory_space=pltpu.SMEM)

    def whole(shape):
        return pl.BlockSpec(shape, lambda tile, group: (0,) * len(shape), pipeline_mode=pl.Buffered(1))

    in_specs = [
        scalars,
        scalars,
        pl.BlockSpec((TILE, D), lambda tile, group: (short_index(tile, short_tiles), 0)),
        pl.BlockSpec((TILE, D), lambda tile, group: (long_index(tile, short_tiles), 0)),
        whole(params.shape),
        whole((D, 3 * D)),
    ]
    out_specs = [
        pl.BlockSpec((TILE, D), lambda tile, group: (tile, 0)),
        rows,
        rows,
        rows,
        rows,
        pl.BlockSpec((1, PAIRS) + short_shape[2:], short_map),
        pl.BlockSpec((1, PAIRS) + long_shape[2:], long_map),
    ]
    out_shape = [jax.ShapeDtypeStruct((tiles * TILE, D), BF16)] * 5 + [
        jax.ShapeDtypeStruct(short_shape, BF16),
        jax.ShapeDtypeStruct(long_shape, BF16),
    ]
    arguments = [len_short, len_long, x_short, x_long, params, w_qkv]
    return pl.pallas_call(
        partial(attention_kernel, short_tiles=short_tiles),
        grid=(tiles, GROUPS),
        in_specs=in_specs,
        out_specs=out_specs,
        out_shape=out_shape,
        scratch_shapes=[pltpu.VMEM((8, D), F32)],
        compiler_params=pltpu.CompilerParams(vmem_limit_bytes=60 * MIB),
        cost_estimate=pl.CostEstimate(
            flops=flops, bytes_accessed=35 * MIB, transcendentals=HEADS * TILE * TILE * tiles // 2
        ),
        name="attention",
    )(*arguments)


def attention_back_kernel(*refs, short_tiles, transfers):
    q_ref, k_ref, v_ref, short_ref, long_ref, dc_ref = refs[:6]
    refs = refs[6:]
    if transfers:
        terms_ref, refs = refs[0], refs[1:]
    out_ref, bq_ref, bv_ref = refs[:3]
    tile = pl.program_id(0)
    group = pl.program_id(1)
    low, high = half_masks()
    width = short_ref.shape[-1]
    per_tile = TILE // width
    if transfers:
        reduce = Reduce(terms_ref, 0, refs[3], refs[4:])
        run_events(tile * GROUPS + group, reduce.events())

    wide = PAIRS * BLK
    start = pl.multiple_of(group * wide, wide)

    def columns(which, cols):
        return pl.ds(pl.multiple_of(which * D + start + cols.start, BLK), BLK)

    def go_back(units, kept_ref, parts):
        sums = {}

        def spread_in(index):
            rows, keys, cols, _ = units[index]
            return right_product(stack_heads(dc_ref[rows, cols], low, high), v_ref[keys, cols])

        def differ(index, d_probs):
            wide = kept_ref[units[index][3]].astype(F32)
            weighted = wide * d_probs
            return (weighted - wide * jnp.sum(weighted, axis=-1, keepdims=True)).astype(BF16)

        def gather_up(index, d_scores):
            rows, keys, cols, place = units[index]
            d_queries = pick_heads(product(d_scores, k_ref[keys, cols])) * 0.125
            out_ref[rows, columns(0, cols)] = d_queries.astype(BF16)
            d_keys = left_product(d_scores, stack_heads(q_ref[rows, cols], low, high))
            d_values = left_product(kept_ref[place], stack_heads(dc_ref[rows, cols], low, high))
            if index % parts:
                d_keys += sums["keys"]
                d_values += sums["values"]
            if index % parts == parts - 1:
                out_ref[keys, columns(1, cols)] = d_keys.astype(BF16)
                out_ref[keys, columns(2, cols)] = d_values.astype(BF16)
            else:
                sums.update(keys=d_keys, values=d_values)

        pipelined(len(units), spread_in, differ, gather_up)

    @pl.when(tile < short_tiles)
    def _():
        units = []
        for seq in range(per_tile):
            rows = slice(seq * width, (seq + 1) * width)
            for pair in range(PAIRS):
                cols = slice(pair * BLK, (pair + 1) * BLK)
                units.append((rows, rows, cols, (0, pair, seq)))
        go_back(units, short_ref, 1)

    @pl.when(tile >= short_tiles)
    def _():
        half = TILE // 2
        units = []
        for pair in range(PAIRS):
            cols = slice(pair * BLK, (pair + 1) * BLK)
            for part in range(2):
                rows = slice(part * half, (part + 1) * half)
                units.append((rows, slice(0, TILE), cols, (0, pair, part)))
        go_back(units, long_ref, 2)

    @pl.when((tile == 0) & (group == 0))
    def _():
        bq_ref[...] = jnp.zeros_like(bq_ref)
        bv_ref[...] = jnp.zeros_like(bv_ref)

    bq_ref[:, pl.ds(start, wide)] += column_sum(out_ref[:, pl.ds(start, wide)])
    bv_ref[:, pl.ds(start, wide)] += column_sum(out_ref[:, pl.ds(2 * D + start, wide)])

    if transfers:

        @pl.when((tile == pl.num_programs(0) - 1) & (group == GROUPS - 1))
        def _():
            reduce.finish()


def attention_back(qkv, probs_short, probs_long, d_context, short_tiles, terms=None, count=0):
    tiles = d_context.shape[0] // TILE
    wide = PAIRS * BLK
    short_map, long_map = probs_maps(short_tiles)
    rows = pl.BlockSpec((TILE, wide), lambda tile, group: (tile, group))
    row = pl.BlockSpec((1, D), lambda tile, group: (0, 0))
    flops = 10 * D * TILE * TILE * tiles
    in_specs = [
        rows,
        rows,
        rows,
        pl.BlockSpec((1, PAIRS) + probs_short.shape[2:], short_map),
        pl.BlockSpec((1, PAIRS) + probs_long.shape[2:], long_map),
        rows,
    ]
    out_specs = [pl.BlockSpec((TILE, 3 * D), lambda tile, group: (tile, 0)), row, row]
    out_shape = [
        jax.ShapeDtypeStruct((tiles * TILE, 3 * D), BF16),
        jax.ShapeDtypeStruct((1, D), F32),
        jax.ShapeDtypeStruct((1, D), F32),
    ]
    arguments = [*qkv, probs_short, probs_long, d_context]
    scratch = []
    params = dict(vmem_limit_bytes=60 * MIB)
    if terms is not None:
        arguments.append(terms)
        in_specs.append(pl.BlockSpec(memory_space=pltpu.HBM))
        out_specs.append(pl.BlockSpec((count, BLK), lambda tile, group: (0, 0)))
        out_shape.append(jax.ShapeDtypeStruct((count, BLK), BF16))
        scratch = reduce_scratch(count)
        params.update(collective_id=2, has_side_effects=True)
    return pl.pallas_call(
        partial(attention_back_kernel, short_tiles=short_tiles, transfers=terms is not None),
        grid=(tiles, GROUPS),
        in_specs=in_specs,
        out_specs=out_specs,
        out_shape=out_shape,
        scratch_shapes=scratch,
        compiler_params=pltpu.CompilerParams(**params),
        cost_estimate=pl.CostEstimate(flops=flops, bytes_accessed=50 * MIB, transcendentals=0),
        name="attention_back",
    )(*arguments)


INPUT_ROWS = 256


def input_product(d_ref, resid_ref, w_ref, short_ref, long_ref, short_steps):
    step = pl.program_id(0)
    total = resid_ref[...] + right_product(d_ref[...], w_ref[...])

    @pl.when(step < short_steps)
    def _():
        short_ref[...] = total

    @pl.when(step >= short_steps)
    def _():
        long_ref[...] = total


def input_specs(short_steps):
    rows = [pl.BlockSpec((INPUT_ROWS, width), lambda step: (step, 0)) for width in (3 * D, D)]
    whole = pl.BlockSpec((D, 3 * D), lambda step: (0, 0), pipeline_mode=pl.Buffered(1))
    outs = [
        pl.BlockSpec((INPUT_ROWS, D), lambda step: (short_index(step, short_steps), 0)),
        pl.BlockSpec((INPUT_ROWS, D), lambda step: (long_index(step, short_steps), 0)),
    ]
    return rows + [whole], outs


def input_grads(d_qkv, resid, w_qkv, short_tiles):
    steps = resid.shape[0] // INPUT_ROWS
    short_steps = short_tiles * TILE // INPUT_ROWS
    in_specs, out_specs = input_specs(short_steps)
    return pl.pallas_call(
        partial(input_product, short_steps=short_steps),
        grid=(steps,),
        in_specs=in_specs,
        out_specs=out_specs,
        out_shape=[
            jax.ShapeDtypeStruct((short_steps * INPUT_ROWS, D), F32),
            jax.ShapeDtypeStruct(((steps - short_steps) * INPUT_ROWS, D), F32),
        ],
        compiler_params=pltpu.CompilerParams(vmem_limit_bytes=60 * MIB),
        name="input_grads",
    )(d_qkv, resid, w_qkv)


def normal_parts(values):
    below = 0.5 * lax.erf(values * 0.7071067811865476) + 0.5
    return below, jnp.exp(-0.5 * values * values) * 0.3989422804014327


B_OUT, GAIN_ONE, SHIFT_ONE, B_UP, B_DOWN, GAIN_TWO, SHIFT_TWO, B_STUDENT, POOL_QUERY, B_HIDDEN = range(10)
VECTORS = (
    (12, 6),
    (18, 6),
    (24, 6),
    (30, 24),
    (54, 6),
    (60, 6),
    (66, 6),
    (72, 1),
    (73, 1),
    (74, 1),
)
CLASS_ROW = 75
LAST_ROW = 91
SMALL_ROWS = 96


def norm_parts(values):
    center = values - jnp.mean(values, axis=-1, keepdims=True)
    spread = jnp.mean(center * center, axis=-1, keepdims=True)
    inverse = lax.rsqrt(spread + NORM_EPSILON)
    return center * inverse, inverse


def norm_back(d_values, gain, unit, inverse):
    d_unit = d_values * gain
    return inverse * (
        d_unit
        - jnp.mean(d_unit, axis=-1, keepdims=True)
        - unit * jnp.mean(d_unit * unit, axis=-1, keepdims=True)
    )


def column_sum(values):
    return jnp.sum(values.astype(F32), axis=0, keepdims=True)


def pool_weights(student, query, length):
    scaled = student * query
    lane = lax.broadcasted_iota(jnp.int32, scaled.shape, 1)
    place = lax.broadcasted_iota(jnp.int32, (scaled.shape[0], 1), 0)
    weights = []
    for side in (lane < SD // PH, lane >= SD // PH):
        scores = jnp.sum(jnp.where(side, scaled, 0.0), axis=-1, keepdims=True)
        scores = jnp.where(place < length, scores, MASKED_SCORE)
        powers = jnp.exp(scores - jnp.max(scores, axis=0, keepdims=True))
        weights.append(powers / jnp.sum(powers, axis=0, keepdims=True))
    return jnp.where(lane < SD // PH, weights[0], weights[1]), weights


def student_back(student, query, weights, both, d_pooled):
    lane = lax.broadcasted_iota(jnp.int32, student.shape, 1)
    moved = student * d_pooled
    d_scores = []
    for side, weight in zip((lane < SD // PH, lane >= SD // PH), weights):
        d_weight = jnp.sum(jnp.where(side, moved, 0.0), axis=-1, keepdims=True)
        d_scores.append(weight * (d_weight - jnp.sum(weight * d_weight, axis=0, keepdims=True)))
    d_score = jnp.where(lane < SD // PH, d_scores[0], d_scores[1])
    d_query = jnp.sum(d_score * student, axis=0, keepdims=True) * 0.125
    return both * d_pooled + d_score * query, d_query


def feed_kernel(
    len_short,
    len_long,
    slot_ref,
    x_ref,
    context_ref,
    cot_short_ref,
    cot_long_ref,
    logit_cot_short,
    logit_cot_long,
    params,
    w_class_ref,
    b_class_ref,
    blocks,
    enc_short_ref,
    enc_long_ref,
    logits_short,
    logits_long,
    first_ref,
    active_ref,
    d_up_ref,
    d_down_ref,
    d_branch_ref,
    d_context_ref,
    d_resid_ref,
    g_student,
    g_hidden,
    g_small,
    slope,
    pooled_ref,
    d_student_ref,
    w_out,
    w_up,
    w_down,
    w_student,
    w_hidden,
    vectors,
    totals,
    g_class,
    g_last,
    w_class,
    b_class,
    logit_cot,
    sems,
    *,
    short_tiles,
    width,
):
    tile = pl.program_id(0)
    per_tile = TILE // width
    loads = ((w_out, 108, 6, 6), (w_up, 144, 6, 24), (w_down, 288, 24, 6), (w_student, 432, 6, 1), (w_hidden, 438, 1, 1))

    def arrive(*indices):
        @pl.when(tile == 0)
        def _():
            for index in indices:
                wait_whole(loads[index][0], sems.at[index])

    @pl.when(tile == 0)
    def _():
        for index, (target, block, row_count, col_count) in enumerate(loads):
            load_blocks(slot_ref, blocks, target, sems.at[index], block, row_count, col_count)
        for index, (start, count) in enumerate(VECTORS):
            for place in range(count):
                vectors[index : index + 1, place * BLK : (place + 1) * BLK] = params[
                    start + place : start + place + 1, :
                ]
        for ref in (totals, g_class, g_last, g_student, g_hidden, w_class, b_class):
            ref[...] = jnp.zeros_like(ref)
        w_class[:, :NCLS] = w_class_ref[...]
        b_class[:, :NCLS] = b_class_ref[...]

    def vector(index):
        return vectors[index : index + 1, : VECTORS[index][1] * BLK]

    def add_total(index, values):
        totals[index : index + 1, : VECTORS[index][1] * BLK] += column_sum(values)

    arrive(0)
    branch = product(context_ref[...], w_out[...]) + vector(B_OUT)
    unit_one, inverse_one = norm_parts(x_ref[...].astype(F32) + branch)
    first = (unit_one * vector(GAIN_ONE) + vector(SHIFT_ONE)).astype(BF16)
    first_ref[...] = first
    arrive(1)
    chunks = [slice(start, start + CHUNK) for start in range(0, FF, CHUNK)]

    def rise(index):
        return product(first, w_up[:, chunks[index]])

    def bend(index, upward):
        upward = upward + vectors[B_UP : B_UP + 1, chunks[index]]
        below, density = normal_parts(upward)
        active_ref[:, chunks[index]] = (upward * below).astype(BF16)
        slope[:, chunks[index]] = (below + upward * density).astype(BF16)

    pipelined(len(chunks), rise, bend, lambda *_: None)
    arrive(2, 3, 4)
    downward = product(active_ref[...], w_down[...]) + vector(B_DOWN)
    unit_two, inverse_two = norm_parts(first.astype(F32) + downward)
    encoded = (unit_two * vector(GAIN_TWO) + vector(SHIFT_TWO)).astype(BF16)

    @pl.when(tile < short_tiles)
    def _():
        enc_short_ref[...] = encoded

    @pl.when(tile >= short_tiles)
    def _():
        enc_long_ref[...] = encoded

    student = product(encoded, w_student[...]) + vector(B_STUDENT)
    query = vector(POOL_QUERY) * 0.125
    pooled_ref[...] = jnp.zeros_like(pooled_ref)

    def head():
        pooled = pooled_ref[...]
        wide_hidden = w_hidden[...].astype(F32)
        hidden = jnp.tanh(product(pooled, wide_hidden, HIGHEST_PRECISION) + vector(B_HIDDEN))
        logits = product(hidden, w_class[...], HIGHEST_PRECISION) + b_class[...]
        d_logits = logit_cot[...]
        g_last[...] += column_sum(d_logits)
        g_class[...] += left_product(d_logits, hidden, HIGHEST_PRECISION)
        d_hidden = right_product(d_logits, w_class[...], HIGHEST_PRECISION)
        d_hidden = d_hidden * (1.0 - hidden * hidden)
        add_total(B_HIDDEN, d_hidden)
        g_hidden[...] += left_product(pooled, d_hidden, HIGHEST_PRECISION)
        return logits, right_product(d_hidden, wide_hidden, HIGHEST_PRECISION)

    def pool(starts, size, lengths, cot_ref, logits_ref, first):
        count = len(starts)
        logit_cot[...] = jnp.zeros_like(logit_cot)
        for index in range(count):
            logit_cot[index : index + 1, :NCLS] = cot_ref[pl.ds(first + index, 1), :]
        kept = []
        for index, (start, length) in enumerate(zip(starts, lengths)):
            rows = student[start : start + size]
            both, weights = pool_weights(rows, query, length)
            pooled_ref[index : index + 1, :] = column_sum(both * rows)
            kept.append((start, rows, both, weights))
        logits, d_pooled = head()
        for index in range(count):
            logits_ref[pl.ds(first + index, 1), :] = logits[index : index + 1, :NCLS]
        for index, (start, rows, both, weights) in enumerate(kept):
            d_rows, d_query = student_back(rows, query, weights, both, d_pooled[index : index + 1])
            d_student_ref[start : start + size, :] = d_rows.astype(BF16)
            add_total(POOL_QUERY, d_query)

    @pl.when(tile < short_tiles)
    def _():
        pool(
            [seq * width for seq in range(per_tile)],
            width,
            [len_short[tile * per_tile + seq] for seq in range(per_tile)],
            logit_cot_short,
            logits_short,
            tile * per_tile,
        )

    @pl.when(tile >= short_tiles)
    def _():
        long = tile - short_tiles
        pool([0], TILE, [len_long[long]], logit_cot_long, logits_long, long)

    d_student = d_student_ref[...]
    add_total(B_STUDENT, d_student)
    g_student[...] += left_product(encoded, d_student)
    cotangent = jnp.where(tile < short_tiles, cot_short_ref[...], cot_long_ref[...])
    d_second = cotangent.astype(F32) + right_product(d_student, w_student[...])
    add_total(GAIN_TWO, d_second * unit_two)
    add_total(SHIFT_TWO, d_second)
    d_resid_two = norm_back(d_second, vector(GAIN_TWO), unit_two, inverse_two)
    d_down = d_resid_two.astype(BF16)
    d_down_ref[...] = d_down
    add_total(B_DOWN, d_down)

    def fall(index):
        return right_product(d_down, w_down[chunks[index], :])

    def bend_back(index, d_active):
        d_up = (d_active * slope[:, chunks[index]].astype(F32)).astype(BF16)
        d_up_ref[:, chunks[index]] = d_up
        totals[B_UP : B_UP + 1, chunks[index]] += column_sum(d_up)

    pipelined(len(chunks), fall, bend_back, lambda *_: None)
    d_first = d_resid_two + right_product(d_up_ref[...], w_up[...])
    add_total(GAIN_ONE, d_first * unit_one)
    add_total(SHIFT_ONE, d_first)
    d_resid_one = norm_back(d_first, vector(GAIN_ONE), unit_one, inverse_one)
    d_resid_ref[...] = d_resid_one
    d_branch = d_resid_one.astype(BF16)
    d_branch_ref[...] = d_branch
    add_total(B_OUT, d_branch)
    d_context_ref[...] = right_product(d_branch, w_out[...]).astype(BF16)

    @pl.when(tile == pl.num_programs(0) - 1)
    def _():
        g_small[...] = jnp.zeros_like(g_small)
        for index, (start, count) in enumerate(VECTORS):
            for place in range(count):
                g_small[start + place : start + place + 1, :] = totals[
                    index : index + 1, place * BLK : (place + 1) * BLK
                ]
        g_small[CLASS_ROW : CLASS_ROW + NCLS, :] = g_class[:NCLS, :]
        g_small[LAST_ROW : LAST_ROW + 1, :] = g_last[...]


def feed(
    len_short, len_long, block_slot, x, context, cot_short, cot_long, logit_cots, small, blocks, short_tiles, width
):
    tiles = x.shape[0] // TILE
    long_tiles = tiles - short_tiles

    def whole(shape):
        return pl.BlockSpec(shape, lambda tile, *_: (0,) * len(shape), pipeline_mode=pl.Buffered(1))

    def kept(shape):
        return pl.BlockSpec(shape, lambda tile, *_: (0,) * len(shape))

    def rows(columns):
        return pl.BlockSpec((TILE, columns), lambda tile, *_: (tile, 0))

    short_rows = pl.BlockSpec((TILE, D), lambda tile, *_: (short_index(tile, short_tiles), 0))
    long_rows = pl.BlockSpec((TILE, D), lambda tile, *_: (long_index(tile, short_tiles), 0))
    grad_shapes = ((D, SD), (SD, SD), (SMALL_ROWS, BLK))
    total = tiles * TILE
    return pl.pallas_call(
        partial(feed_kernel, short_tiles=short_tiles, width=width),
        grid_spec=pltpu.PrefetchScalarGridSpec(
            num_scalar_prefetch=3,
            grid=(tiles,),
            in_specs=[rows(D), rows(D), short_rows, long_rows]
            + [whole(array.shape) for array in (*logit_cots, *small)]
            + [pl.BlockSpec(memory_space=pltpu.HBM)],
            out_specs=[
                short_rows,
                long_rows,
                kept(logit_cots[0].shape),
                kept(logit_cots[1].shape),
                rows(D),
                rows(FF),
                rows(FF),
                rows(D),
                rows(D),
                rows(D),
                rows(D),
            ]
            + [kept(shape) for shape in grad_shapes],
            scratch_shapes=[
                pltpu.VMEM((TILE, FF), BF16),
                pltpu.VMEM((8, SD), F32),
                pltpu.VMEM((TILE, SD), BF16),
                pltpu.VMEM((D, D), BF16),
                pltpu.VMEM((D, FF), BF16),
                pltpu.VMEM((FF, D), BF16),
                pltpu.VMEM((D, SD), BF16),
                pltpu.VMEM((SD, SD), BF16),
                pltpu.VMEM((16, FF), F32),
                pltpu.VMEM((16, FF), F32),
                pltpu.VMEM((SD, SD), F32),
                pltpu.VMEM((1, SD), F32),
                pltpu.VMEM((SD, SD), F32),
                pltpu.VMEM((1, SD), F32),
                pltpu.VMEM((8, SD), F32),
                pltpu.SemaphoreType.DMA((5,)),
            ],
        ),
        out_shape=[
            jax.ShapeDtypeStruct((short_tiles * TILE, D), BF16),
            jax.ShapeDtypeStruct((long_tiles * TILE, D), BF16),
            jax.ShapeDtypeStruct(logit_cots[0].shape, F32),
            jax.ShapeDtypeStruct(logit_cots[1].shape, F32),
            jax.ShapeDtypeStruct((total, D), BF16),
            jax.ShapeDtypeStruct((total, FF), BF16),
            jax.ShapeDtypeStruct((total, FF), BF16),
            jax.ShapeDtypeStruct((total, D), BF16),
            jax.ShapeDtypeStruct((total, D), BF16),
            jax.ShapeDtypeStruct((total, D), BF16),
            jax.ShapeDtypeStruct((total, D), F32),
        ]
        + [jax.ShapeDtypeStruct(shape, F32) for shape in grad_shapes],
        compiler_params=pltpu.CompilerParams(vmem_limit_bytes=62 * MIB),
        cost_estimate=pl.CostEstimate(
            flops=total * (8 * D * FF + 4 * D * D), bytes_accessed=70 * MIB, transcendentals=total * FF
        ),
        name="feed",
    )(len_short, len_long, block_slot, x, context, cot_short, cot_long, *logit_cots, *small, blocks)


class Place:
    def __init__(self):
        self.quarter = lax.axis_index("dp")
        self.shard = lax.axis_index("fsdp")
        x = self.quarter % 2
        y = self.quarter // 2
        self.core = self.shard % 2
        self.z = self.shard // 2
        self.high = self.z // 2
        self.by_x = 2 * y + 1 - x
        self.by_y = 2 * (1 - y) + x
        self.across = 2 * (1 - y) + 1 - x
        self.sibling = (self.quarter, 2 * self.z + 1 - self.core)
        self.next_x = (self.by_x, self.shard)
        self.next_y = (self.by_y, self.shard)
        self.inner = (self.z > 0) & (self.z < 3)

    def at_z(self, z):
        return (self.quarter, 2 * z + self.core)


def transfer(source, target, send_sem, recv_sem, device):
    return pltpu.make_async_remote_copy(
        src_ref=source,
        dst_ref=target,
        send_sem=send_sem,
        recv_sem=recv_sem,
        device_id=device,
        device_id_type=pl.DeviceIdType.MESH,
    )


def greet(place, extra=()):
    barrier = pltpu.get_barrier_semaphore()

    def signal(device):
        pl.semaphore_signal(barrier, inc=1, device_id=device, device_id_type=pl.DeviceIdType.MESH)

    near = (place.sibling, place.next_x, place.next_y) + tuple(extra)
    for device in near:
        signal(device)

    @pl.when(place.z > 0)
    def _():
        signal(place.at_z(place.z - 1))

    @pl.when(place.z < 3)
    def _():
        signal(place.at_z(place.z + 1))

    pl.semaphore_wait(barrier, len(near) + 1 + (place.z + 1) // 2 % 2)


CUTS = 2
GATHER_SEMAPHORES = [
    pltpu.SemaphoreType.DMA((2 * CUTS,)),
    pltpu.SemaphoreType.DMA((3 * CUTS,)),
    pltpu.SemaphoreType.DMA((4 * CUTS,)),
    pltpu.SemaphoreType.DMA((12 * CUTS,)),
    pltpu.SemaphoreType.DMA((12 * CUTS,)),
    pltpu.SemaphoreType.DMA((1 + 15 * CUTS,)),
    pltpu.SemaphoreType.DMA((1 + 15 * CUTS,)),
    pltpu.SemaphoreType.DMA((8,)),
]


class Gather:
    def __init__(self, full, out, sems):
        self.place = place = Place()
        self.full, self.out = full, out
        (
            self.own_send,
            self.relay_send,
            self.z_recv,
            self.xy_send,
            self.xy_recv,
            self.core_send,
            self.core_recv,
            self.out_sems,
        ) = sems
        self.quarter = full.shape[1] // 4
        self.cut = self.quarter // CUTS
        self.first_part = (self.cut // 16 + 1) // 2 * 16
        z = place.z
        self.origins = (z + 1 - 2 * (z % 2), 2 - place.high, 3 * (1 - place.high))
        self.relays = (3 - z, 3 * (z - 1), 3 * (z - 1))

    def region(self, which, start, size):
        return self.full.at[which, pl.ds(pl.multiple_of(start, 16), size)]

    def pieces(self, which, turn):
        place, quarter, cut, part = self.place, self.quarter, self.cut, self.first_part
        skip = turn % CUTS * cut
        return (
            self.region(which, place.quarter * quarter + skip, cut),
            self.region(which, place.by_x * quarter + skip, cut),
            self.region(which, place.by_y * quarter + skip, cut),
            self.region(which, place.across * quarter + skip, part),
            self.region(which, place.across * quarter + skip + part, cut - part),
        )

    def own_copy(self, side, cut):
        place = self.place
        mine = self.pieces(place.shard, cut)[0]
        device = place.at_z(place.z - 1 + 2 * side)
        return transfer(
            mine,
            mine,
            self.own_send.at[side * CUTS + cut],
            self.z_recv.at[place.z * CUTS + cut],
            device,
        )

    def core_copy(self, index, ref):
        return transfer(ref, ref, self.core_send.at[index], self.core_recv.at[index], self.place.sibling)

    def xy_copy(self, index, ref, device):
        return transfer(ref, ref, self.xy_send.at[index], self.xy_recv.at[index], device)

    def store(self, index, which):
        return pltpu.make_async_copy(self.full.at[which], self.out.at[which], self.out_sems.at[index])

    def mirrored(self, step):
        return 2 * self.origins[step] + 1 - self.place.core

    def held(self, step):
        return 2 * self.origins[step] + self.place.core

    def start(self):
        place = self.place
        greet(place)
        for cut in range(CUTS):

            @pl.when(place.z > 0)
            def _():
                self.own_copy(0, cut).start()

            @pl.when(place.z < 3)
            def _():
                self.own_copy(1, cut).start()

        self.core_copy(0, self.full.at[place.shard]).start()
        self.store(0, place.shard).start()

    def relay(self, turn):
        step = turn // CUTS
        piece = self.pieces(self.held(step), turn)[0]
        device = self.place.at_z(self.relays[step])
        sem = self.z_recv.at[self.origins[step] * CUTS + turn % CUTS]
        return transfer(piece, piece, self.relay_send.at[turn], sem, device)

    def along_z(self, turn):
        place = self.place
        self.relay(turn).wait_recv()

        @pl.when(place.inner)
        def _():
            self.relay(turn).start()

        piece = self.pieces(self.held(turn // CUTS), turn)[0]
        self.xy_copy(4 * turn, piece, place.next_x).start()
        self.xy_copy(4 * turn + 1, piece, place.next_y).start()
        self.core_copy(1 + 5 * turn, piece).start()

    def along_xy(self, turn):
        place, part = self.place, self.first_part
        _, by_x, by_y, _, _ = self.pieces(self.held(turn // CUTS), turn)
        self.xy_copy(4 * turn, by_x, place.next_x).wait_recv()
        self.xy_copy(4 * turn + 2, by_x.at[pl.ds(0, part)], place.next_y).start()
        self.core_copy(2 + 5 * turn, by_x).start()
        self.xy_copy(4 * turn + 1, by_y, place.next_y).wait_recv()
        self.xy_copy(4 * turn + 3, by_y.at[pl.ds(part, self.cut - part)], place.next_x).start()
        self.core_copy(3 + 5 * turn, by_y).start()

    def across(self, turn):
        place = self.place
        step = turn // CUTS
        _, _, _, first, last = self.pieces(self.held(step), turn)
        self.xy_copy(4 * turn + 2, first, place.next_y).wait_recv()
        self.core_copy(4 + 5 * turn, first).start()
        self.xy_copy(4 * turn + 3, last, place.next_x).wait_recv()
        self.core_copy(5 + 5 * turn, last).start()
        if turn % CUTS == CUTS - 1:
            self.store(2 + 2 * step, self.held(step)).start()

    def core_own(self):
        which = 2 * self.place.z + 1 - self.place.core
        self.core_copy(0, self.full.at[which]).wait_recv()
        self.store(1, which).start()

    def core(self, step):
        which = self.mirrored(step)
        for turn in range(step * CUTS, (step + 1) * CUTS):
            for index, ref in enumerate(self.pieces(which, turn)):
                self.core_copy(1 + 5 * turn + index, ref).wait_recv()
        self.store(3 + 2 * step, which).start()

    def finish(self):
        place = self.place
        for cut in range(CUTS):

            @pl.when(place.z > 0)
            def _():
                self.own_copy(0, cut).wait_send()

            @pl.when(place.z < 3)
            def _():
                self.own_copy(1, cut).wait_send()

        self.core_copy(0, self.full.at[place.shard]).wait_send()
        self.store(0, place.shard).wait()
        self.store(1, 2 * place.z + 1 - place.core).wait()
        for turn in range(3 * CUTS):

            @pl.when(place.inner)
            def _():
                self.relay(turn).wait_send()

            pieces = self.pieces(self.held(turn // CUTS), turn)
            self.xy_copy(4 * turn, pieces[0], place.next_x).wait_send()
            self.xy_copy(4 * turn + 1, pieces[0], place.next_y).wait_send()
            self.xy_copy(4 * turn + 2, pieces[3], place.next_y).wait_send()
            self.xy_copy(4 * turn + 3, pieces[4], place.next_x).wait_send()
            for index, ref in enumerate(pieces):
                self.core_copy(1 + 5 * turn + index, ref).wait_send()
        for step in range(3):
            self.store(2 + 2 * step, self.held(step)).wait()
            self.store(3 + 2 * step, self.mirrored(step)).wait()


def gather_kernel(master_ref, out_ref, full, *sems):
    gather = Gather(full, out_ref, sems)
    full[gather.place.shard] = master_ref[...].astype(BF16)
    gather.start()
    turns = 3 * CUTS
    for turn in range(turns + 2):
        if turn < turns:
            gather.along_z(turn)
        if 1 <= turn <= turns:
            gather.along_xy(turn - 1)
        if turn >= 2:
            gather.across(turn - 2)
        if turn == 2:
            gather.core_own()
        if turn >= 4 and turn % CUTS == 0:
            gather.core(turn // CUTS - 2)
    gather.core(2)
    gather.finish()


def gather_shards(master):
    rows = master.shape[0] * BLK
    shards = lax.axis_size("fsdp")
    return pl.pallas_call(
        gather_kernel,
        in_specs=[pl.BlockSpec(memory_space=pltpu.VMEM)],
        out_specs=pl.BlockSpec(memory_space=pltpu.HBM),
        out_shape=jax.ShapeDtypeStruct((shards, rows, BLK), BF16),
        scratch_shapes=[pltpu.VMEM((shards, rows, BLK), BF16)] + GATHER_SEMAPHORES,
        compiler_params=pltpu.CompilerParams(
            collective_id=0, has_side_effects=True, vmem_limit_bytes=60 * MIB
        ),
        cost_estimate=pl.CostEstimate(flops=0, bytes_accessed=200 * MIB, transcendentals=0),
        name="gather",
    )(master.reshape(rows, BLK)).reshape(-1, BLK, BLK)


def add_rows(target, former, latter, rows, step):
    @pl.loop(0, rows // step)
    def _(index):
        part = pl.ds(pl.multiple_of(index * step, 16), step)
        target[part] = (former[part].astype(F32) + latter[part].astype(F32)).astype(BF16)


def split_rows(rows):
    slots = rows // BLK
    wide = (2 * slots + 1) // 3
    return wide * BLK, (slots - wide) * BLK


def reduce_scratch(rows):
    wide, long = split_rows(rows)
    return [
        pltpu.VMEM((4, rows, BLK), BF16),
        pltpu.VMEM((4, rows, BLK), BF16),
        pltpu.VMEM((4, 6, wide // 8, BLK), BF16),
        pltpu.VMEM((6, long // 8, BLK), BF16),
        pltpu.VMEM((5, wide // 4, BLK), BF16),
        pltpu.VMEM((5, long, BLK), BF16),
        pltpu.VMEM((rows, BLK), BF16),
        pltpu.SemaphoreType.DMA((4,)),
        pltpu.SemaphoreType.DMA((4,)),
        pltpu.SemaphoreType.DMA((4,)),
        pltpu.SemaphoreType.DMA((30,)),
        pltpu.SemaphoreType.DMA((30,)),
        pltpu.SemaphoreType.DMA((3,)),
        pltpu.SemaphoreType.DMA((5,)),
        pltpu.SemaphoreType.DMA((3,)),
        pltpu.SemaphoreType.DMA((5,)),
        pltpu.SemaphoreType.DMA((8,)),
        pltpu.SemaphoreType.DMA((8,)),
    ]


class Exchange:
    def __init__(self, place, rows, landing, send_sems, recv_sems, base):
        self.place, self.rows, self.landing = place, rows, landing
        self.send_sems, self.recv_sems, self.base = send_sems, recv_sems, base
        self.quarter = rows.shape[0] // 4
        self.half = self.quarter // 2

    def part(self, which, side):
        start = pl.multiple_of(which * self.quarter + side * self.half, 16)
        return self.rows.at[pl.ds(start, self.half)]

    def copy(self, index):
        place = self.place
        source, device = (
            (self.part(place.by_x, 0), place.next_x),
            (self.part(place.across, 0), place.next_x),
            (self.part(place.by_y, 1), place.next_y),
            (self.part(place.across, 1), place.next_y),
            (self.part(place.by_y, 0), place.next_y),
            (self.part(place.by_x, 1), place.next_x),
        )[index]
        where = self.base + index
        return transfer(
            source, self.landing.at[index], self.send_sems.at[where], self.recv_sems.at[where], device
        )

    def begin_x(self):
        self.copy(0).start()
        self.copy(1).start()

    def begin_y(self):
        self.copy(2).start()
        self.copy(3).start()

    def take(self, which, side, index):
        self.copy(index).wait_recv()
        target = self.part(which, side)
        add_rows(target, target, self.landing.at[index], self.half, self.half)

    def first(self):
        place = self.place
        self.take(place.by_y, 0, 1)
        self.copy(4).start()
        self.take(place.by_x, 1, 3)
        self.copy(5).start()
        self.take(place.quarter, 0, 0)
        self.take(place.quarter, 1, 2)

    def second(self):
        self.take(self.place.quarter, 0, 4)
        self.take(self.place.quarter, 1, 5)

    def own(self):
        start = pl.multiple_of(self.place.quarter * self.quarter, 16)
        return self.rows.at[pl.ds(start, self.quarter)]

    def finish(self):
        for index in range(6):
            self.copy(index).wait_send()


class Reduce:
    def __init__(self, terms, base, out, scratch):
        self.place = place = Place()
        self.terms, self.base, self.out = terms, base, out
        (
            self.mine,
            self.sib,
            wide_landing,
            long_landing,
            self.from_z,
            self.long_from_z,
            self.result,
            self.load_sems,
            self.core_send,
            self.core_recv,
            xy_send,
            xy_recv,
            self.z_send,
            self.z_recv,
            self.long_send,
            self.long_recv,
            self.last_send,
            self.last_recv,
        ) = scratch
        self.wide, self.long = split_rows(out.shape[0])
        z, high = place.z, place.high
        low = 1 - high
        self.order = (3 * low, low * (2 - 2 * z) + high * (7 - 2 * z), 1 + z % 2, z)
        self.onward = (z + 1 - 2 * high, z + 1 - 2 * (z % 2), z + 1 - 2 * high)
        self.closing = (0, (z % 2) * low, high)
        self.far = place.at_z(z + 2 - 4 * high)
        self.near = place.at_z(z + 1 - 2 * (z % 2))
        self.exchanges = [
            Exchange(
                place,
                self.mine.at[step, pl.ds(0, self.wide)],
                wide_landing.at[step],
                xy_send,
                xy_recv,
                6 * step,
            )
            for step in range(4)
        ]
        self.long_exchange = Exchange(place, self.long_rows(3), long_landing, xy_send, xy_recv, 24)

    def long_rows(self, step):
        return self.mine.at[step, pl.ds(self.wide, self.long)]

    def shard_terms(self, shard):
        rows = self.out.shape[0]
        return self.terms.at[pl.ds(pl.multiple_of(self.base + shard * rows, 16), rows)]

    def load(self, step):
        source = self.shard_terms(2 * self.order[step] + self.place.core)
        return pltpu.make_async_copy(source, self.mine.at[step], self.load_sems.at[step])

    def core_copy(self, step):
        return transfer(
            self.shard_terms(2 * self.order[step] + 1 - self.place.core),
            self.sib.at[step],
            self.core_send.at[step],
            self.core_recv.at[step],
            self.place.sibling,
        )

    def start(self):
        greet(self.place, (self.far,))
        for step in range(2):
            self.core_copy(step).start()
        for step in range(4):
            self.load(step).start()

    def core(self, step):
        place = self.place
        quarter = self.wide // 4
        exchange = self.exchanges[step]
        self.load(step).wait()
        self.core_copy(step).wait_recv()
        if step < 2:
            self.core_copy(step + 2).start()

        def add(start, size):
            block = pl.ds(pl.multiple_of(start, 16), size)
            mine = self.mine.at[step, block]
            add_rows(mine, mine, self.sib.at[step, block], size, size // 2)

        add(place.by_x * quarter, quarter)
        add(place.across * quarter, quarter)
        exchange.begin_x()
        add(place.by_y * quarter, quarter)
        exchange.begin_y()
        add(place.quarter * quarter, quarter)
        add(self.wide, self.long)

    def first(self, step):
        self.exchanges[step].first()

    def chain_copy(self, step, source, target, send_sems, recv_sems):
        goal = self.order[step]
        slot = goal + self.closing[step] * (4 - goal)
        device = self.place.at_z(self.onward[step])
        return transfer(source, target.at[slot], send_sems.at[step], recv_sems.at[slot], device)

    def z_copy(self, step):
        return self.chain_copy(step, self.exchanges[step].own(), self.from_z, self.z_send, self.z_recv)

    def long_copy(self, step):
        return self.chain_copy(
            step, self.long_rows(step), self.long_from_z, self.long_send, self.long_recv
        )

    def along_z(self, step, block, incoming, recv_sems, copy):
        place = self.place

        def take(slot):
            source = incoming.at[slot]
            transfer(source, source, self.z_send.at[0], recv_sems.at[slot], self.near).wait_recv()
            add_rows(block, block, source, block.shape[0], block.shape[0] // 2)

        if step < 3:

            @pl.when(place.inner)
            def _():
                take(self.order[step])

            copy(step).start()
        else:

            @pl.when(place.z > 0)
            def _():
                take(place.z)

            @pl.when(place.z < 3)
            def _():
                take(4)

    def second(self, step):
        self.exchanges[step].second()
        self.along_z(step, self.exchanges[step].own(), self.from_z, self.z_recv, self.z_copy)

    def long_z(self, step):
        self.along_z(step, self.long_rows(step), self.long_from_z, self.long_recv, self.long_copy)
        if step == 3:
            self.long_exchange.begin_x()
            self.long_exchange.begin_y()

    def long_first(self):
        self.long_exchange.first()

    def long_second(self):
        self.long_exchange.second()

    def final(self, long, which, side=None):
        quarter = (self.long if long else self.wide) // 4
        half = quarter // 2
        start = (self.wide if long else 0) + which * quarter + (0 if side is None else side * half)
        return self.result.at[pl.ds(pl.multiple_of(start, 16), quarter if side is None else half)]

    def last_copy(self, long, index, ref):
        device = (self.place.next_x, self.place.next_y, self.place.next_y, self.place.next_x)[index]
        where = 4 * long + index
        return transfer(ref, ref, self.last_send.at[where], self.last_recv.at[where], device)

    def share(self, long):
        own = self.final(long, self.place.quarter)
        own[...] = (self.long_exchange if long else self.exchanges[3]).own()[...]
        self.last_copy(long, 0, own).start()
        self.last_copy(long, 1, own).start()

    def share_on(self, long):
        place = self.place
        self.last_copy(long, 0, self.final(long, place.by_x)).wait_recv()
        self.last_copy(long, 2, self.final(long, place.by_x, 0)).start()
        self.last_copy(long, 1, self.final(long, place.by_y)).wait_recv()
        self.last_copy(long, 3, self.final(long, place.by_y, 1)).start()

    def events(self):
        return (
            (self.start,),
            (partial(self.core, 0),),
            (partial(self.core, 1), partial(self.first, 0), partial(self.long_z, 0)),
            (
                partial(self.core, 2),
                partial(self.first, 1),
                partial(self.second, 0),
                partial(self.long_z, 1),
            ),
            (
                partial(self.core, 3),
                partial(self.first, 2),
                partial(self.second, 1),
                partial(self.long_z, 2),
            ),
            (partial(self.first, 3), partial(self.second, 2)),
            (partial(self.second, 3), partial(self.share, 0), partial(self.long_z, 3)),
            (self.long_first, partial(self.share_on, 0)),
        )

    def finish(self):
        place = self.place
        self.long_second()
        self.share(1)
        self.share_on(1)
        for long in range(2):
            self.last_copy(long, 2, self.final(long, place.across, 0)).wait_recv()
            self.last_copy(long, 3, self.final(long, place.across, 1)).wait_recv()
        self.out[...] = self.result[...]
        for step in range(4):
            self.core_copy(step).wait_send()
            self.exchanges[step].finish()
            if step < 3:
                self.z_copy(step).wait_send()
                self.long_copy(step).wait_send()
        self.long_exchange.finish()
        for long in range(2):
            own = self.final(long, place.quarter)
            self.last_copy(long, 0, own).wait_send()
            self.last_copy(long, 1, own).wait_send()
            self.last_copy(long, 2, self.final(long, place.by_x, 0)).wait_send()
            self.last_copy(long, 3, self.final(long, place.by_y, 1)).wait_send()


def reduce_kernel(*refs, base, short_steps):
    terms, small_ref, d_ref, resid_ref, w_ref, out_ref, small_out, short_ref, long_ref = refs[:9]
    small_in, small_sum, small_send, small_recv = refs[9:13]
    reduce = Reduce(terms, base, out_ref, refs[13:])
    place = reduce.place
    partners = (place.sibling, place.next_x, place.next_y, reduce.near, reduce.far)

    def small_copy(level):
        return transfer(
            small_sum.at[level],
            small_in.at[level],
            small_send.at[level],
            small_recv.at[level],
            partners[level],
        )

    def small_start():
        small_sum[0] = small_ref[...]
        small_copy(0).start()

    def small_step(level):
        small_copy(level - 1).wait_recv()
        small_sum[level] = small_sum[level - 1] + small_in[level - 1]
        if level < 5:
            small_copy(level).start()
        else:
            small_out[...] = small_sum[5]

    small_events = ((small_start,),) + tuple((partial(small_step, level),) for level in range(1, 6)) + ((), ())
    run_events(
        pl.program_id(0),
        [actions + small for actions, small in zip(reduce.events(), small_events)],
    )
    input_product(d_ref, resid_ref, w_ref, short_ref, long_ref, short_steps)

    @pl.when(pl.program_id(0) == pl.num_programs(0) - 1)
    def _():
        reduce.finish()
        for level in range(5):
            small_copy(level).wait_send()


def reduce_late(terms, base, rows, small, d_qkv, resid, w_qkv, short_tiles):
    steps = resid.shape[0] // INPUT_ROWS
    short_steps = short_tiles * TILE // INPUT_ROWS
    in_specs, out_specs = input_specs(short_steps)

    def whole(shape):
        return pl.BlockSpec(shape, lambda step: (0, 0), pipeline_mode=pl.Buffered(1))

    return pl.pallas_call(
        partial(reduce_kernel, base=base, short_steps=short_steps),
        grid=(steps,),
        in_specs=[pl.BlockSpec(memory_space=pltpu.HBM), whole(small.shape)] + in_specs,
        out_specs=[
            pl.BlockSpec((rows, BLK), lambda step: (0, 0)),
            pl.BlockSpec(small.shape, lambda step: (0, 0)),
        ]
        + out_specs,
        out_shape=[
            jax.ShapeDtypeStruct((rows, BLK), BF16),
            jax.ShapeDtypeStruct((SMALL_ROWS, BLK), F32),
            jax.ShapeDtypeStruct((short_steps * INPUT_ROWS, D), F32),
            jax.ShapeDtypeStruct(((steps - short_steps) * INPUT_ROWS, D), F32),
        ],
        scratch_shapes=[
            pltpu.VMEM((5, SMALL_ROWS, BLK), F32),
            pltpu.VMEM((6, SMALL_ROWS, BLK), F32),
            pltpu.SemaphoreType.DMA((5,)),
            pltpu.SemaphoreType.DMA((5,)),
        ]
        + reduce_scratch(rows),
        compiler_params=pltpu.CompilerParams(
            collective_id=3, has_side_effects=True, vmem_limit_bytes=60 * MIB
        ),
        cost_estimate=pl.CostEstimate(flops=0, bytes_accessed=200 * MIB, transcendentals=0),
        name="reduce",
    )(terms, small, d_qkv, resid, w_qkv)


def count_where(condition, axis):
    return jnp.sum(condition.astype(jnp.int32), axis=axis)


def slot_codes(slots, qkv_slots, slot_count, shards):
    early = slot_count - LATE
    shard = slots // slot_count
    begin = shard * slot_count
    inside = (qkv_slots[None, :] >= begin[:, None]) & (qkv_slots[None, :] < (begin + slot_count)[:, None])
    own = count_where(qkv_slots[None, :] == slots[:, None], 1)
    before = count_where(inside & (qkv_slots[None, :] < slots[:, None]), 1)
    number = count_where(inside, 1)
    position = jnp.where(own > 0, slot_count - number + before, slots - begin - before)
    code = jnp.where(
        position < early,
        shard * early + position,
        shards * early + shard * LATE + position - early,
    )
    return code, position, jnp.max(number)


def update_kernel(
    position_ref,
    held_ref,
    early,
    late,
    master,
    left_stat,
    right_stat,
    left_root,
    right_root,
    slot_grad,
    new_left,
    new_right,
    new_master,
):
    count = master.shape[0]
    first = pl.program_id(0) * count
    split = early.shape[0] // BLK

    def block(ref, place):
        return ref[pl.ds(pl.multiple_of(place * BLK, BLK), BLK)]

    def grad_of(index):
        place = position_ref[first + index]
        grad = jnp.where(
            place < split,
            block(early, jnp.minimum(place, split - 1)),
            block(late, jnp.maximum(place - split, 0)),
        )
        return jnp.where(held_ref[first + index] > 0, grad, jnp.zeros_like(grad))

    for begin in range(0, count, 4):
        some = range(begin, min(begin + 4, count))
        grads = [grad_of(index) for index in some]
        applied = [product(left_root[index].astype(BF16), grad) for index, grad in zip(some, grads)]
        outer_left = [right_product(grad, grad) for grad in grads]
        outer_right = [left_product(grad, grad) for grad in grads]
        totals = [
            product(part.astype(BF16), right_root[index].astype(BF16)) for index, part in zip(some, applied)
        ]
        for place, index in enumerate(some):
            slot_grad[index] = grads[place].astype(F32)
            new_left[index] = STAT_DECAY * left_stat[index] + (1.0 - STAT_DECAY) * outer_left[place]
            new_right[index] = STAT_DECAY * right_stat[index] + (1.0 - STAT_DECAY) * outer_right[place]
            new_master[index] = master[index] - MATRIX_RATE * totals[place]


def update(position, held, early, late, master, left_stat, right_stat, left_root, right_root):
    slot_count = master.shape[0]
    group = max(size for size in range(1, 12) if slot_count % size == 0)
    some = pl.BlockSpec((group, BLK, BLK), lambda step, *_: (step, 0, 0))

    def whole(shape):
        return pl.BlockSpec(shape, lambda step, *_: (0, 0), pipeline_mode=pl.Buffered(1))

    return pl.pallas_call(
        update_kernel,
        grid_spec=pltpu.PrefetchScalarGridSpec(
            num_scalar_prefetch=2,
            grid=(slot_count // group,),
            in_specs=[whole(early.shape), whole(late.shape)] + [some] * 5,
            out_specs=[some] * 4,
        ),
        out_shape=[jax.ShapeDtypeStruct(master.shape, F32)] * 4,
        compiler_params=pltpu.CompilerParams(vmem_limit_bytes=60 * MIB),
        cost_estimate=pl.CostEstimate(
            flops=8 * slot_count * BLK**3, bytes_accessed=36 * slot_count * BLK**2, transcendentals=0
        ),
        name="update",
    )(position, held, early, late, master, left_stat, right_stat, left_root, right_root)


def body(
    x_short,
    x_long,
    cot_short,
    cot_long,
    logit_cot_short,
    logit_cot_long,
    len_short,
    len_long,
    block_slot,
    master,
    left_stat,
    right_stat,
    left_root,
    right_root,
    small_params,
    small_first,
    small_second,
    own_transfers,
):
    slot_count = master.shape[0]
    shards = lax.axis_size("fsdp")
    all_slots = slot_count * shards
    short_seqs, width = x_short.shape[:2]
    long_seqs = x_long.shape[0]
    short_tiles = short_seqs * width // TILE
    per_tile = TILE // width

    own = jnp.arange(slot_count, dtype=jnp.int32) + slot_count * lax.axis_index("fsdp")
    held = jnp.any(block_slot[None, :] == own[:, None], axis=1).astype(jnp.int32)
    if own_transfers:
        early_count = slot_count - LATE
        code, position, most = slot_codes(
            jnp.concatenate([block_slot, own]), block_slot[: 3 * 36], slot_count, shards
        )
        position = position[NBLK:]
        code = code[:NBLK]
        fits = most <= LATE
        gathered = gather_shards(master)
    else:
        gathered = lax.all_gather(master.astype(BF16), "fsdp", axis=0, tiled=True)
    w_qkv = assemble(block_slot, gathered)
    pieces = unpack(small_params)
    params = jnp.pad(small_params, (0, SMALL_ROWS * BLK - small_params.shape[0])).reshape(SMALL_ROWS, BLK)
    w_class = pieces[-2].reshape(SD, NCLS)
    b_class = pieces[-1].reshape(1, NCLS)
    x, *qkv, context, probs_short, probs_long = attention(
        len_short,
        len_long,
        x_short.reshape(-1, D),
        x_long.reshape(-1, D),
        params,
        w_qkv,
        short_tiles,
        width,
    )

    (
        enc_short,
        enc_long,
        logits_short,
        logits_long,
        first,
        active,
        d_up,
        d_down,
        d_branch,
        d_context,
        d_resid,
        g_student,
        g_hidden,
        g_small,
    ) = feed(
        len_short,
        len_long,
        block_slot,
        x,
        context,
        cot_short.reshape(-1, D),
        cot_long.reshape(-1, D),
        (logit_cot_short, logit_cot_long),
        (params, w_class, b_class),
        gathered,
        short_tiles,
        width,
    )
    g_out = left_product(context, d_branch).astype(BF16)
    others = (g_out, g_student.astype(BF16), g_hidden.astype(BF16))
    if own_transfers:
        terms = feed_grads(code, first, d_down, active, d_up, others, all_slots)
        *back, early_reduced = attention_back(
            qkv,
            probs_short,
            probs_long,
            d_context,
            short_tiles,
            terms.reshape(-1, BLK),
            early_count * BLK,
        )
    else:
        back = attention_back(qkv, probs_short, probs_long, d_context, short_tiles)
    d_qkv, g_b_query, g_b_value = back

    def reduce_all():
        slot_terms = feed_grads(block_slot, first, d_down, active, d_up, others, all_slots)
        slot_terms, small_terms = input_weights(
            block_slot, x, d_qkv, g_small, g_b_query, g_b_value, slot_terms
        )
        reduced = lax.psum_scatter(slot_terms, "fsdp", scatter_dimension=0, tiled=True)
        return lax.psum(reduced, "dp").reshape(-1, BLK), small_terms

    def renew(places, early, late):
        return update(
            places, held, early, late, master, left_stat, right_stat, left_root, right_root
        )

    def renew_all(blocks):
        return renew(jnp.arange(slot_count, dtype=jnp.int32), blocks, blocks)

    if own_transfers:
        terms, small_terms = input_weights(code, x, d_qkv, g_small, g_b_query, g_b_value, terms)
        late_reduced, small_total, in_short, in_long = reduce_late(
            terms.reshape(-1, BLK),
            shards * early_count * BLK,
            LATE * BLK,
            small_terms,
            d_qkv,
            d_resid,
            w_qkv,
            short_tiles,
        )

        updated = lax.cond(
            fits,
            lambda: renew(position, early_reduced, late_reduced),
            lambda: renew_all(reduce_all()[0]),
        )
    else:
        in_short, in_long = input_grads(d_qkv, d_resid, w_qkv, short_tiles)
        blocks, small_terms = reduce_all()
        updated = renew_all(blocks)
        small_total = lax.psum(small_terms, ("dp", "fsdp"))
    slot_grad, new_left, new_right, new_master = updated
    small_grad = jnp.concatenate(
        [
            small_total[:CLASS_ROW].reshape(-1),
            small_total[CLASS_ROW : CLASS_ROW + NCLS].T.reshape(-1),
            small_total[LAST_ROW, :NCLS],
        ]
    )
    new_first = BETA_ONE * small_first + (1.0 - BETA_ONE) * small_grad
    new_second = BETA_TWO * small_second + (1.0 - BETA_TWO) * small_grad * small_grad
    first_hat = new_first / (1.0 - BETA_ONE**STEP)
    second_hat = new_second / (1.0 - BETA_TWO**STEP)
    new_small = small_params - ADAM_RATE * first_hat / (jnp.sqrt(second_hat) + ADAM_EPSILON)
    return (
        enc_short.reshape(x_short.shape),
        logits_short,
        enc_long.reshape(x_long.shape),
        logits_long,
        in_short.reshape(x_short.shape),
        in_long.reshape(x_long.shape),
        slot_grad,
        new_left,
        new_right,
        new_master,
        new_first,
        new_second,
        new_small,
    )


def solution(mesh):
    both = ("dp", "fsdp")
    placed = (
        P(both, None, None),
        P(both, None, None),
        P(both, None, None),
        P(both, None, None),
        P(both, None),
        P(both, None),
        P(both),
        P(both),
        P(),
        P("fsdp", None, None),
        P("fsdp", None, None),
        P("fsdp", None, None),
        P("fsdp", None, None),
        P("fsdp", None, None),
        P(),
        P(),
        P(),
    )
    return jax.shard_map(
        partial(body, own_transfers=(mesh.shape["dp"], mesh.shape["fsdp"]) == (4, 8)),
        mesh=mesh,
        in_specs=placed,
        out_specs=(
            P(both, None, None),
            P(both, None),
            P(both, None, None),
            P(both, None),
            P(both, None, None),
            P(both, None, None),
            P("fsdp", None, None),
            P("fsdp", None, None),
            P("fsdp", None, None),
            P("fsdp", None, None),
            P(),
            P(),
            P(),
        ),
        check_vma=False,
    )
```

```python
from functools import partial

import jax
import jax.numpy as jnp
from jax import lax
from jax.experimental import pallas as pl
from jax.experimental.pallas import tpu as pltpu
from jax.sharding import PartitionSpec as P

D = 768
HEADS = 12
FF = 3072
SD = 128
PH = 2
NCLS = 14
BLK = 128
STEP = 10
NBLK = 439
TILE = 512
PAIRS = 3
GROUPS = 2
CHUNK = 768
LATE = 24

NORM_EPSILON = 1e-12
BETA_ONE = 0.9
BETA_TWO = 0.999
ADAM_EPSILON = 1e-08
ADAM_RATE = 0.1
MATRIX_RATE = 0.2
STAT_DECAY = 0.5
MASKED_SCORE = -1e30
HIGHEST_PRECISION = lax.Precision.HIGHEST
MIB = 1024 * 1024
F32 = jnp.float32
BF16 = jnp.bfloat16

def product(former, latter, precision=None):
    return jnp.dot(former, latter, preferred_element_type=F32, precision=precision)


def left_product(former, latter, precision=None):
    return lax.dot_general(
        former, latter, (((0,), (0,)), ((), ())), preferred_element_type=F32, precision=precision
    )


def right_product(former, latter, precision=None):
    return lax.dot_general(
        former, latter, (((1,), (1,)), ((), ())), preferred_element_type=F32, precision=precision
    )


def unpack(small_values):
    widths = (D, D, D, D, D, FF, D, D, D, SD, SD, SD, SD * NCLS, NCLS)
    pieces = []
    offset = 0
    for column_count in widths:
        pieces.append(small_values[offset : offset + column_count])
        offset += column_count
    return pieces


def each_block(first, row_count, col_count, action):
    def one_row(index, carry):
        row = pl.multiple_of(index * BLK, BLK)
        for col in range(col_count):
            action(first + index * col_count + col, row, col * BLK)
        return carry

    lax.fori_loop(0, row_count, one_row, 0)


def load_blocks(slot_ref, blocks, target, sem, first, row_count, col_count, col_start=0):
    def move(block, row, col):
        pltpu.make_async_copy(
            blocks.at[slot_ref[block]],
            target.at[pl.ds(row, BLK), pl.ds(col + col_start * BLK, BLK)],
            sem,
        ).start()

    each_block(first, row_count, col_count, move)


def wait_whole(target, sem):
    pltpu.make_async_copy(target, target, sem).wait()


def assemble_kernel(slot_ref, blocks, out, sem):
    for which in range(3):
        load_blocks(slot_ref, blocks, out, sem, 36 * which, 6, 6, 6 * which)
    wait_whole(out, sem)


def assemble(block_slot, blocks):
    return pl.pallas_call(
        assemble_kernel,
        grid_spec=pltpu.PrefetchScalarGridSpec(
            num_scalar_prefetch=1,
            grid=(1,),
            in_specs=[pl.BlockSpec(memory_space=pltpu.HBM)],
            out_specs=pl.BlockSpec(memory_space=pltpu.VMEM),
            scratch_shapes=[pltpu.SemaphoreType.DMA],
        ),
        out_shape=jax.ShapeDtypeStruct((D, 3 * D), BF16),
        compiler_params=pltpu.CompilerParams(vmem_limit_bytes=60 * MIB),
        name="assemble",
    )(block_slot, blocks)


def join_small(small_ref, query_ref, value_ref, small_out):
    small_out[...] = small_ref[...]
    for start, ref in ((0, query_ref), (D // BLK, value_ref)):
        for index in range(D // BLK):
            small_out[start + index : start + index + 1, :] = ref[:, index * BLK : (index + 1) * BLK]


PART = 256
ACROSS = PART // BLK


def feed_grads_kernel(
    code_ref,
    first_turned,
    down_turned,
    active_ref,
    d_up_ref,
    g_out,
    g_student,
    g_hidden,
    terms,
    up_stage,
    down_stage,
    up_sems,
    down_sems,
    other_sems,
):
    step = pl.program_id(0)
    last = pl.num_programs(0) - 1
    slot = step % 2
    others = ((g_out, 108, 6, 6), (g_student, 432, 6, 1), (g_hidden, 438, 1, 1))

    @pl.when(step == 0)
    def _():
        for which, (grad, first, row_count, col_count) in enumerate(others):

            def move(block, row, col, which=which, grad=grad):
                pltpu.make_async_copy(
                    grad.at[pl.ds(row, BLK), pl.ds(col, BLK)], terms.at[code_ref[block]], other_sems.at[which]
                ).start()

            each_block(first, row_count, col_count, move)

    @pl.when(step >= 2)
    def _():
        wait_whole(up_stage.at[slot], up_sems.at[slot])
        wait_whole(down_stage.at[slot], down_sems.at[slot])

    up_stage[slot] = product(first_turned[...], d_up_ref[...]).astype(BF16)
    down_stage[slot] = product(down_turned[...], active_ref[...]).T.astype(BF16)
    for row in range(D // BLK):
        for col in range(ACROSS):
            pltpu.make_async_copy(
                up_stage.at[slot, pl.ds(row * BLK, BLK), pl.ds(col * BLK, BLK)],
                terms.at[code_ref[144 + row * (FF // BLK) + step * ACROSS + col]],
                up_sems.at[slot],
            ).start()
            pltpu.make_async_copy(
                down_stage.at[slot, pl.ds(col * BLK, BLK), pl.ds(row * BLK, BLK)],
                terms.at[code_ref[288 + (step * ACROSS + col) * (D // BLK) + row]],
                down_sems.at[slot],
            ).start()

    @pl.when(step == last)
    def _():
        for place in range(2):
            wait_whole(up_stage.at[place], up_sems.at[place])
            wait_whole(down_stage.at[place], down_sems.at[place])
        for which, (grad, *_) in enumerate(others):
            wait_whole(grad, other_sems.at[which])


def feed_grads(code, first, d_down, active, d_up, others, slot_count):
    tokens = first.shape[1]

    def whole(shape):
        return pl.BlockSpec(shape, lambda step, *_: (0, 0), pipeline_mode=pl.Buffered(1))

    part = pl.BlockSpec((tokens, PART), lambda step, *_: (0, step))
    return pl.pallas_call(
        feed_grads_kernel,
        grid_spec=pltpu.PrefetchScalarGridSpec(
            num_scalar_prefetch=1,
            grid=(FF // PART,),
            in_specs=[whole(first.shape), whole(d_down.shape), part, part]
            + [whole(other.shape) for other in others],
            out_specs=pl.BlockSpec(memory_space=pltpu.HBM),
            scratch_shapes=[
                pltpu.VMEM((2, D, PART), BF16),
                pltpu.VMEM((2, PART, D), BF16),
                pltpu.SemaphoreType.DMA((2,)),
                pltpu.SemaphoreType.DMA((2,)),
                pltpu.SemaphoreType.DMA((3,)),
            ],
        ),
        out_shape=jax.ShapeDtypeStruct((slot_count, BLK, BLK), BF16),
        compiler_params=pltpu.CompilerParams(vmem_limit_bytes=60 * MIB),
        cost_estimate=pl.CostEstimate(
            flops=4 * tokens * D * FF, bytes_accessed=50 * MIB, transcendentals=0
        ),
        name="feed_grads",
    )(code, first, d_down, active, d_up, *others)


def input_weights_kernel(
    code_ref, turned, d_ref, small_ref, query_ref, value_ref, _, terms, small_out, stage, sems
):
    step = pl.program_id(0)
    slot = step % 2

    @pl.when(step == 0)
    def _():
        join_small(small_ref, query_ref, value_ref, small_out)

    @pl.when(step >= 2)
    def _():
        wait_whole(stage.at[slot], sems.at[slot])

    stage[slot] = product(turned[...], d_ref[...]).astype(BF16)
    steps = D // PART
    first = (step // steps) * 36 + step % steps * ACROSS
    for row in range(D // BLK):
        for col in range(ACROSS):
            pltpu.make_async_copy(
                stage.at[slot, pl.ds(row * BLK, BLK), pl.ds(col * BLK, BLK)],
                terms.at[code_ref[first + row * (D // BLK) + col]],
                sems.at[slot],
            ).start()

    @pl.when(step == pl.num_programs(0) - 1)
    def _():
        for place in range(2):
            wait_whole(stage.at[place], sems.at[place])


def input_weights(code, x, d_qkv, small, g_query, g_value, terms):
    tokens = x.shape[1]

    def whole(shape):
        return pl.BlockSpec(shape, lambda step, *_: (0, 0), pipeline_mode=pl.Buffered(1))

    hbm = pl.BlockSpec(memory_space=pltpu.HBM)
    return pl.pallas_call(
        input_weights_kernel,
        grid_spec=pltpu.PrefetchScalarGridSpec(
            num_scalar_prefetch=1,
            grid=(3 * D // PART,),
            in_specs=[
                whole(x.shape),
                pl.BlockSpec((tokens, PART), lambda step, *_: (0, step)),
                whole(small.shape),
                whole(g_query.shape),
                whole(g_value.shape),
                hbm,
            ],
            out_specs=[hbm, pl.BlockSpec(small.shape, lambda step, *_: (0, 0))],
            scratch_shapes=[
                pltpu.VMEM((2, D, PART), BF16),
                pltpu.SemaphoreType.DMA((2,)),
            ],
        ),
        out_shape=[
            jax.ShapeDtypeStruct(terms.shape, BF16),
            jax.ShapeDtypeStruct(small.shape, F32),
        ],
        input_output_aliases={6: 0},
        compiler_params=pltpu.CompilerParams(vmem_limit_bytes=60 * MIB),
        cost_estimate=pl.CostEstimate(
            flops=6 * tokens * D * D, bytes_accessed=16 * MIB, transcendentals=0
        ),
        name="input_weights",
    )(code, x, d_qkv, small, g_query, g_value, terms)


def half_masks():
    lane = lax.broadcasted_iota(jnp.int32, (1, BLK), 1)
    low = (lane < BLK // 2).astype(BF16)
    return low, (1.0 - low.astype(F32)).astype(BF16)


def stack_heads(values, low, high):
    return jnp.concatenate([values * low, values * high], axis=0)


def pick_heads(values):
    rows = values.shape[0] // 2
    lane = lax.broadcasted_iota(jnp.int32, (rows, BLK), 1)
    return jnp.where(lane < BLK // 2, values[:rows], values[rows:])


def pipelined(count, before, middle, after):
    started = before(0)
    done = None
    for index in range(count):
        current = started
        if index + 1 < count:
            started = before(index + 1)
        if done is not None:
            after(index - 1, done)
        done = middle(index, current)
    after(count - 1, done)


def softmax(scores, length):
    visible = lax.broadcasted_iota(jnp.int32, scores.shape, 1) < length
    scores = jnp.where(visible, scores, MASKED_SCORE)
    powers = jnp.exp(scores - jnp.max(scores, axis=-1, keepdims=True))
    total = jnp.sum(powers, axis=-1, keepdims=True)
    return (powers * (1.0 / total)).astype(BF16)


def attention_kernel(
    len_short,
    len_long,
    x_short_ref,
    x_long_ref,
    params,
    w_ref,
    x_ref,
    q_ref,
    k_ref,
    v_ref,
    context_ref,
    short_ref,
    long_ref,
    bias,
    *,
    short_tiles,
):
    tile = pl.program_id(0)
    group = pl.program_id(1)
    low, high = half_masks()
    width = short_ref.shape[-1]
    per_tile = TILE // width

    wide = PAIRS * BLK
    start = pl.multiple_of(group * wide, wide)

    @pl.when((tile == 0) & (group == 0))
    def _():
        for which in range(2):
            for place in range(D // BLK):
                row = which * (D // BLK) + place
                bias[which : which + 1, place * BLK : (place + 1) * BLK] = params[row : row + 1, :]

    @pl.when((tile < short_tiles) & (group == 0))
    def _():
        x_ref[...] = x_short_ref[...]

    @pl.when((tile >= short_tiles) & (group == 0))
    def _():
        x_ref[...] = x_long_ref[...]

    rows_in = x_ref[...]
    queries = product(rows_in, w_ref[:, pl.ds(start, wide)]) + bias[0:1, pl.ds(start, wide)]
    q_ref[...] = (queries * 0.125).astype(BF16)
    k_ref[...] = product(rows_in, w_ref[:, pl.ds(D + start, wide)]).astype(BF16)
    values = product(rows_in, w_ref[:, pl.ds(2 * D + start, wide)]) + bias[1:2, pl.ds(start, wide)]
    v_ref[...] = values.astype(BF16)

    def attend(units, kept_ref):
        def scores(index):
            rows, keys, cols, _, _ = units[index]
            return right_product(stack_heads(q_ref[rows, cols], low, high), k_ref[keys, cols])

        def weigh(index, values):
            _, _, _, length, place = units[index]
            probs = softmax(values, length)
            kept_ref[place] = probs
            return probs

        def mix(index, probs):
            rows, keys, cols, _, _ = units[index]
            context_ref[rows, cols] = pick_heads(product(probs, v_ref[keys, cols])).astype(BF16)

        pipelined(len(units), scores, weigh, mix)

    @pl.when(tile < short_tiles)
    def _():
        units = []
        for seq in range(per_tile):
            rows = slice(seq * width, (seq + 1) * width)
            length = len_short[tile * per_tile + seq]
            for pair in range(PAIRS):
                cols = slice(pair * BLK, (pair + 1) * BLK)
                units.append((rows, rows, cols, length, (0, pair, seq)))
        attend(units, short_ref)

    @pl.when(tile >= short_tiles)
    def _():
        length = len_long[tile - short_tiles]
        half = TILE // 2
        units = []
        for pair in range(PAIRS):
            cols = slice(pair * BLK, (pair + 1) * BLK)
            for part in range(2):
                rows = slice(part * half, (part + 1) * half)
                units.append((rows, slice(0, TILE), cols, length, (0, pair, part)))
        attend(units, long_ref)


def run_events(step, events):
    for index, actions in enumerate(events):

        @pl.when(step == index)
        def _(actions=actions):
            for action in actions:
                action()


def probs_shapes(short_tiles, long_tiles, width):
    per_tile = TILE // width
    return (
        (short_tiles, 2 * PAIRS, per_tile, 2 * width, width),
        (long_tiles, 2 * PAIRS, 2, TILE, TILE),
    )


def short_index(tile, short_tiles):
    return jnp.minimum(tile, short_tiles - 1)


def long_index(tile, short_tiles):
    return jnp.maximum(tile - short_tiles, 0)


def probs_maps(short_tiles):
    def short_map(tile, group):
        last = jnp.minimum(tile // short_tiles, 1)
        return (short_index(tile, short_tiles), group + last * (GROUPS - 1 - group), 0, 0, 0)

    def long_map(tile, group):
        begun = jnp.minimum(tile // short_tiles, 1)
        return (long_index(tile, short_tiles), begun * group, 0, 0, 0)

    return short_map, long_map


def attention(len_short, len_long, x_short, x_long, params, w_qkv, short_tiles, width):
    tiles = (x_short.shape[0] + x_long.shape[0]) // TILE
    wide = PAIRS * BLK
    short_shape, long_shape = probs_shapes(short_tiles, tiles - short_tiles, width)
    short_map, long_map = probs_maps(short_tiles)
    flops = 4 * D * TILE * TILE * tiles + 6 * D * D * TILE * tiles
    rows = pl.BlockSpec((TILE, wide), lambda tile, group: (tile, group))
    scalars = pl.BlockSpec(memory_space=pltpu.SMEM)

    def whole(shape):
        return pl.BlockSpec(shape, lambda tile, group: (0,) * len(shape), pipeline_mode=pl.Buffered(1))

    in_specs = [
        scalars,
        scalars,
        pl.BlockSpec((TILE, D), lambda tile, group: (short_index(tile, short_tiles), 0)),
        pl.BlockSpec((TILE, D), lambda tile, group: (long_index(tile, short_tiles), 0)),
        whole(params.shape),
        whole((D, 3 * D)),
    ]
    out_specs = [
        pl.BlockSpec((TILE, D), lambda tile, group: (tile, 0)),
        rows,
        rows,
        rows,
        rows,
        pl.BlockSpec((1, PAIRS) + short_shape[2:], short_map),
        pl.BlockSpec((1, PAIRS) + long_shape[2:], long_map),
    ]
    out_shape = [jax.ShapeDtypeStruct((tiles * TILE, D), BF16)] * 5 + [
        jax.ShapeDtypeStruct(short_shape, BF16),
        jax.ShapeDtypeStruct(long_shape, BF16),
    ]
    arguments = [len_short, len_long, x_short, x_long, params, w_qkv]
    return pl.pallas_call(
        partial(attention_kernel, short_tiles=short_tiles),
        grid=(tiles, GROUPS),
        in_specs=in_specs,
        out_specs=out_specs,
        out_shape=out_shape,
        scratch_shapes=[pltpu.VMEM((8, D), F32)],
        compiler_params=pltpu.CompilerParams(vmem_limit_bytes=60 * MIB),
        cost_estimate=pl.CostEstimate(
            flops=flops, bytes_accessed=35 * MIB, transcendentals=HEADS * TILE * TILE * tiles // 2
        ),
        name="attention",
    )(*arguments)


def attention_back_kernel(*refs, short_tiles, transfers):
    q_ref, k_ref, v_ref, short_ref, long_ref, dc_ref, x_ref = refs[:7]
    refs = refs[7:]
    if transfers:
        terms_ref, refs = refs[0], refs[1:]
    out_ref, bq_ref, bv_ref, turned_ref = refs[:4]
    tile = pl.program_id(0)
    group = pl.program_id(1)
    low, high = half_masks()
    width = short_ref.shape[-1]
    per_tile = TILE // width
    if transfers:
        reduce = Reduce(terms_ref, 0, refs[4], refs[5:])
        run_events(
            tile * GROUPS + group,
            (
                (reduce.start,),
                (partial(reduce.core, 0),),
                (partial(reduce.core, 1), partial(reduce.first, 0)),
                (partial(reduce.core, 2), partial(reduce.first, 1), partial(reduce.second, 0)),
                (partial(reduce.core, 3), partial(reduce.first, 2), partial(reduce.second, 1)),
                (partial(reduce.first, 3), partial(reduce.second, 2)),
                (partial(reduce.second, 3), reduce.share),
                (reduce.share_on,),
            ),
        )

    wide = PAIRS * BLK
    start = pl.multiple_of(group * wide, wide)

    def columns(which, cols):
        return pl.ds(pl.multiple_of(which * D + start + cols.start, BLK), BLK)

    def go_back(units, kept_ref, parts):
        sums = {}

        def spread_in(index):
            rows, keys, cols, _ = units[index]
            return right_product(stack_heads(dc_ref[rows, cols], low, high), v_ref[keys, cols])

        def differ(index, d_probs):
            wide = kept_ref[units[index][3]].astype(F32)
            weighted = wide * d_probs
            return (weighted - wide * jnp.sum(weighted, axis=-1, keepdims=True)).astype(BF16)

        def gather_up(index, d_scores):
            rows, keys, cols, place = units[index]
            d_queries = pick_heads(product(d_scores, k_ref[keys, cols])) * 0.125
            out_ref[rows, columns(0, cols)] = d_queries.astype(BF16)
            d_keys = left_product(d_scores, stack_heads(q_ref[rows, cols], low, high))
            d_values = left_product(kept_ref[place], stack_heads(dc_ref[rows, cols], low, high))
            if index % parts:
                d_keys += sums["keys"]
                d_values += sums["values"]
            if index % parts == parts - 1:
                out_ref[keys, columns(1, cols)] = d_keys.astype(BF16)
                out_ref[keys, columns(2, cols)] = d_values.astype(BF16)
            else:
                sums.update(keys=d_keys, values=d_values)

        pipelined(len(units), spread_in, differ, gather_up)

    @pl.when(tile < short_tiles)
    def _():
        units = []
        for seq in range(per_tile):
            rows = slice(seq * width, (seq + 1) * width)
            for pair in range(PAIRS):
                cols = slice(pair * BLK, (pair + 1) * BLK)
                units.append((rows, rows, cols, (0, pair, seq)))
        go_back(units, short_ref, 1)

    @pl.when(tile >= short_tiles)
    def _():
        half = TILE // 2
        units = []
        for pair in range(PAIRS):
            cols = slice(pair * BLK, (pair + 1) * BLK)
            for part in range(2):
                rows = slice(part * half, (part + 1) * half)
                units.append((rows, slice(0, TILE), cols, (0, pair, part)))
        go_back(units, long_ref, 2)

    @pl.when(group == 0)
    def _():
        turned_ref[...] = x_ref[...].T

    @pl.when((tile == 0) & (group == 0))
    def _():
        bq_ref[...] = jnp.zeros_like(bq_ref)
        bv_ref[...] = jnp.zeros_like(bv_ref)

    bq_ref[:, pl.ds(start, wide)] += column_sum(out_ref[:, pl.ds(start, wide)])
    bv_ref[:, pl.ds(start, wide)] += column_sum(out_ref[:, pl.ds(2 * D + start, wide)])

    if transfers:

        @pl.when((tile == pl.num_programs(0) - 1) & (group == GROUPS - 1))
        def _():
            reduce.finish()


def attention_back(qkv, probs_short, probs_long, d_context, x, short_tiles, terms=None, count=0):
    tiles = d_context.shape[0] // TILE
    wide = PAIRS * BLK
    short_map, long_map = probs_maps(short_tiles)
    rows = pl.BlockSpec((TILE, wide), lambda tile, group: (tile, group))
    row = pl.BlockSpec((1, D), lambda tile, group: (0, 0))
    flops = 10 * D * TILE * TILE * tiles
    in_specs = [
        rows,
        rows,
        rows,
        pl.BlockSpec((1, PAIRS) + probs_short.shape[2:], short_map),
        pl.BlockSpec((1, PAIRS) + probs_long.shape[2:], long_map),
        rows,
        pl.BlockSpec((TILE, D), lambda tile, group: (tile, 0)),
    ]
    out_specs = [
        pl.BlockSpec((TILE, 3 * D), lambda tile, group: (tile, 0)),
        row,
        row,
        pl.BlockSpec((D, TILE), lambda tile, group: (0, tile)),
    ]
    out_shape = [
        jax.ShapeDtypeStruct((tiles * TILE, 3 * D), BF16),
        jax.ShapeDtypeStruct((1, D), F32),
        jax.ShapeDtypeStruct((1, D), F32),
        jax.ShapeDtypeStruct((D, tiles * TILE), BF16),
    ]
    arguments = [*qkv, probs_short, probs_long, d_context, x]
    scratch = []
    params = dict(vmem_limit_bytes=60 * MIB)
    if terms is not None:
        arguments.append(terms)
        in_specs.append(pl.BlockSpec(memory_space=pltpu.HBM))
        out_specs.append(pl.BlockSpec((count, BLK), lambda tile, group: (0, 0)))
        out_shape.append(jax.ShapeDtypeStruct((count, BLK), BF16))
        scratch = reduce_scratch(count)
        params.update(collective_id=2, has_side_effects=True)
    return pl.pallas_call(
        partial(attention_back_kernel, short_tiles=short_tiles, transfers=terms is not None),
        grid=(tiles, GROUPS),
        in_specs=in_specs,
        out_specs=out_specs,
        out_shape=out_shape,
        scratch_shapes=scratch,
        compiler_params=pltpu.CompilerParams(**params),
        cost_estimate=pl.CostEstimate(flops=flops, bytes_accessed=50 * MIB, transcendentals=0),
        name="attention_back",
    )(*arguments)


INPUT_ROWS = 256


def input_product(d_ref, resid_ref, w_ref, short_ref, long_ref, short_steps):
    step = pl.program_id(0)
    total = resid_ref[...] + right_product(d_ref[...], w_ref[...])

    @pl.when(step < short_steps)
    def _():
        short_ref[...] = total

    @pl.when(step >= short_steps)
    def _():
        long_ref[...] = total


def input_specs(short_steps):
    rows = [pl.BlockSpec((INPUT_ROWS, width), lambda step: (step, 0)) for width in (3 * D, D)]
    whole = pl.BlockSpec((D, 3 * D), lambda step: (0, 0), pipeline_mode=pl.Buffered(1))
    outs = [
        pl.BlockSpec((INPUT_ROWS, D), lambda step: (short_index(step, short_steps), 0)),
        pl.BlockSpec((INPUT_ROWS, D), lambda step: (long_index(step, short_steps), 0)),
    ]
    return rows + [whole], outs


def input_grads(d_qkv, resid, w_qkv, short_tiles):
    steps = resid.shape[0] // INPUT_ROWS
    short_steps = short_tiles * TILE // INPUT_ROWS
    in_specs, out_specs = input_specs(short_steps)
    return pl.pallas_call(
        partial(input_product, short_steps=short_steps),
        grid=(steps,),
        in_specs=in_specs,
        out_specs=out_specs,
        out_shape=[
            jax.ShapeDtypeStruct((short_steps * INPUT_ROWS, D), F32),
            jax.ShapeDtypeStruct(((steps - short_steps) * INPUT_ROWS, D), F32),
        ],
        compiler_params=pltpu.CompilerParams(vmem_limit_bytes=60 * MIB),
        name="input_grads",
    )(d_qkv, resid, w_qkv)


def normal_parts(values):
    below = 0.5 * lax.erf(values * 0.7071067811865476) + 0.5
    return below, jnp.exp(-0.5 * values * values) * 0.3989422804014327


B_OUT, GAIN_ONE, SHIFT_ONE, B_UP, B_DOWN, GAIN_TWO, SHIFT_TWO, B_STUDENT, POOL_QUERY, B_HIDDEN = range(10)
VECTORS = (
    (12, 6),
    (18, 6),
    (24, 6),
    (30, 24),
    (54, 6),
    (60, 6),
    (66, 6),
    (72, 1),
    (73, 1),
    (74, 1),
)
CLASS_ROW = 75
LAST_ROW = 91
SMALL_ROWS = 96


def norm_parts(values):
    center = values - jnp.mean(values, axis=-1, keepdims=True)
    spread = jnp.mean(center * center, axis=-1, keepdims=True)
    inverse = lax.rsqrt(spread + NORM_EPSILON)
    return center * inverse, inverse


def norm_back(d_values, gain, unit, inverse):
    d_unit = d_values * gain
    return inverse * (
        d_unit
        - jnp.mean(d_unit, axis=-1, keepdims=True)
        - unit * jnp.mean(d_unit * unit, axis=-1, keepdims=True)
    )


def column_sum(values):
    return jnp.sum(values.astype(F32), axis=0, keepdims=True)


def pool_weights(student, query, length):
    scaled = student * query
    lane = lax.broadcasted_iota(jnp.int32, scaled.shape, 1)
    place = lax.broadcasted_iota(jnp.int32, (scaled.shape[0], 1), 0)
    weights = []
    for side in (lane < SD // PH, lane >= SD // PH):
        scores = jnp.sum(jnp.where(side, scaled, 0.0), axis=-1, keepdims=True)
        scores = jnp.where(place < length, scores, MASKED_SCORE)
        powers = jnp.exp(scores - jnp.max(scores, axis=0, keepdims=True))
        weights.append(powers / jnp.sum(powers, axis=0, keepdims=True))
    return jnp.where(lane < SD // PH, weights[0], weights[1]), weights


def student_back(student, query, weights, both, d_pooled):
    lane = lax.broadcasted_iota(jnp.int32, student.shape, 1)
    moved = student * d_pooled
    d_scores = []
    for side, weight in zip((lane < SD // PH, lane >= SD // PH), weights):
        d_weight = jnp.sum(jnp.where(side, moved, 0.0), axis=-1, keepdims=True)
        d_scores.append(weight * (d_weight - jnp.sum(weight * d_weight, axis=0, keepdims=True)))
    d_score = jnp.where(lane < SD // PH, d_scores[0], d_scores[1])
    d_query = jnp.sum(d_score * student, axis=0, keepdims=True) * 0.125
    return both * d_pooled + d_score * query, d_query


def feed_kernel(
    len_short,
    len_long,
    slot_ref,
    x_ref,
    context_ref,
    cot_short_ref,
    cot_long_ref,
    logit_cot_short,
    logit_cot_long,
    params,
    w_class_ref,
    b_class_ref,
    blocks,
    enc_short_ref,
    enc_long_ref,
    logits_short,
    logits_long,
    first_ref,
    active_ref,
    d_up_ref,
    d_down_ref,
    d_branch_ref,
    d_context_ref,
    d_resid_ref,
    g_student,
    g_hidden,
    g_small,
    slope,
    pooled_ref,
    d_student_ref,
    w_out,
    w_up,
    w_down,
    w_student,
    w_hidden,
    vectors,
    totals,
    g_class,
    g_last,
    w_class,
    b_class,
    logit_cot,
    sems,
    *,
    short_tiles,
    width,
):
    tile = pl.program_id(0)
    per_tile = TILE // width
    loads = ((w_out, 108, 6, 6), (w_up, 144, 6, 24), (w_down, 288, 24, 6), (w_student, 432, 6, 1), (w_hidden, 438, 1, 1))

    def arrive(*indices):
        @pl.when(tile == 0)
        def _():
            for index in indices:
                wait_whole(loads[index][0], sems.at[index])

    @pl.when(tile == 0)
    def _():
        for index, (target, block, row_count, col_count) in enumerate(loads):
            load_blocks(slot_ref, blocks, target, sems.at[index], block, row_count, col_count)
        for index, (start, count) in enumerate(VECTORS):
            for place in range(count):
                vectors[index : index + 1, place * BLK : (place + 1) * BLK] = params[
                    start + place : start + place + 1, :
                ]
        for ref in (totals, g_class, g_last, g_student, g_hidden, w_class, b_class):
            ref[...] = jnp.zeros_like(ref)
        w_class[:, :NCLS] = w_class_ref[...]
        b_class[:, :NCLS] = b_class_ref[...]

    def vector(index):
        return vectors[index : index + 1, : VECTORS[index][1] * BLK]

    def add_total(index, values):
        totals[index : index + 1, : VECTORS[index][1] * BLK] += column_sum(values)

    arrive(0)
    branch = product(context_ref[...], w_out[...]) + vector(B_OUT)
    unit_one, inverse_one = norm_parts(x_ref[...].astype(F32) + branch)
    first = (unit_one * vector(GAIN_ONE) + vector(SHIFT_ONE)).astype(BF16)
    first_ref[...] = first.T
    arrive(1)
    chunks = [slice(start, start + CHUNK) for start in range(0, FF, CHUNK)]

    def rise(index):
        return product(first, w_up[:, chunks[index]])

    def bend(index, upward):
        upward = upward + vectors[B_UP : B_UP + 1, chunks[index]]
        below, density = normal_parts(upward)
        active_ref[:, chunks[index]] = (upward * below).astype(BF16)
        slope[:, chunks[index]] = (below + upward * density).astype(BF16)

    pipelined(len(chunks), rise, bend, lambda *_: None)
    arrive(2, 3, 4)
    downward = product(active_ref[...], w_down[...]) + vector(B_DOWN)
    unit_two, inverse_two = norm_parts(first.astype(F32) + downward)
    encoded = (unit_two * vector(GAIN_TWO) + vector(SHIFT_TWO)).astype(BF16)

    @pl.when(tile < short_tiles)
    def _():
        enc_short_ref[...] = encoded

    @pl.when(tile >= short_tiles)
    def _():
        enc_long_ref[...] = encoded

    student = product(encoded, w_student[...]) + vector(B_STUDENT)
    query = vector(POOL_QUERY) * 0.125
    pooled_ref[...] = jnp.zeros_like(pooled_ref)

    def head():
        pooled = pooled_ref[...]
        wide_hidden = w_hidden[...].astype(F32)
        hidden = jnp.tanh(product(pooled, wide_hidden, HIGHEST_PRECISION) + vector(B_HIDDEN))
        logits = product(hidden, w_class[...], HIGHEST_PRECISION) + b_class[...]
        d_logits = logit_cot[...]
        g_last[...] += column_sum(d_logits)
        g_class[...] += left_product(d_logits, hidden, HIGHEST_PRECISION)
        d_hidden = right_product(d_logits, w_class[...], HIGHEST_PRECISION)
        d_hidden = d_hidden * (1.0 - hidden * hidden)
        add_total(B_HIDDEN, d_hidden)
        g_hidden[...] += left_product(pooled, d_hidden, HIGHEST_PRECISION)
        return logits, right_product(d_hidden, wide_hidden, HIGHEST_PRECISION)

    def pool(starts, size, lengths, cot_ref, logits_ref, first):
        count = len(starts)
        logit_cot[...] = jnp.zeros_like(logit_cot)
        for index in range(count):
            logit_cot[index : index + 1, :NCLS] = cot_ref[pl.ds(first + index, 1), :]
        kept = []
        for index, (start, length) in enumerate(zip(starts, lengths)):
            rows = student[start : start + size]
            both, weights = pool_weights(rows, query, length)
            pooled_ref[index : index + 1, :] = column_sum(both * rows)
            kept.append((start, rows, both, weights))
        logits, d_pooled = head()
        for index in range(count):
            logits_ref[pl.ds(first + index, 1), :] = logits[index : index + 1, :NCLS]
        for index, (start, rows, both, weights) in enumerate(kept):
            d_rows, d_query = student_back(rows, query, weights, both, d_pooled[index : index + 1])
            d_student_ref[start : start + size, :] = d_rows.astype(BF16)
            add_total(POOL_QUERY, d_query)

    @pl.when(tile < short_tiles)
    def _():
        pool(
            [seq * width for seq in range(per_tile)],
            width,
            [len_short[tile * per_tile + seq] for seq in range(per_tile)],
            logit_cot_short,
            logits_short,
            tile * per_tile,
        )

    @pl.when(tile >= short_tiles)
    def _():
        long = tile - short_tiles
        pool([0], TILE, [len_long[long]], logit_cot_long, logits_long, long)

    d_student = d_student_ref[...]
    add_total(B_STUDENT, d_student)
    g_student[...] += left_product(encoded, d_student)
    cotangent = jnp.where(tile < short_tiles, cot_short_ref[...], cot_long_ref[...])
    d_second = cotangent.astype(F32) + right_product(d_student, w_student[...])
    add_total(GAIN_TWO, d_second * unit_two)
    add_total(SHIFT_TWO, d_second)
    d_resid_two = norm_back(d_second, vector(GAIN_TWO), unit_two, inverse_two)
    d_down = d_resid_two.astype(BF16)
    d_down_ref[...] = d_down.T
    add_total(B_DOWN, d_down)

    def fall(index):
        return right_product(d_down, w_down[chunks[index], :])

    def bend_back(index, d_active):
        d_up = (d_active * slope[:, chunks[index]].astype(F32)).astype(BF16)
        d_up_ref[:, chunks[index]] = d_up
        totals[B_UP : B_UP + 1, chunks[index]] += column_sum(d_up)

    pipelined(len(chunks), fall, bend_back, lambda *_: None)
    d_first = d_resid_two + right_product(d_up_ref[...], w_up[...])
    add_total(GAIN_ONE, d_first * unit_one)
    add_total(SHIFT_ONE, d_first)
    d_resid_one = norm_back(d_first, vector(GAIN_ONE), unit_one, inverse_one)
    d_resid_ref[...] = d_resid_one
    d_branch = d_resid_one.astype(BF16)
    d_branch_ref[...] = d_branch
    add_total(B_OUT, d_branch)
    d_context_ref[...] = right_product(d_branch, w_out[...]).astype(BF16)

    @pl.when(tile == pl.num_programs(0) - 1)
    def _():
        g_small[...] = jnp.zeros_like(g_small)
        for index, (start, count) in enumerate(VECTORS):
            for place in range(count):
                g_small[start + place : start + place + 1, :] = totals[
                    index : index + 1, place * BLK : (place + 1) * BLK
                ]
        g_small[CLASS_ROW : CLASS_ROW + NCLS, :] = g_class[:NCLS, :]
        g_small[LAST_ROW : LAST_ROW + 1, :] = g_last[...]


def feed(
    len_short, len_long, block_slot, x, context, cot_short, cot_long, logit_cots, small, blocks, short_tiles, width
):
    tiles = x.shape[0] // TILE
    long_tiles = tiles - short_tiles

    def whole(shape):
        return pl.BlockSpec(shape, lambda tile, *_: (0,) * len(shape), pipeline_mode=pl.Buffered(1))

    def kept(shape):
        return pl.BlockSpec(shape, lambda tile, *_: (0,) * len(shape))

    def rows(columns):
        return pl.BlockSpec((TILE, columns), lambda tile, *_: (tile, 0))

    turned = pl.BlockSpec((D, TILE), lambda tile, *_: (0, tile))
    short_rows = pl.BlockSpec((TILE, D), lambda tile, *_: (short_index(tile, short_tiles), 0))
    long_rows = pl.BlockSpec((TILE, D), lambda tile, *_: (long_index(tile, short_tiles), 0))
    grad_shapes = ((D, SD), (SD, SD), (SMALL_ROWS, BLK))
    total = tiles * TILE
    return pl.pallas_call(
        partial(feed_kernel, short_tiles=short_tiles, width=width),
        grid_spec=pltpu.PrefetchScalarGridSpec(
            num_scalar_prefetch=3,
            grid=(tiles,),
            in_specs=[rows(D), rows(D), short_rows, long_rows]
            + [whole(array.shape) for array in (*logit_cots, *small)]
            + [pl.BlockSpec(memory_space=pltpu.HBM)],
            out_specs=[
                short_rows,
                long_rows,
                kept(logit_cots[0].shape),
                kept(logit_cots[1].shape),
                turned,
                rows(FF),
                rows(FF),
                turned,
                rows(D),
                rows(D),
                rows(D),
            ]
            + [kept(shape) for shape in grad_shapes],
            scratch_shapes=[
                pltpu.VMEM((TILE, FF), BF16),
                pltpu.VMEM((8, SD), F32),
                pltpu.VMEM((TILE, SD), BF16),
                pltpu.VMEM((D, D), BF16),
                pltpu.VMEM((D, FF), BF16),
                pltpu.VMEM((FF, D), BF16),
                pltpu.VMEM((D, SD), BF16),
                pltpu.VMEM((SD, SD), BF16),
                pltpu.VMEM((16, FF), F32),
                pltpu.VMEM((16, FF), F32),
                pltpu.VMEM((SD, SD), F32),
                pltpu.VMEM((1, SD), F32),
                pltpu.VMEM((SD, SD), F32),
                pltpu.VMEM((1, SD), F32),
                pltpu.VMEM((8, SD), F32),
                pltpu.SemaphoreType.DMA((5,)),
            ],
        ),
        out_shape=[
            jax.ShapeDtypeStruct((short_tiles * TILE, D), BF16),
            jax.ShapeDtypeStruct((long_tiles * TILE, D), BF16),
            jax.ShapeDtypeStruct(logit_cots[0].shape, F32),
            jax.ShapeDtypeStruct(logit_cots[1].shape, F32),
            jax.ShapeDtypeStruct((D, total), BF16),
            jax.ShapeDtypeStruct((total, FF), BF16),
            jax.ShapeDtypeStruct((total, FF), BF16),
            jax.ShapeDtypeStruct((D, total), BF16),
            jax.ShapeDtypeStruct((total, D), BF16),
            jax.ShapeDtypeStruct((total, D), BF16),
            jax.ShapeDtypeStruct((total, D), F32),
        ]
        + [jax.ShapeDtypeStruct(shape, F32) for shape in grad_shapes],
        compiler_params=pltpu.CompilerParams(vmem_limit_bytes=62 * MIB),
        cost_estimate=pl.CostEstimate(
            flops=total * (8 * D * FF + 4 * D * D), bytes_accessed=70 * MIB, transcendentals=total * FF
        ),
        name="feed",
    )(len_short, len_long, block_slot, x, context, cot_short, cot_long, *logit_cots, *small, blocks)


class Place:
    def __init__(self):
        self.quarter = lax.axis_index("dp")
        self.shard = lax.axis_index("fsdp")
        x = self.quarter % 2
        y = self.quarter // 2
        self.core = self.shard % 2
        self.z = self.shard // 2
        self.high = self.z // 2
        self.by_x = 2 * y + 1 - x
        self.by_y = 2 * (1 - y) + x
        self.across = 2 * (1 - y) + 1 - x
        self.sibling = (self.quarter, 2 * self.z + 1 - self.core)
        self.next_x = (self.by_x, self.shard)
        self.next_y = (self.by_y, self.shard)
        self.inner = (self.z > 0) & (self.z < 3)

    def at_z(self, z):
        return (self.quarter, 2 * z + self.core)


def transfer(source, target, send_sem, recv_sem, device):
    return pltpu.make_async_remote_copy(
        src_ref=source,
        dst_ref=target,
        send_sem=send_sem,
        recv_sem=recv_sem,
        device_id=device,
        device_id_type=pl.DeviceIdType.MESH,
    )


def greet(place, extra=()):
    barrier = pltpu.get_barrier_semaphore()

    def signal(device):
        pl.semaphore_signal(barrier, inc=1, device_id=device, device_id_type=pl.DeviceIdType.MESH)

    near = (place.sibling, place.next_x, place.next_y) + tuple(extra)
    for device in near:
        signal(device)

    @pl.when(place.z > 0)
    def _():
        signal(place.at_z(place.z - 1))

    @pl.when(place.z < 3)
    def _():
        signal(place.at_z(place.z + 1))

    pl.semaphore_wait(barrier, len(near) + 1 + (place.z + 1) // 2 % 2)


CUTS = 2
GATHER_SEMAPHORES = [
    pltpu.SemaphoreType.DMA((2 * CUTS,)),
    pltpu.SemaphoreType.DMA((3 * CUTS,)),
    pltpu.SemaphoreType.DMA((4 * CUTS,)),
    pltpu.SemaphoreType.DMA((12 * CUTS,)),
    pltpu.SemaphoreType.DMA((12 * CUTS,)),
    pltpu.SemaphoreType.DMA((1 + 18 * CUTS,)),
    pltpu.SemaphoreType.DMA((1 + 18 * CUTS,)),
    pltpu.SemaphoreType.DMA((8,)),
    pltpu.SemaphoreType.DMA((2 * CUTS,)),
    pltpu.SemaphoreType.DMA((3 * CUTS,)),
    pltpu.SemaphoreType.DMA((4 * CUTS,)),
]


class Gather:
    def __init__(self, full, out, sems):
        self.place = place = Place()
        self.full, self.out = full, out
        (
            self.own_send,
            self.relay_send,
            self.z_recv,
            self.xy_send,
            self.xy_recv,
            self.core_send,
            self.core_recv,
            self.out_sems,
            self.own_more,
            self.relay_more,
            self.z_more,
        ) = sems
        self.quarter = full.shape[1] // 4
        self.cut = self.quarter // CUTS
        self.z_part = self.cut // 64 * 16
        self.first_part = ((self.cut - self.z_part) // 16 + 1) // 2 * 16
        self.last_part = self.cut - self.z_part - self.first_part
        z = place.z
        self.origins = (z + 1 - 2 * (z % 2), 2 - place.high, 3 * (1 - place.high))
        self.relays = (3 - z, 3 * (z - 1), 3 * (z - 1))

    def region(self, which, start, size):
        return self.full.at[which, pl.ds(pl.multiple_of(start, 16), size)]

    def pieces(self, which, turn):
        place, quarter, cut, part = self.place, self.quarter, self.cut, self.first_part
        skip = turn % CUTS * cut
        return (
            self.region(which, place.quarter * quarter + skip, cut),
            self.region(which, place.by_x * quarter + skip, cut),
            self.region(which, place.by_y * quarter + skip, cut),
            self.region(which, place.across * quarter + skip, part),
            self.region(which, place.across * quarter + skip + part, self.last_part),
            self.region(which, place.across * quarter + skip + cut - self.z_part, self.z_part),
        )

    def own_copy(self, side, cut, more=False):
        place = self.place
        mine = self.pieces(place.shard, cut)[5 if more else 0]
        device = place.at_z(place.z - 1 + 2 * side)
        send, recv = (self.own_more, self.z_more) if more else (self.own_send, self.z_recv)
        return transfer(
            mine, mine, send.at[side * CUTS + cut], recv.at[place.z * CUTS + cut], device
        )

    def core_copy(self, index, ref):
        return transfer(ref, ref, self.core_send.at[index], self.core_recv.at[index], self.place.sibling)

    def xy_copy(self, index, ref, device):
        return transfer(ref, ref, self.xy_send.at[index], self.xy_recv.at[index], device)

    def store(self, index, which):
        return pltpu.make_async_copy(self.full.at[which], self.out.at[which], self.out_sems.at[index])

    def mirrored(self, step):
        return 2 * self.origins[step] + 1 - self.place.core

    def held(self, step):
        return 2 * self.origins[step] + self.place.core

    def start(self):
        place = self.place
        greet(place)
        for cut in range(CUTS):

            for more in (False, True):

                @pl.when(place.z > 0)
                def _():
                    self.own_copy(0, cut, more).start()

                @pl.when(place.z < 3)
                def _():
                    self.own_copy(1, cut, more).start()

        self.core_copy(0, self.full.at[place.shard]).start()
        self.store(0, place.shard).start()

    def relay(self, turn, more=False):
        step = turn // CUTS
        piece = self.pieces(self.held(step), turn)[5 if more else 0]
        device = self.place.at_z(self.relays[step])
        send, recv = (self.relay_more, self.z_more) if more else (self.relay_send, self.z_recv)
        sem = recv.at[self.origins[step] * CUTS + turn % CUTS]
        return transfer(piece, piece, send.at[turn], sem, device)

    def along_z(self, turn):
        place = self.place
        self.relay(turn).wait_recv()

        @pl.when(place.inner)
        def _():
            self.relay(turn).start()

        pieces = self.pieces(self.held(turn // CUTS), turn)
        self.xy_copy(4 * turn, pieces[0], place.next_x).start()
        self.xy_copy(4 * turn + 1, pieces[0], place.next_y).start()
        self.core_copy(1 + 6 * turn, pieces[0]).start()
        self.relay(turn, True).wait_recv()

        @pl.when(place.inner)
        def _():
            self.relay(turn, True).start()

        self.core_copy(6 + 6 * turn, pieces[5]).start()

    def along_xy(self, turn):
        place, part = self.place, self.first_part
        _, by_x, by_y, *_ = self.pieces(self.held(turn // CUTS), turn)
        self.xy_copy(4 * turn, by_x, place.next_x).wait_recv()
        self.xy_copy(4 * turn + 2, by_x.at[pl.ds(0, part)], place.next_y).start()
        self.core_copy(2 + 6 * turn, by_x).start()
        self.xy_copy(4 * turn + 1, by_y, place.next_y).wait_recv()
        self.xy_copy(4 * turn + 3, by_y.at[pl.ds(part, self.last_part)], place.next_x).start()
        self.core_copy(3 + 6 * turn, by_y).start()

    def across(self, turn):
        place = self.place
        step = turn // CUTS
        _, _, _, first, last, _ = self.pieces(self.held(step), turn)
        self.xy_copy(4 * turn + 2, first, place.next_y).wait_recv()
        self.core_copy(4 + 6 * turn, first).start()
        self.xy_copy(4 * turn + 3, last, place.next_x).wait_recv()
        self.core_copy(5 + 6 * turn, last).start()
        if turn % CUTS == CUTS - 1:
            self.store(2 + 2 * step, self.held(step)).start()

    def core_own(self):
        which = 2 * self.place.z + 1 - self.place.core
        self.core_copy(0, self.full.at[which]).wait_recv()
        self.store(1, which).start()

    def core(self, step):
        which = self.mirrored(step)
        for turn in range(step * CUTS, (step + 1) * CUTS):
            for index, ref in enumerate(self.pieces(which, turn)):
                self.core_copy(1 + 6 * turn + index, ref).wait_recv()
        self.store(3 + 2 * step, which).start()

    def finish(self):
        place = self.place
        for cut in range(CUTS):

            for more in (False, True):

                @pl.when(place.z > 0)
                def _():
                    self.own_copy(0, cut, more).wait_send()

                @pl.when(place.z < 3)
                def _():
                    self.own_copy(1, cut, more).wait_send()

        self.core_copy(0, self.full.at[place.shard]).wait_send()
        self.store(0, place.shard).wait()
        self.store(1, 2 * place.z + 1 - place.core).wait()
        for turn in range(3 * CUTS):

            @pl.when(place.inner)
            def _():
                self.relay(turn).wait_send()
                self.relay(turn, True).wait_send()

            pieces = self.pieces(self.held(turn // CUTS), turn)
            self.xy_copy(4 * turn, pieces[0], place.next_x).wait_send()
            self.xy_copy(4 * turn + 1, pieces[0], place.next_y).wait_send()
            self.xy_copy(4 * turn + 2, pieces[3], place.next_y).wait_send()
            self.xy_copy(4 * turn + 3, pieces[4], place.next_x).wait_send()
            for index, ref in enumerate(pieces):
                self.core_copy(1 + 6 * turn + index, ref).wait_send()
        for step in range(3):
            self.store(2 + 2 * step, self.held(step)).wait()
            self.store(3 + 2 * step, self.mirrored(step)).wait()


def gather_kernel(master_ref, out_ref, full, *sems):
    gather = Gather(full, out_ref, sems)
    full[gather.place.shard] = master_ref[...].astype(BF16)
    gather.start()
    turns = 3 * CUTS
    for turn in range(turns + 2):
        if turn < turns:
            gather.along_z(turn)
        if 1 <= turn <= turns:
            gather.along_xy(turn - 1)
        if turn >= 2:
            gather.across(turn - 2)
        if turn == 2:
            gather.core_own()
        if turn >= 4 and turn % CUTS == 0:
            gather.core(turn // CUTS - 2)
    gather.core(2)
    gather.finish()


def gather_shards(master):
    rows = master.shape[0] * BLK
    shards = lax.axis_size("fsdp")
    return pl.pallas_call(
        gather_kernel,
        in_specs=[pl.BlockSpec(memory_space=pltpu.VMEM)],
        out_specs=pl.BlockSpec(memory_space=pltpu.HBM),
        out_shape=jax.ShapeDtypeStruct((shards, rows, BLK), BF16),
        scratch_shapes=[pltpu.VMEM((shards, rows, BLK), BF16)] + GATHER_SEMAPHORES,
        compiler_params=pltpu.CompilerParams(
            collective_id=0, has_side_effects=True, vmem_limit_bytes=60 * MIB
        ),
        cost_estimate=pl.CostEstimate(flops=0, bytes_accessed=200 * MIB, transcendentals=0),
        name="gather",
    )(master.reshape(rows, BLK)).reshape(-1, BLK, BLK)


def add_rows(target, former, latter, rows, step):
    @pl.loop(0, rows // step)
    def _(index):
        part = pl.ds(pl.multiple_of(index * step, 16), step)
        target[part] = (former[part].astype(F32) + latter[part].astype(F32)).astype(BF16)


def reduce_scratch(rows):
    quarter = rows // 4
    half = quarter // 2
    return [
        pltpu.VMEM((4, rows, BLK), BF16),
        pltpu.VMEM((4, rows, BLK), BF16),
        pltpu.VMEM((4, 2, half, BLK), BF16),
        pltpu.VMEM((4, 2, half, BLK), BF16),
        pltpu.VMEM((4, half, BLK), BF16),
        pltpu.VMEM((4, half, BLK), BF16),
        pltpu.VMEM((5, quarter, BLK), BF16),
        pltpu.VMEM((rows, BLK), BF16),
        pltpu.SemaphoreType.DMA((4,)),
        pltpu.SemaphoreType.DMA((4,)),
        pltpu.SemaphoreType.DMA((4,)),
        pltpu.SemaphoreType.DMA((24,)),
        pltpu.SemaphoreType.DMA((24,)),
        pltpu.SemaphoreType.DMA((3,)),
        pltpu.SemaphoreType.DMA((5,)),
        pltpu.SemaphoreType.DMA((4,)),
        pltpu.SemaphoreType.DMA((4,)),
    ]


class Reduce:
    def __init__(self, terms, base, out, scratch):
        self.place = place = Place()
        self.terms, self.base, self.out = terms, base, out
        (
            self.mine,
            self.sib,
            self.from_x,
            self.from_y,
            self.late_y,
            self.late_x,
            self.from_z,
            self.result,
            self.load_sems,
            self.core_send,
            self.core_recv,
            self.xy_send,
            self.xy_recv,
            self.z_send,
            self.z_recv,
            self.last_send,
            self.last_recv,
        ) = scratch
        self.quarter = out.shape[0] // 4
        self.half = self.quarter // 2
        z, high = place.z, place.high
        low = 1 - high
        self.order = (3 * low, low * (2 - 2 * z) + high * (7 - 2 * z), 1 + z % 2, z)
        self.onward = (z + 1 - 2 * high, z + 1 - 2 * (z % 2), z + 1 - 2 * high)
        self.closing = (0, (z % 2) * low, high)
        self.far = place.at_z(z + 2 - 4 * high)
        self.near = place.at_z(z + 1 - 2 * (z % 2))

    def shard_terms(self, shard):
        rows = self.out.shape[0]
        return self.terms.at[pl.ds(pl.multiple_of(self.base + shard * rows, 16), rows)]

    def load(self, step):
        source = self.shard_terms(2 * self.order[step] + self.place.core)
        return pltpu.make_async_copy(source, self.mine.at[step], self.load_sems.at[step])

    def core_copy(self, step):
        return transfer(
            self.shard_terms(2 * self.order[step] + 1 - self.place.core),
            self.sib.at[step],
            self.core_send.at[step],
            self.core_recv.at[step],
            self.place.sibling,
        )

    def part(self, step, which, side):
        start = pl.multiple_of(which * self.quarter + side * self.half, 16)
        return self.mine.at[step, pl.ds(start, self.half)]

    def xy_copy(self, step, index):
        place = self.place
        source, target, device = (
            (self.part(step, place.by_x, 0), self.from_x.at[step, 0], place.next_x),
            (self.part(step, place.across, 0), self.from_x.at[step, 1], place.next_x),
            (self.part(step, place.by_y, 1), self.from_y.at[step, 0], place.next_y),
            (self.part(step, place.across, 1), self.from_y.at[step, 1], place.next_y),
            (self.part(step, place.by_y, 0), self.late_y.at[step], place.next_y),
            (self.part(step, place.by_x, 1), self.late_x.at[step], place.next_x),
        )[index]
        place = 6 * step + index
        return transfer(source, target, self.xy_send.at[place], self.xy_recv.at[place], device)

    def start(self):
        greet(self.place, (self.far,))
        for step in range(2):
            self.core_copy(step).start()
        for step in range(4):
            self.load(step).start()

    def core(self, step):
        place, quarter = self.place, self.quarter
        self.load(step).wait()
        self.core_copy(step).wait_recv()
        if step < 2:
            self.core_copy(step + 2).start()

        def add(which):
            block = pl.ds(pl.multiple_of(which * quarter, 16), quarter)
            mine = self.mine.at[step, block]
            add_rows(mine, mine, self.sib.at[step, block], quarter, self.half)

        add(place.by_x)
        add(place.across)
        self.xy_copy(step, 0).start()
        self.xy_copy(step, 1).start()
        add(place.by_y)
        self.xy_copy(step, 2).start()
        self.xy_copy(step, 3).start()
        add(place.quarter)

    def take(self, step, which, side, index, source):
        self.xy_copy(step, index).wait_recv()
        target = self.part(step, which, side)
        add_rows(target, target, source, self.half, self.half)

    def first(self, step):
        place = self.place
        self.take(step, place.by_y, 0, 1, self.from_x.at[step, 1])
        self.xy_copy(step, 4).start()
        self.take(step, place.by_x, 1, 3, self.from_y.at[step, 1])
        self.xy_copy(step, 5).start()
        self.take(step, place.quarter, 0, 0, self.from_x.at[step, 0])
        self.take(step, place.quarter, 1, 2, self.from_y.at[step, 0])

    def own_block(self, step):
        return self.mine.at[step, pl.ds(pl.multiple_of(self.place.quarter * self.quarter, 16), self.quarter)]

    def z_copy(self, step):
        goal = self.order[step]
        slot = goal + self.closing[step] * (4 - goal)
        return transfer(
            self.own_block(step),
            self.from_z.at[slot],
            self.z_send.at[step],
            self.z_recv.at[slot],
            self.place.at_z(self.onward[step]),
        )

    def take_z(self, step, slot):
        source = self.from_z.at[slot]
        transfer(source, source, self.z_send.at[0], self.z_recv.at[slot], self.near).wait_recv()
        block = self.own_block(step)
        add_rows(block, block, source, self.quarter, self.half)

    def second(self, step):
        place = self.place
        self.take(step, place.quarter, 0, 4, self.late_y.at[step])
        self.take(step, place.quarter, 1, 5, self.late_x.at[step])
        if step < 3:

            @pl.when(place.inner)
            def _():
                self.take_z(step, self.order[step])

            self.z_copy(step).start()
        else:

            @pl.when(place.z > 0)
            def _():
                self.take_z(step, place.z)

            @pl.when(place.z < 3)
            def _():
                self.take_z(step, 4)

    def final(self, which, side=None):
        start = pl.multiple_of(which * self.quarter + (0 if side is None else side * self.half), 16)
        return self.result.at[pl.ds(start, self.quarter if side is None else self.half)]

    def last_copy(self, index, ref):
        device = (self.place.next_x, self.place.next_y, self.place.next_y, self.place.next_x)[index]
        return transfer(ref, ref, self.last_send.at[index], self.last_recv.at[index], device)

    def share(self):
        own = self.final(self.place.quarter)
        own[...] = self.own_block(3)[...]
        self.last_copy(0, own).start()
        self.last_copy(1, own).start()

    def share_on(self):
        place = self.place
        self.last_copy(0, self.final(place.by_x)).wait_recv()
        self.last_copy(2, self.final(place.by_x, 0)).start()
        self.last_copy(1, self.final(place.by_y)).wait_recv()
        self.last_copy(3, self.final(place.by_y, 1)).start()

    def finish(self):
        place = self.place
        self.last_copy(2, self.final(place.across, 0)).wait_recv()
        self.last_copy(3, self.final(place.across, 1)).wait_recv()
        self.out[...] = self.result[...]
        for step in range(4):
            self.core_copy(step).wait_send()
            for index in range(6):
                self.xy_copy(step, index).wait_send()
            if step < 3:
                self.z_copy(step).wait_send()
        own = self.final(place.quarter)
        self.last_copy(0, own).wait_send()
        self.last_copy(1, own).wait_send()
        self.last_copy(2, self.final(place.by_x, 0)).wait_send()
        self.last_copy(3, self.final(place.by_y, 1)).wait_send()


def reduce_kernel(*refs, base, short_steps):
    terms, small_ref, d_ref, resid_ref, w_ref, out_ref, small_out, short_ref, long_ref = refs[:9]
    small_in, small_sum, small_send, small_recv = refs[9:13]
    reduce = Reduce(terms, base, out_ref, refs[13:])
    place = reduce.place
    partners = (place.sibling, place.next_x, place.next_y, reduce.near, reduce.far)

    def small_copy(level):
        return transfer(
            small_sum.at[level],
            small_in.at[level],
            small_send.at[level],
            small_recv.at[level],
            partners[level],
        )

    def small_start():
        small_sum[0] = small_ref[...]
        small_copy(0).start()

    def small_step(level):
        small_copy(level - 1).wait_recv()
        small_sum[level] = small_sum[level - 1] + small_in[level - 1]
        if level < 5:
            small_copy(level).start()
        else:
            small_out[...] = small_sum[5]

    run_events(
        pl.program_id(0),
        (
            (reduce.start, small_start),
            (partial(reduce.core, 0), partial(small_step, 1)),
            (partial(reduce.core, 1), partial(reduce.first, 0), partial(small_step, 2)),
            (
                partial(reduce.core, 2),
                partial(reduce.first, 1),
                partial(reduce.second, 0),
                partial(small_step, 3),
            ),
            (
                partial(reduce.core, 3),
                partial(reduce.first, 2),
                partial(reduce.second, 1),
                partial(small_step, 4),
            ),
            (partial(reduce.first, 3), partial(reduce.second, 2), partial(small_step, 5)),
            (partial(reduce.second, 3), reduce.share),
            (reduce.share_on,),
        ),
    )
    input_product(d_ref, resid_ref, w_ref, short_ref, long_ref, short_steps)

    @pl.when(pl.program_id(0) == pl.num_programs(0) - 1)
    def _():
        reduce.finish()
        for level in range(5):
            small_copy(level).wait_send()


def reduce_late(terms, base, rows, small, d_qkv, resid, w_qkv, short_tiles):
    steps = resid.shape[0] // INPUT_ROWS
    short_steps = short_tiles * TILE // INPUT_ROWS
    in_specs, out_specs = input_specs(short_steps)

    def whole(shape):
        return pl.BlockSpec(shape, lambda step: (0, 0), pipeline_mode=pl.Buffered(1))

    return pl.pallas_call(
        partial(reduce_kernel, base=base, short_steps=short_steps),
        grid=(steps,),
        in_specs=[pl.BlockSpec(memory_space=pltpu.HBM), whole(small.shape)] + in_specs,
        out_specs=[
            pl.BlockSpec((rows, BLK), lambda step: (0, 0)),
            pl.BlockSpec(small.shape, lambda step: (0, 0)),
        ]
        + out_specs,
        out_shape=[
            jax.ShapeDtypeStruct((rows, BLK), BF16),
            jax.ShapeDtypeStruct((SMALL_ROWS, BLK), F32),
            jax.ShapeDtypeStruct((short_steps * INPUT_ROWS, D), F32),
            jax.ShapeDtypeStruct(((steps - short_steps) * INPUT_ROWS, D), F32),
        ],
        scratch_shapes=[
            pltpu.VMEM((5, SMALL_ROWS, BLK), F32),
            pltpu.VMEM((6, SMALL_ROWS, BLK), F32),
            pltpu.SemaphoreType.DMA((5,)),
            pltpu.SemaphoreType.DMA((5,)),
        ]
        + reduce_scratch(rows),
        compiler_params=pltpu.CompilerParams(
            collective_id=3, has_side_effects=True, vmem_limit_bytes=60 * MIB
        ),
        cost_estimate=pl.CostEstimate(flops=0, bytes_accessed=200 * MIB, transcendentals=0),
        name="reduce",
    )(terms, small, d_qkv, resid, w_qkv)


def count_where(condition, axis):
    return jnp.sum(condition.astype(jnp.int32), axis=axis)


def slot_codes(slots, qkv_slots, slot_count, shards):
    early = slot_count - LATE
    shard = slots // slot_count
    begin = shard * slot_count
    inside = (qkv_slots[None, :] >= begin[:, None]) & (qkv_slots[None, :] < (begin + slot_count)[:, None])
    own = count_where(qkv_slots[None, :] == slots[:, None], 1)
    before = count_where(inside & (qkv_slots[None, :] < slots[:, None]), 1)
    number = count_where(inside, 1)
    position = jnp.where(own > 0, slot_count - number + before, slots - begin - before)
    code = jnp.where(
        position < early,
        shard * early + position,
        shards * early + shard * LATE + position - early,
    )
    return code, position, jnp.max(number)


def update_kernel(
    position_ref,
    held_ref,
    early,
    late,
    master,
    left_stat,
    right_stat,
    left_root,
    right_root,
    slot_grad,
    new_left,
    new_right,
    new_master,
):
    count = master.shape[0]
    first = pl.program_id(0) * count
    split = early.shape[0] // BLK

    def block(ref, place):
        return ref[pl.ds(pl.multiple_of(place * BLK, BLK), BLK)]

    def grad_of(index):
        place = position_ref[first + index]
        grad = jnp.where(
            place < split,
            block(early, jnp.minimum(place, split - 1)),
            block(late, jnp.maximum(place - split, 0)),
        )
        return jnp.where(held_ref[first + index] > 0, grad, jnp.zeros_like(grad))

    for begin in range(0, count, 4):
        some = range(begin, min(begin + 4, count))
        grads = [grad_of(index) for index in some]
        applied = [product(left_root[index].astype(BF16), grad) for index, grad in zip(some, grads)]
        outer_left = [right_product(grad, grad) for grad in grads]
        outer_right = [left_product(grad, grad) for grad in grads]
        totals = [
            product(part.astype(BF16), right_root[index].astype(BF16)) for index, part in zip(some, applied)
        ]
        for place, index in enumerate(some):
            slot_grad[index] = grads[place].astype(F32)
            new_left[index] = STAT_DECAY * left_stat[index] + (1.0 - STAT_DECAY) * outer_left[place]
            new_right[index] = STAT_DECAY * right_stat[index] + (1.0 - STAT_DECAY) * outer_right[place]
            new_master[index] = master[index] - MATRIX_RATE * totals[place]


def update(position, held, early, late, master, left_stat, right_stat, left_root, right_root):
    slot_count = master.shape[0]
    group = max(size for size in range(1, 12) if slot_count % size == 0)
    some = pl.BlockSpec((group, BLK, BLK), lambda step, *_: (step, 0, 0))

    def whole(shape):
        return pl.BlockSpec(shape, lambda step, *_: (0, 0), pipeline_mode=pl.Buffered(1))

    return pl.pallas_call(
        update_kernel,
        grid_spec=pltpu.PrefetchScalarGridSpec(
            num_scalar_prefetch=2,
            grid=(slot_count // group,),
            in_specs=[whole(early.shape), whole(late.shape)] + [some] * 5,
            out_specs=[some] * 4,
        ),
        out_shape=[jax.ShapeDtypeStruct(master.shape, F32)] * 4,
        compiler_params=pltpu.CompilerParams(vmem_limit_bytes=60 * MIB),
        cost_estimate=pl.CostEstimate(
            flops=8 * slot_count * BLK**3, bytes_accessed=36 * slot_count * BLK**2, transcendentals=0
        ),
        name="update",
    )(position, held, early, late, master, left_stat, right_stat, left_root, right_root)


def body(
    x_short,
    x_long,
    cot_short,
    cot_long,
    logit_cot_short,
    logit_cot_long,
    len_short,
    len_long,
    block_slot,
    master,
    left_stat,
    right_stat,
    left_root,
    right_root,
    small_params,
    small_first,
    small_second,
    own_transfers,
):
    slot_count = master.shape[0]
    shards = lax.axis_size("fsdp")
    all_slots = slot_count * shards
    short_seqs, width = x_short.shape[:2]
    long_seqs = x_long.shape[0]
    short_tiles = short_seqs * width // TILE
    per_tile = TILE // width

    own = jnp.arange(slot_count, dtype=jnp.int32) + slot_count * lax.axis_index("fsdp")
    held = jnp.any(block_slot[None, :] == own[:, None], axis=1).astype(jnp.int32)
    if own_transfers:
        early_count = slot_count - LATE
        code, position, most = slot_codes(
            jnp.concatenate([block_slot, own]), block_slot[: 3 * 36], slot_count, shards
        )
        position = position[NBLK:]
        code = code[:NBLK]
        fits = most <= LATE
        gathered = gather_shards(master)
    else:
        gathered = lax.all_gather(master.astype(BF16), "fsdp", axis=0, tiled=True)
    w_qkv = assemble(block_slot, gathered)
    pieces = unpack(small_params)
    params = jnp.pad(small_params, (0, SMALL_ROWS * BLK - small_params.shape[0])).reshape(SMALL_ROWS, BLK)
    w_class = pieces[-2].reshape(SD, NCLS)
    b_class = pieces[-1].reshape(1, NCLS)
    x, *qkv, context, probs_short, probs_long = attention(
        len_short,
        len_long,
        x_short.reshape(-1, D),
        x_long.reshape(-1, D),
        params,
        w_qkv,
        short_tiles,
        width,
    )

    (
        enc_short,
        enc_long,
        logits_short,
        logits_long,
        first,
        active,
        d_up,
        d_down,
        d_branch,
        d_context,
        d_resid,
        g_student,
        g_hidden,
        g_small,
    ) = feed(
        len_short,
        len_long,
        block_slot,
        x,
        context,
        cot_short.reshape(-1, D),
        cot_long.reshape(-1, D),
        (logit_cot_short, logit_cot_long),
        (params, w_class, b_class),
        gathered,
        short_tiles,
        width,
    )
    g_out = left_product(context, d_branch).astype(BF16)
    others = (g_out, g_student.astype(BF16), g_hidden.astype(BF16))
    if own_transfers:
        terms = feed_grads(code, first, d_down, active, d_up, others, all_slots)
        *back, early_reduced = attention_back(
            qkv,
            probs_short,
            probs_long,
            d_context,
            x,
            short_tiles,
            terms.reshape(-1, BLK),
            early_count * BLK,
        )
    else:
        back = attention_back(qkv, probs_short, probs_long, d_context, x, short_tiles)
    d_qkv, g_b_query, g_b_value, x_turned = back

    def reduce_all():
        slot_terms = feed_grads(block_slot, first, d_down, active, d_up, others, all_slots)
        slot_terms, small_terms = input_weights(
            block_slot, x_turned, d_qkv, g_small, g_b_query, g_b_value, slot_terms
        )
        reduced = lax.psum_scatter(slot_terms, "fsdp", scatter_dimension=0, tiled=True)
        return lax.psum(reduced, "dp").reshape(-1, BLK), small_terms

    def renew(places, early, late):
        return update(
            places, held, early, late, master, left_stat, right_stat, left_root, right_root
        )

    def renew_all(blocks):
        return renew(jnp.arange(slot_count, dtype=jnp.int32), blocks, blocks)

    if own_transfers:
        terms, small_terms = input_weights(code, x_turned, d_qkv, g_small, g_b_query, g_b_value, terms)
        late_reduced, small_total, in_short, in_long = reduce_late(
            terms.reshape(-1, BLK),
            shards * early_count * BLK,
            LATE * BLK,
            small_terms,
            d_qkv,
            d_resid,
            w_qkv,
            short_tiles,
        )

        updated = lax.cond(
            fits,
            lambda: renew(position, early_reduced, late_reduced),
            lambda: renew_all(reduce_all()[0]),
        )
    else:
        in_short, in_long = input_grads(d_qkv, d_resid, w_qkv, short_tiles)
        blocks, small_terms = reduce_all()
        updated = renew_all(blocks)
        small_total = lax.psum(small_terms, ("dp", "fsdp"))
    slot_grad, new_left, new_right, new_master = updated
    small_grad = jnp.concatenate(
        [
            small_total[:CLASS_ROW].reshape(-1),
            small_total[CLASS_ROW : CLASS_ROW + NCLS].T.reshape(-1),
            small_total[LAST_ROW, :NCLS],
        ]
    )
    new_first = BETA_ONE * small_first + (1.0 - BETA_ONE) * small_grad
    new_second = BETA_TWO * small_second + (1.0 - BETA_TWO) * small_grad * small_grad
    first_hat = new_first / (1.0 - BETA_ONE**STEP)
    second_hat = new_second / (1.0 - BETA_TWO**STEP)
    new_small = small_params - ADAM_RATE * first_hat / (jnp.sqrt(second_hat) + ADAM_EPSILON)
    return (
        enc_short.reshape(x_short.shape),
        logits_short,
        enc_long.reshape(x_long.shape),
        logits_long,
        in_short.reshape(x_short.shape),
        in_long.reshape(x_long.shape),
        slot_grad,
        new_left,
        new_right,
        new_master,
        new_first,
        new_second,
        new_small,
    )


def solution(mesh):
    both = ("dp", "fsdp")
    placed = (
        P(both, None, None),
        P(both, None, None),
        P(both, None, None),
        P(both, None, None),
        P(both, None),
        P(both, None),
        P(both),
        P(both),
        P(),
        P("fsdp", None, None),
        P("fsdp", None, None),
        P("fsdp", None, None),
        P("fsdp", None, None),
        P("fsdp", None, None),
        P(),
        P(),
        P(),
    )
    return jax.shard_map(
        partial(body, own_transfers=(mesh.shape["dp"], mesh.shape["fsdp"]) == (4, 8)),
        mesh=mesh,
        in_specs=placed,
        out_specs=(
            P(both, None, None),
            P(both, None),
            P(both, None, None),
            P(both, None),
            P(both, None, None),
            P(both, None, None),
            P("fsdp", None, None),
            P("fsdp", None, None),
            P("fsdp", None, None),
            P("fsdp", None, None),
            P(),
            P(),
            P(),
        ),
        check_vma=False,
    )
```

```python
from functools import partial

import jax
import jax.numpy as jnp
from jax import lax
from jax.experimental import pallas as pl
from jax.experimental.pallas import tpu as pltpu
from jax.sharding import PartitionSpec as P

D = 768
HEADS = 12
FF = 3072
SD = 128
PH = 2
NCLS = 14
BLK = 128
STEP = 10
NBLK = 439
TILE = 512
PAIRS = 3
GROUPS = 2
CHUNK = 1024
LATE = 24

NORM_EPSILON = 1e-12
BETA_ONE = 0.9
BETA_TWO = 0.999
ADAM_EPSILON = 1e-08
ADAM_RATE = 0.1
MATRIX_RATE = 0.2
STAT_DECAY = 0.5
MASKED_SCORE = -1e30
HIGHEST_PRECISION = lax.Precision.HIGHEST
MIB = 1024 * 1024
F32 = jnp.float32
BF16 = jnp.bfloat16

def product(former, latter, precision=None):
    return jnp.dot(former, latter, preferred_element_type=F32, precision=precision)


def left_product(former, latter, precision=None):
    return lax.dot_general(
        former, latter, (((0,), (0,)), ((), ())), preferred_element_type=F32, precision=precision
    )


def right_product(former, latter, precision=None):
    return lax.dot_general(
        former, latter, (((1,), (1,)), ((), ())), preferred_element_type=F32, precision=precision
    )


def unpack(small_values):
    widths = (D, D, D, D, D, FF, D, D, D, SD, SD, SD, SD * NCLS, NCLS)
    pieces = []
    offset = 0
    for column_count in widths:
        pieces.append(small_values[offset : offset + column_count])
        offset += column_count
    return pieces


def each_block(first, row_count, col_count, action):
    def one_row(index, carry):
        row = pl.multiple_of(index * BLK, BLK)
        for col in range(col_count):
            action(first + index * col_count + col, row, col * BLK)
        return carry

    lax.fori_loop(0, row_count, one_row, 0)


def load_blocks(slot_ref, blocks, target, sem, first, row_count, col_count, col_start=0):
    def move(block, row, col):
        pltpu.make_async_copy(
            blocks.at[slot_ref[block]],
            target.at[pl.ds(row, BLK), pl.ds(col + col_start * BLK, BLK)],
            sem,
        ).start()

    each_block(first, row_count, col_count, move)


def wait_whole(target, sem):
    pltpu.make_async_copy(target, target, sem).wait()


def assemble_kernel(slot_ref, blocks, out, sem):
    for which in range(3):
        load_blocks(slot_ref, blocks, out, sem, 36 * which, 6, 6, 6 * which)
    wait_whole(out, sem)


def assemble(block_slot, blocks):
    return pl.pallas_call(
        assemble_kernel,
        grid_spec=pltpu.PrefetchScalarGridSpec(
            num_scalar_prefetch=1,
            grid=(1,),
            in_specs=[pl.BlockSpec(memory_space=pltpu.HBM)],
            out_specs=pl.BlockSpec(memory_space=pltpu.VMEM),
            scratch_shapes=[pltpu.SemaphoreType.DMA],
        ),
        out_shape=jax.ShapeDtypeStruct((D, 3 * D), BF16),
        compiler_params=pltpu.CompilerParams(vmem_limit_bytes=60 * MIB),
        name="assemble",
    )(block_slot, blocks)


def join_small(small_ref, query_ref, value_ref, small_out):
    small_out[...] = small_ref[...]
    for start, ref in ((0, query_ref), (D // BLK, value_ref)):
        for index in range(D // BLK):
            small_out[start + index : start + index + 1, :] = ref[:, index * BLK : (index + 1) * BLK]


PART = 512
ACROSS = PART // BLK


def feed_grads_kernel(
    code_ref,
    first_turned,
    down_turned,
    active_ref,
    d_up_ref,
    g_out,
    g_student,
    g_hidden,
    terms,
    up_stage,
    down_stage,
    up_sems,
    down_sems,
    other_sems,
):
    step = pl.program_id(0)
    last = pl.num_programs(0) - 1
    slot = step % 2
    others = ((g_out, 108, 6, 6), (g_student, 432, 6, 1), (g_hidden, 438, 1, 1))

    @pl.when(step == 0)
    def _():
        for which, (grad, first, row_count, col_count) in enumerate(others):

            def move(block, row, col, which=which, grad=grad):
                pltpu.make_async_copy(
                    grad.at[pl.ds(row, BLK), pl.ds(col, BLK)], terms.at[code_ref[block]], other_sems.at[which]
                ).start()

            each_block(first, row_count, col_count, move)

    @pl.when(step >= 2)
    def _():
        wait_whole(up_stage.at[slot], up_sems.at[slot])
        wait_whole(down_stage.at[slot], down_sems.at[slot])

    up_stage[slot] = product(first_turned[...], d_up_ref[...]).astype(BF16)
    down_stage[slot] = product(down_turned[...], active_ref[...]).T.astype(BF16)
    for row in range(D // BLK):
        for col in range(ACROSS):
            pltpu.make_async_copy(
                up_stage.at[slot, pl.ds(row * BLK, BLK), pl.ds(col * BLK, BLK)],
                terms.at[code_ref[144 + row * (FF // BLK) + step * ACROSS + col]],
                up_sems.at[slot],
            ).start()
            pltpu.make_async_copy(
                down_stage.at[slot, pl.ds(col * BLK, BLK), pl.ds(row * BLK, BLK)],
                terms.at[code_ref[288 + (step * ACROSS + col) * (D // BLK) + row]],
                down_sems.at[slot],
            ).start()

    @pl.when(step == last)
    def _():
        for place in range(2):
            wait_whole(up_stage.at[place], up_sems.at[place])
            wait_whole(down_stage.at[place], down_sems.at[place])
        for which, (grad, *_) in enumerate(others):
            wait_whole(grad, other_sems.at[which])


def feed_grads(code, first, d_down, active, d_up, others, slot_count):
    tokens = first.shape[1]

    def whole(shape):
        return pl.BlockSpec(shape, lambda step, *_: (0, 0), pipeline_mode=pl.Buffered(1))

    part = pl.BlockSpec((tokens, PART), lambda step, *_: (0, step))
    return pl.pallas_call(
        feed_grads_kernel,
        grid_spec=pltpu.PrefetchScalarGridSpec(
            num_scalar_prefetch=1,
            grid=(FF // PART,),
            in_specs=[whole(first.shape), whole(d_down.shape), part, part]
            + [whole(other.shape) for other in others],
            out_specs=pl.BlockSpec(memory_space=pltpu.HBM),
            scratch_shapes=[
                pltpu.VMEM((2, D, PART), BF16),
                pltpu.VMEM((2, PART, D), BF16),
                pltpu.SemaphoreType.DMA((2,)),
                pltpu.SemaphoreType.DMA((2,)),
                pltpu.SemaphoreType.DMA((3,)),
            ],
        ),
        out_shape=jax.ShapeDtypeStruct((slot_count, BLK, BLK), BF16),
        compiler_params=pltpu.CompilerParams(vmem_limit_bytes=60 * MIB),
        cost_estimate=pl.CostEstimate(
            flops=4 * tokens * D * FF, bytes_accessed=50 * MIB, transcendentals=0
        ),
        name="feed_grads",
    )(code, first, d_down, active, d_up, *others)


def input_weights_kernel(
    code_ref, turned, d_ref, small_ref, query_ref, value_ref, _, terms, small_out, stage, sems
):
    step = pl.program_id(0)
    slot = step % 2

    @pl.when(step == 0)
    def _():
        join_small(small_ref, query_ref, value_ref, small_out)

    @pl.when(step >= 2)
    def _():
        wait_whole(stage.at[slot], sems.at[slot])

    stage[slot] = product(turned[...], d_ref[...]).astype(BF16)
    for row in range(D // BLK):
        for col in range(D // BLK):
            pltpu.make_async_copy(
                stage.at[slot, pl.ds(row * BLK, BLK), pl.ds(col * BLK, BLK)],
                terms.at[code_ref[36 * step + row * (D // BLK) + col]],
                sems.at[slot],
            ).start()

    @pl.when(step == pl.num_programs(0) - 1)
    def _():
        for place in range(2):
            wait_whole(stage.at[place], sems.at[place])


def input_weights(code, x, d_qkv, small, g_query, g_value, terms):
    tokens = x.shape[1]

    def whole(shape):
        return pl.BlockSpec(shape, lambda step, *_: (0, 0), pipeline_mode=pl.Buffered(1))

    hbm = pl.BlockSpec(memory_space=pltpu.HBM)
    return pl.pallas_call(
        input_weights_kernel,
        grid_spec=pltpu.PrefetchScalarGridSpec(
            num_scalar_prefetch=1,
            grid=(3,),
            in_specs=[
                whole(x.shape),
                pl.BlockSpec((tokens, D), lambda step, *_: (0, step)),
                whole(small.shape),
                whole(g_query.shape),
                whole(g_value.shape),
                hbm,
            ],
            out_specs=[hbm, pl.BlockSpec(small.shape, lambda step, *_: (0, 0))],
            scratch_shapes=[
                pltpu.VMEM((2, D, D), BF16),
                pltpu.SemaphoreType.DMA((2,)),
            ],
        ),
        out_shape=[
            jax.ShapeDtypeStruct(terms.shape, BF16),
            jax.ShapeDtypeStruct(small.shape, F32),
        ],
        input_output_aliases={6: 0},
        compiler_params=pltpu.CompilerParams(vmem_limit_bytes=60 * MIB),
        cost_estimate=pl.CostEstimate(
            flops=6 * tokens * D * D, bytes_accessed=16 * MIB, transcendentals=0
        ),
        name="input_weights",
    )(code, x, d_qkv, small, g_query, g_value, terms)


def half_masks():
    lane = lax.broadcasted_iota(jnp.int32, (1, BLK), 1)
    low = (lane < BLK // 2).astype(BF16)
    return low, (1.0 - low.astype(F32)).astype(BF16)


def stack_heads(values, low, high):
    return jnp.concatenate([values * low, values * high], axis=0)


def pick_heads(values):
    rows = values.shape[0] // 2
    lane = lax.broadcasted_iota(jnp.int32, (rows, BLK), 1)
    return jnp.where(lane < BLK // 2, values[:rows], values[rows:])


def pipelined(count, before, middle, after):
    started = before(0)
    done = None
    for index in range(count):
        current = started
        if index + 1 < count:
            started = before(index + 1)
        if done is not None:
            after(index - 1, done)
        done = middle(index, current)
    after(count - 1, done)


def softmax(scores, length):
    visible = lax.broadcasted_iota(jnp.int32, scores.shape, 1) < length
    scores = jnp.where(visible, scores, MASKED_SCORE)
    powers = jnp.exp(scores - jnp.max(scores, axis=-1, keepdims=True))
    total = jnp.sum(powers, axis=-1, keepdims=True)
    return (powers * (1.0 / total)).astype(BF16)


def attention_kernel(
    len_short,
    len_long,
    x_short_ref,
    x_long_ref,
    params,
    w_ref,
    x_ref,
    q_ref,
    k_ref,
    v_ref,
    context_ref,
    short_ref,
    long_ref,
    bias,
    *,
    short_tiles,
):
    tile = pl.program_id(0)
    group = pl.program_id(1)
    low, high = half_masks()
    width = short_ref.shape[-1]
    per_tile = TILE // width

    wide = PAIRS * BLK
    start = pl.multiple_of(group * wide, wide)

    @pl.when((tile == 0) & (group == 0))
    def _():
        for which in range(2):
            for place in range(D // BLK):
                row = which * (D // BLK) + place
                bias[which : which + 1, place * BLK : (place + 1) * BLK] = params[row : row + 1, :]

    @pl.when((tile < short_tiles) & (group == 0))
    def _():
        x_ref[...] = x_short_ref[...]

    @pl.when((tile >= short_tiles) & (group == 0))
    def _():
        x_ref[...] = x_long_ref[...]

    @pl.when(group == 0)
    def _():
        rows_in = x_ref[...]
        queries = product(rows_in, w_ref[:, :D]) + bias[0:1, :]
        q_ref[...] = (queries * 0.125).astype(BF16)
        k_ref[...] = product(rows_in, w_ref[:, D : 2 * D]).astype(BF16)
        v_ref[...] = (product(rows_in, w_ref[:, 2 * D :]) + bias[1:2, :]).astype(BF16)

    def inner(pair):
        return pl.ds(pl.multiple_of(start + pair * BLK, BLK), BLK)

    def attend(units, kept_ref):
        def scores(index):
            rows, keys, pair, _, _ = units[index]
            return right_product(stack_heads(q_ref[rows, inner(pair)], low, high), k_ref[keys, inner(pair)])

        def weigh(index, values):
            _, _, _, length, place = units[index]
            probs = softmax(values, length)
            kept_ref[place] = probs
            return probs

        def mix(index, probs):
            rows, keys, pair, _, _ = units[index]
            mixed = pick_heads(product(probs, v_ref[keys, inner(pair)])).astype(BF16)
            context_ref[rows, pair * BLK : (pair + 1) * BLK] = mixed

        pipelined(len(units), scores, weigh, mix)

    @pl.when(tile < short_tiles)
    def _():
        units = []
        for seq in range(per_tile):
            rows = slice(seq * width, (seq + 1) * width)
            length = len_short[tile * per_tile + seq]
            for pair in range(PAIRS):
                units.append((rows, rows, pair, length, (0, pair, seq)))
        attend(units, short_ref)

    @pl.when(tile >= short_tiles)
    def _():
        length = len_long[tile - short_tiles]
        half = TILE // 2
        units = []
        for pair in range(PAIRS):
            for part in range(2):
                rows = slice(part * half, (part + 1) * half)
                units.append((rows, slice(0, TILE), pair, length, (0, pair, part)))
        attend(units, long_ref)


def run_events(step, events):
    for index, actions in enumerate(events):

        @pl.when(step == index)
        def _(actions=actions):
            for action in actions:
                action()


def probs_shapes(short_tiles, long_tiles, width):
    per_tile = TILE // width
    return (
        (short_tiles, 2 * PAIRS, per_tile, 2 * width, width),
        (long_tiles, 2 * PAIRS, 2, TILE, TILE),
    )


def short_index(tile, short_tiles):
    return jnp.minimum(tile, short_tiles - 1)


def long_index(tile, short_tiles):
    return jnp.maximum(tile - short_tiles, 0)


def probs_maps(short_tiles):
    def short_map(tile, group):
        last = jnp.minimum(tile // short_tiles, 1)
        return (short_index(tile, short_tiles), group + last * (GROUPS - 1 - group), 0, 0, 0)

    def long_map(tile, group):
        begun = jnp.minimum(tile // short_tiles, 1)
        return (long_index(tile, short_tiles), begun * group, 0, 0, 0)

    return short_map, long_map


def attention(len_short, len_long, x_short, x_long, params, w_qkv, short_tiles, width):
    tiles = (x_short.shape[0] + x_long.shape[0]) // TILE
    wide = PAIRS * BLK
    short_shape, long_shape = probs_shapes(short_tiles, tiles - short_tiles, width)
    short_map, long_map = probs_maps(short_tiles)
    flops = 4 * D * TILE * TILE * tiles + 6 * D * D * TILE * tiles
    rows = pl.BlockSpec((TILE, wide), lambda tile, group: (tile, group))
    scalars = pl.BlockSpec(memory_space=pltpu.SMEM)

    def whole(shape):
        return pl.BlockSpec(shape, lambda tile, group: (0,) * len(shape), pipeline_mode=pl.Buffered(1))

    in_specs = [
        scalars,
        scalars,
        pl.BlockSpec((TILE, D), lambda tile, group: (short_index(tile, short_tiles), 0)),
        pl.BlockSpec((TILE, D), lambda tile, group: (long_index(tile, short_tiles), 0)),
        whole(params.shape),
        whole((D, 3 * D)),
    ]
    full_rows = pl.BlockSpec((TILE, D), lambda tile, group: (tile, 0))
    out_specs = [
        full_rows,
        full_rows,
        full_rows,
        full_rows,
        rows,
        pl.BlockSpec((1, PAIRS) + short_shape[2:], short_map),
        pl.BlockSpec((1, PAIRS) + long_shape[2:], long_map),
    ]
    out_shape = [jax.ShapeDtypeStruct((tiles * TILE, D), BF16)] * 5 + [
        jax.ShapeDtypeStruct(short_shape, BF16),
        jax.ShapeDtypeStruct(long_shape, BF16),
    ]
    arguments = [len_short, len_long, x_short, x_long, params, w_qkv]
    return pl.pallas_call(
        partial(attention_kernel, short_tiles=short_tiles),
        grid=(tiles, GROUPS),
        in_specs=in_specs,
        out_specs=out_specs,
        out_shape=out_shape,
        scratch_shapes=[pltpu.VMEM((8, D), F32)],
        compiler_params=pltpu.CompilerParams(vmem_limit_bytes=60 * MIB),
        cost_estimate=pl.CostEstimate(
            flops=flops, bytes_accessed=35 * MIB, transcendentals=HEADS * TILE * TILE * tiles // 2
        ),
        name="attention",
    )(*arguments)


def attention_back_kernel(*refs, short_tiles, transfers):
    q_ref, k_ref, v_ref, short_ref, long_ref, dc_ref, x_ref = refs[:7]
    refs = refs[7:]
    if transfers:
        terms_ref, refs = refs[0], refs[1:]
    out_ref, bq_ref, bv_ref, turned_ref = refs[:4]
    tile = pl.program_id(0)
    group = pl.program_id(1)
    low, high = half_masks()
    width = short_ref.shape[-1]
    per_tile = TILE // width
    if transfers:
        reduce = Reduce(terms_ref, 0, refs[4], refs[5:])
        run_events(
            tile * GROUPS + group,
            (
                (reduce.start,),
                (partial(reduce.core, 0),),
                (partial(reduce.core, 1), partial(reduce.first, 0)),
                (partial(reduce.core, 2), partial(reduce.first, 1), partial(reduce.second, 0)),
                (partial(reduce.core, 3), partial(reduce.first, 2), partial(reduce.second, 1)),
                (partial(reduce.first, 3), partial(reduce.second, 2)),
                (partial(reduce.second, 3), reduce.share),
                (reduce.share_on,),
            ),
        )

    wide = PAIRS * BLK
    start = pl.multiple_of(group * wide, wide)

    def columns(which, cols):
        return pl.ds(pl.multiple_of(which * D + start + cols.start, BLK), BLK)

    def go_back(units, kept_ref, parts):
        sums = {}

        def spread_in(index):
            rows, keys, cols, _ = units[index]
            return right_product(stack_heads(dc_ref[rows, cols], low, high), v_ref[keys, cols])

        def differ(index, d_probs):
            wide = kept_ref[units[index][3]].astype(F32)
            weighted = wide * d_probs
            return (weighted - wide * jnp.sum(weighted, axis=-1, keepdims=True)).astype(BF16)

        def gather_up(index, d_scores):
            rows, keys, cols, place = units[index]
            d_queries = pick_heads(product(d_scores, k_ref[keys, cols])) * 0.125
            out_ref[rows, columns(0, cols)] = d_queries.astype(BF16)
            d_keys = left_product(d_scores, stack_heads(q_ref[rows, cols], low, high))
            d_values = left_product(kept_ref[place], stack_heads(dc_ref[rows, cols], low, high))
            if index % parts:
                d_keys += sums["keys"]
                d_values += sums["values"]
            if index % parts == parts - 1:
                out_ref[keys, columns(1, cols)] = d_keys.astype(BF16)
                out_ref[keys, columns(2, cols)] = d_values.astype(BF16)
            else:
                sums.update(keys=d_keys, values=d_values)

        pipelined(len(units), spread_in, differ, gather_up)

    @pl.when(tile < short_tiles)
    def _():
        units = []
        for seq in range(per_tile):
            rows = slice(seq * width, (seq + 1) * width)
            for pair in range(PAIRS):
                cols = slice(pair * BLK, (pair + 1) * BLK)
                units.append((rows, rows, cols, (0, pair, seq)))
        go_back(units, short_ref, 1)

    @pl.when(tile >= short_tiles)
    def _():
        half = TILE // 2
        units = []
        for pair in range(PAIRS):
            cols = slice(pair * BLK, (pair + 1) * BLK)
            for part in range(2):
                rows = slice(part * half, (part + 1) * half)
                units.append((rows, slice(0, TILE), cols, (0, pair, part)))
        go_back(units, long_ref, 2)

    @pl.when(group == 0)
    def _():
        turned_ref[...] = x_ref[...].T

    @pl.when((tile == 0) & (group == 0))
    def _():
        bq_ref[...] = jnp.zeros_like(bq_ref)
        bv_ref[...] = jnp.zeros_like(bv_ref)

    bq_ref[:, pl.ds(start, wide)] += column_sum(out_ref[:, pl.ds(start, wide)])
    bv_ref[:, pl.ds(start, wide)] += column_sum(out_ref[:, pl.ds(2 * D + start, wide)])

    if transfers:

        @pl.when((tile == pl.num_programs(0) - 1) & (group == GROUPS - 1))
        def _():
            reduce.finish()


def attention_back(qkv, probs_short, probs_long, d_context, x, short_tiles, terms=None, count=0):
    tiles = d_context.shape[0] // TILE
    wide = PAIRS * BLK
    short_map, long_map = probs_maps(short_tiles)
    rows = pl.BlockSpec((TILE, wide), lambda tile, group: (tile, group))
    row = pl.BlockSpec((1, D), lambda tile, group: (0, 0))
    flops = 10 * D * TILE * TILE * tiles
    in_specs = [
        rows,
        rows,
        rows,
        pl.BlockSpec((1, PAIRS) + probs_short.shape[2:], short_map),
        pl.BlockSpec((1, PAIRS) + probs_long.shape[2:], long_map),
        rows,
        pl.BlockSpec((TILE, D), lambda tile, group: (tile, 0)),
    ]
    out_specs = [
        pl.BlockSpec((TILE, 3 * D), lambda tile, group: (tile, 0)),
        row,
        row,
        pl.BlockSpec((D, TILE), lambda tile, group: (0, tile)),
    ]
    out_shape = [
        jax.ShapeDtypeStruct((tiles * TILE, 3 * D), BF16),
        jax.ShapeDtypeStruct((1, D), F32),
        jax.ShapeDtypeStruct((1, D), F32),
        jax.ShapeDtypeStruct((D, tiles * TILE), BF16),
    ]
    arguments = [*qkv, probs_short, probs_long, d_context, x]
    scratch = []
    params = dict(vmem_limit_bytes=60 * MIB)
    if terms is not None:
        arguments.append(terms)
        in_specs.append(pl.BlockSpec(memory_space=pltpu.HBM))
        out_specs.append(pl.BlockSpec((count, BLK), lambda tile, group: (0, 0)))
        out_shape.append(jax.ShapeDtypeStruct((count, BLK), BF16))
        scratch = reduce_scratch(count)
        params.update(collective_id=2, has_side_effects=True)
    return pl.pallas_call(
        partial(attention_back_kernel, short_tiles=short_tiles, transfers=terms is not None),
        grid=(tiles, GROUPS),
        in_specs=in_specs,
        out_specs=out_specs,
        out_shape=out_shape,
        scratch_shapes=scratch,
        compiler_params=pltpu.CompilerParams(**params),
        cost_estimate=pl.CostEstimate(flops=flops, bytes_accessed=50 * MIB, transcendentals=0),
        name="attention_back",
    )(*arguments)


INPUT_ROWS = 256


def input_product(d_ref, resid_ref, w_ref, short_ref, long_ref, short_steps):
    step = pl.program_id(0)
    total = resid_ref[...] + right_product(d_ref[...], w_ref[...])

    @pl.when(step < short_steps)
    def _():
        short_ref[...] = total

    @pl.when(step >= short_steps)
    def _():
        long_ref[...] = total


def input_specs(short_steps):
    rows = [pl.BlockSpec((INPUT_ROWS, width), lambda step: (step, 0)) for width in (3 * D, D)]
    whole = pl.BlockSpec((D, 3 * D), lambda step: (0, 0), pipeline_mode=pl.Buffered(1))
    outs = [
        pl.BlockSpec((INPUT_ROWS, D), lambda step: (short_index(step, short_steps), 0)),
        pl.BlockSpec((INPUT_ROWS, D), lambda step: (long_index(step, short_steps), 0)),
    ]
    return rows + [whole], outs


def input_grads(d_qkv, resid, w_qkv, short_tiles):
    steps = resid.shape[0] // INPUT_ROWS
    short_steps = short_tiles * TILE // INPUT_ROWS
    in_specs, out_specs = input_specs(short_steps)
    return pl.pallas_call(
        partial(input_product, short_steps=short_steps),
        grid=(steps,),
        in_specs=in_specs,
        out_specs=out_specs,
        out_shape=[
            jax.ShapeDtypeStruct((short_steps * INPUT_ROWS, D), F32),
            jax.ShapeDtypeStruct(((steps - short_steps) * INPUT_ROWS, D), F32),
        ],
        compiler_params=pltpu.CompilerParams(vmem_limit_bytes=60 * MIB),
        name="input_grads",
    )(d_qkv, resid, w_qkv)


def normal_parts(values):
    below = 0.5 * lax.erf(values * 0.7071067811865476) + 0.5
    return below, jnp.exp(-0.5 * values * values) * 0.3989422804014327


B_OUT, GAIN_ONE, SHIFT_ONE, B_UP, B_DOWN, GAIN_TWO, SHIFT_TWO, B_STUDENT, POOL_QUERY, B_HIDDEN = range(10)
VECTORS = (
    (12, 6),
    (18, 6),
    (24, 6),
    (30, 24),
    (54, 6),
    (60, 6),
    (66, 6),
    (72, 1),
    (73, 1),
    (74, 1),
)
CLASS_ROW = 75
LAST_ROW = 91
SMALL_ROWS = 96


def norm_parts(values):
    center = values - jnp.mean(values, axis=-1, keepdims=True)
    spread = jnp.mean(center * center, axis=-1, keepdims=True)
    inverse = lax.rsqrt(spread + NORM_EPSILON)
    return center * inverse, inverse


def norm_back(d_values, gain, unit, inverse):
    d_unit = d_values * gain
    return inverse * (
        d_unit
        - jnp.mean(d_unit, axis=-1, keepdims=True)
        - unit * jnp.mean(d_unit * unit, axis=-1, keepdims=True)
    )


def column_sum(values):
    return jnp.sum(values.astype(F32), axis=0, keepdims=True)


def pool_weights(student, query, length):
    scaled = student * query
    lane = lax.broadcasted_iota(jnp.int32, scaled.shape, 1)
    place = lax.broadcasted_iota(jnp.int32, (scaled.shape[0], 1), 0)
    weights = []
    for side in (lane < SD // PH, lane >= SD // PH):
        scores = jnp.sum(jnp.where(side, scaled, 0.0), axis=-1, keepdims=True)
        scores = jnp.where(place < length, scores, MASKED_SCORE)
        powers = jnp.exp(scores - jnp.max(scores, axis=0, keepdims=True))
        weights.append(powers / jnp.sum(powers, axis=0, keepdims=True))
    return jnp.where(lane < SD // PH, weights[0], weights[1]), weights


def student_back(student, query, weights, both, d_pooled):
    lane = lax.broadcasted_iota(jnp.int32, student.shape, 1)
    moved = student * d_pooled
    d_scores = []
    for side, weight in zip((lane < SD // PH, lane >= SD // PH), weights):
        d_weight = jnp.sum(jnp.where(side, moved, 0.0), axis=-1, keepdims=True)
        d_scores.append(weight * (d_weight - jnp.sum(weight * d_weight, axis=0, keepdims=True)))
    d_score = jnp.where(lane < SD // PH, d_scores[0], d_scores[1])
    d_query = jnp.sum(d_score * student, axis=0, keepdims=True) * 0.125
    return both * d_pooled + d_score * query, d_query


def feed_kernel(
    len_short,
    len_long,
    slot_ref,
    x_ref,
    context_ref,
    cot_short_ref,
    cot_long_ref,
    logit_cot_short,
    logit_cot_long,
    params,
    w_class_ref,
    b_class_ref,
    blocks,
    enc_short_ref,
    enc_long_ref,
    logits_short,
    logits_long,
    first_ref,
    active_ref,
    d_up_ref,
    d_down_ref,
    d_branch_ref,
    d_context_ref,
    d_resid_ref,
    g_student,
    g_hidden,
    g_small,
    slope,
    pooled_ref,
    d_student_ref,
    w_out,
    w_up,
    w_down,
    w_student,
    w_hidden,
    vectors,
    totals,
    g_class,
    g_last,
    w_class,
    b_class,
    logit_cot,
    sems,
    *,
    short_tiles,
    width,
):
    tile = pl.program_id(0)
    per_tile = TILE // width
    loads = ((w_out, 108, 6, 6), (w_up, 144, 6, 24), (w_down, 288, 24, 6), (w_student, 432, 6, 1), (w_hidden, 438, 1, 1))

    def arrive(*indices):
        @pl.when(tile == 0)
        def _():
            for index in indices:
                wait_whole(loads[index][0], sems.at[index])

    @pl.when(tile == 0)
    def _():
        for index, (target, block, row_count, col_count) in enumerate(loads):
            load_blocks(slot_ref, blocks, target, sems.at[index], block, row_count, col_count)
        for index, (start, count) in enumerate(VECTORS):
            for place in range(count):
                vectors[index : index + 1, place * BLK : (place + 1) * BLK] = params[
                    start + place : start + place + 1, :
                ]
        for ref in (totals, g_class, g_last, g_student, g_hidden, w_class, b_class):
            ref[...] = jnp.zeros_like(ref)
        w_class[:, :NCLS] = w_class_ref[...]
        b_class[:, :NCLS] = b_class_ref[...]

    def vector(index):
        return vectors[index : index + 1, : VECTORS[index][1] * BLK]

    def add_total(index, values):
        totals[index : index + 1, : VECTORS[index][1] * BLK] += column_sum(values)

    arrive(0)
    branch = product(context_ref[...], w_out[...]) + vector(B_OUT)
    unit_one, inverse_one = norm_parts(x_ref[...].astype(F32) + branch)
    first = (unit_one * vector(GAIN_ONE) + vector(SHIFT_ONE)).astype(BF16)
    first_ref[...] = first.T
    arrive(1)
    chunks = [slice(start, start + CHUNK) for start in range(0, FF, CHUNK)]

    def rise(index):
        return product(first, w_up[:, chunks[index]])

    def bend(index, upward):
        upward = upward + vectors[B_UP : B_UP + 1, chunks[index]]
        below, density = normal_parts(upward)
        active_ref[:, chunks[index]] = (upward * below).astype(BF16)
        slope[:, chunks[index]] = (below + upward * density).astype(BF16)

    pipelined(len(chunks), rise, bend, lambda *_: None)
    arrive(2, 3, 4)
    downward = product(active_ref[...], w_down[...]) + vector(B_DOWN)
    unit_two, inverse_two = norm_parts(first.astype(F32) + downward)
    encoded = (unit_two * vector(GAIN_TWO) + vector(SHIFT_TWO)).astype(BF16)

    @pl.when(tile < short_tiles)
    def _():
        enc_short_ref[...] = encoded

    @pl.when(tile >= short_tiles)
    def _():
        enc_long_ref[...] = encoded

    student = product(encoded, w_student[...]) + vector(B_STUDENT)
    query = vector(POOL_QUERY) * 0.125
    pooled_ref[...] = jnp.zeros_like(pooled_ref)

    def head():
        pooled = pooled_ref[...]
        wide_hidden = w_hidden[...].astype(F32)
        hidden = jnp.tanh(product(pooled, wide_hidden, HIGHEST_PRECISION) + vector(B_HIDDEN))
        logits = product(hidden, w_class[...], HIGHEST_PRECISION) + b_class[...]
        d_logits = logit_cot[...]
        g_last[...] += column_sum(d_logits)
        g_class[...] += left_product(d_logits, hidden, HIGHEST_PRECISION)
        d_hidden = right_product(d_logits, w_class[...], HIGHEST_PRECISION)
        d_hidden = d_hidden * (1.0 - hidden * hidden)
        add_total(B_HIDDEN, d_hidden)
        g_hidden[...] += left_product(pooled, d_hidden, HIGHEST_PRECISION)
        return logits, right_product(d_hidden, wide_hidden, HIGHEST_PRECISION)

    def pool(starts, size, lengths, cot_ref, logits_ref, first):
        count = len(starts)
        logit_cot[...] = jnp.zeros_like(logit_cot)
        for index in range(count):
            logit_cot[index : index + 1, :NCLS] = cot_ref[pl.ds(first + index, 1), :]
        kept = []
        for index, (start, length) in enumerate(zip(starts, lengths)):
            rows = student[start : start + size]
            both, weights = pool_weights(rows, query, length)
            pooled_ref[index : index + 1, :] = column_sum(both * rows)
            kept.append((start, rows, both, weights))
        logits, d_pooled = head()
        for index in range(count):
            logits_ref[pl.ds(first + index, 1), :] = logits[index : index + 1, :NCLS]
        for index, (start, rows, both, weights) in enumerate(kept):
            d_rows, d_query = student_back(rows, query, weights, both, d_pooled[index : index + 1])
            d_student_ref[start : start + size, :] = d_rows.astype(BF16)
            add_total(POOL_QUERY, d_query)

    @pl.when(tile < short_tiles)
    def _():
        pool(
            [seq * width for seq in range(per_tile)],
            width,
            [len_short[tile * per_tile + seq] for seq in range(per_tile)],
            logit_cot_short,
            logits_short,
            tile * per_tile,
        )

    @pl.when(tile >= short_tiles)
    def _():
        long = tile - short_tiles
        pool([0], TILE, [len_long[long]], logit_cot_long, logits_long, long)

    d_student = d_student_ref[...]
    add_total(B_STUDENT, d_student)
    g_student[...] += left_product(encoded, d_student)
    cotangent = jnp.where(tile < short_tiles, cot_short_ref[...], cot_long_ref[...])
    d_second = cotangent.astype(F32) + right_product(d_student, w_student[...])
    add_total(GAIN_TWO, d_second * unit_two)
    add_total(SHIFT_TWO, d_second)
    d_resid_two = norm_back(d_second, vector(GAIN_TWO), unit_two, inverse_two)
    d_down = d_resid_two.astype(BF16)
    d_down_ref[...] = d_down.T
    add_total(B_DOWN, d_down)

    def fall(index):
        return right_product(d_down, w_down[chunks[index], :])

    def bend_back(index, d_active):
        d_up = (d_active * slope[:, chunks[index]].astype(F32)).astype(BF16)
        d_up_ref[:, chunks[index]] = d_up
        totals[B_UP : B_UP + 1, chunks[index]] += column_sum(d_up)

    pipelined(len(chunks), fall, bend_back, lambda *_: None)
    d_first = d_resid_two + right_product(d_up_ref[...], w_up[...])
    add_total(GAIN_ONE, d_first * unit_one)
    add_total(SHIFT_ONE, d_first)
    d_resid_one = norm_back(d_first, vector(GAIN_ONE), unit_one, inverse_one)
    d_resid_ref[...] = d_resid_one
    d_branch = d_resid_one.astype(BF16)
    d_branch_ref[...] = d_branch
    add_total(B_OUT, d_branch)
    d_context_ref[...] = right_product(d_branch, w_out[...]).astype(BF16)

    @pl.when(tile == pl.num_programs(0) - 1)
    def _():
        g_small[...] = jnp.zeros_like(g_small)
        for index, (start, count) in enumerate(VECTORS):
            for place in range(count):
                g_small[start + place : start + place + 1, :] = totals[
                    index : index + 1, place * BLK : (place + 1) * BLK
                ]
        g_small[CLASS_ROW : CLASS_ROW + NCLS, :] = g_class[:NCLS, :]
        g_small[LAST_ROW : LAST_ROW + 1, :] = g_last[...]


def feed(
    len_short, len_long, block_slot, x, context, cot_short, cot_long, logit_cots, small, blocks, short_tiles, width
):
    tiles = x.shape[0] // TILE
    long_tiles = tiles - short_tiles

    def whole(shape):
        return pl.BlockSpec(shape, lambda tile, *_: (0,) * len(shape), pipeline_mode=pl.Buffered(1))

    def kept(shape):
        return pl.BlockSpec(shape, lambda tile, *_: (0,) * len(shape))

    def rows(columns):
        return pl.BlockSpec((TILE, columns), lambda tile, *_: (tile, 0))

    turned = pl.BlockSpec((D, TILE), lambda tile, *_: (0, tile))
    short_rows = pl.BlockSpec((TILE, D), lambda tile, *_: (short_index(tile, short_tiles), 0))
    long_rows = pl.BlockSpec((TILE, D), lambda tile, *_: (long_index(tile, short_tiles), 0))
    grad_shapes = ((D, SD), (SD, SD), (SMALL_ROWS, BLK))
    total = tiles * TILE
    return pl.pallas_call(
        partial(feed_kernel, short_tiles=short_tiles, width=width),
        grid_spec=pltpu.PrefetchScalarGridSpec(
            num_scalar_prefetch=3,
            grid=(tiles,),
            in_specs=[rows(D), rows(D), short_rows, long_rows]
            + [whole(array.shape) for array in (*logit_cots, *small)]
            + [pl.BlockSpec(memory_space=pltpu.HBM)],
            out_specs=[
                short_rows,
                long_rows,
                kept(logit_cots[0].shape),
                kept(logit_cots[1].shape),
                turned,
                rows(FF),
                rows(FF),
                turned,
                rows(D),
                rows(D),
                rows(D),
            ]
            + [kept(shape) for shape in grad_shapes],
            scratch_shapes=[
                pltpu.VMEM((TILE, FF), BF16),
                pltpu.VMEM((8, SD), F32),
                pltpu.VMEM((TILE, SD), BF16),
                pltpu.VMEM((D, D), BF16),
                pltpu.VMEM((D, FF), BF16),
                pltpu.VMEM((FF, D), BF16),
                pltpu.VMEM((D, SD), BF16),
                pltpu.VMEM((SD, SD), BF16),
                pltpu.VMEM((16, FF), F32),
                pltpu.VMEM((16, FF), F32),
                pltpu.VMEM((SD, SD), F32),
                pltpu.VMEM((1, SD), F32),
                pltpu.VMEM((SD, SD), F32),
                pltpu.VMEM((1, SD), F32),
                pltpu.VMEM((8, SD), F32),
                pltpu.SemaphoreType.DMA((5,)),
            ],
        ),
        out_shape=[
            jax.ShapeDtypeStruct((short_tiles * TILE, D), BF16),
            jax.ShapeDtypeStruct((long_tiles * TILE, D), BF16),
            jax.ShapeDtypeStruct(logit_cots[0].shape, F32),
            jax.ShapeDtypeStruct(logit_cots[1].shape, F32),
            jax.ShapeDtypeStruct((D, total), BF16),
            jax.ShapeDtypeStruct((total, FF), BF16),
            jax.ShapeDtypeStruct((total, FF), BF16),
            jax.ShapeDtypeStruct((D, total), BF16),
            jax.ShapeDtypeStruct((total, D), BF16),
            jax.ShapeDtypeStruct((total, D), BF16),
            jax.ShapeDtypeStruct((total, D), F32),
        ]
        + [jax.ShapeDtypeStruct(shape, F32) for shape in grad_shapes],
        compiler_params=pltpu.CompilerParams(vmem_limit_bytes=62 * MIB),
        cost_estimate=pl.CostEstimate(
            flops=total * (8 * D * FF + 4 * D * D), bytes_accessed=70 * MIB, transcendentals=total * FF
        ),
        name="feed",
    )(len_short, len_long, block_slot, x, context, cot_short, cot_long, *logit_cots, *small, blocks)


class Place:
    def __init__(self):
        self.quarter = lax.axis_index("dp")
        self.shard = lax.axis_index("fsdp")
        x = self.quarter % 2
        y = self.quarter // 2
        self.core = self.shard % 2
        self.z = self.shard // 2
        self.high = self.z // 2
        self.by_x = 2 * y + 1 - x
        self.by_y = 2 * (1 - y) + x
        self.across = 2 * (1 - y) + 1 - x
        self.sibling = (self.quarter, 2 * self.z + 1 - self.core)
        self.next_x = (self.by_x, self.shard)
        self.next_y = (self.by_y, self.shard)
        self.inner = (self.z > 0) & (self.z < 3)

    def at_z(self, z):
        return (self.quarter, 2 * z + self.core)


def transfer(source, target, send_sem, recv_sem, device):
    return pltpu.make_async_remote_copy(
        src_ref=source,
        dst_ref=target,
        send_sem=send_sem,
        recv_sem=recv_sem,
        device_id=device,
        device_id_type=pl.DeviceIdType.MESH,
    )


def greet(place, extra=()):
    barrier = pltpu.get_barrier_semaphore()

    def signal(device):
        pl.semaphore_signal(barrier, inc=1, device_id=device, device_id_type=pl.DeviceIdType.MESH)

    near = (place.sibling, place.next_x, place.next_y) + tuple(extra)
    for device in near:
        signal(device)

    @pl.when(place.z > 0)
    def _():
        signal(place.at_z(place.z - 1))

    @pl.when(place.z < 3)
    def _():
        signal(place.at_z(place.z + 1))

    pl.semaphore_wait(barrier, len(near) + 1 + (place.z + 1) // 2 % 2)


CUTS = 2
GATHER_SEMAPHORES = [
    pltpu.SemaphoreType.DMA((2 * CUTS,)),
    pltpu.SemaphoreType.DMA((3 * CUTS,)),
    pltpu.SemaphoreType.DMA((4 * CUTS,)),
    pltpu.SemaphoreType.DMA((12 * CUTS,)),
    pltpu.SemaphoreType.DMA((12 * CUTS,)),
    pltpu.SemaphoreType.DMA((1 + 18 * CUTS,)),
    pltpu.SemaphoreType.DMA((1 + 18 * CUTS,)),
    pltpu.SemaphoreType.DMA((8,)),
    pltpu.SemaphoreType.DMA((2 * CUTS,)),
    pltpu.SemaphoreType.DMA((3 * CUTS,)),
    pltpu.SemaphoreType.DMA((4 * CUTS,)),
]


class Gather:
    def __init__(self, full, out, sems):
        self.place = place = Place()
        self.full, self.out = full, out
        (
            self.own_send,
            self.relay_send,
            self.z_recv,
            self.xy_send,
            self.xy_recv,
            self.core_send,
            self.core_recv,
            self.out_sems,
            self.own_more,
            self.relay_more,
            self.z_more,
        ) = sems
        self.quarter = full.shape[1] // 4
        self.cut = self.quarter // CUTS
        self.z_part = self.cut // 64 * 16
        self.first_part = ((self.cut - self.z_part) // 16 + 1) // 2 * 16
        self.last_part = self.cut - self.z_part - self.first_part
        z = place.z
        self.origins = (z + 1 - 2 * (z % 2), 2 - place.high, 3 * (1 - place.high))
        self.relays = (3 - z, 3 * (z - 1), 3 * (z - 1))

    def region(self, which, start, size):
        return self.full.at[which, pl.ds(pl.multiple_of(start, 16), size)]

    def pieces(self, which, turn):
        place, quarter, cut, part = self.place, self.quarter, self.cut, self.first_part
        skip = turn % CUTS * cut
        return (
            self.region(which, place.quarter * quarter + skip, cut),
            self.region(which, place.by_x * quarter + skip, cut),
            self.region(which, place.by_y * quarter + skip, cut),
            self.region(which, place.across * quarter + skip, part),
            self.region(which, place.across * quarter + skip + part, self.last_part),
            self.region(which, place.across * quarter + skip + cut - self.z_part, self.z_part),
        )

    def own_copy(self, side, cut, more=False):
        place = self.place
        mine = self.pieces(place.shard, cut)[5 if more else 0]
        device = place.at_z(place.z - 1 + 2 * side)
        send, recv = (self.own_more, self.z_more) if more else (self.own_send, self.z_recv)
        return transfer(
            mine, mine, send.at[side * CUTS + cut], recv.at[place.z * CUTS + cut], device
        )

    def core_copy(self, index, ref):
        return transfer(ref, ref, self.core_send.at[index], self.core_recv.at[index], self.place.sibling)

    def xy_copy(self, index, ref, device):
        return transfer(ref, ref, self.xy_send.at[index], self.xy_recv.at[index], device)

    def store(self, index, which):
        return pltpu.make_async_copy(self.full.at[which], self.out.at[which], self.out_sems.at[index])

    def mirrored(self, step):
        return 2 * self.origins[step] + 1 - self.place.core

    def held(self, step):
        return 2 * self.origins[step] + self.place.core

    def start(self):
        place = self.place
        greet(place)
        for cut in range(CUTS):

            for more in (False, True):

                @pl.when(place.z > 0)
                def _():
                    self.own_copy(0, cut, more).start()

                @pl.when(place.z < 3)
                def _():
                    self.own_copy(1, cut, more).start()

        self.core_copy(0, self.full.at[place.shard]).start()
        self.store(0, place.shard).start()

    def relay(self, turn, more=False):
        step = turn // CUTS
        piece = self.pieces(self.held(step), turn)[5 if more else 0]
        device = self.place.at_z(self.relays[step])
        send, recv = (self.relay_more, self.z_more) if more else (self.relay_send, self.z_recv)
        sem = recv.at[self.origins[step] * CUTS + turn % CUTS]
        return transfer(piece, piece, send.at[turn], sem, device)

    def along_z(self, turn):
        place = self.place
        self.relay(turn).wait_recv()

        @pl.when(place.inner)
        def _():
            self.relay(turn).start()

        pieces = self.pieces(self.held(turn // CUTS), turn)
        self.xy_copy(4 * turn, pieces[0], place.next_x).start()
        self.xy_copy(4 * turn + 1, pieces[0], place.next_y).start()
        self.core_copy(1 + 6 * turn, pieces[0]).start()
        self.relay(turn, True).wait_recv()

        @pl.when(place.inner)
        def _():
            self.relay(turn, True).start()

        self.core_copy(6 + 6 * turn, pieces[5]).start()

    def along_xy(self, turn):
        place, part = self.place, self.first_part
        _, by_x, by_y, *_ = self.pieces(self.held(turn // CUTS), turn)
        self.xy_copy(4 * turn, by_x, place.next_x).wait_recv()
        self.xy_copy(4 * turn + 2, by_x.at[pl.ds(0, part)], place.next_y).start()
        self.core_copy(2 + 6 * turn, by_x).start()
        self.xy_copy(4 * turn + 1, by_y, place.next_y).wait_recv()
        self.xy_copy(4 * turn + 3, by_y.at[pl.ds(part, self.last_part)], place.next_x).start()
        self.core_copy(3 + 6 * turn, by_y).start()

    def across(self, turn):
        place = self.place
        step = turn // CUTS
        _, _, _, first, last, _ = self.pieces(self.held(step), turn)
        self.xy_copy(4 * turn + 2, first, place.next_y).wait_recv()
        self.core_copy(4 + 6 * turn, first).start()
        self.xy_copy(4 * turn + 3, last, place.next_x).wait_recv()
        self.core_copy(5 + 6 * turn, last).start()
        if turn % CUTS == CUTS - 1:
            self.store(2 + 2 * step, self.held(step)).start()

    def core_own(self):
        which = 2 * self.place.z + 1 - self.place.core
        self.core_copy(0, self.full.at[which]).wait_recv()
        self.store(1, which).start()

    def core(self, step):
        which = self.mirrored(step)
        for turn in range(step * CUTS, (step + 1) * CUTS):
            for index, ref in enumerate(self.pieces(which, turn)):
                self.core_copy(1 + 6 * turn + index, ref).wait_recv()
        self.store(3 + 2 * step, which).start()

    def finish(self):
        place = self.place
        for cut in range(CUTS):

            for more in (False, True):

                @pl.when(place.z > 0)
                def _():
                    self.own_copy(0, cut, more).wait_send()

                @pl.when(place.z < 3)
                def _():
                    self.own_copy(1, cut, more).wait_send()

        self.core_copy(0, self.full.at[place.shard]).wait_send()
        self.store(0, place.shard).wait()
        self.store(1, 2 * place.z + 1 - place.core).wait()
        for turn in range(3 * CUTS):

            @pl.when(place.inner)
            def _():
                self.relay(turn).wait_send()
                self.relay(turn, True).wait_send()

            pieces = self.pieces(self.held(turn // CUTS), turn)
            self.xy_copy(4 * turn, pieces[0], place.next_x).wait_send()
            self.xy_copy(4 * turn + 1, pieces[0], place.next_y).wait_send()
            self.xy_copy(4 * turn + 2, pieces[3], place.next_y).wait_send()
            self.xy_copy(4 * turn + 3, pieces[4], place.next_x).wait_send()
            for index, ref in enumerate(pieces):
                self.core_copy(1 + 6 * turn + index, ref).wait_send()
        for step in range(3):
            self.store(2 + 2 * step, self.held(step)).wait()
            self.store(3 + 2 * step, self.mirrored(step)).wait()


def gather_kernel(master_ref, out_ref, full, *sems):
    gather = Gather(full, out_ref, sems)
    full[gather.place.shard] = master_ref[...].astype(BF16)
    gather.start()
    turns = 3 * CUTS
    for turn in range(turns + 2):
        if turn < turns:
            gather.along_z(turn)
        if 1 <= turn <= turns:
            gather.along_xy(turn - 1)
        if turn >= 2:
            gather.across(turn - 2)
        if turn == 2:
            gather.core_own()
        if turn >= 4 and turn % CUTS == 0:
            gather.core(turn // CUTS - 2)
    gather.core(2)
    gather.finish()


def gather_shards(master):
    rows = master.shape[0] * BLK
    shards = lax.axis_size("fsdp")
    return pl.pallas_call(
        gather_kernel,
        in_specs=[pl.BlockSpec(memory_space=pltpu.VMEM)],
        out_specs=pl.BlockSpec(memory_space=pltpu.HBM),
        out_shape=jax.ShapeDtypeStruct((shards, rows, BLK), BF16),
        scratch_shapes=[pltpu.VMEM((shards, rows, BLK), BF16)] + GATHER_SEMAPHORES,
        compiler_params=pltpu.CompilerParams(
            collective_id=0, has_side_effects=True, vmem_limit_bytes=60 * MIB
        ),
        cost_estimate=pl.CostEstimate(flops=0, bytes_accessed=200 * MIB, transcendentals=0),
        name="gather",
    )(master.reshape(rows, BLK)).reshape(-1, BLK, BLK)


def add_rows(target, former, latter, rows, step):
    @pl.loop(0, rows // step)
    def _(index):
        part = pl.ds(pl.multiple_of(index * step, 16), step)
        target[part] = (former[part].astype(F32) + latter[part].astype(F32)).astype(BF16)


def reduce_scratch(rows):
    quarter = rows // 4
    half = quarter // 2
    return [
        pltpu.VMEM((4, rows, BLK), BF16),
        pltpu.VMEM((4, rows, BLK), BF16),
        pltpu.VMEM((4, 2, half, BLK), BF16),
        pltpu.VMEM((4, 2, half, BLK), BF16),
        pltpu.VMEM((4, half, BLK), BF16),
        pltpu.VMEM((4, half, BLK), BF16),
        pltpu.VMEM((5, quarter, BLK), BF16),
        pltpu.VMEM((rows, BLK), BF16),
        pltpu.SemaphoreType.DMA((4,)),
        pltpu.SemaphoreType.DMA((4,)),
        pltpu.SemaphoreType.DMA((4,)),
        pltpu.SemaphoreType.DMA((24,)),
        pltpu.SemaphoreType.DMA((24,)),
        pltpu.SemaphoreType.DMA((3,)),
        pltpu.SemaphoreType.DMA((5,)),
        pltpu.SemaphoreType.DMA((4,)),
        pltpu.SemaphoreType.DMA((4,)),
    ]


class Reduce:
    def __init__(self, terms, base, out, scratch):
        self.place = place = Place()
        self.terms, self.base, self.out = terms, base, out
        (
            self.mine,
            self.sib,
            self.from_x,
            self.from_y,
            self.late_y,
            self.late_x,
            self.from_z,
            self.result,
            self.load_sems,
            self.core_send,
            self.core_recv,
            self.xy_send,
            self.xy_recv,
            self.z_send,
            self.z_recv,
            self.last_send,
            self.last_recv,
        ) = scratch
        self.quarter = out.shape[0] // 4
        self.half = self.quarter // 2
        z, high = place.z, place.high
        low = 1 - high
        self.order = (3 * low, low * (2 - 2 * z) + high * (7 - 2 * z), 1 + z % 2, z)
        self.onward = (z + 1 - 2 * high, z + 1 - 2 * (z % 2), z + 1 - 2 * high)
        self.closing = (0, (z % 2) * low, high)
        self.far = place.at_z(z + 2 - 4 * high)
        self.near = place.at_z(z + 1 - 2 * (z % 2))

    def shard_terms(self, shard):
        rows = self.out.shape[0]
        return self.terms.at[pl.ds(pl.multiple_of(self.base + shard * rows, 16), rows)]

    def load(self, step):
        source = self.shard_terms(2 * self.order[step] + self.place.core)
        return pltpu.make_async_copy(source, self.mine.at[step], self.load_sems.at[step])

    def core_copy(self, step):
        return transfer(
            self.shard_terms(2 * self.order[step] + 1 - self.place.core),
            self.sib.at[step],
            self.core_send.at[step],
            self.core_recv.at[step],
            self.place.sibling,
        )

    def part(self, step, which, side):
        start = pl.multiple_of(which * self.quarter + side * self.half, 16)
        return self.mine.at[step, pl.ds(start, self.half)]

    def xy_copy(self, step, index):
        place = self.place
        source, target, device = (
            (self.part(step, place.by_x, 0), self.from_x.at[step, 0], place.next_x),
            (self.part(step, place.across, 0), self.from_x.at[step, 1], place.next_x),
            (self.part(step, place.by_y, 1), self.from_y.at[step, 0], place.next_y),
            (self.part(step, place.across, 1), self.from_y.at[step, 1], place.next_y),
            (self.part(step, place.by_y, 0), self.late_y.at[step], place.next_y),
            (self.part(step, place.by_x, 1), self.late_x.at[step], place.next_x),
        )[index]
        place = 6 * step + index
        return transfer(source, target, self.xy_send.at[place], self.xy_recv.at[place], device)

    def start(self):
        greet(self.place, (self.far,))
        for step in range(2):
            self.core_copy(step).start()
        for step in range(4):
            self.load(step).start()

    def core(self, step):
        place, quarter = self.place, self.quarter
        self.load(step).wait()
        self.core_copy(step).wait_recv()
        if step < 2:
            self.core_copy(step + 2).start()

        def add(which):
            block = pl.ds(pl.multiple_of(which * quarter, 16), quarter)
            mine = self.mine.at[step, block]
            add_rows(mine, mine, self.sib.at[step, block], quarter, self.half)

        add(place.by_x)
        add(place.across)
        self.xy_copy(step, 0).start()
        self.xy_copy(step, 1).start()
        add(place.by_y)
        self.xy_copy(step, 2).start()
        self.xy_copy(step, 3).start()
        add(place.quarter)

    def take(self, step, which, side, index, source):
        self.xy_copy(step, index).wait_recv()
        target = self.part(step, which, side)
        add_rows(target, target, source, self.half, self.half)

    def first(self, step):
        place = self.place
        self.take(step, place.by_y, 0, 1, self.from_x.at[step, 1])
        self.xy_copy(step, 4).start()
        self.take(step, place.by_x, 1, 3, self.from_y.at[step, 1])
        self.xy_copy(step, 5).start()
        self.take(step, place.quarter, 0, 0, self.from_x.at[step, 0])
        self.take(step, place.quarter, 1, 2, self.from_y.at[step, 0])

    def own_block(self, step):
        return self.mine.at[step, pl.ds(pl.multiple_of(self.place.quarter * self.quarter, 16), self.quarter)]

    def z_copy(self, step):
        goal = self.order[step]
        slot = goal + self.closing[step] * (4 - goal)
        return transfer(
            self.own_block(step),
            self.from_z.at[slot],
            self.z_send.at[step],
            self.z_recv.at[slot],
            self.place.at_z(self.onward[step]),
        )

    def take_z(self, step, slot):
        source = self.from_z.at[slot]
        transfer(source, source, self.z_send.at[0], self.z_recv.at[slot], self.near).wait_recv()
        block = self.own_block(step)
        add_rows(block, block, source, self.quarter, self.half)

    def second(self, step):
        place = self.place
        self.take(step, place.quarter, 0, 4, self.late_y.at[step])
        self.take(step, place.quarter, 1, 5, self.late_x.at[step])
        if step < 3:

            @pl.when(place.inner)
            def _():
                self.take_z(step, self.order[step])

            self.z_copy(step).start()
        else:

            @pl.when(place.z > 0)
            def _():
                self.take_z(step, place.z)

            @pl.when(place.z < 3)
            def _():
                self.take_z(step, 4)

    def final(self, which, side=None):
        start = pl.multiple_of(which * self.quarter + (0 if side is None else side * self.half), 16)
        return self.result.at[pl.ds(start, self.quarter if side is None else self.half)]

    def last_copy(self, index, ref):
        device = (self.place.next_x, self.place.next_y, self.place.next_y, self.place.next_x)[index]
        return transfer(ref, ref, self.last_send.at[index], self.last_recv.at[index], device)

    def share(self):
        own = self.final(self.place.quarter)
        own[...] = self.own_block(3)[...]
        self.last_copy(0, own).start()
        self.last_copy(1, own).start()

    def share_on(self):
        place = self.place
        self.last_copy(0, self.final(place.by_x)).wait_recv()
        self.last_copy(2, self.final(place.by_x, 0)).start()
        self.last_copy(1, self.final(place.by_y)).wait_recv()
        self.last_copy(3, self.final(place.by_y, 1)).start()

    def finish(self):
        place = self.place
        self.last_copy(2, self.final(place.across, 0)).wait_recv()
        self.last_copy(3, self.final(place.across, 1)).wait_recv()
        self.out[...] = self.result[...]
        for step in range(4):
            self.core_copy(step).wait_send()
            for index in range(6):
                self.xy_copy(step, index).wait_send()
            if step < 3:
                self.z_copy(step).wait_send()
        own = self.final(place.quarter)
        self.last_copy(0, own).wait_send()
        self.last_copy(1, own).wait_send()
        self.last_copy(2, self.final(place.by_x, 0)).wait_send()
        self.last_copy(3, self.final(place.by_y, 1)).wait_send()


def reduce_kernel(*refs, base, short_steps):
    terms, small_ref, d_ref, resid_ref, w_ref, out_ref, small_out, short_ref, long_ref = refs[:9]
    small_in, small_sum, small_send, small_recv = refs[9:13]
    reduce = Reduce(terms, base, out_ref, refs[13:])
    place = reduce.place
    partners = (place.sibling, place.next_x, place.next_y, reduce.near, reduce.far)

    def small_copy(level):
        return transfer(
            small_sum.at[level],
            small_in.at[level],
            small_send.at[level],
            small_recv.at[level],
            partners[level],
        )

    def small_start():
        small_sum[0] = small_ref[...]
        small_copy(0).start()

    def small_step(level):
        small_copy(level - 1).wait_recv()
        small_sum[level] = small_sum[level - 1] + small_in[level - 1]
        if level < 5:
            small_copy(level).start()
        else:
            small_out[...] = small_sum[5]

    run_events(
        pl.program_id(0),
        (
            (reduce.start, small_start),
            (partial(reduce.core, 0), partial(small_step, 1)),
            (partial(reduce.core, 1), partial(reduce.first, 0), partial(small_step, 2)),
            (
                partial(reduce.core, 2),
                partial(reduce.first, 1),
                partial(reduce.second, 0),
                partial(small_step, 3),
            ),
            (
                partial(reduce.core, 3),
                partial(reduce.first, 2),
                partial(reduce.second, 1),
                partial(small_step, 4),
            ),
            (partial(reduce.first, 3), partial(reduce.second, 2), partial(small_step, 5)),
            (partial(reduce.second, 3), reduce.share),
            (reduce.share_on,),
        ),
    )
    input_product(d_ref, resid_ref, w_ref, short_ref, long_ref, short_steps)

    @pl.when(pl.program_id(0) == pl.num_programs(0) - 1)
    def _():
        reduce.finish()
        for level in range(5):
            small_copy(level).wait_send()


def reduce_late(terms, base, rows, small, d_qkv, resid, w_qkv, short_tiles):
    steps = resid.shape[0] // INPUT_ROWS
    short_steps = short_tiles * TILE // INPUT_ROWS
    in_specs, out_specs = input_specs(short_steps)

    def whole(shape):
        return pl.BlockSpec(shape, lambda step: (0, 0), pipeline_mode=pl.Buffered(1))

    return pl.pallas_call(
        partial(reduce_kernel, base=base, short_steps=short_steps),
        grid=(steps,),
        in_specs=[pl.BlockSpec(memory_space=pltpu.HBM), whole(small.shape)] + in_specs,
        out_specs=[
            pl.BlockSpec((rows, BLK), lambda step: (0, 0)),
            pl.BlockSpec(small.shape, lambda step: (0, 0)),
        ]
        + out_specs,
        out_shape=[
            jax.ShapeDtypeStruct((rows, BLK), BF16),
            jax.ShapeDtypeStruct((SMALL_ROWS, BLK), F32),
            jax.ShapeDtypeStruct((short_steps * INPUT_ROWS, D), F32),
            jax.ShapeDtypeStruct(((steps - short_steps) * INPUT_ROWS, D), F32),
        ],
        scratch_shapes=[
            pltpu.VMEM((5, SMALL_ROWS, BLK), F32),
            pltpu.VMEM((6, SMALL_ROWS, BLK), F32),
            pltpu.SemaphoreType.DMA((5,)),
            pltpu.SemaphoreType.DMA((5,)),
        ]
        + reduce_scratch(rows),
        compiler_params=pltpu.CompilerParams(
            collective_id=3, has_side_effects=True, vmem_limit_bytes=60 * MIB
        ),
        cost_estimate=pl.CostEstimate(flops=0, bytes_accessed=200 * MIB, transcendentals=0),
        name="reduce",
    )(terms, small, d_qkv, resid, w_qkv)


def count_where(condition, axis):
    return jnp.sum(condition.astype(jnp.int32), axis=axis)


def slot_codes(slots, qkv_slots, slot_count, shards):
    early = slot_count - LATE
    shard = slots // slot_count
    begin = shard * slot_count
    inside = (qkv_slots[None, :] >= begin[:, None]) & (qkv_slots[None, :] < (begin + slot_count)[:, None])
    own = count_where(qkv_slots[None, :] == slots[:, None], 1)
    before = count_where(inside & (qkv_slots[None, :] < slots[:, None]), 1)
    number = count_where(inside, 1)
    position = jnp.where(own > 0, slot_count - number + before, slots - begin - before)
    code = jnp.where(
        position < early,
        shard * early + position,
        shards * early + shard * LATE + position - early,
    )
    return code, position, jnp.max(number)


def update_kernel(
    position_ref,
    held_ref,
    early,
    late,
    master,
    left_stat,
    right_stat,
    left_root,
    right_root,
    slot_grad,
    new_left,
    new_right,
    new_master,
):
    count = master.shape[0]
    first = pl.program_id(0) * count
    split = early.shape[0] // BLK

    def block(ref, place):
        return ref[pl.ds(pl.multiple_of(place * BLK, BLK), BLK)]

    def grad_of(index):
        place = position_ref[first + index]
        grad = jnp.where(
            place < split,
            block(early, jnp.minimum(place, split - 1)),
            block(late, jnp.maximum(place - split, 0)),
        )
        return jnp.where(held_ref[first + index] > 0, grad, jnp.zeros_like(grad))

    for begin in range(0, count, 4):
        some = range(begin, min(begin + 4, count))
        grads = [grad_of(index) for index in some]
        applied = [product(left_root[index].astype(BF16), grad) for index, grad in zip(some, grads)]
        outer_left = [right_product(grad, grad) for grad in grads]
        outer_right = [left_product(grad, grad) for grad in grads]
        totals = [
            product(part.astype(BF16), right_root[index].astype(BF16)) for index, part in zip(some, applied)
        ]
        for place, index in enumerate(some):
            slot_grad[index] = grads[place].astype(F32)
            new_left[index] = STAT_DECAY * left_stat[index] + (1.0 - STAT_DECAY) * outer_left[place]
            new_right[index] = STAT_DECAY * right_stat[index] + (1.0 - STAT_DECAY) * outer_right[place]
            new_master[index] = master[index] - MATRIX_RATE * totals[place]


def update(position, held, early, late, master, left_stat, right_stat, left_root, right_root):
    slot_count = master.shape[0]
    group = max(size for size in range(1, 12) if slot_count % size == 0)
    some = pl.BlockSpec((group, BLK, BLK), lambda step, *_: (step, 0, 0))

    def whole(shape):
        return pl.BlockSpec(shape, lambda step, *_: (0, 0), pipeline_mode=pl.Buffered(1))

    return pl.pallas_call(
        update_kernel,
        grid_spec=pltpu.PrefetchScalarGridSpec(
            num_scalar_prefetch=2,
            grid=(slot_count // group,),
            in_specs=[whole(early.shape), whole(late.shape)] + [some] * 5,
            out_specs=[some] * 4,
        ),
        out_shape=[jax.ShapeDtypeStruct(master.shape, F32)] * 4,
        compiler_params=pltpu.CompilerParams(vmem_limit_bytes=60 * MIB),
        cost_estimate=pl.CostEstimate(
            flops=8 * slot_count * BLK**3, bytes_accessed=36 * slot_count * BLK**2, transcendentals=0
        ),
        name="update",
    )(position, held, early, late, master, left_stat, right_stat, left_root, right_root)


def body(
    x_short,
    x_long,
    cot_short,
    cot_long,
    logit_cot_short,
    logit_cot_long,
    len_short,
    len_long,
    block_slot,
    master,
    left_stat,
    right_stat,
    left_root,
    right_root,
    small_params,
    small_first,
    small_second,
    own_transfers,
):
    slot_count = master.shape[0]
    shards = lax.axis_size("fsdp")
    all_slots = slot_count * shards
    short_seqs, width = x_short.shape[:2]
    long_seqs = x_long.shape[0]
    short_tiles = short_seqs * width // TILE
    per_tile = TILE // width

    own = jnp.arange(slot_count, dtype=jnp.int32) + slot_count * lax.axis_index("fsdp")
    held = jnp.any(block_slot[None, :] == own[:, None], axis=1).astype(jnp.int32)
    if own_transfers:
        early_count = slot_count - LATE
        code, position, most = slot_codes(
            jnp.concatenate([block_slot, own]), block_slot[: 3 * 36], slot_count, shards
        )
        position = position[NBLK:]
        code = code[:NBLK]
        fits = most <= LATE
        gathered = gather_shards(master)
    else:
        gathered = lax.all_gather(master.astype(BF16), "fsdp", axis=0, tiled=True)
    w_qkv = assemble(block_slot, gathered)
    pieces = unpack(small_params)
    params = jnp.pad(small_params, (0, SMALL_ROWS * BLK - small_params.shape[0])).reshape(SMALL_ROWS, BLK)
    w_class = pieces[-2].reshape(SD, NCLS)
    b_class = pieces[-1].reshape(1, NCLS)
    x, *qkv, context, probs_short, probs_long = attention(
        len_short,
        len_long,
        x_short.reshape(-1, D),
        x_long.reshape(-1, D),
        params,
        w_qkv,
        short_tiles,
        width,
    )

    (
        enc_short,
        enc_long,
        logits_short,
        logits_long,
        first,
        active,
        d_up,
        d_down,
        d_branch,
        d_context,
        d_resid,
        g_student,
        g_hidden,
        g_small,
    ) = feed(
        len_short,
        len_long,
        block_slot,
        x,
        context,
        cot_short.reshape(-1, D),
        cot_long.reshape(-1, D),
        (logit_cot_short, logit_cot_long),
        (params, w_class, b_class),
        gathered,
        short_tiles,
        width,
    )
    g_out = left_product(context, d_branch).astype(BF16)
    others = (g_out, g_student.astype(BF16), g_hidden.astype(BF16))
    if own_transfers:
        terms = feed_grads(code, first, d_down, active, d_up, others, all_slots)
        *back, early_reduced = attention_back(
            qkv,
            probs_short,
            probs_long,
            d_context,
            x,
            short_tiles,
            terms.reshape(-1, BLK),
            early_count * BLK,
        )
    else:
        back = attention_back(qkv, probs_short, probs_long, d_context, x, short_tiles)
    d_qkv, g_b_query, g_b_value, x_turned = back

    def reduce_all():
        slot_terms = feed_grads(block_slot, first, d_down, active, d_up, others, all_slots)
        slot_terms, small_terms = input_weights(
            block_slot, x_turned, d_qkv, g_small, g_b_query, g_b_value, slot_terms
        )
        reduced = lax.psum_scatter(slot_terms, "fsdp", scatter_dimension=0, tiled=True)
        return lax.psum(reduced, "dp").reshape(-1, BLK), small_terms

    def renew(places, early, late):
        return update(
            places, held, early, late, master, left_stat, right_stat, left_root, right_root
        )

    def renew_all(blocks):
        return renew(jnp.arange(slot_count, dtype=jnp.int32), blocks, blocks)

    if own_transfers:
        terms, small_terms = input_weights(code, x_turned, d_qkv, g_small, g_b_query, g_b_value, terms)
        late_reduced, small_total, in_short, in_long = reduce_late(
            terms.reshape(-1, BLK),
            shards * early_count * BLK,
            LATE * BLK,
            small_terms,
            d_qkv,
            d_resid,
            w_qkv,
            short_tiles,
        )

        updated = lax.cond(
            fits,
            lambda: renew(position, early_reduced, late_reduced),
            lambda: renew_all(reduce_all()[0]),
        )
    else:
        in_short, in_long = input_grads(d_qkv, d_resid, w_qkv, short_tiles)
        blocks, small_terms = reduce_all()
        updated = renew_all(blocks)
        small_total = lax.psum(small_terms, ("dp", "fsdp"))
    slot_grad, new_left, new_right, new_master = updated
    small_grad = jnp.concatenate(
        [
            small_total[:CLASS_ROW].reshape(-1),
            small_total[CLASS_ROW : CLASS_ROW + NCLS].T.reshape(-1),
            small_total[LAST_ROW, :NCLS],
        ]
    )
    new_first = BETA_ONE * small_first + (1.0 - BETA_ONE) * small_grad
    new_second = BETA_TWO * small_second + (1.0 - BETA_TWO) * small_grad * small_grad
    first_hat = new_first / (1.0 - BETA_ONE**STEP)
    second_hat = new_second / (1.0 - BETA_TWO**STEP)
    new_small = small_params - ADAM_RATE * first_hat / (jnp.sqrt(second_hat) + ADAM_EPSILON)
    return (
        enc_short.reshape(x_short.shape),
        logits_short,
        enc_long.reshape(x_long.shape),
        logits_long,
        in_short.reshape(x_short.shape),
        in_long.reshape(x_long.shape),
        slot_grad,
        new_left,
        new_right,
        new_master,
        new_first,
        new_second,
        new_small,
    )


def solution(mesh):
    both = ("dp", "fsdp")
    placed = (
        P(both, None, None),
        P(both, None, None),
        P(both, None, None),
        P(both, None, None),
        P(both, None),
        P(both, None),
        P(both),
        P(both),
        P(),
        P("fsdp", None, None),
        P("fsdp", None, None),
        P("fsdp", None, None),
        P("fsdp", None, None),
        P("fsdp", None, None),
        P(),
        P(),
        P(),
    )
    return jax.shard_map(
        partial(body, own_transfers=(mesh.shape["dp"], mesh.shape["fsdp"]) == (4, 8)),
        mesh=mesh,
        in_specs=placed,
        out_specs=(
            P(both, None, None),
            P(both, None),
            P(both, None, None),
            P(both, None),
            P(both, None, None),
            P(both, None, None),
            P("fsdp", None, None),
            P("fsdp", None, None),
            P("fsdp", None, None),
            P("fsdp", None, None),
            P(),
            P(),
            P(),
        ),
        check_vma=False,
    )
```

```python
from functools import partial

import jax
import jax.numpy as jnp
from jax import lax
from jax.experimental import pallas as pl
from jax.experimental.pallas import tpu as pltpu
from jax.sharding import PartitionSpec as P

D = 768
HEADS = 12
FF = 3072
SD = 128
PH = 2
NCLS = 14
BLK = 128
STEP = 10
NBLK = 439
TILE = 512
PAIRS = 3
GROUPS = 2
CHUNK = 1024
LATE = 24

NORM_EPSILON = 1e-12
BETA_ONE = 0.9
BETA_TWO = 0.999
ADAM_EPSILON = 1e-08
ADAM_RATE = 0.1
MATRIX_RATE = 0.2
STAT_DECAY = 0.5
MASKED_SCORE = -1e30
MIB = 1024 * 1024
F32 = jnp.float32
BF16 = jnp.bfloat16

def product(former, latter, precision=None):
    return jnp.dot(former, latter, preferred_element_type=F32, precision=precision)


def left_product(former, latter, precision=None):
    return lax.dot_general(
        former, latter, (((0,), (0,)), ((), ())), preferred_element_type=F32, precision=precision
    )


def right_product(former, latter, precision=None):
    return lax.dot_general(
        former, latter, (((1,), (1,)), ((), ())), preferred_element_type=F32, precision=precision
    )


def unpack(small_values):
    widths = (D, D, D, D, D, FF, D, D, D, SD, SD, SD, SD * NCLS, NCLS)
    pieces = []
    offset = 0
    for column_count in widths:
        pieces.append(small_values[offset : offset + column_count])
        offset += column_count
    return pieces


def each_block(first, row_count, col_count, action):
    def one_row(index, carry):
        row = pl.multiple_of(index * BLK, BLK)
        for col in range(col_count):
            action(first + index * col_count + col, row, col * BLK)
        return carry

    lax.fori_loop(0, row_count, one_row, 0)


def load_blocks(slot_ref, blocks, target, sem, first, row_count, col_count, col_start=0):
    def move(block, row, col):
        pltpu.make_async_copy(
            blocks.at[slot_ref[block]],
            target.at[pl.ds(row, BLK), pl.ds(col + col_start * BLK, BLK)],
            sem,
        ).start()

    each_block(first, row_count, col_count, move)


def wait_whole(target, sem):
    pltpu.make_async_copy(target, target, sem).wait()


def assemble_kernel(slot_ref, blocks, out, sem):
    for which in range(3):
        load_blocks(slot_ref, blocks, out, sem, 36 * which, 6, 6, 6 * which)
    wait_whole(out, sem)


def assemble(block_slot, blocks):
    return pl.pallas_call(
        assemble_kernel,
        grid_spec=pltpu.PrefetchScalarGridSpec(
            num_scalar_prefetch=1,
            grid=(1,),
            in_specs=[pl.BlockSpec(memory_space=pltpu.HBM)],
            out_specs=pl.BlockSpec(memory_space=pltpu.VMEM),
            scratch_shapes=[pltpu.SemaphoreType.DMA],
        ),
        out_shape=jax.ShapeDtypeStruct((D, 3 * D), BF16),
        compiler_params=pltpu.CompilerParams(vmem_limit_bytes=60 * MIB),
        name="assemble",
    )(block_slot, blocks)


def join_small(small_ref, query_ref, value_ref, small_out):
    small_out[...] = small_ref[...]
    for start, ref in ((0, query_ref), (D // BLK, value_ref)):
        for index in range(D // BLK):
            small_out[start + index : start + index + 1, :] = ref[:, index * BLK : (index + 1) * BLK]


PART = 512
ACROSS = PART // BLK


def feed_grads_kernel(
    code_ref,
    first_turned,
    down_turned,
    active_ref,
    d_up_ref,
    g_out,
    g_student,
    g_hidden,
    terms,
    up_stage,
    down_stage,
    up_sems,
    down_sems,
    other_sems,
):
    step = pl.program_id(0)
    last = pl.num_programs(0) - 1
    slot = step % 2
    others = ((g_out, 108, 6, 6), (g_student, 432, 6, 1), (g_hidden, 438, 1, 1))

    @pl.when(step == 0)
    def _():
        for which, (grad, first, row_count, col_count) in enumerate(others):

            def move(block, row, col, which=which, grad=grad):
                pltpu.make_async_copy(
                    grad.at[pl.ds(row, BLK), pl.ds(col, BLK)], terms.at[code_ref[block]], other_sems.at[which]
                ).start()

            each_block(first, row_count, col_count, move)

    @pl.when(step >= 2)
    def _():
        wait_whole(up_stage.at[slot], up_sems.at[slot])
        wait_whole(down_stage.at[slot], down_sems.at[slot])

    up_stage[slot] = product(first_turned[...], d_up_ref[...]).astype(BF16)
    down_stage[slot] = product(down_turned[...], active_ref[...]).T.astype(BF16)
    for row in range(D // BLK):
        for col in range(ACROSS):
            pltpu.make_async_copy(
                up_stage.at[slot, pl.ds(row * BLK, BLK), pl.ds(col * BLK, BLK)],
                terms.at[code_ref[144 + row * (FF // BLK) + step * ACROSS + col]],
                up_sems.at[slot],
            ).start()
            pltpu.make_async_copy(
                down_stage.at[slot, pl.ds(col * BLK, BLK), pl.ds(row * BLK, BLK)],
                terms.at[code_ref[288 + (step * ACROSS + col) * (D // BLK) + row]],
                down_sems.at[slot],
            ).start()

    @pl.when(step == last)
    def _():
        for place in range(2):
            wait_whole(up_stage.at[place], up_sems.at[place])
            wait_whole(down_stage.at[place], down_sems.at[place])
        for which, (grad, *_) in enumerate(others):
            wait_whole(grad, other_sems.at[which])


def feed_grads(code, first, d_down, active, d_up, others, slot_count):
    tokens = first.shape[1]

    def whole(shape):
        return pl.BlockSpec(shape, lambda step, *_: (0, 0), pipeline_mode=pl.Buffered(1))

    part = pl.BlockSpec((tokens, PART), lambda step, *_: (0, step))
    return pl.pallas_call(
        feed_grads_kernel,
        grid_spec=pltpu.PrefetchScalarGridSpec(
            num_scalar_prefetch=1,
            grid=(FF // PART,),
            in_specs=[whole(first.shape), whole(d_down.shape), part, part]
            + [whole(other.shape) for other in others],
            out_specs=pl.BlockSpec(memory_space=pltpu.HBM),
            scratch_shapes=[
                pltpu.VMEM((2, D, PART), BF16),
                pltpu.VMEM((2, PART, D), BF16),
                pltpu.SemaphoreType.DMA((2,)),
                pltpu.SemaphoreType.DMA((2,)),
                pltpu.SemaphoreType.DMA((3,)),
            ],
        ),
        out_shape=jax.ShapeDtypeStruct((slot_count, BLK, BLK), BF16),
        compiler_params=pltpu.CompilerParams(vmem_limit_bytes=60 * MIB),
        cost_estimate=pl.CostEstimate(
            flops=4 * tokens * D * FF, bytes_accessed=50 * MIB, transcendentals=0
        ),
        name="feed_grads",
    )(code, first, d_down, active, d_up, *others)


def input_weights_kernel(
    code_ref, turned, d_ref, small_ref, query_ref, value_ref, _, terms, small_out, stage, sems
):
    step = pl.program_id(0)
    slot = step % 2

    @pl.when(step == 0)
    def _():
        join_small(small_ref, query_ref, value_ref, small_out)

    @pl.when(step >= 2)
    def _():
        wait_whole(stage.at[slot], sems.at[slot])

    stage[slot] = product(turned[...], d_ref[...]).astype(BF16)
    for row in range(D // BLK):
        for col in range(D // BLK):
            pltpu.make_async_copy(
                stage.at[slot, pl.ds(row * BLK, BLK), pl.ds(col * BLK, BLK)],
                terms.at[code_ref[36 * step + row * (D // BLK) + col]],
                sems.at[slot],
            ).start()

    @pl.when(step == pl.num_programs(0) - 1)
    def _():
        for place in range(2):
            wait_whole(stage.at[place], sems.at[place])


def input_weights(code, x, d_qkv, small, g_query, g_value, terms):
    tokens = x.shape[1]

    def whole(shape):
        return pl.BlockSpec(shape, lambda step, *_: (0, 0), pipeline_mode=pl.Buffered(1))

    hbm = pl.BlockSpec(memory_space=pltpu.HBM)
    return pl.pallas_call(
        input_weights_kernel,
        grid_spec=pltpu.PrefetchScalarGridSpec(
            num_scalar_prefetch=1,
            grid=(3,),
            in_specs=[
                whole(x.shape),
                pl.BlockSpec((tokens, D), lambda step, *_: (0, step)),
                whole(small.shape),
                whole(g_query.shape),
                whole(g_value.shape),
                hbm,
            ],
            out_specs=[hbm, pl.BlockSpec(small.shape, lambda step, *_: (0, 0))],
            scratch_shapes=[
                pltpu.VMEM((2, D, D), BF16),
                pltpu.SemaphoreType.DMA((2,)),
            ],
        ),
        out_shape=[
            jax.ShapeDtypeStruct(terms.shape, BF16),
            jax.ShapeDtypeStruct(small.shape, F32),
        ],
        input_output_aliases={6: 0},
        compiler_params=pltpu.CompilerParams(vmem_limit_bytes=60 * MIB),
        cost_estimate=pl.CostEstimate(
            flops=6 * tokens * D * D, bytes_accessed=16 * MIB, transcendentals=0
        ),
        name="input_weights",
    )(code, x, d_qkv, small, g_query, g_value, terms)


def half_masks():
    lane = lax.broadcasted_iota(jnp.int32, (1, BLK), 1)
    low = (lane < BLK // 2).astype(BF16)
    return low, (1.0 - low.astype(F32)).astype(BF16)


def stack_heads(values, low, high):
    return jnp.concatenate([values * low, values * high], axis=0)


def pick_heads(values):
    rows = values.shape[0] // 2
    lane = lax.broadcasted_iota(jnp.int32, (rows, BLK), 1)
    return jnp.where(lane < BLK // 2, values[:rows], values[rows:])


def pipelined(count, before, middle, after):
    started = before(0)
    done = None
    for index in range(count):
        current = started
        if index + 1 < count:
            started = before(index + 1)
        if done is not None:
            after(index - 1, done)
        done = middle(index, current)
    after(count - 1, done)


def softmax(scores, length):
    visible = lax.broadcasted_iota(jnp.int32, scores.shape, 1) < length
    scores = jnp.where(visible, scores, MASKED_SCORE)
    powers = jnp.exp(scores - jnp.max(scores, axis=-1, keepdims=True))
    total = jnp.sum(powers, axis=-1, keepdims=True)
    return (powers * (1.0 / total)).astype(BF16)


def attention_kernel(
    len_short,
    len_long,
    x_short_ref,
    x_long_ref,
    params,
    w_ref,
    x_ref,
    q_ref,
    k_ref,
    v_ref,
    context_ref,
    short_ref,
    long_ref,
    bias,
    *,
    short_tiles,
):
    tile = pl.program_id(0)
    group = pl.program_id(1)
    low, high = half_masks()
    width = short_ref.shape[-1]
    per_tile = TILE // width

    wide = PAIRS * BLK
    start = pl.multiple_of(group * wide, wide)

    @pl.when((tile == 0) & (group == 0))
    def _():
        for which in range(2):
            for place in range(D // BLK):
                row = which * (D // BLK) + place
                bias[which : which + 1, place * BLK : (place + 1) * BLK] = params[row : row + 1, :]

    @pl.when((tile < short_tiles) & (group == 0))
    def _():
        x_ref[...] = x_short_ref[...]

    @pl.when((tile >= short_tiles) & (group == 0))
    def _():
        x_ref[...] = x_long_ref[...]

    @pl.when(group == 0)
    def _():
        rows_in = x_ref[...]
        queries = product(rows_in, w_ref[:, :D]) + bias[0:1, :]
        q_ref[...] = (queries * 0.125).astype(BF16)
        k_ref[...] = product(rows_in, w_ref[:, D : 2 * D]).astype(BF16)
        v_ref[...] = (product(rows_in, w_ref[:, 2 * D :]) + bias[1:2, :]).astype(BF16)

    def inner(pair):
        return pl.ds(pl.multiple_of(start + pair * BLK, BLK), BLK)

    def attend(units, kept_ref):
        def scores(index):
            rows, keys, pair, _, _ = units[index]
            return right_product(stack_heads(q_ref[rows, inner(pair)], low, high), k_ref[keys, inner(pair)])

        def weigh(index, values):
            _, _, _, length, place = units[index]
            probs = softmax(values, length)
            kept_ref[place] = probs
            return probs

        def mix(index, probs):
            rows, keys, pair, _, _ = units[index]
            mixed = pick_heads(product(probs, v_ref[keys, inner(pair)])).astype(BF16)
            context_ref[rows, pair * BLK : (pair + 1) * BLK] = mixed

        pipelined(len(units), scores, weigh, mix)

    @pl.when(tile < short_tiles)
    def _():
        units = []
        for seq in range(per_tile):
            rows = slice(seq * width, (seq + 1) * width)
            length = len_short[tile * per_tile + seq]
            for pair in range(PAIRS):
                units.append((rows, rows, pair, length, (0, pair, seq)))
        attend(units, short_ref)

    @pl.when(tile >= short_tiles)
    def _():
        length = len_long[tile - short_tiles]
        half = TILE // 2
        units = []
        for pair in range(PAIRS):
            for part in range(2):
                rows = slice(part * half, (part + 1) * half)
                units.append((rows, slice(0, TILE), pair, length, (0, pair, part)))
        attend(units, long_ref)


def run_events(step, events):
    for index, actions in enumerate(events):

        @pl.when(step == index)
        def _(actions=actions):
            for action in actions:
                action()


def probs_shapes(short_tiles, long_tiles, width):
    per_tile = TILE // width
    return (
        (short_tiles, 2 * PAIRS, per_tile, 2 * width, width),
        (long_tiles, 2 * PAIRS, 2, TILE, TILE),
    )


def short_index(tile, short_tiles):
    return jnp.minimum(tile, short_tiles - 1)


def long_index(tile, short_tiles):
    return jnp.maximum(tile - short_tiles, 0)


def probs_maps(short_tiles):
    def short_map(tile, group):
        last = jnp.minimum(tile // short_tiles, 1)
        return (short_index(tile, short_tiles), group + last * (GROUPS - 1 - group), 0, 0, 0)

    def long_map(tile, group):
        begun = jnp.minimum(tile // short_tiles, 1)
        return (long_index(tile, short_tiles), begun * group, 0, 0, 0)

    return short_map, long_map


def attention(len_short, len_long, x_short, x_long, params, w_qkv, short_tiles, width):
    tiles = (x_short.shape[0] + x_long.shape[0]) // TILE
    wide = PAIRS * BLK
    short_shape, long_shape = probs_shapes(short_tiles, tiles - short_tiles, width)
    short_map, long_map = probs_maps(short_tiles)
    flops = 4 * D * TILE * TILE * tiles + 6 * D * D * TILE * tiles
    rows = pl.BlockSpec((TILE, wide), lambda tile, group: (tile, group))
    scalars = pl.BlockSpec(memory_space=pltpu.SMEM)

    def whole(shape):
        return pl.BlockSpec(shape, lambda tile, group: (0,) * len(shape), pipeline_mode=pl.Buffered(1))

    in_specs = [
        scalars,
        scalars,
        pl.BlockSpec((TILE, D), lambda tile, group: (short_index(tile, short_tiles), 0)),
        pl.BlockSpec((TILE, D), lambda tile, group: (long_index(tile, short_tiles), 0)),
        whole(params.shape),
        whole((D, 3 * D)),
    ]
    full_rows = pl.BlockSpec((TILE, D), lambda tile, group: (tile, 0))
    out_specs = [
        full_rows,
        full_rows,
        full_rows,
        full_rows,
        rows,
        pl.BlockSpec((1, PAIRS) + short_shape[2:], short_map),
        pl.BlockSpec((1, PAIRS) + long_shape[2:], long_map),
    ]
    out_shape = [jax.ShapeDtypeStruct((tiles * TILE, D), BF16)] * 5 + [
        jax.ShapeDtypeStruct(short_shape, BF16),
        jax.ShapeDtypeStruct(long_shape, BF16),
    ]
    arguments = [len_short, len_long, x_short, x_long, params, w_qkv]
    return pl.pallas_call(
        partial(attention_kernel, short_tiles=short_tiles),
        grid=(tiles, GROUPS),
        in_specs=in_specs,
        out_specs=out_specs,
        out_shape=out_shape,
        scratch_shapes=[pltpu.VMEM((8, D), F32)],
        compiler_params=pltpu.CompilerParams(vmem_limit_bytes=60 * MIB),
        cost_estimate=pl.CostEstimate(
            flops=flops, bytes_accessed=35 * MIB, transcendentals=HEADS * TILE * TILE * tiles // 2
        ),
        name="attention",
    )(*arguments)


def attention_back_kernel(*refs, short_tiles, transfers):
    q_ref, k_ref, v_ref, short_ref, long_ref, dc_ref, x_ref = refs[:7]
    refs = refs[7:]
    if transfers:
        terms_ref, refs = refs[0], refs[1:]
    out_ref, bq_ref, bv_ref, turned_ref = refs[:4]
    tile = pl.program_id(0)
    group = pl.program_id(1)
    low, high = half_masks()
    width = short_ref.shape[-1]
    per_tile = TILE // width
    if transfers:
        reduce = Reduce(terms_ref, 0, refs[4], refs[5:])
        run_events(
            tile * GROUPS + group,
            (
                (reduce.start,),
                (partial(reduce.core, 0),),
                (partial(reduce.core, 1), partial(reduce.first, 0)),
                (partial(reduce.core, 2), partial(reduce.first, 1), partial(reduce.second, 0)),
                (partial(reduce.core, 3), partial(reduce.first, 2), partial(reduce.second, 1)),
                (partial(reduce.first, 3), partial(reduce.second, 2)),
                (partial(reduce.second, 3), reduce.share),
                (reduce.share_on,),
            ),
        )

    wide = PAIRS * BLK
    start = pl.multiple_of(group * wide, wide)

    def columns(which, cols):
        return pl.ds(pl.multiple_of(which * D + start + cols.start, BLK), BLK)

    def go_back(units, kept_ref, parts):
        sums = {}

        def spread_in(index):
            rows, keys, cols, _ = units[index]
            return right_product(stack_heads(dc_ref[rows, cols], low, high), v_ref[keys, cols])

        def differ(index, d_probs):
            wide = kept_ref[units[index][3]].astype(F32)
            weighted = wide * d_probs
            return (weighted - wide * jnp.sum(weighted, axis=-1, keepdims=True)).astype(BF16)

        def gather_up(index, d_scores):
            rows, keys, cols, place = units[index]
            d_queries = pick_heads(product(d_scores, k_ref[keys, cols])) * 0.125
            out_ref[rows, columns(0, cols)] = d_queries.astype(BF16)
            d_keys = left_product(d_scores, stack_heads(q_ref[rows, cols], low, high))
            d_values = left_product(kept_ref[place], stack_heads(dc_ref[rows, cols], low, high))
            if index % parts:
                d_keys += sums["keys"]
                d_values += sums["values"]
            if index % parts == parts - 1:
                out_ref[keys, columns(1, cols)] = d_keys.astype(BF16)
                out_ref[keys, columns(2, cols)] = d_values.astype(BF16)
            else:
                sums.update(keys=d_keys, values=d_values)

        pipelined(len(units), spread_in, differ, gather_up)

    @pl.when(tile < short_tiles)
    def _():
        units = []
        for seq in range(per_tile):
            rows = slice(seq * width, (seq + 1) * width)
            for pair in range(PAIRS):
                cols = slice(pair * BLK, (pair + 1) * BLK)
                units.append((rows, rows, cols, (0, pair, seq)))
        go_back(units, short_ref, 1)

    @pl.when(tile >= short_tiles)
    def _():
        half = TILE // 2
        units = []
        for pair in range(PAIRS):
            cols = slice(pair * BLK, (pair + 1) * BLK)
            for part in range(2):
                rows = slice(part * half, (part + 1) * half)
                units.append((rows, slice(0, TILE), cols, (0, pair, part)))
        go_back(units, long_ref, 2)

    @pl.when(group == 0)
    def _():
        turned_ref[...] = x_ref[...].T

    @pl.when((tile == 0) & (group == 0))
    def _():
        bq_ref[...] = jnp.zeros_like(bq_ref)
        bv_ref[...] = jnp.zeros_like(bv_ref)

    bq_ref[:, pl.ds(start, wide)] += column_sum(out_ref[:, pl.ds(start, wide)])
    bv_ref[:, pl.ds(start, wide)] += column_sum(out_ref[:, pl.ds(2 * D + start, wide)])

    if transfers:

        @pl.when((tile == pl.num_programs(0) - 1) & (group == GROUPS - 1))
        def _():
            reduce.finish()


def attention_back(qkv, probs_short, probs_long, d_context, x, short_tiles, terms=None, count=0):
    tiles = d_context.shape[0] // TILE
    wide = PAIRS * BLK
    short_map, long_map = probs_maps(short_tiles)
    rows = pl.BlockSpec((TILE, wide), lambda tile, group: (tile, group))
    row = pl.BlockSpec((1, D), lambda tile, group: (0, 0))
    flops = 10 * D * TILE * TILE * tiles
    in_specs = [
        rows,
        rows,
        rows,
        pl.BlockSpec((1, PAIRS) + probs_short.shape[2:], short_map),
        pl.BlockSpec((1, PAIRS) + probs_long.shape[2:], long_map),
        rows,
        pl.BlockSpec((TILE, D), lambda tile, group: (tile, 0)),
    ]
    out_specs = [
        pl.BlockSpec((TILE, 3 * D), lambda tile, group: (tile, 0)),
        row,
        row,
        pl.BlockSpec((D, TILE), lambda tile, group: (0, tile)),
    ]
    out_shape = [
        jax.ShapeDtypeStruct((tiles * TILE, 3 * D), BF16),
        jax.ShapeDtypeStruct((1, D), F32),
        jax.ShapeDtypeStruct((1, D), F32),
        jax.ShapeDtypeStruct((D, tiles * TILE), BF16),
    ]
    arguments = [*qkv, probs_short, probs_long, d_context, x]
    scratch = []
    params = dict(vmem_limit_bytes=60 * MIB)
    if terms is not None:
        arguments.append(terms)
        in_specs.append(pl.BlockSpec(memory_space=pltpu.HBM))
        out_specs.append(pl.BlockSpec((count, BLK), lambda tile, group: (0, 0)))
        out_shape.append(jax.ShapeDtypeStruct((count, BLK), BF16))
        scratch = reduce_scratch(count)
        params.update(collective_id=2, has_side_effects=True)
    return pl.pallas_call(
        partial(attention_back_kernel, short_tiles=short_tiles, transfers=terms is not None),
        grid=(tiles, GROUPS),
        in_specs=in_specs,
        out_specs=out_specs,
        out_shape=out_shape,
        scratch_shapes=scratch,
        compiler_params=pltpu.CompilerParams(**params),
        cost_estimate=pl.CostEstimate(flops=flops, bytes_accessed=50 * MIB, transcendentals=0),
        name="attention_back",
    )(*arguments)


INPUT_ROWS = 256


def input_product(d_ref, resid_ref, w_ref, short_ref, long_ref, short_steps):
    step = pl.program_id(0)
    total = resid_ref[...] + right_product(d_ref[...], w_ref[...])

    @pl.when(step < short_steps)
    def _():
        short_ref[...] = total

    @pl.when(step >= short_steps)
    def _():
        long_ref[...] = total


def input_specs(short_steps):
    rows = [pl.BlockSpec((INPUT_ROWS, width), lambda step: (step, 0)) for width in (3 * D, D)]
    whole = pl.BlockSpec((D, 3 * D), lambda step: (0, 0), pipeline_mode=pl.Buffered(1))
    outs = [
        pl.BlockSpec((INPUT_ROWS, D), lambda step: (short_index(step, short_steps), 0)),
        pl.BlockSpec((INPUT_ROWS, D), lambda step: (long_index(step, short_steps), 0)),
    ]
    return rows + [whole], outs


def input_grads(d_qkv, resid, w_qkv, short_tiles):
    steps = resid.shape[0] // INPUT_ROWS
    short_steps = short_tiles * TILE // INPUT_ROWS
    in_specs, out_specs = input_specs(short_steps)
    return pl.pallas_call(
        partial(input_product, short_steps=short_steps),
        grid=(steps,),
        in_specs=in_specs,
        out_specs=out_specs,
        out_shape=[
            jax.ShapeDtypeStruct((short_steps * INPUT_ROWS, D), F32),
            jax.ShapeDtypeStruct(((steps - short_steps) * INPUT_ROWS, D), F32),
        ],
        compiler_params=pltpu.CompilerParams(vmem_limit_bytes=60 * MIB),
        name="input_grads",
    )(d_qkv, resid, w_qkv)


def normal_parts(values):
    below = 0.5 * lax.erf(values * 0.7071067811865476) + 0.5
    return below, jnp.exp(-0.5 * values * values) * 0.3989422804014327


B_OUT, GAIN_ONE, SHIFT_ONE, B_UP, B_DOWN, GAIN_TWO, SHIFT_TWO, B_STUDENT, POOL_QUERY, B_HIDDEN = range(10)
VECTORS = (
    (12, 6),
    (18, 6),
    (24, 6),
    (30, 24),
    (54, 6),
    (60, 6),
    (66, 6),
    (72, 1),
    (73, 1),
    (74, 1),
)
CLASS_ROW = 75
LAST_ROW = 91
SMALL_ROWS = 96


def norm_parts(values):
    center = values - jnp.mean(values, axis=-1, keepdims=True)
    spread = jnp.mean(center * center, axis=-1, keepdims=True)
    inverse = lax.rsqrt(spread + NORM_EPSILON)
    return center * inverse, inverse


def norm_back(d_values, gain, unit, inverse):
    d_unit = d_values * gain
    return inverse * (
        d_unit
        - jnp.mean(d_unit, axis=-1, keepdims=True)
        - unit * jnp.mean(d_unit * unit, axis=-1, keepdims=True)
    )


def column_sum(values):
    return jnp.sum(values.astype(F32), axis=0, keepdims=True)


def pool_weights(student, query, length):
    scaled = student * query
    lane = lax.broadcasted_iota(jnp.int32, scaled.shape, 1)
    place = lax.broadcasted_iota(jnp.int32, (scaled.shape[0], 1), 0)
    weights = []
    for side in (lane < SD // PH, lane >= SD // PH):
        scores = jnp.sum(jnp.where(side, scaled, 0.0), axis=-1, keepdims=True)
        scores = jnp.where(place < length, scores, MASKED_SCORE)
        powers = jnp.exp(scores - jnp.max(scores, axis=0, keepdims=True))
        weights.append(powers / jnp.sum(powers, axis=0, keepdims=True))
    return jnp.where(lane < SD // PH, weights[0], weights[1]), weights


def student_back(student, query, weights, both, d_pooled):
    lane = lax.broadcasted_iota(jnp.int32, student.shape, 1)
    moved = student * d_pooled
    d_scores = []
    for side, weight in zip((lane < SD // PH, lane >= SD // PH), weights):
        d_weight = jnp.sum(jnp.where(side, moved, 0.0), axis=-1, keepdims=True)
        d_scores.append(weight * (d_weight - jnp.sum(weight * d_weight, axis=0, keepdims=True)))
    d_score = jnp.where(lane < SD // PH, d_scores[0], d_scores[1])
    d_query = jnp.sum(d_score * student, axis=0, keepdims=True) * 0.125
    return both * d_pooled + d_score * query, d_query


def feed_kernel(
    len_short,
    len_long,
    slot_ref,
    x_ref,
    context_ref,
    cot_short_ref,
    cot_long_ref,
    logit_cot_short,
    logit_cot_long,
    params,
    w_class_ref,
    b_class_ref,
    blocks,
    enc_short_ref,
    enc_long_ref,
    logits_short,
    logits_long,
    first_ref,
    active_ref,
    d_up_ref,
    d_down_ref,
    d_branch_ref,
    d_context_ref,
    d_resid_ref,
    g_student,
    g_hidden,
    g_small,
    slope,
    pooled_ref,
    d_student_ref,
    w_out,
    w_up,
    w_down,
    w_student,
    w_hidden,
    vectors,
    totals,
    g_class,
    g_last,
    w_class,
    b_class,
    logit_cot,
    sems,
    *,
    short_tiles,
    width,
):
    tile = pl.program_id(0)
    per_tile = TILE // width
    loads = ((w_out, 108, 6, 6), (w_up, 144, 6, 24), (w_down, 288, 24, 6), (w_student, 432, 6, 1), (w_hidden, 438, 1, 1))

    def arrive(*indices):
        @pl.when(tile == 0)
        def _():
            for index in indices:
                wait_whole(loads[index][0], sems.at[index])

    @pl.when(tile == 0)
    def _():
        for index, (target, block, row_count, col_count) in enumerate(loads):
            load_blocks(slot_ref, blocks, target, sems.at[index], block, row_count, col_count)
        for index, (start, count) in enumerate(VECTORS):
            for place in range(count):
                vectors[index : index + 1, place * BLK : (place + 1) * BLK] = params[
                    start + place : start + place + 1, :
                ]
        for ref in (totals, g_class, g_last, g_student, g_hidden, w_class, b_class):
            ref[...] = jnp.zeros_like(ref)
        w_class[:, :NCLS] = w_class_ref[...]
        b_class[:, :NCLS] = b_class_ref[...]

    def vector(index):
        return vectors[index : index + 1, : VECTORS[index][1] * BLK]

    def add_total(index, values):
        totals[index : index + 1, : VECTORS[index][1] * BLK] += column_sum(values)

    arrive(0)
    sides = [slice(start, start + TILE // 2) for start in range(0, TILE, TILE // 2)]
    units_one, inverses_one, firsts = [], [], []

    def branch(index):
        return product(context_ref[sides[index]], w_out[...])

    def norm_first(index, values):
        rows = sides[index]
        unit, inverse = norm_parts(x_ref[rows].astype(F32) + (values + vector(B_OUT)))
        units_one.append(unit)
        inverses_one.append(inverse)
        firsts.append((unit * vector(GAIN_ONE) + vector(SHIFT_ONE)).astype(BF16))
        first_ref[:, rows] = firsts[-1].T

    pipelined(2, branch, norm_first, lambda *_: None)
    first = jnp.concatenate(firsts, axis=0)
    arrive(1)
    chunks = [slice(start, start + CHUNK) for start in range(0, FF, CHUNK)]

    def rise(index):
        return product(first, w_up[:, chunks[index]])

    def bend(index, upward):
        upward = upward + vectors[B_UP : B_UP + 1, chunks[index]]
        below, density = normal_parts(upward)
        active_ref[:, chunks[index]] = (upward * below).astype(BF16)
        slope[:, chunks[index]] = (below + upward * density).astype(BF16)

    pipelined(len(chunks), rise, bend, lambda *_: None)
    arrive(2, 3, 4)
    units_two, inverses_two, encodeds = [], [], []

    def sink(index):
        return product(active_ref[sides[index]], w_down[...])

    def norm_second(index, values):
        unit, inverse = norm_parts(firsts[index].astype(F32) + (values + vector(B_DOWN)))
        units_two.append(unit)
        inverses_two.append(inverse)
        encodeds.append((unit * vector(GAIN_TWO) + vector(SHIFT_TWO)).astype(BF16))

    pipelined(2, sink, norm_second, lambda *_: None)
    encoded = jnp.concatenate(encodeds, axis=0)

    @pl.when(tile < short_tiles)
    def _():
        enc_short_ref[...] = encoded

    @pl.when(tile >= short_tiles)
    def _():
        enc_long_ref[...] = encoded

    student = product(encoded, w_student[...]) + vector(B_STUDENT)
    query = vector(POOL_QUERY) * 0.125
    pooled_ref[...] = jnp.zeros_like(pooled_ref)

    def head():
        pooled = pooled_ref[...]
        wide_hidden = w_hidden[...].astype(F32)
        hidden = jnp.tanh(product(pooled, wide_hidden) + vector(B_HIDDEN))
        logits = product(hidden, w_class[...]) + b_class[...]
        d_logits = logit_cot[...]
        g_last[...] += column_sum(d_logits)
        g_class[...] += left_product(d_logits, hidden)
        d_hidden = right_product(d_logits, w_class[...])
        d_hidden = d_hidden * (1.0 - hidden * hidden)
        add_total(B_HIDDEN, d_hidden)
        g_hidden[...] += left_product(pooled, d_hidden)
        return logits, right_product(d_hidden, wide_hidden)

    def pool(starts, size, lengths, cot_ref, logits_ref, first):
        count = len(starts)
        logit_cot[...] = jnp.zeros_like(logit_cot)
        for index in range(count):
            logit_cot[index : index + 1, :NCLS] = cot_ref[pl.ds(first + index, 1), :]
        kept = []
        for index, (start, length) in enumerate(zip(starts, lengths)):
            rows = student[start : start + size]
            both, weights = pool_weights(rows, query, length)
            pooled_ref[index : index + 1, :] = column_sum(both * rows)
            kept.append((start, rows, both, weights))
        logits, d_pooled = head()
        for index in range(count):
            logits_ref[pl.ds(first + index, 1), :] = logits[index : index + 1, :NCLS]
        for index, (start, rows, both, weights) in enumerate(kept):
            d_rows, d_query = student_back(rows, query, weights, both, d_pooled[index : index + 1])
            d_student_ref[start : start + size, :] = d_rows.astype(BF16)
            add_total(POOL_QUERY, d_query)

    @pl.when(tile < short_tiles)
    def _():
        pool(
            [seq * width for seq in range(per_tile)],
            width,
            [len_short[tile * per_tile + seq] for seq in range(per_tile)],
            logit_cot_short,
            logits_short,
            tile * per_tile,
        )

    @pl.when(tile >= short_tiles)
    def _():
        long = tile - short_tiles
        pool([0], TILE, [len_long[long]], logit_cot_long, logits_long, long)

    d_student = d_student_ref[...]
    add_total(B_STUDENT, d_student)
    g_student[...] += left_product(encoded, d_student)
    d_resids, d_downs = [], []

    def through_student(index):
        return right_product(d_student[sides[index]], w_student[...])

    def norm_second_back(index, values):
        rows = sides[index]
        cotangent = jnp.where(tile < short_tiles, cot_short_ref[rows], cot_long_ref[rows])
        d_second = cotangent.astype(F32) + values
        add_total(GAIN_TWO, d_second * units_two[index])
        add_total(SHIFT_TWO, d_second)
        d_resids.append(norm_back(d_second, vector(GAIN_TWO), units_two[index], inverses_two[index]))
        d_downs.append(d_resids[-1].astype(BF16))
        d_down_ref[:, rows] = d_downs[-1].T
        add_total(B_DOWN, d_downs[-1])

    pipelined(2, through_student, norm_second_back, lambda *_: None)
    d_down = jnp.concatenate(d_downs, axis=0)

    def fall(index):
        return right_product(d_down, w_down[chunks[index], :])

    def bend_back(index, d_active):
        d_up = (d_active * slope[:, chunks[index]].astype(F32)).astype(BF16)
        d_up_ref[:, chunks[index]] = d_up
        totals[B_UP : B_UP + 1, chunks[index]] += column_sum(d_up)

    pipelined(len(chunks), fall, bend_back, lambda *_: None)

    def rise_back(index):
        return right_product(d_up_ref[sides[index]], w_up[...])

    def norm_first_back(index, values):
        rows = sides[index]
        d_first = d_resids[index] + values
        add_total(GAIN_ONE, d_first * units_one[index])
        add_total(SHIFT_ONE, d_first)
        d_resid = norm_back(d_first, vector(GAIN_ONE), units_one[index], inverses_one[index])
        d_resid_ref[rows] = d_resid
        d_branch = d_resid.astype(BF16)
        d_branch_ref[rows] = d_branch
        add_total(B_OUT, d_branch)
        return d_branch

    def branch_back(index, d_branch):
        d_context_ref[sides[index]] = right_product(d_branch, w_out[...]).astype(BF16)

    pipelined(2, rise_back, norm_first_back, branch_back)

    @pl.when(tile == pl.num_programs(0) - 1)
    def _():
        g_small[...] = jnp.zeros_like(g_small)
        for index, (start, count) in enumerate(VECTORS):
            for place in range(count):
                g_small[start + place : start + place + 1, :] = totals[
                    index : index + 1, place * BLK : (place + 1) * BLK
                ]
        g_small[CLASS_ROW : CLASS_ROW + NCLS, :] = g_class[:NCLS, :]
        g_small[LAST_ROW : LAST_ROW + 1, :] = g_last[...]


def feed(
    len_short, len_long, block_slot, x, context, cot_short, cot_long, logit_cots, small, blocks, short_tiles, width
):
    tiles = x.shape[0] // TILE
    long_tiles = tiles - short_tiles

    def whole(shape):
        return pl.BlockSpec(shape, lambda tile, *_: (0,) * len(shape), pipeline_mode=pl.Buffered(1))

    def kept(shape):
        return pl.BlockSpec(shape, lambda tile, *_: (0,) * len(shape))

    def rows(columns):
        return pl.BlockSpec((TILE, columns), lambda tile, *_: (tile, 0))

    turned = pl.BlockSpec((D, TILE), lambda tile, *_: (0, tile))
    short_rows = pl.BlockSpec((TILE, D), lambda tile, *_: (short_index(tile, short_tiles), 0))
    long_rows = pl.BlockSpec((TILE, D), lambda tile, *_: (long_index(tile, short_tiles), 0))
    grad_shapes = ((D, SD), (SD, SD), (SMALL_ROWS, BLK))
    total = tiles * TILE
    return pl.pallas_call(
        partial(feed_kernel, short_tiles=short_tiles, width=width),
        grid_spec=pltpu.PrefetchScalarGridSpec(
            num_scalar_prefetch=3,
            grid=(tiles,),
            in_specs=[rows(D), rows(D), short_rows, long_rows]
            + [whole(array.shape) for array in (*logit_cots, *small)]
            + [pl.BlockSpec(memory_space=pltpu.HBM)],
            out_specs=[
                short_rows,
                long_rows,
                kept(logit_cots[0].shape),
                kept(logit_cots[1].shape),
                turned,
                rows(FF),
                rows(FF),
                turned,
                rows(D),
                rows(D),
                rows(D),
            ]
            + [kept(shape) for shape in grad_shapes],
            scratch_shapes=[
                pltpu.VMEM((TILE, FF), BF16),
                pltpu.VMEM((8, SD), F32),
                pltpu.VMEM((TILE, SD), BF16),
                pltpu.VMEM((D, D), BF16),
                pltpu.VMEM((D, FF), BF16),
                pltpu.VMEM((FF, D), BF16),
                pltpu.VMEM((D, SD), BF16),
                pltpu.VMEM((SD, SD), BF16),
                pltpu.VMEM((16, FF), F32),
                pltpu.VMEM((16, FF), F32),
                pltpu.VMEM((SD, SD), F32),
                pltpu.VMEM((1, SD), F32),
                pltpu.VMEM((SD, SD), F32),
                pltpu.VMEM((1, SD), F32),
                pltpu.VMEM((8, SD), F32),
                pltpu.SemaphoreType.DMA((5,)),
            ],
        ),
        out_shape=[
            jax.ShapeDtypeStruct((short_tiles * TILE, D), BF16),
            jax.ShapeDtypeStruct((long_tiles * TILE, D), BF16),
            jax.ShapeDtypeStruct(logit_cots[0].shape, F32),
            jax.ShapeDtypeStruct(logit_cots[1].shape, F32),
            jax.ShapeDtypeStruct((D, total), BF16),
            jax.ShapeDtypeStruct((total, FF), BF16),
            jax.ShapeDtypeStruct((total, FF), BF16),
            jax.ShapeDtypeStruct((D, total), BF16),
            jax.ShapeDtypeStruct((total, D), BF16),
            jax.ShapeDtypeStruct((total, D), BF16),
            jax.ShapeDtypeStruct((total, D), F32),
        ]
        + [jax.ShapeDtypeStruct(shape, F32) for shape in grad_shapes],
        compiler_params=pltpu.CompilerParams(vmem_limit_bytes=62 * MIB),
        cost_estimate=pl.CostEstimate(
            flops=total * (8 * D * FF + 4 * D * D), bytes_accessed=70 * MIB, transcendentals=total * FF
        ),
        name="feed",
    )(len_short, len_long, block_slot, x, context, cot_short, cot_long, *logit_cots, *small, blocks)


class Place:
    def __init__(self):
        self.quarter = lax.axis_index("dp")
        self.shard = lax.axis_index("fsdp")
        x = self.quarter % 2
        y = self.quarter // 2
        self.core = self.shard % 2
        self.z = self.shard // 2
        self.high = self.z // 2
        self.by_x = 2 * y + 1 - x
        self.by_y = 2 * (1 - y) + x
        self.across = 2 * (1 - y) + 1 - x
        self.sibling = (self.quarter, 2 * self.z + 1 - self.core)
        self.next_x = (self.by_x, self.shard)
        self.next_y = (self.by_y, self.shard)
        self.inner = (self.z > 0) & (self.z < 3)

    def at_z(self, z):
        return (self.quarter, 2 * z + self.core)


def transfer(source, target, send_sem, recv_sem, device):
    return pltpu.make_async_remote_copy(
        src_ref=source,
        dst_ref=target,
        send_sem=send_sem,
        recv_sem=recv_sem,
        device_id=device,
        device_id_type=pl.DeviceIdType.MESH,
    )


def greet(place, extra=()):
    barrier = pltpu.get_barrier_semaphore()

    def signal(device):
        pl.semaphore_signal(barrier, inc=1, device_id=device, device_id_type=pl.DeviceIdType.MESH)

    near = (place.sibling, place.next_x, place.next_y) + tuple(extra)
    for device in near:
        signal(device)

    @pl.when(place.z > 0)
    def _():
        signal(place.at_z(place.z - 1))

    @pl.when(place.z < 3)
    def _():
        signal(place.at_z(place.z + 1))

    pl.semaphore_wait(barrier, len(near) + 1 + (place.z + 1) // 2 % 2)


CUTS = 2
GATHER_SEMAPHORES = [
    pltpu.SemaphoreType.DMA((2 * CUTS,)),
    pltpu.SemaphoreType.DMA((3 * CUTS,)),
    pltpu.SemaphoreType.DMA((4 * CUTS,)),
    pltpu.SemaphoreType.DMA((12 * CUTS,)),
    pltpu.SemaphoreType.DMA((12 * CUTS,)),
    pltpu.SemaphoreType.DMA((1 + 18 * CUTS,)),
    pltpu.SemaphoreType.DMA((1 + 18 * CUTS,)),
    pltpu.SemaphoreType.DMA((8,)),
    pltpu.SemaphoreType.DMA((2 * CUTS,)),
    pltpu.SemaphoreType.DMA((3 * CUTS,)),
    pltpu.SemaphoreType.DMA((4 * CUTS,)),
]


class Gather:
    def __init__(self, full, out, sems):
        self.place = place = Place()
        self.full, self.out = full, out
        (
            self.own_send,
            self.relay_send,
            self.z_recv,
            self.xy_send,
            self.xy_recv,
            self.core_send,
            self.core_recv,
            self.out_sems,
            self.own_more,
            self.relay_more,
            self.z_more,
        ) = sems
        self.quarter = full.shape[1] // 4
        self.cut = self.quarter // CUTS
        self.z_part = self.cut // 64 * 16
        self.first_part = ((self.cut - self.z_part) // 16 + 1) // 2 * 16
        self.last_part = self.cut - self.z_part - self.first_part
        z = place.z
        self.origins = (z + 1 - 2 * (z % 2), 2 - place.high, 3 * (1 - place.high))
        self.relays = (3 - z, 3 * (z - 1), 3 * (z - 1))

    def region(self, which, start, size):
        return self.full.at[which, pl.ds(pl.multiple_of(start, 16), size)]

    def pieces(self, which, turn):
        place, quarter, cut, part = self.place, self.quarter, self.cut, self.first_part
        skip = turn % CUTS * cut
        return (
            self.region(which, place.quarter * quarter + skip, cut),
            self.region(which, place.by_x * quarter + skip, cut),
            self.region(which, place.by_y * quarter + skip, cut),
            self.region(which, place.across * quarter + skip, part),
            self.region(which, place.across * quarter + skip + part, self.last_part),
            self.region(which, place.across * quarter + skip + cut - self.z_part, self.z_part),
        )

    def own_copy(self, side, cut, more=False):
        place = self.place
        mine = self.pieces(place.shard, cut)[5 if more else 0]
        device = place.at_z(place.z - 1 + 2 * side)
        send, recv = (self.own_more, self.z_more) if more else (self.own_send, self.z_recv)
        return transfer(
            mine, mine, send.at[side * CUTS + cut], recv.at[place.z * CUTS + cut], device
        )

    def core_copy(self, index, ref):
        return transfer(ref, ref, self.core_send.at[index], self.core_recv.at[index], self.place.sibling)

    def xy_copy(self, index, ref, device):
        return transfer(ref, ref, self.xy_send.at[index], self.xy_recv.at[index], device)

    def store(self, index, which):
        return pltpu.make_async_copy(self.full.at[which], self.out.at[which], self.out_sems.at[index])

    def mirrored(self, step):
        return 2 * self.origins[step] + 1 - self.place.core

    def held(self, step):
        return 2 * self.origins[step] + self.place.core

    def start(self):
        place = self.place
        greet(place)
        for cut in range(CUTS):

            for more in (False, True):

                @pl.when(place.z > 0)
                def _():
                    self.own_copy(0, cut, more).start()

                @pl.when(place.z < 3)
                def _():
                    self.own_copy(1, cut, more).start()

        self.core_copy(0, self.full.at[place.shard]).start()
        self.store(0, place.shard).start()

    def relay(self, turn, more=False):
        step = turn // CUTS
        piece = self.pieces(self.held(step), turn)[5 if more else 0]
        device = self.place.at_z(self.relays[step])
        send, recv = (self.relay_more, self.z_more) if more else (self.relay_send, self.z_recv)
        sem = recv.at[self.origins[step] * CUTS + turn % CUTS]
        return transfer(piece, piece, send.at[turn], sem, device)

    def along_z(self, turn):
        place = self.place
        self.relay(turn).wait_recv()

        @pl.when(place.inner)
        def _():
            self.relay(turn).start()

        pieces = self.pieces(self.held(turn // CUTS), turn)
        self.xy_copy(4 * turn, pieces[0], place.next_x).start()
        self.xy_copy(4 * turn + 1, pieces[0], place.next_y).start()
        self.core_copy(1 + 6 * turn, pieces[0]).start()
        self.relay(turn, True).wait_recv()

        @pl.when(place.inner)
        def _():
            self.relay(turn, True).start()

        self.core_copy(6 + 6 * turn, pieces[5]).start()

    def along_xy(self, turn):
        place, part = self.place, self.first_part
        _, by_x, by_y, *_ = self.pieces(self.held(turn // CUTS), turn)
        self.xy_copy(4 * turn, by_x, place.next_x).wait_recv()
        self.xy_copy(4 * turn + 2, by_x.at[pl.ds(0, part)], place.next_y).start()
        self.core_copy(2 + 6 * turn, by_x).start()
        self.xy_copy(4 * turn + 1, by_y, place.next_y).wait_recv()
        self.xy_copy(4 * turn + 3, by_y.at[pl.ds(part, self.last_part)], place.next_x).start()
        self.core_copy(3 + 6 * turn, by_y).start()

    def across(self, turn):
        place = self.place
        step = turn // CUTS
        _, _, _, first, last, _ = self.pieces(self.held(step), turn)
        self.xy_copy(4 * turn + 2, first, place.next_y).wait_recv()
        self.core_copy(4 + 6 * turn, first).start()
        self.xy_copy(4 * turn + 3, last, place.next_x).wait_recv()
        self.core_copy(5 + 6 * turn, last).start()
        if turn % CUTS == CUTS - 1:
            self.store(2 + 2 * step, self.held(step)).start()

    def core_own(self):
        which = 2 * self.place.z + 1 - self.place.core
        self.core_copy(0, self.full.at[which]).wait_recv()
        self.store(1, which).start()

    def core(self, step):
        which = self.mirrored(step)
        for turn in range(step * CUTS, (step + 1) * CUTS):
            for index, ref in enumerate(self.pieces(which, turn)):
                self.core_copy(1 + 6 * turn + index, ref).wait_recv()
        self.store(3 + 2 * step, which).start()

    def finish(self):
        place = self.place
        for cut in range(CUTS):

            for more in (False, True):

                @pl.when(place.z > 0)
                def _():
                    self.own_copy(0, cut, more).wait_send()

                @pl.when(place.z < 3)
                def _():
                    self.own_copy(1, cut, more).wait_send()

        self.core_copy(0, self.full.at[place.shard]).wait_send()
        self.store(0, place.shard).wait()
        self.store(1, 2 * place.z + 1 - place.core).wait()
        for turn in range(3 * CUTS):

            @pl.when(place.inner)
            def _():
                self.relay(turn).wait_send()
                self.relay(turn, True).wait_send()

            pieces = self.pieces(self.held(turn // CUTS), turn)
            self.xy_copy(4 * turn, pieces[0], place.next_x).wait_send()
            self.xy_copy(4 * turn + 1, pieces[0], place.next_y).wait_send()
            self.xy_copy(4 * turn + 2, pieces[3], place.next_y).wait_send()
            self.xy_copy(4 * turn + 3, pieces[4], place.next_x).wait_send()
            for index, ref in enumerate(pieces):
                self.core_copy(1 + 6 * turn + index, ref).wait_send()
        for step in range(3):
            self.store(2 + 2 * step, self.held(step)).wait()
            self.store(3 + 2 * step, self.mirrored(step)).wait()


def gather_kernel(master_ref, out_ref, full, *sems):
    gather = Gather(full, out_ref, sems)
    full[gather.place.shard] = master_ref[...].astype(BF16)
    gather.start()
    turns = 3 * CUTS
    for turn in range(turns + 2):
        if turn < turns:
            gather.along_z(turn)
        if 1 <= turn <= turns:
            gather.along_xy(turn - 1)
        if turn >= 2:
            gather.across(turn - 2)
        if turn == 2:
            gather.core_own()
        if turn >= 4 and turn % CUTS == 0:
            gather.core(turn // CUTS - 2)
    gather.core(2)
    gather.finish()


def gather_shards(master):
    rows = master.shape[0] * BLK
    shards = lax.axis_size("fsdp")
    return pl.pallas_call(
        gather_kernel,
        in_specs=[pl.BlockSpec(memory_space=pltpu.VMEM)],
        out_specs=pl.BlockSpec(memory_space=pltpu.HBM),
        out_shape=jax.ShapeDtypeStruct((shards, rows, BLK), BF16),
        scratch_shapes=[pltpu.VMEM((shards, rows, BLK), BF16)] + GATHER_SEMAPHORES,
        compiler_params=pltpu.CompilerParams(
            collective_id=0, has_side_effects=True, vmem_limit_bytes=60 * MIB
        ),
        cost_estimate=pl.CostEstimate(flops=0, bytes_accessed=200 * MIB, transcendentals=0),
        name="gather",
    )(master.reshape(rows, BLK)).reshape(-1, BLK, BLK)


def add_rows(target, former, latter, rows, step):
    @pl.loop(0, rows // step)
    def _(index):
        part = pl.ds(pl.multiple_of(index * step, 16), step)
        target[part] = (former[part].astype(F32) + latter[part].astype(F32)).astype(BF16)


def reduce_scratch(rows):
    quarter = rows // 4
    half = quarter // 2
    return [
        pltpu.VMEM((4, rows, BLK), BF16),
        pltpu.VMEM((4, rows, BLK), BF16),
        pltpu.VMEM((4, 2, half, BLK), BF16),
        pltpu.VMEM((4, 2, half, BLK), BF16),
        pltpu.VMEM((4, half, BLK), BF16),
        pltpu.VMEM((4, half, BLK), BF16),
        pltpu.VMEM((5, quarter, BLK), BF16),
        pltpu.VMEM((rows, BLK), BF16),
        pltpu.SemaphoreType.DMA((4,)),
        pltpu.SemaphoreType.DMA((4,)),
        pltpu.SemaphoreType.DMA((4,)),
        pltpu.SemaphoreType.DMA((24,)),
        pltpu.SemaphoreType.DMA((24,)),
        pltpu.SemaphoreType.DMA((3,)),
        pltpu.SemaphoreType.DMA((5,)),
        pltpu.SemaphoreType.DMA((4,)),
        pltpu.SemaphoreType.DMA((4,)),
    ]


class Reduce:
    def __init__(self, terms, base, out, scratch):
        self.place = place = Place()
        self.terms, self.base, self.out = terms, base, out
        (
            self.mine,
            self.sib,
            self.from_x,
            self.from_y,
            self.late_y,
            self.late_x,
            self.from_z,
            self.result,
            self.load_sems,
            self.core_send,
            self.core_recv,
            self.xy_send,
            self.xy_recv,
            self.z_send,
            self.z_recv,
            self.last_send,
            self.last_recv,
        ) = scratch
        self.quarter = out.shape[0] // 4
        self.half = self.quarter // 2
        z, high = place.z, place.high
        low = 1 - high
        self.order = (3 * low, low * (2 - 2 * z) + high * (7 - 2 * z), 1 + z % 2, z)
        self.onward = (z + 1 - 2 * high, z + 1 - 2 * (z % 2), z + 1 - 2 * high)
        self.closing = (0, (z % 2) * low, high)
        self.far = place.at_z(z + 2 - 4 * high)
        self.near = place.at_z(z + 1 - 2 * (z % 2))

    def shard_terms(self, shard):
        rows = self.out.shape[0]
        return self.terms.at[pl.ds(pl.multiple_of(self.base + shard * rows, 16), rows)]

    def load(self, step):
        source = self.shard_terms(2 * self.order[step] + self.place.core)
        return pltpu.make_async_copy(source, self.mine.at[step], self.load_sems.at[step])

    def core_copy(self, step):
        return transfer(
            self.shard_terms(2 * self.order[step] + 1 - self.place.core),
            self.sib.at[step],
            self.core_send.at[step],
            self.core_recv.at[step],
            self.place.sibling,
        )

    def part(self, step, which, side):
        start = pl.multiple_of(which * self.quarter + side * self.half, 16)
        return self.mine.at[step, pl.ds(start, self.half)]

    def xy_copy(self, step, index):
        place = self.place
        source, target, device = (
            (self.part(step, place.by_x, 0), self.from_x.at[step, 0], place.next_x),
            (self.part(step, place.across, 0), self.from_x.at[step, 1], place.next_x),
            (self.part(step, place.by_y, 1), self.from_y.at[step, 0], place.next_y),
            (self.part(step, place.across, 1), self.from_y.at[step, 1], place.next_y),
            (self.part(step, place.by_y, 0), self.late_y.at[step], place.next_y),
            (self.part(step, place.by_x, 1), self.late_x.at[step], place.next_x),
        )[index]
        place = 6 * step + index
        return transfer(source, target, self.xy_send.at[place], self.xy_recv.at[place], device)

    def start(self):
        greet(self.place, (self.far,))
        for step in range(2):
            self.core_copy(step).start()
        for step in range(4):
            self.load(step).start()

    def core(self, step):
        place, quarter = self.place, self.quarter
        self.load(step).wait()
        self.core_copy(step).wait_recv()
        if step < 2:
            self.core_copy(step + 2).start()

        def add(which):
            block = pl.ds(pl.multiple_of(which * quarter, 16), quarter)
            mine = self.mine.at[step, block]
            add_rows(mine, mine, self.sib.at[step, block], quarter, self.half)

        add(place.by_x)
        add(place.across)
        self.xy_copy(step, 0).start()
        self.xy_copy(step, 1).start()
        add(place.by_y)
        self.xy_copy(step, 2).start()
        self.xy_copy(step, 3).start()
        add(place.quarter)

    def take(self, step, which, side, index, source):
        self.xy_copy(step, index).wait_recv()
        target = self.part(step, which, side)
        add_rows(target, target, source, self.half, self.half)

    def first(self, step):
        place = self.place
        self.take(step, place.by_y, 0, 1, self.from_x.at[step, 1])
        self.xy_copy(step, 4).start()
        self.take(step, place.by_x, 1, 3, self.from_y.at[step, 1])
        self.xy_copy(step, 5).start()
        self.take(step, place.quarter, 0, 0, self.from_x.at[step, 0])
        self.take(step, place.quarter, 1, 2, self.from_y.at[step, 0])

    def own_block(self, step):
        return self.mine.at[step, pl.ds(pl.multiple_of(self.place.quarter * self.quarter, 16), self.quarter)]

    def z_copy(self, step):
        goal = self.order[step]
        slot = goal + self.closing[step] * (4 - goal)
        return transfer(
            self.own_block(step),
            self.from_z.at[slot],
            self.z_send.at[step],
            self.z_recv.at[slot],
            self.place.at_z(self.onward[step]),
        )

    def take_z(self, step, slot):
        source = self.from_z.at[slot]
        transfer(source, source, self.z_send.at[0], self.z_recv.at[slot], self.near).wait_recv()
        block = self.own_block(step)
        add_rows(block, block, source, self.quarter, self.half)

    def second(self, step):
        place = self.place
        self.take(step, place.quarter, 0, 4, self.late_y.at[step])
        self.take(step, place.quarter, 1, 5, self.late_x.at[step])
        if step < 3:

            @pl.when(place.inner)
            def _():
                self.take_z(step, self.order[step])

            self.z_copy(step).start()
        else:

            @pl.when(place.z > 0)
            def _():
                self.take_z(step, place.z)

            @pl.when(place.z < 3)
            def _():
                self.take_z(step, 4)

    def final(self, which, side=None):
        start = pl.multiple_of(which * self.quarter + (0 if side is None else side * self.half), 16)
        return self.result.at[pl.ds(start, self.quarter if side is None else self.half)]

    def last_copy(self, index, ref):
        device = (self.place.next_x, self.place.next_y, self.place.next_y, self.place.next_x)[index]
        return transfer(ref, ref, self.last_send.at[index], self.last_recv.at[index], device)

    def share(self):
        own = self.final(self.place.quarter)
        own[...] = self.own_block(3)[...]
        self.last_copy(0, own).start()
        self.last_copy(1, own).start()

    def share_on(self):
        place = self.place
        self.last_copy(0, self.final(place.by_x)).wait_recv()
        self.last_copy(2, self.final(place.by_x, 0)).start()
        self.last_copy(1, self.final(place.by_y)).wait_recv()
        self.last_copy(3, self.final(place.by_y, 1)).start()

    def finish(self):
        place = self.place
        self.last_copy(2, self.final(place.across, 0)).wait_recv()
        self.last_copy(3, self.final(place.across, 1)).wait_recv()
        self.out[...] = self.result[...]
        for step in range(4):
            self.core_copy(step).wait_send()
            for index in range(6):
                self.xy_copy(step, index).wait_send()
            if step < 3:
                self.z_copy(step).wait_send()
        own = self.final(place.quarter)
        self.last_copy(0, own).wait_send()
        self.last_copy(1, own).wait_send()
        self.last_copy(2, self.final(place.by_x, 0)).wait_send()
        self.last_copy(3, self.final(place.by_y, 1)).wait_send()


def reduce_kernel(*refs, base, short_steps):
    terms, small_ref, d_ref, resid_ref, w_ref, out_ref, small_out, short_ref, long_ref = refs[:9]
    small_in, small_sum, small_send, small_recv = refs[9:13]
    reduce = Reduce(terms, base, out_ref, refs[13:])
    place = reduce.place
    partners = (place.sibling, place.next_x, place.next_y, reduce.near, reduce.far)

    def small_copy(level):
        return transfer(
            small_sum.at[level],
            small_in.at[level],
            small_send.at[level],
            small_recv.at[level],
            partners[level],
        )

    def small_start():
        small_sum[0] = small_ref[...]
        small_copy(0).start()

    def small_step(level):
        small_copy(level - 1).wait_recv()
        small_sum[level] = small_sum[level - 1] + small_in[level - 1]
        if level < 5:
            small_copy(level).start()
        else:
            small_out[...] = small_sum[5]

    run_events(
        pl.program_id(0),
        (
            (reduce.start, small_start),
            (partial(reduce.core, 0), partial(small_step, 1)),
            (partial(reduce.core, 1), partial(reduce.first, 0), partial(small_step, 2)),
            (
                partial(reduce.core, 2),
                partial(reduce.first, 1),
                partial(reduce.second, 0),
                partial(small_step, 3),
            ),
            (
                partial(reduce.core, 3),
                partial(reduce.first, 2),
                partial(reduce.second, 1),
                partial(small_step, 4),
            ),
            (partial(reduce.first, 3), partial(reduce.second, 2), partial(small_step, 5)),
            (partial(reduce.second, 3), reduce.share),
            (reduce.share_on,),
        ),
    )
    input_product(d_ref, resid_ref, w_ref, short_ref, long_ref, short_steps)

    @pl.when(pl.program_id(0) == pl.num_programs(0) - 1)
    def _():
        reduce.finish()
        for level in range(5):
            small_copy(level).wait_send()


def reduce_late(terms, base, rows, small, d_qkv, resid, w_qkv, short_tiles):
    steps = resid.shape[0] // INPUT_ROWS
    short_steps = short_tiles * TILE // INPUT_ROWS
    in_specs, out_specs = input_specs(short_steps)

    def whole(shape):
        return pl.BlockSpec(shape, lambda step: (0, 0), pipeline_mode=pl.Buffered(1))

    return pl.pallas_call(
        partial(reduce_kernel, base=base, short_steps=short_steps),
        grid=(steps,),
        in_specs=[pl.BlockSpec(memory_space=pltpu.HBM), whole(small.shape)] + in_specs,
        out_specs=[
            pl.BlockSpec((rows, BLK), lambda step: (0, 0)),
            pl.BlockSpec(small.shape, lambda step: (0, 0)),
        ]
        + out_specs,
        out_shape=[
            jax.ShapeDtypeStruct((rows, BLK), BF16),
            jax.ShapeDtypeStruct((SMALL_ROWS, BLK), F32),
            jax.ShapeDtypeStruct((short_steps * INPUT_ROWS, D), F32),
            jax.ShapeDtypeStruct(((steps - short_steps) * INPUT_ROWS, D), F32),
        ],
        scratch_shapes=[
            pltpu.VMEM((5, SMALL_ROWS, BLK), F32),
            pltpu.VMEM((6, SMALL_ROWS, BLK), F32),
            pltpu.SemaphoreType.DMA((5,)),
            pltpu.SemaphoreType.DMA((5,)),
        ]
        + reduce_scratch(rows),
        compiler_params=pltpu.CompilerParams(
            collective_id=3, has_side_effects=True, vmem_limit_bytes=60 * MIB
        ),
        cost_estimate=pl.CostEstimate(flops=0, bytes_accessed=200 * MIB, transcendentals=0),
        name="reduce",
    )(terms, small, d_qkv, resid, w_qkv)


def count_where(condition, axis):
    return jnp.sum(condition.astype(jnp.int32), axis=axis)


def slot_codes(slots, qkv_slots, slot_count, shards):
    early = slot_count - LATE
    shard = slots // slot_count
    begin = shard * slot_count
    inside = (qkv_slots[None, :] >= begin[:, None]) & (qkv_slots[None, :] < (begin + slot_count)[:, None])
    own = count_where(qkv_slots[None, :] == slots[:, None], 1)
    before = count_where(inside & (qkv_slots[None, :] < slots[:, None]), 1)
    number = count_where(inside, 1)
    position = jnp.where(own > 0, slot_count - number + before, slots - begin - before)
    code = jnp.where(
        position < early,
        shard * early + position,
        shards * early + shard * LATE + position - early,
    )
    return code, position, jnp.max(number)


def update_kernel(
    position_ref,
    held_ref,
    early,
    late,
    master,
    left_stat,
    right_stat,
    left_root,
    right_root,
    slot_grad,
    new_left,
    new_right,
    new_master,
):
    count = master.shape[0]
    first = pl.program_id(0) * count
    split = early.shape[0] // BLK

    def block(ref, place):
        return ref[pl.ds(pl.multiple_of(place * BLK, BLK), BLK)]

    def grad_of(index):
        place = position_ref[first + index]
        grad = jnp.where(
            place < split,
            block(early, jnp.minimum(place, split - 1)),
            block(late, jnp.maximum(place - split, 0)),
        )
        return jnp.where(held_ref[first + index] > 0, grad, jnp.zeros_like(grad))

    for begin in range(0, count, 4):
        some = range(begin, min(begin + 4, count))
        grads = [grad_of(index) for index in some]
        applied = [product(left_root[index].astype(BF16), grad) for index, grad in zip(some, grads)]
        outer_left = [right_product(grad, grad) for grad in grads]
        outer_right = [left_product(grad, grad) for grad in grads]
        totals = [
            product(part.astype(BF16), right_root[index].astype(BF16)) for index, part in zip(some, applied)
        ]
        for place, index in enumerate(some):
            slot_grad[index] = grads[place].astype(F32)
            new_left[index] = STAT_DECAY * left_stat[index] + (1.0 - STAT_DECAY) * outer_left[place]
            new_right[index] = STAT_DECAY * right_stat[index] + (1.0 - STAT_DECAY) * outer_right[place]
            new_master[index] = master[index] - MATRIX_RATE * totals[place]


def update(position, held, early, late, master, left_stat, right_stat, left_root, right_root):
    slot_count = master.shape[0]
    group = max(size for size in range(1, 12) if slot_count % size == 0)
    some = pl.BlockSpec((group, BLK, BLK), lambda step, *_: (step, 0, 0))

    def whole(shape):
        return pl.BlockSpec(shape, lambda step, *_: (0, 0), pipeline_mode=pl.Buffered(1))

    return pl.pallas_call(
        update_kernel,
        grid_spec=pltpu.PrefetchScalarGridSpec(
            num_scalar_prefetch=2,
            grid=(slot_count // group,),
            in_specs=[whole(early.shape), whole(late.shape)] + [some] * 5,
            out_specs=[some] * 4,
        ),
        out_shape=[jax.ShapeDtypeStruct(master.shape, F32)] * 4,
        compiler_params=pltpu.CompilerParams(vmem_limit_bytes=60 * MIB),
        cost_estimate=pl.CostEstimate(
            flops=8 * slot_count * BLK**3, bytes_accessed=36 * slot_count * BLK**2, transcendentals=0
        ),
        name="update",
    )(position, held, early, late, master, left_stat, right_stat, left_root, right_root)


def body(
    x_short,
    x_long,
    cot_short,
    cot_long,
    logit_cot_short,
    logit_cot_long,
    len_short,
    len_long,
    block_slot,
    master,
    left_stat,
    right_stat,
    left_root,
    right_root,
    small_params,
    small_first,
    small_second,
    own_transfers,
):
    slot_count = master.shape[0]
    shards = lax.axis_size("fsdp")
    all_slots = slot_count * shards
    short_seqs, width = x_short.shape[:2]
    long_seqs = x_long.shape[0]
    short_tiles = short_seqs * width // TILE
    per_tile = TILE // width

    own = jnp.arange(slot_count, dtype=jnp.int32) + slot_count * lax.axis_index("fsdp")
    held = jnp.any(block_slot[None, :] == own[:, None], axis=1).astype(jnp.int32)
    if own_transfers:
        early_count = slot_count - LATE
        code, position, most = slot_codes(
            jnp.concatenate([block_slot, own]), block_slot[: 3 * 36], slot_count, shards
        )
        position = position[NBLK:]
        code = code[:NBLK]
        fits = most <= LATE
        gathered = gather_shards(master)
    else:
        gathered = lax.all_gather(master.astype(BF16), "fsdp", axis=0, tiled=True)
    w_qkv = assemble(block_slot, gathered)
    pieces = unpack(small_params)
    params = jnp.pad(small_params, (0, SMALL_ROWS * BLK - small_params.shape[0])).reshape(SMALL_ROWS, BLK)
    w_class = pieces[-2].reshape(SD, NCLS)
    b_class = pieces[-1].reshape(1, NCLS)
    x, *qkv, context, probs_short, probs_long = attention(
        len_short,
        len_long,
        x_short.reshape(-1, D),
        x_long.reshape(-1, D),
        params,
        w_qkv,
        short_tiles,
        width,
    )

    (
        enc_short,
        enc_long,
        logits_short,
        logits_long,
        first,
        active,
        d_up,
        d_down,
        d_branch,
        d_context,
        d_resid,
        g_student,
        g_hidden,
        g_small,
    ) = feed(
        len_short,
        len_long,
        block_slot,
        x,
        context,
        cot_short.reshape(-1, D),
        cot_long.reshape(-1, D),
        (logit_cot_short, logit_cot_long),
        (params, w_class, b_class),
        gathered,
        short_tiles,
        width,
    )
    g_out = left_product(context, d_branch).astype(BF16)
    others = (g_out, g_student.astype(BF16), g_hidden.astype(BF16))
    if own_transfers:
        terms = feed_grads(code, first, d_down, active, d_up, others, all_slots)
        *back, early_reduced = attention_back(
            qkv,
            probs_short,
            probs_long,
            d_context,
            x,
            short_tiles,
            terms.reshape(-1, BLK),
            early_count * BLK,
        )
    else:
        back = attention_back(qkv, probs_short, probs_long, d_context, x, short_tiles)
    d_qkv, g_b_query, g_b_value, x_turned = back

    def reduce_all():
        slot_terms = feed_grads(block_slot, first, d_down, active, d_up, others, all_slots)
        slot_terms, small_terms = input_weights(
            block_slot, x_turned, d_qkv, g_small, g_b_query, g_b_value, slot_terms
        )
        reduced = lax.psum_scatter(slot_terms, "fsdp", scatter_dimension=0, tiled=True)
        return lax.psum(reduced, "dp").reshape(-1, BLK), small_terms

    def renew(places, early, late):
        return update(
            places, held, early, late, master, left_stat, right_stat, left_root, right_root
        )

    def renew_all(blocks):
        return renew(jnp.arange(slot_count, dtype=jnp.int32), blocks, blocks)

    if own_transfers:
        terms, small_terms = input_weights(code, x_turned, d_qkv, g_small, g_b_query, g_b_value, terms)
        late_reduced, small_total, in_short, in_long = reduce_late(
            terms.reshape(-1, BLK),
            shards * early_count * BLK,
            LATE * BLK,
            small_terms,
            d_qkv,
            d_resid,
            w_qkv,
            short_tiles,
        )

        updated = lax.cond(
            fits,
            lambda: renew(position, early_reduced, late_reduced),
            lambda: renew_all(reduce_all()[0]),
        )
    else:
        in_short, in_long = input_grads(d_qkv, d_resid, w_qkv, short_tiles)
        blocks, small_terms = reduce_all()
        updated = renew_all(blocks)
        small_total = lax.psum(small_terms, ("dp", "fsdp"))
    slot_grad, new_left, new_right, new_master = updated
    small_grad = jnp.concatenate(
        [
            small_total[:CLASS_ROW].reshape(-1),
            small_total[CLASS_ROW : CLASS_ROW + NCLS].T.reshape(-1),
            small_total[LAST_ROW, :NCLS],
        ]
    )
    new_first = BETA_ONE * small_first + (1.0 - BETA_ONE) * small_grad
    new_second = BETA_TWO * small_second + (1.0 - BETA_TWO) * small_grad * small_grad
    first_hat = new_first / (1.0 - BETA_ONE**STEP)
    second_hat = new_second / (1.0 - BETA_TWO**STEP)
    new_small = small_params - ADAM_RATE * first_hat / (jnp.sqrt(second_hat) + ADAM_EPSILON)
    return (
        enc_short.reshape(x_short.shape),
        logits_short,
        enc_long.reshape(x_long.shape),
        logits_long,
        in_short.reshape(x_short.shape),
        in_long.reshape(x_long.shape),
        slot_grad,
        new_left,
        new_right,
        new_master,
        new_first,
        new_second,
        new_small,
    )


def solution(mesh):
    both = ("dp", "fsdp")
    placed = (
        P(both, None, None),
        P(both, None, None),
        P(both, None, None),
        P(both, None, None),
        P(both, None),
        P(both, None),
        P(both),
        P(both),
        P(),
        P("fsdp", None, None),
        P("fsdp", None, None),
        P("fsdp", None, None),
        P("fsdp", None, None),
        P("fsdp", None, None),
        P(),
        P(),
        P(),
    )
    return jax.shard_map(
        partial(body, own_transfers=(mesh.shape["dp"], mesh.shape["fsdp"]) == (4, 8)),
        mesh=mesh,
        in_specs=placed,
        out_specs=(
            P(both, None, None),
            P(both, None),
            P(both, None, None),
            P(both, None),
            P(both, None, None),
            P(both, None, None),
            P("fsdp", None, None),
            P("fsdp", None, None),
            P("fsdp", None, None),
            P("fsdp", None, None),
            P(),
            P(),
            P(),
        ),
        check_vma=False,
    )
```

```python
from functools import partial

import jax
import jax.numpy as jnp
from jax import lax
from jax.experimental import pallas as pl
from jax.experimental.pallas import tpu as pltpu
from jax.sharding import PartitionSpec as P

D = 768
HEADS = 12
FF = 3072
SD = 128
PH = 2
NCLS = 14
BLK = 128
STEP = 10
NBLK = 439
TILE = 512
PAIRS = 3
GROUPS = 2
CHUNK = 1024
LATE = 24

NORM_EPSILON = 1e-12
BETA_ONE = 0.9
BETA_TWO = 0.999
ADAM_EPSILON = 1e-08
ADAM_RATE = 0.1
MATRIX_RATE = 0.2
STAT_DECAY = 0.5
MASKED_SCORE = -1e30
MIB = 1024 * 1024
F32 = jnp.float32
BF16 = jnp.bfloat16

def product(former, latter, precision=None):
    return jnp.dot(former, latter, preferred_element_type=F32, precision=precision)


def left_product(former, latter, precision=None):
    return lax.dot_general(
        former, latter, (((0,), (0,)), ((), ())), preferred_element_type=F32, precision=precision
    )


def right_product(former, latter, precision=None):
    return lax.dot_general(
        former, latter, (((1,), (1,)), ((), ())), preferred_element_type=F32, precision=precision
    )


def unpack(small_values):
    widths = (D, D, D, D, D, FF, D, D, D, SD, SD, SD, SD * NCLS, NCLS)
    pieces = []
    offset = 0
    for column_count in widths:
        pieces.append(small_values[offset : offset + column_count])
        offset += column_count
    return pieces


def each_block(first, row_count, col_count, action):
    def one_row(index, carry):
        row = pl.multiple_of(index * BLK, BLK)
        for col in range(col_count):
            action(first + index * col_count + col, row, col * BLK)
        return carry

    lax.fori_loop(0, row_count, one_row, 0)


def load_blocks(slot_ref, blocks, target, sem, first, row_count, col_count, col_start=0):
    def move(block, row, col):
        pltpu.make_async_copy(
            blocks.at[slot_ref[block]],
            target.at[pl.ds(row, BLK), pl.ds(col + col_start * BLK, BLK)],
            sem,
        ).start()

    each_block(first, row_count, col_count, move)


def wait_whole(target, sem):
    pltpu.make_async_copy(target, target, sem).wait()


def assemble_kernel(slot_ref, blocks, out, sem):
    for which in range(3):
        load_blocks(slot_ref, blocks, out, sem, 36 * which, 6, 6, 6 * which)
    wait_whole(out, sem)


def assemble(block_slot, blocks):
    return pl.pallas_call(
        assemble_kernel,
        grid_spec=pltpu.PrefetchScalarGridSpec(
            num_scalar_prefetch=1,
            grid=(1,),
            in_specs=[pl.BlockSpec(memory_space=pltpu.HBM)],
            out_specs=pl.BlockSpec(memory_space=pltpu.VMEM),
            scratch_shapes=[pltpu.SemaphoreType.DMA],
        ),
        out_shape=jax.ShapeDtypeStruct((D, 3 * D), BF16),
        compiler_params=pltpu.CompilerParams(vmem_limit_bytes=60 * MIB),
        name="assemble",
    )(block_slot, blocks)


def join_small(small_ref, query_ref, value_ref, small_out):
    small_out[...] = small_ref[...]
    for start, ref in ((0, query_ref), (D // BLK, value_ref)):
        for index in range(D // BLK):
            small_out[start + index : start + index + 1, :] = ref[:, index * BLK : (index + 1) * BLK]


PART = 512
UNIT = 256
ACROSS = PART // BLK


def feed_grads_kernel(
    code_ref,
    first_turned,
    down_turned,
    active_ref,
    d_up_ref,
    g_out,
    g_student,
    g_hidden,
    terms,
    up_stage,
    down_stage,
    up_sems,
    down_sems,
    other_sems,
):
    step = pl.program_id(0)
    last = pl.num_programs(0) - 1
    slot = step % 2
    others = ((g_out, 108, 6, 6), (g_student, 432, 6, 1), (g_hidden, 438, 1, 1))

    @pl.when(step == 0)
    def _():
        for which, (grad, first, row_count, col_count) in enumerate(others):

            def move(block, row, col, which=which, grad=grad):
                pltpu.make_async_copy(
                    grad.at[pl.ds(row, BLK), pl.ds(col, BLK)], terms.at[code_ref[block]], other_sems.at[which]
                ).start()

            each_block(first, row_count, col_count, move)

    @pl.when(step >= 2)
    def _():
        wait_whole(up_stage.at[slot], up_sems.at[slot])
        wait_whole(down_stage.at[slot], down_sems.at[slot])


    def keep_up(cols, values):
        up_stage[slot, :, cols] = values.astype(BF16)

    def keep_down(cols, values):
        down_stage[slot, cols, :] = values.T.astype(BF16)

    units = [slice(begin, begin + UNIT) for begin in range(0, PART, UNIT)]
    in_turn(
        [
            (lambda cols=cols: product(first_turned[...], d_up_ref[:, cols]), partial(keep_up, cols))
            for cols in units
        ]
        + [
            (lambda cols=cols: product(down_turned[...], active_ref[:, cols]), partial(keep_down, cols))
            for cols in units
        ]
    )
    for row in range(D // BLK):
        for col in range(ACROSS):
            pltpu.make_async_copy(
                up_stage.at[slot, pl.ds(row * BLK, BLK), pl.ds(col * BLK, BLK)],
                terms.at[code_ref[144 + row * (FF // BLK) + step * ACROSS + col]],
                up_sems.at[slot],
            ).start()
            pltpu.make_async_copy(
                down_stage.at[slot, pl.ds(col * BLK, BLK), pl.ds(row * BLK, BLK)],
                terms.at[code_ref[288 + (step * ACROSS + col) * (D // BLK) + row]],
                down_sems.at[slot],
            ).start()

    @pl.when(step == last)
    def _():
        for place in range(2):
            wait_whole(up_stage.at[place], up_sems.at[place])
            wait_whole(down_stage.at[place], down_sems.at[place])
        for which, (grad, *_) in enumerate(others):
            wait_whole(grad, other_sems.at[which])


def feed_grads(code, first, d_down, active, d_up, others, slot_count):
    tokens = first.shape[1]

    def whole(shape):
        return pl.BlockSpec(shape, lambda step, *_: (0, 0), pipeline_mode=pl.Buffered(1))

    part = pl.BlockSpec((tokens, PART), lambda step, *_: (0, step))
    return pl.pallas_call(
        feed_grads_kernel,
        grid_spec=pltpu.PrefetchScalarGridSpec(
            num_scalar_prefetch=1,
            grid=(FF // PART,),
            in_specs=[whole(first.shape), whole(d_down.shape), part, part]
            + [whole(other.shape) for other in others],
            out_specs=pl.BlockSpec(memory_space=pltpu.HBM),
            scratch_shapes=[
                pltpu.VMEM((2, D, PART), BF16),
                pltpu.VMEM((2, PART, D), BF16),
                pltpu.SemaphoreType.DMA((2,)),
                pltpu.SemaphoreType.DMA((2,)),
                pltpu.SemaphoreType.DMA((3,)),
            ],
        ),
        out_shape=jax.ShapeDtypeStruct((slot_count, BLK, BLK), BF16),
        compiler_params=pltpu.CompilerParams(vmem_limit_bytes=60 * MIB),
        cost_estimate=pl.CostEstimate(
            flops=4 * tokens * D * FF, bytes_accessed=50 * MIB, transcendentals=0
        ),
        name="feed_grads",
    )(code, first, d_down, active, d_up, *others)


def input_weights_kernel(
    code_ref, turned, d_ref, small_ref, query_ref, value_ref, _, terms, small_out, stage, sems
):
    step = pl.program_id(0)
    slot = step % 2

    @pl.when(step == 0)
    def _():
        join_small(small_ref, query_ref, value_ref, small_out)

    @pl.when(step >= 2)
    def _():
        wait_whole(stage.at[slot], sems.at[slot])

    def keep(cols, values):
        stage[slot, :, cols] = values.astype(BF16)

    units = [slice(begin, begin + UNIT) for begin in range(0, D, UNIT)]
    in_turn(
        [(lambda cols=cols: product(turned[...], d_ref[:, cols]), partial(keep, cols)) for cols in units]
    )
    for row in range(D // BLK):
        for col in range(D // BLK):
            pltpu.make_async_copy(
                stage.at[slot, pl.ds(row * BLK, BLK), pl.ds(col * BLK, BLK)],
                terms.at[code_ref[36 * step + row * (D // BLK) + col]],
                sems.at[slot],
            ).start()

    @pl.when(step == pl.num_programs(0) - 1)
    def _():
        for place in range(2):
            wait_whole(stage.at[place], sems.at[place])


def input_weights(code, x, d_qkv, small, g_query, g_value, terms):
    tokens = x.shape[1]

    def whole(shape):
        return pl.BlockSpec(shape, lambda step, *_: (0, 0), pipeline_mode=pl.Buffered(1))

    hbm = pl.BlockSpec(memory_space=pltpu.HBM)
    return pl.pallas_call(
        input_weights_kernel,
        grid_spec=pltpu.PrefetchScalarGridSpec(
            num_scalar_prefetch=1,
            grid=(3,),
            in_specs=[
                whole(x.shape),
                pl.BlockSpec((tokens, D), lambda step, *_: (0, step)),
                whole(small.shape),
                whole(g_query.shape),
                whole(g_value.shape),
                hbm,
            ],
            out_specs=[hbm, pl.BlockSpec(small.shape, lambda step, *_: (0, 0))],
            scratch_shapes=[
                pltpu.VMEM((2, D, D), BF16),
                pltpu.SemaphoreType.DMA((2,)),
            ],
        ),
        out_shape=[
            jax.ShapeDtypeStruct(terms.shape, BF16),
            jax.ShapeDtypeStruct(small.shape, F32),
        ],
        input_output_aliases={6: 0},
        compiler_params=pltpu.CompilerParams(vmem_limit_bytes=60 * MIB),
        cost_estimate=pl.CostEstimate(
            flops=6 * tokens * D * D, bytes_accessed=16 * MIB, transcendentals=0
        ),
        name="input_weights",
    )(code, x, d_qkv, small, g_query, g_value, terms)


def half_masks():
    lane = lax.broadcasted_iota(jnp.int32, (1, BLK), 1)
    low = (lane < BLK // 2).astype(BF16)
    return low, (1.0 - low.astype(F32)).astype(BF16)


def stack_heads(values, low, high):
    return jnp.concatenate([values * low, values * high], axis=0)


def pick_heads(values):
    rows = values.shape[0] // 2
    lane = lax.broadcasted_iota(jnp.int32, (rows, BLK), 1)
    return jnp.where(lane < BLK // 2, values[:rows], values[rows:])


def pipelined(count, before, middle, after):
    started = before(0)
    done = None
    for index in range(count):
        current = started
        if index + 1 < count:
            started = before(index + 1)
        if done is not None:
            after(index - 1, done)
        done = middle(index, current)
    after(count - 1, done)


def in_turn(stages):
    pipelined(
        len(stages),
        lambda index: stages[index][0](),
        lambda index, values: stages[index][1](values),
        lambda *_: None,
    )


def softmax(scores, length):
    visible = lax.broadcasted_iota(jnp.int32, scores.shape, 1) < length
    scores = jnp.where(visible, scores, MASKED_SCORE)
    powers = jnp.exp(scores - jnp.max(scores, axis=-1, keepdims=True))
    total = jnp.sum(powers, axis=-1, keepdims=True)
    return (powers * (1.0 / total)).astype(BF16)


def attention_kernel(
    len_short,
    len_long,
    x_short_ref,
    x_long_ref,
    params,
    w_ref,
    x_ref,
    q_ref,
    k_ref,
    v_ref,
    context_ref,
    short_ref,
    long_ref,
    bias,
    *,
    short_tiles,
):
    tile = pl.program_id(0)
    group = pl.program_id(1)
    low, high = half_masks()
    width = short_ref.shape[-1]
    per_tile = TILE // width

    wide = PAIRS * BLK
    start = pl.multiple_of(group * wide, wide)

    @pl.when((tile == 0) & (group == 0))
    def _():
        for which in range(2):
            for place in range(D // BLK):
                row = which * (D // BLK) + place
                bias[which : which + 1, place * BLK : (place + 1) * BLK] = params[row : row + 1, :]

    @pl.when((tile < short_tiles) & (group == 0))
    def _():
        x_ref[...] = x_short_ref[...]

    @pl.when((tile >= short_tiles) & (group == 0))
    def _():
        x_ref[...] = x_long_ref[...]

    @pl.when(group == 0)
    def _():
        rows_in = x_ref[...]
        queries = product(rows_in, w_ref[:, :D]) + bias[0:1, :]
        q_ref[...] = (queries * 0.125).astype(BF16)
        k_ref[...] = product(rows_in, w_ref[:, D : 2 * D]).astype(BF16)
        v_ref[...] = (product(rows_in, w_ref[:, 2 * D :]) + bias[1:2, :]).astype(BF16)

    def inner(pair):
        return pl.ds(pl.multiple_of(start + pair * BLK, BLK), BLK)

    def attend(units, kept_ref):
        def scores(index):
            rows, keys, pair, _, _ = units[index]
            return right_product(stack_heads(q_ref[rows, inner(pair)], low, high), k_ref[keys, inner(pair)])

        def weigh(index, values):
            _, _, _, length, place = units[index]
            probs = softmax(values, length)
            kept_ref[place] = probs
            return probs

        def mix(index, probs):
            rows, keys, pair, _, _ = units[index]
            mixed = pick_heads(product(probs, v_ref[keys, inner(pair)])).astype(BF16)
            context_ref[rows, pair * BLK : (pair + 1) * BLK] = mixed

        pipelined(len(units), scores, weigh, mix)

    @pl.when(tile < short_tiles)
    def _():
        units = []
        for seq in range(per_tile):
            rows = slice(seq * width, (seq + 1) * width)
            length = len_short[tile * per_tile + seq]
            for pair in range(PAIRS):
                units.append((rows, rows, pair, length, (0, pair, seq)))
        attend(units, short_ref)

    @pl.when(tile >= short_tiles)
    def _():
        length = len_long[tile - short_tiles]
        half = TILE // 2
        units = []
        for pair in range(PAIRS):
            for part in range(2):
                rows = slice(part * half, (part + 1) * half)
                units.append((rows, slice(0, TILE), pair, length, (0, pair, part)))
        attend(units, long_ref)


def run_events(step, events):
    for index, actions in enumerate(events):

        @pl.when(step == index)
        def _(actions=actions):
            for action in actions:
                action()


def probs_shapes(short_tiles, long_tiles, width):
    per_tile = TILE // width
    return (
        (short_tiles, 2 * PAIRS, per_tile, 2 * width, width),
        (long_tiles, 2 * PAIRS, 2, TILE, TILE),
    )


def short_index(tile, short_tiles):
    return jnp.minimum(tile, short_tiles - 1)


def long_index(tile, short_tiles):
    return jnp.maximum(tile - short_tiles, 0)


def probs_maps(short_tiles):
    def short_map(tile, group):
        last = jnp.minimum(tile // short_tiles, 1)
        return (short_index(tile, short_tiles), group + last * (GROUPS - 1 - group), 0, 0, 0)

    def long_map(tile, group):
        begun = jnp.minimum(tile // short_tiles, 1)
        return (long_index(tile, short_tiles), begun * group, 0, 0, 0)

    return short_map, long_map


def attention(len_short, len_long, x_short, x_long, params, w_qkv, short_tiles, width):
    tiles = (x_short.shape[0] + x_long.shape[0]) // TILE
    wide = PAIRS * BLK
    short_shape, long_shape = probs_shapes(short_tiles, tiles - short_tiles, width)
    short_map, long_map = probs_maps(short_tiles)
    flops = 4 * D * TILE * TILE * tiles + 6 * D * D * TILE * tiles
    rows = pl.BlockSpec((TILE, wide), lambda tile, group: (tile, group))
    scalars = pl.BlockSpec(memory_space=pltpu.SMEM)

    def whole(shape):
        return pl.BlockSpec(shape, lambda tile, group: (0,) * len(shape), pipeline_mode=pl.Buffered(1))

    in_specs = [
        scalars,
        scalars,
        pl.BlockSpec((TILE, D), lambda tile, group: (short_index(tile, short_tiles), 0)),
        pl.BlockSpec((TILE, D), lambda tile, group: (long_index(tile, short_tiles), 0)),
        whole(params.shape),
        whole((D, 3 * D)),
    ]
    full_rows = pl.BlockSpec((TILE, D), lambda tile, group: (tile, 0))
    out_specs = [
        full_rows,
        full_rows,
        full_rows,
        full_rows,
        rows,
        pl.BlockSpec((1, PAIRS) + short_shape[2:], short_map),
        pl.BlockSpec((1, PAIRS) + long_shape[2:], long_map),
    ]
    out_shape = [jax.ShapeDtypeStruct((tiles * TILE, D), BF16)] * 5 + [
        jax.ShapeDtypeStruct(short_shape, BF16),
        jax.ShapeDtypeStruct(long_shape, BF16),
    ]
    arguments = [len_short, len_long, x_short, x_long, params, w_qkv]
    return pl.pallas_call(
        partial(attention_kernel, short_tiles=short_tiles),
        grid=(tiles, GROUPS),
        in_specs=in_specs,
        out_specs=out_specs,
        out_shape=out_shape,
        scratch_shapes=[pltpu.VMEM((8, D), F32)],
        compiler_params=pltpu.CompilerParams(vmem_limit_bytes=60 * MIB),
        cost_estimate=pl.CostEstimate(
            flops=flops, bytes_accessed=35 * MIB, transcendentals=HEADS * TILE * TILE * tiles // 2
        ),
        name="attention",
    )(*arguments)


def attention_back_kernel(*refs, short_tiles, transfers):
    q_ref, k_ref, v_ref, short_ref, long_ref, dc_ref, x_ref = refs[:7]
    refs = refs[7:]
    if transfers:
        terms_ref, refs = refs[0], refs[1:]
    out_ref, bq_ref, bv_ref, turned_ref = refs[:4]
    tile = pl.program_id(0)
    group = pl.program_id(1)
    low, high = half_masks()
    width = short_ref.shape[-1]
    per_tile = TILE // width
    if transfers:
        reduce = Reduce(terms_ref, 0, refs[4], refs[5:])
        run_events(
            tile * GROUPS + group,
            (
                (reduce.start,),
                (partial(reduce.core, 0),),
                (partial(reduce.core, 1), partial(reduce.first, 0)),
                (partial(reduce.core, 2), partial(reduce.first, 1), partial(reduce.second, 0)),
                (partial(reduce.core, 3), partial(reduce.first, 2), partial(reduce.second, 1)),
                (partial(reduce.first, 3), partial(reduce.second, 2)),
                (partial(reduce.second, 3), reduce.share),
                (reduce.share_on,),
            ),
        )

    wide = PAIRS * BLK
    start = pl.multiple_of(group * wide, wide)

    def columns(which, cols):
        return pl.ds(pl.multiple_of(which * D + start + cols.start, BLK), BLK)

    def go_back(units, kept_ref, parts):
        sums = {}

        def spread_in(index):
            rows, keys, cols, _ = units[index]
            return right_product(stack_heads(dc_ref[rows, cols], low, high), v_ref[keys, cols])

        def differ(index, d_probs):
            wide = kept_ref[units[index][3]].astype(F32)
            weighted = wide * d_probs
            return (weighted - wide * jnp.sum(weighted, axis=-1, keepdims=True)).astype(BF16)

        def gather_up(index, d_scores):
            rows, keys, cols, place = units[index]
            d_queries = pick_heads(product(d_scores, k_ref[keys, cols])) * 0.125
            out_ref[rows, columns(0, cols)] = d_queries.astype(BF16)
            d_keys = left_product(d_scores, stack_heads(q_ref[rows, cols], low, high))
            d_values = left_product(kept_ref[place], stack_heads(dc_ref[rows, cols], low, high))
            if index % parts:
                d_keys += sums["keys"]
                d_values += sums["values"]
            if index % parts == parts - 1:
                out_ref[keys, columns(1, cols)] = d_keys.astype(BF16)
                out_ref[keys, columns(2, cols)] = d_values.astype(BF16)
            else:
                sums.update(keys=d_keys, values=d_values)

        pipelined(len(units), spread_in, differ, gather_up)

    @pl.when(tile < short_tiles)
    def _():
        units = []
        for seq in range(per_tile):
            rows = slice(seq * width, (seq + 1) * width)
            for pair in range(PAIRS):
                cols = slice(pair * BLK, (pair + 1) * BLK)
                units.append((rows, rows, cols, (0, pair, seq)))
        go_back(units, short_ref, 1)

    @pl.when(tile >= short_tiles)
    def _():
        half = TILE // 2
        units = []
        for pair in range(PAIRS):
            cols = slice(pair * BLK, (pair + 1) * BLK)
            for part in range(2):
                rows = slice(part * half, (part + 1) * half)
                units.append((rows, slice(0, TILE), cols, (0, pair, part)))
        go_back(units, long_ref, 2)

    @pl.when(group == 0)
    def _():
        turned_ref[...] = x_ref[...].T

    @pl.when((tile == 0) & (group == 0))
    def _():
        bq_ref[...] = jnp.zeros_like(bq_ref)
        bv_ref[...] = jnp.zeros_like(bv_ref)

    bq_ref[:, pl.ds(start, wide)] += column_sum(out_ref[:, pl.ds(start, wide)])
    bv_ref[:, pl.ds(start, wide)] += column_sum(out_ref[:, pl.ds(2 * D + start, wide)])

    if transfers:

        @pl.when((tile == pl.num_programs(0) - 1) & (group == GROUPS - 1))
        def _():
            reduce.finish()


def attention_back(qkv, probs_short, probs_long, d_context, x, short_tiles, terms=None, count=0):
    tiles = d_context.shape[0] // TILE
    wide = PAIRS * BLK
    short_map, long_map = probs_maps(short_tiles)
    rows = pl.BlockSpec((TILE, wide), lambda tile, group: (tile, group))
    row = pl.BlockSpec((1, D), lambda tile, group: (0, 0))
    flops = 10 * D * TILE * TILE * tiles
    in_specs = [
        rows,
        rows,
        rows,
        pl.BlockSpec((1, PAIRS) + probs_short.shape[2:], short_map),
        pl.BlockSpec((1, PAIRS) + probs_long.shape[2:], long_map),
        rows,
        pl.BlockSpec((TILE, D), lambda tile, group: (tile, 0)),
    ]
    out_specs = [
        pl.BlockSpec((TILE, 3 * D), lambda tile, group: (tile, 0)),
        row,
        row,
        pl.BlockSpec((D, TILE), lambda tile, group: (0, tile)),
    ]
    out_shape = [
        jax.ShapeDtypeStruct((tiles * TILE, 3 * D), BF16),
        jax.ShapeDtypeStruct((1, D), F32),
        jax.ShapeDtypeStruct((1, D), F32),
        jax.ShapeDtypeStruct((D, tiles * TILE), BF16),
    ]
    arguments = [*qkv, probs_short, probs_long, d_context, x]
    scratch = []
    params = dict(vmem_limit_bytes=60 * MIB)
    if terms is not None:
        arguments.append(terms)
        in_specs.append(pl.BlockSpec(memory_space=pltpu.HBM))
        out_specs.append(pl.BlockSpec((count, BLK), lambda tile, group: (0, 0)))
        out_shape.append(jax.ShapeDtypeStruct((count, BLK), BF16))
        scratch = reduce_scratch(count)
        params.update(collective_id=2, has_side_effects=True)
    return pl.pallas_call(
        partial(attention_back_kernel, short_tiles=short_tiles, transfers=terms is not None),
        grid=(tiles, GROUPS),
        in_specs=in_specs,
        out_specs=out_specs,
        out_shape=out_shape,
        scratch_shapes=scratch,
        compiler_params=pltpu.CompilerParams(**params),
        cost_estimate=pl.CostEstimate(flops=flops, bytes_accessed=50 * MIB, transcendentals=0),
        name="attention_back",
    )(*arguments)


INPUT_ROWS = 256


def input_product(d_ref, resid_ref, w_ref, short_ref, long_ref, short_steps):
    step = pl.program_id(0)
    total = resid_ref[...] + right_product(d_ref[...], w_ref[...])

    @pl.when(step < short_steps)
    def _():
        short_ref[...] = total

    @pl.when(step >= short_steps)
    def _():
        long_ref[...] = total


def input_specs(short_steps):
    rows = [pl.BlockSpec((INPUT_ROWS, width), lambda step: (step, 0)) for width in (3 * D, D)]
    whole = pl.BlockSpec((D, 3 * D), lambda step: (0, 0), pipeline_mode=pl.Buffered(1))
    outs = [
        pl.BlockSpec((INPUT_ROWS, D), lambda step: (short_index(step, short_steps), 0)),
        pl.BlockSpec((INPUT_ROWS, D), lambda step: (long_index(step, short_steps), 0)),
    ]
    return rows + [whole], outs


def input_grads(d_qkv, resid, w_qkv, short_tiles):
    steps = resid.shape[0] // INPUT_ROWS
    short_steps = short_tiles * TILE // INPUT_ROWS
    in_specs, out_specs = input_specs(short_steps)
    return pl.pallas_call(
        partial(input_product, short_steps=short_steps),
        grid=(steps,),
        in_specs=in_specs,
        out_specs=out_specs,
        out_shape=[
            jax.ShapeDtypeStruct((short_steps * INPUT_ROWS, D), F32),
            jax.ShapeDtypeStruct(((steps - short_steps) * INPUT_ROWS, D), F32),
        ],
        compiler_params=pltpu.CompilerParams(vmem_limit_bytes=60 * MIB),
        name="input_grads",
    )(d_qkv, resid, w_qkv)


def normal_parts(values):
    below = 0.5 * lax.erf(values * 0.7071067811865476) + 0.5
    return below, jnp.exp(-0.5 * values * values) * 0.3989422804014327


B_OUT, GAIN_ONE, SHIFT_ONE, B_UP, B_DOWN, GAIN_TWO, SHIFT_TWO, B_STUDENT, POOL_QUERY, B_HIDDEN = range(10)
VECTORS = (
    (12, 6),
    (18, 6),
    (24, 6),
    (30, 24),
    (54, 6),
    (60, 6),
    (66, 6),
    (72, 1),
    (73, 1),
    (74, 1),
)
CLASS_ROW = 75
LAST_ROW = 91
SMALL_ROWS = 96


def norm_parts(values):
    center = values - jnp.mean(values, axis=-1, keepdims=True)
    spread = jnp.mean(center * center, axis=-1, keepdims=True)
    inverse = lax.rsqrt(spread + NORM_EPSILON)
    return center * inverse, inverse


def norm_back(d_values, gain, unit, inverse):
    d_unit = d_values * gain
    return inverse * (
        d_unit
        - jnp.mean(d_unit, axis=-1, keepdims=True)
        - unit * jnp.mean(d_unit * unit, axis=-1, keepdims=True)
    )


def column_sum(values):
    return jnp.sum(values.astype(F32), axis=0, keepdims=True)


def pool_weights(student, query, length):
    scaled = student * query
    lane = lax.broadcasted_iota(jnp.int32, scaled.shape, 1)
    place = lax.broadcasted_iota(jnp.int32, (scaled.shape[0], 1), 0)
    weights = []
    for side in (lane < SD // PH, lane >= SD // PH):
        scores = jnp.sum(jnp.where(side, scaled, 0.0), axis=-1, keepdims=True)
        scores = jnp.where(place < length, scores, MASKED_SCORE)
        powers = jnp.exp(scores - jnp.max(scores, axis=0, keepdims=True))
        weights.append(powers / jnp.sum(powers, axis=0, keepdims=True))
    return jnp.where(lane < SD // PH, weights[0], weights[1]), weights


def student_back(student, query, weights, both, d_pooled):
    lane = lax.broadcasted_iota(jnp.int32, student.shape, 1)
    moved = student * d_pooled
    d_scores = []
    for side, weight in zip((lane < SD // PH, lane >= SD // PH), weights):
        d_weight = jnp.sum(jnp.where(side, moved, 0.0), axis=-1, keepdims=True)
        d_scores.append(weight * (d_weight - jnp.sum(weight * d_weight, axis=0, keepdims=True)))
    d_score = jnp.where(lane < SD // PH, d_scores[0], d_scores[1])
    d_query = jnp.sum(d_score * student, axis=0, keepdims=True) * 0.125
    return both * d_pooled + d_score * query, d_query


def feed_kernel(
    len_short,
    len_long,
    slot_ref,
    x_ref,
    context_ref,
    cot_short_ref,
    cot_long_ref,
    logit_cot_short,
    logit_cot_long,
    params,
    w_class_ref,
    b_class_ref,
    blocks,
    enc_short_ref,
    enc_long_ref,
    logits_short,
    logits_long,
    first_ref,
    active_ref,
    d_up_ref,
    d_down_ref,
    d_branch_ref,
    d_context_ref,
    d_resid_ref,
    g_student,
    g_hidden,
    g_small,
    slope,
    pooled_ref,
    d_student_ref,
    w_out,
    w_up,
    w_down,
    w_student,
    w_hidden,
    vectors,
    totals,
    g_class,
    g_last,
    w_class,
    b_class,
    logit_cot,
    sems,
    *,
    short_tiles,
    width,
):
    tile = pl.program_id(0)
    per_tile = TILE // width
    loads = ((w_out, 108, 6, 6), (w_up, 144, 6, 24), (w_down, 288, 24, 6), (w_student, 432, 6, 1), (w_hidden, 438, 1, 1))

    def arrive(*indices):
        @pl.when(tile == 0)
        def _():
            for index in indices:
                wait_whole(loads[index][0], sems.at[index])

    @pl.when(tile == 0)
    def _():
        for index, (target, block, row_count, col_count) in enumerate(loads):
            load_blocks(slot_ref, blocks, target, sems.at[index], block, row_count, col_count)
        for index, (start, count) in enumerate(VECTORS):
            for place in range(count):
                vectors[index : index + 1, place * BLK : (place + 1) * BLK] = params[
                    start + place : start + place + 1, :
                ]
        for ref in (totals, g_class, g_last, g_student, g_hidden, w_class, b_class):
            ref[...] = jnp.zeros_like(ref)
        w_class[:, :NCLS] = w_class_ref[...]
        b_class[:, :NCLS] = b_class_ref[...]

    def vector(index):
        return vectors[index : index + 1, : VECTORS[index][1] * BLK]

    def add_total(index, values):
        totals[index : index + 1, : VECTORS[index][1] * BLK] += column_sum(values)

    arrive(0, 1, 2, 3, 4)
    sides = [slice(start, start + TILE // 2) for start in range(0, TILE, TILE // 2)]
    units_one, inverses_one, firsts = [], [], []

    def branch(index):
        return product(context_ref[sides[index]], w_out[...])

    def norm_first(index, values):
        rows = sides[index]
        unit, inverse = norm_parts(x_ref[rows].astype(F32) + (values + vector(B_OUT)))
        units_one.append(unit)
        inverses_one.append(inverse)
        firsts.append((unit * vector(GAIN_ONE) + vector(SHIFT_ONE)).astype(BF16))
        first_ref[:, rows] = firsts[-1].T


    chunks = [slice(start, start + CHUNK) for start in range(0, FF, CHUNK)]

    def rise(chunk, index):
        return product(firsts[index], w_up[:, chunks[chunk]])

    def bend(chunk, index, upward):
        rows, cols = sides[index], chunks[chunk]
        upward = upward + vectors[B_UP : B_UP + 1, cols]
        below, density = normal_parts(upward)
        active_ref[rows, cols] = (upward * below).astype(BF16)
        slope[rows, cols] = (below + upward * density).astype(BF16)

    units_two, inverses_two, encodeds = [], [], []

    def sink(index):
        return product(active_ref[sides[index]], w_down[...])

    def norm_second(index, values):
        unit, inverse = norm_parts(firsts[index].astype(F32) + (values + vector(B_DOWN)))
        units_two.append(unit)
        inverses_two.append(inverse)
        encodeds.append((unit * vector(GAIN_TWO) + vector(SHIFT_TWO)).astype(BF16))

    students = []

    def learn(index):
        return product(encodeds[index], w_student[...])

    def keep_student(index, values):
        students.append(values + vector(B_STUDENT))

    in_turn(
        [(partial(branch, index), partial(norm_first, index)) for index in range(2)]
        + [
            (partial(rise, chunk, index), partial(bend, chunk, index))
            for chunk in range(len(chunks))
            for index in range(2)
        ]
        + [(partial(sink, index), partial(norm_second, index)) for index in range(2)]
        + [(partial(learn, index), partial(keep_student, index)) for index in range(2)]
    )
    encoded = jnp.concatenate(encodeds, axis=0)

    @pl.when(tile < short_tiles)
    def _():
        enc_short_ref[...] = encoded

    @pl.when(tile >= short_tiles)
    def _():
        enc_long_ref[...] = encoded

    student = jnp.concatenate(students, axis=0)
    query = vector(POOL_QUERY) * 0.125
    pooled_ref[...] = jnp.zeros_like(pooled_ref)

    def head():
        pooled = pooled_ref[...]
        wide_hidden = w_hidden[...].astype(F32)
        hidden = jnp.tanh(product(pooled, wide_hidden) + vector(B_HIDDEN))
        logits = product(hidden, w_class[...]) + b_class[...]
        d_logits = logit_cot[...]
        g_last[...] += column_sum(d_logits)
        g_class[...] += left_product(d_logits, hidden)
        d_hidden = right_product(d_logits, w_class[...])
        d_hidden = d_hidden * (1.0 - hidden * hidden)
        add_total(B_HIDDEN, d_hidden)
        g_hidden[...] += left_product(pooled, d_hidden)
        return logits, right_product(d_hidden, wide_hidden)

    def pool(starts, size, lengths, cot_ref, logits_ref, first):
        count = len(starts)
        logit_cot[...] = jnp.zeros_like(logit_cot)
        for index in range(count):
            logit_cot[index : index + 1, :NCLS] = cot_ref[pl.ds(first + index, 1), :]
        kept = []
        for index, (start, length) in enumerate(zip(starts, lengths)):
            rows = student[start : start + size]
            both, weights = pool_weights(rows, query, length)
            pooled_ref[index : index + 1, :] = column_sum(both * rows)
            kept.append((start, rows, both, weights))
        logits, d_pooled = head()
        for index in range(count):
            logits_ref[pl.ds(first + index, 1), :] = logits[index : index + 1, :NCLS]
        for index, (start, rows, both, weights) in enumerate(kept):
            d_rows, d_query = student_back(rows, query, weights, both, d_pooled[index : index + 1])
            d_student_ref[start : start + size, :] = d_rows.astype(BF16)
            add_total(POOL_QUERY, d_query)

    @pl.when(tile < short_tiles)
    def _():
        pool(
            [seq * width for seq in range(per_tile)],
            width,
            [len_short[tile * per_tile + seq] for seq in range(per_tile)],
            logit_cot_short,
            logits_short,
            tile * per_tile,
        )

    @pl.when(tile >= short_tiles)
    def _():
        long = tile - short_tiles
        pool([0], TILE, [len_long[long]], logit_cot_long, logits_long, long)

    d_student = d_student_ref[...]
    add_total(B_STUDENT, d_student)
    g_student[...] += left_product(encoded, d_student)
    d_resids, d_downs = [], []

    def through_student(index):
        return right_product(d_student[sides[index]], w_student[...])

    def norm_second_back(index, values):
        rows = sides[index]
        cotangent = jnp.where(tile < short_tiles, cot_short_ref[rows], cot_long_ref[rows])
        d_second = cotangent.astype(F32) + values
        add_total(GAIN_TWO, d_second * units_two[index])
        add_total(SHIFT_TWO, d_second)
        d_resids.append(norm_back(d_second, vector(GAIN_TWO), units_two[index], inverses_two[index]))
        d_downs.append(d_resids[-1].astype(BF16))
        d_down_ref[:, rows] = d_downs[-1].T
        add_total(B_DOWN, d_downs[-1])

    def fall(chunk, index):
        return right_product(d_downs[index], w_down[chunks[chunk], :])

    def bend_back(chunk, index, d_active):
        rows, cols = sides[index], chunks[chunk]
        d_up = (d_active * slope[rows, cols].astype(F32)).astype(BF16)
        d_up_ref[rows, cols] = d_up
        totals[B_UP : B_UP + 1, cols] += column_sum(d_up)

    def rise_back(index):
        return right_product(d_up_ref[sides[index]], w_up[...])

    def norm_first_back(index, values):
        rows = sides[index]
        d_first = d_resids[index] + values
        add_total(GAIN_ONE, d_first * units_one[index])
        add_total(SHIFT_ONE, d_first)
        d_resid = norm_back(d_first, vector(GAIN_ONE), units_one[index], inverses_one[index])
        d_resid_ref[rows] = d_resid
        d_branch = d_resid.astype(BF16)
        d_branch_ref[rows] = d_branch
        add_total(B_OUT, d_branch)
        d_branches.append(d_branch)

    d_branches = []

    def branch_back(index):
        return right_product(d_branches[index], w_out[...])

    def keep_context(index, values):
        d_context_ref[sides[index]] = values.astype(BF16)

    in_turn(
        [(partial(through_student, index), partial(norm_second_back, index)) for index in range(2)]
        + [
            (partial(fall, chunk, index), partial(bend_back, chunk, index))
            for chunk in range(len(chunks))
            for index in range(2)
        ]
        + [(partial(rise_back, index), partial(norm_first_back, index)) for index in range(2)]
        + [(partial(branch_back, index), partial(keep_context, index)) for index in range(2)]
    )

    @pl.when(tile == pl.num_programs(0) - 1)
    def _():
        g_small[...] = jnp.zeros_like(g_small)
        for index, (start, count) in enumerate(VECTORS):
            for place in range(count):
                g_small[start + place : start + place + 1, :] = totals[
                    index : index + 1, place * BLK : (place + 1) * BLK
                ]
        g_small[CLASS_ROW : CLASS_ROW + NCLS, :] = g_class[:NCLS, :]
        g_small[LAST_ROW : LAST_ROW + 1, :] = g_last[...]


def feed(
    len_short, len_long, block_slot, x, context, cot_short, cot_long, logit_cots, small, blocks, short_tiles, width
):
    tiles = x.shape[0] // TILE
    long_tiles = tiles - short_tiles

    def whole(shape):
        return pl.BlockSpec(shape, lambda tile, *_: (0,) * len(shape), pipeline_mode=pl.Buffered(1))

    def kept(shape):
        return pl.BlockSpec(shape, lambda tile, *_: (0,) * len(shape))

    def rows(columns):
        return pl.BlockSpec((TILE, columns), lambda tile, *_: (tile, 0))

    turned = pl.BlockSpec((D, TILE), lambda tile, *_: (0, tile))
    short_rows = pl.BlockSpec((TILE, D), lambda tile, *_: (short_index(tile, short_tiles), 0))
    long_rows = pl.BlockSpec((TILE, D), lambda tile, *_: (long_index(tile, short_tiles), 0))
    grad_shapes = ((D, SD), (SD, SD), (SMALL_ROWS, BLK))
    total = tiles * TILE
    return pl.pallas_call(
        partial(feed_kernel, short_tiles=short_tiles, width=width),
        grid_spec=pltpu.PrefetchScalarGridSpec(
            num_scalar_prefetch=3,
            grid=(tiles,),
            in_specs=[rows(D), rows(D), short_rows, long_rows]
            + [whole(array.shape) for array in (*logit_cots, *small)]
            + [pl.BlockSpec(memory_space=pltpu.HBM)],
            out_specs=[
                short_rows,
                long_rows,
                kept(logit_cots[0].shape),
                kept(logit_cots[1].shape),
                turned,
                rows(FF),
                rows(FF),
                turned,
                rows(D),
                rows(D),
                rows(D),
            ]
            + [kept(shape) for shape in grad_shapes],
            scratch_shapes=[
                pltpu.VMEM((TILE, FF), BF16),
                pltpu.VMEM((8, SD), F32),
                pltpu.VMEM((TILE, SD), BF16),
                pltpu.VMEM((D, D), BF16),
                pltpu.VMEM((D, FF), BF16),
                pltpu.VMEM((FF, D), BF16),
                pltpu.VMEM((D, SD), BF16),
                pltpu.VMEM((SD, SD), BF16),
                pltpu.VMEM((16, FF), F32),
                pltpu.VMEM((16, FF), F32),
                pltpu.VMEM((SD, SD), F32),
                pltpu.VMEM((1, SD), F32),
                pltpu.VMEM((SD, SD), F32),
                pltpu.VMEM((1, SD), F32),
                pltpu.VMEM((8, SD), F32),
                pltpu.SemaphoreType.DMA((5,)),
            ],
        ),
        out_shape=[
            jax.ShapeDtypeStruct((short_tiles * TILE, D), BF16),
            jax.ShapeDtypeStruct((long_tiles * TILE, D), BF16),
            jax.ShapeDtypeStruct(logit_cots[0].shape, F32),
            jax.ShapeDtypeStruct(logit_cots[1].shape, F32),
            jax.ShapeDtypeStruct((D, total), BF16),
            jax.ShapeDtypeStruct((total, FF), BF16),
            jax.ShapeDtypeStruct((total, FF), BF16),
            jax.ShapeDtypeStruct((D, total), BF16),
            jax.ShapeDtypeStruct((total, D), BF16),
            jax.ShapeDtypeStruct((total, D), BF16),
            jax.ShapeDtypeStruct((total, D), F32),
        ]
        + [jax.ShapeDtypeStruct(shape, F32) for shape in grad_shapes],
        compiler_params=pltpu.CompilerParams(vmem_limit_bytes=62 * MIB),
        cost_estimate=pl.CostEstimate(
            flops=total * (8 * D * FF + 4 * D * D), bytes_accessed=70 * MIB, transcendentals=total * FF
        ),
        name="feed",
    )(len_short, len_long, block_slot, x, context, cot_short, cot_long, *logit_cots, *small, blocks)


class Place:
    def __init__(self):
        self.quarter = lax.axis_index("dp")
        self.shard = lax.axis_index("fsdp")
        x = self.quarter % 2
        y = self.quarter // 2
        self.core = self.shard % 2
        self.z = self.shard // 2
        self.high = self.z // 2
        self.by_x = 2 * y + 1 - x
        self.by_y = 2 * (1 - y) + x
        self.across = 2 * (1 - y) + 1 - x
        self.sibling = (self.quarter, 2 * self.z + 1 - self.core)
        self.next_x = (self.by_x, self.shard)
        self.next_y = (self.by_y, self.shard)
        self.inner = (self.z > 0) & (self.z < 3)

    def at_z(self, z):
        return (self.quarter, 2 * z + self.core)


def transfer(source, target, send_sem, recv_sem, device):
    return pltpu.make_async_remote_copy(
        src_ref=source,
        dst_ref=target,
        send_sem=send_sem,
        recv_sem=recv_sem,
        device_id=device,
        device_id_type=pl.DeviceIdType.MESH,
    )


def greet(place, extra=()):
    barrier = pltpu.get_barrier_semaphore()

    def signal(device):
        pl.semaphore_signal(barrier, inc=1, device_id=device, device_id_type=pl.DeviceIdType.MESH)

    near = (place.sibling, place.next_x, place.next_y) + tuple(extra)
    for device in near:
        signal(device)

    @pl.when(place.z > 0)
    def _():
        signal(place.at_z(place.z - 1))

    @pl.when(place.z < 3)
    def _():
        signal(place.at_z(place.z + 1))

    pl.semaphore_wait(barrier, len(near) + 1 + (place.z + 1) // 2 % 2)


CUTS = 2
GATHER_SEMAPHORES = [
    pltpu.SemaphoreType.DMA((2 * CUTS,)),
    pltpu.SemaphoreType.DMA((3 * CUTS,)),
    pltpu.SemaphoreType.DMA((4 * CUTS,)),
    pltpu.SemaphoreType.DMA((12 * CUTS,)),
    pltpu.SemaphoreType.DMA((12 * CUTS,)),
    pltpu.SemaphoreType.DMA((1 + 18 * CUTS,)),
    pltpu.SemaphoreType.DMA((1 + 18 * CUTS,)),
    pltpu.SemaphoreType.DMA((8,)),
    pltpu.SemaphoreType.DMA((2 * CUTS,)),
    pltpu.SemaphoreType.DMA((3 * CUTS,)),
    pltpu.SemaphoreType.DMA((4 * CUTS,)),
]


class Gather:
    def __init__(self, full, out, sems):
        self.place = place = Place()
        self.full, self.out = full, out
        (
            self.own_send,
            self.relay_send,
            self.z_recv,
            self.xy_send,
            self.xy_recv,
            self.core_send,
            self.core_recv,
            self.out_sems,
            self.own_more,
            self.relay_more,
            self.z_more,
        ) = sems
        self.quarter = full.shape[1] // 4
        self.cut = self.quarter // CUTS
        self.z_part = self.cut // 64 * 16
        self.first_part = ((self.cut - self.z_part) // 16 + 1) // 2 * 16
        self.last_part = self.cut - self.z_part - self.first_part
        z = place.z
        self.origins = (z + 1 - 2 * (z % 2), 2 - place.high, 3 * (1 - place.high))
        self.relays = (3 - z, 3 * (z - 1), 3 * (z - 1))

    def region(self, which, start, size):
        return self.full.at[which, pl.ds(pl.multiple_of(start, 16), size)]

    def pieces(self, which, turn):
        place, quarter, cut, part = self.place, self.quarter, self.cut, self.first_part
        skip = turn % CUTS * cut
        return (
            self.region(which, place.quarter * quarter + skip, cut),
            self.region(which, place.by_x * quarter + skip, cut),
            self.region(which, place.by_y * quarter + skip, cut),
            self.region(which, place.across * quarter + skip, part),
            self.region(which, place.across * quarter + skip + part, self.last_part),
            self.region(which, place.across * quarter + skip + cut - self.z_part, self.z_part),
        )

    def own_copy(self, side, cut, more=False):
        place = self.place
        mine = self.pieces(place.shard, cut)[5 if more else 0]
        device = place.at_z(place.z - 1 + 2 * side)
        send, recv = (self.own_more, self.z_more) if more else (self.own_send, self.z_recv)
        return transfer(
            mine, mine, send.at[side * CUTS + cut], recv.at[place.z * CUTS + cut], device
        )

    def core_copy(self, index, ref):
        return transfer(ref, ref, self.core_send.at[index], self.core_recv.at[index], self.place.sibling)

    def xy_copy(self, index, ref, device):
        return transfer(ref, ref, self.xy_send.at[index], self.xy_recv.at[index], device)

    def store(self, index, which):
        return pltpu.make_async_copy(self.full.at[which], self.out.at[which], self.out_sems.at[index])

    def mirrored(self, step):
        return 2 * self.origins[step] + 1 - self.place.core

    def held(self, step):
        return 2 * self.origins[step] + self.place.core

    def start(self):
        place = self.place
        greet(place)
        for cut in range(CUTS):

            for more in (False, True):

                @pl.when(place.z > 0)
                def _():
                    self.own_copy(0, cut, more).start()

                @pl.when(place.z < 3)
                def _():
                    self.own_copy(1, cut, more).start()

        self.core_copy(0, self.full.at[place.shard]).start()
        self.store(0, place.shard).start()

    def relay(self, turn, more=False):
        step = turn // CUTS
        piece = self.pieces(self.held(step), turn)[5 if more else 0]
        device = self.place.at_z(self.relays[step])
        send, recv = (self.relay_more, self.z_more) if more else (self.relay_send, self.z_recv)
        sem = recv.at[self.origins[step] * CUTS + turn % CUTS]
        return transfer(piece, piece, send.at[turn], sem, device)

    def along_z(self, turn):
        place = self.place
        self.relay(turn).wait_recv()

        @pl.when(place.inner)
        def _():
            self.relay(turn).start()

        pieces = self.pieces(self.held(turn // CUTS), turn)
        self.xy_copy(4 * turn, pieces[0], place.next_x).start()
        self.xy_copy(4 * turn + 1, pieces[0], place.next_y).start()
        self.core_copy(1 + 6 * turn, pieces[0]).start()
        self.relay(turn, True).wait_recv()

        @pl.when(place.inner)
        def _():
            self.relay(turn, True).start()

        self.core_copy(6 + 6 * turn, pieces[5]).start()

    def along_xy(self, turn):
        place, part = self.place, self.first_part
        _, by_x, by_y, *_ = self.pieces(self.held(turn // CUTS), turn)
        self.xy_copy(4 * turn, by_x, place.next_x).wait_recv()
        self.xy_copy(4 * turn + 2, by_x.at[pl.ds(0, part)], place.next_y).start()
        self.core_copy(2 + 6 * turn, by_x).start()
        self.xy_copy(4 * turn + 1, by_y, place.next_y).wait_recv()
        self.xy_copy(4 * turn + 3, by_y.at[pl.ds(part, self.last_part)], place.next_x).start()
        self.core_copy(3 + 6 * turn, by_y).start()

    def across(self, turn):
        place = self.place
        step = turn // CUTS
        _, _, _, first, last, _ = self.pieces(self.held(step), turn)
        self.xy_copy(4 * turn + 2, first, place.next_y).wait_recv()
        self.core_copy(4 + 6 * turn, first).start()
        self.xy_copy(4 * turn + 3, last, place.next_x).wait_recv()
        self.core_copy(5 + 6 * turn, last).start()
        if turn % CUTS == CUTS - 1:
            self.store(2 + 2 * step, self.held(step)).start()

    def core_own(self):
        which = 2 * self.place.z + 1 - self.place.core
        self.core_copy(0, self.full.at[which]).wait_recv()
        self.store(1, which).start()

    def core(self, step):
        which = self.mirrored(step)
        for turn in range(step * CUTS, (step + 1) * CUTS):
            for index, ref in enumerate(self.pieces(which, turn)):
                self.core_copy(1 + 6 * turn + index, ref).wait_recv()
        self.store(3 + 2 * step, which).start()

    def finish(self):
        place = self.place
        for cut in range(CUTS):

            for more in (False, True):

                @pl.when(place.z > 0)
                def _():
                    self.own_copy(0, cut, more).wait_send()

                @pl.when(place.z < 3)
                def _():
                    self.own_copy(1, cut, more).wait_send()

        self.core_copy(0, self.full.at[place.shard]).wait_send()
        self.store(0, place.shard).wait()
        self.store(1, 2 * place.z + 1 - place.core).wait()
        for turn in range(3 * CUTS):

            @pl.when(place.inner)
            def _():
                self.relay(turn).wait_send()
                self.relay(turn, True).wait_send()

            pieces = self.pieces(self.held(turn // CUTS), turn)
            self.xy_copy(4 * turn, pieces[0], place.next_x).wait_send()
            self.xy_copy(4 * turn + 1, pieces[0], place.next_y).wait_send()
            self.xy_copy(4 * turn + 2, pieces[3], place.next_y).wait_send()
            self.xy_copy(4 * turn + 3, pieces[4], place.next_x).wait_send()
            for index, ref in enumerate(pieces):
                self.core_copy(1 + 6 * turn + index, ref).wait_send()
        for step in range(3):
            self.store(2 + 2 * step, self.held(step)).wait()
            self.store(3 + 2 * step, self.mirrored(step)).wait()


def gather_kernel(master_ref, out_ref, full, *sems):
    gather = Gather(full, out_ref, sems)
    full[gather.place.shard] = master_ref[...].astype(BF16)
    gather.start()
    turns = 3 * CUTS
    for turn in range(turns + 2):
        if turn < turns:
            gather.along_z(turn)
        if 1 <= turn <= turns:
            gather.along_xy(turn - 1)
        if turn >= 2:
            gather.across(turn - 2)
        if turn == 2:
            gather.core_own()
        if turn >= 4 and turn % CUTS == 0:
            gather.core(turn // CUTS - 2)
    gather.core(2)
    gather.finish()


def gather_shards(master):
    rows = master.shape[0] * BLK
    shards = lax.axis_size("fsdp")
    return pl.pallas_call(
        gather_kernel,
        in_specs=[pl.BlockSpec(memory_space=pltpu.VMEM)],
        out_specs=pl.BlockSpec(memory_space=pltpu.HBM),
        out_shape=jax.ShapeDtypeStruct((shards, rows, BLK), BF16),
        scratch_shapes=[pltpu.VMEM((shards, rows, BLK), BF16)] + GATHER_SEMAPHORES,
        compiler_params=pltpu.CompilerParams(
            collective_id=0, has_side_effects=True, vmem_limit_bytes=60 * MIB
        ),
        cost_estimate=pl.CostEstimate(flops=0, bytes_accessed=200 * MIB, transcendentals=0),
        name="gather",
    )(master.reshape(rows, BLK)).reshape(-1, BLK, BLK)


def add_rows(target, former, latter, rows, step):
    @pl.loop(0, rows // step)
    def _(index):
        part = pl.ds(pl.multiple_of(index * step, 16), step)
        target[part] = (former[part].astype(F32) + latter[part].astype(F32)).astype(BF16)


def reduce_scratch(rows):
    quarter = rows // 4
    half = quarter // 2
    return [
        pltpu.VMEM((4, rows, BLK), BF16),
        pltpu.VMEM((4, rows, BLK), BF16),
        pltpu.VMEM((4, 2, half, BLK), BF16),
        pltpu.VMEM((4, 2, half, BLK), BF16),
        pltpu.VMEM((4, half, BLK), BF16),
        pltpu.VMEM((4, half, BLK), BF16),
        pltpu.VMEM((5, quarter, BLK), BF16),
        pltpu.VMEM((rows, BLK), BF16),
        pltpu.SemaphoreType.DMA((4,)),
        pltpu.SemaphoreType.DMA((4,)),
        pltpu.SemaphoreType.DMA((4,)),
        pltpu.SemaphoreType.DMA((24,)),
        pltpu.SemaphoreType.DMA((24,)),
        pltpu.SemaphoreType.DMA((3,)),
        pltpu.SemaphoreType.DMA((5,)),
        pltpu.SemaphoreType.DMA((4,)),
        pltpu.SemaphoreType.DMA((4,)),
    ]


class Reduce:
    def __init__(self, terms, base, out, scratch):
        self.place = place = Place()
        self.terms, self.base, self.out = terms, base, out
        (
            self.mine,
            self.sib,
            self.from_x,
            self.from_y,
            self.late_y,
            self.late_x,
            self.from_z,
            self.result,
            self.load_sems,
            self.core_send,
            self.core_recv,
            self.xy_send,
            self.xy_recv,
            self.z_send,
            self.z_recv,
            self.last_send,
            self.last_recv,
        ) = scratch
        self.quarter = out.shape[0] // 4
        self.half = self.quarter // 2
        z, high = place.z, place.high
        low = 1 - high
        self.order = (3 * low, low * (2 - 2 * z) + high * (7 - 2 * z), 1 + z % 2, z)
        self.onward = (z + 1 - 2 * high, z + 1 - 2 * (z % 2), z + 1 - 2 * high)
        self.closing = (0, (z % 2) * low, high)
        self.far = place.at_z(z + 2 - 4 * high)
        self.near = place.at_z(z + 1 - 2 * (z % 2))

    def shard_terms(self, shard):
        rows = self.out.shape[0]
        return self.terms.at[pl.ds(pl.multiple_of(self.base + shard * rows, 16), rows)]

    def load(self, step):
        source = self.shard_terms(2 * self.order[step] + self.place.core)
        return pltpu.make_async_copy(source, self.mine.at[step], self.load_sems.at[step])

    def core_copy(self, step):
        return transfer(
            self.shard_terms(2 * self.order[step] + 1 - self.place.core),
            self.sib.at[step],
            self.core_send.at[step],
            self.core_recv.at[step],
            self.place.sibling,
        )

    def part(self, step, which, side):
        start = pl.multiple_of(which * self.quarter + side * self.half, 16)
        return self.mine.at[step, pl.ds(start, self.half)]

    def xy_copy(self, step, index):
        place = self.place
        source, target, device = (
            (self.part(step, place.by_x, 0), self.from_x.at[step, 0], place.next_x),
            (self.part(step, place.across, 0), self.from_x.at[step, 1], place.next_x),
            (self.part(step, place.by_y, 1), self.from_y.at[step, 0], place.next_y),
            (self.part(step, place.across, 1), self.from_y.at[step, 1], place.next_y),
            (self.part(step, place.by_y, 0), self.late_y.at[step], place.next_y),
            (self.part(step, place.by_x, 1), self.late_x.at[step], place.next_x),
        )[index]
        place = 6 * step + index
        return transfer(source, target, self.xy_send.at[place], self.xy_recv.at[place], device)

    def start(self):
        greet(self.place, (self.far,))
        for step in range(2):
            self.core_copy(step).start()
        for step in range(4):
            self.load(step).start()

    def core(self, step):
        place, quarter = self.place, self.quarter
        self.load(step).wait()
        self.core_copy(step).wait_recv()
        if step < 2:
            self.core_copy(step + 2).start()

        def add(which):
            block = pl.ds(pl.multiple_of(which * quarter, 16), quarter)
            mine = self.mine.at[step, block]
            add_rows(mine, mine, self.sib.at[step, block], quarter, self.half)

        add(place.by_x)
        add(place.across)
        self.xy_copy(step, 0).start()
        self.xy_copy(step, 1).start()
        add(place.by_y)
        self.xy_copy(step, 2).start()
        self.xy_copy(step, 3).start()
        add(place.quarter)

    def take(self, step, which, side, index, source):
        self.xy_copy(step, index).wait_recv()
        target = self.part(step, which, side)
        add_rows(target, target, source, self.half, self.half)

    def first(self, step):
        place = self.place
        self.take(step, place.by_y, 0, 1, self.from_x.at[step, 1])
        self.xy_copy(step, 4).start()
        self.take(step, place.by_x, 1, 3, self.from_y.at[step, 1])
        self.xy_copy(step, 5).start()
        self.take(step, place.quarter, 0, 0, self.from_x.at[step, 0])
        self.take(step, place.quarter, 1, 2, self.from_y.at[step, 0])

    def own_block(self, step):
        return self.mine.at[step, pl.ds(pl.multiple_of(self.place.quarter * self.quarter, 16), self.quarter)]

    def z_copy(self, step):
        goal = self.order[step]
        slot = goal + self.closing[step] * (4 - goal)
        return transfer(
            self.own_block(step),
            self.from_z.at[slot],
            self.z_send.at[step],
            self.z_recv.at[slot],
            self.place.at_z(self.onward[step]),
        )

    def take_z(self, step, slot):
        source = self.from_z.at[slot]
        transfer(source, source, self.z_send.at[0], self.z_recv.at[slot], self.near).wait_recv()
        block = self.own_block(step)
        add_rows(block, block, source, self.quarter, self.half)

    def second(self, step):
        place = self.place
        self.take(step, place.quarter, 0, 4, self.late_y.at[step])
        self.take(step, place.quarter, 1, 5, self.late_x.at[step])
        if step < 3:

            @pl.when(place.inner)
            def _():
                self.take_z(step, self.order[step])

            self.z_copy(step).start()
        else:

            @pl.when(place.z > 0)
            def _():
                self.take_z(step, place.z)

            @pl.when(place.z < 3)
            def _():
                self.take_z(step, 4)

    def final(self, which, side=None):
        start = pl.multiple_of(which * self.quarter + (0 if side is None else side * self.half), 16)
        return self.result.at[pl.ds(start, self.quarter if side is None else self.half)]

    def last_copy(self, index, ref):
        device = (self.place.next_x, self.place.next_y, self.place.next_y, self.place.next_x)[index]
        return transfer(ref, ref, self.last_send.at[index], self.last_recv.at[index], device)

    def share(self):
        own = self.final(self.place.quarter)
        own[...] = self.own_block(3)[...]
        self.last_copy(0, own).start()
        self.last_copy(1, own).start()

    def share_on(self):
        place = self.place
        self.last_copy(0, self.final(place.by_x)).wait_recv()
        self.last_copy(2, self.final(place.by_x, 0)).start()
        self.last_copy(1, self.final(place.by_y)).wait_recv()
        self.last_copy(3, self.final(place.by_y, 1)).start()

    def finish(self):
        place = self.place
        self.last_copy(2, self.final(place.across, 0)).wait_recv()
        self.last_copy(3, self.final(place.across, 1)).wait_recv()
        self.out[...] = self.result[...]
        for step in range(4):
            self.core_copy(step).wait_send()
            for index in range(6):
                self.xy_copy(step, index).wait_send()
            if step < 3:
                self.z_copy(step).wait_send()
        own = self.final(place.quarter)
        self.last_copy(0, own).wait_send()
        self.last_copy(1, own).wait_send()
        self.last_copy(2, self.final(place.by_x, 0)).wait_send()
        self.last_copy(3, self.final(place.by_y, 1)).wait_send()


def reduce_kernel(*refs, base, short_steps):
    terms, small_ref, d_ref, resid_ref, w_ref, out_ref, small_out, short_ref, long_ref = refs[:9]
    small_in, small_sum, small_send, small_recv = refs[9:13]
    reduce = Reduce(terms, base, out_ref, refs[13:])
    place = reduce.place
    partners = (place.sibling, place.next_x, place.next_y, reduce.near, reduce.far)

    def small_copy(level):
        return transfer(
            small_sum.at[level],
            small_in.at[level],
            small_send.at[level],
            small_recv.at[level],
            partners[level],
        )

    def small_start():
        small_sum[0] = small_ref[...]
        small_copy(0).start()

    def small_step(level):
        small_copy(level - 1).wait_recv()
        small_sum[level] = small_sum[level - 1] + small_in[level - 1]
        if level < 5:
            small_copy(level).start()
        else:
            small_out[...] = small_sum[5]

    run_events(
        pl.program_id(0),
        (
            (reduce.start, small_start),
            (partial(reduce.core, 0), partial(small_step, 1)),
            (partial(reduce.core, 1), partial(reduce.first, 0), partial(small_step, 2)),
            (
                partial(reduce.core, 2),
                partial(reduce.first, 1),
                partial(reduce.second, 0),
                partial(small_step, 3),
            ),
            (
                partial(reduce.core, 3),
                partial(reduce.first, 2),
                partial(reduce.second, 1),
                partial(small_step, 4),
            ),
            (partial(reduce.first, 3), partial(reduce.second, 2), partial(small_step, 5)),
            (partial(reduce.second, 3), reduce.share),
            (reduce.share_on,),
        ),
    )
    input_product(d_ref, resid_ref, w_ref, short_ref, long_ref, short_steps)

    @pl.when(pl.program_id(0) == pl.num_programs(0) - 1)
    def _():
        reduce.finish()
        for level in range(5):
            small_copy(level).wait_send()


def reduce_late(terms, base, rows, small, d_qkv, resid, w_qkv, short_tiles):
    steps = resid.shape[0] // INPUT_ROWS
    short_steps = short_tiles * TILE // INPUT_ROWS
    in_specs, out_specs = input_specs(short_steps)

    def whole(shape):
        return pl.BlockSpec(shape, lambda step: (0, 0), pipeline_mode=pl.Buffered(1))

    return pl.pallas_call(
        partial(reduce_kernel, base=base, short_steps=short_steps),
        grid=(steps,),
        in_specs=[pl.BlockSpec(memory_space=pltpu.HBM), whole(small.shape)] + in_specs,
        out_specs=[
            pl.BlockSpec((rows, BLK), lambda step: (0, 0)),
            pl.BlockSpec(small.shape, lambda step: (0, 0)),
        ]
        + out_specs,
        out_shape=[
            jax.ShapeDtypeStruct((rows, BLK), BF16),
            jax.ShapeDtypeStruct((SMALL_ROWS, BLK), F32),
            jax.ShapeDtypeStruct((short_steps * INPUT_ROWS, D), F32),
            jax.ShapeDtypeStruct(((steps - short_steps) * INPUT_ROWS, D), F32),
        ],
        scratch_shapes=[
            pltpu.VMEM((5, SMALL_ROWS, BLK), F32),
            pltpu.VMEM((6, SMALL_ROWS, BLK), F32),
            pltpu.SemaphoreType.DMA((5,)),
            pltpu.SemaphoreType.DMA((5,)),
        ]
        + reduce_scratch(rows),
        compiler_params=pltpu.CompilerParams(
            collective_id=3, has_side_effects=True, vmem_limit_bytes=60 * MIB
        ),
        cost_estimate=pl.CostEstimate(flops=0, bytes_accessed=200 * MIB, transcendentals=0),
        name="reduce",
    )(terms, small, d_qkv, resid, w_qkv)


def count_where(condition, axis):
    return jnp.sum(condition.astype(jnp.int32), axis=axis)


def slot_codes(slots, qkv_slots, slot_count, shards):
    early = slot_count - LATE
    shard = slots // slot_count
    begin = shard * slot_count
    inside = (qkv_slots[None, :] >= begin[:, None]) & (qkv_slots[None, :] < (begin + slot_count)[:, None])
    own = count_where(qkv_slots[None, :] == slots[:, None], 1)
    before = count_where(inside & (qkv_slots[None, :] < slots[:, None]), 1)
    number = count_where(inside, 1)
    position = jnp.where(own > 0, slot_count - number + before, slots - begin - before)
    code = jnp.where(
        position < early,
        shard * early + position,
        shards * early + shard * LATE + position - early,
    )
    return code, position, jnp.max(number)


def update_kernel(
    position_ref,
    held_ref,
    early,
    late,
    master,
    left_stat,
    right_stat,
    left_root,
    right_root,
    slot_grad,
    new_left,
    new_right,
    new_master,
):
    count = master.shape[0]
    first = pl.program_id(0) * count
    split = early.shape[0] // BLK

    def block(ref, place):
        return ref[pl.ds(pl.multiple_of(place * BLK, BLK), BLK)]

    def grad_of(index):
        place = position_ref[first + index]
        grad = jnp.where(
            place < split,
            block(early, jnp.minimum(place, split - 1)),
            block(late, jnp.maximum(place - split, 0)),
        )
        return jnp.where(held_ref[first + index] > 0, grad, jnp.zeros_like(grad))

    for begin in range(0, count, 4):
        some = range(begin, min(begin + 4, count))
        grads = [grad_of(index) for index in some]
        applied = [product(left_root[index].astype(BF16), grad) for index, grad in zip(some, grads)]
        outer_left = [right_product(grad, grad) for grad in grads]
        outer_right = [left_product(grad, grad) for grad in grads]
        totals = [
            product(part.astype(BF16), right_root[index].astype(BF16)) for index, part in zip(some, applied)
        ]
        for place, index in enumerate(some):
            slot_grad[index] = grads[place].astype(F32)
            new_left[index] = STAT_DECAY * left_stat[index] + (1.0 - STAT_DECAY) * outer_left[place]
            new_right[index] = STAT_DECAY * right_stat[index] + (1.0 - STAT_DECAY) * outer_right[place]
            new_master[index] = master[index] - MATRIX_RATE * totals[place]


def update(position, held, early, late, master, left_stat, right_stat, left_root, right_root):
    slot_count = master.shape[0]
    group = max(size for size in range(1, 12) if slot_count % size == 0)
    some = pl.BlockSpec((group, BLK, BLK), lambda step, *_: (step, 0, 0))

    def whole(shape):
        return pl.BlockSpec(shape, lambda step, *_: (0, 0), pipeline_mode=pl.Buffered(1))

    return pl.pallas_call(
        update_kernel,
        grid_spec=pltpu.PrefetchScalarGridSpec(
            num_scalar_prefetch=2,
            grid=(slot_count // group,),
            in_specs=[whole(early.shape), whole(late.shape)] + [some] * 5,
            out_specs=[some] * 4,
        ),
        out_shape=[jax.ShapeDtypeStruct(master.shape, F32)] * 4,
        compiler_params=pltpu.CompilerParams(vmem_limit_bytes=60 * MIB),
        cost_estimate=pl.CostEstimate(
            flops=8 * slot_count * BLK**3, bytes_accessed=36 * slot_count * BLK**2, transcendentals=0
        ),
        name="update",
    )(position, held, early, late, master, left_stat, right_stat, left_root, right_root)


def body(
    x_short,
    x_long,
    cot_short,
    cot_long,
    logit_cot_short,
    logit_cot_long,
    len_short,
    len_long,
    block_slot,
    master,
    left_stat,
    right_stat,
    left_root,
    right_root,
    small_params,
    small_first,
    small_second,
    own_transfers,
):
    slot_count = master.shape[0]
    shards = lax.axis_size("fsdp")
    all_slots = slot_count * shards
    short_seqs, width = x_short.shape[:2]
    long_seqs = x_long.shape[0]
    short_tiles = short_seqs * width // TILE
    per_tile = TILE // width

    own = jnp.arange(slot_count, dtype=jnp.int32) + slot_count * lax.axis_index("fsdp")
    held = jnp.any(block_slot[None, :] == own[:, None], axis=1).astype(jnp.int32)
    if own_transfers:
        early_count = slot_count - LATE
        code, position, most = slot_codes(
            jnp.concatenate([block_slot, own]), block_slot[: 3 * 36], slot_count, shards
        )
        position = position[NBLK:]
        code = code[:NBLK]
        fits = most <= LATE
        gathered = gather_shards(master)
    else:
        gathered = lax.all_gather(master.astype(BF16), "fsdp", axis=0, tiled=True)
    w_qkv = assemble(block_slot, gathered)
    pieces = unpack(small_params)
    params = jnp.pad(small_params, (0, SMALL_ROWS * BLK - small_params.shape[0])).reshape(SMALL_ROWS, BLK)
    w_class = pieces[-2].reshape(SD, NCLS)
    b_class = pieces[-1].reshape(1, NCLS)
    x, *qkv, context, probs_short, probs_long = attention(
        len_short,
        len_long,
        x_short.reshape(-1, D),
        x_long.reshape(-1, D),
        params,
        w_qkv,
        short_tiles,
        width,
    )

    (
        enc_short,
        enc_long,
        logits_short,
        logits_long,
        first,
        active,
        d_up,
        d_down,
        d_branch,
        d_context,
        d_resid,
        g_student,
        g_hidden,
        g_small,
    ) = feed(
        len_short,
        len_long,
        block_slot,
        x,
        context,
        cot_short.reshape(-1, D),
        cot_long.reshape(-1, D),
        (logit_cot_short, logit_cot_long),
        (params, w_class, b_class),
        gathered,
        short_tiles,
        width,
    )
    g_out = left_product(context, d_branch).astype(BF16)
    others = (g_out, g_student.astype(BF16), g_hidden.astype(BF16))
    if own_transfers:
        terms = feed_grads(code, first, d_down, active, d_up, others, all_slots)
        *back, early_reduced = attention_back(
            qkv,
            probs_short,
            probs_long,
            d_context,
            x,
            short_tiles,
            terms.reshape(-1, BLK),
            early_count * BLK,
        )
    else:
        back = attention_back(qkv, probs_short, probs_long, d_context, x, short_tiles)
    d_qkv, g_b_query, g_b_value, x_turned = back

    def reduce_all():
        slot_terms = feed_grads(block_slot, first, d_down, active, d_up, others, all_slots)
        slot_terms, small_terms = input_weights(
            block_slot, x_turned, d_qkv, g_small, g_b_query, g_b_value, slot_terms
        )
        reduced = lax.psum_scatter(slot_terms, "fsdp", scatter_dimension=0, tiled=True)
        return lax.psum(reduced, "dp").reshape(-1, BLK), small_terms

    def renew(places, early, late):
        return update(
            places, held, early, late, master, left_stat, right_stat, left_root, right_root
        )

    def renew_all(blocks):
        return renew(jnp.arange(slot_count, dtype=jnp.int32), blocks, blocks)

    if own_transfers:
        terms, small_terms = input_weights(code, x_turned, d_qkv, g_small, g_b_query, g_b_value, terms)
        late_reduced, small_total, in_short, in_long = reduce_late(
            terms.reshape(-1, BLK),
            shards * early_count * BLK,
            LATE * BLK,
            small_terms,
            d_qkv,
            d_resid,
            w_qkv,
            short_tiles,
        )

        updated = lax.cond(
            fits,
            lambda: renew(position, early_reduced, late_reduced),
            lambda: renew_all(reduce_all()[0]),
        )
    else:
        in_short, in_long = input_grads(d_qkv, d_resid, w_qkv, short_tiles)
        blocks, small_terms = reduce_all()
        updated = renew_all(blocks)
        small_total = lax.psum(small_terms, ("dp", "fsdp"))
    slot_grad, new_left, new_right, new_master = updated
    small_grad = jnp.concatenate(
        [
            small_total[:CLASS_ROW].reshape(-1),
            small_total[CLASS_ROW : CLASS_ROW + NCLS].T.reshape(-1),
            small_total[LAST_ROW, :NCLS],
        ]
    )
    new_first = BETA_ONE * small_first + (1.0 - BETA_ONE) * small_grad
    new_second = BETA_TWO * small_second + (1.0 - BETA_TWO) * small_grad * small_grad
    first_hat = new_first / (1.0 - BETA_ONE**STEP)
    second_hat = new_second / (1.0 - BETA_TWO**STEP)
    new_small = small_params - ADAM_RATE * first_hat / (jnp.sqrt(second_hat) + ADAM_EPSILON)
    return (
        enc_short.reshape(x_short.shape),
        logits_short,
        enc_long.reshape(x_long.shape),
        logits_long,
        in_short.reshape(x_short.shape),
        in_long.reshape(x_long.shape),
        slot_grad,
        new_left,
        new_right,
        new_master,
        new_first,
        new_second,
        new_small,
    )


def solution(mesh):
    both = ("dp", "fsdp")
    placed = (
        P(both, None, None),
        P(both, None, None),
        P(both, None, None),
        P(both, None, None),
        P(both, None),
        P(both, None),
        P(both),
        P(both),
        P(),
        P("fsdp", None, None),
        P("fsdp", None, None),
        P("fsdp", None, None),
        P("fsdp", None, None),
        P("fsdp", None, None),
        P(),
        P(),
        P(),
    )
    return jax.shard_map(
        partial(body, own_transfers=(mesh.shape["dp"], mesh.shape["fsdp"]) == (4, 8)),
        mesh=mesh,
        in_specs=placed,
        out_specs=(
            P(both, None, None),
            P(both, None),
            P(both, None, None),
            P(both, None),
            P(both, None, None),
            P(both, None, None),
            P("fsdp", None, None),
            P("fsdp", None, None),
            P("fsdp", None, None),
            P("fsdp", None, None),
            P(),
            P(),
            P(),
        ),
        check_vma=False,
    )
```

```python
from functools import partial

import jax
import jax.numpy as jnp
from jax import lax
from jax.experimental import pallas as pl
from jax.experimental.pallas import tpu as pltpu
from jax.sharding import PartitionSpec as P

D = 768
HEADS = 12
FF = 3072
SD = 128
PH = 2
NCLS = 14
BLK = 128
STEP = 10
NBLK = 439
TILE = 512
PAIRS = 3
GROUPS = 2
CHUNK = 1024
LATE = 24

NORM_EPSILON = 1e-12
BETA_ONE = 0.9
BETA_TWO = 0.999
ADAM_EPSILON = 1e-08
ADAM_RATE = 0.1
MATRIX_RATE = 0.2
STAT_DECAY = 0.5
MASKED_SCORE = -1e30
MIB = 1024 * 1024
F32 = jnp.float32
BF16 = jnp.bfloat16

def product(former, latter, precision=None):
    return jnp.dot(former, latter, preferred_element_type=F32, precision=precision)


def left_product(former, latter, precision=None):
    return lax.dot_general(
        former, latter, (((0,), (0,)), ((), ())), preferred_element_type=F32, precision=precision
    )


def right_product(former, latter, precision=None):
    return lax.dot_general(
        former, latter, (((1,), (1,)), ((), ())), preferred_element_type=F32, precision=precision
    )


def unpack(small_values):
    widths = (D, D, D, D, D, FF, D, D, D, SD, SD, SD, SD * NCLS, NCLS)
    pieces = []
    offset = 0
    for column_count in widths:
        pieces.append(small_values[offset : offset + column_count])
        offset += column_count
    return pieces


def each_block(first, row_count, col_count, action):
    def one_row(index, carry):
        row = pl.multiple_of(index * BLK, BLK)
        for col in range(col_count):
            action(first + index * col_count + col, row, col * BLK)
        return carry

    lax.fori_loop(0, row_count, one_row, 0)


def load_blocks(slot_ref, blocks, target, sem, first, row_count, col_count, col_start=0):
    def move(block, row, col):
        pltpu.make_async_copy(
            blocks.at[slot_ref[block]],
            target.at[pl.ds(row, BLK), pl.ds(col + col_start * BLK, BLK)],
            sem,
        ).start()

    each_block(first, row_count, col_count, move)


def wait_whole(target, sem):
    pltpu.make_async_copy(target, target, sem).wait()


def assemble_kernel(slot_ref, blocks, out, sem):
    for which in range(3):
        load_blocks(slot_ref, blocks, out, sem, 36 * which, 6, 6, 6 * which)
    wait_whole(out, sem)


def assemble(block_slot, blocks):
    return pl.pallas_call(
        assemble_kernel,
        grid_spec=pltpu.PrefetchScalarGridSpec(
            num_scalar_prefetch=1,
            grid=(1,),
            in_specs=[pl.BlockSpec(memory_space=pltpu.HBM)],
            out_specs=pl.BlockSpec(memory_space=pltpu.VMEM),
            scratch_shapes=[pltpu.SemaphoreType.DMA],
        ),
        out_shape=jax.ShapeDtypeStruct((D, 3 * D), BF16),
        compiler_params=pltpu.CompilerParams(vmem_limit_bytes=60 * MIB),
        name="assemble",
    )(block_slot, blocks)


def join_small(small_ref, query_ref, value_ref, small_out):
    small_out[...] = small_ref[...]
    for start, ref in ((0, query_ref), (D // BLK, value_ref)):
        for index in range(D // BLK):
            small_out[start + index : start + index + 1, :] = ref[:, index * BLK : (index + 1) * BLK]


PART = 512
ACROSS = PART // BLK


def feed_grads_kernel(
    code_ref,
    first_turned,
    down_turned,
    active_ref,
    d_up_ref,
    g_out,
    g_student,
    g_hidden,
    terms,
    up_stage,
    down_stage,
    up_sems,
    down_sems,
    other_sems,
):
    step = pl.program_id(0)
    last = pl.num_programs(0) - 1
    slot = step % 2
    others = ((g_out, 108, 6, 6), (g_student, 432, 6, 1), (g_hidden, 438, 1, 1))

    @pl.when(step == 0)
    def _():
        for which, (grad, first, row_count, col_count) in enumerate(others):

            def move(block, row, col, which=which, grad=grad):
                pltpu.make_async_copy(
                    grad.at[pl.ds(row, BLK), pl.ds(col, BLK)], terms.at[code_ref[block]], other_sems.at[which]
                ).start()

            each_block(first, row_count, col_count, move)

    @pl.when(step >= 2)
    def _():
        wait_whole(up_stage.at[slot], up_sems.at[slot])
        wait_whole(down_stage.at[slot], down_sems.at[slot])

    up_stage[slot] = product(first_turned[...], d_up_ref[...]).astype(BF16)
    down_stage[slot] = product(down_turned[...], active_ref[...]).T.astype(BF16)
    for row in range(D // BLK):
        for col in range(ACROSS):
            pltpu.make_async_copy(
                up_stage.at[slot, pl.ds(row * BLK, BLK), pl.ds(col * BLK, BLK)],
                terms.at[code_ref[144 + row * (FF // BLK) + step * ACROSS + col]],
                up_sems.at[slot],
            ).start()
            pltpu.make_async_copy(
                down_stage.at[slot, pl.ds(col * BLK, BLK), pl.ds(row * BLK, BLK)],
                terms.at[code_ref[288 + (step * ACROSS + col) * (D // BLK) + row]],
                down_sems.at[slot],
            ).start()

    @pl.when(step == last)
    def _():
        for place in range(2):
            wait_whole(up_stage.at[place], up_sems.at[place])
            wait_whole(down_stage.at[place], down_sems.at[place])
        for which, (grad, *_) in enumerate(others):
            wait_whole(grad, other_sems.at[which])


def feed_grads(code, first, d_down, active, d_up, others, slot_count):
    tokens = first.shape[1]

    def whole(shape):
        return pl.BlockSpec(shape, lambda step, *_: (0, 0), pipeline_mode=pl.Buffered(1))

    part = pl.BlockSpec((tokens, PART), lambda step, *_: (0, step))
    return pl.pallas_call(
        feed_grads_kernel,
        grid_spec=pltpu.PrefetchScalarGridSpec(
            num_scalar_prefetch=1,
            grid=(FF // PART,),
            in_specs=[whole(first.shape), whole(d_down.shape), part, part]
            + [whole(other.shape) for other in others],
            out_specs=pl.BlockSpec(memory_space=pltpu.HBM),
            scratch_shapes=[
                pltpu.VMEM((2, D, PART), BF16),
                pltpu.VMEM((2, PART, D), BF16),
                pltpu.SemaphoreType.DMA((2,)),
                pltpu.SemaphoreType.DMA((2,)),
                pltpu.SemaphoreType.DMA((3,)),
            ],
        ),
        out_shape=jax.ShapeDtypeStruct((slot_count, BLK, BLK), BF16),
        compiler_params=pltpu.CompilerParams(vmem_limit_bytes=60 * MIB),
        cost_estimate=pl.CostEstimate(
            flops=4 * tokens * D * FF, bytes_accessed=50 * MIB, transcendentals=0
        ),
        name="feed_grads",
    )(code, first, d_down, active, d_up, *others)


QKV_PLACES = ((0, 6, 6), (36, 6, 6), (72, 6, 6))


def spread_late_kernel(code_ref, grad, small_ref, query_ref, value_ref, _, out, small_out, sem):
    for which, place in enumerate(QKV_PLACES):

        def move(block, row, col, which=which):
            pltpu.make_async_copy(
                grad.at[pl.ds(row, BLK), pl.ds(which * D + col, BLK)], out.at[code_ref[block]], sem
            ).start()

        each_block(*place, move)
    join_small(small_ref, query_ref, value_ref, small_out)
    wait_whole(grad, sem)


def spread_late(code, grad, small, g_query, g_value, terms):
    vmem = pl.BlockSpec(memory_space=pltpu.VMEM)
    anywhere = pl.BlockSpec(memory_space=pltpu.HBM)
    return pl.pallas_call(
        spread_late_kernel,
        grid_spec=pltpu.PrefetchScalarGridSpec(
            num_scalar_prefetch=1,
            grid=(1,),
            in_specs=[vmem] * 4 + [anywhere],
            out_specs=[anywhere, vmem],
            scratch_shapes=[pltpu.SemaphoreType.DMA],
        ),
        out_shape=[
            jax.ShapeDtypeStruct(terms.shape, BF16),
            jax.ShapeDtypeStruct(small.shape, F32),
        ],
        input_output_aliases={5: 0},
        compiler_params=pltpu.CompilerParams(vmem_limit_bytes=44 * MIB),
        name="spread_late",
    )(code, grad, small, g_query, g_value, terms)


def half_masks():
    lane = lax.broadcasted_iota(jnp.int32, (1, BLK), 1)
    low = (lane < BLK // 2).astype(BF16)
    return low, (1.0 - low.astype(F32)).astype(BF16)


def stack_heads(values, low, high):
    return jnp.concatenate([values * low, values * high], axis=0)


def pick_heads(values):
    rows = values.shape[0] // 2
    lane = lax.broadcasted_iota(jnp.int32, (rows, BLK), 1)
    return jnp.where(lane < BLK // 2, values[:rows], values[rows:])


def pipelined(count, before, middle, after):
    started = before(0)
    done = None
    for index in range(count):
        current = started
        if index + 1 < count:
            started = before(index + 1)
        if done is not None:
            after(index - 1, done)
        done = middle(index, current)
    after(count - 1, done)


def softmax(scores, length):
    visible = lax.broadcasted_iota(jnp.int32, scores.shape, 1) < length
    scores = jnp.where(visible, scores, MASKED_SCORE)
    powers = jnp.exp(scores - jnp.max(scores, axis=-1, keepdims=True))
    total = jnp.sum(powers, axis=-1, keepdims=True)
    return (powers * (1.0 / total)).astype(BF16)


def attention_kernel(
    len_short,
    len_long,
    x_short_ref,
    x_long_ref,
    params,
    w_ref,
    x_ref,
    q_ref,
    k_ref,
    v_ref,
    context_ref,
    short_ref,
    long_ref,
    bias,
    *,
    short_tiles,
):
    tile = pl.program_id(0)
    group = pl.program_id(1)
    low, high = half_masks()
    width = short_ref.shape[-1]
    per_tile = TILE // width

    wide = PAIRS * BLK
    start = pl.multiple_of(group * wide, wide)

    @pl.when((tile == 0) & (group == 0))
    def _():
        for which in range(2):
            for place in range(D // BLK):
                row = which * (D // BLK) + place
                bias[which : which + 1, place * BLK : (place + 1) * BLK] = params[row : row + 1, :]

    @pl.when((tile < short_tiles) & (group == 0))
    def _():
        x_ref[...] = x_short_ref[...]

    @pl.when((tile >= short_tiles) & (group == 0))
    def _():
        x_ref[...] = x_long_ref[...]

    @pl.when(group == 0)
    def _():
        rows_in = x_ref[...]
        queries = product(rows_in, w_ref[:, :D]) + bias[0:1, :]
        q_ref[...] = (queries * 0.125).astype(BF16)
        k_ref[...] = product(rows_in, w_ref[:, D : 2 * D]).astype(BF16)
        v_ref[...] = (product(rows_in, w_ref[:, 2 * D :]) + bias[1:2, :]).astype(BF16)

    def inner(pair):
        return pl.ds(pl.multiple_of(start + pair * BLK, BLK), BLK)

    def attend(units, kept_ref):
        def scores(index):
            rows, keys, pair, _, _ = units[index]
            return right_product(stack_heads(q_ref[rows, inner(pair)], low, high), k_ref[keys, inner(pair)])

        def weigh(index, values):
            _, _, _, length, place = units[index]
            probs = softmax(values, length)
            kept_ref[place] = probs
            return probs

        def mix(index, probs):
            rows, keys, pair, _, _ = units[index]
            mixed = pick_heads(product(probs, v_ref[keys, inner(pair)])).astype(BF16)
            context_ref[rows, pair * BLK : (pair + 1) * BLK] = mixed

        pipelined(len(units), scores, weigh, mix)

    @pl.when(tile < short_tiles)
    def _():
        units = []
        for seq in range(per_tile):
            rows = slice(seq * width, (seq + 1) * width)
            length = len_short[tile * per_tile + seq]
            for pair in range(PAIRS):
                units.append((rows, rows, pair, length, (0, pair, seq)))
        attend(units, short_ref)

    @pl.when(tile >= short_tiles)
    def _():
        length = len_long[tile - short_tiles]
        half = TILE // 2
        units = []
        for pair in range(PAIRS):
            for part in range(2):
                rows = slice(part * half, (part + 1) * half)
                units.append((rows, slice(0, TILE), pair, length, (0, pair, part)))
        attend(units, long_ref)


def run_events(step, events):
    for index, actions in enumerate(events):

        @pl.when(step == index)
        def _(actions=actions):
            for action in actions:
                action()


def probs_shapes(short_tiles, long_tiles, width):
    per_tile = TILE // width
    return (
        (short_tiles, 2 * PAIRS, per_tile, 2 * width, width),
        (long_tiles, 2 * PAIRS, 2, TILE, TILE),
    )


def short_index(tile, short_tiles):
    return jnp.minimum(tile, short_tiles - 1)


def long_index(tile, short_tiles):
    return jnp.maximum(tile - short_tiles, 0)


def probs_maps(short_tiles):
    def short_map(tile, group):
        last = jnp.minimum(tile // short_tiles, 1)
        return (short_index(tile, short_tiles), group + last * (GROUPS - 1 - group), 0, 0, 0)

    def long_map(tile, group):
        begun = jnp.minimum(tile // short_tiles, 1)
        return (long_index(tile, short_tiles), begun * group, 0, 0, 0)

    return short_map, long_map


def attention(len_short, len_long, x_short, x_long, params, w_qkv, short_tiles, width):
    tiles = (x_short.shape[0] + x_long.shape[0]) // TILE
    wide = PAIRS * BLK
    short_shape, long_shape = probs_shapes(short_tiles, tiles - short_tiles, width)
    short_map, long_map = probs_maps(short_tiles)
    flops = 4 * D * TILE * TILE * tiles + 6 * D * D * TILE * tiles
    rows = pl.BlockSpec((TILE, wide), lambda tile, group: (tile, group))
    scalars = pl.BlockSpec(memory_space=pltpu.SMEM)

    def whole(shape):
        return pl.BlockSpec(shape, lambda tile, group: (0,) * len(shape), pipeline_mode=pl.Buffered(1))

    in_specs = [
        scalars,
        scalars,
        pl.BlockSpec((TILE, D), lambda tile, group: (short_index(tile, short_tiles), 0)),
        pl.BlockSpec((TILE, D), lambda tile, group: (long_index(tile, short_tiles), 0)),
        whole(params.shape),
        whole((D, 3 * D)),
    ]
    full_rows = pl.BlockSpec((TILE, D), lambda tile, group: (tile, 0))
    out_specs = [
        full_rows,
        full_rows,
        full_rows,
        full_rows,
        rows,
        pl.BlockSpec((1, PAIRS) + short_shape[2:], short_map),
        pl.BlockSpec((1, PAIRS) + long_shape[2:], long_map),
    ]
    out_shape = [jax.ShapeDtypeStruct((tiles * TILE, D), BF16)] * 5 + [
        jax.ShapeDtypeStruct(short_shape, BF16),
        jax.ShapeDtypeStruct(long_shape, BF16),
    ]
    arguments = [len_short, len_long, x_short, x_long, params, w_qkv]
    return pl.pallas_call(
        partial(attention_kernel, short_tiles=short_tiles),
        grid=(tiles, GROUPS),
        in_specs=in_specs,
        out_specs=out_specs,
        out_shape=out_shape,
        scratch_shapes=[pltpu.VMEM((8, D), F32)],
        compiler_params=pltpu.CompilerParams(vmem_limit_bytes=60 * MIB),
        cost_estimate=pl.CostEstimate(
            flops=flops, bytes_accessed=35 * MIB, transcendentals=HEADS * TILE * TILE * tiles // 2
        ),
        name="attention",
    )(*arguments)


def back_place(step, work_steps):
    last = jnp.minimum(step // work_steps, 1)
    tile = jnp.minimum(step // GROUPS, work_steps // GROUPS - 1)
    return tile, step % GROUPS * (1 - last) + (GROUPS - 1) * last


def attention_back_kernel(*refs, short_tiles, transfers):
    q_ref, k_ref, v_ref, short_ref, long_ref, dc_ref, x_ref = refs[:7]
    refs = refs[7:]
    if transfers:
        terms_ref, refs = refs[0], refs[1:]
    out_ref, bq_ref, bv_ref, weights_ref = refs[:4]
    turned, kept = refs[-2:]
    step = pl.program_id(0)
    work_steps = pl.num_programs(0) - 3
    tile, group = back_place(step, work_steps)
    low, high = half_masks()
    width = short_ref.shape[-1]
    per_tile = TILE // width
    if transfers:
        reduce = Reduce(terms_ref, 0, refs[4], refs[5:-2])
        run_events(
            step,
            (
                (reduce.start,),
                (partial(reduce.core, 0),),
                (partial(reduce.core, 1), partial(reduce.first, 0)),
                (partial(reduce.core, 2), partial(reduce.first, 1), partial(reduce.second, 0)),
                (partial(reduce.core, 3), partial(reduce.first, 2), partial(reduce.second, 1)),
                (),
                (),
                (partial(reduce.first, 3), partial(reduce.second, 2)),
                (partial(reduce.second, 3), reduce.share),
                (reduce.share_on,),
            ),
        )

    wide = PAIRS * BLK
    start = pl.multiple_of(group * wide, wide)

    def columns(which, cols):
        return pl.ds(pl.multiple_of(which * D + start + cols.start, BLK), BLK)

    def go_back(units, kept_ref, parts):
        sums = {}

        def spread_in(index):
            rows, keys, cols, _ = units[index]
            return right_product(stack_heads(dc_ref[rows, cols], low, high), v_ref[keys, cols])

        def differ(index, d_probs):
            wide = kept_ref[units[index][3]].astype(F32)
            weighted = wide * d_probs
            return (weighted - wide * jnp.sum(weighted, axis=-1, keepdims=True)).astype(BF16)

        def gather_up(index, d_scores):
            rows, keys, cols, place = units[index]
            d_queries = pick_heads(product(d_scores, k_ref[keys, cols])) * 0.125
            out_ref[rows, columns(0, cols)] = d_queries.astype(BF16)
            d_keys = left_product(d_scores, stack_heads(q_ref[rows, cols], low, high))
            d_values = left_product(kept_ref[place], stack_heads(dc_ref[rows, cols], low, high))
            if index % parts:
                d_keys += sums["keys"]
                d_values += sums["values"]
            if index % parts == parts - 1:
                out_ref[keys, columns(1, cols)] = d_keys.astype(BF16)
                out_ref[keys, columns(2, cols)] = d_values.astype(BF16)
            else:
                sums.update(keys=d_keys, values=d_values)

        pipelined(len(units), spread_in, differ, gather_up)

    @pl.when((tile < short_tiles) & (step < work_steps))
    def _():
        units = []
        for seq in range(per_tile):
            rows = slice(seq * width, (seq + 1) * width)
            for pair in range(PAIRS):
                cols = slice(pair * BLK, (pair + 1) * BLK)
                units.append((rows, rows, cols, (0, pair, seq)))
        go_back(units, short_ref, 1)

    @pl.when((tile >= short_tiles) & (step < work_steps))
    def _():
        half = TILE // 2
        units = []
        for pair in range(PAIRS):
            cols = slice(pair * BLK, (pair + 1) * BLK)
            for part in range(2):
                rows = slice(part * half, (part + 1) * half)
                units.append((rows, slice(0, TILE), cols, (0, pair, part)))
        go_back(units, long_ref, 2)

    tokens = pl.ds(pl.multiple_of(tile * TILE, TILE), TILE)

    @pl.when((group == 0) & (step < work_steps))
    def _():
        turned[:, tokens] = x_ref[...].T

    @pl.when(step == 0)
    def _():
        bq_ref[...] = jnp.zeros_like(bq_ref)
        bv_ref[...] = jnp.zeros_like(bv_ref)

    @pl.when(step < work_steps)
    def _():
        for which in range(3):
            cols = pl.ds(pl.multiple_of(which * D + start, BLK), wide)
            kept[tokens, cols] = out_ref[:, cols]
        bq_ref[:, pl.ds(start, wide)] += column_sum(out_ref[:, pl.ds(start, wide)])
        bv_ref[:, pl.ds(start, wide)] += column_sum(out_ref[:, pl.ds(2 * D + start, wide)])

    @pl.when(step >= work_steps)
    def _():
        cols = pl.ds(pl.multiple_of((step - work_steps) * D, BLK), D)
        weights_ref[...] = product(turned[...], kept[:, cols]).astype(BF16)

    if transfers:

        @pl.when(step == pl.num_programs(0) - 1)
        def _():
            reduce.finish()


def attention_back(qkv, probs_short, probs_long, d_context, x, short_tiles, terms=None, count=0):
    tiles = d_context.shape[0] // TILE
    wide = PAIRS * BLK
    short_map, long_map = probs_maps(short_tiles)
    work_steps = tiles * GROUPS

    def spec(shape, index):
        return pl.BlockSpec(shape, lambda step: index(*back_place(step, work_steps)))

    rows = spec((TILE, wide), lambda tile, group: (tile, group))
    row = pl.BlockSpec((1, D), lambda step: (0, 0))
    flops = 10 * D * TILE * TILE * tiles + 6 * D * D * TILE * tiles
    in_specs = [
        rows,
        rows,
        rows,
        spec((1, PAIRS) + probs_short.shape[2:], short_map),
        spec((1, PAIRS) + probs_long.shape[2:], long_map),
        rows,
        spec((TILE, D), lambda tile, group: (tile, 0)),
    ]
    out_specs = [
        spec((TILE, 3 * D), lambda tile, group: (tile, 0)),
        row,
        row,
        pl.BlockSpec((D, D), lambda step: (0, jnp.maximum(step - work_steps, 0))),
    ]
    out_shape = [
        jax.ShapeDtypeStruct((tiles * TILE, 3 * D), BF16),
        jax.ShapeDtypeStruct((1, D), F32),
        jax.ShapeDtypeStruct((1, D), F32),
        jax.ShapeDtypeStruct((D, 3 * D), BF16),
    ]
    arguments = [*qkv, probs_short, probs_long, d_context, x]
    scratch = []
    params = dict(vmem_limit_bytes=60 * MIB)
    if terms is not None:
        arguments.append(terms)
        in_specs.append(pl.BlockSpec(memory_space=pltpu.HBM))
        out_specs.append(pl.BlockSpec((count, BLK), lambda step: (0, 0)))
        out_shape.append(jax.ShapeDtypeStruct((count, BLK), BF16))
        scratch = reduce_scratch(count)
        params.update(collective_id=2, has_side_effects=True)
    return pl.pallas_call(
        partial(attention_back_kernel, short_tiles=short_tiles, transfers=terms is not None),
        grid=(work_steps + 3,),
        in_specs=in_specs,
        out_specs=out_specs,
        out_shape=out_shape,
        scratch_shapes=scratch
        + [pltpu.VMEM((D, tiles * TILE), BF16), pltpu.VMEM((tiles * TILE, 3 * D), BF16)],
        compiler_params=pltpu.CompilerParams(**params),
        cost_estimate=pl.CostEstimate(flops=flops, bytes_accessed=50 * MIB, transcendentals=0),
        name="attention_back",
    )(*arguments)


INPUT_ROWS = 256


def input_product(d_ref, resid_ref, w_ref, short_ref, long_ref, short_steps):
    step = pl.program_id(0)
    total = resid_ref[...] + right_product(d_ref[...], w_ref[...])

    @pl.when(step < short_steps)
    def _():
        short_ref[...] = total

    @pl.when(step >= short_steps)
    def _():
        long_ref[...] = total


def input_specs(short_steps):
    rows = [pl.BlockSpec((INPUT_ROWS, width), lambda step: (step, 0)) for width in (3 * D, D)]
    whole = pl.BlockSpec((D, 3 * D), lambda step: (0, 0), pipeline_mode=pl.Buffered(1))
    outs = [
        pl.BlockSpec((INPUT_ROWS, D), lambda step: (short_index(step, short_steps), 0)),
        pl.BlockSpec((INPUT_ROWS, D), lambda step: (long_index(step, short_steps), 0)),
    ]
    return rows + [whole], outs


def input_grads(d_qkv, resid, w_qkv, short_tiles):
    steps = resid.shape[0] // INPUT_ROWS
    short_steps = short_tiles * TILE // INPUT_ROWS
    in_specs, out_specs = input_specs(short_steps)
    return pl.pallas_call(
        partial(input_product, short_steps=short_steps),
        grid=(steps,),
        in_specs=in_specs,
        out_specs=out_specs,
        out_shape=[
            jax.ShapeDtypeStruct((short_steps * INPUT_ROWS, D), F32),
            jax.ShapeDtypeStruct(((steps - short_steps) * INPUT_ROWS, D), F32),
        ],
        compiler_params=pltpu.CompilerParams(vmem_limit_bytes=60 * MIB),
        name="input_grads",
    )(d_qkv, resid, w_qkv)


def normal_parts(values):
    below = 0.5 * lax.erf(values * 0.7071067811865476) + 0.5
    return below, jnp.exp(-0.5 * values * values) * 0.3989422804014327


B_OUT, GAIN_ONE, SHIFT_ONE, B_UP, B_DOWN, GAIN_TWO, SHIFT_TWO, B_STUDENT, POOL_QUERY, B_HIDDEN = range(10)
VECTORS = (
    (12, 6),
    (18, 6),
    (24, 6),
    (30, 24),
    (54, 6),
    (60, 6),
    (66, 6),
    (72, 1),
    (73, 1),
    (74, 1),
)
CLASS_ROW = 75
LAST_ROW = 91
SMALL_ROWS = 96


def norm_parts(values):
    center = values - jnp.mean(values, axis=-1, keepdims=True)
    spread = jnp.mean(center * center, axis=-1, keepdims=True)
    inverse = lax.rsqrt(spread + NORM_EPSILON)
    return center * inverse, inverse


def norm_back(d_values, gain, unit, inverse):
    d_unit = d_values * gain
    return inverse * (
        d_unit
        - jnp.mean(d_unit, axis=-1, keepdims=True)
        - unit * jnp.mean(d_unit * unit, axis=-1, keepdims=True)
    )


def column_sum(values):
    return jnp.sum(values.astype(F32), axis=0, keepdims=True)


def pool_weights(student, query, length):
    scaled = student * query
    lane = lax.broadcasted_iota(jnp.int32, scaled.shape, 1)
    place = lax.broadcasted_iota(jnp.int32, (scaled.shape[0], 1), 0)
    weights = []
    for side in (lane < SD // PH, lane >= SD // PH):
        scores = jnp.sum(jnp.where(side, scaled, 0.0), axis=-1, keepdims=True)
        scores = jnp.where(place < length, scores, MASKED_SCORE)
        powers = jnp.exp(scores - jnp.max(scores, axis=0, keepdims=True))
        weights.append(powers / jnp.sum(powers, axis=0, keepdims=True))
    return jnp.where(lane < SD // PH, weights[0], weights[1]), weights


def student_back(student, query, weights, both, d_pooled):
    lane = lax.broadcasted_iota(jnp.int32, student.shape, 1)
    moved = student * d_pooled
    d_scores = []
    for side, weight in zip((lane < SD // PH, lane >= SD // PH), weights):
        d_weight = jnp.sum(jnp.where(side, moved, 0.0), axis=-1, keepdims=True)
        d_scores.append(weight * (d_weight - jnp.sum(weight * d_weight, axis=0, keepdims=True)))
    d_score = jnp.where(lane < SD // PH, d_scores[0], d_scores[1])
    d_query = jnp.sum(d_score * student, axis=0, keepdims=True) * 0.125
    return both * d_pooled + d_score * query, d_query


def feed_kernel(
    len_short,
    len_long,
    slot_ref,
    x_ref,
    context_ref,
    cot_short_ref,
    cot_long_ref,
    logit_cot_short,
    logit_cot_long,
    params,
    w_class_ref,
    b_class_ref,
    blocks,
    enc_short_ref,
    enc_long_ref,
    logits_short,
    logits_long,
    first_ref,
    active_ref,
    d_up_ref,
    d_down_ref,
    d_branch_ref,
    d_context_ref,
    d_resid_ref,
    g_student,
    g_hidden,
    g_small,
    slope,
    pooled_ref,
    d_student_ref,
    w_out,
    w_up,
    w_down,
    w_student,
    w_hidden,
    vectors,
    totals,
    g_class,
    g_last,
    w_class,
    b_class,
    logit_cot,
    sems,
    *,
    short_tiles,
    width,
):
    tile = pl.program_id(0)
    per_tile = TILE // width
    loads = ((w_out, 108, 6, 6), (w_up, 144, 6, 24), (w_down, 288, 24, 6), (w_student, 432, 6, 1), (w_hidden, 438, 1, 1))

    def arrive(*indices):
        @pl.when(tile == 0)
        def _():
            for index in indices:
                wait_whole(loads[index][0], sems.at[index])

    @pl.when(tile == 0)
    def _():
        for index, (target, block, row_count, col_count) in enumerate(loads):
            load_blocks(slot_ref, blocks, target, sems.at[index], block, row_count, col_count)
        for index, (start, count) in enumerate(VECTORS):
            for place in range(count):
                vectors[index : index + 1, place * BLK : (place + 1) * BLK] = params[
                    start + place : start + place + 1, :
                ]
        for ref in (totals, g_class, g_last, g_student, g_hidden, w_class, b_class):
            ref[...] = jnp.zeros_like(ref)
        w_class[:, :NCLS] = w_class_ref[...]
        b_class[:, :NCLS] = b_class_ref[...]

    def vector(index):
        return vectors[index : index + 1, : VECTORS[index][1] * BLK]

    def add_total(index, values):
        totals[index : index + 1, : VECTORS[index][1] * BLK] += column_sum(values)

    arrive(0)
    sides = [slice(start, start + TILE // 2) for start in range(0, TILE, TILE // 2)]
    units_one, inverses_one, firsts = [], [], []

    def branch(index):
        return product(context_ref[sides[index]], w_out[...])

    def norm_first(index, values):
        rows = sides[index]
        unit, inverse = norm_parts(x_ref[rows].astype(F32) + (values + vector(B_OUT)))
        units_one.append(unit)
        inverses_one.append(inverse)
        firsts.append((unit * vector(GAIN_ONE) + vector(SHIFT_ONE)).astype(BF16))
        first_ref[:, rows] = firsts[-1].T

    pipelined(2, branch, norm_first, lambda *_: None)
    first = jnp.concatenate(firsts, axis=0)
    arrive(1)
    chunks = [slice(start, start + CHUNK) for start in range(0, FF, CHUNK)]

    def rise(index):
        return product(first, w_up[:, chunks[index]])

    def bend(index, upward):
        upward = upward + vectors[B_UP : B_UP + 1, chunks[index]]
        below, density = normal_parts(upward)
        active_ref[:, chunks[index]] = (upward * below).astype(BF16)
        slope[:, chunks[index]] = (below + upward * density).astype(BF16)

    pipelined(len(chunks), rise, bend, lambda *_: None)
    arrive(2, 3, 4)
    units_two, inverses_two, encodeds = [], [], []

    def sink(index):
        return product(active_ref[sides[index]], w_down[...])

    def norm_second(index, values):
        unit, inverse = norm_parts(firsts[index].astype(F32) + (values + vector(B_DOWN)))
        units_two.append(unit)
        inverses_two.append(inverse)
        encodeds.append((unit * vector(GAIN_TWO) + vector(SHIFT_TWO)).astype(BF16))

    pipelined(2, sink, norm_second, lambda *_: None)
    encoded = jnp.concatenate(encodeds, axis=0)

    @pl.when(tile < short_tiles)
    def _():
        enc_short_ref[...] = encoded

    @pl.when(tile >= short_tiles)
    def _():
        enc_long_ref[...] = encoded

    student = product(encoded, w_student[...]) + vector(B_STUDENT)
    query = vector(POOL_QUERY) * 0.125
    pooled_ref[...] = jnp.zeros_like(pooled_ref)

    def head():
        pooled = pooled_ref[...]
        wide_hidden = w_hidden[...].astype(F32)
        hidden = jnp.tanh(product(pooled, wide_hidden) + vector(B_HIDDEN))
        logits = product(hidden, w_class[...]) + b_class[...]
        d_logits = logit_cot[...]
        g_last[...] += column_sum(d_logits)
        g_class[...] += left_product(d_logits, hidden)
        d_hidden = right_product(d_logits, w_class[...])
        d_hidden = d_hidden * (1.0 - hidden * hidden)
        add_total(B_HIDDEN, d_hidden)
        g_hidden[...] += left_product(pooled, d_hidden)
        return logits, right_product(d_hidden, wide_hidden)

    def pool(starts, size, lengths, cot_ref, logits_ref, first):
        count = len(starts)
        logit_cot[...] = jnp.zeros_like(logit_cot)
        for index in range(count):
            logit_cot[index : index + 1, :NCLS] = cot_ref[pl.ds(first + index, 1), :]
        kept = []
        for index, (start, length) in enumerate(zip(starts, lengths)):
            rows = student[start : start + size]
            both, weights = pool_weights(rows, query, length)
            pooled_ref[index : index + 1, :] = column_sum(both * rows)
            kept.append((start, rows, both, weights))
        logits, d_pooled = head()
        for index in range(count):
            logits_ref[pl.ds(first + index, 1), :] = logits[index : index + 1, :NCLS]
        for index, (start, rows, both, weights) in enumerate(kept):
            d_rows, d_query = student_back(rows, query, weights, both, d_pooled[index : index + 1])
            d_student_ref[start : start + size, :] = d_rows.astype(BF16)
            add_total(POOL_QUERY, d_query)

    @pl.when(tile < short_tiles)
    def _():
        pool(
            [seq * width for seq in range(per_tile)],
            width,
            [len_short[tile * per_tile + seq] for seq in range(per_tile)],
            logit_cot_short,
            logits_short,
            tile * per_tile,
        )

    @pl.when(tile >= short_tiles)
    def _():
        long = tile - short_tiles
        pool([0], TILE, [len_long[long]], logit_cot_long, logits_long, long)

    d_student = d_student_ref[...]
    add_total(B_STUDENT, d_student)
    g_student[...] += left_product(encoded, d_student)
    d_resids, d_downs = [], []

    def through_student(index):
        return right_product(d_student[sides[index]], w_student[...])

    def norm_second_back(index, values):
        rows = sides[index]
        cotangent = jnp.where(tile < short_tiles, cot_short_ref[rows], cot_long_ref[rows])
        d_second = cotangent.astype(F32) + values
        add_total(GAIN_TWO, d_second * units_two[index])
        add_total(SHIFT_TWO, d_second)
        d_resids.append(norm_back(d_second, vector(GAIN_TWO), units_two[index], inverses_two[index]))
        d_downs.append(d_resids[-1].astype(BF16))
        d_down_ref[:, rows] = d_downs[-1].T
        add_total(B_DOWN, d_downs[-1])

    pipelined(2, through_student, norm_second_back, lambda *_: None)
    d_down = jnp.concatenate(d_downs, axis=0)

    def fall(index):
        return right_product(d_down, w_down[chunks[index], :])

    def bend_back(index, d_active):
        d_up = (d_active * slope[:, chunks[index]].astype(F32)).astype(BF16)
        d_up_ref[:, chunks[index]] = d_up
        totals[B_UP : B_UP + 1, chunks[index]] += column_sum(d_up)

    pipelined(len(chunks), fall, bend_back, lambda *_: None)

    def rise_back(index):
        return right_product(d_up_ref[sides[index]], w_up[...])

    def norm_first_back(index, values):
        rows = sides[index]
        d_first = d_resids[index] + values
        add_total(GAIN_ONE, d_first * units_one[index])
        add_total(SHIFT_ONE, d_first)
        d_resid = norm_back(d_first, vector(GAIN_ONE), units_one[index], inverses_one[index])
        d_resid_ref[rows] = d_resid
        d_branch = d_resid.astype(BF16)
        d_branch_ref[rows] = d_branch
        add_total(B_OUT, d_branch)
        return d_branch

    def branch_back(index, d_branch):
        d_context_ref[sides[index]] = right_product(d_branch, w_out[...]).astype(BF16)

    pipelined(2, rise_back, norm_first_back, branch_back)

    @pl.when(tile == pl.num_programs(0) - 1)
    def _():
        g_small[...] = jnp.zeros_like(g_small)
        for index, (start, count) in enumerate(VECTORS):
            for place in range(count):
                g_small[start + place : start + place + 1, :] = totals[
                    index : index + 1, place * BLK : (place + 1) * BLK
                ]
        g_small[CLASS_ROW : CLASS_ROW + NCLS, :] = g_class[:NCLS, :]
        g_small[LAST_ROW : LAST_ROW + 1, :] = g_last[...]


def feed(
    len_short, len_long, block_slot, x, context, cot_short, cot_long, logit_cots, small, blocks, short_tiles, width
):
    tiles = x.shape[0] // TILE
    long_tiles = tiles - short_tiles

    def whole(shape):
        return pl.BlockSpec(shape, lambda tile, *_: (0,) * len(shape), pipeline_mode=pl.Buffered(1))

    def kept(shape):
        return pl.BlockSpec(shape, lambda tile, *_: (0,) * len(shape))

    def rows(columns):
        return pl.BlockSpec((TILE, columns), lambda tile, *_: (tile, 0))

    turned = pl.BlockSpec((D, TILE), lambda tile, *_: (0, tile))
    short_rows = pl.BlockSpec((TILE, D), lambda tile, *_: (short_index(tile, short_tiles), 0))
    long_rows = pl.BlockSpec((TILE, D), lambda tile, *_: (long_index(tile, short_tiles), 0))
    grad_shapes = ((D, SD), (SD, SD), (SMALL_ROWS, BLK))
    total = tiles * TILE
    return pl.pallas_call(
        partial(feed_kernel, short_tiles=short_tiles, width=width),
        grid_spec=pltpu.PrefetchScalarGridSpec(
            num_scalar_prefetch=3,
            grid=(tiles,),
            in_specs=[rows(D), rows(D), short_rows, long_rows]
            + [whole(array.shape) for array in (*logit_cots, *small)]
            + [pl.BlockSpec(memory_space=pltpu.HBM)],
            out_specs=[
                short_rows,
                long_rows,
                kept(logit_cots[0].shape),
                kept(logit_cots[1].shape),
                turned,
                rows(FF),
                rows(FF),
                turned,
                rows(D),
                rows(D),
                rows(D),
            ]
            + [kept(shape) for shape in grad_shapes],
            scratch_shapes=[
                pltpu.VMEM((TILE, FF), BF16),
                pltpu.VMEM((8, SD), F32),
                pltpu.VMEM((TILE, SD), BF16),
                pltpu.VMEM((D, D), BF16),
                pltpu.VMEM((D, FF), BF16),
                pltpu.VMEM((FF, D), BF16),
                pltpu.VMEM((D, SD), BF16),
                pltpu.VMEM((SD, SD), BF16),
                pltpu.VMEM((16, FF), F32),
                pltpu.VMEM((16, FF), F32),
                pltpu.VMEM((SD, SD), F32),
                pltpu.VMEM((1, SD), F32),
                pltpu.VMEM((SD, SD), F32),
                pltpu.VMEM((1, SD), F32),
                pltpu.VMEM((8, SD), F32),
                pltpu.SemaphoreType.DMA((5,)),
            ],
        ),
        out_shape=[
            jax.ShapeDtypeStruct((short_tiles * TILE, D), BF16),
            jax.ShapeDtypeStruct((long_tiles * TILE, D), BF16),
            jax.ShapeDtypeStruct(logit_cots[0].shape, F32),
            jax.ShapeDtypeStruct(logit_cots[1].shape, F32),
            jax.ShapeDtypeStruct((D, total), BF16),
            jax.ShapeDtypeStruct((total, FF), BF16),
            jax.ShapeDtypeStruct((total, FF), BF16),
            jax.ShapeDtypeStruct((D, total), BF16),
            jax.ShapeDtypeStruct((total, D), BF16),
            jax.ShapeDtypeStruct((total, D), BF16),
            jax.ShapeDtypeStruct((total, D), F32),
        ]
        + [jax.ShapeDtypeStruct(shape, F32) for shape in grad_shapes],
        compiler_params=pltpu.CompilerParams(vmem_limit_bytes=62 * MIB),
        cost_estimate=pl.CostEstimate(
            flops=total * (8 * D * FF + 4 * D * D), bytes_accessed=70 * MIB, transcendentals=total * FF
        ),
        name="feed",
    )(len_short, len_long, block_slot, x, context, cot_short, cot_long, *logit_cots, *small, blocks)


class Place:
    def __init__(self):
        self.quarter = lax.axis_index("dp")
        self.shard = lax.axis_index("fsdp")
        x = self.quarter % 2
        y = self.quarter // 2
        self.core = self.shard % 2
        self.z = self.shard // 2
        self.high = self.z // 2
        self.by_x = 2 * y + 1 - x
        self.by_y = 2 * (1 - y) + x
        self.across = 2 * (1 - y) + 1 - x
        self.sibling = (self.quarter, 2 * self.z + 1 - self.core)
        self.next_x = (self.by_x, self.shard)
        self.next_y = (self.by_y, self.shard)
        self.inner = (self.z > 0) & (self.z < 3)

    def at_z(self, z):
        return (self.quarter, 2 * z + self.core)


def transfer(source, target, send_sem, recv_sem, device):
    return pltpu.make_async_remote_copy(
        src_ref=source,
        dst_ref=target,
        send_sem=send_sem,
        recv_sem=recv_sem,
        device_id=device,
        device_id_type=pl.DeviceIdType.MESH,
    )


def greet(place, extra=()):
    barrier = pltpu.get_barrier_semaphore()

    def signal(device):
        pl.semaphore_signal(barrier, inc=1, device_id=device, device_id_type=pl.DeviceIdType.MESH)

    near = (place.sibling, place.next_x, place.next_y) + tuple(extra)
    for device in near:
        signal(device)

    @pl.when(place.z > 0)
    def _():
        signal(place.at_z(place.z - 1))

    @pl.when(place.z < 3)
    def _():
        signal(place.at_z(place.z + 1))

    pl.semaphore_wait(barrier, len(near) + 1 + (place.z + 1) // 2 % 2)


CUTS = 2
GATHER_SEMAPHORES = [
    pltpu.SemaphoreType.DMA((2 * CUTS,)),
    pltpu.SemaphoreType.DMA((3 * CUTS,)),
    pltpu.SemaphoreType.DMA((4 * CUTS,)),
    pltpu.SemaphoreType.DMA((12 * CUTS,)),
    pltpu.SemaphoreType.DMA((12 * CUTS,)),
    pltpu.SemaphoreType.DMA((1 + 18 * CUTS,)),
    pltpu.SemaphoreType.DMA((1 + 18 * CUTS,)),
    pltpu.SemaphoreType.DMA((8,)),
    pltpu.SemaphoreType.DMA((2 * CUTS,)),
    pltpu.SemaphoreType.DMA((3 * CUTS,)),
    pltpu.SemaphoreType.DMA((4 * CUTS,)),
]


class Gather:
    def __init__(self, full, out, sems):
        self.place = place = Place()
        self.full, self.out = full, out
        (
            self.own_send,
            self.relay_send,
            self.z_recv,
            self.xy_send,
            self.xy_recv,
            self.core_send,
            self.core_recv,
            self.out_sems,
            self.own_more,
            self.relay_more,
            self.z_more,
        ) = sems
        self.quarter = full.shape[1] // 4
        self.cut = self.quarter // CUTS
        self.z_part = self.cut // 64 * 16
        self.first_part = ((self.cut - self.z_part) // 16 + 1) // 2 * 16
        self.last_part = self.cut - self.z_part - self.first_part
        z = place.z
        self.origins = (z + 1 - 2 * (z % 2), 2 - place.high, 3 * (1 - place.high))
        self.relays = (3 - z, 3 * (z - 1), 3 * (z - 1))

    def region(self, which, start, size):
        return self.full.at[which, pl.ds(pl.multiple_of(start, 16), size)]

    def pieces(self, which, turn):
        place, quarter, cut, part = self.place, self.quarter, self.cut, self.first_part
        skip = turn % CUTS * cut
        return (
            self.region(which, place.quarter * quarter + skip, cut),
            self.region(which, place.by_x * quarter + skip, cut),
            self.region(which, place.by_y * quarter + skip, cut),
            self.region(which, place.across * quarter + skip, part),
            self.region(which, place.across * quarter + skip + part, self.last_part),
            self.region(which, place.across * quarter + skip + cut - self.z_part, self.z_part),
        )

    def own_copy(self, side, cut, more=False):
        place = self.place
        mine = self.pieces(place.shard, cut)[5 if more else 0]
        device = place.at_z(place.z - 1 + 2 * side)
        send, recv = (self.own_more, self.z_more) if more else (self.own_send, self.z_recv)
        return transfer(
            mine, mine, send.at[side * CUTS + cut], recv.at[place.z * CUTS + cut], device
        )

    def core_copy(self, index, ref):
        return transfer(ref, ref, self.core_send.at[index], self.core_recv.at[index], self.place.sibling)

    def xy_copy(self, index, ref, device):
        return transfer(ref, ref, self.xy_send.at[index], self.xy_recv.at[index], device)

    def store(self, index, which):
        return pltpu.make_async_copy(self.full.at[which], self.out.at[which], self.out_sems.at[index])

    def mirrored(self, step):
        return 2 * self.origins[step] + 1 - self.place.core

    def held(self, step):
        return 2 * self.origins[step] + self.place.core

    def start(self):
        place = self.place
        greet(place)
        for cut in range(CUTS):

            for more in (False, True):

                @pl.when(place.z > 0)
                def _():
                    self.own_copy(0, cut, more).start()

                @pl.when(place.z < 3)
                def _():
                    self.own_copy(1, cut, more).start()

        self.core_copy(0, self.full.at[place.shard]).start()
        self.store(0, place.shard).start()

    def relay(self, turn, more=False):
        step = turn // CUTS
        piece = self.pieces(self.held(step), turn)[5 if more else 0]
        device = self.place.at_z(self.relays[step])
        send, recv = (self.relay_more, self.z_more) if more else (self.relay_send, self.z_recv)
        sem = recv.at[self.origins[step] * CUTS + turn % CUTS]
        return transfer(piece, piece, send.at[turn], sem, device)

    def along_z(self, turn):
        place = self.place
        self.relay(turn).wait_recv()

        @pl.when(place.inner)
        def _():
            self.relay(turn).start()

        pieces = self.pieces(self.held(turn // CUTS), turn)
        self.xy_copy(4 * turn, pieces[0], place.next_x).start()
        self.xy_copy(4 * turn + 1, pieces[0], place.next_y).start()
        self.core_copy(1 + 6 * turn, pieces[0]).start()
        self.relay(turn, True).wait_recv()

        @pl.when(place.inner)
        def _():
            self.relay(turn, True).start()

        self.core_copy(6 + 6 * turn, pieces[5]).start()

    def along_xy(self, turn):
        place, part = self.place, self.first_part
        _, by_x, by_y, *_ = self.pieces(self.held(turn // CUTS), turn)
        self.xy_copy(4 * turn, by_x, place.next_x).wait_recv()
        self.xy_copy(4 * turn + 2, by_x.at[pl.ds(0, part)], place.next_y).start()
        self.core_copy(2 + 6 * turn, by_x).start()
        self.xy_copy(4 * turn + 1, by_y, place.next_y).wait_recv()
        self.xy_copy(4 * turn + 3, by_y.at[pl.ds(part, self.last_part)], place.next_x).start()
        self.core_copy(3 + 6 * turn, by_y).start()

    def across(self, turn):
        place = self.place
        step = turn // CUTS
        _, _, _, first, last, _ = self.pieces(self.held(step), turn)
        self.xy_copy(4 * turn + 2, first, place.next_y).wait_recv()
        self.core_copy(4 + 6 * turn, first).start()
        self.xy_copy(4 * turn + 3, last, place.next_x).wait_recv()
        self.core_copy(5 + 6 * turn, last).start()
        if turn % CUTS == CUTS - 1:
            self.store(2 + 2 * step, self.held(step)).start()

    def core_own(self):
        which = 2 * self.place.z + 1 - self.place.core
        self.core_copy(0, self.full.at[which]).wait_recv()
        self.store(1, which).start()

    def core(self, step):
        which = self.mirrored(step)
        for turn in range(step * CUTS, (step + 1) * CUTS):
            for index, ref in enumerate(self.pieces(which, turn)):
                self.core_copy(1 + 6 * turn + index, ref).wait_recv()
        self.store(3 + 2 * step, which).start()

    def finish(self):
        place = self.place
        for cut in range(CUTS):

            for more in (False, True):

                @pl.when(place.z > 0)
                def _():
                    self.own_copy(0, cut, more).wait_send()

                @pl.when(place.z < 3)
                def _():
                    self.own_copy(1, cut, more).wait_send()

        self.core_copy(0, self.full.at[place.shard]).wait_send()
        self.store(0, place.shard).wait()
        self.store(1, 2 * place.z + 1 - place.core).wait()
        for turn in range(3 * CUTS):

            @pl.when(place.inner)
            def _():
                self.relay(turn).wait_send()
                self.relay(turn, True).wait_send()

            pieces = self.pieces(self.held(turn // CUTS), turn)
            self.xy_copy(4 * turn, pieces[0], place.next_x).wait_send()
            self.xy_copy(4 * turn + 1, pieces[0], place.next_y).wait_send()
            self.xy_copy(4 * turn + 2, pieces[3], place.next_y).wait_send()
            self.xy_copy(4 * turn + 3, pieces[4], place.next_x).wait_send()
            for index, ref in enumerate(pieces):
                self.core_copy(1 + 6 * turn + index, ref).wait_send()
        for step in range(3):
            self.store(2 + 2 * step, self.held(step)).wait()
            self.store(3 + 2 * step, self.mirrored(step)).wait()


def gather_kernel(master_ref, out_ref, full, *sems):
    gather = Gather(full, out_ref, sems)
    full[gather.place.shard] = master_ref[...].astype(BF16)
    gather.start()
    turns = 3 * CUTS
    for turn in range(turns + 2):
        if turn < turns:
            gather.along_z(turn)
        if 1 <= turn <= turns:
            gather.along_xy(turn - 1)
        if turn >= 2:
            gather.across(turn - 2)
        if turn == 2:
            gather.core_own()
        if turn >= 4 and turn % CUTS == 0:
            gather.core(turn // CUTS - 2)
    gather.core(2)
    gather.finish()


def gather_shards(master):
    rows = master.shape[0] * BLK
    shards = lax.axis_size("fsdp")
    return pl.pallas_call(
        gather_kernel,
        in_specs=[pl.BlockSpec(memory_space=pltpu.VMEM)],
        out_specs=pl.BlockSpec(memory_space=pltpu.HBM),
        out_shape=jax.ShapeDtypeStruct((shards, rows, BLK), BF16),
        scratch_shapes=[pltpu.VMEM((shards, rows, BLK), BF16)] + GATHER_SEMAPHORES,
        compiler_params=pltpu.CompilerParams(
            collective_id=0, has_side_effects=True, vmem_limit_bytes=60 * MIB
        ),
        cost_estimate=pl.CostEstimate(flops=0, bytes_accessed=200 * MIB, transcendentals=0),
        name="gather",
    )(master.reshape(rows, BLK)).reshape(-1, BLK, BLK)


def add_rows(target, former, latter, rows, step):
    @pl.loop(0, rows // step)
    def _(index):
        part = pl.ds(pl.multiple_of(index * step, 16), step)
        target[part] = (former[part].astype(F32) + latter[part].astype(F32)).astype(BF16)


def reduce_scratch(rows):
    quarter = rows // 4
    half = quarter // 2
    return [
        pltpu.VMEM((4, rows, BLK), BF16),
        pltpu.VMEM((4, rows, BLK), BF16),
        pltpu.VMEM((4, 2, half, BLK), BF16),
        pltpu.VMEM((4, 2, half, BLK), BF16),
        pltpu.VMEM((4, half, BLK), BF16),
        pltpu.VMEM((4, half, BLK), BF16),
        pltpu.VMEM((5, quarter, BLK), BF16),
        pltpu.VMEM((rows, BLK), BF16),
        pltpu.SemaphoreType.DMA((4,)),
        pltpu.SemaphoreType.DMA((4,)),
        pltpu.SemaphoreType.DMA((4,)),
        pltpu.SemaphoreType.DMA((24,)),
        pltpu.SemaphoreType.DMA((24,)),
        pltpu.SemaphoreType.DMA((3,)),
        pltpu.SemaphoreType.DMA((5,)),
        pltpu.SemaphoreType.DMA((4,)),
        pltpu.SemaphoreType.DMA((4,)),
    ]


class Reduce:
    def __init__(self, terms, base, out, scratch):
        self.place = place = Place()
        self.terms, self.base, self.out = terms, base, out
        (
            self.mine,
            self.sib,
            self.from_x,
            self.from_y,
            self.late_y,
            self.late_x,
            self.from_z,
            self.result,
            self.load_sems,
            self.core_send,
            self.core_recv,
            self.xy_send,
            self.xy_recv,
            self.z_send,
            self.z_recv,
            self.last_send,
            self.last_recv,
        ) = scratch
        self.quarter = out.shape[0] // 4
        self.half = self.quarter // 2
        z, high = place.z, place.high
        low = 1 - high
        self.order = (3 * low, low * (2 - 2 * z) + high * (7 - 2 * z), 1 + z % 2, z)
        self.onward = (z + 1 - 2 * high, z + 1 - 2 * (z % 2), z + 1 - 2 * high)
        self.closing = (0, (z % 2) * low, high)
        self.far = place.at_z(z + 2 - 4 * high)
        self.near = place.at_z(z + 1 - 2 * (z % 2))

    def shard_terms(self, shard):
        rows = self.out.shape[0]
        return self.terms.at[pl.ds(pl.multiple_of(self.base + shard * rows, 16), rows)]

    def load(self, step):
        source = self.shard_terms(2 * self.order[step] + self.place.core)
        return pltpu.make_async_copy(source, self.mine.at[step], self.load_sems.at[step])

    def core_copy(self, step):
        return transfer(
            self.shard_terms(2 * self.order[step] + 1 - self.place.core),
            self.sib.at[step],
            self.core_send.at[step],
            self.core_recv.at[step],
            self.place.sibling,
        )

    def part(self, step, which, side):
        start = pl.multiple_of(which * self.quarter + side * self.half, 16)
        return self.mine.at[step, pl.ds(start, self.half)]

    def xy_copy(self, step, index):
        place = self.place
        source, target, device = (
            (self.part(step, place.by_x, 0), self.from_x.at[step, 0], place.next_x),
            (self.part(step, place.across, 0), self.from_x.at[step, 1], place.next_x),
            (self.part(step, place.by_y, 1), self.from_y.at[step, 0], place.next_y),
            (self.part(step, place.across, 1), self.from_y.at[step, 1], place.next_y),
            (self.part(step, place.by_y, 0), self.late_y.at[step], place.next_y),
            (self.part(step, place.by_x, 1), self.late_x.at[step], place.next_x),
        )[index]
        place = 6 * step + index
        return transfer(source, target, self.xy_send.at[place], self.xy_recv.at[place], device)

    def start(self):
        greet(self.place, (self.far,))
        for step in range(2):
            self.core_copy(step).start()
        for step in range(4):
            self.load(step).start()

    def core(self, step):
        place, quarter = self.place, self.quarter
        self.load(step).wait()
        self.core_copy(step).wait_recv()
        if step < 2:
            self.core_copy(step + 2).start()

        def add(which):
            block = pl.ds(pl.multiple_of(which * quarter, 16), quarter)
            mine = self.mine.at[step, block]
            add_rows(mine, mine, self.sib.at[step, block], quarter, self.half)

        add(place.by_x)
        add(place.across)
        self.xy_copy(step, 0).start()
        self.xy_copy(step, 1).start()
        add(place.by_y)
        self.xy_copy(step, 2).start()
        self.xy_copy(step, 3).start()
        add(place.quarter)

    def take(self, step, which, side, index, source):
        self.xy_copy(step, index).wait_recv()
        target = self.part(step, which, side)
        add_rows(target, target, source, self.half, self.half)

    def first(self, step):
        place = self.place
        self.take(step, place.by_y, 0, 1, self.from_x.at[step, 1])
        self.xy_copy(step, 4).start()
        self.take(step, place.by_x, 1, 3, self.from_y.at[step, 1])
        self.xy_copy(step, 5).start()
        self.take(step, place.quarter, 0, 0, self.from_x.at[step, 0])
        self.take(step, place.quarter, 1, 2, self.from_y.at[step, 0])

    def own_block(self, step):
        return self.mine.at[step, pl.ds(pl.multiple_of(self.place.quarter * self.quarter, 16), self.quarter)]

    def z_copy(self, step):
        goal = self.order[step]
        slot = goal + self.closing[step] * (4 - goal)
        return transfer(
            self.own_block(step),
            self.from_z.at[slot],
            self.z_send.at[step],
            self.z_recv.at[slot],
            self.place.at_z(self.onward[step]),
        )

    def take_z(self, step, slot):
        source = self.from_z.at[slot]
        transfer(source, source, self.z_send.at[0], self.z_recv.at[slot], self.near).wait_recv()
        block = self.own_block(step)
        add_rows(block, block, source, self.quarter, self.half)

    def second(self, step):
        place = self.place
        self.take(step, place.quarter, 0, 4, self.late_y.at[step])
        self.take(step, place.quarter, 1, 5, self.late_x.at[step])
        if step < 3:

            @pl.when(place.inner)
            def _():
                self.take_z(step, self.order[step])

            self.z_copy(step).start()
        else:

            @pl.when(place.z > 0)
            def _():
                self.take_z(step, place.z)

            @pl.when(place.z < 3)
            def _():
                self.take_z(step, 4)

    def final(self, which, side=None):
        start = pl.multiple_of(which * self.quarter + (0 if side is None else side * self.half), 16)
        return self.result.at[pl.ds(start, self.quarter if side is None else self.half)]

    def last_copy(self, index, ref):
        device = (self.place.next_x, self.place.next_y, self.place.next_y, self.place.next_x)[index]
        return transfer(ref, ref, self.last_send.at[index], self.last_recv.at[index], device)

    def share(self):
        own = self.final(self.place.quarter)
        own[...] = self.own_block(3)[...]
        self.last_copy(0, own).start()
        self.last_copy(1, own).start()

    def share_on(self):
        place = self.place
        self.last_copy(0, self.final(place.by_x)).wait_recv()
        self.last_copy(2, self.final(place.by_x, 0)).start()
        self.last_copy(1, self.final(place.by_y)).wait_recv()
        self.last_copy(3, self.final(place.by_y, 1)).start()

    def finish(self):
        place = self.place
        self.last_copy(2, self.final(place.across, 0)).wait_recv()
        self.last_copy(3, self.final(place.across, 1)).wait_recv()
        self.out[...] = self.result[...]
        for step in range(4):
            self.core_copy(step).wait_send()
            for index in range(6):
                self.xy_copy(step, index).wait_send()
            if step < 3:
                self.z_copy(step).wait_send()
        own = self.final(place.quarter)
        self.last_copy(0, own).wait_send()
        self.last_copy(1, own).wait_send()
        self.last_copy(2, self.final(place.by_x, 0)).wait_send()
        self.last_copy(3, self.final(place.by_y, 1)).wait_send()


def reduce_kernel(*refs, base, short_steps):
    terms, small_ref, d_ref, resid_ref, w_ref, out_ref, small_out, short_ref, long_ref = refs[:9]
    small_in, small_sum, small_send, small_recv = refs[9:13]
    reduce = Reduce(terms, base, out_ref, refs[13:])
    place = reduce.place
    partners = (place.sibling, place.next_x, place.next_y, reduce.near, reduce.far)

    def small_copy(level):
        return transfer(
            small_sum.at[level],
            small_in.at[level],
            small_send.at[level],
            small_recv.at[level],
            partners[level],
        )

    def small_start():
        small_sum[0] = small_ref[...]
        small_copy(0).start()

    def small_step(level):
        small_copy(level - 1).wait_recv()
        small_sum[level] = small_sum[level - 1] + small_in[level - 1]
        if level < 5:
            small_copy(level).start()
        else:
            small_out[...] = small_sum[5]

    run_events(
        pl.program_id(0),
        (
            (reduce.start, small_start),
            (partial(reduce.core, 0), partial(small_step, 1)),
            (partial(reduce.core, 1), partial(reduce.first, 0), partial(small_step, 2)),
            (
                partial(reduce.core, 2),
                partial(reduce.first, 1),
                partial(reduce.second, 0),
                partial(small_step, 3),
            ),
            (
                partial(reduce.core, 3),
                partial(reduce.first, 2),
                partial(reduce.second, 1),
                partial(small_step, 4),
            ),
            (partial(reduce.first, 3), partial(reduce.second, 2), partial(small_step, 5)),
            (partial(reduce.second, 3), reduce.share),
            (reduce.share_on,),
        ),
    )
    input_product(d_ref, resid_ref, w_ref, short_ref, long_ref, short_steps)

    @pl.when(pl.program_id(0) == pl.num_programs(0) - 1)
    def _():
        reduce.finish()
        for level in range(5):
            small_copy(level).wait_send()


def reduce_late(terms, base, rows, small, d_qkv, resid, w_qkv, short_tiles):
    steps = resid.shape[0] // INPUT_ROWS
    short_steps = short_tiles * TILE // INPUT_ROWS
    in_specs, out_specs = input_specs(short_steps)

    def whole(shape):
        return pl.BlockSpec(shape, lambda step: (0, 0), pipeline_mode=pl.Buffered(1))

    return pl.pallas_call(
        partial(reduce_kernel, base=base, short_steps=short_steps),
        grid=(steps,),
        in_specs=[pl.BlockSpec(memory_space=pltpu.HBM), whole(small.shape)] + in_specs,
        out_specs=[
            pl.BlockSpec((rows, BLK), lambda step: (0, 0)),
            pl.BlockSpec(small.shape, lambda step: (0, 0)),
        ]
        + out_specs,
        out_shape=[
            jax.ShapeDtypeStruct((rows, BLK), BF16),
            jax.ShapeDtypeStruct((SMALL_ROWS, BLK), F32),
            jax.ShapeDtypeStruct((short_steps * INPUT_ROWS, D), F32),
            jax.ShapeDtypeStruct(((steps - short_steps) * INPUT_ROWS, D), F32),
        ],
        scratch_shapes=[
            pltpu.VMEM((5, SMALL_ROWS, BLK), F32),
            pltpu.VMEM((6, SMALL_ROWS, BLK), F32),
            pltpu.SemaphoreType.DMA((5,)),
            pltpu.SemaphoreType.DMA((5,)),
        ]
        + reduce_scratch(rows),
        compiler_params=pltpu.CompilerParams(
            collective_id=3, has_side_effects=True, vmem_limit_bytes=60 * MIB
        ),
        cost_estimate=pl.CostEstimate(flops=0, bytes_accessed=200 * MIB, transcendentals=0),
        name="reduce",
    )(terms, small, d_qkv, resid, w_qkv)


def count_where(condition, axis):
    return jnp.sum(condition.astype(jnp.int32), axis=axis)


def slot_codes(slots, qkv_slots, slot_count, shards):
    early = slot_count - LATE
    shard = slots // slot_count
    begin = shard * slot_count
    inside = (qkv_slots[None, :] >= begin[:, None]) & (qkv_slots[None, :] < (begin + slot_count)[:, None])
    own = count_where(qkv_slots[None, :] == slots[:, None], 1)
    before = count_where(inside & (qkv_slots[None, :] < slots[:, None]), 1)
    number = count_where(inside, 1)
    position = jnp.where(own > 0, slot_count - number + before, slots - begin - before)
    code = jnp.where(
        position < early,
        shard * early + position,
        shards * early + shard * LATE + position - early,
    )
    return code, position, jnp.max(number)


def update_kernel(
    position_ref,
    held_ref,
    early,
    late,
    master,
    left_stat,
    right_stat,
    left_root,
    right_root,
    slot_grad,
    new_left,
    new_right,
    new_master,
):
    count = master.shape[0]
    first = pl.program_id(0) * count
    split = early.shape[0] // BLK

    def block(ref, place):
        return ref[pl.ds(pl.multiple_of(place * BLK, BLK), BLK)]

    def grad_of(index):
        place = position_ref[first + index]
        grad = jnp.where(
            place < split,
            block(early, jnp.minimum(place, split - 1)),
            block(late, jnp.maximum(place - split, 0)),
        )
        return jnp.where(held_ref[first + index] > 0, grad, jnp.zeros_like(grad))

    for begin in range(0, count, 4):
        some = range(begin, min(begin + 4, count))
        grads = [grad_of(index) for index in some]
        applied = [product(left_root[index].astype(BF16), grad) for index, grad in zip(some, grads)]
        outer_left = [right_product(grad, grad) for grad in grads]
        outer_right = [left_product(grad, grad) for grad in grads]
        totals = [
            product(part.astype(BF16), right_root[index].astype(BF16)) for index, part in zip(some, applied)
        ]
        for place, index in enumerate(some):
            slot_grad[index] = grads[place].astype(F32)
            new_left[index] = STAT_DECAY * left_stat[index] + (1.0 - STAT_DECAY) * outer_left[place]
            new_right[index] = STAT_DECAY * right_stat[index] + (1.0 - STAT_DECAY) * outer_right[place]
            new_master[index] = master[index] - MATRIX_RATE * totals[place]


def update(position, held, early, late, master, left_stat, right_stat, left_root, right_root):
    slot_count = master.shape[0]
    group = max(size for size in range(1, 12) if slot_count % size == 0)
    some = pl.BlockSpec((group, BLK, BLK), lambda step, *_: (step, 0, 0))

    def whole(shape):
        return pl.BlockSpec(shape, lambda step, *_: (0, 0), pipeline_mode=pl.Buffered(1))

    return pl.pallas_call(
        update_kernel,
        grid_spec=pltpu.PrefetchScalarGridSpec(
            num_scalar_prefetch=2,
            grid=(slot_count // group,),
            in_specs=[whole(early.shape), whole(late.shape)] + [some] * 5,
            out_specs=[some] * 4,
        ),
        out_shape=[jax.ShapeDtypeStruct(master.shape, F32)] * 4,
        compiler_params=pltpu.CompilerParams(vmem_limit_bytes=60 * MIB),
        cost_estimate=pl.CostEstimate(
            flops=8 * slot_count * BLK**3, bytes_accessed=36 * slot_count * BLK**2, transcendentals=0
        ),
        name="update",
    )(position, held, early, late, master, left_stat, right_stat, left_root, right_root)


def body(
    x_short,
    x_long,
    cot_short,
    cot_long,
    logit_cot_short,
    logit_cot_long,
    len_short,
    len_long,
    block_slot,
    master,
    left_stat,
    right_stat,
    left_root,
    right_root,
    small_params,
    small_first,
    small_second,
    own_transfers,
):
    slot_count = master.shape[0]
    shards = lax.axis_size("fsdp")
    all_slots = slot_count * shards
    short_seqs, width = x_short.shape[:2]
    long_seqs = x_long.shape[0]
    short_tiles = short_seqs * width // TILE
    per_tile = TILE // width

    own = jnp.arange(slot_count, dtype=jnp.int32) + slot_count * lax.axis_index("fsdp")
    held = jnp.any(block_slot[None, :] == own[:, None], axis=1).astype(jnp.int32)
    if own_transfers:
        early_count = slot_count - LATE
        code, position, most = slot_codes(
            jnp.concatenate([block_slot, own]), block_slot[: 3 * 36], slot_count, shards
        )
        position = position[NBLK:]
        code = code[:NBLK]
        fits = most <= LATE
        gathered = gather_shards(master)
    else:
        gathered = lax.all_gather(master.astype(BF16), "fsdp", axis=0, tiled=True)
    w_qkv = assemble(block_slot, gathered)
    pieces = unpack(small_params)
    params = jnp.pad(small_params, (0, SMALL_ROWS * BLK - small_params.shape[0])).reshape(SMALL_ROWS, BLK)
    w_class = pieces[-2].reshape(SD, NCLS)
    b_class = pieces[-1].reshape(1, NCLS)
    x, *qkv, context, probs_short, probs_long = attention(
        len_short,
        len_long,
        x_short.reshape(-1, D),
        x_long.reshape(-1, D),
        params,
        w_qkv,
        short_tiles,
        width,
    )

    (
        enc_short,
        enc_long,
        logits_short,
        logits_long,
        first,
        active,
        d_up,
        d_down,
        d_branch,
        d_context,
        d_resid,
        g_student,
        g_hidden,
        g_small,
    ) = feed(
        len_short,
        len_long,
        block_slot,
        x,
        context,
        cot_short.reshape(-1, D),
        cot_long.reshape(-1, D),
        (logit_cot_short, logit_cot_long),
        (params, w_class, b_class),
        gathered,
        short_tiles,
        width,
    )
    g_out = left_product(context, d_branch).astype(BF16)
    others = (g_out, g_student.astype(BF16), g_hidden.astype(BF16))
    if own_transfers:
        terms = feed_grads(code, first, d_down, active, d_up, others, all_slots)
        *back, early_reduced = attention_back(
            qkv,
            probs_short,
            probs_long,
            d_context,
            x,
            short_tiles,
            terms.reshape(-1, BLK),
            early_count * BLK,
        )
    else:
        back = attention_back(qkv, probs_short, probs_long, d_context, x, short_tiles)
    d_qkv, g_b_query, g_b_value, g_qkv = back

    def reduce_all():
        slot_terms = feed_grads(block_slot, first, d_down, active, d_up, others, all_slots)
        slot_terms, small_terms = spread_late(
            block_slot, g_qkv, g_small, g_b_query, g_b_value, slot_terms
        )
        reduced = lax.psum_scatter(slot_terms, "fsdp", scatter_dimension=0, tiled=True)
        return lax.psum(reduced, "dp").reshape(-1, BLK), small_terms

    def renew(places, early, late):
        return update(
            places, held, early, late, master, left_stat, right_stat, left_root, right_root
        )

    def renew_all(blocks):
        return renew(jnp.arange(slot_count, dtype=jnp.int32), blocks, blocks)

    if own_transfers:
        terms, small_terms = spread_late(code, g_qkv, g_small, g_b_query, g_b_value, terms)
        late_reduced, small_total, in_short, in_long = reduce_late(
            terms.reshape(-1, BLK),
            shards * early_count * BLK,
            LATE * BLK,
            small_terms,
            d_qkv,
            d_resid,
            w_qkv,
            short_tiles,
        )

        updated = lax.cond(
            fits,
            lambda: renew(position, early_reduced, late_reduced),
            lambda: renew_all(reduce_all()[0]),
        )
    else:
        in_short, in_long = input_grads(d_qkv, d_resid, w_qkv, short_tiles)
        blocks, small_terms = reduce_all()
        updated = renew_all(blocks)
        small_total = lax.psum(small_terms, ("dp", "fsdp"))
    slot_grad, new_left, new_right, new_master = updated
    small_grad = jnp.concatenate(
        [
            small_total[:CLASS_ROW].reshape(-1),
            small_total[CLASS_ROW : CLASS_ROW + NCLS].T.reshape(-1),
            small_total[LAST_ROW, :NCLS],
        ]
    )
    new_first = BETA_ONE * small_first + (1.0 - BETA_ONE) * small_grad
    new_second = BETA_TWO * small_second + (1.0 - BETA_TWO) * small_grad * small_grad
    first_hat = new_first / (1.0 - BETA_ONE**STEP)
    second_hat = new_second / (1.0 - BETA_TWO**STEP)
    new_small = small_params - ADAM_RATE * first_hat / (jnp.sqrt(second_hat) + ADAM_EPSILON)
    return (
        enc_short.reshape(x_short.shape),
        logits_short,
        enc_long.reshape(x_long.shape),
        logits_long,
        in_short.reshape(x_short.shape),
        in_long.reshape(x_long.shape),
        slot_grad,
        new_left,
        new_right,
        new_master,
        new_first,
        new_second,
        new_small,
    )


def solution(mesh):
    both = ("dp", "fsdp")
    placed = (
        P(both, None, None),
        P(both, None, None),
        P(both, None, None),
        P(both, None, None),
        P(both, None),
        P(both, None),
        P(both),
        P(both),
        P(),
        P("fsdp", None, None),
        P("fsdp", None, None),
        P("fsdp", None, None),
        P("fsdp", None, None),
        P("fsdp", None, None),
        P(),
        P(),
        P(),
    )
    return jax.shard_map(
        partial(body, own_transfers=(mesh.shape["dp"], mesh.shape["fsdp"]) == (4, 8)),
        mesh=mesh,
        in_specs=placed,
        out_specs=(
            P(both, None, None),
            P(both, None),
            P(both, None, None),
            P(both, None),
            P(both, None, None),
            P(both, None, None),
            P("fsdp", None, None),
            P("fsdp", None, None),
            P("fsdp", None, None),
            P("fsdp", None, None),
            P(),
            P(),
            P(),
        ),
        check_vma=False,
    )
```
